128 devices in a mesh: ctx: 8 (over z_hi, y), exp: 16 (over x, z_lo, core).
Axes of the slice: x: 4, y: 4, z: 4 (z_hi: 2, z_lo: 2; z = z_hi * 2 + z_lo), core: 2. Of those that a mesh axis runs over, the one named last changes fastest.
Arguments:
- tokens: bfloat16 [16, 1024, 1536], P('exp', 'ctx'), may hold values from -6 to 6
- routes: int32 [16, 1024, 6], P('exp', 'ctx'), may hold values from 0 to 31, all different within a row; in each aligned block of 128 rows (0 to 127, 128 to 255, ..., all dimensions but the last counted through in order) at most 48 rows name the same one
- route_gates: float32 [16, 1024, 6], P('exp', 'ctx'), may hold values from 0.1 to 0.25
- norm_attn: bfloat16 [1536], P('exp'), may hold values from 0.099609375 to 1.8984375
- norm_ffn: bfloat16 [1536], P('exp'), may hold values from 0.099609375 to 1.8984375
- query_weight: bfloat16 [1536, 1536], P('exp'), may hold values from -0.3125 to 0.3125
- key_weight: bfloat16 [1536, 512], P('exp'), may hold values from -0.15625 to 0.15625
- value_weight: bfloat16 [1536, 512], P('exp'), may hold values from -0.15625 to 0.15625
- out_weight: bfloat16 [1536, 1536], P('exp'), may hold values from -0.625 to 0.625
- shared_gate: bfloat16 [1536, 1024], P('exp'), may hold values from -0.15625 to 0.15625
- shared_up: bfloat16 [1536, 1024], P('exp'), may hold values from -0.15625 to 0.15625
- shared_down: bfloat16 [1024, 1536], P('exp'), may hold values from -0.375 to 0.375
- expert_gate: bfloat16 [32, 1536, 512], P('exp'), may hold values from -0.15625 to 0.15625
- expert_up: bfloat16 [32, 1536, 512], P('exp'), may hold values from -0.15625 to 0.15625
- expert_down: bfloat16 [32, 512, 1536], P('exp'), may hold values from -0.75 to 0.75
- cotangent: bfloat16 [16, 1024, 1536], P('exp', 'ctx'), may hold values from -6 to 6
Outputs:
- mixed: bfloat16 [16, 1024, 1536], P('exp', 'ctx')
- input_grad: bfloat16 [16, 1024, 1536], P('exp', 'ctx')
- grad_norm_attn: float32 [1536], P('exp')
- grad_norm_ffn: float32 [1536], P('exp')
- grad_query: float32 [1536, 1536], P('exp')
- grad_key: float32 [1536, 512], P('exp')
- grad_value: float32 [1536, 512], P('exp')
- grad_out: float32 [1536, 1536], P('exp')
- grad_shared_gate: float32 [1536, 1024], P('exp')
- grad_shared_up: float32 [1536, 1024], P('exp')
- grad_shared_down: float32 [1024, 1536], P('exp')
- grad_expert_gate: float32 [32, 1536, 512], P('exp')
- grad_expert_up: float32 [32, 1536, 512], P('exp')
- grad_expert_down: float32 [32, 512, 1536], P('exp')
The draws below stay inside these ranges and needn't reach their ends.
Inputs may be any that keep to these rules, and one draw needn't show every extreme that they name: `routes`: each token names 6 different experts. Among the 128 tokens of one device (aligned blocks of positions) no expert is named by more than 48 tokens, and in some blocks one is named by exactly 48.
All inputs are finite; a program needn't handle non-finite values.
Results may differ from the reference program's by a relative error of at most 0.028.
Values may be sent and summed in bfloat16 or wider, within the bound.
No kernel may reach another device: no remote copies, remote signals or barrier semaphores. Data moves between devices by JAX's collectives and lax.ppermute only.
A program may use at most 192 MiB of HBM per device.

```python
import math
import jax
import jax.numpy as jnp
import numpy as np
from jax import lax

D = 1536
HEADS = 12
KV_HEADS = 4
HEAD_DIM = 128
FF_E = 512
FF_S = 1024
TOPK = 6
GROUP = 3
BLOCK = 128
SEQ_LEN = 1024
SEQS = 16
EXPERTS = 32
CAP = 48
N_CTX = 8


def level_of(rng, dims, shards, smallest, high):
    level, own = 1.0, jax.random.fold_in(rng, 6)
    for axis_at, blocks in shards:
        steps = jnp.exp(jax.random.uniform(jax.random.fold_in(own, axis_at), (blocks,), jnp.float32, smallest / len(shards), high / len(shards)))
        level = level * jnp.repeat(steps, dims[axis_at] // blocks).reshape([-1 if axis == axis_at else 1 for axis in range(len(dims))])
    return level


def deal_out(rng, own, number, rows, amount, top, reach, slope):
    ranking = jax.random.permutation(rng, amount)
    crowded, ordinary = portions_of(amount, rows * top, reach, slope, True), portions_of(amount, rows * top, reach, slope, False)
    places = jnp.arange(amount)

    def named(sizes, offset_by):
        used = int((sizes > 0).sum())
        fixed = max(1, used // 4)
        moved = fixed + (places - fixed + offset_by * (used - fixed)) % max(1, amount - fixed)
        return jnp.zeros((amount,), jnp.int32).at[ranking[jnp.where(places < fixed, places, moved)]].set(jnp.asarray(sizes, jnp.int32))

    sizes = jnp.where(number % 4 == 0, named(crowded, number // 4), named(ordinary, number - number // 4 - 1))
    mixed = jax.random.permutation(jax.random.fold_in(own, 3), amount)
    donor, sink = mixed[0:amount // 2 * 2:2], mixed[1:amount // 2 * 2:2]
    room = jnp.minimum(sizes[donor] - 1, reach - sizes[sink]) // 2
    room = jnp.where((donor == ranking[0]) | (sink == ranking[0]) | (sizes[sink] == 0), 0, jnp.maximum(room, 0))
    moved = jax.random.randint(jax.random.fold_in(own, 4), (amount // 2,), 0, 1 << 20) % (room + 1)
    sizes = sizes.at[donor].add(-moved).at[sink].add(moved)
    members = jnp.searchsorted(jnp.cumsum(sizes), jnp.arange(rows * top), side="right").astype(jnp.int32)
    listing = members.reshape(top, rows).T
    listing = listing[jax.random.permutation(jax.random.fold_in(own, 1), rows)]
    offset_by = jax.random.randint(jax.random.fold_in(own, 2), (rows, 1), 0, top)
    return jnp.take_along_axis(listing, (jnp.arange(top)[None, :] + offset_by) % top, axis=1)


def portions_of(number_of, total, most, slope, full):
    loads = [(1 << 20) // math.isqrt(rank ** slope) + 1 for rank in range(1, number_of + 1)]
    largest = most if full else min(most, max(-(-total // number_of), total * loads[0] // sum(loads)))
    least = 1 if total - largest >= number_of - 1 else 0
    counts, spare = [largest] + [least] * (number_of - 1), total - largest - least * (number_of - 1)
    while spare > 0:
        free = [i for i in range(1, number_of) if counts[i] < largest] or [i for i in range(1, number_of) if counts[i] < most]
        whole, budget = sum([loads[i] for i in free]), spare
        for i in free:
            extra = min(most - counts[i], max(1, budget * loads[i] // whole), spare)
            counts[i] = counts[i] + extra
            spare = spare - extra
    return np.array(counts)


def bell_draw(key, dims, spread, reach, split=(), kind=jnp.bfloat16):
    drawn = jax.random.normal(key, dims, jnp.float32) * spread
    if len(split) > 0:
        drawn = level_of(key, dims, split, -0.22, 0.18) * drawn
    return jnp.clip(drawn, min=-reach, max=reach).astype(kind)


def setup_inputs(seed: int = 0) -> dict:
    key_of = jax.random.split(jax.random.key(seed), 17)
    tokens = bell_draw(key_of[0], (SEQS, SEQ_LEN, D), 1.0, 6.0, ((0, 16), (1, 8)))
    routes_keys = jax.random.split(jax.random.fold_in(key_of[1], 1), SEQS * SEQ_LEN // BLOCK)
    routes_turns = jax.random.permutation(jax.random.fold_in(key_of[1], 3), SEQS * SEQ_LEN // BLOCK)
    routes = jax.vmap(lambda own, number: deal_out(jax.random.fold_in(key_of[1], 2), own, number, BLOCK, EXPERTS, TOPK, CAP, 1))(routes_keys, routes_turns).reshape((SEQS, SEQ_LEN, TOPK))
    route_gates = jnp.clip(0.1 + 0.15 * jax.random.uniform(key_of[2], (SEQS, SEQ_LEN, TOPK), jnp.float32) ** level_of(key_of[2], (SEQS, SEQ_LEN, TOPK), ((0, 16), (1, 8)), -0.2, 0.2), 0.1, 0.25)
    norm_attn = jnp.clip(1.0 + 0.18 * jax.random.normal(key_of[3], (D,), jnp.float32), 0.099609375, 1.8984375).astype(jnp.bfloat16)
    norm_ffn = jnp.clip(1.0 + 0.18 * jax.random.normal(key_of[4], (D,), jnp.float32), 0.099609375, 1.8984375).astype(jnp.bfloat16)
    query_weight = bell_draw(key_of[5], (D, HEADS * HEAD_DIM), (D // 4) ** -0.5, 0.3125, ((0, 16),))
    key_weight = bell_draw(key_of[6], (D, KV_HEADS * HEAD_DIM), D ** -0.5, 0.15625, ((0, 16),))
    value_weight = bell_draw(key_of[7], (D, KV_HEADS * HEAD_DIM), D ** -0.5, 0.15625, ((0, 16),))
    out_weight = bell_draw(key_of[8], (HEADS * HEAD_DIM, D), (HEADS * HEAD_DIM // 16) ** -0.5, 0.625, ((0, 16),))
    shared_gate = bell_draw(key_of[9], (D, FF_S), D ** -0.5, 0.15625, ((0, 16),))
    shared_up = bell_draw(key_of[10], (D, FF_S), D ** -0.5, 0.15625, ((0, 16),))
    shared_down = bell_draw(key_of[11], (FF_S, D), (FF_S // 4) ** -0.5, 0.375, ((0, 16),))
    expert_gate = bell_draw(key_of[12], (EXPERTS, D, FF_E), D ** -0.5, 0.15625, ((0, 16),))
    expert_up = bell_draw(key_of[13], (EXPERTS, D, FF_E), D ** -0.5, 0.15625, ((0, 16),))
    expert_down = bell_draw(key_of[14], (EXPERTS, FF_E, D), (FF_E // 8) ** -0.5, 0.75, ((0, 16),))
    cotangent = bell_draw(key_of[15], (SEQS, SEQ_LEN, D), 1.0, 6.0, ((0, 16), (1, 8)))
    return dict(tokens=tokens, routes=routes, route_gates=route_gates, norm_attn=norm_attn, norm_ffn=norm_ffn, query_weight=query_weight, key_weight=key_weight, value_weight=value_weight, out_weight=out_weight, shared_gate=shared_gate, shared_up=shared_up, shared_down=shared_down, expert_gate=expert_gate, expert_up=expert_up, expert_down=expert_down, cotangent=cotangent)


@jax.custom_vjp
def low(v):
    return lax.optimization_barrier(v.astype(jnp.bfloat16)).astype(jnp.float32)

@jax.custom_vjp
def low_back(v):
    return v

def low_keep(v):
    return (low(v), None)

def low_pass(kept, grad):
    return (grad,)

def back_keep(v):
    return (v, None)

def back_low(kept, grad):
    return (low(grad),)
low.defvjp(low_keep, low_pass)
low_back.defvjp(back_keep, back_low)
epsilon = 1e-05
masked_score = -1e+30
top_precision = lax.Precision.HIGHEST

def both_ways(operand):
    return low(low_back(operand))

def rms_norm(operand, gain_vec):
    inv_root = lax.rsqrt(lax.optimization_barrier(jnp.mean(operand * operand, axis=-1, keepdims=True)) + epsilon)
    return operand * inv_root * gain_vec

def slot_tables(route_ids):
    blocks = route_ids.reshape(N_CTX, BLOCK * TOPK).astype(jnp.int32)
    expert_ids = jnp.arange(EXPERTS, dtype=jnp.int32)
    onehot = (blocks[:, :, None] == expert_ids[None, None, :]).astype(jnp.int32)
    before = jnp.cumsum(onehot, axis=1) - onehot
    slot_rank = lax.optimization_barrier(jnp.sum(before * onehot, axis=2)).astype(jnp.int32)
    pair_flat = (blocks * CAP + slot_rank).astype(jnp.int32)
    pair_token = (jnp.arange(BLOCK * TOPK, dtype=jnp.int32) // TOPK).astype(jnp.int32)

    def fill_table(one_flat):
        return jnp.full((EXPERTS * CAP,), BLOCK, jnp.int32).at[one_flat].set(pair_token)
    slot_token = jax.vmap(fill_table)(pair_flat)
    return (pair_flat, slot_token)

def take_rows(rows_in, index_of):
    return rows_in[index_of]

def sequence_forward(inputs, gain_attn, gain_ffn, query_w, key_w, value_w, out_w, shared_gw, shared_uw, shared_dw, expert_gw, expert_uw, expert_dw, pair_flat, slot_token, gate_values):
    seq_length = inputs.shape[0]
    hidden_one = low(rms_norm(inputs, gain_attn))
    queries = both_ways(jnp.dot(hidden_one, query_w, precision=top_precision)).reshape(seq_length, KV_HEADS, GROUP, HEAD_DIM)
    key_rows = both_ways(jnp.dot(hidden_one, key_w, precision=top_precision)).reshape(seq_length, KV_HEADS, HEAD_DIM)
    value_rows = both_ways(jnp.dot(hidden_one, value_w, precision=top_precision)).reshape(seq_length, KV_HEADS, HEAD_DIM)
    scores = jnp.einsum('tgjd,sgd->gjts', queries, key_rows, precision=top_precision) * HEAD_DIM ** (-0.5)
    scores = low_back(scores)
    positions = jnp.arange(seq_length, dtype=jnp.int32)
    causal = positions[:, None] >= positions[None, :]
    scores = jnp.where(causal, scores, masked_score)
    softmax_p = jax.nn.softmax(scores, axis=-1)
    attended = jnp.einsum('gjts,sgd->tgjd', softmax_p, value_rows, precision=top_precision).reshape(seq_length, HEADS * HEAD_DIM)
    attended = both_ways(attended)
    middle = inputs + low_back(jnp.dot(attended, out_w, precision=top_precision))
    hidden_two = low(rms_norm(middle, gain_ffn))
    shared_pre_gate = low_back(jnp.dot(hidden_two, shared_gw, precision=top_precision))
    shared_pre_up = low_back(jnp.dot(hidden_two, shared_uw, precision=top_precision))
    shared_hidden = low(jax.nn.silu(shared_pre_gate) * shared_pre_up)
    shared_out = jnp.dot(shared_hidden, shared_dw, precision=top_precision)
    padded_tokens = jnp.concatenate([hidden_two.reshape(N_CTX, BLOCK, D), jnp.zeros((N_CTX, 1, D), jnp.float32)], axis=1)
    buffer = jax.vmap(take_rows)(padded_tokens, slot_token).reshape(N_CTX, EXPERTS, CAP, D)
    buffer = low_back(buffer)
    pre_gate = low_back(jnp.einsum('becd,edf->becf', buffer, expert_gw, precision=top_precision))
    pre_up = low_back(jnp.einsum('becd,edf->becf', buffer, expert_uw, precision=top_precision))
    expert_hidden = low(jax.nn.silu(pre_gate) * pre_up)
    expert_out = both_ways(jnp.einsum('becf,efd->becd', expert_hidden, expert_dw, precision=top_precision))
    expert_out = expert_out.reshape(N_CTX, EXPERTS * CAP, D)
    picked = jax.vmap(take_rows)(expert_out, pair_flat).reshape(N_CTX, BLOCK, TOPK, D)
    routed = lax.optimization_barrier(jnp.sum(gate_values.reshape(N_CTX, BLOCK, TOPK, 1) * picked, axis=2)).reshape(seq_length, D)
    return middle + shared_out + routed

def reference(tokens, routes, route_gates, norm_attn, norm_ffn, query_weight, key_weight, value_weight, out_weight, shared_gate, shared_up, shared_down, expert_gate, expert_up, expert_down, cotangent):
    weights = tuple((w.astype(jnp.float32) for w in (norm_attn, norm_ffn, query_weight, key_weight, value_weight, out_weight, shared_gate, shared_up, shared_down, expert_gate, expert_up, expert_down)))

    def one_sequence(totals, inputs):
        seq_tokens, seq_routes, seq_gates, seq_cot = inputs
        pair_flat, slot_token = slot_tables(seq_routes)

        def forward(values, *params):
            return sequence_forward(values, *params, pair_flat, slot_token, seq_gates.astype(jnp.float32))
        output, pullback = jax.vjp(forward, seq_tokens.astype(jnp.float32), *weights)
        grads = pullback(seq_cot.astype(jnp.float32))
        totals = tuple((a + b for a, b in zip(totals, grads[1:])))
        return (totals, (output.astype(jnp.bfloat16), grads[0].astype(jnp.bfloat16)))
    zero_grads = tuple((jnp.zeros(w.shape, jnp.float32) for w in weights))
    totals, outputs = lax.scan(one_sequence, zero_grads, (tokens, routes, route_gates, cotangent))
    return (outputs[0], outputs[1], totals[0], totals[1], totals[2], totals[3], totals[4], totals[5], totals[6], totals[7], totals[8], totals[9], totals[10], totals[11])
```

```python
import jax
import jax.numpy as jnp
from jax import lax
from jax.sharding import PartitionSpec as P

HEADS = 12
KV_HEADS = 4
HEAD_DIM = 128
TOPK = 6
GROUP = 3
BLOCK = 128
WIDTH = 1536
KV_WIDTH = KV_HEADS * HEAD_DIM
CAP = 48
N_EXP = 16
N_CTX = 8
LOCAL_E = 2
FF_E = 512
SHARED = 64
META = 128

epsilon = 1e-05
masked_score = -1e30
f32 = jnp.float32
bf16 = jnp.bfloat16

same_core = [[2 * i + c for i in range(8)] for c in range(2)]
core_swap = [(i, i ^ 1) for i in range(N_EXP)]
y_groups = [[0, 1, 2, 3], [4, 5, 6, 7]]
z_swap = [(i, i ^ 4) for i in range(N_CTX)]


def silu_slope(operand):
    sigmoid_v = jax.nn.sigmoid(operand)
    return sigmoid_v * (1.0 + operand * (1.0 - sigmoid_v))


def norm_back(grad_normed, normed, inv_root):
    return inv_root * (
        grad_normed - normed * jnp.mean(grad_normed * normed, axis=-1, keepdims=True)
    )


def mm(a, b, dims=None):
    if dims is None:
        return jnp.dot(a, b, preferred_element_type=f32)
    return lax.dot_general(a, b, (dims, ((), ())), preferred_element_type=f32)


def swap_all(rows, axis, groups=None):
    return lax.all_to_all(
        rows, axis, split_axis=0, concat_axis=0, tiled=True, axis_index_groups=groups
    )


def pick(parts, at):
    return lax.dynamic_index_in_dim(parts, at, 0, keepdims=False)


def add_low(a, b):
    return (a.astype(f32) + b.astype(f32)).astype(bf16)


def reduce_exp(parts, core):
    by_core = parts.reshape(8, 2, BLOCK, WIDTH)
    keep = lax.dynamic_index_in_dim(by_core, core, 1, keepdims=False)
    send = lax.dynamic_index_in_dim(by_core, 1 - core, 1, keepdims=False)
    got = lax.ppermute(send, "exp", core_swap)
    pieces = swap_all(add_low(keep, got), "exp", same_core)
    return jnp.sum(pieces.astype(f32), axis=0)


def sum_ctx_y(grad, z_at):
    rows, cols = grad.shape
    piece = rows // N_CTX
    pieces = swap_all(grad.reshape(4, 2, piece, cols), "ctx", y_groups)
    summed = jnp.sum(pieces.astype(f32), axis=0).astype(bf16)
    got = lax.ppermute(pick(summed, 1 - z_at), "ctx", z_swap)
    own = add_low(pick(summed, z_at), got)
    other = lax.ppermute(own, "ctx", z_swap)
    pair = jnp.where(z_at == 0, jnp.stack([own, other]), jnp.stack([other, own]))
    return swap_all(jnp.broadcast_to(pair, (4, 2, piece, cols)), "ctx", y_groups).reshape(rows, cols)


def sum_ctx_z(grad, z_at):
    rows, cols = grad.shape
    piece = rows // N_CTX
    halves = grad.reshape(2, 4, piece, cols)
    got = lax.ppermute(pick(halves, 1 - z_at), "ctx", z_swap)
    pieces = swap_all(add_low(pick(halves, z_at), got), "ctx", y_groups)
    own = jnp.sum(pieces.astype(f32), axis=0).astype(bf16)
    side = swap_all(jnp.broadcast_to(own, (4, piece, cols)), "ctx", y_groups)
    other = lax.ppermute(side, "ctx", z_swap)
    pair = jnp.where(z_at == 0, jnp.stack([side, other]), jnp.stack([other, side]))
    return pair.reshape(rows, cols)


def sum_ctx_small(grad):
    rows, cols = grad.shape
    pieces = swap_all(grad.reshape(N_CTX, rows // N_CTX, cols), "ctx")
    own = jnp.sum(pieces.astype(f32), axis=0).astype(bf16)
    return swap_all(jnp.broadcast_to(own, (N_CTX,) + own.shape), "ctx").reshape(rows, cols)


def on_device(
    tokens,
    routes,
    route_gates,
    norm_attn,
    norm_ffn,
    query_weight,
    key_weight,
    value_weight,
    out_weight,
    shared_gate,
    shared_up,
    shared_down,
    expert_gate,
    expert_up,
    expert_down,
    cotangent,
):
    exp_at = lax.axis_index("exp")
    ctx_at = lax.axis_index("ctx")
    core = exp_at % 2
    z_at = ctx_at // 4
    head_scale = HEAD_DIM ** (-0.5)

    w_attn = lax.all_gather(
        jnp.concatenate([query_weight, key_weight, value_weight], axis=1), "exp", axis=0, tiled=True
    )
    w_out = lax.all_gather(out_weight, "exp", axis=0, tiled=True)
    gains = jnp.concatenate([norm_attn, norm_ffn])
    gains = swap_all(jnp.broadcast_to(gains, (N_EXP, gains.shape[0])), "exp")
    gain_attn = gains[:, :96].reshape(WIDTH).astype(f32)
    gain_ffn = gains[:, 96:].reshape(WIDTH).astype(f32)
    shared_cols = jnp.concatenate(
        [shared_gate.reshape(96, N_EXP, SHARED), shared_up.reshape(96, N_EXP, SHARED)], axis=2
    ).transpose(1, 0, 2)
    w_shared = swap_all(shared_cols, "exp").reshape(WIDTH, 2 * SHARED)
    gates_high = route_gates[0].astype(bf16)
    gates_low = (route_gates[0] - gates_high.astype(f32)).astype(bf16)
    meta = jnp.concatenate(
        [
            routes[0].astype(bf16),
            gates_high,
            gates_low,
            jnp.zeros((BLOCK, META - 3 * TOPK), bf16),
        ],
        axis=1,
    )
    up_meta = lax.all_gather(
        jnp.concatenate([cotangent[0], meta], axis=1), "exp", axis=0, tiled=True
    )

    inputs = tokens[0].astype(f32)
    scale_one = lax.rsqrt(jnp.mean(inputs * inputs, axis=-1, keepdims=True) + epsilon)
    normed_one = inputs * scale_one
    hidden_one = (normed_one * gain_attn).astype(bf16)
    qkv = mm(hidden_one, w_attn).astype(bf16)
    queries = qkv[:, :WIDTH].reshape(BLOCK, KV_HEADS, GROUP, HEAD_DIM)
    own_kv = qkv[:, WIDTH:]

    y_at = ctx_at % 4
    block_of, kv_pieces = [], []
    from_z = lax.ppermute(own_kv, "ctx", [(i, i + 4) for i in range(4)])
    for step in range(4):
        if step == 0:
            kv_pieces.append(own_kv)
        else:
            kv_pieces.append(
                lax.ppermute(
                    own_kv,
                    "ctx",
                    [(4 * z + y, 4 * z + (y + step) % 4) for z in range(2) for y in range(4)],
                )
            )
        block_of.append(4 * z_at + (y_at - step) % 4)
    for step in range(4):
        if step == 0:
            kv_pieces.append(from_z)
        else:
            kv_pieces.append(
                lax.ppermute(from_z, "ctx", [(4 + y, 4 + (y + step) % 4) for y in range(4)])
            )
        block_of.append(jnp.where(z_at == 0, N_CTX, (y_at - step) % 4))
    kv_all = jnp.concatenate(kv_pieces, axis=0)
    keys = kv_all[:, :KV_WIDTH].reshape(-1, KV_HEADS, HEAD_DIM)
    values = kv_all[:, KV_WIDTH:].reshape(-1, KV_HEADS, HEAD_DIM)
    row_in = jnp.arange(BLOCK, dtype=jnp.int32)
    key_at = (jnp.stack(block_of)[:, None] * BLOCK + row_in[None, :]).reshape(-1)
    allowed = (ctx_at * BLOCK + row_in)[:, None] >= key_at[None, :]

    raw_scores = jnp.where(
        allowed,
        jnp.einsum("tgjd,sgd->gjts", queries, keys, preferred_element_type=f32) * head_scale,
        masked_score,
    )
    row_max = jnp.max(raw_scores, axis=-1)
    weights = jnp.exp(raw_scores - row_max[..., None])
    row_sum = jnp.sum(weights, axis=-1)
    running_out = jnp.einsum(
        "gjts,sgd->gjtd", weights.astype(bf16), values, preferred_element_type=f32
    )
    log_total = row_max + jnp.log(row_sum)
    attended_heads = running_out / row_sum[..., None]
    attended = attended_heads.transpose(2, 0, 1, 3).reshape(BLOCK, WIDTH).astype(bf16)
    middle = inputs + mm(attended, w_out)
    second_scale = lax.rsqrt(jnp.mean(middle * middle, axis=-1, keepdims=True) + epsilon)
    normed_two = middle * second_scale
    hidden_two = (normed_two * gain_ffn).astype(bf16)

    hidden_all = lax.all_gather(hidden_two, "exp", axis=0, tiled=True)
    routes_all = up_meta[:, WIDTH : WIDTH + TOPK].astype(f32)
    gates_all = up_meta[:, WIDTH + TOPK : WIDTH + 2 * TOPK].astype(f32) + up_meta[
        :, WIDTH + 2 * TOPK : WIDTH + 3 * TOPK
    ].astype(f32)
    local_id = (exp_at * LOCAL_E + jnp.arange(LOCAL_E, dtype=jnp.int32)).astype(f32)
    hit = (routes_all[None] == local_id[:, None, None]).astype(f32)
    mask = jnp.sum(hit, axis=-1).reshape(LOCAL_E, N_EXP, BLOCK)
    gate_of = jnp.sum(hit * gates_all[None], axis=-1).reshape(LOCAL_E, N_EXP, BLOCK)
    before = (row_in[:, None] > row_in[None, :]).astype(bf16)
    rank = jnp.einsum("ut,ebt->ebu", before, mask.astype(bf16), preferred_element_type=f32)
    slots = jnp.arange(CAP, dtype=jnp.int32).astype(f32)
    place_f = jnp.where(
        (mask[..., None] > 0.5) & (rank[..., None] == slots), jnp.float32(1.0), jnp.float32(0.0)
    )
    place = place_f.astype(bf16)
    slot_gate = jnp.sum(place_f * gate_of[..., None], axis=2)
    upstream_all = up_meta[:, :WIDTH].reshape(N_EXP, BLOCK, WIDTH)
    rows_e = N_EXP * CAP
    grad_eo = (
        slot_gate[..., None]
        * jnp.einsum("ebts,btd->ebsd", place, upstream_all, preferred_element_type=f32)
    ).astype(bf16).reshape(LOCAL_E, rows_e, WIDTH)
    grad_eh = jnp.einsum("erd,efd->erf", grad_eo, expert_down, preferred_element_type=f32)
    upstream_rows = upstream_all.reshape(N_EXP * BLOCK, WIDTH)
    grad_sh = mm(upstream_rows, shared_down, ((1,), (1,)))

    hidden_blocks = hidden_all.reshape(N_EXP, BLOCK, WIDTH)
    arrived = (
        jnp.einsum("ebts,btd->ebsd", place, hidden_blocks, preferred_element_type=f32)
        .astype(bf16)
        .reshape(LOCAL_E, rows_e, WIDTH)
    )
    pre_gate = jnp.einsum("erd,edf->erf", arrived, expert_gate, preferred_element_type=f32)
    pre_up = jnp.einsum("erd,edf->erf", arrived, expert_up, preferred_element_type=f32)
    expert_hidden = (jax.nn.silu(pre_gate) * pre_up).astype(bf16)
    grad_pre_gate = (grad_eh * pre_up * silu_slope(pre_gate)).astype(bf16)
    grad_pre_up = (grad_eh * jax.nn.silu(pre_gate)).astype(bf16)
    pair_in = (
        jnp.einsum("erf,edf->erd", grad_pre_gate, expert_gate, preferred_element_type=f32)
        + jnp.einsum("erf,edf->erd", grad_pre_up, expert_up, preferred_element_type=f32)
    ).astype(bf16)
    shared_pre = mm(hidden_all, w_shared)
    shared_pre_gate, shared_pre_up = shared_pre[:, :SHARED], shared_pre[:, SHARED:]
    shared_hidden = (jax.nn.silu(shared_pre_gate) * shared_pre_up).astype(bf16)
    grad_shared_pre = jnp.concatenate(
        [
            (grad_sh * shared_pre_up * silu_slope(shared_pre_gate)).astype(bf16),
            (grad_sh * jax.nn.silu(shared_pre_gate)).astype(bf16),
        ],
        axis=1,
    )
    grad_two_part = (
        jnp.einsum(
            "ebts,ebsd->btd",
            place,
            pair_in.reshape(LOCAL_E, N_EXP, CAP, WIDTH),
            preferred_element_type=f32,
        )
        + mm(grad_shared_pre, w_shared, ((1,), (1,))).reshape(N_EXP, BLOCK, WIDTH)
    ).astype(bf16)
    grad_two = reduce_exp(grad_two_part, core)

    grad_edown = jnp.einsum("erf,erd->efd", expert_hidden, grad_eo, preferred_element_type=f32)
    grad_egate = jnp.einsum("erd,erf->edf", arrived, grad_pre_gate, preferred_element_type=f32)
    grad_eup = jnp.einsum("erd,erf->edf", arrived, grad_pre_up, preferred_element_type=f32)
    sum_edown = sum_ctx_y(grad_edown.astype(bf16).reshape(LOCAL_E * FF_E, WIDTH), z_at)
    sum_egate = sum_ctx_y(grad_egate.astype(bf16).reshape(LOCAL_E * WIDTH, FF_E), z_at)
    sum_eup = sum_ctx_z(grad_eup.astype(bf16).reshape(LOCAL_E * WIDTH, FF_E), z_at)

    expert_out = jnp.einsum("erf,efd->erd", expert_hidden, expert_down, preferred_element_type=f32)
    gated_out = (
        expert_out.astype(bf16).astype(f32) * slot_gate.reshape(LOCAL_E, rows_e, 1)
    ).astype(bf16)
    out_part = (
        jnp.einsum(
            "ebts,ebsd->btd",
            place,
            gated_out.reshape(LOCAL_E, N_EXP, CAP, WIDTH),
            preferred_element_type=f32,
        )
        + mm(shared_hidden, shared_down).reshape(N_EXP, BLOCK, WIDTH)
    ).astype(bf16)
    mixed = (middle + reduce_exp(out_part, core)).astype(bf16)[None]

    grad_sdown = mm(shared_hidden, upstream_rows, ((0,), (0,)))
    grad_scols = mm(hidden_all, grad_shared_pre, ((0,), (0,))).astype(bf16)
    grad_scols = swap_all(grad_scols.reshape(N_EXP, 96, 2 * SHARED), "exp").transpose(1, 0, 2)

    upstream_f = cotangent[0].astype(f32)
    grad_gain_ffn = jnp.sum(grad_two * normed_two, axis=0)
    grad_middle = upstream_f + norm_back(grad_two * gain_ffn, normed_two, second_scale)
    grad_attn = grad_middle.astype(bf16)
    grad_heads = mm(grad_attn, w_out, ((1,), (1,))).astype(bf16)
    grad_heads = grad_heads.reshape(BLOCK, KV_HEADS, GROUP, HEAD_DIM)
    grad_heads_f = grad_heads.astype(f32)
    row_difference = jnp.einsum("tgjd,gjtd->gjt", grad_heads_f, attended_heads)
    weights_b = jnp.exp(raw_scores - log_total[..., None])
    grad_weights = jnp.einsum("tgjd,sgd->gjts", grad_heads, values, preferred_element_type=f32)
    grad_raw = (weights_b * (grad_weights - row_difference[..., None])).astype(bf16)
    grad_query = (
        jnp.einsum("gjts,sgd->tgjd", grad_raw, keys, preferred_element_type=f32) * head_scale
    ).reshape(BLOCK, WIDTH).astype(bf16)
    part_keys = (
        jnp.einsum("gjts,tgjd->sgd", grad_raw, queries, preferred_element_type=f32) * head_scale
    ).reshape(-1, KV_WIDTH)
    part_values = jnp.einsum(
        "gjts,tgjd->sgd", weights_b.astype(bf16), grad_heads, preferred_element_type=f32
    ).reshape(-1, KV_WIDTH)
    part_kv = jnp.concatenate([part_keys, part_values], axis=1).astype(bf16)
    part_kv = part_kv.reshape(2, 4, BLOCK, 2 * KV_WIDTH)

    grad_kv = part_kv[0, 0].astype(f32)
    grad_z = part_kv[1, 0].astype(f32)
    for step in range(1, 4):
        grad_kv = grad_kv + lax.ppermute(
            part_kv[0, step],
            "ctx",
            [(4 * z + (y + step) % 4, 4 * z + y) for z in range(2) for y in range(4)],
        ).astype(f32)
        grad_z = grad_z + lax.ppermute(
            part_kv[1, step], "ctx", [(4 + (y + step) % 4, 4 + y) for y in range(4)]
        ).astype(f32)
    grad_kv = grad_kv + lax.ppermute(
        grad_z.astype(bf16), "ctx", [(i + 4, i) for i in range(4)]
    ).astype(f32)
    grad_kv = grad_kv.astype(bf16)

    grad_qkv = jnp.concatenate([grad_query, grad_kv], axis=1)
    grad_one = mm(grad_qkv, w_attn, ((1,), (1,)))
    grad_gain_attn = jnp.sum(grad_one * normed_one, axis=0)
    input_grad = (
        grad_middle + norm_back(grad_one * gain_attn, normed_one, scale_one)
    ).astype(bf16)[None]

    hidden_one_all = lax.all_gather(hidden_one, "exp", axis=0, tiled=True)
    grad_attn_all = lax.all_gather(grad_attn, "exp", axis=0, tiled=True)
    attended_cols = swap_all(
        attended.reshape(BLOCK, N_EXP, 96).transpose(1, 0, 2), "exp"
    ).reshape(N_EXP * BLOCK, 96)
    grad_wout = mm(attended_cols, grad_attn_all, ((0,), (0,)))

    cols = jnp.concatenate(
        [
            grad_query.reshape(BLOCK, N_EXP, 96),
            grad_kv[:, :KV_WIDTH].reshape(BLOCK, N_EXP, 32),
            grad_kv[:, KV_WIDTH:].reshape(BLOCK, N_EXP, 32),
        ],
        axis=2,
    ).transpose(1, 0, 2)
    cols = swap_all(cols, "exp").reshape(N_EXP * BLOCK, 160)
    grad_cols = mm(hidden_one_all, cols, ((0,), (0,))).astype(bf16).reshape(N_EXP, 96, 160)
    gain_parts = jnp.stack(
        [grad_gain_attn.reshape(N_EXP, 96), grad_gain_ffn.reshape(N_EXP, 96)], axis=-1
    ).astype(bf16)
    back = swap_all(
        jnp.concatenate([grad_cols, gain_parts, jnp.zeros((N_EXP, 96, 30), bf16)], axis=2), "exp"
    )
    gain_sum = jnp.sum(back[:, :, 160:162].astype(f32), axis=0).astype(bf16)
    back = back.transpose(1, 0, 2)

    early = sum_ctx_small(
        jnp.concatenate(
            [
                grad_wout.astype(bf16),
                grad_sdown.astype(bf16),
                grad_scols[:, :, :SHARED].reshape(96 * 1024 // WIDTH, WIDTH),
                grad_scols[:, :, SHARED:].reshape(96 * 1024 // WIDTH, WIDTH),
            ],
            axis=0,
        )
    )
    late = sum_ctx_small(
        jnp.concatenate(
            [
                back[:, :, :96].reshape(96, WIDTH),
                back[:, :, 96:128].reshape(96, KV_WIDTH),
                back[:, :, 128:160].reshape(96, KV_WIDTH),
                jnp.pad(gain_sum, ((0, 0), (0, 126))),
            ],
            axis=1,
        )
    ).astype(f32)
    early = early.astype(f32)
    return (
        mixed,
        input_grad,
        late[:, 2560],
        late[:, 2561],
        late[:, :WIDTH],
        late[:, WIDTH : WIDTH + KV_WIDTH],
        late[:, WIDTH + KV_WIDTH : WIDTH + 2 * KV_WIDTH],
        early[:96],
        early[160:224].reshape(96, 1024),
        early[224:288].reshape(96, 1024),
        early[96:160],
        sum_egate.astype(f32).reshape(LOCAL_E, WIDTH, FF_E),
        sum_eup.astype(f32).reshape(LOCAL_E, WIDTH, FF_E),
        sum_edown.astype(f32).reshape(LOCAL_E, FF_E, WIDTH),
    )


def solution(mesh):
    token_spec = P("exp", "ctx", None)
    rows = P("exp", None)
    expert = P("exp", None, None)
    placed = (token_spec,) * 3 + (P("exp"),) * 2 + (rows,) * 7 + (expert,) * 3 + (token_spec,)
    return jax.shard_map(
        on_device,
        mesh=mesh,
        in_specs=placed,
        out_specs=(token_spec,) * 2 + (P("exp"),) * 2 + (rows,) * 7 + (expert,) * 3,
        check_vma=False,
    )
```

```python
import jax
import jax.numpy as jnp
from jax import lax
from jax.sharding import PartitionSpec as P
from jax.experimental import pallas as pl
from jax.experimental.pallas import tpu as pltpu

HEADS = 12
KV_HEADS = 4
HEAD_DIM = 128
TOPK = 6
GROUP = 3
BLOCK = 128
WIDTH = 1536
KV_WIDTH = KV_HEADS * HEAD_DIM
CAP = 48
N_EXP = 16
N_CTX = 8
LOCAL_E = 2
FF_E = 512
SHARED = 64
META = 128
HALF = 8
ROWS = HALF * CAP

epsilon = 1e-05
masked_score = -1e30
f32 = jnp.float32
bf16 = jnp.bfloat16
log2_e = 1.4426950408889634
score_scale = HEAD_DIM ** (-0.5) * log2_e

NN = (((1,), (0,)), ((), ()))
NT = (((1,), (1,)), ((), ()))
TN = (((0,), (0,)), ((), ()))


def dg(a, b, dims):
    return lax.dot_general(a, b, dims, preferred_element_type=f32)


def params(mib):
    return pltpu.CompilerParams(vmem_limit_bytes=mib * 1024 * 1024)


def whole(shape):
    return pl.BlockSpec(shape, lambda *_: (0,) * len(shape), pipeline_mode=pl.Buffered(1))


def sigmoid(v):
    return 1.0 / (1.0 + jnp.exp(-v))


def allowed_scores(ctx_at):
    rows = lax.broadcasted_iota(jnp.int32, (GROUP * BLOCK, N_CTX * BLOCK), 0) % BLOCK
    cols = lax.broadcasted_iota(jnp.int32, (GROUP * BLOCK, N_CTX * BLOCK), 1)
    return rows + ctx_at * BLOCK >= cols


def stack_heads(block):
    return jnp.concatenate([block[:, j * HEAD_DIM : (j + 1) * HEAD_DIM] for j in range(GROUP)], axis=0)


def unstack_heads(rows):
    return jnp.concatenate([rows[j * BLOCK : (j + 1) * BLOCK] for j in range(GROUP)], axis=1)


def attend_kernel(ctx_ref, q_ref, k_ref, v_ref, att_ref, attf_ref, log_ref):
    q = stack_heads(q_ref[...])
    keys = k_ref[...].reshape(N_CTX * BLOCK, HEAD_DIM)
    values = v_ref[...].reshape(N_CTX * BLOCK, HEAD_DIM)
    scores = jnp.where(allowed_scores(ctx_ref[0]), dg(q, keys, NT) * score_scale, masked_score)
    top = jnp.max(scores, axis=-1, keepdims=True)
    weights = jnp.exp2(scores - top)
    total = jnp.sum(weights, axis=-1, keepdims=True)
    out = dg(weights.astype(bf16), values, NN) * (1.0 / total)
    out = unstack_heads(out)
    attf_ref[...] = out
    att_ref[...] = out.astype(bf16)
    log_ref[...] = jnp.broadcast_to(top + jnp.log2(total), (GROUP * BLOCK, HEAD_DIM))


def kv_specs():
    return [
        pl.BlockSpec((N_CTX, BLOCK, HEAD_DIM), lambda g: (0, 0, 2 * g)),
        pl.BlockSpec((N_CTX, BLOCK, HEAD_DIM), lambda g: (0, 0, 2 * g + 1)),
    ]


def head_spec():
    return pl.BlockSpec((BLOCK, GROUP * HEAD_DIM), lambda g: (0, g))


def attend(ctx_at, qkv, kv_all):
    return pl.pallas_call(
        attend_kernel,
        grid=(KV_HEADS,),
        in_specs=[pl.BlockSpec(memory_space=pltpu.SMEM), head_spec()] + kv_specs(),
        out_specs=[
            head_spec(),
            head_spec(),
            pl.BlockSpec((GROUP * BLOCK, HEAD_DIM), lambda g: (g, 0)),
        ],
        out_shape=[
            jax.ShapeDtypeStruct((BLOCK, WIDTH), bf16),
            jax.ShapeDtypeStruct((BLOCK, WIDTH), f32),
            jax.ShapeDtypeStruct((HEADS * BLOCK, HEAD_DIM), f32),
        ],
        compiler_params=params(48),
        name="attend",
    )(ctx_at, qkv, kv_all, kv_all)


def attend_back_kernel(
    ctx_ref, q_ref, ga_ref, attf_ref, log_ref, k_ref, v_ref, dq_ref, dkv_ref
):
    q = stack_heads(q_ref[...])
    grad = stack_heads(ga_ref[...])
    delta = jnp.sum(grad.astype(f32) * stack_heads(attf_ref[...]), axis=-1, keepdims=True)
    keys = k_ref[...].reshape(N_CTX * BLOCK, HEAD_DIM)
    values = v_ref[...].reshape(N_CTX * BLOCK, HEAD_DIM)
    scores = jnp.where(allowed_scores(ctx_ref[0]), dg(q, keys, NT) * score_scale, masked_score)
    weights = jnp.exp2(scores - log_ref[:, :1])
    grad_weights = dg(grad, values, NT)
    grad_raw = (weights * (grad_weights - delta)).astype(bf16)
    scale = HEAD_DIM ** (-0.5)
    dq_ref[...] = unstack_heads(dg(grad_raw, keys, NN) * scale).astype(bf16)
    grad_k = (dg(grad_raw, q, TN) * scale).astype(bf16)
    grad_v = dg(weights.astype(bf16), grad, TN).astype(bf16)
    dkv_ref[:, :, :HEAD_DIM] = grad_k.reshape(N_CTX, BLOCK, HEAD_DIM)
    dkv_ref[:, :, HEAD_DIM:] = grad_v.reshape(N_CTX, BLOCK, HEAD_DIM)


def attend_back(ctx_at, qkv, grad_att, att_f, logs, kv_all):
    part = pl.BlockSpec((N_CTX, BLOCK, 2 * HEAD_DIM), lambda g: (0, 0, g))
    return pl.pallas_call(
        attend_back_kernel,
        grid=(KV_HEADS,),
        in_specs=[
            pl.BlockSpec(memory_space=pltpu.SMEM),
            head_spec(),
            head_spec(),
            head_spec(),
            pl.BlockSpec((GROUP * BLOCK, HEAD_DIM), lambda g: (g, 0)),
        ]
        + kv_specs(),
        out_specs=[head_spec(), part],
        out_shape=[
            jax.ShapeDtypeStruct((BLOCK, WIDTH), bf16),
            jax.ShapeDtypeStruct((N_CTX, BLOCK, 2 * KV_WIDTH), bf16),
        ],
        compiler_params=params(48),
        name="attend_back",
    )(ctx_at, qkv, grad_att, att_f, logs, kv_all, kv_all)


def middle_kernel(att_ref, w_ref, x_ref, gain_ref, middle_ref, hidden_ref):
    middle = x_ref[...].astype(f32) + dg(att_ref[...], w_ref[...], NN)
    inv = lax.rsqrt(jnp.mean(middle * middle, axis=-1, keepdims=True) + epsilon)
    middle_ref[...] = middle
    hidden_ref[...] = (middle * inv * gain_ref[...]).astype(bf16)


def middle_norm(attended, w_out, tokens, gain):
    return pl.pallas_call(
        middle_kernel,
        out_shape=[
            jax.ShapeDtypeStruct((BLOCK, WIDTH), f32),
            jax.ShapeDtypeStruct((BLOCK, WIDTH), bf16),
        ],
        compiler_params=params(32),
        name="middle_norm",
    )(attended, w_out, tokens, gain)


def norm_back(grad_normed, normed, inv_root):
    return inv_root * (
        grad_normed - normed * jnp.mean(grad_normed * normed, axis=-1, keepdims=True)
    )


def middle_back_kernel(
    pieces_ref, middle_ref, up_ref, gain_ref, w_ref, gm_ref, ga_ref, gh_ref, gg_ref
):
    grad_two = pieces_ref[0].astype(f32)
    for i in range(1, HALF):
        grad_two = grad_two + pieces_ref[i].astype(f32)
    middle = middle_ref[...]
    inv = lax.rsqrt(jnp.mean(middle * middle, axis=-1, keepdims=True) + epsilon)
    normed = middle * inv
    gg_ref[...] = jnp.sum(grad_two * normed, axis=0, keepdims=True)
    grad_middle = up_ref[...].astype(f32) + norm_back(grad_two * gain_ref[...], normed, inv)
    gm_ref[...] = grad_middle
    grad_attn = grad_middle.astype(bf16)
    ga_ref[...] = grad_attn
    gh_ref[...] = dg(grad_attn, w_ref[...], NT).astype(bf16)


def middle_back(pieces, middle, upstream, gain, w_out):
    return pl.pallas_call(
        middle_back_kernel,
        out_shape=[
            jax.ShapeDtypeStruct((BLOCK, WIDTH), f32),
            jax.ShapeDtypeStruct((BLOCK, WIDTH), bf16),
            jax.ShapeDtypeStruct((BLOCK, WIDTH), bf16),
            jax.ShapeDtypeStruct((1, WIDTH), f32),
        ],
        compiler_params=params(48),
        name="middle_back",
    )(pieces, middle, upstream, gain, w_out)


def place_kernel(
    at_ref, own_ref, other_ref, down_ref, sdown_ref, place_ref, geo_ref, geh_ref, gsh_ref, gate_ref
):
    step = pl.program_id(0)
    lane = lax.broadcasted_iota(jnp.int32, (BLOCK, META), 1)
    row = lax.broadcasted_iota(jnp.int32, (BLOCK, META), 0)
    before = (row > lane).astype(bf16)
    slot = (lane % 64).astype(f32)
    first_id = (at_ref[0] * LOCAL_E).astype(f32)
    row_id = first_id + (row >= 64).astype(f32)

    def run(up_ref):
        for chip in range(HALF):
            meta = up_ref[chip, :, WIDTH:].astype(f32)
            named = lane < TOPK
            zero = jnp.zeros((BLOCK, META), f32)
            hit0 = jnp.where(named & (meta == first_id), 1.0, zero)
            hit1 = jnp.where(named & (meta == first_id + 1.0), 1.0, zero)
            mask = jnp.where(
                lane < 64,
                jnp.sum(hit0, axis=1, keepdims=True),
                jnp.sum(hit1, axis=1, keepdims=True),
            )
            rank = dg(before, mask.astype(bf16), NN)
            place = jnp.where((mask > 0.5) & (rank == slot), 1.0, zero).astype(bf16)
            place_ref[chip, 0] = place
            rows = dg(place, up_ref[chip], TN)
            slot_meta = rows[:, WIDTH:]
            gates = pltpu.roll(slot_meta, META - TOPK, 1) + pltpu.roll(
                slot_meta, META - 2 * TOPK, 1
            )
            gate = jnp.sum(
                jnp.where(named & (slot_meta == row_id), gates, zero), axis=1, keepdims=True
            )
            geo = (gate * rows[:, :WIDTH]).astype(bf16)
            wide_gate = jnp.broadcast_to(gate, (BLOCK, META))
            at = chip * CAP
            for e in range(LOCAL_E):
                geo_ref[e, 0, at : at + CAP] = geo[64 * e : 64 * e + CAP]
                gate_ref[e, 0, at : at + CAP] = wide_gate[64 * e : 64 * e + CAP]
            gsh_ref[chip, 0] = dg(up_ref[chip, :, :WIDTH], sdown_ref[...], NT)
        for e in range(LOCAL_E):
            geh_ref[e, 0] = dg(geo_ref[e, 0], down_ref[e], NT)

    @pl.when(step == 0)
    def _():
        run(other_ref)

    @pl.when(step == 1)
    def _():
        run(own_ref)


def by_core(cols):
    return pl.BlockSpec(
        (HALF, 1, BLOCK, cols),
        lambda s, at: (0, jnp.where(s == 0, 1 - at[0] % 2, at[0] % 2), 0, 0),
    )


def by_step(cols):
    return pl.BlockSpec((LOCAL_E, 1, ROWS, cols), lambda s, at: (0, s, 0, 0))


def place_rows(exp_at, own_up, other_up, expert_down, shared_two):
    return pl.pallas_call(
        place_kernel,
        grid_spec=pltpu.PrefetchScalarGridSpec(
            num_scalar_prefetch=1,
            grid=(2,),
            in_specs=[
                whole((HALF, BLOCK, WIDTH + META)),
                whole((HALF, BLOCK, WIDTH + META)),
                whole((LOCAL_E, FF_E, WIDTH)),
                whole((2 * SHARED, WIDTH)),
            ],
            out_specs=[by_core(META), by_step(WIDTH), by_step(FF_E), by_core(META), by_step(META)],
        ),
        out_shape=[
            jax.ShapeDtypeStruct((HALF, 2, BLOCK, META), bf16),
            jax.ShapeDtypeStruct((LOCAL_E, 2, ROWS, WIDTH), bf16),
            jax.ShapeDtypeStruct((LOCAL_E, 2, ROWS, FF_E), f32),
            jax.ShapeDtypeStruct((HALF, 2, BLOCK, META), f32),
            jax.ShapeDtypeStruct((LOCAL_E, 2, ROWS, META), f32),
        ],
        compiler_params=params(56),
        name="place_rows",
    )(exp_at, own_up, other_up, expert_down, shared_two)


def expert_kernel(
    at_ref,
    hid_ref,
    place_ref,
    geh_ref,
    gsh_ref,
    wg_ref,
    wu_ref,
    ws_ref,
    part_ref,
    x_ref,
    act_ref,
    dgu_ref,
    sact_ref,
    sgrad_ref,
):
    for chip in range(HALF):
        rows = dg(place_ref[chip, 0], hid_ref[chip, 0], TN).astype(bf16)
        at = chip * CAP
        for e in range(LOCAL_E):
            x_ref[e, 0, at : at + CAP] = rows[64 * e : 64 * e + CAP]
    pairs = []
    for e in range(LOCAL_E):
        pre_gate = dg(x_ref[e, 0], wg_ref[e], NN)
        pre_up = dg(x_ref[e, 0], wu_ref[e], NN)
        sig = sigmoid(pre_gate)
        act = pre_gate * sig
        act_ref[e, 0] = (act * pre_up).astype(bf16)
        geh = geh_ref[e, 0]
        d_gate = (geh * pre_up * (sig * (1.0 + pre_gate * (1.0 - sig)))).astype(bf16)
        d_up = (geh * act).astype(bf16)
        dgu_ref[e, 0, :, :FF_E] = d_gate
        dgu_ref[e, 0, :, FF_E:] = d_up
        pairs.append((dg(d_gate, wg_ref[e], NT) + dg(d_up, wu_ref[e], NT)).astype(bf16))
    lane = lax.broadcasted_iota(jnp.int32, (BLOCK, 2 * SHARED), 1) < SHARED
    gap = jnp.zeros((64 - CAP, WIDTH), bf16)
    for chip in range(HALF):
        pre = dg(hid_ref[chip, 0], ws_ref[...], NN)
        turned = pltpu.roll(pre, SHARED, 1)
        gate, up = jnp.where(lane, pre, turned), jnp.where(lane, turned, pre)
        sig = sigmoid(gate)
        act = gate * sig
        sact_ref[chip, 0] = jnp.where(lane, act * up, 0.0).astype(bf16)
        slope = sig * (1.0 + gate * (1.0 - sig))
        sgrad = (gsh_ref[chip, 0] * jnp.where(lane, up * slope, act)).astype(bf16)
        sgrad_ref[chip, 0] = sgrad
        at = chip * CAP
        stacked = jnp.concatenate([pairs[0][at : at + CAP], gap, pairs[1][at : at + CAP], gap], 0)
        part_ref[0, chip] = (
            dg(place_ref[chip, 0], stacked, NN) + dg(sgrad, ws_ref[...], NT)
        ).astype(bf16)


def expert_back(exp_at, hidden, place, geh, gsh, wg, wu, ws):
    return pl.pallas_call(
        expert_kernel,
        grid_spec=pltpu.PrefetchScalarGridSpec(
            num_scalar_prefetch=1,
            grid=(2,),
            in_specs=[
                by_core(WIDTH),
                by_core(META),
                by_step(FF_E),
                by_core(META),
                whole((LOCAL_E, WIDTH, FF_E)),
                whole((LOCAL_E, WIDTH, FF_E)),
                whole((WIDTH, 2 * SHARED)),
            ],
            out_specs=[
                pl.BlockSpec((1, HALF, BLOCK, WIDTH), lambda s, at: (s, 0, 0, 0)),
                by_step(WIDTH),
                by_step(FF_E),
                by_step(2 * FF_E),
                by_core(META),
                by_core(META),
            ],
        ),
        out_shape=[
            jax.ShapeDtypeStruct((2, HALF, BLOCK, WIDTH), bf16),
            jax.ShapeDtypeStruct((LOCAL_E, 2, ROWS, WIDTH), bf16),
            jax.ShapeDtypeStruct((LOCAL_E, 2, ROWS, FF_E), bf16),
            jax.ShapeDtypeStruct((LOCAL_E, 2, ROWS, 2 * FF_E), bf16),
            jax.ShapeDtypeStruct((HALF, 2, BLOCK, META), bf16),
            jax.ShapeDtypeStruct((HALF, 2, BLOCK, META), bf16),
        ],
        compiler_params=params(60),
        name="expert_back",
    )(exp_at, hidden, place, geh, gsh, wg, wu, ws)


def output_kernel(at_ref, act_ref, gate_ref, place_ref, sact_ref, wd_ref, sd_ref, part_ref):
    outs = []
    for e in range(LOCAL_E):
        out = dg(act_ref[e, 0], wd_ref[e], NN).astype(bf16).astype(f32)
        outs.append((out * gate_ref[e, 0, :, :1]).astype(bf16))
    gap = jnp.zeros((64 - CAP, WIDTH), bf16)
    for chip in range(HALF):
        at = chip * CAP
        stacked = jnp.concatenate([outs[0][at : at + CAP], gap, outs[1][at : at + CAP], gap], 0)
        part_ref[0, chip] = (
            dg(place_ref[chip, 0], stacked, NN) + dg(sact_ref[chip, 0], sd_ref[...], NN)
        ).astype(bf16)


def expert_output(exp_at, act, gate, place, sact, wd, sd):
    return pl.pallas_call(
        output_kernel,
        grid_spec=pltpu.PrefetchScalarGridSpec(
            num_scalar_prefetch=1,
            grid=(2,),
            in_specs=[
                by_step(FF_E),
                by_step(META),
                by_core(META),
                by_core(META),
                whole((LOCAL_E, FF_E, WIDTH)),
                whole((2 * SHARED, WIDTH)),
            ],
            out_specs=pl.BlockSpec((1, HALF, BLOCK, WIDTH), lambda s, at: (s, 0, 0, 0)),
        ),
        out_shape=jax.ShapeDtypeStruct((2, HALF, BLOCK, WIDTH), bf16),
        compiler_params=params(48),
        name="expert_output",
    )(exp_at, act, gate, place, sact, wd, sd)


def turn_kernel(dq_ref, pieces_ref, ga_ref, gqkv_ref, cols_ref):
    total = pieces_ref[0].astype(f32)
    for i in range(1, N_CTX):
        total = total + pieces_ref[i].astype(f32)
    grad_kv = total.astype(bf16)
    gqkv_ref[:, :WIDTH] = dq_ref[...]
    gqkv_ref[:, WIDTH:] = grad_kv
    turned = jnp.concatenate([dq_ref[...].T, grad_kv.T], axis=0)
    turned_out = ga_ref[...].T
    for j in range(N_EXP):
        cols_ref[j, :160] = turned[160 * j : 160 * j + 160]
        cols_ref[j, 160:] = turned_out[96 * j : 96 * j + 96]


def turn_cols(dq, pieces, grad_attn):
    return pl.pallas_call(
        turn_kernel,
        out_shape=[
            jax.ShapeDtypeStruct((BLOCK, WIDTH + 2 * KV_WIDTH), bf16),
            jax.ShapeDtypeStruct((N_EXP, 256, BLOCK), bf16),
        ],
        compiler_params=params(32),
        name="turn_cols",
    )(dq, pieces, grad_attn)


def input_kernel(gqkv_ref, w_ref, x_ref, gain_ref, gm_ref, out_ref, gg_ref):
    grad_one = dg(gqkv_ref[...], w_ref[...], NT)
    inputs = x_ref[...].astype(f32)
    inv = lax.rsqrt(jnp.mean(inputs * inputs, axis=-1, keepdims=True) + epsilon)
    normed = inputs * inv
    gg_ref[...] = jnp.sum(grad_one * normed, axis=0, keepdims=True)
    out_ref[...] = (gm_ref[...] + norm_back(grad_one * gain_ref[...], normed, inv)).astype(bf16)


def input_back(grad_qkv, w_attn, tokens, gain, grad_middle):
    return pl.pallas_call(
        input_kernel,
        out_shape=[
            jax.ShapeDtypeStruct((BLOCK, WIDTH), bf16),
            jax.ShapeDtypeStruct((1, WIDTH), f32),
        ],
        compiler_params=params(48),
        name="input_back",
    )(grad_qkv, w_attn, tokens, gain, grad_middle)


def cols_kernel(cols_ref, rows_ref, out_ref):
    lhs = jnp.concatenate([cols_ref[j] for j in range(N_EXP)], axis=1)
    row = lax.broadcasted_iota(jnp.int32, (256, N_EXP * BLOCK), 0)
    zero = jnp.zeros_like(lhs)
    attn = dg(jnp.where(row < 160, lhs, zero), rows_ref[:, :WIDTH], NN)
    out = dg(jnp.where(row < 160, zero, lhs), rows_ref[:, WIDTH:], NN)
    out_ref[...] = (attn + out).T.astype(bf16).reshape(N_EXP, 96, 256)


def cols_grad(cols, rows_all):
    return pl.pallas_call(
        cols_kernel,
        out_shape=jax.ShapeDtypeStruct((N_EXP, 96, 256), bf16),
        compiler_params=params(56),
        name="cols_grad",
    )(cols, rows_all)


same_core = [[2 * i + c for i in range(8)] for c in range(2)]
core_swap = [(i, i ^ 1) for i in range(N_EXP)]


def swap_all(rows, axis, groups=None):
    return lax.all_to_all(
        rows, axis, split_axis=0, concat_axis=0, tiled=True, axis_index_groups=groups
    )


def after(value, *others):
    return lax.optimization_barrier((value,) + others)[0]


def add_low(a, b):
    return (a.astype(f32) + b.astype(f32)).astype(bf16)


def on_device(
    tokens,
    routes,
    route_gates,
    norm_attn,
    norm_ffn,
    query_weight,
    key_weight,
    value_weight,
    out_weight,
    shared_gate,
    shared_up,
    shared_down,
    expert_gate,
    expert_up,
    expert_down,
    cotangent,
):
    exp_at = lax.axis_index("exp").astype(jnp.int32)
    ctx_at = lax.axis_index("ctx").astype(jnp.int32)
    chip = exp_at // 2
    exp_s, ctx_s = exp_at.reshape(1), ctx_at.reshape(1)

    heads = [w[:, i * 128 : i * 128 + 128] for i in range(4) for w in (key_weight, value_weight)]
    w_attn = lax.all_gather(
        jnp.concatenate([query_weight] + heads, axis=1), "exp", axis=0, tiled=True
    )
    w_out = lax.all_gather(out_weight, "exp", axis=0, tiled=True)
    gains = jnp.concatenate([norm_attn, norm_ffn])
    gains = swap_all(jnp.broadcast_to(gains, (N_EXP, gains.shape[0])), "exp")
    gain_attn = gains[:, :96].reshape(1, WIDTH).astype(f32)
    gain_ffn = gains[:, 96:].reshape(1, WIDTH).astype(f32)

    gates_high = route_gates[0].astype(bf16)
    gates_low = (route_gates[0] - gates_high.astype(f32)).astype(bf16)
    pad = jnp.zeros((BLOCK, META - 3 * TOPK), bf16)
    up_meta = jnp.concatenate(
        [cotangent[0], routes[0].astype(bf16), gates_high, gates_low, pad], axis=1
    )
    up_pieces = [up_meta] + [
        lax.ppermute(up_meta, "exp", [(i, i ^ (2 * k)) for i in range(N_EXP)]) for k in range(1, 8)
    ]
    shared_cols = jnp.concatenate(
        [shared_gate.reshape(96, N_EXP, SHARED), shared_up.reshape(96, N_EXP, SHARED)], axis=2
    ).transpose(1, 0, 2)
    w_shared = swap_all(shared_cols, "exp").reshape(WIDTH, 2 * SHARED)
    shared_two = jnp.concatenate([shared_down, shared_down], axis=0)

    inputs = tokens[0].astype(f32)
    scale_one = lax.rsqrt(jnp.mean(inputs * inputs, axis=-1, keepdims=True) + epsilon)
    hidden_one = (inputs * scale_one * gain_attn).astype(bf16)
    hidden_one = after(hidden_one, w_shared)
    qkv = dg(hidden_one, w_attn, NN).astype(bf16)
    own_kv = qkv[:, WIDTH:]
    kv_all = swap_all(jnp.broadcast_to(own_kv, (N_CTX,) + own_kv.shape), "ctx")

    up_own = jnp.zeros((HALF,) + up_meta.shape, bf16)
    for k, piece in enumerate(up_pieces):
        up_own = lax.dynamic_update_index_in_dim(up_own, after(piece, own_kv), chip ^ k, 0)
    up_other = lax.ppermute(up_own, "exp", core_swap)

    attended, att_f, logs = attend(ctx_s, qkv, kv_all)
    middle, hidden_two = middle_norm(attended, w_out, tokens[0], gain_ffn)

    hidden_all = lax.all_gather(hidden_two, "exp", axis=0, tiled=True)
    hidden_all = hidden_all.reshape(HALF, 2, BLOCK, WIDTH)
    rows_all = lax.all_gather(
        after(jnp.concatenate([hidden_one, attended], axis=1), hidden_two),
        "exp",
        axis=0,
        tiled=True,
    )
    place, grad_eo, grad_eh, grad_sh, slot_gate = place_rows(
        exp_s, after(up_own, hidden_two), up_other, expert_down, shared_two
    )
    part, arrived, act, grad_gu, shared_act, shared_grad = expert_back(
        exp_s, hidden_all, place, grad_eh, grad_sh, expert_gate, expert_up, w_shared
    )
    summed = add_low(part[1], lax.ppermute(part[0], "exp", core_swap))
    grad_two = swap_all(summed, "exp", same_core)

    rows_e = 2 * ROWS
    act_late = after(act, summed).reshape(LOCAL_E, rows_e, FF_E)
    arrived_late = after(arrived, summed).reshape(LOCAL_E, rows_e, WIDTH)
    shared_grad_late = after(shared_grad, summed).reshape(N_EXP * BLOCK, META)
    grad_scols = dg(hidden_all.reshape(N_EXP * BLOCK, WIDTH), shared_grad_late, TN).astype(bf16)
    grad_scols = swap_all(grad_scols.reshape(N_EXP, 96, META), "exp")
    grad_egu = jnp.einsum(
        "erd,erf->edf",
        arrived_late,
        grad_gu.reshape(LOCAL_E, rows_e, 2 * FF_E),
        preferred_element_type=f32,
    ).astype(bf16)
    grad_edown = jnp.einsum(
        "erf,erd->efd",
        act_late,
        grad_eo.reshape(LOCAL_E, rows_e, WIDTH),
        preferred_element_type=f32,
    ).astype(bf16)
    core = exp_at % 2
    act_pair = shared_act.reshape(HALF, 2, BLOCK, META)
    act_own = lax.dynamic_index_in_dim(act_pair, core, 1, keepdims=False)
    act_other = lax.dynamic_index_in_dim(act_pair, 1 - core, 1, keepdims=False)
    flat = (HALF * BLOCK, -1)
    grad_sdown = (
        dg(act_own.reshape(flat), up_own.reshape(flat), TN)
        + dg(act_other.reshape(flat), up_other.reshape(flat), TN)
    )[:SHARED, :WIDTH].astype(bf16)
    grad_egu, grad_edown, grad_sdown, grad_scols = lax.psum(
        (grad_egu, grad_edown, grad_sdown, grad_scols), "ctx"
    )

    grad_middle, grad_attn, grad_heads, grad_gain_ffn = middle_back(
        grad_two, middle, cotangent[0], gain_ffn, w_out
    )
    grad_query, part_kv = attend_back(ctx_s, qkv, grad_heads, att_f, logs, kv_all)
    kv_pieces = swap_all(part_kv, "ctx")

    out_part = expert_output(
        exp_s, after(act, part_kv), slot_gate, place, shared_act, expert_down, shared_two
    )
    out_sum = add_low(out_part[1], lax.ppermute(out_part[0], "exp", core_swap))

    grad_qkv, cols = turn_cols(grad_query, kv_pieces, grad_attn)
    cols = swap_all(cols, "exp")
    input_grad, grad_gain_attn = input_back(
        grad_qkv, w_attn, tokens[0], gain_attn, grad_middle
    )
    grad_cols = cols_grad(cols, rows_all)
    gain_rows = jnp.concatenate(
        [grad_gain_attn.reshape(N_EXP, 1, 96), grad_gain_ffn.reshape(N_EXP, 1, 96)], axis=1
    ).astype(bf16)
    gain_rows = jnp.pad(gain_rows, ((0, 0), (0, 14), (0, 160)))
    back = swap_all(jnp.concatenate([grad_cols, gain_rows], axis=1), "exp")
    pieces = swap_all(back.reshape(N_CTX, 2, 112, 256), "ctx")
    own = jnp.sum(pieces.astype(f32), axis=0).astype(bf16)
    late = swap_all(jnp.broadcast_to(own, (N_CTX, 2, 112, 256)), "ctx").reshape(N_EXP, 112, 256)

    out_pieces = swap_all(after(out_sum, cols), "exp", same_core)
    mixed = (middle + jnp.sum(out_pieces.astype(f32), axis=0)).astype(bf16)[None]

    grad_wqkv = late[:, :96, :160].transpose(1, 0, 2).reshape(96, WIDTH + 2 * KV_WIDTH)
    grad_wkv = grad_wqkv[:, WIDTH:].reshape(96, KV_HEADS, 2, HEAD_DIM)
    gain_sum = jnp.sum(late[:, 96:98, :96].astype(f32), axis=0)
    return (
        mixed,
        input_grad[None],
        gain_sum[0],
        gain_sum[1],
        grad_wqkv[:, :WIDTH].astype(f32),
        grad_wkv[:, :, 0].reshape(96, KV_WIDTH).astype(f32),
        grad_wkv[:, :, 1].reshape(96, KV_WIDTH).astype(f32),
        late[:, :96, 160:].transpose(1, 0, 2).reshape(96, WIDTH).astype(f32),
        grad_scols[:, :, :SHARED].transpose(1, 0, 2).reshape(96, 1024).astype(f32),
        grad_scols[:, :, SHARED:].transpose(1, 0, 2).reshape(96, 1024).astype(f32),
        grad_sdown.astype(f32),
        grad_egu[:, :, :FF_E].astype(f32),
        grad_egu[:, :, FF_E:].astype(f32),
        grad_edown.astype(f32),
    )


def solution(mesh):
    token_spec = P("exp", "ctx", None)
    rows = P("exp", None)
    expert = P("exp", None, None)
    placed = (token_spec,) * 3 + (P("exp"),) * 2 + (rows,) * 7 + (expert,) * 3 + (token_spec,)
    return jax.shard_map(
        on_device,
        mesh=mesh,
        in_specs=placed,
        out_specs=(token_spec,) * 2 + (P("exp"),) * 2 + (rows,) * 7 + (expert,) * 3,
        check_vma=False,
    )
```

```python
import jax
import jax.numpy as jnp
from jax import lax
from jax.sharding import PartitionSpec as P
from jax.experimental import pallas as pl
from jax.experimental.pallas import tpu as pltpu

HEADS = 12
KV_HEADS = 4
HEAD_DIM = 128
TOPK = 6
GROUP = 3
BLOCK = 128
WIDTH = 1536
KV_WIDTH = KV_HEADS * HEAD_DIM
CAP = 48
N_EXP = 16
N_CTX = 8
LOCAL_E = 2
FF_E = 512
SHARED = 64
META = 128
HALF = 8
ROWS = HALF * CAP

epsilon = 1e-05
masked_score = -1e30
f32 = jnp.float32
bf16 = jnp.bfloat16
log2_e = 1.4426950408889634
score_scale = HEAD_DIM ** (-0.5) * log2_e

NN = (((1,), (0,)), ((), ()))
NT = (((1,), (1,)), ((), ()))
TN = (((0,), (0,)), ((), ()))


def dg(a, b, dims):
    return lax.dot_general(a, b, dims, preferred_element_type=f32)


def params(mib):
    return pltpu.CompilerParams(vmem_limit_bytes=mib * 1024 * 1024)


def whole(shape):
    return pl.BlockSpec(shape, lambda *_: (0,) * len(shape), pipeline_mode=pl.Buffered(1))


def sigmoid(v):
    return 1.0 / (1.0 + jnp.exp(-v))


def allowed_scores(ctx_at):
    rows = lax.broadcasted_iota(jnp.int32, (GROUP * BLOCK, N_CTX * BLOCK), 0) % BLOCK
    cols = lax.broadcasted_iota(jnp.int32, (GROUP * BLOCK, N_CTX * BLOCK), 1)
    return rows + ctx_at * BLOCK >= cols


def stack_heads(block):
    return jnp.concatenate([block[:, j * HEAD_DIM : (j + 1) * HEAD_DIM] for j in range(GROUP)], axis=0)


def unstack_heads(rows):
    return jnp.concatenate([rows[j * BLOCK : (j + 1) * BLOCK] for j in range(GROUP)], axis=1)


def attend_kernel(ctx_ref, q_ref, k_ref, v_ref, att_ref, attf_ref, log_ref):
    q = stack_heads(q_ref[...])
    keys = k_ref[...].reshape(N_CTX * BLOCK, HEAD_DIM)
    values = v_ref[...].reshape(N_CTX * BLOCK, HEAD_DIM)
    scores = jnp.where(allowed_scores(ctx_ref[0]), dg(q, keys, NT) * score_scale, masked_score)
    top = jnp.max(scores, axis=-1, keepdims=True)
    weights = jnp.exp2(scores - top)
    total = jnp.sum(weights, axis=-1, keepdims=True)
    out = dg(weights.astype(bf16), values, NN) * (1.0 / total)
    out = unstack_heads(out)
    attf_ref[...] = out
    att_ref[...] = out.astype(bf16)
    log_ref[...] = jnp.broadcast_to(top + jnp.log2(total), (GROUP * BLOCK, HEAD_DIM))


def kv_specs():
    return [
        pl.BlockSpec((N_CTX, BLOCK, HEAD_DIM), lambda g: (0, 0, g)),
        pl.BlockSpec((N_CTX, BLOCK, HEAD_DIM), lambda g: (0, 0, KV_HEADS + g)),
    ]


def head_spec():
    return pl.BlockSpec((BLOCK, GROUP * HEAD_DIM), lambda g: (0, g))


def attend(ctx_at, qkv, kv_all):
    return pl.pallas_call(
        attend_kernel,
        grid=(KV_HEADS,),
        in_specs=[pl.BlockSpec(memory_space=pltpu.SMEM), head_spec()] + kv_specs(),
        out_specs=[
            head_spec(),
            head_spec(),
            pl.BlockSpec((GROUP * BLOCK, HEAD_DIM), lambda g: (g, 0)),
        ],
        out_shape=[
            jax.ShapeDtypeStruct((BLOCK, WIDTH), bf16),
            jax.ShapeDtypeStruct((BLOCK, WIDTH), f32),
            jax.ShapeDtypeStruct((HEADS * BLOCK, HEAD_DIM), f32),
        ],
        compiler_params=params(48),
        name="attend",
    )(ctx_at, qkv, kv_all, kv_all)


def attend_back_kernel(
    ctx_ref, q_ref, ga_ref, attf_ref, log_ref, k_ref, v_ref, dq_ref, dkv_ref
):
    q = stack_heads(q_ref[...])
    grad = stack_heads(ga_ref[...])
    delta = jnp.sum(grad.astype(f32) * stack_heads(attf_ref[...]), axis=-1, keepdims=True)
    keys = k_ref[...].reshape(N_CTX * BLOCK, HEAD_DIM)
    values = v_ref[...].reshape(N_CTX * BLOCK, HEAD_DIM)
    scores = jnp.where(allowed_scores(ctx_ref[0]), dg(q, keys, NT) * score_scale, masked_score)
    weights = jnp.exp2(scores - log_ref[:, :1])
    grad_weights = dg(grad, values, NT)
    grad_raw = (weights * (grad_weights - delta)).astype(bf16)
    scale = HEAD_DIM ** (-0.5)
    dq_ref[...] = unstack_heads(dg(grad_raw, keys, NN) * scale).astype(bf16)
    grad_k = (dg(grad_raw, q, TN) * scale).astype(bf16)
    grad_v = dg(weights.astype(bf16), grad, TN).astype(bf16)
    dkv_ref[:, :, :HEAD_DIM] = grad_k.reshape(N_CTX, BLOCK, HEAD_DIM)
    dkv_ref[:, :, HEAD_DIM:] = grad_v.reshape(N_CTX, BLOCK, HEAD_DIM)


def attend_back(ctx_at, qkv, grad_att, att_f, logs, kv_all):
    part = pl.BlockSpec((N_CTX, BLOCK, 2 * HEAD_DIM), lambda g: (0, 0, g))
    return pl.pallas_call(
        attend_back_kernel,
        grid=(KV_HEADS,),
        in_specs=[
            pl.BlockSpec(memory_space=pltpu.SMEM),
            head_spec(),
            head_spec(),
            head_spec(),
            pl.BlockSpec((GROUP * BLOCK, HEAD_DIM), lambda g: (g, 0)),
        ]
        + kv_specs(),
        out_specs=[head_spec(), part],
        out_shape=[
            jax.ShapeDtypeStruct((BLOCK, WIDTH), bf16),
            jax.ShapeDtypeStruct((N_CTX, BLOCK, 2 * KV_WIDTH), bf16),
        ],
        compiler_params=params(48),
        name="attend_back",
    )(ctx_at, qkv, grad_att, att_f, logs, kv_all, kv_all)


def middle_kernel(att_ref, w_ref, x_ref, gain_ref, middle_ref, hidden_ref):
    middle = x_ref[...].astype(f32) + dg(att_ref[...], w_ref[...], NN)
    inv = lax.rsqrt(jnp.mean(middle * middle, axis=-1, keepdims=True) + epsilon)
    middle_ref[...] = middle
    hidden_ref[...] = (middle * inv * gain_ref[...]).astype(bf16)


def w_cols(width, at):
    return pl.BlockSpec((WIDTH, width), lambda *_: (0, at), pipeline_mode=pl.Buffered(1))


def middle_norm(attended, w_all, tokens, gain):
    return pl.pallas_call(
        middle_kernel,
        grid=(1,),
        in_specs=[
            whole((BLOCK, WIDTH)),
            w_cols(WIDTH, 1),
            whole((BLOCK, WIDTH)),
            whole((1, WIDTH)),
        ],
        out_specs=[whole((BLOCK, WIDTH)), whole((BLOCK, WIDTH))],
        out_shape=[
            jax.ShapeDtypeStruct((BLOCK, WIDTH), f32),
            jax.ShapeDtypeStruct((BLOCK, WIDTH), bf16),
        ],
        compiler_params=params(32),
        name="middle_norm",
    )(attended, w_all, tokens, gain)


def norm_back(grad_normed, normed, inv_root):
    return inv_root * (
        grad_normed - normed * jnp.mean(grad_normed * normed, axis=-1, keepdims=True)
    )


def middle_back_kernel(
    pieces_ref, middle_ref, up_ref, gain_ref, w_ref, gm_ref, ga_ref, gh_ref, gg_ref
):
    grad_two = pieces_ref[0].astype(f32)
    for i in range(1, HALF):
        grad_two = grad_two + pieces_ref[i].astype(f32)
    middle = middle_ref[...]
    inv = lax.rsqrt(jnp.mean(middle * middle, axis=-1, keepdims=True) + epsilon)
    normed = middle * inv
    gg_ref[...] = jnp.sum(grad_two * normed, axis=0, keepdims=True)
    grad_middle = up_ref[...].astype(f32) + norm_back(grad_two * gain_ref[...], normed, inv)
    gm_ref[...] = grad_middle
    grad_attn = grad_middle.astype(bf16)
    ga_ref[...] = grad_attn
    gh_ref[...] = dg(grad_attn, w_ref[...], NT).astype(bf16)


def middle_back(pieces, middle, upstream, gain, w_all):
    return pl.pallas_call(
        middle_back_kernel,
        grid=(1,),
        in_specs=[
            whole((HALF, BLOCK, WIDTH)),
            whole((BLOCK, WIDTH)),
            whole((BLOCK, WIDTH)),
            whole((1, WIDTH)),
            w_cols(WIDTH, 1),
        ],
        out_specs=[whole((BLOCK, WIDTH))] * 3 + [whole((1, WIDTH))],
        out_shape=[
            jax.ShapeDtypeStruct((BLOCK, WIDTH), f32),
            jax.ShapeDtypeStruct((BLOCK, WIDTH), bf16),
            jax.ShapeDtypeStruct((BLOCK, WIDTH), bf16),
            jax.ShapeDtypeStruct((1, WIDTH), f32),
        ],
        compiler_params=params(48),
        name="middle_back",
    )(pieces, middle, upstream, gain, w_all)


def place_kernel(
    at_ref, own_ref, other_ref, down_ref, sdown_ref, place_ref, geo_ref, geh_ref, gsh_ref, gate_ref
):
    step = pl.program_id(0)
    lane = lax.broadcasted_iota(jnp.int32, (BLOCK, META), 1)
    row = lax.broadcasted_iota(jnp.int32, (BLOCK, META), 0)
    before = (row > lane).astype(bf16)
    slot = (lane % 64).astype(f32)
    first_id = (at_ref[0] * LOCAL_E).astype(f32)
    row_id = first_id + (row >= 64).astype(f32)

    def run(up_ref):
        for chip in range(HALF):
            meta = up_ref[chip, :, WIDTH:].astype(f32)
            named = lane < TOPK
            zero = jnp.zeros((BLOCK, META), f32)
            hit0 = jnp.where(named & (meta == first_id), 1.0, zero)
            hit1 = jnp.where(named & (meta == first_id + 1.0), 1.0, zero)
            mask = jnp.where(
                lane < 64,
                jnp.sum(hit0, axis=1, keepdims=True),
                jnp.sum(hit1, axis=1, keepdims=True),
            )
            rank = dg(before, mask.astype(bf16), NN)
            place = jnp.where((mask > 0.5) & (rank == slot), 1.0, zero).astype(bf16)
            place_ref[chip, 0] = place
            rows = dg(place, up_ref[chip], TN)
            slot_meta = rows[:, WIDTH:]
            gates = pltpu.roll(slot_meta, META - TOPK, 1) + pltpu.roll(
                slot_meta, META - 2 * TOPK, 1
            )
            gate = jnp.sum(
                jnp.where(named & (slot_meta == row_id), gates, zero), axis=1, keepdims=True
            )
            geo = (gate * rows[:, :WIDTH]).astype(bf16)
            wide_gate = jnp.broadcast_to(gate, (BLOCK, META))
            at = chip * CAP
            for e in range(LOCAL_E):
                geo_ref[e, 0, at : at + CAP] = geo[64 * e : 64 * e + CAP]
                gate_ref[e, 0, at : at + CAP] = wide_gate[64 * e : 64 * e + CAP]
            gsh_ref[chip, 0] = dg(up_ref[chip, :, :WIDTH], sdown_ref[...], NT)
        for e in range(LOCAL_E):
            geh_ref[e, 0] = dg(geo_ref[e, 0], down_ref[e], NT)

    @pl.when(step == 0)
    def _():
        run(other_ref)

    @pl.when(step == 1)
    def _():
        run(own_ref)


def by_core(cols):
    return pl.BlockSpec(
        (HALF, 1, BLOCK, cols),
        lambda s, at: (0, jnp.where(s == 0, 1 - at[0] % 2, at[0] % 2), 0, 0),
    )


def by_step(cols):
    return pl.BlockSpec((LOCAL_E, 1, ROWS, cols), lambda s, at: (0, s, 0, 0))


def place_rows(exp_at, own_up, other_up, expert_down, shared_two):
    return pl.pallas_call(
        place_kernel,
        grid_spec=pltpu.PrefetchScalarGridSpec(
            num_scalar_prefetch=1,
            grid=(2,),
            in_specs=[
                whole((HALF, BLOCK, WIDTH + META)),
                whole((HALF, BLOCK, WIDTH + META)),
                whole((LOCAL_E, FF_E, WIDTH)),
                whole((2 * SHARED, WIDTH)),
            ],
            out_specs=[by_core(META), by_step(WIDTH), by_step(FF_E), by_core(META), by_step(META)],
        ),
        out_shape=[
            jax.ShapeDtypeStruct((HALF, 2, BLOCK, META), bf16),
            jax.ShapeDtypeStruct((LOCAL_E, 2, ROWS, WIDTH), bf16),
            jax.ShapeDtypeStruct((LOCAL_E, 2, ROWS, FF_E), f32),
            jax.ShapeDtypeStruct((HALF, 2, BLOCK, META), f32),
            jax.ShapeDtypeStruct((LOCAL_E, 2, ROWS, META), f32),
        ],
        compiler_params=params(56),
        name="place_rows",
    )(exp_at, own_up, other_up, expert_down, shared_two)


def expert_kernel(
    at_ref,
    hid_ref,
    place_ref,
    geh_ref,
    gsh_ref,
    wg_ref,
    wu_ref,
    ws_ref,
    part_ref,
    x_ref,
    act_ref,
    dgu_ref,
    sact_ref,
    sgrad_ref,
):
    for chip in range(HALF):
        rows = dg(place_ref[chip, 0], hid_ref[chip, 0], TN).astype(bf16)
        at = chip * CAP
        for e in range(LOCAL_E):
            x_ref[e, 0, at : at + CAP] = rows[64 * e : 64 * e + CAP]
    pairs = []
    for e in range(LOCAL_E):
        pre_gate = dg(x_ref[e, 0], wg_ref[e], NN)
        pre_up = dg(x_ref[e, 0], wu_ref[e], NN)
        sig = sigmoid(pre_gate)
        act = pre_gate * sig
        act_ref[e, 0] = (act * pre_up).astype(bf16)
        geh = geh_ref[e, 0]
        d_gate = (geh * pre_up * (sig * (1.0 + pre_gate * (1.0 - sig)))).astype(bf16)
        d_up = (geh * act).astype(bf16)
        dgu_ref[e, 0, :, :FF_E] = d_gate
        dgu_ref[e, 0, :, FF_E:] = d_up
        pairs.append((dg(d_gate, wg_ref[e], NT) + dg(d_up, wu_ref[e], NT)).astype(bf16))
    lane = lax.broadcasted_iota(jnp.int32, (BLOCK, 2 * SHARED), 1) < SHARED
    gap = jnp.zeros((64 - CAP, WIDTH), bf16)
    for chip in range(HALF):
        pre = dg(hid_ref[chip, 0], ws_ref[...], NN)
        turned = pltpu.roll(pre, SHARED, 1)
        gate, up = jnp.where(lane, pre, turned), jnp.where(lane, turned, pre)
        sig = sigmoid(gate)
        act = gate * sig
        sact_ref[chip, 0] = jnp.where(lane, act * up, 0.0).astype(bf16)
        slope = sig * (1.0 + gate * (1.0 - sig))
        sgrad = (gsh_ref[chip, 0] * jnp.where(lane, up * slope, act)).astype(bf16)
        sgrad_ref[chip, 0] = sgrad
        at = chip * CAP
        stacked = jnp.concatenate([pairs[0][at : at + CAP], gap, pairs[1][at : at + CAP], gap], 0)
        part_ref[0, chip] = (
            dg(place_ref[chip, 0], stacked, NN) + dg(sgrad, ws_ref[...], NT)
        ).astype(bf16)


def expert_back(exp_at, hidden, place, geh, gsh, wg, wu, ws):
    return pl.pallas_call(
        expert_kernel,
        grid_spec=pltpu.PrefetchScalarGridSpec(
            num_scalar_prefetch=1,
            grid=(2,),
            in_specs=[
                by_core(WIDTH),
                by_core(META),
                by_step(FF_E),
                by_core(META),
                whole((LOCAL_E, WIDTH, FF_E)),
                whole((LOCAL_E, WIDTH, FF_E)),
                whole((WIDTH, 2 * SHARED)),
            ],
            out_specs=[
                pl.BlockSpec((1, HALF, BLOCK, WIDTH), lambda s, at: (s, 0, 0, 0)),
                by_step(WIDTH),
                by_step(FF_E),
                by_step(2 * FF_E),
                by_core(META),
                by_core(META),
            ],
        ),
        out_shape=[
            jax.ShapeDtypeStruct((2, HALF, BLOCK, WIDTH), bf16),
            jax.ShapeDtypeStruct((LOCAL_E, 2, ROWS, WIDTH), bf16),
            jax.ShapeDtypeStruct((LOCAL_E, 2, ROWS, FF_E), bf16),
            jax.ShapeDtypeStruct((LOCAL_E, 2, ROWS, 2 * FF_E), bf16),
            jax.ShapeDtypeStruct((HALF, 2, BLOCK, META), bf16),
            jax.ShapeDtypeStruct((HALF, 2, BLOCK, META), bf16),
        ],
        compiler_params=params(60),
        name="expert_back",
    )(exp_at, hidden, place, geh, gsh, wg, wu, ws)


def output_kernel(at_ref, act_ref, gate_ref, place_ref, sact_ref, wd_ref, sd_ref, part_ref):
    outs = []
    for e in range(LOCAL_E):
        out = dg(act_ref[e, 0], wd_ref[e], NN).astype(bf16).astype(f32)
        outs.append((out * gate_ref[e, 0, :, :1]).astype(bf16))
    gap = jnp.zeros((64 - CAP, WIDTH), bf16)
    for chip in range(HALF):
        at = chip * CAP
        stacked = jnp.concatenate([outs[0][at : at + CAP], gap, outs[1][at : at + CAP], gap], 0)
        part_ref[0, chip] = (
            dg(place_ref[chip, 0], stacked, NN) + dg(sact_ref[chip, 0], sd_ref[...], NN)
        ).astype(bf16)


def expert_output(exp_at, act, gate, place, sact, wd, sd):
    return pl.pallas_call(
        output_kernel,
        grid_spec=pltpu.PrefetchScalarGridSpec(
            num_scalar_prefetch=1,
            grid=(2,),
            in_specs=[
                by_step(FF_E),
                by_step(META),
                by_core(META),
                by_core(META),
                whole((LOCAL_E, FF_E, WIDTH)),
                whole((2 * SHARED, WIDTH)),
            ],
            out_specs=pl.BlockSpec((1, HALF, BLOCK, WIDTH), lambda s, at: (s, 0, 0, 0)),
        ),
        out_shape=jax.ShapeDtypeStruct((2, HALF, BLOCK, WIDTH), bf16),
        compiler_params=params(48),
        name="expert_output",
    )(exp_at, act, gate, place, sact, wd, sd)


def turn_kernel(dq_ref, pieces_ref, ga_ref, gqkv_ref, cols_ref):
    total = pieces_ref[0].astype(f32)
    for i in range(1, N_CTX):
        total = total + pieces_ref[i].astype(f32)
    total = total.astype(bf16)
    parts = [total[:, i * HEAD_DIM : (i + 1) * HEAD_DIM] for i in range(2 * KV_HEADS)]
    grad_kv = jnp.concatenate(parts[0::2] + parts[1::2], axis=1)
    gqkv_ref[:, :WIDTH] = dq_ref[...]
    gqkv_ref[:, WIDTH:] = grad_kv
    turned = jnp.concatenate([dq_ref[...].T, grad_kv.T], axis=0)
    turned_out = ga_ref[...].T
    for j in range(N_EXP):
        cols_ref[j, :160] = turned[160 * j : 160 * j + 160]
        cols_ref[j, 160:] = turned_out[96 * j : 96 * j + 96]


def turn_cols(dq, pieces, grad_attn):
    return pl.pallas_call(
        turn_kernel,
        out_shape=[
            jax.ShapeDtypeStruct((BLOCK, WIDTH + 2 * KV_WIDTH), bf16),
            jax.ShapeDtypeStruct((N_EXP, 256, BLOCK), bf16),
        ],
        compiler_params=params(32),
        name="turn_cols",
    )(dq, pieces, grad_attn)


def input_kernel(gqkv_ref, wq_ref, wkv_ref, x_ref, gain_ref, gm_ref, out_ref, gg_ref):
    grad_one = dg(gqkv_ref[:, :WIDTH], wq_ref[...], NT) + dg(gqkv_ref[:, WIDTH:], wkv_ref[...], NT)
    inputs = x_ref[...].astype(f32)
    inv = lax.rsqrt(jnp.mean(inputs * inputs, axis=-1, keepdims=True) + epsilon)
    normed = inputs * inv
    gg_ref[...] = jnp.sum(grad_one * normed, axis=0, keepdims=True)
    out_ref[...] = (gm_ref[...] + norm_back(grad_one * gain_ref[...], normed, inv)).astype(bf16)


def input_back(grad_qkv, w_all, tokens, gain, grad_middle):
    return pl.pallas_call(
        input_kernel,
        grid=(1,),
        in_specs=[
            whole((BLOCK, WIDTH + 2 * KV_WIDTH)),
            w_cols(WIDTH, 0),
            w_cols(2 * KV_WIDTH, 3),
            whole((BLOCK, WIDTH)),
            whole((1, WIDTH)),
            whole((BLOCK, WIDTH)),
        ],
        out_specs=[whole((BLOCK, WIDTH)), whole((1, WIDTH))],
        out_shape=[
            jax.ShapeDtypeStruct((BLOCK, WIDTH), bf16),
            jax.ShapeDtypeStruct((1, WIDTH), f32),
        ],
        compiler_params=params(48),
        name="input_back",
    )(grad_qkv, w_all, w_all, tokens, gain, grad_middle)


def cols_kernel(cols_ref, rows_ref, out_ref):
    lhs = jnp.concatenate([cols_ref[j] for j in range(N_EXP)], axis=1)
    row = lax.broadcasted_iota(jnp.int32, (256, N_EXP * BLOCK), 0)
    zero = jnp.zeros_like(lhs)
    attn = dg(jnp.where(row < 160, lhs, zero), rows_ref[:, :WIDTH], NN)
    out = dg(jnp.where(row < 160, zero, lhs), rows_ref[:, WIDTH:], NN)
    out_ref[...] = (attn + out).T.astype(bf16).reshape(N_EXP, 96, 256)


def cols_grad(cols, rows_all):
    return pl.pallas_call(
        cols_kernel,
        out_shape=jax.ShapeDtypeStruct((N_EXP, 96, 256), bf16),
        compiler_params=params(56),
        name="cols_grad",
    )(cols, rows_all)


def norm_rows_kernel(x_ref, gain_ref, out_ref):
    inputs = x_ref[0].astype(f32)
    inv = lax.rsqrt(jnp.mean(inputs * inputs, axis=-1, keepdims=True) + epsilon)
    out_ref[0] = (inputs * inv * gain_ref[...]).astype(bf16)


def norm_rows(rows, gain):
    count = rows.shape[0]
    spec = pl.BlockSpec((1, BLOCK, WIDTH), lambda i: (i, 0, 0))
    return pl.pallas_call(
        norm_rows_kernel,
        grid=(count,),
        in_specs=[spec, whole((1, WIDTH))],
        out_specs=spec,
        out_shape=jax.ShapeDtypeStruct(rows.shape, bf16),
        compiler_params=params(32),
        name="norm_rows",
    )(rows, gain)


def project_kernel(own_ref, seq_ref, w_ref, q_ref, kv_ref):
    step = pl.program_id(0)

    @pl.when(step < 3)
    def _():
        q_ref[...] = dg(own_ref[0], w_ref[...], NN).astype(bf16)

    @pl.when(step >= 3)
    def _():
        rows = seq_ref[...].reshape(N_CTX * BLOCK, WIDTH)
        kv_ref[...] = dg(rows, w_ref[...], NN).astype(bf16).reshape(N_CTX, BLOCK, KV_WIDTH)


def project(own, seq, w_all):
    return pl.pallas_call(
        project_kernel,
        grid=(5,),
        in_specs=[
            whole((1, BLOCK, WIDTH)),
            whole((N_CTX, BLOCK, WIDTH)),
            pl.BlockSpec((WIDTH, KV_WIDTH), lambda i: (0, jnp.where(i < 3, i, i + 3))),
        ],
        out_specs=[
            pl.BlockSpec((BLOCK, KV_WIDTH), lambda i: (0, jnp.minimum(i, 2))),
            pl.BlockSpec((N_CTX, BLOCK, KV_WIDTH), lambda i: (0, 0, jnp.maximum(i - 3, 0))),
        ],
        out_shape=[
            jax.ShapeDtypeStruct((BLOCK, WIDTH), bf16),
            jax.ShapeDtypeStruct((N_CTX, BLOCK, 2 * KV_WIDTH), bf16),
        ],
        compiler_params=params(48),
        name="project",
    )(own, seq, w_all)


PIECE = 2 * WIDTH + WIDTH * BLOCK // HEAD_DIM


def expert_weights_kernel(at_ref, x_ref, geo_ref, act_ref, dgate_ref, dup_ref, *refs):
    outs, turned = refs[:8], refs[8]
    step = pl.program_id(0)

    @pl.when(step == 0)
    def _():
        for e in range(LOCAL_E):
            turned[e] = x_ref[e].T

    for r in range(4):

        @pl.when(step == r)
        def _():
            for side in range(2):
                e = at_ref[1] if side == 0 else 1 - at_ref[1]
                out = outs[2 * r + side]
                rhs = jnp.concatenate([dgate_ref[e], dup_ref[e]], axis=1)
                both = dg(turned[e], rhs, NN).astype(bf16)
                out[:WIDTH] = both[:, :HEAD_DIM]
                out[WIDTH : 2 * WIDTH] = both[:, HEAD_DIM:]
                down = dg(act_ref[e], geo_ref[e], TN).astype(bf16)
                for m in range(WIDTH // HEAD_DIM):
                    at = 2 * WIDTH + m * BLOCK
                    out[at : at + BLOCK] = down[:, m * HEAD_DIM : (m + 1) * HEAD_DIM]


def expert_weights(at, arrived, grad_eo, act, grad_gu):
    rows = 2 * ROWS
    lanes = lambda shift: pl.BlockSpec(
        (LOCAL_E, rows, HEAD_DIM), lambda r, at: (0, 0, shift + (at[0] ^ r))
    )
    piece = jax.ShapeDtypeStruct((PIECE, HEAD_DIM), bf16)
    return pl.pallas_call(
        expert_weights_kernel,
        grid_spec=pltpu.PrefetchScalarGridSpec(
            num_scalar_prefetch=1,
            grid=(4,),
            in_specs=[
                whole((LOCAL_E, rows, WIDTH)),
                whole((LOCAL_E, rows, WIDTH)),
                lanes(0),
                lanes(0),
                lanes(4),
            ],
            out_specs=[whole((PIECE, HEAD_DIM))] * 8,
            scratch_shapes=[pltpu.VMEM((LOCAL_E, WIDTH, rows), bf16)],
        ),
        out_shape=[piece] * 8,
        compiler_params=params(56),
        name="expert_weights",
    )(at, arrived, grad_eo, act, grad_gu, grad_gu)


def unpack_kernel(at_ref, *refs):
    pieces, (gate_ref, up_ref, down_ref) = refs[:8], refs[8:]
    step = pl.program_id(0)
    for i in range(8):

        @pl.when(step == i)
        def _():
            piece = pieces[i]
            gate_ref[0] = piece[:WIDTH].astype(f32)
            up_ref[0] = piece[WIDTH : 2 * WIDTH].astype(f32)
            for m in range(WIDTH // HEAD_DIM):
                at = 2 * WIDTH + m * BLOCK
                down_ref[0, :, m * HEAD_DIM : (m + 1) * HEAD_DIM] = piece[at : at + BLOCK].astype(
                    f32
                )


def unpack_experts(at, pieces):
    cols = pl.BlockSpec(
        (1, WIDTH, HEAD_DIM), lambda s, at: (at[1] ^ (s // 4), 0, at[0] ^ (s % 4))
    )
    return pl.pallas_call(
        unpack_kernel,
        grid_spec=pltpu.PrefetchScalarGridSpec(
            num_scalar_prefetch=1,
            grid=(8,),
            in_specs=[whole((PIECE, HEAD_DIM))] * 8,
            out_specs=[
                cols,
                cols,
                pl.BlockSpec(
                    (1, BLOCK, WIDTH), lambda s, at: (at[1] ^ (s // 4), at[0] ^ (s % 4), 0)
                ),
            ],
        ),
        out_shape=[
            jax.ShapeDtypeStruct((LOCAL_E, WIDTH, FF_E), f32),
            jax.ShapeDtypeStruct((LOCAL_E, WIDTH, FF_E), f32),
            jax.ShapeDtypeStruct((LOCAL_E, FF_E, WIDTH), f32),
        ],
        compiler_params=params(48),
        name="unpack_experts",
    )(at, *pieces)


same_core = [[2 * i + c for i in range(8)] for c in range(2)]
core_swap = [(i, i ^ 1) for i in range(N_EXP)]


def swap_all(rows, axis, groups=None):
    return lax.all_to_all(
        rows, axis, split_axis=0, concat_axis=0, tiled=True, axis_index_groups=groups
    )


def after(value, *others):
    return lax.optimization_barrier((value,) + others)[0]


def add_low(a, b):
    return (a.astype(f32) + b.astype(f32)).astype(bf16)


def on_device(
    tokens,
    routes,
    route_gates,
    norm_attn,
    norm_ffn,
    query_weight,
    key_weight,
    value_weight,
    out_weight,
    shared_gate,
    shared_up,
    shared_down,
    expert_gate,
    expert_up,
    expert_down,
    cotangent,
):
    exp_at = lax.axis_index("exp").astype(jnp.int32)
    ctx_at = lax.axis_index("ctx").astype(jnp.int32)
    chip = exp_at // 2
    exp_s, ctx_s = exp_at.reshape(1), ctx_at.reshape(1)

    y_at, z_at = ctx_at % 4, ctx_at // 4
    yz_s = jnp.stack([y_at, z_at])

    w_all = lax.all_gather(
        jnp.concatenate([query_weight, out_weight, key_weight, value_weight], axis=1),
        "exp",
        axis=0,
        tiled=True,
    )
    gates_high = route_gates[0].astype(bf16)
    gates_low = (route_gates[0] - gates_high.astype(f32)).astype(bf16)
    pad = jnp.zeros((BLOCK, META - 3 * TOPK), bf16)
    up_meta = jnp.concatenate(
        [cotangent[0], routes[0].astype(bf16), gates_high, gates_low, pad], axis=1
    )
    up_pieces = [up_meta] + [
        lax.ppermute(up_meta, "exp", [(i, i ^ (2 * k)) for i in range(N_EXP)]) for k in range(1, 8)
    ]
    gains = jnp.concatenate([norm_attn, norm_ffn])
    gains = swap_all(jnp.broadcast_to(gains, (N_EXP, gains.shape[0])), "exp")
    gain_attn = gains[:, :96].reshape(1, WIDTH).astype(f32)
    gain_ffn = gains[:, 96:].reshape(1, WIDTH).astype(f32)
    tokens_seq = swap_all(jnp.broadcast_to(tokens, (N_CTX, BLOCK, WIDTH)), "ctx")
    shared_cols = jnp.concatenate(
        [shared_gate.reshape(96, N_EXP, SHARED), shared_up.reshape(96, N_EXP, SHARED)], axis=2
    ).transpose(1, 0, 2)
    w_shared = swap_all(shared_cols, "exp").reshape(WIDTH, 2 * SHARED)
    shared_two = jnp.concatenate([shared_down, shared_down], axis=0)
    up_own = jnp.zeros((HALF,) + up_meta.shape, bf16)
    for k, piece in enumerate(up_pieces):
        up_own = lax.dynamic_update_index_in_dim(up_own, piece, chip ^ k, 0)
    up_other = lax.ppermute(up_own, "exp", core_swap)

    hidden_one = norm_rows(tokens, gain_attn)
    hidden_seq = norm_rows(tokens_seq, gain_attn)
    hidden_seq = after(hidden_seq, w_shared, up_own)
    queries, kv_all = project(hidden_one, hidden_seq, w_all)
    attended, att_f, logs = attend(ctx_s, queries, kv_all)
    middle, hidden_two = middle_norm(attended, w_all, tokens[0], gain_ffn)

    hidden_all = lax.all_gather(hidden_two, "exp", axis=0, tiled=True)
    hidden_all = hidden_all.reshape(HALF, 2, BLOCK, WIDTH)
    rows_all = lax.all_gather(
        after(jnp.concatenate([hidden_one[0], attended], axis=1), hidden_two),
        "exp",
        axis=0,
        tiled=True,
    )
    place, grad_eo, grad_eh, grad_sh, slot_gate = place_rows(
        exp_s, after(up_own, hidden_two), up_other, expert_down, shared_two
    )
    part, arrived, act, grad_gu, shared_act, shared_grad = expert_back(
        exp_s, hidden_all, place, grad_eh, grad_sh, expert_gate, expert_up, w_shared
    )
    summed = add_low(part[1], lax.ppermute(part[0], "exp", core_swap))
    grad_two = swap_all(summed, "exp", same_core)

    rows_e = 2 * ROWS
    p = expert_weights(
        yz_s,
        after(arrived, summed).reshape(LOCAL_E, rows_e, WIDTH),
        grad_eo.reshape(LOCAL_E, rows_e, WIDTH),
        act.reshape(LOCAL_E, rows_e, FF_E),
        grad_gu.reshape(LOCAL_E, rows_e, 2 * FF_E),
    )

    def to(rows, k):
        return lax.ppermute(rows, "ctx", [(i, i ^ k) for i in range(N_CTX)])

    relay_a, relay_b = to(p[4], 1), to(p[5], 3)
    got_10, got_31 = to(p[2], 1), to(p[7], 3)

    shared_grad_late = after(shared_grad, p[0]).reshape(N_EXP * BLOCK, META)
    grad_scols = dg(hidden_all.reshape(N_EXP * BLOCK, WIDTH), shared_grad_late, TN).astype(bf16)
    core = exp_at % 2
    act_pair = after(shared_act, p[0])
    act_own = lax.dynamic_index_in_dim(act_pair, core, 1, keepdims=False)
    act_other = lax.dynamic_index_in_dim(act_pair, 1 - core, 1, keepdims=False)
    flat = (HALF * BLOCK, -1)
    grad_sdown = (
        dg(act_own.reshape(flat), up_own.reshape(flat), TN)
        + dg(act_other.reshape(flat), up_other.reshape(flat), TN)
    )[:SHARED, :WIDTH].astype(bf16)
    out_part = expert_output(
        exp_s, after(act, p[0]), slot_gate, place, shared_act, expert_down, shared_two
    )

    grad_middle, grad_attn, grad_heads, grad_gain_ffn = middle_back(
        grad_two, middle, cotangent[0], gain_ffn, w_all
    )
    grad_query, part_kv = attend_back(ctx_s, queries, grad_heads, att_f, logs, kv_all)
    kv_pieces = swap_all(part_kv, "ctx")

    relay_a, relay_b = after((relay_a, relay_b), part_kv)
    got_11, got_30 = to(add_low(p[3], relay_b), 1), to(add_low(p[6], relay_a), 3)
    out_other = lax.ppermute(after(out_part[0], part_kv), "exp", core_swap)
    out_sum = add_low(out_part[1], out_other)

    grad_qkv, cols = turn_cols(grad_query, kv_pieces, grad_attn)
    cols_sent = cols
    cols = swap_all(cols, "exp")
    got_11, got_30, out_sum = after((got_11, got_30, out_sum), cols_sent)
    out_pieces = swap_all(out_sum, "exp", same_core)
    across = to(
        (p[1].astype(f32) + got_11.astype(f32) + got_31.astype(f32)).astype(bf16), 4
    )
    input_grad, grad_gain_attn = input_back(
        grad_qkv, w_all, tokens[0], gain_attn, grad_middle
    )
    grad_cols = cols_grad(cols, rows_all)
    gain_rows = jnp.concatenate(
        [grad_gain_attn.reshape(N_EXP, 1, 96), grad_gain_ffn.reshape(N_EXP, 1, 96)], axis=1
    ).astype(bf16)
    gain_rows = jnp.pad(gain_rows, ((0, 0), (0, 14), (0, 160)))
    sent = jnp.concatenate(
        [
            jnp.concatenate([grad_cols, gain_rows], axis=1),
            jnp.pad(grad_scols.reshape(N_EXP, 96, META), ((0, 0), (0, 16), (0, 0))),
        ],
        axis=2,
    )
    back = swap_all(sent, "exp")

    own = (
        p[0].astype(f32)
        + got_10.astype(f32)
        + got_30.astype(f32)
        + after(across, sent).astype(f32)
    ).astype(bf16)
    at_1, at_3, at_z = to(own, 1), to(own, 3), to(own, 4)

    small = jnp.concatenate(
        [back.reshape(N_CTX, 224, 384), grad_sdown.reshape(N_CTX, 32, 384)], axis=1
    )
    pieces = swap_all(small, "ctx")
    late_own = jnp.sum(pieces.astype(f32), axis=0).astype(bf16)
    at_2 = to(after(at_3, small), 1)
    at_z1, at_z3 = to(after(at_z, small), 1), to(after(at_z, small), 3)
    late = swap_all(jnp.broadcast_to(late_own, (N_CTX, 256, 384)), "ctx")
    at_z2 = to(after(at_z1, late_own), 3)
    grad_sdown = late[:, 224:].reshape(SHARED, WIDTH).astype(f32)
    late = late[:, :224].reshape(N_EXP, 112, 384)

    mixed = (middle + jnp.sum(out_pieces.astype(f32), axis=0)).astype(bf16)[None]
    grad_wqkv = late[:, :96, :160].transpose(1, 0, 2).reshape(96, WIDTH + 2 * KV_WIDTH)
    gain_sum = jnp.sum(late[:, 96:98, :96].astype(f32), axis=0)
    grad_egate, grad_eup, grad_edown = unpack_experts(
        yz_s, (own, at_1, at_2, at_3, at_z, at_z1, at_z2, at_z3)
    )
    return (
        mixed,
        input_grad[None],
        gain_sum[0],
        gain_sum[1],
        grad_wqkv[:, :WIDTH].astype(f32),
        grad_wqkv[:, WIDTH : WIDTH + KV_WIDTH].astype(f32),
        grad_wqkv[:, WIDTH + KV_WIDTH :].astype(f32),
        late[:, :96, 160:256].transpose(1, 0, 2).reshape(96, WIDTH).astype(f32),
        late[:, :96, 256 : 256 + SHARED].transpose(1, 0, 2).reshape(96, 1024).astype(f32),
        late[:, :96, 256 + SHARED :].transpose(1, 0, 2).reshape(96, 1024).astype(f32),
        grad_sdown,
        grad_egate,
        grad_eup,
        grad_edown,
    )


def solution(mesh):
    token_spec = P("exp", "ctx", None)
    rows = P("exp", None)
    expert = P("exp", None, None)
    placed = (token_spec,) * 3 + (P("exp"),) * 2 + (rows,) * 7 + (expert,) * 3 + (token_spec,)
    return jax.shard_map(
        on_device,
        mesh=mesh,
        in_specs=placed,
        out_specs=(token_spec,) * 2 + (P("exp"),) * 2 + (rows,) * 7 + (expert,) * 3,
        check_vma=False,
    )
```

```python
import jax
import jax.numpy as jnp
from jax import lax
from jax.sharding import PartitionSpec as P
from jax.experimental import pallas as pl
from jax.experimental.pallas import tpu as pltpu

HEADS = 12
KV_HEADS = 4
HEAD_DIM = 128
TOPK = 6
GROUP = 3
BLOCK = 128
WIDTH = 1536
KV_WIDTH = KV_HEADS * HEAD_DIM
CAP = 48
N_EXP = 16
N_CTX = 8
LOCAL_E = 2
FF_E = 512
SHARED = 64
META = 128
HALF = 8
ROWS = HALF * CAP

epsilon = 1e-05
masked_score = -1e30
f32 = jnp.float32
bf16 = jnp.bfloat16
log2_e = 1.4426950408889634
score_scale = HEAD_DIM ** (-0.5) * log2_e

NN = (((1,), (0,)), ((), ()))
NT = (((1,), (1,)), ((), ()))
TN = (((0,), (0,)), ((), ()))


def dg(a, b, dims):
    return lax.dot_general(a, b, dims, preferred_element_type=f32)


def params(mib):
    return pltpu.CompilerParams(vmem_limit_bytes=mib * 1024 * 1024)


def whole(shape):
    return pl.BlockSpec(shape, lambda *_: (0,) * len(shape), pipeline_mode=pl.Buffered(1))


def sigmoid(v):
    return 1.0 / (1.0 + jnp.exp(-v))


def allowed_scores(ctx_at):
    rows = lax.broadcasted_iota(jnp.int32, (GROUP * BLOCK, N_CTX * BLOCK), 0) % BLOCK
    cols = lax.broadcasted_iota(jnp.int32, (GROUP * BLOCK, N_CTX * BLOCK), 1)
    return rows + ctx_at * BLOCK >= cols


def stack_heads(block):
    return jnp.concatenate([block[:, j * HEAD_DIM : (j + 1) * HEAD_DIM] for j in range(GROUP)], axis=0)


def unstack_heads(rows):
    return jnp.concatenate([rows[j * BLOCK : (j + 1) * BLOCK] for j in range(GROUP)], axis=1)


def attend_kernel(ctx_ref, q_ref, k_ref, v_ref, att_ref, attf_ref, log_ref):
    q = stack_heads(q_ref[...])
    keys = k_ref[...].reshape(N_CTX * BLOCK, HEAD_DIM)
    values = v_ref[...].reshape(N_CTX * BLOCK, HEAD_DIM)
    scores = jnp.where(allowed_scores(ctx_ref[0]), dg(q, keys, NT) * score_scale, masked_score)
    top = jnp.max(scores, axis=-1, keepdims=True)
    weights = jnp.exp2(scores - top)
    total = jnp.sum(weights, axis=-1, keepdims=True)
    out = dg(weights.astype(bf16), values, NN) * (1.0 / total)
    out = unstack_heads(out)
    attf_ref[...] = out
    att_ref[...] = out.astype(bf16)
    log_ref[...] = jnp.broadcast_to(top + jnp.log2(total), (GROUP * BLOCK, HEAD_DIM))


def kv_specs():
    return [
        pl.BlockSpec((N_CTX, BLOCK, HEAD_DIM), lambda g: (0, 0, g)),
        pl.BlockSpec((N_CTX, BLOCK, HEAD_DIM), lambda g: (0, 0, KV_HEADS + g)),
    ]


def head_spec():
    return pl.BlockSpec((BLOCK, GROUP * HEAD_DIM), lambda g: (0, g))


def attend(ctx_at, qkv, kv_all):
    return pl.pallas_call(
        attend_kernel,
        grid=(KV_HEADS,),
        in_specs=[pl.BlockSpec(memory_space=pltpu.SMEM), head_spec()] + kv_specs(),
        out_specs=[
            head_spec(),
            head_spec(),
            pl.BlockSpec((GROUP * BLOCK, HEAD_DIM), lambda g: (g, 0)),
        ],
        out_shape=[
            jax.ShapeDtypeStruct((BLOCK, WIDTH), bf16),
            jax.ShapeDtypeStruct((BLOCK, WIDTH), f32),
            jax.ShapeDtypeStruct((HEADS * BLOCK, HEAD_DIM), f32),
        ],
        compiler_params=params(48),
        name="attend",
    )(ctx_at, qkv, kv_all, kv_all)


def attend_back_kernel(
    ctx_ref, q_ref, ga_ref, attf_ref, log_ref, k_ref, v_ref, dq_ref, dkv_ref
):
    q = stack_heads(q_ref[...])
    grad = stack_heads(ga_ref[...])
    delta = jnp.sum(grad.astype(f32) * stack_heads(attf_ref[...]), axis=-1, keepdims=True)
    keys = k_ref[...].reshape(N_CTX * BLOCK, HEAD_DIM)
    values = v_ref[...].reshape(N_CTX * BLOCK, HEAD_DIM)
    scores = jnp.where(allowed_scores(ctx_ref[0]), dg(q, keys, NT) * score_scale, masked_score)
    weights = jnp.exp2(scores - log_ref[:, :1])
    grad_weights = dg(grad, values, NT)
    grad_raw = (weights * (grad_weights - delta)).astype(bf16)
    scale = HEAD_DIM ** (-0.5)
    dq_ref[...] = unstack_heads(dg(grad_raw, keys, NN) * scale).astype(bf16)
    grad_k = (dg(grad_raw, q, TN) * scale).astype(bf16)
    grad_v = dg(weights.astype(bf16), grad, TN).astype(bf16)
    dkv_ref[:, :, :HEAD_DIM] = grad_k.reshape(N_CTX, BLOCK, HEAD_DIM)
    dkv_ref[:, :, HEAD_DIM:] = grad_v.reshape(N_CTX, BLOCK, HEAD_DIM)


def attend_back(ctx_at, qkv, grad_att, att_f, logs, kv_all):
    part = pl.BlockSpec((N_CTX, BLOCK, 2 * HEAD_DIM), lambda g: (0, 0, g))
    return pl.pallas_call(
        attend_back_kernel,
        grid=(KV_HEADS,),
        in_specs=[
            pl.BlockSpec(memory_space=pltpu.SMEM),
            head_spec(),
            head_spec(),
            head_spec(),
            pl.BlockSpec((GROUP * BLOCK, HEAD_DIM), lambda g: (g, 0)),
        ]
        + kv_specs(),
        out_specs=[head_spec(), part],
        out_shape=[
            jax.ShapeDtypeStruct((BLOCK, WIDTH), bf16),
            jax.ShapeDtypeStruct((N_CTX, BLOCK, 2 * KV_WIDTH), bf16),
        ],
        compiler_params=params(48),
        name="attend_back",
    )(ctx_at, qkv, grad_att, att_f, logs, kv_all, kv_all)


def middle_kernel(att_ref, w_ref, x_ref, gain_ref, middle_ref, hidden_ref):
    middle = x_ref[...].astype(f32) + dg(att_ref[...], w_ref[...], NN)
    inv = lax.rsqrt(jnp.mean(middle * middle, axis=-1, keepdims=True) + epsilon)
    middle_ref[...] = middle
    hidden_ref[...] = (middle * inv * gain_ref[...]).astype(bf16)


def w_cols(width, at):
    return pl.BlockSpec((WIDTH, width), lambda *_: (0, at), pipeline_mode=pl.Buffered(1))


def middle_norm(attended, w_all, tokens, gain):
    return pl.pallas_call(
        middle_kernel,
        grid=(1,),
        in_specs=[
            whole((BLOCK, WIDTH)),
            w_cols(WIDTH, 1),
            whole((BLOCK, WIDTH)),
            whole((1, WIDTH)),
        ],
        out_specs=[whole((BLOCK, WIDTH)), whole((BLOCK, WIDTH))],
        out_shape=[
            jax.ShapeDtypeStruct((BLOCK, WIDTH), f32),
            jax.ShapeDtypeStruct((BLOCK, WIDTH), bf16),
        ],
        compiler_params=params(32),
        name="middle_norm",
    )(attended, w_all, tokens, gain)


def norm_back(grad_normed, normed, inv_root):
    return inv_root * (
        grad_normed - normed * jnp.mean(grad_normed * normed, axis=-1, keepdims=True)
    )


def middle_back_kernel(
    pieces_ref, middle_ref, up_ref, gain_ref, w_ref, gm_ref, ga_ref, gh_ref, gg_ref
):
    grad_two = pieces_ref[0].astype(f32)
    for i in range(1, HALF):
        grad_two = grad_two + pieces_ref[i].astype(f32)
    middle = middle_ref[...]
    inv = lax.rsqrt(jnp.mean(middle * middle, axis=-1, keepdims=True) + epsilon)
    normed = middle * inv
    gg_ref[...] = jnp.sum(grad_two * normed, axis=0, keepdims=True)
    grad_middle = up_ref[...].astype(f32) + norm_back(grad_two * gain_ref[...], normed, inv)
    gm_ref[...] = grad_middle
    grad_attn = grad_middle.astype(bf16)
    ga_ref[...] = grad_attn
    gh_ref[...] = dg(grad_attn, w_ref[...], NT).astype(bf16)


def middle_back(pieces, middle, upstream, gain, w_all):
    return pl.pallas_call(
        middle_back_kernel,
        grid=(1,),
        in_specs=[
            whole((HALF, BLOCK, WIDTH)),
            whole((BLOCK, WIDTH)),
            whole((BLOCK, WIDTH)),
            whole((1, WIDTH)),
            w_cols(WIDTH, 1),
        ],
        out_specs=[whole((BLOCK, WIDTH))] * 3 + [whole((1, WIDTH))],
        out_shape=[
            jax.ShapeDtypeStruct((BLOCK, WIDTH), f32),
            jax.ShapeDtypeStruct((BLOCK, WIDTH), bf16),
            jax.ShapeDtypeStruct((BLOCK, WIDTH), bf16),
            jax.ShapeDtypeStruct((1, WIDTH), f32),
        ],
        compiler_params=params(48),
        name="middle_back",
    )(pieces, middle, upstream, gain, w_all)


def place_kernel(
    at_ref, up_ref, down_ref, sdown_ref, place_ref, geo_ref, geh_ref, gsh_ref, gate_ref
):
    lane = lax.broadcasted_iota(jnp.int32, (BLOCK, META), 1)
    row = lax.broadcasted_iota(jnp.int32, (BLOCK, META), 0)
    before = (row > lane).astype(bf16)
    slot = (lane % 64).astype(f32)
    first_id = (at_ref[0] * LOCAL_E).astype(f32)
    row_id = first_id + (row >= 64).astype(f32)

    for chip in range(HALF):
        meta = up_ref[chip, 0, :, WIDTH:].astype(f32)
        named = lane < TOPK
        zero = jnp.zeros((BLOCK, META), f32)
        hit0 = jnp.where(named & (meta == first_id), 1.0, zero)
        hit1 = jnp.where(named & (meta == first_id + 1.0), 1.0, zero)
        mask = jnp.where(
            lane < 64,
            jnp.sum(hit0, axis=1, keepdims=True),
            jnp.sum(hit1, axis=1, keepdims=True),
        )
        rank = dg(before, mask.astype(bf16), NN)
        place = jnp.where((mask > 0.5) & (rank == slot), 1.0, zero).astype(bf16)
        place_ref[chip, 0] = place
        rows = dg(place, up_ref[chip, 0], TN)
        slot_meta = rows[:, WIDTH:]
        gates = pltpu.roll(slot_meta, META - TOPK, 1) + pltpu.roll(
            slot_meta, META - 2 * TOPK, 1
        )
        gate = jnp.sum(
            jnp.where(named & (slot_meta == row_id), gates, zero), axis=1, keepdims=True
        )
        geo = (gate * rows[:, :WIDTH]).astype(bf16)
        wide_gate = jnp.broadcast_to(gate, (BLOCK, META))
        at = chip * CAP
        for e in range(LOCAL_E):
            geo_ref[e, 0, at : at + CAP] = geo[64 * e : 64 * e + CAP]
            gate_ref[e, 0, at : at + CAP] = wide_gate[64 * e : 64 * e + CAP]
        gsh_ref[chip, 0] = dg(up_ref[chip, 0, :, :WIDTH], sdown_ref[...], NT)
    for e in range(LOCAL_E):
        geh_ref[e, 0] = dg(geo_ref[e, 0], down_ref[e], NT)


def by_core(cols):
    return pl.BlockSpec(
        (HALF, 1, BLOCK, cols),
        lambda s, at: (0, jnp.where(s == 0, 1 - at[0] % 2, at[0] % 2), 0, 0),
    )


def by_step(cols):
    return pl.BlockSpec((LOCAL_E, 1, ROWS, cols), lambda s, at: (0, s, 0, 0))


def place_rows(exp_at, up_all, expert_down, shared_two):
    return pl.pallas_call(
        place_kernel,
        grid_spec=pltpu.PrefetchScalarGridSpec(
            num_scalar_prefetch=1,
            grid=(2,),
            in_specs=[
                by_core(WIDTH + META),
                whole((LOCAL_E, FF_E, WIDTH)),
                whole((2 * SHARED, WIDTH)),
            ],
            out_specs=[by_core(META), by_step(WIDTH), by_step(FF_E), by_core(META), by_step(META)],
        ),
        out_shape=[
            jax.ShapeDtypeStruct((HALF, 2, BLOCK, META), bf16),
            jax.ShapeDtypeStruct((LOCAL_E, 2, ROWS, WIDTH), bf16),
            jax.ShapeDtypeStruct((LOCAL_E, 2, ROWS, FF_E), f32),
            jax.ShapeDtypeStruct((HALF, 2, BLOCK, META), f32),
            jax.ShapeDtypeStruct((LOCAL_E, 2, ROWS, META), f32),
        ],
        compiler_params=params(56),
        name="place_rows",
    )(exp_at, up_all, expert_down, shared_two)


def expert_kernel(
    at_ref,
    hid_ref,
    place_ref,
    geh_ref,
    gsh_ref,
    wg_ref,
    wu_ref,
    ws_ref,
    part_ref,
    x_ref,
    act_ref,
    dgu_ref,
    sact_ref,
    sgrad_ref,
):
    for chip in range(HALF):
        rows = dg(place_ref[chip, 0], hid_ref[chip, 0], TN).astype(bf16)
        at = chip * CAP
        for e in range(LOCAL_E):
            x_ref[e, 0, at : at + CAP] = rows[64 * e : 64 * e + CAP]
    pairs = []
    for e in range(LOCAL_E):
        pre_gate = dg(x_ref[e, 0], wg_ref[e], NN)
        pre_up = dg(x_ref[e, 0], wu_ref[e], NN)
        sig = sigmoid(pre_gate)
        act = pre_gate * sig
        act_ref[e, 0] = (act * pre_up).astype(bf16)
        geh = geh_ref[e, 0]
        d_gate = (geh * pre_up * (sig * (1.0 + pre_gate * (1.0 - sig)))).astype(bf16)
        d_up = (geh * act).astype(bf16)
        dgu_ref[e, 0, :, :FF_E] = d_gate
        dgu_ref[e, 0, :, FF_E:] = d_up
        pairs.append((dg(d_gate, wg_ref[e], NT) + dg(d_up, wu_ref[e], NT)).astype(bf16))
    lane = lax.broadcasted_iota(jnp.int32, (BLOCK, 2 * SHARED), 1) < SHARED
    gap = jnp.zeros((64 - CAP, WIDTH), bf16)
    for chip in range(HALF):
        pre = dg(hid_ref[chip, 0], ws_ref[...], NN)
        turned = pltpu.roll(pre, SHARED, 1)
        gate, up = jnp.where(lane, pre, turned), jnp.where(lane, turned, pre)
        sig = sigmoid(gate)
        act = gate * sig
        sact_ref[chip, 0] = jnp.where(lane, act * up, 0.0).astype(bf16)
        slope = sig * (1.0 + gate * (1.0 - sig))
        sgrad = (gsh_ref[chip, 0] * jnp.where(lane, up * slope, act)).astype(bf16)
        sgrad_ref[chip, 0] = sgrad
        at = chip * CAP
        stacked = jnp.concatenate([pairs[0][at : at + CAP], gap, pairs[1][at : at + CAP], gap], 0)
        part_ref[0, chip] = (
            dg(place_ref[chip, 0], stacked, NN) + dg(sgrad, ws_ref[...], NT)
        ).astype(bf16)


def expert_back(exp_at, hidden, place, geh, gsh, wg, wu, ws):
    return pl.pallas_call(
        expert_kernel,
        grid_spec=pltpu.PrefetchScalarGridSpec(
            num_scalar_prefetch=1,
            grid=(2,),
            in_specs=[
                by_core(WIDTH),
                by_core(META),
                by_step(FF_E),
                by_core(META),
                whole((LOCAL_E, WIDTH, FF_E)),
                whole((LOCAL_E, WIDTH, FF_E)),
                whole((WIDTH, 2 * SHARED)),
            ],
            out_specs=[
                pl.BlockSpec((1, HALF, BLOCK, WIDTH), lambda s, at: (s, 0, 0, 0)),
                by_step(WIDTH),
                by_step(FF_E),
                by_step(2 * FF_E),
                by_core(META),
                by_core(META),
            ],
        ),
        out_shape=[
            jax.ShapeDtypeStruct((2, HALF, BLOCK, WIDTH), bf16),
            jax.ShapeDtypeStruct((LOCAL_E, 2, ROWS, WIDTH), bf16),
            jax.ShapeDtypeStruct((LOCAL_E, 2, ROWS, FF_E), bf16),
            jax.ShapeDtypeStruct((LOCAL_E, 2, ROWS, 2 * FF_E), bf16),
            jax.ShapeDtypeStruct((HALF, 2, BLOCK, META), bf16),
            jax.ShapeDtypeStruct((HALF, 2, BLOCK, META), bf16),
        ],
        compiler_params=params(60),
        name="expert_back",
    )(exp_at, hidden, place, geh, gsh, wg, wu, ws)


def output_kernel(at_ref, act_ref, gate_ref, place_ref, sact_ref, wd_ref, sd_ref, part_ref):
    outs = []
    for e in range(LOCAL_E):
        out = dg(act_ref[e, 0], wd_ref[e], NN).astype(bf16).astype(f32)
        outs.append((out * gate_ref[e, 0, :, :1]).astype(bf16))
    gap = jnp.zeros((64 - CAP, WIDTH), bf16)
    for chip in range(HALF):
        at = chip * CAP
        stacked = jnp.concatenate([outs[0][at : at + CAP], gap, outs[1][at : at + CAP], gap], 0)
        part_ref[0, chip] = (
            dg(place_ref[chip, 0], stacked, NN) + dg(sact_ref[chip, 0], sd_ref[...], NN)
        ).astype(bf16)


def expert_output(exp_at, act, gate, place, sact, wd, sd):
    return pl.pallas_call(
        output_kernel,
        grid_spec=pltpu.PrefetchScalarGridSpec(
            num_scalar_prefetch=1,
            grid=(2,),
            in_specs=[
                by_step(FF_E),
                by_step(META),
                by_core(META),
                by_core(META),
                whole((LOCAL_E, FF_E, WIDTH)),
                whole((2 * SHARED, WIDTH)),
            ],
            out_specs=pl.BlockSpec((1, HALF, BLOCK, WIDTH), lambda s, at: (s, 0, 0, 0)),
        ),
        out_shape=jax.ShapeDtypeStruct((2, HALF, BLOCK, WIDTH), bf16),
        compiler_params=params(48),
        name="expert_output",
    )(exp_at, act, gate, place, sact, wd, sd)


def turn_kernel(dq_ref, pieces_ref, ga_ref, gqkv_ref, cols_ref):
    total = pieces_ref[0].astype(f32)
    for i in range(1, N_CTX):
        total = total + pieces_ref[i].astype(f32)
    total = total.astype(bf16)
    parts = [total[:, i * HEAD_DIM : (i + 1) * HEAD_DIM] for i in range(2 * KV_HEADS)]
    grad_kv = jnp.concatenate(parts[0::2] + parts[1::2], axis=1)
    gqkv_ref[:, :WIDTH] = dq_ref[...]
    gqkv_ref[:, WIDTH:] = grad_kv
    turned = jnp.concatenate([dq_ref[...].T, grad_kv.T], axis=0)
    turned_out = ga_ref[...].T
    for j in range(N_EXP):
        cols_ref[j, :160] = turned[160 * j : 160 * j + 160]
        cols_ref[j, 160:] = turned_out[96 * j : 96 * j + 96]


def turn_cols(dq, pieces, grad_attn):
    return pl.pallas_call(
        turn_kernel,
        out_shape=[
            jax.ShapeDtypeStruct((BLOCK, WIDTH + 2 * KV_WIDTH), bf16),
            jax.ShapeDtypeStruct((N_EXP, 256, BLOCK), bf16),
        ],
        compiler_params=params(32),
        name="turn_cols",
    )(dq, pieces, grad_attn)


def input_kernel(gqkv_ref, wq_ref, wkv_ref, x_ref, gain_ref, gm_ref, out_ref, gg_ref):
    grad_one = dg(gqkv_ref[:, :WIDTH], wq_ref[...], NT) + dg(gqkv_ref[:, WIDTH:], wkv_ref[...], NT)
    inputs = x_ref[...].astype(f32)
    inv = lax.rsqrt(jnp.mean(inputs * inputs, axis=-1, keepdims=True) + epsilon)
    normed = inputs * inv
    gg_ref[...] = jnp.sum(grad_one * normed, axis=0, keepdims=True)
    out_ref[...] = (gm_ref[...] + norm_back(grad_one * gain_ref[...], normed, inv)).astype(bf16)


def input_back(grad_qkv, w_all, tokens, gain, grad_middle):
    return pl.pallas_call(
        input_kernel,
        grid=(1,),
        in_specs=[
            whole((BLOCK, WIDTH + 2 * KV_WIDTH)),
            w_cols(WIDTH, 0),
            w_cols(2 * KV_WIDTH, 3),
            whole((BLOCK, WIDTH)),
            whole((1, WIDTH)),
            whole((BLOCK, WIDTH)),
        ],
        out_specs=[whole((BLOCK, WIDTH)), whole((1, WIDTH))],
        out_shape=[
            jax.ShapeDtypeStruct((BLOCK, WIDTH), bf16),
            jax.ShapeDtypeStruct((1, WIDTH), f32),
        ],
        compiler_params=params(48),
        name="input_back",
    )(grad_qkv, w_all, w_all, tokens, gain, grad_middle)


def cols_kernel(cols_ref, hidden_ref, att_ref, out_ref):
    lhs = jnp.concatenate([cols_ref[j] for j in range(N_EXP)], axis=1)
    row = lax.broadcasted_iota(jnp.int32, (256, N_EXP * BLOCK), 0)
    zero = jnp.zeros_like(lhs)
    attn = dg(jnp.where(row < 160, lhs, zero), hidden_ref[...], NN)
    out = dg(jnp.where(row < 160, zero, lhs), att_ref[...], NN)
    out_ref[...] = (attn + out).T.astype(bf16).reshape(N_EXP, 96, 256)


def cols_grad(cols, hidden_all, att_all):
    return pl.pallas_call(
        cols_kernel,
        out_shape=jax.ShapeDtypeStruct((N_EXP, 96, 256), bf16),
        compiler_params=params(56),
        name="cols_grad",
    )(cols, hidden_all, att_all)


def norm_rows_kernel(x_ref, gain_ref, out_ref):
    inputs = x_ref[0].astype(f32)
    inv = lax.rsqrt(jnp.mean(inputs * inputs, axis=-1, keepdims=True) + epsilon)
    out_ref[0] = (inputs * inv * gain_ref[...]).astype(bf16)


def norm_rows(rows, gain):
    count = rows.shape[0]
    spec = pl.BlockSpec((1, BLOCK, WIDTH), lambda i: (i, 0, 0))
    return pl.pallas_call(
        norm_rows_kernel,
        grid=(count,),
        in_specs=[spec, whole((1, WIDTH))],
        out_specs=spec,
        out_shape=jax.ShapeDtypeStruct(rows.shape, bf16),
        compiler_params=params(32),
        name="norm_rows",
    )(rows, gain)


def project_kernel(own_ref, seq_ref, w_ref, q_ref, kv_ref):
    step = pl.program_id(0)

    @pl.when(step < 3)
    def _():
        q_ref[...] = dg(own_ref[0], w_ref[...], NN).astype(bf16)

    @pl.when(step >= 3)
    def _():
        rows = seq_ref[...].reshape(N_CTX * BLOCK, WIDTH)
        kv_ref[...] = dg(rows, w_ref[...], NN).astype(bf16).reshape(N_CTX, BLOCK, KV_WIDTH)


def project(own, seq, w_all):
    return pl.pallas_call(
        project_kernel,
        grid=(5,),
        in_specs=[
            whole((1, BLOCK, WIDTH)),
            whole((N_CTX, BLOCK, WIDTH)),
            pl.BlockSpec((WIDTH, KV_WIDTH), lambda i: (0, jnp.where(i < 3, i, i + 3))),
        ],
        out_specs=[
            pl.BlockSpec((BLOCK, KV_WIDTH), lambda i: (0, jnp.minimum(i, 2))),
            pl.BlockSpec((N_CTX, BLOCK, KV_WIDTH), lambda i: (0, 0, jnp.maximum(i - 3, 0))),
        ],
        out_shape=[
            jax.ShapeDtypeStruct((BLOCK, WIDTH), bf16),
            jax.ShapeDtypeStruct((N_CTX, BLOCK, 2 * KV_WIDTH), bf16),
        ],
        compiler_params=params(48),
        name="project",
    )(own, seq, w_all)


PIECE = 2 * WIDTH + WIDTH * BLOCK // HEAD_DIM


def expert_weights_kernel(at_ref, x_ref, geo_ref, act_ref, dgate_ref, dup_ref, *refs):
    outs, turned = refs[:8], refs[8]
    step = pl.program_id(0)

    @pl.when(step == 0)
    def _():
        for e in range(LOCAL_E):
            turned[e] = x_ref[e].T

    for r in range(4):

        @pl.when(step == r)
        def _():
            for side in range(2):
                e = at_ref[1] if side == 0 else 1 - at_ref[1]
                out = outs[2 * r + side]
                rhs = jnp.concatenate([dgate_ref[e], dup_ref[e]], axis=1)
                both = dg(turned[e], rhs, NN).astype(bf16)
                out[:WIDTH] = both[:, :HEAD_DIM]
                out[WIDTH : 2 * WIDTH] = both[:, HEAD_DIM:]
                down = dg(act_ref[e], geo_ref[e], TN).astype(bf16)
                for m in range(WIDTH // HEAD_DIM):
                    at = 2 * WIDTH + m * BLOCK
                    out[at : at + BLOCK] = down[:, m * HEAD_DIM : (m + 1) * HEAD_DIM]


def expert_weights(at, arrived, grad_eo, act, grad_gu):
    rows = 2 * ROWS
    lanes = lambda shift: pl.BlockSpec(
        (LOCAL_E, rows, HEAD_DIM), lambda r, at: (0, 0, shift + (at[0] ^ r))
    )
    piece = jax.ShapeDtypeStruct((PIECE, HEAD_DIM), bf16)
    return pl.pallas_call(
        expert_weights_kernel,
        grid_spec=pltpu.PrefetchScalarGridSpec(
            num_scalar_prefetch=1,
            grid=(4,),
            in_specs=[
                whole((LOCAL_E, rows, WIDTH)),
                whole((LOCAL_E, rows, WIDTH)),
                lanes(0),
                lanes(0),
                lanes(4),
            ],
            out_specs=[whole((PIECE, HEAD_DIM))] * 8,
            scratch_shapes=[pltpu.VMEM((LOCAL_E, WIDTH, rows), bf16)],
        ),
        out_shape=[piece] * 8,
        compiler_params=params(56),
        name="expert_weights",
    )(at, arrived, grad_eo, act, grad_gu, grad_gu)


def unpack_kernel(at_ref, *refs):
    pieces, (gate_ref, up_ref, down_ref) = refs[:8], refs[8:]
    step = pl.program_id(0)
    for i in range(8):

        @pl.when(step == i)
        def _():
            piece = pieces[i]
            gate_ref[0] = piece[:WIDTH].astype(f32)
            up_ref[0] = piece[WIDTH : 2 * WIDTH].astype(f32)
            for m in range(WIDTH // HEAD_DIM):
                at = 2 * WIDTH + m * BLOCK
                down_ref[0, :, m * HEAD_DIM : (m + 1) * HEAD_DIM] = piece[at : at + BLOCK].astype(
                    f32
                )


def unpack_experts(at, pieces):
    cols = pl.BlockSpec(
        (1, WIDTH, HEAD_DIM), lambda s, at: (at[1] ^ (s // 4), 0, at[0] ^ (s % 4))
    )
    return pl.pallas_call(
        unpack_kernel,
        grid_spec=pltpu.PrefetchScalarGridSpec(
            num_scalar_prefetch=1,
            grid=(8,),
            in_specs=[whole((PIECE, HEAD_DIM))] * 8,
            out_specs=[
                cols,
                cols,
                pl.BlockSpec(
                    (1, BLOCK, WIDTH), lambda s, at: (at[1] ^ (s // 4), at[0] ^ (s % 4), 0)
                ),
            ],
        ),
        out_shape=[
            jax.ShapeDtypeStruct((LOCAL_E, WIDTH, FF_E), f32),
            jax.ShapeDtypeStruct((LOCAL_E, WIDTH, FF_E), f32),
            jax.ShapeDtypeStruct((LOCAL_E, FF_E, WIDTH), f32),
        ],
        compiler_params=params(48),
        name="unpack_experts",
    )(at, *pieces)


def relay_kernel(p3, p6, relay_a, relay_b, add_a, add_b):
    add_a[...] = (p6[...].astype(f32) + relay_a[...].astype(f32)).astype(bf16)
    add_b[...] = (p3[...].astype(f32) + relay_b[...].astype(f32)).astype(bf16)


def side_kernel(p0, p1, got_10, got_31, got_11, got_30, own, side):
    own[...] = p0[...].astype(f32) + got_10[...].astype(f32) + got_30[...].astype(f32)
    side[...] = (
        p1[...].astype(f32) + got_31[...].astype(f32) + got_11[...].astype(f32)
    ).astype(bf16)


def piece_sums(kernel, kinds, *pieces):
    spec = pl.BlockSpec((PIECE // 4, HEAD_DIM), lambda i: (i, 0))
    return pl.pallas_call(
        kernel,
        grid=(4,),
        in_specs=[spec] * len(pieces),
        out_specs=[spec] * len(kinds),
        out_shape=[jax.ShapeDtypeStruct((PIECE, HEAD_DIM), kind) for kind in kinds],
        compiler_params=params(32),
        name="piece_sums",
    )(*pieces)


same_core = [[2 * i + c for i in range(8)] for c in range(2)]
core_swap = [(i, i ^ 1) for i in range(N_EXP)]


def swap_all(rows, axis, groups=None):
    return lax.all_to_all(
        rows, axis, split_axis=0, concat_axis=0, tiled=True, axis_index_groups=groups
    )


def after(value, *others):
    return lax.optimization_barrier((value,) + others)[0]


def add_low(a, b):
    return (a.astype(f32) + b.astype(f32)).astype(bf16)


def on_device(
    tokens,
    routes,
    route_gates,
    norm_attn,
    norm_ffn,
    query_weight,
    key_weight,
    value_weight,
    out_weight,
    shared_gate,
    shared_up,
    shared_down,
    expert_gate,
    expert_up,
    expert_down,
    cotangent,
):
    exp_at = lax.axis_index("exp").astype(jnp.int32)
    ctx_at = lax.axis_index("ctx").astype(jnp.int32)
    exp_s, ctx_s = exp_at.reshape(1), ctx_at.reshape(1)

    y_at, z_at = ctx_at % 4, ctx_at // 4
    yz_s = jnp.stack([y_at, z_at])

    w_cat = jnp.concatenate([query_weight, out_weight, key_weight, value_weight], axis=1)
    w_all = lax.all_gather(w_cat, "exp", axis=0, tiled=True)
    gates_high = route_gates[0].astype(bf16)
    gates_low = (route_gates[0] - gates_high.astype(f32)).astype(bf16)
    pad = jnp.zeros((BLOCK, META - 3 * TOPK), bf16)
    up_meta = jnp.concatenate(
        [cotangent[0], routes[0].astype(bf16), gates_high, gates_low, pad], axis=1
    )
    up_all = lax.all_gather(after(up_meta, w_cat), "exp", axis=0, tiled=True)
    gains = after(jnp.concatenate([norm_attn, norm_ffn]), w_cat)
    gains = swap_all(jnp.broadcast_to(gains, (N_EXP, gains.shape[0])), "exp")
    gain_attn = gains[:, :96].reshape(1, WIDTH).astype(f32)
    gain_ffn = gains[:, 96:].reshape(1, WIDTH).astype(f32)
    tokens_seq = swap_all(jnp.broadcast_to(tokens, (N_CTX, BLOCK, WIDTH)), "ctx")
    shared_cols = jnp.concatenate(
        [shared_gate.reshape(96, N_EXP, SHARED), shared_up.reshape(96, N_EXP, SHARED)], axis=2
    ).transpose(1, 0, 2)
    w_shared = swap_all(shared_cols, "exp").reshape(WIDTH, 2 * SHARED)
    shared_two = jnp.concatenate([shared_down, shared_down], axis=0)

    hidden_one = norm_rows(tokens, gain_attn)
    hidden_seq = norm_rows(tokens_seq, gain_attn)
    hidden_seq = after(hidden_seq, w_shared)
    queries, kv_all = project(hidden_one, hidden_seq, w_all)
    attended, att_f, logs = attend(ctx_s, queries, kv_all)
    middle, hidden_two = middle_norm(attended, w_all, tokens[0], gain_ffn)

    hidden_all = lax.all_gather(hidden_two, "exp", axis=0, tiled=True)
    hidden_all = hidden_all.reshape(HALF, 2, BLOCK, WIDTH)
    hidden_one_all = lax.all_gather(after(hidden_one[0], hidden_two), "exp", axis=0, tiled=True)
    place, grad_eo, grad_eh, grad_sh, slot_gate = place_rows(
        exp_s,
        after(up_all, hidden_two).reshape(HALF, 2, BLOCK, WIDTH + META),
        expert_down,
        shared_two,
    )
    part, arrived, act, grad_gu, shared_act, shared_grad = expert_back(
        exp_s, hidden_all, place, grad_eh, grad_sh, expert_gate, expert_up, w_shared
    )
    summed = add_low(part[1], lax.ppermute(part[0], "exp", core_swap))
    grad_two = swap_all(summed, "exp", same_core)

    rows_e = 2 * ROWS
    p = expert_weights(
        yz_s,
        after(arrived, summed).reshape(LOCAL_E, rows_e, WIDTH),
        grad_eo.reshape(LOCAL_E, rows_e, WIDTH),
        act.reshape(LOCAL_E, rows_e, FF_E),
        grad_gu.reshape(LOCAL_E, rows_e, 2 * FF_E),
    )

    def to(rows, k):
        return lax.ppermute(rows, "ctx", [(i, i ^ k) for i in range(N_CTX)])

    relay_a, relay_b, got_10, got_31 = to(p[4], 1), to(p[5], 3), to(p[2], 1), to(p[7], 3)
    shared_grad_late = after(shared_grad, p[0]).reshape(N_EXP * BLOCK, META)
    grad_scols = dg(hidden_all.reshape(N_EXP * BLOCK, WIDTH), shared_grad_late, TN).astype(bf16)
    act_late = after(shared_act, p[0]).reshape(N_EXP * BLOCK, META)
    grad_sdown = dg(act_late, up_all, TN)[:SHARED, :WIDTH].astype(bf16)

    add_a, add_b = piece_sums(relay_kernel, (bf16, bf16), p[3], p[6], relay_a, relay_b)
    got_11, got_30 = to(add_b, 1), to(add_a, 3)
    grad_two = after(grad_two, add_a)
    grad_middle, grad_attn, grad_heads, grad_gain_ffn = middle_back(
        grad_two, middle, cotangent[0], gain_ffn, w_all
    )
    att_all = lax.all_gather(after(attended, grad_two), "exp", axis=0, tiled=True)
    grad_query, part_kv = attend_back(ctx_s, queries, grad_heads, att_f, logs, kv_all)
    kv_pieces = swap_all(part_kv, "ctx")

    out_part = expert_output(
        exp_s, after(act, part_kv), slot_gate, place, shared_act, expert_down, shared_two
    )

    grad_qkv, cols_sent = turn_cols(grad_query, kv_pieces, grad_attn)
    cols = swap_all(cols_sent, "exp")
    own_part, side = piece_sums(
        side_kernel, (f32, bf16), p[0], p[1], got_10, got_31, after(got_11, cols_sent), got_30
    )
    across = to(side, 4)
    input_grad, grad_gain_attn = input_back(
        grad_qkv, w_all, tokens[0], gain_attn, grad_middle
    )
    grad_cols = cols_grad(cols, hidden_one_all, att_all)
    gain_rows = jnp.concatenate(
        [grad_gain_attn.reshape(N_EXP, 1, 96), grad_gain_ffn.reshape(N_EXP, 1, 96)], axis=1
    ).astype(bf16)
    gain_rows = jnp.pad(gain_rows, ((0, 0), (0, 14), (0, 160)))
    sent = jnp.concatenate(
        [
            jnp.concatenate([grad_cols, gain_rows], axis=1),
            jnp.pad(grad_scols.reshape(N_EXP, 96, META), ((0, 0), (0, 16), (0, 0))),
        ],
        axis=2,
    )
    back = swap_all(sent, "exp")
    own = (own_part + after(across, sent).astype(f32)).astype(bf16)
    at_1, at_3, at_z = to(own, 1), to(own, 3), to(own, 4)
    out_other = lax.ppermute(after(out_part[0], own), "exp", core_swap)
    out_sum = add_low(out_part[1], out_other)

    small = jnp.concatenate(
        [back.reshape(N_CTX, 224, 384), grad_sdown.reshape(N_CTX, 32, 384)], axis=1
    )
    pieces = swap_all(small, "ctx")
    late_own = jnp.sum(pieces.astype(f32), axis=0).astype(bf16)
    late = swap_all(jnp.broadcast_to(late_own, (N_CTX, 256, 384)), "ctx")
    at_1, at_3, at_z = after((at_1, at_3, at_z), late_own)
    at_2, at_z1, at_z3 = to(at_3, 1), to(at_z, 1), to(at_z, 3)
    out_pieces = swap_all(after(out_sum, late_own), "exp", same_core)
    at_z2 = to(at_z1, 3)
    mixed = (middle + jnp.sum(out_pieces.astype(f32), axis=0)).astype(bf16)[None]
    grad_sdown = late[:, 224:].reshape(SHARED, WIDTH).astype(f32)
    late = late[:, :224].reshape(N_EXP, 112, 384)
    grad_wqkv = late[:, :96, :160].transpose(1, 0, 2).reshape(96, WIDTH + 2 * KV_WIDTH)
    gain_sum = jnp.sum(late[:, 96:98, :96].astype(f32), axis=0)
    dense = (
        gain_sum[0],
        gain_sum[1],
        grad_wqkv[:, :WIDTH].astype(f32),
        grad_wqkv[:, WIDTH : WIDTH + KV_WIDTH].astype(f32),
        grad_wqkv[:, WIDTH + KV_WIDTH :].astype(f32),
        late[:, :96, 160:256].transpose(1, 0, 2).reshape(96, WIDTH).astype(f32),
        late[:, :96, 256 : 256 + SHARED].transpose(1, 0, 2).reshape(96, 1024).astype(f32),
        late[:, :96, 256 + SHARED :].transpose(1, 0, 2).reshape(96, 1024).astype(f32),
        grad_sdown,
    )
    own = after(own, mixed, *dense)
    experts = unpack_experts(yz_s, (own, at_1, at_2, at_3, at_z, at_z1, at_z2, at_z3))
    return (mixed, input_grad[None]) + dense + tuple(experts)


def solution(mesh):
    token_spec = P("exp", "ctx", None)
    rows = P("exp", None)
    expert = P("exp", None, None)
    placed = (token_spec,) * 3 + (P("exp"),) * 2 + (rows,) * 7 + (expert,) * 3 + (token_spec,)
    return jax.shard_map(
        on_device,
        mesh=mesh,
        in_specs=placed,
        out_specs=(token_spec,) * 2 + (P("exp"),) * 2 + (rows,) * 7 + (expert,) * 3,
        check_vma=False,
    )
```

```python
import jax
import jax.numpy as jnp
from jax import lax
from jax.sharding import PartitionSpec as P
from jax.experimental import pallas as pl
from jax.experimental.pallas import tpu as pltpu

HEADS = 12
KV_HEADS = 4
HEAD_DIM = 128
TOPK = 6
GROUP = 3
BLOCK = 128
WIDTH = 1536
KV_WIDTH = KV_HEADS * HEAD_DIM
CAP = 48
N_EXP = 16
N_CTX = 8
LOCAL_E = 2
FF_E = 512
SHARED = 64
META = 128
HALF = 8
ROWS = HALF * CAP

epsilon = 1e-05
masked_score = -1e30
f32 = jnp.float32
bf16 = jnp.bfloat16
log2_e = 1.4426950408889634
score_scale = HEAD_DIM ** (-0.5) * log2_e

NN = (((1,), (0,)), ((), ()))
NT = (((1,), (1,)), ((), ()))
TN = (((0,), (0,)), ((), ()))


def dg(a, b, dims):
    return lax.dot_general(a, b, dims, preferred_element_type=f32)


def params(mib):
    return pltpu.CompilerParams(vmem_limit_bytes=mib * 1024 * 1024)


def cost(us):
    return pl.CostEstimate(flops=0, bytes_accessed=int(us * 3690000), transcendentals=0)


def whole(shape):
    return pl.BlockSpec(shape, lambda *_: (0,) * len(shape), pipeline_mode=pl.Buffered(1))


def sigmoid(v):
    return 1.0 / (1.0 + jnp.exp(-v))


def allowed_scores(ctx_at):
    rows = lax.broadcasted_iota(jnp.int32, (GROUP * BLOCK, N_CTX * BLOCK), 0) % BLOCK
    cols = lax.broadcasted_iota(jnp.int32, (GROUP * BLOCK, N_CTX * BLOCK), 1)
    return rows + ctx_at * BLOCK >= cols


def stack_heads(block):
    return jnp.concatenate([block[:, j * HEAD_DIM : (j + 1) * HEAD_DIM] for j in range(GROUP)], axis=0)


def unstack_heads(rows):
    return jnp.concatenate([rows[j * BLOCK : (j + 1) * BLOCK] for j in range(GROUP)], axis=1)


def attend_kernel(ctx_ref, q_ref, k_ref, v_ref, att_ref, attf_ref, log_ref):
    q = stack_heads(q_ref[...])
    keys = k_ref[...].reshape(N_CTX * BLOCK, HEAD_DIM)
    values = v_ref[...].reshape(N_CTX * BLOCK, HEAD_DIM)
    scores = jnp.where(allowed_scores(ctx_ref[0]), dg(q, keys, NT) * score_scale, masked_score)
    top = jnp.max(scores, axis=-1, keepdims=True)
    weights = jnp.exp2(scores - top)
    total = jnp.sum(weights, axis=-1, keepdims=True)
    out = dg(weights.astype(bf16), values, NN) * (1.0 / total)
    out = unstack_heads(out)
    attf_ref[...] = out
    att_ref[...] = out.astype(bf16)
    log_ref[...] = jnp.broadcast_to(top + jnp.log2(total), (GROUP * BLOCK, HEAD_DIM))


def kv_specs():
    return [
        pl.BlockSpec((N_CTX, BLOCK, HEAD_DIM), lambda g: (0, 0, g)),
        pl.BlockSpec((N_CTX, BLOCK, HEAD_DIM), lambda g: (0, 0, KV_HEADS + g)),
    ]


def head_spec():
    return pl.BlockSpec((BLOCK, GROUP * HEAD_DIM), lambda g: (0, g))


def attend(ctx_at, qkv, kv_all):
    return pl.pallas_call(
        attend_kernel,
        grid=(KV_HEADS,),
        in_specs=[pl.BlockSpec(memory_space=pltpu.SMEM), head_spec()] + kv_specs(),
        out_specs=[
            head_spec(),
            head_spec(),
            pl.BlockSpec((GROUP * BLOCK, HEAD_DIM), lambda g: (g, 0)),
        ],
        out_shape=[
            jax.ShapeDtypeStruct((BLOCK, WIDTH), bf16),
            jax.ShapeDtypeStruct((BLOCK, WIDTH), f32),
            jax.ShapeDtypeStruct((HEADS * BLOCK, HEAD_DIM), f32),
        ],
        cost_estimate=cost(6),
        compiler_params=params(48),
        name="attend",
    )(ctx_at, qkv, kv_all, kv_all)


def attend_back_kernel(
    ctx_ref, q_ref, ga_ref, attf_ref, log_ref, k_ref, v_ref, dq_ref, dkv_ref
):
    q = stack_heads(q_ref[...])
    grad = stack_heads(ga_ref[...])
    delta = jnp.sum(grad.astype(f32) * stack_heads(attf_ref[...]), axis=-1, keepdims=True)
    keys = k_ref[...].reshape(N_CTX * BLOCK, HEAD_DIM)
    values = v_ref[...].reshape(N_CTX * BLOCK, HEAD_DIM)
    scores = jnp.where(allowed_scores(ctx_ref[0]), dg(q, keys, NT) * score_scale, masked_score)
    weights = jnp.exp2(scores - log_ref[:, :1])
    grad_weights = dg(grad, values, NT)
    grad_raw = (weights * (grad_weights - delta)).astype(bf16)
    scale = HEAD_DIM ** (-0.5)
    dq_ref[...] = unstack_heads(dg(grad_raw, keys, NN) * scale).astype(bf16)
    grad_k = (dg(grad_raw, q, TN) * scale).astype(bf16)
    grad_v = dg(weights.astype(bf16), grad, TN).astype(bf16)
    dkv_ref[:, :, :HEAD_DIM] = grad_k.reshape(N_CTX, BLOCK, HEAD_DIM)
    dkv_ref[:, :, HEAD_DIM:] = grad_v.reshape(N_CTX, BLOCK, HEAD_DIM)


def attend_back(ctx_at, qkv, grad_att, att_f, logs, kv_all):
    part = pl.BlockSpec((N_CTX, BLOCK, 2 * HEAD_DIM), lambda g: (0, 0, g))
    return pl.pallas_call(
        attend_back_kernel,
        grid=(KV_HEADS,),
        in_specs=[
            pl.BlockSpec(memory_space=pltpu.SMEM),
            head_spec(),
            head_spec(),
            head_spec(),
            pl.BlockSpec((GROUP * BLOCK, HEAD_DIM), lambda g: (g, 0)),
        ]
        + kv_specs(),
        out_specs=[head_spec(), part],
        out_shape=[
            jax.ShapeDtypeStruct((BLOCK, WIDTH), bf16),
            jax.ShapeDtypeStruct((N_CTX, BLOCK, 2 * KV_WIDTH), bf16),
        ],
        cost_estimate=cost(7),
        compiler_params=params(48),
        name="attend_back",
    )(ctx_at, qkv, grad_att, att_f, logs, kv_all, kv_all)


def middle_kernel(att_ref, w_ref, x_ref, gain_ref, middle_ref, hidden_ref):
    middle = x_ref[...].astype(f32) + dg(att_ref[...], w_ref[...], NN)
    inv = lax.rsqrt(jnp.mean(middle * middle, axis=-1, keepdims=True) + epsilon)
    middle_ref[...] = middle
    hidden_ref[...] = (middle * inv * gain_ref[...]).astype(bf16)


def w_cols(width, at):
    return pl.BlockSpec((WIDTH, width), lambda *_: (0, at), pipeline_mode=pl.Buffered(1))


def middle_norm(attended, w_all, tokens, gain):
    return pl.pallas_call(
        middle_kernel,
        grid=(1,),
        in_specs=[
            whole((BLOCK, WIDTH)),
            w_cols(WIDTH, 1),
            whole((BLOCK, WIDTH)),
            whole((1, WIDTH)),
        ],
        out_specs=[whole((BLOCK, WIDTH)), whole((BLOCK, WIDTH))],
        out_shape=[
            jax.ShapeDtypeStruct((BLOCK, WIDTH), f32),
            jax.ShapeDtypeStruct((BLOCK, WIDTH), bf16),
        ],
        cost_estimate=cost(2),
        compiler_params=params(32),
        name="middle_norm",
    )(attended, w_all, tokens, gain)


def norm_back(grad_normed, normed, inv_root):
    return inv_root * (
        grad_normed - normed * jnp.mean(grad_normed * normed, axis=-1, keepdims=True)
    )


def middle_back_kernel(
    pieces_ref, middle_ref, up_ref, gain_ref, w_ref, gm_ref, ga_ref, gh_ref, gg_ref
):
    grad_two = pieces_ref[0].astype(f32)
    for i in range(1, HALF):
        grad_two = grad_two + pieces_ref[i].astype(f32)
    middle = middle_ref[...]
    inv = lax.rsqrt(jnp.mean(middle * middle, axis=-1, keepdims=True) + epsilon)
    normed = middle * inv
    gg_ref[...] = jnp.sum(grad_two * normed, axis=0, keepdims=True)
    grad_middle = up_ref[...].astype(f32) + norm_back(grad_two * gain_ref[...], normed, inv)
    gm_ref[...] = grad_middle
    grad_attn = grad_middle.astype(bf16)
    ga_ref[...] = grad_attn
    gh_ref[...] = dg(grad_attn, w_ref[...], NT).astype(bf16)


def middle_back(pieces, middle, upstream, gain, w_all):
    return pl.pallas_call(
        middle_back_kernel,
        grid=(1,),
        in_specs=[
            whole((HALF, BLOCK, WIDTH)),
            whole((BLOCK, WIDTH)),
            whole((BLOCK, WIDTH)),
            whole((1, WIDTH)),
            w_cols(WIDTH, 1),
        ],
        out_specs=[whole((BLOCK, WIDTH))] * 3 + [whole((1, WIDTH))],
        out_shape=[
            jax.ShapeDtypeStruct((BLOCK, WIDTH), f32),
            jax.ShapeDtypeStruct((BLOCK, WIDTH), bf16),
            jax.ShapeDtypeStruct((BLOCK, WIDTH), bf16),
            jax.ShapeDtypeStruct((1, WIDTH), f32),
        ],
        cost_estimate=cost(5),
        compiler_params=params(48),
        name="middle_back",
    )(pieces, middle, upstream, gain, w_all)


def place_kernel(
    at_ref, up_ref, down_ref, sdown_ref, place_ref, geo_ref, geh_ref, gsh_ref, gate_ref
):
    lane = lax.broadcasted_iota(jnp.int32, (BLOCK, META), 1)
    row = lax.broadcasted_iota(jnp.int32, (BLOCK, META), 0)
    before = (row > lane).astype(bf16)
    slot = (lane % 64).astype(f32)
    first_id = (at_ref[0] * LOCAL_E).astype(f32)
    row_id = first_id + (row >= 64).astype(f32)

    for chip in range(HALF):
        meta = up_ref[chip, 0, :, WIDTH:].astype(f32)
        named = lane < TOPK
        zero = jnp.zeros((BLOCK, META), f32)
        hit0 = jnp.where(named & (meta == first_id), 1.0, zero)
        hit1 = jnp.where(named & (meta == first_id + 1.0), 1.0, zero)
        mask = jnp.where(
            lane < 64,
            jnp.sum(hit0, axis=1, keepdims=True),
            jnp.sum(hit1, axis=1, keepdims=True),
        )
        rank = dg(before, mask.astype(bf16), NN)
        place = jnp.where((mask > 0.5) & (rank == slot), 1.0, zero).astype(bf16)
        place_ref[chip, 0] = place
        rows = dg(place, up_ref[chip, 0], TN)
        slot_meta = rows[:, WIDTH:]
        gates = pltpu.roll(slot_meta, META - TOPK, 1) + pltpu.roll(
            slot_meta, META - 2 * TOPK, 1
        )
        gate = jnp.sum(
            jnp.where(named & (slot_meta == row_id), gates, zero), axis=1, keepdims=True
        )
        geo = (gate * rows[:, :WIDTH]).astype(bf16)
        wide_gate = jnp.broadcast_to(gate, (BLOCK, META))
        at = chip * CAP
        for e in range(LOCAL_E):
            geo_ref[e, 0, at : at + CAP] = geo[64 * e : 64 * e + CAP]
            gate_ref[e, 0, at : at + CAP] = wide_gate[64 * e : 64 * e + CAP]
        gsh_ref[chip, 0] = dg(up_ref[chip, 0, :, :WIDTH], sdown_ref[...], NT)
    for e in range(LOCAL_E):
        geh_ref[e, 0] = dg(geo_ref[e, 0], down_ref[e], NT)


def by_core(cols):
    return pl.BlockSpec(
        (HALF, 1, BLOCK, cols),
        lambda s, at: (0, jnp.where(s == 0, 1 - at[0] % 2, at[0] % 2), 0, 0),
    )


def by_step(cols):
    return pl.BlockSpec((LOCAL_E, 1, ROWS, cols), lambda s, at: (0, s, 0, 0))


def place_rows(exp_at, up_all, expert_down, shared_two):
    return pl.pallas_call(
        place_kernel,
        grid_spec=pltpu.PrefetchScalarGridSpec(
            num_scalar_prefetch=1,
            grid=(2,),
            in_specs=[
                by_core(WIDTH + META),
                whole((LOCAL_E, FF_E, WIDTH)),
                whole((2 * SHARED, WIDTH)),
            ],
            out_specs=[by_core(META), by_step(WIDTH), by_step(FF_E), by_core(META), by_step(META)],
        ),
        out_shape=[
            jax.ShapeDtypeStruct((HALF, 2, BLOCK, META), bf16),
            jax.ShapeDtypeStruct((LOCAL_E, 2, ROWS, WIDTH), bf16),
            jax.ShapeDtypeStruct((LOCAL_E, 2, ROWS, FF_E), f32),
            jax.ShapeDtypeStruct((HALF, 2, BLOCK, META), f32),
            jax.ShapeDtypeStruct((LOCAL_E, 2, ROWS, META), f32),
        ],
        cost_estimate=cost(14),
        compiler_params=params(56),
        name="place_rows",
    )(exp_at, up_all, expert_down, shared_two)


def expert_kernel(
    at_ref,
    hid_ref,
    place_ref,
    geh_ref,
    gsh_ref,
    wg_ref,
    wu_ref,
    ws_ref,
    part_ref,
    x_ref,
    act_ref,
    dgu_ref,
    sact_ref,
    sgrad_ref,
):
    for chip in range(HALF):
        rows = dg(place_ref[chip, 0], hid_ref[chip, 0], TN).astype(bf16)
        at = chip * CAP
        for e in range(LOCAL_E):
            x_ref[e, 0, at : at + CAP] = rows[64 * e : 64 * e + CAP]
    pairs = []
    for e in range(LOCAL_E):
        pre_gate = dg(x_ref[e, 0], wg_ref[e], NN)
        pre_up = dg(x_ref[e, 0], wu_ref[e], NN)
        sig = sigmoid(pre_gate)
        act = pre_gate * sig
        act_ref[e, 0] = (act * pre_up).astype(bf16)
        geh = geh_ref[e, 0]
        d_gate = (geh * pre_up * (sig * (1.0 + pre_gate * (1.0 - sig)))).astype(bf16)
        d_up = (geh * act).astype(bf16)
        dgu_ref[e, 0, :, :FF_E] = d_gate
        dgu_ref[e, 0, :, FF_E:] = d_up
        pairs.append((dg(d_gate, wg_ref[e], NT) + dg(d_up, wu_ref[e], NT)).astype(bf16))
    lane = lax.broadcasted_iota(jnp.int32, (BLOCK, 2 * SHARED), 1) < SHARED
    gap = jnp.zeros((64 - CAP, WIDTH), bf16)
    for chip in range(HALF):
        pre = dg(hid_ref[chip, 0], ws_ref[...], NN)
        turned = pltpu.roll(pre, SHARED, 1)
        gate, up = jnp.where(lane, pre, turned), jnp.where(lane, turned, pre)
        sig = sigmoid(gate)
        act = gate * sig
        sact_ref[chip, 0] = jnp.where(lane, act * up, 0.0).astype(bf16)
        slope = sig * (1.0 + gate * (1.0 - sig))
        sgrad = (gsh_ref[chip, 0] * jnp.where(lane, up * slope, act)).astype(bf16)
        sgrad_ref[chip, 0] = sgrad
        at = chip * CAP
        stacked = jnp.concatenate([pairs[0][at : at + CAP], gap, pairs[1][at : at + CAP], gap], 0)
        part_ref[0, chip] = (
            dg(place_ref[chip, 0], stacked, NN) + dg(sgrad, ws_ref[...], NT)
        ).astype(bf16)


def expert_back(exp_at, hidden, place, geh, gsh, wg, wu, ws):
    return pl.pallas_call(
        expert_kernel,
        grid_spec=pltpu.PrefetchScalarGridSpec(
            num_scalar_prefetch=1,
            grid=(2,),
            in_specs=[
                by_core(WIDTH),
                by_core(META),
                by_step(FF_E),
                by_core(META),
                whole((LOCAL_E, WIDTH, FF_E)),
                whole((LOCAL_E, WIDTH, FF_E)),
                whole((WIDTH, 2 * SHARED)),
            ],
            out_specs=[
                pl.BlockSpec((1, HALF, BLOCK, WIDTH), lambda s, at: (s, 0, 0, 0)),
                by_step(WIDTH),
                by_step(FF_E),
                by_step(2 * FF_E),
                by_core(META),
                by_core(META),
            ],
        ),
        out_shape=[
            jax.ShapeDtypeStruct((2, HALF, BLOCK, WIDTH), bf16),
            jax.ShapeDtypeStruct((LOCAL_E, 2, ROWS, WIDTH), bf16),
            jax.ShapeDtypeStruct((LOCAL_E, 2, ROWS, FF_E), bf16),
            jax.ShapeDtypeStruct((LOCAL_E, 2, ROWS, 2 * FF_E), bf16),
            jax.ShapeDtypeStruct((HALF, 2, BLOCK, META), bf16),
            jax.ShapeDtypeStruct((HALF, 2, BLOCK, META), bf16),
        ],
        cost_estimate=cost(28),
        compiler_params=params(60),
        name="expert_back",
    )(exp_at, hidden, place, geh, gsh, wg, wu, ws)


def output_kernel(at_ref, act_ref, gate_ref, place_ref, sact_ref, wd_ref, sd_ref, part_ref):
    outs = []
    for e in range(LOCAL_E):
        out = dg(act_ref[e, 0], wd_ref[e], NN).astype(bf16).astype(f32)
        outs.append((out * gate_ref[e, 0, :, :1]).astype(bf16))
    gap = jnp.zeros((64 - CAP, WIDTH), bf16)
    for chip in range(HALF):
        at = chip * CAP
        stacked = jnp.concatenate([outs[0][at : at + CAP], gap, outs[1][at : at + CAP], gap], 0)
        part_ref[chip, 0] = (
            dg(place_ref[chip, 0], stacked, NN) + dg(sact_ref[chip, 0], sd_ref[...], NN)
        ).astype(bf16)


def expert_output(exp_at, act, gate, place, sact, wd, sd):
    return pl.pallas_call(
        output_kernel,
        grid_spec=pltpu.PrefetchScalarGridSpec(
            num_scalar_prefetch=1,
            grid=(2,),
            in_specs=[
                by_step(FF_E),
                by_step(META),
                by_core(META),
                by_core(META),
                whole((LOCAL_E, FF_E, WIDTH)),
                whole((2 * SHARED, WIDTH)),
            ],
            out_specs=by_core(WIDTH),
        ),
        out_shape=jax.ShapeDtypeStruct((HALF, 2, BLOCK, WIDTH), bf16),
        cost_estimate=cost(10),
        compiler_params=params(48),
        name="expert_output",
    )(exp_at, act, gate, place, sact, wd, sd)


def turn_kernel(dq_ref, pieces_ref, ga_ref, gqkv_ref, cols_ref):
    total = pieces_ref[0].astype(f32)
    for i in range(1, N_CTX):
        total = total + pieces_ref[i].astype(f32)
    total = total.astype(bf16)
    parts = [total[:, i * HEAD_DIM : (i + 1) * HEAD_DIM] for i in range(2 * KV_HEADS)]
    grad_kv = jnp.concatenate(parts[0::2] + parts[1::2], axis=1)
    gqkv_ref[:, :WIDTH] = dq_ref[...]
    gqkv_ref[:, WIDTH:] = grad_kv
    turned = jnp.concatenate([dq_ref[...].T, grad_kv.T], axis=0)
    turned_out = ga_ref[...].T
    for j in range(N_EXP):
        cols_ref[j, :128] = turned[128 * j : 128 * j + 128]
        cols_ref[j, 128:160] = turned[2048 + 32 * j : 2048 + 32 * j + 32]
        cols_ref[j, 160:192] = turned_out[1024 + 32 * j : 1024 + 32 * j + 32]
        cols_ref[j, 192:] = turned_out[64 * j : 64 * j + 64]


def turn_cols(dq, pieces, grad_attn):
    return pl.pallas_call(
        turn_kernel,
        out_shape=[
            jax.ShapeDtypeStruct((BLOCK, WIDTH + 2 * KV_WIDTH), bf16),
            jax.ShapeDtypeStruct((N_EXP, 256, BLOCK), bf16),
        ],
        cost_estimate=cost(2),
        compiler_params=params(32),
        name="turn_cols",
    )(dq, pieces, grad_attn)


def input_kernel(gqkv_ref, wq_ref, wkv_ref, x_ref, gain_ref, gm_ref, out_ref, gg_ref):
    grad_one = dg(gqkv_ref[:, :WIDTH], wq_ref[...], NT) + dg(gqkv_ref[:, WIDTH:], wkv_ref[...], NT)
    inputs = x_ref[...].astype(f32)
    inv = lax.rsqrt(jnp.mean(inputs * inputs, axis=-1, keepdims=True) + epsilon)
    normed = inputs * inv
    gg_ref[...] = jnp.sum(grad_one * normed, axis=0, keepdims=True)
    out_ref[...] = (gm_ref[...] + norm_back(grad_one * gain_ref[...], normed, inv)).astype(bf16)


def input_back(grad_qkv, w_all, tokens, gain, grad_middle):
    return pl.pallas_call(
        input_kernel,
        grid=(1,),
        in_specs=[
            whole((BLOCK, WIDTH + 2 * KV_WIDTH)),
            w_cols(WIDTH, 0),
            w_cols(2 * KV_WIDTH, 3),
            whole((BLOCK, WIDTH)),
            whole((1, WIDTH)),
            whole((BLOCK, WIDTH)),
        ],
        out_specs=[whole((BLOCK, WIDTH)), whole((1, WIDTH))],
        out_shape=[
            jax.ShapeDtypeStruct((BLOCK, WIDTH), bf16),
            jax.ShapeDtypeStruct((1, WIDTH), f32),
        ],
        cost_estimate=cost(7),
        compiler_params=params(48),
        name="input_back",
    )(grad_qkv, w_all, w_all, tokens, gain, grad_middle)


def cols_kernel(cols_ref, rows_ref, gain_ref, shared_ref, out_ref):
    lhs = jnp.concatenate([cols_ref[j] for j in range(N_EXP)], axis=1)
    row = lax.broadcasted_iota(jnp.int32, (256, N_EXP * BLOCK), 0)
    zero = jnp.zeros_like(lhs)
    attn = dg(jnp.where(row < 160, lhs, zero), rows_ref[:, :WIDTH], NN)
    out = dg(jnp.where(row < 160, zero, lhs), rows_ref[:, WIDTH:], NN)
    out_ref[:, :96, :256] = (attn + out).T.astype(bf16).reshape(N_EXP, 96, 256)
    out_ref[:, 96:, :256] = gain_ref[...]
    out_ref[:, :96, 256:] = shared_ref[...]
    out_ref[:, 96:, 256:] = jnp.zeros((N_EXP, 16, META), bf16)


def cols_grad(cols, rows_all, gain_rows, shared_cols):
    return pl.pallas_call(
        cols_kernel,
        out_shape=jax.ShapeDtypeStruct((N_EXP, 112, 384), bf16),
        cost_estimate=cost(9),
        compiler_params=params(56),
        name="cols_grad",
    )(cols, rows_all, gain_rows, shared_cols)


def finish_kernel(late_ref, gain_ref, q_ref, k_ref, v_ref, out_ref, sg_ref, su_ref, sd_ref):
    lane = lax.broadcasted_iota(jnp.int32, (96, 128), 1)

    def tile(j, m):
        return late_ref[j // 2, 112 * (j % 2) : 112 * (j % 2) + 96, 128 * m : 128 * m + 128].astype(
            f32
        )

    def half(a, b, first):
        if first:
            return jnp.where(lane < 64, a, pltpu.roll(b, 64, 1))
        return jnp.where(lane < 64, pltpu.roll(a, 64, 1), b)

    def quarter(tiles, start):
        total = jnp.zeros((96, 128), f32)
        for i, one in enumerate(tiles):
            shift = (32 * i - start) % 128
            moved = one if shift == 0 else pltpu.roll(one, shift, 1)
            total = jnp.where((lane >= 32 * i) & (lane < 32 * i + 32), moved, total)
        return total

    gains = jnp.zeros((16, 128), f32)
    for j in range(N_EXP):
        at = 112 * (j % 2) + 96
        gains = gains + late_ref[j // 2, at : at + 16, :128].astype(f32)
        whole_tile = tile(j, 0)
        if j < 12:
            q_ref[:, 128 * j : 128 * j + 128] = whole_tile
        else:
            k_ref[:, 128 * (j - 12) : 128 * (j - 12) + 128] = whole_tile
    gain_ref[...] = gains
    for m in range(N_EXP // 2):
        at = 128 * m
        a, b = tile(2 * m, 2), tile(2 * m + 1, 2)
        sg_ref[:, at : at + 128] = half(a, b, True)
        su_ref[:, at : at + 128] = half(a, b, False)
        out_ref[:, at : at + 128] = half(tile(2 * m, 1), tile(2 * m + 1, 1), False)
    for m in range(N_EXP // 4):
        at = 128 * m
        tiles = [tile(4 * m + i, 1) for i in range(4)]
        v_ref[:, at : at + 128] = quarter(tiles, 0)
        out_ref[:, 1024 + at : 1024 + at + 128] = quarter(tiles, 32)
    for c in range(N_CTX):
        rows = late_ref[c, 224:].astype(f32)
        for q in range(4):
            sd_ref[8 * c : 8 * c + 8, 384 * q : 384 * q + 384] = rows[8 * q : 8 * q + 8]


def finish(late):
    shapes = [(16, 128), (96, 1536), (96, 512), (96, 512), (96, 1536), (96, 1024), (96, 1024)]
    return pl.pallas_call(
        finish_kernel,
        out_shape=[jax.ShapeDtypeStruct(s, f32) for s in shapes + [(SHARED, WIDTH)]],
        cost_estimate=cost(5),
        compiler_params=params(32),
        name="finish",
    )(late)


def norm_rows_kernel(x_ref, gain_ref, out_ref):
    inputs = x_ref[0].astype(f32)
    inv = lax.rsqrt(jnp.mean(inputs * inputs, axis=-1, keepdims=True) + epsilon)
    out_ref[0] = (inputs * inv * gain_ref[...]).astype(bf16)


def norm_rows(rows, gain):
    count = rows.shape[0]
    spec = pl.BlockSpec((1, BLOCK, WIDTH), lambda i: (i, 0, 0))
    turned = pl.BlockSpec((1, BLOCK, WIDTH), lambda i: ((i % 2) * 4 + i // 2, 0, 0))
    return pl.pallas_call(
        norm_rows_kernel,
        grid=(count,),
        in_specs=[spec, whole((1, WIDTH))],
        out_specs=spec if count == 1 else turned,
        out_shape=jax.ShapeDtypeStruct(rows.shape, bf16),
        cost_estimate=cost(2),
        compiler_params=params(32),
        name="norm_rows",
    )(rows, gain)


def project_kernel(own_ref, seq_ref, w_ref, q_ref, kv_ref):
    step = pl.program_id(0)

    @pl.when(step < 3)
    def _():
        q_ref[...] = dg(own_ref[0], w_ref[...], NN).astype(bf16)

    @pl.when(step >= 3)
    def _():
        rows = seq_ref[...].reshape(N_CTX * BLOCK, WIDTH)
        kv_ref[...] = dg(rows, w_ref[...], NN).astype(bf16).reshape(N_CTX, BLOCK, KV_WIDTH)


def project(own, seq, w_all):
    return pl.pallas_call(
        project_kernel,
        grid=(5,),
        in_specs=[
            whole((1, BLOCK, WIDTH)),
            whole((N_CTX, BLOCK, WIDTH)),
            pl.BlockSpec((WIDTH, KV_WIDTH), lambda i: (0, jnp.where(i < 3, i, i + 3))),
        ],
        out_specs=[
            pl.BlockSpec((BLOCK, KV_WIDTH), lambda i: (0, jnp.minimum(i, 2))),
            pl.BlockSpec((N_CTX, BLOCK, KV_WIDTH), lambda i: (0, 0, jnp.maximum(i - 3, 0))),
        ],
        out_shape=[
            jax.ShapeDtypeStruct((BLOCK, WIDTH), bf16),
            jax.ShapeDtypeStruct((N_CTX, BLOCK, 2 * KV_WIDTH), bf16),
        ],
        cost_estimate=cost(8),
        compiler_params=params(48),
        name="project",
    )(own, seq, w_all)


PIECE = 2 * WIDTH + WIDTH * BLOCK // HEAD_DIM


def expert_weights_kernel(
    halves, at_ref, x_ref, geo_ref, act_ref, dgate_ref, dup_ref, *refs
):
    outs, turned = refs[:-1], refs[-1]
    step = pl.program_id(0)

    @pl.when(step % 2 == 0)
    def _():
        turned[...] = x_ref[0].T

    rhs = jnp.concatenate([dgate_ref[0], dup_ref[0]], axis=1)
    both = dg(turned[...], rhs, NN).astype(bf16)
    down = dg(act_ref[0], geo_ref[0], TN).astype(bf16)
    for i in range(4):

        @pl.when(step == i)
        def _():
            start = (i % 2) * PIECE if halves else 0
            out = outs[i // 2 if halves else i].at[pl.ds(start, PIECE)]
            out[:WIDTH] = both[:, :HEAD_DIM]
            out[WIDTH : 2 * WIDTH] = both[:, HEAD_DIM:]
            for m in range(WIDTH // HEAD_DIM):
                at = 2 * WIDTH + m * BLOCK
                out[at : at + BLOCK] = down[:, m * HEAD_DIM : (m + 1) * HEAD_DIM]


def expert_weights(yz, steps, halves, arrived, grad_eo, act, grad_gu):
    rows = 2 * ROWS
    at = jnp.stack([yz[0] ^ r for r, _ in steps] + [yz[1] ^ side for _, side in steps])
    rows_of = pl.BlockSpec((1, rows, WIDTH), lambda s, at: (at[4 + s], 0, 0))

    def lanes(shift):
        return pl.BlockSpec((1, rows, HEAD_DIM), lambda s, at: (at[4 + s], 0, shift + at[s]))

    count, length = (2, 2 * PIECE) if halves else (4, PIECE)
    return pl.pallas_call(
        lambda *refs: expert_weights_kernel(halves, *refs),
        grid_spec=pltpu.PrefetchScalarGridSpec(
            num_scalar_prefetch=1,
            grid=(4,),
            in_specs=[rows_of, rows_of, lanes(0), lanes(0), lanes(4)],
            out_specs=[whole((length, HEAD_DIM))] * count,
            scratch_shapes=[pltpu.VMEM((WIDTH, rows), bf16)],
        ),
        out_shape=[jax.ShapeDtypeStruct((length, HEAD_DIM), bf16)] * count,
        cost_estimate=cost(9),
        compiler_params=params(56),
        name="expert_weights",
    )(at, arrived, grad_eo, act, grad_gu, grad_gu)


def unpack_kernel(at_ref, *refs):
    pieces, (gate_ref, up_ref, down_ref) = refs[:4], refs[-3:]
    step = pl.program_id(0)
    for i in range(4):

        @pl.when(step == i)
        def _():
            piece = pieces[i]
            gate_ref[0] = piece[:WIDTH].astype(f32)
            up_ref[0] = piece[WIDTH : 2 * WIDTH].astype(f32)
            for m in range(WIDTH // HEAD_DIM):
                at = 2 * WIDTH + m * BLOCK
                down_ref[0, :, m * HEAD_DIM : (m + 1) * HEAD_DIM] = piece[at : at + BLOCK].astype(
                    f32
                )


def unpack_experts(at, side, pieces, filled=()):
    cols = pl.BlockSpec((1, WIDTH, HEAD_DIM), lambda s, at: (at[1] ^ side, 0, at[0] ^ s))
    rows = pl.BlockSpec((1, BLOCK, WIDTH), lambda s, at: (at[1] ^ side, at[0] ^ s, 0))
    anywhere = pl.BlockSpec(memory_space=pl.ANY)
    return pl.pallas_call(
        unpack_kernel,
        grid_spec=pltpu.PrefetchScalarGridSpec(
            num_scalar_prefetch=1,
            grid=(4,),
            in_specs=[whole((PIECE, HEAD_DIM))] * 4 + [anywhere] * len(filled),
            out_specs=[cols, cols, rows],
        ),
        out_shape=[
            jax.ShapeDtypeStruct((LOCAL_E, WIDTH, FF_E), f32),
            jax.ShapeDtypeStruct((LOCAL_E, WIDTH, FF_E), f32),
            jax.ShapeDtypeStruct((LOCAL_E, FF_E, WIDTH), f32),
        ],
        input_output_aliases={5 + i: i for i in range(len(filled))},
        cost_estimate=cost(5),
        compiler_params=params(48),
        name="unpack_experts",
    )(at, *pieces, *filled)


def relay_kernel(
    p0, p1, p3, p6, relay_a, relay_b, got_10, got_31, add_a, add_b, part_0, part_1
):
    add_a[...] = (p6[...].astype(f32) + relay_a[...].astype(f32)).astype(bf16)
    add_b[...] = (p3[...].astype(f32) + relay_b[...].astype(f32)).astype(bf16)
    part_0[...] = p0[...].astype(f32) + got_10[...].astype(f32)
    part_1[...] = p1[...].astype(f32) + got_31[...].astype(f32)


def side_kernel(part_0, part_1, got_11, got_30, own, side):
    own[...] = part_0[...] + got_30[...].astype(f32)
    side[...] = (part_1[...] + got_11[...].astype(f32)).astype(bf16)


def piece_sums(kernel, kinds, *pieces):
    specs, arrays = [], []
    for piece in pieces:
        array, second = piece if isinstance(piece, tuple) else (piece, 0)
        specs.append(pl.BlockSpec((PIECE // 4, HEAD_DIM), lambda i, at=4 * second: (i + at, 0)))
        arrays.append(array)
    return pl.pallas_call(
        kernel,
        grid=(4,),
        in_specs=specs,
        out_specs=[pl.BlockSpec((PIECE // 4, HEAD_DIM), lambda i: (i, 0))] * len(kinds),
        out_shape=[jax.ShapeDtypeStruct((PIECE, HEAD_DIM), kind) for kind in kinds],
        cost_estimate=cost(4),
        compiler_params=params(32),
        name="piece_sums",
    )(*arrays)


same_core = [[2 * i + c for i in range(8)] for c in range(2)]
core_swap = [(i, i ^ 1) for i in range(N_EXP)]
y_groups = [[0, 1, 2, 3], [4, 5, 6, 7]]
z_swap = [(i, i ^ 4) for i in range(N_CTX)]


def swap_all(rows, axis, groups=None):
    return lax.all_to_all(
        rows, axis, split_axis=0, concat_axis=0, tiled=True, axis_index_groups=groups
    )


def after(value, *others):
    return lax.optimization_barrier((value,) + others)[0]


def add_low(a, b):
    return (a.astype(f32) + b.astype(f32)).astype(bf16)


def on_device(
    tokens,
    routes,
    route_gates,
    norm_attn,
    norm_ffn,
    query_weight,
    key_weight,
    value_weight,
    out_weight,
    shared_gate,
    shared_up,
    shared_down,
    expert_gate,
    expert_up,
    expert_down,
    cotangent,
):
    exp_at = lax.axis_index("exp").astype(jnp.int32)
    ctx_at = lax.axis_index("ctx").astype(jnp.int32)
    exp_s, ctx_s = exp_at.reshape(1), ctx_at.reshape(1)

    y_at, z_at = ctx_at % 4, ctx_at // 4
    yz_s = jnp.stack([y_at, z_at])

    w_cat = jnp.concatenate([query_weight, out_weight, key_weight, value_weight], axis=1)
    w_all = lax.all_gather(w_cat, "exp", axis=0, tiled=True)
    gates_high = route_gates[0].astype(bf16)
    gates_low = (route_gates[0] - gates_high.astype(f32)).astype(bf16)
    pad = jnp.zeros((BLOCK, META - 3 * TOPK), bf16)
    up_meta = jnp.concatenate(
        [cotangent[0], routes[0].astype(bf16), gates_high, gates_low, pad], axis=1
    )
    up_all = lax.all_gather(after(up_meta, w_cat), "exp", axis=0, tiled=True)
    gains = after(jnp.concatenate([norm_attn, norm_ffn]), w_cat)
    gains = swap_all(jnp.broadcast_to(gains, (N_EXP, gains.shape[0])), "exp")
    gain_attn = gains[:, :96].reshape(1, WIDTH).astype(f32)
    gain_ffn = gains[:, 96:].reshape(1, WIDTH).astype(f32)
    tokens_z = lax.ppermute(after(tokens, w_cat), "ctx", z_swap)
    pair = jnp.where(
        z_at == 0,
        jnp.concatenate([tokens, tokens_z], axis=0),
        jnp.concatenate([tokens_z, tokens], axis=0),
    )
    tokens_seq = swap_all(jnp.broadcast_to(pair, (4, 2, BLOCK, WIDTH)), "ctx", y_groups)
    tokens_seq = tokens_seq.reshape(N_CTX, BLOCK, WIDTH)
    shared_cols = jnp.concatenate(
        [shared_gate.reshape(96, N_EXP, SHARED), shared_up.reshape(96, N_EXP, SHARED)], axis=2
    ).transpose(1, 0, 2)
    w_shared = swap_all(shared_cols, "exp").reshape(WIDTH, 2 * SHARED)
    shared_two = jnp.concatenate([shared_down, shared_down], axis=0)

    hidden_one = norm_rows(tokens, gain_attn)
    hidden_seq = norm_rows(tokens_seq, gain_attn)
    hidden_seq = after(hidden_seq, w_shared)
    queries, kv_all = project(hidden_one, hidden_seq, w_all)
    attended, att_f, logs = attend(ctx_s, queries, kv_all)
    middle, hidden_two = middle_norm(attended, w_all, tokens[0], gain_ffn)

    hidden_all = lax.all_gather(hidden_two, "exp", axis=0, tiled=True)
    hidden_all = hidden_all.reshape(HALF, 2, BLOCK, WIDTH)
    rows_all = lax.all_gather(
        after(jnp.concatenate([hidden_one[0], attended], axis=1), hidden_two),
        "exp",
        axis=0,
        tiled=True,
    )
    place, grad_eo, grad_eh, grad_sh, slot_gate = place_rows(
        exp_s,
        after(up_all, hidden_two).reshape(HALF, 2, BLOCK, WIDTH + META),
        expert_down,
        shared_two,
    )
    part, arrived, act, grad_gu, shared_act, shared_grad = expert_back(
        exp_s, hidden_all, place, grad_eh, grad_sh, expert_gate, expert_up, w_shared
    )
    summed = add_low(part[1], lax.ppermute(part[0], "exp", core_swap))
    grad_two = swap_all(summed, "exp", same_core)

    rows_e = 2 * ROWS
    operands = (
        after(arrived, summed).reshape(LOCAL_E, rows_e, WIDTH),
        grad_eo.reshape(LOCAL_E, rows_e, WIDTH),
        act.reshape(LOCAL_E, rows_e, FF_E),
        grad_gu.reshape(LOCAL_E, rows_e, 2 * FF_E),
    )
    for_1, for_3 = expert_weights(yz_s, ((2, 0), (1, 0), (2, 1), (3, 1)), True, *operands)
    operands = (after(operands[0], for_1),) + operands[1:]
    p0, p6, p1, p3 = expert_weights(yz_s, ((0, 0), (3, 0), (0, 1), (1, 1)), False, *operands)

    def to(rows, k):
        return lax.ppermute(rows, "ctx", [(i, i ^ k) for i in range(N_CTX)])

    from_1, from_3 = to(for_1, 1), to(for_3, 3)
    shared_grad_late = after(shared_grad, p0).reshape(N_EXP * BLOCK, META)
    grad_scols = dg(hidden_all.reshape(N_EXP * BLOCK, WIDTH), shared_grad_late, TN).astype(bf16)
    act_late = after(shared_act, p0).reshape(N_EXP * BLOCK, META)
    grad_sdown = dg(act_late, up_all, TN)[:SHARED, :WIDTH].astype(bf16)

    out_part = expert_output(
        exp_s, after(act, p0), slot_gate, place, shared_act, expert_down, shared_two
    )

    grad_two = after(grad_two, out_part)
    grad_middle, grad_attn, grad_heads, grad_gain_ffn = middle_back(
        grad_two, middle, cotangent[0], gain_ffn, w_all
    )
    grad_query, part_kv = attend_back(ctx_s, queries, grad_heads, att_f, logs, kv_all)

    from_1, from_3 = after((from_1, from_3), grad_heads)
    add_a, add_b, part_0, part_1 = piece_sums(
        relay_kernel,
        (bf16, bf16, f32, f32),
        p0,
        p1,
        p3,
        p6,
        (from_1, 0),
        (from_3, 0),
        (from_1, 1),
        (from_3, 1),
    )
    got_11, got_30 = to(add_b, 1), to(add_a, 3)
    kv_pieces = swap_all(after(part_kv, add_a), "ctx")

    grad_qkv, cols_sent = turn_cols(grad_query, kv_pieces, grad_attn)
    cols = swap_all(cols_sent, "exp")
    input_grad, grad_gain_attn = input_back(
        grad_qkv, w_all, tokens[0], gain_attn, grad_middle
    )
    cols = after(cols, input_grad)
    own_part, side = piece_sums(
        side_kernel, (f32, bf16), part_0, part_1, after(got_11, cols), got_30
    )
    across = to(side, 4)
    gain_rows = jnp.concatenate(
        [grad_gain_attn.reshape(N_EXP, 1, 96), grad_gain_ffn.reshape(N_EXP, 1, 96)], axis=1
    ).astype(bf16)
    gain_rows = jnp.pad(gain_rows, ((0, 0), (0, 14), (0, 160)))
    sent = cols_grad(
        after(cols, side),
        rows_all,
        gain_rows,
        grad_scols.reshape(N_EXP, 96, META),
    )
    back = swap_all(sent, "exp")
    own = (own_part + after(across, sent).astype(f32)).astype(bf16)
    at_1, at_3, at_z = to(own, 1), to(own, 3), to(own, 4)

    sdown_rows = grad_sdown.reshape(N_CTX, 8, 4, 384).transpose(0, 2, 1, 3)
    small = jnp.concatenate(
        [back.reshape(N_CTX, 224, 384), sdown_rows.reshape(N_CTX, 32, 384)], axis=1
    )
    small, at_1, at_3, at_z = lax.optimization_barrier((small, at_1, at_3, at_z))
    pieces = swap_all(small, "ctx")
    at_z1, at_z3 = to(at_z, 1), to(at_z, 3)
    late_own = jnp.sum(pieces.astype(f32), axis=0).astype(bf16)
    late_own, at_z1, at_z3 = lax.optimization_barrier((late_own, at_z1, at_z3))
    late = swap_all(jnp.broadcast_to(late_own, (N_CTX, 256, 384)), "ctx")
    at_2, at_z2 = to(after(at_3, late_own), 1), to(at_z1, 3)
    gain_sum, *dense = finish(late)
    out_rows = lax.psum_scatter(
        after(out_part, own).reshape(N_EXP * BLOCK, WIDTH), "exp", scatter_dimension=0, tiled=True
    )
    mixed = (middle + out_rows.astype(f32)).astype(bf16)[None]
    near = unpack_experts(yz_s, 0, after((own, at_1, at_2, at_3), mixed, *dense))
    experts = unpack_experts(yz_s, 1, (at_z, at_z1, at_z2, at_z3), near)
    return (mixed, input_grad[None], gain_sum[0, :96], gain_sum[1, :96], *dense, *experts)


def solution(mesh):
    token_spec = P("exp", "ctx", None)
    rows = P("exp", None)
    expert = P("exp", None, None)
    placed = (token_spec,) * 3 + (P("exp"),) * 2 + (rows,) * 7 + (expert,) * 3 + (token_spec,)
    return jax.shard_map(
        on_device,
        mesh=mesh,
        in_specs=placed,
        out_specs=(token_spec,) * 2 + (P("exp"),) * 2 + (rows,) * 7 + (expert,) * 3,
        check_vma=False,
    )
```

```python
import jax
import jax.numpy as jnp
from jax import lax
from jax.sharding import PartitionSpec as P
from jax.experimental import pallas as pl
from jax.experimental.pallas import tpu as pltpu

HEADS = 12
KV_HEADS = 4
HEAD_DIM = 128
TOPK = 6
GROUP = 3
BLOCK = 128
WIDTH = 1536
KV_WIDTH = KV_HEADS * HEAD_DIM
CAP = 48
N_EXP = 16
N_CTX = 8
LOCAL_E = 2
FF_E = 512
SHARED = 64
META = 128
HALF = 8
ROWS = HALF * CAP

epsilon = 1e-05
masked_score = -1e30
f32 = jnp.float32
bf16 = jnp.bfloat16
log2_e = 1.4426950408889634
score_scale = HEAD_DIM ** (-0.5) * log2_e

NN = (((1,), (0,)), ((), ()))
NT = (((1,), (1,)), ((), ()))
TN = (((0,), (0,)), ((), ()))


def dg(a, b, dims):
    return lax.dot_general(a, b, dims, preferred_element_type=f32)


def params(mib):
    return pltpu.CompilerParams(vmem_limit_bytes=mib * 1024 * 1024)


def cost(us):
    return pl.CostEstimate(flops=0, bytes_accessed=int(us * 3690000), transcendentals=0)


def whole(shape):
    return pl.BlockSpec(shape, lambda *_: (0,) * len(shape), pipeline_mode=pl.Buffered(1))


def sigmoid(v):
    return 1.0 / (1.0 + jnp.exp(-v))


def allowed_scores(ctx_at):
    rows = lax.broadcasted_iota(jnp.int32, (GROUP * BLOCK, N_CTX * BLOCK), 0) % BLOCK
    cols = lax.broadcasted_iota(jnp.int32, (GROUP * BLOCK, N_CTX * BLOCK), 1)
    return rows + ctx_at * BLOCK >= cols


def stack_heads(block):
    return jnp.concatenate([block[:, j * HEAD_DIM : (j + 1) * HEAD_DIM] for j in range(GROUP)], axis=0)


def unstack_heads(rows):
    return jnp.concatenate([rows[j * BLOCK : (j + 1) * BLOCK] for j in range(GROUP)], axis=1)


def attend_kernel(ctx_ref, q_ref, k_ref, v_ref, att_ref, attf_ref, log_ref):
    q = stack_heads(q_ref[...])
    keys = k_ref[...].reshape(N_CTX * BLOCK, HEAD_DIM)
    values = v_ref[...].reshape(N_CTX * BLOCK, HEAD_DIM)
    scores = jnp.where(allowed_scores(ctx_ref[0]), dg(q, keys, NT) * score_scale, masked_score)
    top = jnp.max(scores, axis=-1, keepdims=True)
    weights = jnp.exp2(scores - top)
    total = jnp.sum(weights, axis=-1, keepdims=True)
    out = dg(weights.astype(bf16), values, NN) * (1.0 / total)
    out = unstack_heads(out)
    attf_ref[...] = out
    att_ref[...] = out.astype(bf16)
    log_ref[...] = jnp.broadcast_to(top + jnp.log2(total), (GROUP * BLOCK, HEAD_DIM))


def kv_specs():
    return [
        pl.BlockSpec((N_CTX, BLOCK, HEAD_DIM), lambda g: (0, 0, g)),
        pl.BlockSpec((N_CTX, BLOCK, HEAD_DIM), lambda g: (0, 0, KV_HEADS + g)),
    ]


def head_spec():
    return pl.BlockSpec((BLOCK, GROUP * HEAD_DIM), lambda g: (0, g))


def attend(ctx_at, qkv, kv_all):
    return pl.pallas_call(
        attend_kernel,
        grid=(KV_HEADS,),
        in_specs=[pl.BlockSpec(memory_space=pltpu.SMEM), head_spec()] + kv_specs(),
        out_specs=[
            head_spec(),
            head_spec(),
            pl.BlockSpec((GROUP * BLOCK, HEAD_DIM), lambda g: (g, 0)),
        ],
        out_shape=[
            jax.ShapeDtypeStruct((BLOCK, WIDTH), bf16),
            jax.ShapeDtypeStruct((BLOCK, WIDTH), f32),
            jax.ShapeDtypeStruct((HEADS * BLOCK, HEAD_DIM), f32),
        ],
        cost_estimate=cost(6),
        compiler_params=params(48),
        name="attend",
    )(ctx_at, qkv, kv_all, kv_all)


SEQ = N_CTX * BLOCK
AT_QUERY, AT_MIXED, AT_OUT = SEQ, SEQ + BLOCK, SEQ + 2 * BLOCK
AT_SHARED = SEQ + 3 * BLOCK
AT_DOWN = AT_SHARED + 16 * N_EXP
AT_GAIN = AT_DOWN + 96
SENT_ROWS = AT_GAIN + 16


def halves(a, b, lane):
    low = jnp.where(lane < 64, a, pltpu.roll(b, 64, 1))
    high = jnp.where(lane < 64, pltpu.roll(a, 64, 1), b)
    return low, high


def attend_back_kernel(
    ctx_ref,
    q_ref,
    ga_ref,
    attf_ref,
    log_ref,
    k_ref,
    v_ref,
    all_ga_ref,
    extra_ref,
    gain_ref,
    dq_ref,
    sent_ref,
    kept_ref,
):
    group = pl.program_id(0)
    q = stack_heads(q_ref[...])
    grad = stack_heads(ga_ref[...])
    delta = jnp.sum(grad.astype(f32) * stack_heads(attf_ref[...]), axis=-1, keepdims=True)
    keys = k_ref[...].reshape(SEQ, HEAD_DIM)
    values = v_ref[...].reshape(SEQ, HEAD_DIM)
    scores = jnp.where(allowed_scores(ctx_ref[0]), dg(q, keys, NT) * score_scale, masked_score)
    weights = jnp.exp2(scores - log_ref[:, :1])
    grad_weights = dg(grad, values, NT)
    grad_raw = (weights * (grad_weights - delta)).astype(bf16)
    scale = HEAD_DIM ** (-0.5)
    dq = unstack_heads(dg(grad_raw, keys, NN) * scale)
    dq_ref[...] = dq.astype(bf16)
    kept_ref[group] = dq
    grad_k = dg(grad_raw, q, TN) * scale
    grad_v = dg(weights.astype(bf16), grad, TN)
    low, high = halves(grad_k, grad_v, lax.broadcasted_iota(jnp.int32, (SEQ, HEAD_DIM), 1))
    sent_ref[2 * group, :SEQ] = low.astype(bf16)
    sent_ref[2 * group + 1, :SEQ] = high.astype(bf16)

    @pl.when(group == KV_HEADS - 1)
    def _():
        lane = lax.broadcasted_iota(jnp.int32, (BLOCK, HEAD_DIM), 1)

        def dq_tile(m):
            return kept_ref[m // GROUP, :, HEAD_DIM * (m % GROUP) : HEAD_DIM * (m % GROUP + 1)]

        def ga_tile(m):
            return all_ga_ref[:, HEAD_DIM * m : HEAD_DIM * (m + 1)].astype(f32)

        for m in range(KV_HEADS):
            low, high = halves(dq_tile(N_CTX + m), ga_tile(N_CTX + m), lane)
            sent_ref[2 * m, AT_MIXED:AT_OUT] = low.astype(bf16)
            sent_ref[2 * m + 1, AT_MIXED:AT_OUT] = high.astype(bf16)
        gains = gain_ref[...].astype(bf16)
        for c in range(N_CTX):
            sent_ref[c, AT_QUERY:AT_MIXED] = dq_tile(c).astype(bf16)
            sent_ref[c, AT_OUT:AT_SHARED] = ga_tile(c).astype(bf16)
            sent_ref[c, AT_SHARED:AT_GAIN] = extra_ref[c]
            sent_ref[c, AT_GAIN:] = gains


def attend_back(ctx_at, qkv, grad_att, att_f, logs, kv_all, grad_attn, extra, gain_rows):
    return pl.pallas_call(
        attend_back_kernel,
        grid=(KV_HEADS,),
        in_specs=[
            pl.BlockSpec(memory_space=pltpu.SMEM),
            head_spec(),
            head_spec(),
            head_spec(),
            pl.BlockSpec((GROUP * BLOCK, HEAD_DIM), lambda g: (g, 0)),
        ]
        + kv_specs()
        + [
            whole((BLOCK, WIDTH)),
            whole((N_CTX, AT_GAIN - AT_SHARED, HEAD_DIM)),
            whole((16, HEAD_DIM)),
        ],
        out_specs=[head_spec(), whole((N_CTX, SENT_ROWS, HEAD_DIM))],
        out_shape=[
            jax.ShapeDtypeStruct((BLOCK, WIDTH), bf16),
            jax.ShapeDtypeStruct((N_CTX, SENT_ROWS, HEAD_DIM), bf16),
        ],
        scratch_shapes=[pltpu.VMEM((KV_HEADS, BLOCK, GROUP * HEAD_DIM), f32)],
        cost_estimate=cost(9),
        compiler_params=params(48),
        name="attend_back",
    )(ctx_at, qkv, grad_att, att_f, logs, kv_all, kv_all, grad_attn, extra, gain_rows)


def middle_kernel(att_ref, w_ref, x_ref, gain_ref, middle_ref, hidden_ref):
    middle = x_ref[...].astype(f32) + dg(att_ref[...], w_ref[...], NN)
    inv = lax.rsqrt(jnp.mean(middle * middle, axis=-1, keepdims=True) + epsilon)
    middle_ref[...] = middle
    hidden_ref[...] = (middle * inv * gain_ref[...]).astype(bf16)


def w_cols(width, at):
    return pl.BlockSpec((WIDTH, width), lambda *_: (0, at), pipeline_mode=pl.Buffered(1))


def middle_norm(attended, w_all, tokens, gain):
    return pl.pallas_call(
        middle_kernel,
        grid=(1,),
        in_specs=[
            whole((BLOCK, WIDTH)),
            w_cols(WIDTH, 1),
            whole((BLOCK, WIDTH)),
            whole((1, WIDTH)),
        ],
        out_specs=[whole((BLOCK, WIDTH)), whole((BLOCK, WIDTH))],
        out_shape=[
            jax.ShapeDtypeStruct((BLOCK, WIDTH), f32),
            jax.ShapeDtypeStruct((BLOCK, WIDTH), bf16),
        ],
        cost_estimate=cost(2),
        compiler_params=params(32),
        name="middle_norm",
    )(attended, w_all, tokens, gain)


def norm_back(grad_normed, normed, inv_root):
    return inv_root * (
        grad_normed - normed * jnp.mean(grad_normed * normed, axis=-1, keepdims=True)
    )


def middle_back_kernel(
    pieces_ref, middle_ref, up_ref, gain_ref, w_ref, gm_ref, ga_ref, gh_ref, gg_ref
):
    grad_two = pieces_ref[0].astype(f32)
    for i in range(1, HALF):
        grad_two = grad_two + pieces_ref[i].astype(f32)
    middle = middle_ref[...]
    inv = lax.rsqrt(jnp.mean(middle * middle, axis=-1, keepdims=True) + epsilon)
    normed = middle * inv
    gains = jnp.sum(grad_two * normed, axis=0, keepdims=True)
    gg_ref[...] = jnp.zeros((16, HEAD_DIM), f32)
    for m in range(HEADS):
        gg_ref[m : m + 1] = gains[:, HEAD_DIM * m : HEAD_DIM * (m + 1)]
    grad_middle = up_ref[...].astype(f32) + norm_back(grad_two * gain_ref[...], normed, inv)
    gm_ref[...] = grad_middle
    grad_attn = grad_middle.astype(bf16)
    ga_ref[...] = grad_attn
    gh_ref[...] = dg(grad_attn, w_ref[...], NT).astype(bf16)


def middle_back(pieces, middle, upstream, gain, w_all):
    return pl.pallas_call(
        middle_back_kernel,
        grid=(1,),
        in_specs=[
            whole((HALF, BLOCK, WIDTH)),
            whole((BLOCK, WIDTH)),
            whole((BLOCK, WIDTH)),
            whole((1, WIDTH)),
            w_cols(WIDTH, 1),
        ],
        out_specs=[whole((BLOCK, WIDTH))] * 3 + [whole((16, HEAD_DIM))],
        out_shape=[
            jax.ShapeDtypeStruct((BLOCK, WIDTH), f32),
            jax.ShapeDtypeStruct((BLOCK, WIDTH), bf16),
            jax.ShapeDtypeStruct((BLOCK, WIDTH), bf16),
            jax.ShapeDtypeStruct((16, HEAD_DIM), f32),
        ],
        cost_estimate=cost(5),
        compiler_params=params(48),
        name="middle_back",
    )(pieces, middle, upstream, gain, w_all)


def place_kernel(
    at_ref, up_ref, down_ref, sdown_ref, place_ref, geo_ref, geh_ref, gsh_ref, gate_ref
):
    lane = lax.broadcasted_iota(jnp.int32, (BLOCK, META), 1)
    row = lax.broadcasted_iota(jnp.int32, (BLOCK, META), 0)
    before = (row > lane).astype(bf16)
    slot = (lane % 64).astype(f32)
    first_id = (at_ref[0] * LOCAL_E).astype(f32)
    row_id = first_id + (row >= 64).astype(f32)

    for chip in range(HALF):
        meta = up_ref[chip, 0, :, WIDTH:].astype(f32)
        named = lane < TOPK
        zero = jnp.zeros((BLOCK, META), f32)
        hit0 = jnp.where(named & (meta == first_id), 1.0, zero)
        hit1 = jnp.where(named & (meta == first_id + 1.0), 1.0, zero)
        mask = jnp.where(
            lane < 64,
            jnp.sum(hit0, axis=1, keepdims=True),
            jnp.sum(hit1, axis=1, keepdims=True),
        )
        rank = dg(before, mask.astype(bf16), NN)
        place = jnp.where((mask > 0.5) & (rank == slot), 1.0, zero).astype(bf16)
        place_ref[chip, 0] = place
        rows = dg(place, up_ref[chip, 0], TN)
        slot_meta = rows[:, WIDTH:]
        gates = pltpu.roll(slot_meta, META - TOPK, 1) + pltpu.roll(
            slot_meta, META - 2 * TOPK, 1
        )
        gate = jnp.sum(
            jnp.where(named & (slot_meta == row_id), gates, zero), axis=1, keepdims=True
        )
        geo = (gate * rows[:, :WIDTH]).astype(bf16)
        wide_gate = jnp.broadcast_to(gate, (BLOCK, META))
        at = chip * CAP
        for e in range(LOCAL_E):
            geo_ref[e, 0, at : at + CAP] = geo[64 * e : 64 * e + CAP]
            gate_ref[e, 0, at : at + CAP] = wide_gate[64 * e : 64 * e + CAP]
        gsh_ref[chip, 0] = dg(up_ref[chip, 0, :, :WIDTH], sdown_ref[...], NT)
    for e in range(LOCAL_E):
        geh_ref[e, 0] = dg(geo_ref[e, 0], down_ref[e], NT)


def by_core(cols):
    return pl.BlockSpec(
        (HALF, 1, BLOCK, cols),
        lambda s, at: (0, jnp.where(s == 0, 1 - at[0] % 2, at[0] % 2), 0, 0),
    )


def by_step(cols):
    return pl.BlockSpec((LOCAL_E, 1, ROWS, cols), lambda s, at: (0, s, 0, 0))


def place_rows(exp_at, up_all, expert_down, shared_two):
    return pl.pallas_call(
        place_kernel,
        grid_spec=pltpu.PrefetchScalarGridSpec(
            num_scalar_prefetch=1,
            grid=(2,),
            in_specs=[
                by_core(WIDTH + META),
                whole((LOCAL_E, FF_E, WIDTH)),
                whole((2 * SHARED, WIDTH)),
            ],
            out_specs=[by_core(META), by_step(WIDTH), by_step(FF_E), by_core(META), by_step(META)],
        ),
        out_shape=[
            jax.ShapeDtypeStruct((HALF, 2, BLOCK, META), bf16),
            jax.ShapeDtypeStruct((LOCAL_E, 2, ROWS, WIDTH), bf16),
            jax.ShapeDtypeStruct((LOCAL_E, 2, ROWS, FF_E), f32),
            jax.ShapeDtypeStruct((HALF, 2, BLOCK, META), f32),
            jax.ShapeDtypeStruct((LOCAL_E, 2, ROWS, META), f32),
        ],
        cost_estimate=cost(14),
        compiler_params=params(56),
        name="place_rows",
    )(exp_at, up_all, expert_down, shared_two)


def expert_kernel(
    at_ref,
    hid_ref,
    place_ref,
    geh_ref,
    gsh_ref,
    wg_ref,
    wu_ref,
    ws_ref,
    part_ref,
    x_ref,
    act_ref,
    dgu_ref,
    sact_ref,
    sgrad_ref,
):
    for chip in range(HALF):
        rows = dg(place_ref[chip, 0], hid_ref[chip, 0], TN).astype(bf16)
        at = chip * CAP
        for e in range(LOCAL_E):
            x_ref[e, 0, at : at + CAP] = rows[64 * e : 64 * e + CAP]
    pairs = []
    for e in range(LOCAL_E):
        pre_gate = dg(x_ref[e, 0], wg_ref[e], NN)
        pre_up = dg(x_ref[e, 0], wu_ref[e], NN)
        sig = sigmoid(pre_gate)
        act = pre_gate * sig
        act_ref[e, 0] = (act * pre_up).astype(bf16)
        geh = geh_ref[e, 0]
        d_gate = (geh * pre_up * (sig * (1.0 + pre_gate * (1.0 - sig)))).astype(bf16)
        d_up = (geh * act).astype(bf16)
        dgu_ref[e, 0, :, :FF_E] = d_gate
        dgu_ref[e, 0, :, FF_E:] = d_up
        pairs.append((dg(d_gate, wg_ref[e], NT) + dg(d_up, wu_ref[e], NT)).astype(bf16))
    lane = lax.broadcasted_iota(jnp.int32, (BLOCK, 2 * SHARED), 1) < SHARED
    gap = jnp.zeros((64 - CAP, WIDTH), bf16)
    for chip in range(HALF):
        pre = dg(hid_ref[chip, 0], ws_ref[...], NN)
        turned = pltpu.roll(pre, SHARED, 1)
        gate, up = jnp.where(lane, pre, turned), jnp.where(lane, turned, pre)
        sig = sigmoid(gate)
        act = gate * sig
        sact_ref[chip, 0] = jnp.where(lane, act * up, 0.0).astype(bf16)
        slope = sig * (1.0 + gate * (1.0 - sig))
        sgrad = (gsh_ref[chip, 0] * jnp.where(lane, up * slope, act)).astype(bf16)
        sgrad_ref[chip, 0] = sgrad
        at = chip * CAP
        stacked = jnp.concatenate([pairs[0][at : at + CAP], gap, pairs[1][at : at + CAP], gap], 0)
        part_ref[0, chip] = (
            dg(place_ref[chip, 0], stacked, NN) + dg(sgrad, ws_ref[...], NT)
        ).astype(bf16)


def expert_back(exp_at, hidden, place, geh, gsh, wg, wu, ws):
    return pl.pallas_call(
        expert_kernel,
        grid_spec=pltpu.PrefetchScalarGridSpec(
            num_scalar_prefetch=1,
            grid=(2,),
            in_specs=[
                by_core(WIDTH),
                by_core(META),
                by_step(FF_E),
                by_core(META),
                whole((LOCAL_E, WIDTH, FF_E)),
                whole((LOCAL_E, WIDTH, FF_E)),
                whole((WIDTH, 2 * SHARED)),
            ],
            out_specs=[
                pl.BlockSpec((1, HALF, BLOCK, WIDTH), lambda s, at: (s, 0, 0, 0)),
                by_step(WIDTH),
                by_step(FF_E),
                by_step(2 * FF_E),
                by_core(META),
                by_core(META),
            ],
        ),
        out_shape=[
            jax.ShapeDtypeStruct((2, HALF, BLOCK, WIDTH), bf16),
            jax.ShapeDtypeStruct((LOCAL_E, 2, ROWS, WIDTH), bf16),
            jax.ShapeDtypeStruct((LOCAL_E, 2, ROWS, FF_E), bf16),
            jax.ShapeDtypeStruct((LOCAL_E, 2, ROWS, 2 * FF_E), bf16),
            jax.ShapeDtypeStruct((HALF, 2, BLOCK, META), bf16),
            jax.ShapeDtypeStruct((HALF, 2, BLOCK, META), bf16),
        ],
        cost_estimate=cost(28),
        compiler_params=params(60),
        name="expert_back",
    )(exp_at, hidden, place, geh, gsh, wg, wu, ws)


def output_kernel(at_ref, act_ref, gate_ref, place_ref, sact_ref, wd_ref, sd_ref, part_ref):
    outs = []
    for e in range(LOCAL_E):
        out = dg(act_ref[e, 0], wd_ref[e], NN).astype(bf16).astype(f32)
        outs.append((out * gate_ref[e, 0, :, :1]).astype(bf16))
    gap = jnp.zeros((64 - CAP, WIDTH), bf16)
    for chip in range(HALF):
        at = chip * CAP
        stacked = jnp.concatenate([outs[0][at : at + CAP], gap, outs[1][at : at + CAP], gap], 0)
        part_ref[chip, 0] = (
            dg(place_ref[chip, 0], stacked, NN) + dg(sact_ref[chip, 0], sd_ref[...], NN)
        ).astype(bf16)


def expert_output(exp_at, act, gate, place, sact, wd, sd):
    return pl.pallas_call(
        output_kernel,
        grid_spec=pltpu.PrefetchScalarGridSpec(
            num_scalar_prefetch=1,
            grid=(2,),
            in_specs=[
                by_step(FF_E),
                by_step(META),
                by_core(META),
                by_core(META),
                whole((LOCAL_E, FF_E, WIDTH)),
                whole((2 * SHARED, WIDTH)),
            ],
            out_specs=by_core(WIDTH),
        ),
        out_shape=jax.ShapeDtypeStruct((HALF, 2, BLOCK, WIDTH), bf16),
        cost_estimate=cost(10),
        compiler_params=params(48),
        name="expert_output",
    )(exp_at, act, gate, place, sact, wd, sd)


def columns_kernel(got_ref, hidden_ref, att_ref, sent_ref, kv_ref, down_ref):
    total = got_ref[0, :SEQ].astype(f32)
    for src in range(1, N_CTX):
        total = total + got_ref[src, :SEQ].astype(f32)
    grad_kv = total.astype(bf16)
    kv_ref[...] = grad_kv.reshape(N_CTX, BLOCK, HEAD_DIM)

    def rows_of(at, order):
        return jnp.concatenate([got_ref[src, at : at + BLOCK] for src in order], axis=0)

    in_order = list(range(N_CTX))
    y_order = [(i % 2) * 4 + i // 2 for i in range(N_CTX)]
    lane = lax.broadcasted_iota(jnp.int32, (SEQ, HEAD_DIM), 1)
    zero = jnp.zeros((SEQ, HEAD_DIM), bf16)
    mixed_q = jnp.where(lane < 64, rows_of(AT_MIXED, in_order), zero)
    mixed_o = jnp.where(lane < 64, zero, rows_of(AT_MIXED, y_order))
    left = jnp.concatenate([rows_of(AT_QUERY, in_order).T, mixed_q.T, grad_kv.T], axis=0)
    right = jnp.concatenate([mixed_o.T, rows_of(AT_OUT, y_order).T], axis=0)
    by_hidden = dg(left, hidden_ref[...].reshape(SEQ, WIDTH), NN)
    by_att = dg(right, att_ref[...].reshape(SEQ, WIDTH), NN)
    tiles = [
        by_hidden[:BLOCK],
        by_hidden[BLOCK : 2 * BLOCK] + by_att[:BLOCK],
        by_att[BLOCK:],
        by_hidden[2 * BLOCK :],
    ]
    for t, tile in enumerate(tiles):
        sent_ref[:, :96, HEAD_DIM * t : HEAD_DIM * (t + 1)] = (
            tile.T.astype(bf16).reshape(N_EXP, 96, HEAD_DIM)
        )

    def summed(start, stop):
        out = got_ref[0, start:stop].astype(f32)
        for src in range(1, N_CTX):
            out = out + got_ref[src, start:stop].astype(f32)
        return out

    down_ref[...] = summed(AT_DOWN, AT_GAIN).astype(bf16)
    shared = summed(AT_SHARED, AT_DOWN)
    gains = summed(AT_GAIN, SENT_ROWS)
    row = lax.broadcasted_iota(jnp.int32, (16, HEAD_DIM), 0)
    one_lane = lax.broadcasted_iota(jnp.int32, (1, HEAD_DIM), 1)
    for i in range(N_EXP):
        m, offset = (96 * i) // HEAD_DIM, (96 * i) % HEAD_DIM
        gain = gains[m : m + 1]
        if offset:
            shift = HEAD_DIM - offset
            gain = jnp.where(
                one_lane < shift,
                pltpu.roll(gain, shift, 1),
                pltpu.roll(gains[m + 1 : m + 2], shift, 1),
            )
        rows = jnp.where(row == 12, jnp.broadcast_to(gain, (16, HEAD_DIM)), shared[16 * i : 16 * i + 16])
        sent_ref[i, 96:, :HEAD_DIM] = rows.astype(bf16)
        sent_ref[i, 96:, HEAD_DIM:] = jnp.zeros((16, 512 - HEAD_DIM), bf16)


def column_grads(got, hidden_seq, att_seq):
    return pl.pallas_call(
        columns_kernel,
        out_shape=[
            jax.ShapeDtypeStruct((N_EXP, 112, 512), bf16),
            jax.ShapeDtypeStruct((N_CTX, BLOCK, HEAD_DIM), bf16),
            jax.ShapeDtypeStruct((96, HEAD_DIM), bf16),
        ],
        cost_estimate=cost(8),
        compiler_params=params(56),
        name="column_grads",
    )(got, hidden_seq, att_seq)


OWNED_ROWS = 4 * 96 + 16 * N_EXP + 96


def owned_kernel(got_ref, down_ref, owned_ref, gain_ref):
    total = got_ref[0, :96].astype(f32)
    gains = got_ref[0, 96:, :HEAD_DIM].astype(f32)
    for src in range(1, N_EXP):
        total = total + got_ref[src, :96].astype(f32)
        gains = gains + got_ref[src, 96:, :HEAD_DIM].astype(f32)
    gain_ref[...] = gains
    for t in range(4):
        owned_ref[96 * t : 96 * t + 96] = total[:, HEAD_DIM * t : HEAD_DIM * (t + 1)].astype(bf16)
    for src in range(N_EXP):
        at = 384 + 16 * src
        owned_ref[at : at + 16] = got_ref[src, 96:, :HEAD_DIM]
    owned_ref[384 + 16 * N_EXP :] = down_ref[...]


def owned_sums(got, down):
    return pl.pallas_call(
        owned_kernel,
        out_shape=[
            jax.ShapeDtypeStruct((OWNED_ROWS, HEAD_DIM), bf16),
            jax.ShapeDtypeStruct((16, HEAD_DIM), f32),
        ],
        cost_estimate=cost(3),
        compiler_params=params(32),
        name="owned_sums",
    )(got, down)


def finish_kernel(
    got_ref,
    gain_in_ref,
    wq_ref,
    wk_ref,
    wv_ref,
    gain_ref,
    q_ref,
    k_ref,
    v_ref,
    out_ref,
    sg_ref,
    su_ref,
    sd_ref,
):
    lane = lax.broadcasted_iota(jnp.int32, (96, HEAD_DIM), 1)

    def tile(c, t):
        return got_ref[c, 96 * t : 96 * t + 96].astype(f32)

    for c in range(N_CTX):
        at = HEAD_DIM * c
        q_ref[:, at : at + HEAD_DIM] = tile(c, 0)
        out_ref[:, at : at + HEAD_DIM] = tile(c, 2)
    for m in range(N_CTX // 2):
        at = HEAD_DIM * m
        low, high = halves(tile(2 * m, 1), tile(2 * m + 1, 1), lane)
        q_ref[:, 1024 + at : 1024 + at + HEAD_DIM] = low
        out_ref[:, 1024 + at : 1024 + at + HEAD_DIM] = high
        low, high = halves(tile(2 * m, 3), tile(2 * m + 1, 3), lane)
        k_ref[:, at : at + HEAD_DIM] = low
        v_ref[:, at : at + HEAD_DIM] = high
    gain = (
        jnp.sum(q_ref[...] * wq_ref[...].astype(f32), axis=1, keepdims=True)
        + jnp.sum(k_ref[...] * wk_ref[...].astype(f32), axis=1, keepdims=True)
        + jnp.sum(v_ref[...] * wv_ref[...].astype(f32), axis=1, keepdims=True)
    ) / gain_in_ref[...]
    gain_ref[...] = jnp.broadcast_to(gain, (96, HEAD_DIM))
    row = lax.broadcasted_iota(jnp.int32, (96, HEAD_DIM), 0)
    picks = jnp.where((lane % 16 < 12) & (row == 12 * (lane // 16) + lane % 16), 1.0, 0.0)
    picks = picks.astype(bf16)

    def shared_tile(j):
        at = 384 + 16 * j
        rows = jnp.concatenate([got_ref[c, at : at + 16] for c in range(N_CTX)], axis=0)
        return dg(picks, rows, NN)

    for m in range(N_EXP // 2):
        at = HEAD_DIM * m
        low, high = halves(shared_tile(2 * m), shared_tile(2 * m + 1), lane)
        sg_ref[:, at : at + HEAD_DIM] = low
        su_ref[:, at : at + HEAD_DIM] = high
    for c in range(N_CTX):
        rows = got_ref[c, 384 + 16 * N_EXP :].astype(f32)
        for m in range(HEADS):
            sd_ref[8 * c : 8 * c + 8, HEAD_DIM * m : HEAD_DIM * (m + 1)] = rows[8 * m : 8 * m + 8]


def finish(got, gain_column, query_weight, key_weight, value_weight):
    shapes = [(96, 128), (96, 1536), (96, 512), (96, 512), (96, 1536), (96, 1024), (96, 1024)]
    return pl.pallas_call(
        finish_kernel,
        out_shape=[jax.ShapeDtypeStruct(s, f32) for s in shapes + [(SHARED, WIDTH)]],
        cost_estimate=cost(4),
        compiler_params=params(32),
        name="finish",
    )(got, gain_column, query_weight, key_weight, value_weight)


def input_kernel(dq_ref, got_ref, wq_ref, wkv_ref, x_ref, gain_ref, gm_ref, out_ref):
    lane = lax.broadcasted_iota(jnp.int32, (BLOCK, HEAD_DIM), 1)
    lows, highs = [], []
    for m in range(KV_HEADS):
        low, high = halves(got_ref[2 * m].astype(f32), got_ref[2 * m + 1].astype(f32), lane)
        lows.append(low.astype(bf16))
        highs.append(high.astype(bf16))
    grad_kv = jnp.concatenate(lows + highs, axis=1)
    grad_one = dg(dq_ref[...], wq_ref[...], NT) + dg(grad_kv, wkv_ref[...], NT)
    inputs = x_ref[...].astype(f32)
    inv = lax.rsqrt(jnp.mean(inputs * inputs, axis=-1, keepdims=True) + epsilon)
    out_ref[...] = (gm_ref[...] + norm_back(grad_one * gain_ref[...], inputs * inv, inv)).astype(bf16)


def input_back(grad_query, grad_kv, w_all, tokens, gain, grad_middle):
    return pl.pallas_call(
        input_kernel,
        grid=(1,),
        in_specs=[
            whole((BLOCK, WIDTH)),
            whole((N_CTX, BLOCK, HEAD_DIM)),
            w_cols(WIDTH, 0),
            w_cols(2 * KV_WIDTH, 3),
            whole((BLOCK, WIDTH)),
            whole((1, WIDTH)),
            whole((BLOCK, WIDTH)),
        ],
        out_specs=whole((BLOCK, WIDTH)),
        out_shape=jax.ShapeDtypeStruct((BLOCK, WIDTH), bf16),
        cost_estimate=cost(7),
        compiler_params=params(48),
        name="input_back",
    )(grad_query, grad_kv, w_all, w_all, tokens, gain, grad_middle)


def norm_rows_kernel(x_ref, gain_ref, out_ref):
    inputs = x_ref[0].astype(f32)
    inv = lax.rsqrt(jnp.mean(inputs * inputs, axis=-1, keepdims=True) + epsilon)
    out_ref[0] = (inputs * inv * gain_ref[...]).astype(bf16)


def norm_rows(rows, gain):
    count = rows.shape[0]
    spec = pl.BlockSpec((1, BLOCK, WIDTH), lambda i: (i, 0, 0))
    turned = pl.BlockSpec((1, BLOCK, WIDTH), lambda i: ((i % 2) * 4 + i // 2, 0, 0))
    return pl.pallas_call(
        norm_rows_kernel,
        grid=(count,),
        in_specs=[spec, whole((1, WIDTH))],
        out_specs=spec if count == 1 else turned,
        out_shape=jax.ShapeDtypeStruct(rows.shape, bf16),
        cost_estimate=cost(2),
        compiler_params=params(32),
        name="norm_rows",
    )(rows, gain)


def project_kernel(own_ref, seq_ref, w_ref, q_ref, kv_ref):
    step = pl.program_id(0)

    @pl.when(step < 3)
    def _():
        q_ref[...] = dg(own_ref[0], w_ref[...], NN).astype(bf16)

    @pl.when(step >= 3)
    def _():
        rows = seq_ref[...].reshape(N_CTX * BLOCK, WIDTH)
        kv_ref[...] = dg(rows, w_ref[...], NN).astype(bf16).reshape(N_CTX, BLOCK, KV_WIDTH)


def project(own, seq, w_all):
    return pl.pallas_call(
        project_kernel,
        grid=(5,),
        in_specs=[
            whole((1, BLOCK, WIDTH)),
            whole((N_CTX, BLOCK, WIDTH)),
            pl.BlockSpec((WIDTH, KV_WIDTH), lambda i: (0, jnp.where(i < 3, i, i + 3))),
        ],
        out_specs=[
            pl.BlockSpec((BLOCK, KV_WIDTH), lambda i: (0, jnp.minimum(i, 2))),
            pl.BlockSpec((N_CTX, BLOCK, KV_WIDTH), lambda i: (0, 0, jnp.maximum(i - 3, 0))),
        ],
        out_shape=[
            jax.ShapeDtypeStruct((BLOCK, WIDTH), bf16),
            jax.ShapeDtypeStruct((N_CTX, BLOCK, 2 * KV_WIDTH), bf16),
        ],
        cost_estimate=cost(8),
        compiler_params=params(48),
        name="project",
    )(own, seq, w_all)


PIECE = 2 * WIDTH + WIDTH * BLOCK // HEAD_DIM


def expert_weights_kernel(
    halves, at_ref, x_ref, geo_ref, act_ref, dgate_ref, dup_ref, *refs
):
    outs, turned = refs[:-1], refs[-1]
    step = pl.program_id(0)

    @pl.when(step % 2 == 0)
    def _():
        turned[...] = x_ref[0].T

    rhs = jnp.concatenate([dgate_ref[0], dup_ref[0]], axis=1)
    both = dg(turned[...], rhs, NN).astype(bf16)
    down = dg(act_ref[0], geo_ref[0], TN).astype(bf16)
    for i in range(4):

        @pl.when(step == i)
        def _():
            start = (i % 2) * PIECE if halves else 0
            out = outs[i // 2 if halves else i].at[pl.ds(start, PIECE)]
            out[:WIDTH] = both[:, :HEAD_DIM]
            out[WIDTH : 2 * WIDTH] = both[:, HEAD_DIM:]
            for m in range(WIDTH // HEAD_DIM):
                at = 2 * WIDTH + m * BLOCK
                out[at : at + BLOCK] = down[:, m * HEAD_DIM : (m + 1) * HEAD_DIM]


def expert_weights(yz, steps, halves, arrived, grad_eo, act, grad_gu):
    rows = 2 * ROWS
    at = jnp.stack([yz[0] ^ r for r, _ in steps] + [yz[1] ^ side for _, side in steps])
    rows_of = pl.BlockSpec((1, rows, WIDTH), lambda s, at: (at[4 + s], 0, 0))

    def lanes(shift):
        return pl.BlockSpec((1, rows, HEAD_DIM), lambda s, at: (at[4 + s], 0, shift + at[s]))

    count, length = (2, 2 * PIECE) if halves else (4, PIECE)
    return pl.pallas_call(
        lambda *refs: expert_weights_kernel(halves, *refs),
        grid_spec=pltpu.PrefetchScalarGridSpec(
            num_scalar_prefetch=1,
            grid=(4,),
            in_specs=[rows_of, rows_of, lanes(0), lanes(0), lanes(4)],
            out_specs=[whole((length, HEAD_DIM))] * count,
            scratch_shapes=[pltpu.VMEM((WIDTH, rows), bf16)],
        ),
        out_shape=[jax.ShapeDtypeStruct((length, HEAD_DIM), bf16)] * count,
        cost_estimate=cost(9),
        compiler_params=params(56),
        name="expert_weights",
    )(at, arrived, grad_eo, act, grad_gu, grad_gu)


def unpack_kernel(at_ref, *refs):
    pieces, (gate_ref, up_ref, down_ref) = refs[:4], refs[-3:]
    step = pl.program_id(0)
    for i in range(4):

        @pl.when(step == i)
        def _():
            piece = pieces[i]
            gate_ref[0] = piece[:WIDTH].astype(f32)
            up_ref[0] = piece[WIDTH : 2 * WIDTH].astype(f32)
            for m in range(WIDTH // HEAD_DIM):
                at = 2 * WIDTH + m * BLOCK
                down_ref[0, :, m * HEAD_DIM : (m + 1) * HEAD_DIM] = piece[at : at + BLOCK].astype(
                    f32
                )


def unpack_experts(at, side, pieces, filled=()):
    cols = pl.BlockSpec((1, WIDTH, HEAD_DIM), lambda s, at: (at[1] ^ side, 0, at[0] ^ s))
    rows = pl.BlockSpec((1, BLOCK, WIDTH), lambda s, at: (at[1] ^ side, at[0] ^ s, 0))
    anywhere = pl.BlockSpec(memory_space=pl.ANY)
    return pl.pallas_call(
        unpack_kernel,
        grid_spec=pltpu.PrefetchScalarGridSpec(
            num_scalar_prefetch=1,
            grid=(4,),
            in_specs=[whole((PIECE, HEAD_DIM))] * 4 + [anywhere] * len(filled),
            out_specs=[cols, cols, rows],
        ),
        out_shape=[
            jax.ShapeDtypeStruct((LOCAL_E, WIDTH, FF_E), f32),
            jax.ShapeDtypeStruct((LOCAL_E, WIDTH, FF_E), f32),
            jax.ShapeDtypeStruct((LOCAL_E, FF_E, WIDTH), f32),
        ],
        input_output_aliases={5 + i: i for i in range(len(filled))},
        cost_estimate=cost(5),
        compiler_params=params(48),
        name="unpack_experts",
    )(at, *pieces, *filled)


def relay_kernel(
    p0, p1, p3, p6, relay_a, relay_b, got_10, got_31, add_a, add_b, part_0, part_1
):
    add_a[...] = (p6[...].astype(f32) + relay_a[...].astype(f32)).astype(bf16)
    add_b[...] = (p3[...].astype(f32) + relay_b[...].astype(f32)).astype(bf16)
    part_0[...] = p0[...].astype(f32) + got_10[...].astype(f32)
    part_1[...] = p1[...].astype(f32) + got_31[...].astype(f32)


def side_kernel(part_0, part_1, got_11, got_30, own, side):
    own[...] = part_0[...] + got_30[...].astype(f32)
    side[...] = (part_1[...] + got_11[...].astype(f32)).astype(bf16)


def piece_sums(kernel, kinds, *pieces):
    specs, arrays = [], []
    for piece in pieces:
        array, second = piece if isinstance(piece, tuple) else (piece, 0)
        specs.append(pl.BlockSpec((PIECE // 4, HEAD_DIM), lambda i, at=4 * second: (i + at, 0)))
        arrays.append(array)
    return pl.pallas_call(
        kernel,
        grid=(4,),
        in_specs=specs,
        out_specs=[pl.BlockSpec((PIECE // 4, HEAD_DIM), lambda i: (i, 0))] * len(kinds),
        out_shape=[jax.ShapeDtypeStruct((PIECE, HEAD_DIM), kind) for kind in kinds],
        cost_estimate=cost(4),
        compiler_params=params(32),
        name="piece_sums",
    )(*arrays)


same_core = [[2 * i + c for i in range(8)] for c in range(2)]
core_swap = [(i, i ^ 1) for i in range(N_EXP)]
y_groups = [[0, 1, 2, 3], [4, 5, 6, 7]]
z_swap = [(i, i ^ 4) for i in range(N_CTX)]


def swap_all(rows, axis, groups=None):
    return lax.all_to_all(
        rows, axis, split_axis=0, concat_axis=0, tiled=True, axis_index_groups=groups
    )


def after(value, *others):
    return lax.optimization_barrier((value,) + others)[0]


def add_low(a, b):
    return (a.astype(f32) + b.astype(f32)).astype(bf16)


def on_device(
    tokens,
    routes,
    route_gates,
    norm_attn,
    norm_ffn,
    query_weight,
    key_weight,
    value_weight,
    out_weight,
    shared_gate,
    shared_up,
    shared_down,
    expert_gate,
    expert_up,
    expert_down,
    cotangent,
):
    exp_at = lax.axis_index("exp").astype(jnp.int32)
    ctx_at = lax.axis_index("ctx").astype(jnp.int32)
    exp_s, ctx_s = exp_at.reshape(1), ctx_at.reshape(1)

    y_at, z_at = ctx_at % 4, ctx_at // 4
    yz_s = jnp.stack([y_at, z_at])

    w_cat = jnp.concatenate([query_weight, out_weight, key_weight, value_weight], axis=1)
    w_all = lax.all_gather(w_cat, "exp", axis=0, tiled=True)
    gates_high = route_gates[0].astype(bf16)
    gates_low = (route_gates[0] - gates_high.astype(f32)).astype(bf16)
    pad = jnp.zeros((BLOCK, META - 3 * TOPK), bf16)
    up_meta = jnp.concatenate(
        [cotangent[0], routes[0].astype(bf16), gates_high, gates_low, pad], axis=1
    )
    up_all = lax.all_gather(after(up_meta, w_cat), "exp", axis=0, tiled=True)
    gains = after(jnp.concatenate([norm_attn, norm_ffn]), w_cat)
    gains = swap_all(jnp.broadcast_to(gains, (N_EXP, gains.shape[0])), "exp")
    gain_attn = gains[:, :96].reshape(1, WIDTH).astype(f32)
    gain_ffn = gains[:, 96:].reshape(1, WIDTH).astype(f32)

    def of_sequence(rows):
        other = lax.ppermute(rows, "ctx", z_swap)
        pair = jnp.where(
            z_at == 0,
            jnp.concatenate([rows, other], axis=0),
            jnp.concatenate([other, rows], axis=0),
        )
        got = swap_all(jnp.broadcast_to(pair, (4, 2, BLOCK, WIDTH)), "ctx", y_groups)
        return got.reshape(N_CTX, BLOCK, WIDTH)

    tokens_seq = of_sequence(after(tokens, w_cat))
    shared_cols = jnp.concatenate(
        [shared_gate.reshape(96, N_EXP, SHARED), shared_up.reshape(96, N_EXP, SHARED)], axis=2
    ).transpose(1, 0, 2)
    w_shared = swap_all(shared_cols, "exp").reshape(WIDTH, 2 * SHARED)
    shared_two = jnp.concatenate([shared_down, shared_down], axis=0)

    hidden_one = norm_rows(tokens, gain_attn)
    hidden_seq = norm_rows(tokens_seq, gain_attn)
    hidden_seq = after(hidden_seq, w_shared)
    queries, kv_all = project(hidden_one, hidden_seq, w_all)
    attended, att_f, logs = attend(ctx_s, queries, kv_all)
    middle, hidden_two = middle_norm(attended, w_all, tokens[0], gain_ffn)

    hidden_all = lax.all_gather(hidden_two, "exp", axis=0, tiled=True)
    hidden_all = hidden_all.reshape(HALF, 2, BLOCK, WIDTH)
    att_seq = of_sequence(attended[None])
    place, grad_eo, grad_eh, grad_sh, slot_gate = place_rows(
        exp_s,
        after(up_all, hidden_two, att_seq).reshape(HALF, 2, BLOCK, WIDTH + META),
        expert_down,
        shared_two,
    )
    part, arrived, act, grad_gu, shared_act, shared_grad = expert_back(
        exp_s, hidden_all, place, grad_eh, grad_sh, expert_gate, expert_up, w_shared
    )
    summed = add_low(part[1], lax.ppermute(part[0], "exp", core_swap))
    grad_two = swap_all(summed, "exp", same_core)

    rows_e = 2 * ROWS
    operands = (
        after(arrived, summed).reshape(LOCAL_E, rows_e, WIDTH),
        grad_eo.reshape(LOCAL_E, rows_e, WIDTH),
        act.reshape(LOCAL_E, rows_e, FF_E),
        grad_gu.reshape(LOCAL_E, rows_e, 2 * FF_E),
    )
    for_1, for_3 = expert_weights(yz_s, ((2, 0), (1, 0), (2, 1), (3, 1)), True, *operands)
    operands = (after(operands[0], for_1),) + operands[1:]
    p0, p6, p1, p3 = expert_weights(yz_s, ((0, 0), (3, 0), (0, 1), (1, 1)), False, *operands)

    def to(rows, k):
        return lax.ppermute(rows, "ctx", [(i, i ^ k) for i in range(N_CTX)])

    from_1, from_3 = to(for_1, 1), to(for_3, 3)
    shared_grad_late = after(shared_grad, p0).reshape(N_EXP * BLOCK, META)
    grad_scols = dg(hidden_all.reshape(N_EXP * BLOCK, WIDTH), shared_grad_late, TN).astype(bf16)
    act_late = after(shared_act, p0).reshape(N_EXP * BLOCK, META)
    grad_sdown = dg(act_late, up_all, TN)[:SHARED, :WIDTH].astype(bf16)

    extra = jnp.concatenate(
        [
            jnp.pad(
                grad_scols.reshape(N_EXP, N_CTX, 12, META).transpose(1, 0, 2, 3),
                ((0, 0), (0, 0), (0, 4), (0, 0)),
            ).reshape(N_CTX, 16 * N_EXP, META),
            grad_sdown.reshape(N_CTX, 8, HEADS, 128).transpose(0, 2, 1, 3).reshape(N_CTX, 96, 128),
        ],
        axis=1,
    )
    out_part = expert_output(
        exp_s, after(act, p0), slot_gate, place, shared_act, expert_down, shared_two
    )

    grad_two = after(grad_two, out_part, extra)
    grad_middle, grad_attn, grad_heads, gain_rows = middle_back(
        grad_two, middle, cotangent[0], gain_ffn, w_all
    )
    grad_query, sent = attend_back(
        ctx_s, queries, grad_heads, att_f, logs, kv_all, grad_attn, extra, gain_rows
    )
    from_1, from_3 = after((from_1, from_3), sent)
    add_a, add_b, part_0, part_1 = piece_sums(
        relay_kernel,
        (bf16, bf16, f32, f32),
        p0,
        p1,
        p3,
        p6,
        (from_1, 0),
        (from_3, 0),
        (from_1, 1),
        (from_3, 1),
    )
    got_11, got_30 = to(add_b, 1), to(add_a, 3)
    out_rows = lax.psum_scatter(
        after(out_part, add_a).reshape(N_EXP * BLOCK, WIDTH),
        "exp",
        scatter_dimension=0,
        tiled=True,
    )

    columns, grad_kv, grad_down = column_grads(
        swap_all(after(sent, add_a), "ctx"), hidden_seq, att_seq
    )
    owned = swap_all(columns, "exp")
    own_part, side = piece_sums(
        side_kernel, (f32, bf16), part_0, part_1, after(got_11, columns), got_30
    )
    across = to(side, 4)
    owned, gain_sum = owned_sums(owned, grad_down)
    own = (own_part + after(across, columns).astype(f32)).astype(bf16)
    at_1, at_3, at_z = to(own, 1), to(own, 3), to(own, 4)
    owned = swap_all(
        jnp.broadcast_to(after(owned, own), (N_CTX, OWNED_ROWS, HEAD_DIM)), "ctx"
    )
    gain_attn_sum, *dense = finish(
        owned,
        norm_attn.astype(f32).reshape(96, 1),
        query_weight,
        key_weight,
        value_weight,
    )

    grad_kv, at_1, at_3, at_z = lax.optimization_barrier((grad_kv, at_1, at_3, at_z))
    grad_kv = swap_all(after(grad_kv, owned), "ctx")
    at_z1, at_z3 = to(at_z, 1), to(at_z, 3)
    grad_query, at_z1, at_z3 = lax.optimization_barrier((grad_query, at_z1, at_z3))
    at_2, at_z2 = to(after(at_3, grad_query), 1), to(at_z1, 3)
    input_grad = input_back(grad_query, grad_kv, w_all, tokens[0], gain_attn, grad_middle)
    mixed = (middle + out_rows.astype(f32)).astype(bf16)[None]
    near = unpack_experts(yz_s, 0, after((own, at_1, at_2, at_3), mixed, input_grad, *dense))
    experts = unpack_experts(yz_s, 1, (at_z, at_z1, at_z2, at_z3), near)
    return (
        mixed,
        input_grad[None],
        gain_attn_sum[:, 0],
        gain_sum[12, :96],
        *dense,
        *experts,
    )


def solution(mesh):
    token_spec = P("exp", "ctx", None)
    rows = P("exp", None)
    expert = P("exp", None, None)
    placed = (token_spec,) * 3 + (P("exp"),) * 2 + (rows,) * 7 + (expert,) * 3 + (token_spec,)
    return jax.shard_map(
        on_device,
        mesh=mesh,
        in_specs=placed,
        out_specs=(token_spec,) * 2 + (P("exp"),) * 2 + (rows,) * 7 + (expert,) * 3,
        check_vma=False,
    )
```

```python
import jax
import jax.numpy as jnp
from jax import lax
from jax.sharding import PartitionSpec as P
from jax.experimental import pallas as pl
from jax.experimental.pallas import tpu as pltpu

HEADS = 12
KV_HEADS = 4
HEAD_DIM = 128
TOPK = 6
GROUP = 3
BLOCK = 128
WIDTH = 1536
KV_WIDTH = KV_HEADS * HEAD_DIM
CAP = 48
N_EXP = 16
N_CTX = 8
LOCAL_E = 2
FF_E = 512
SHARED = 64
META = 128
HALF = 8
ROWS = HALF * CAP

epsilon = 1e-05
masked_score = -1e30
f32 = jnp.float32
bf16 = jnp.bfloat16
log2_e = 1.4426950408889634
score_scale = HEAD_DIM ** (-0.5) * log2_e

NN = (((1,), (0,)), ((), ()))
NT = (((1,), (1,)), ((), ()))
TN = (((0,), (0,)), ((), ()))


def dg(a, b, dims):
    return lax.dot_general(a, b, dims, preferred_element_type=f32)


def params(mib):
    return pltpu.CompilerParams(vmem_limit_bytes=mib * 1024 * 1024)


def cost(us):
    return pl.CostEstimate(flops=0, bytes_accessed=int(us * 3690000), transcendentals=0)


def whole(shape):
    return pl.BlockSpec(shape, lambda *_: (0,) * len(shape), pipeline_mode=pl.Buffered(1))


def sigmoid(v):
    return 1.0 / (1.0 + jnp.exp(-v))


def allowed_scores(ctx_at):
    rows = lax.broadcasted_iota(jnp.int32, (GROUP * BLOCK, N_CTX * BLOCK), 0) % BLOCK
    cols = lax.broadcasted_iota(jnp.int32, (GROUP * BLOCK, N_CTX * BLOCK), 1)
    return rows + ctx_at * BLOCK >= cols


def stack_heads(block):
    return jnp.concatenate([block[:, j * HEAD_DIM : (j + 1) * HEAD_DIM] for j in range(GROUP)], axis=0)


def unstack_heads(rows):
    return jnp.concatenate([rows[j * BLOCK : (j + 1) * BLOCK] for j in range(GROUP)], axis=1)


def attend_kernel(ctx_ref, q_ref, k_ref, v_ref, att_ref, attf_ref, log_ref):
    q = stack_heads(q_ref[...])
    keys = k_ref[...].reshape(N_CTX * BLOCK, HEAD_DIM)
    values = v_ref[...].reshape(N_CTX * BLOCK, HEAD_DIM)
    scores = jnp.where(allowed_scores(ctx_ref[0]), dg(q, keys, NT) * score_scale, masked_score)
    top = jnp.max(scores, axis=-1, keepdims=True)
    weights = jnp.exp2(scores - top)
    total = jnp.sum(weights, axis=-1, keepdims=True)
    out = dg(weights.astype(bf16), values, NN) * (1.0 / total)
    out = unstack_heads(out)
    attf_ref[...] = out
    att_ref[...] = out.astype(bf16)
    log_ref[...] = jnp.broadcast_to(top + jnp.log2(total), (GROUP * BLOCK, HEAD_DIM))


def kv_specs():
    return [
        pl.BlockSpec((N_CTX, BLOCK, HEAD_DIM), lambda g: (0, 0, g)),
        pl.BlockSpec((N_CTX, BLOCK, HEAD_DIM), lambda g: (0, 0, KV_HEADS + g)),
    ]


def head_spec():
    return pl.BlockSpec((BLOCK, GROUP * HEAD_DIM), lambda g: (0, g))


def attend(ctx_at, qkv, kv_all):
    return pl.pallas_call(
        attend_kernel,
        grid=(KV_HEADS,),
        in_specs=[pl.BlockSpec(memory_space=pltpu.SMEM), head_spec()] + kv_specs(),
        out_specs=[
            head_spec(),
            head_spec(),
            pl.BlockSpec((GROUP * BLOCK, HEAD_DIM), lambda g: (g, 0)),
        ],
        out_shape=[
            jax.ShapeDtypeStruct((BLOCK, WIDTH), bf16),
            jax.ShapeDtypeStruct((BLOCK, WIDTH), f32),
            jax.ShapeDtypeStruct((HEADS * BLOCK, HEAD_DIM), f32),
        ],
        cost_estimate=cost(6),
        compiler_params=params(48),
        name="attend",
    )(ctx_at, qkv, kv_all, kv_all)


SEQ = N_CTX * BLOCK
AT_QUERY, AT_MIXED, AT_OUT = SEQ, SEQ + BLOCK, SEQ + 2 * BLOCK
AT_SHARED = SEQ + 3 * BLOCK
AT_DOWN = AT_SHARED + 16 * N_EXP
AT_GAIN = AT_DOWN + 96
SENT_ROWS = AT_GAIN + 16


def halves(a, b, lane):
    low = jnp.where(lane < 64, a, pltpu.roll(b, 64, 1))
    high = jnp.where(lane < 64, pltpu.roll(a, 64, 1), b)
    return low, high


def attend_back_kernel(
    ctx_ref,
    q_ref,
    ga_ref,
    attf_ref,
    log_ref,
    k_ref,
    v_ref,
    all_ga_ref,
    extra_ref,
    gain_ref,
    dq_ref,
    sent_ref,
    kept_ref,
):
    group = pl.program_id(0)
    q = stack_heads(q_ref[...])
    grad = stack_heads(ga_ref[...])
    delta = jnp.sum(grad.astype(f32) * stack_heads(attf_ref[...]), axis=-1, keepdims=True)
    keys = k_ref[...].reshape(SEQ, HEAD_DIM)
    values = v_ref[...].reshape(SEQ, HEAD_DIM)
    scores = jnp.where(allowed_scores(ctx_ref[0]), dg(q, keys, NT) * score_scale, masked_score)
    weights = jnp.exp2(scores - log_ref[:, :1])
    grad_weights = dg(grad, values, NT)
    grad_raw = (weights * (grad_weights - delta)).astype(bf16)
    scale = HEAD_DIM ** (-0.5)
    dq = unstack_heads(dg(grad_raw, keys, NN) * scale)
    dq_ref[...] = dq.astype(bf16)
    kept_ref[group] = dq
    grad_k = dg(grad_raw, q, TN) * scale
    grad_v = dg(weights.astype(bf16), grad, TN)
    low, high = halves(grad_k, grad_v, lax.broadcasted_iota(jnp.int32, (SEQ, HEAD_DIM), 1))
    sent_ref[2 * group, :SEQ] = low.astype(bf16)
    sent_ref[2 * group + 1, :SEQ] = high.astype(bf16)

    @pl.when(group == KV_HEADS - 1)
    def _():
        lane = lax.broadcasted_iota(jnp.int32, (BLOCK, HEAD_DIM), 1)

        def dq_tile(m):
            return kept_ref[m // GROUP, :, HEAD_DIM * (m % GROUP) : HEAD_DIM * (m % GROUP + 1)]

        def ga_tile(m):
            return all_ga_ref[:, HEAD_DIM * m : HEAD_DIM * (m + 1)].astype(f32)

        for m in range(KV_HEADS):
            low, high = halves(dq_tile(N_CTX + m), ga_tile(N_CTX + m), lane)
            sent_ref[2 * m, AT_MIXED:AT_OUT] = low.astype(bf16)
            sent_ref[2 * m + 1, AT_MIXED:AT_OUT] = high.astype(bf16)
        gains = gain_ref[...].astype(bf16)
        for c in range(N_CTX):
            sent_ref[c, AT_QUERY:AT_MIXED] = dq_tile(c).astype(bf16)
            sent_ref[c, AT_OUT:AT_SHARED] = ga_tile(c).astype(bf16)
            sent_ref[c, AT_SHARED:AT_GAIN] = extra_ref[c]
            sent_ref[c, AT_GAIN:] = gains


def attend_back(ctx_at, qkv, grad_att, att_f, logs, kv_all, grad_attn, extra, gain_rows):
    return pl.pallas_call(
        attend_back_kernel,
        grid=(KV_HEADS,),
        in_specs=[
            pl.BlockSpec(memory_space=pltpu.SMEM),
            head_spec(),
            head_spec(),
            head_spec(),
            pl.BlockSpec((GROUP * BLOCK, HEAD_DIM), lambda g: (g, 0)),
        ]
        + kv_specs()
        + [
            whole((BLOCK, WIDTH)),
            whole((N_CTX, AT_GAIN - AT_SHARED, HEAD_DIM)),
            whole((16, HEAD_DIM)),
        ],
        out_specs=[head_spec(), whole((N_CTX, SENT_ROWS, HEAD_DIM))],
        out_shape=[
            jax.ShapeDtypeStruct((BLOCK, WIDTH), bf16),
            jax.ShapeDtypeStruct((N_CTX, SENT_ROWS, HEAD_DIM), bf16),
        ],
        scratch_shapes=[pltpu.VMEM((KV_HEADS, BLOCK, GROUP * HEAD_DIM), f32)],
        cost_estimate=cost(9),
        compiler_params=params(48),
        name="attend_back",
    )(ctx_at, qkv, grad_att, att_f, logs, kv_all, kv_all, grad_attn, extra, gain_rows)


def middle_kernel(att_ref, w_ref, x_ref, gain_ref, middle_ref, hidden_ref):
    middle = x_ref[...].astype(f32) + dg(att_ref[...], w_ref[...], NN)
    inv = lax.rsqrt(jnp.mean(middle * middle, axis=-1, keepdims=True) + epsilon)
    middle_ref[...] = middle
    hidden_ref[...] = (middle * inv * gain_ref[...]).astype(bf16)


def w_cols(width, at):
    return pl.BlockSpec((WIDTH, width), lambda *_: (0, at), pipeline_mode=pl.Buffered(1))


def middle_norm(attended, w_all, tokens, gain):
    return pl.pallas_call(
        middle_kernel,
        grid=(1,),
        in_specs=[
            whole((BLOCK, WIDTH)),
            w_cols(WIDTH, 1),
            whole((BLOCK, WIDTH)),
            whole((1, WIDTH)),
        ],
        out_specs=[whole((BLOCK, WIDTH)), whole((BLOCK, WIDTH))],
        out_shape=[
            jax.ShapeDtypeStruct((BLOCK, WIDTH), f32),
            jax.ShapeDtypeStruct((BLOCK, WIDTH), bf16),
        ],
        cost_estimate=cost(2),
        compiler_params=params(32),
        name="middle_norm",
    )(attended, w_all, tokens, gain)


def norm_back(grad_normed, normed, inv_root):
    return inv_root * (
        grad_normed - normed * jnp.mean(grad_normed * normed, axis=-1, keepdims=True)
    )


def middle_back_kernel(
    pieces_ref, middle_ref, up_ref, gain_ref, w_ref, gm_ref, ga_ref, gh_ref, gg_ref
):
    grad_two = pieces_ref[0].astype(f32)
    for i in range(1, HALF):
        grad_two = grad_two + pieces_ref[i].astype(f32)
    middle = middle_ref[...]
    inv = lax.rsqrt(jnp.mean(middle * middle, axis=-1, keepdims=True) + epsilon)
    normed = middle * inv
    gains = jnp.sum(grad_two * normed, axis=0, keepdims=True)
    gg_ref[...] = jnp.zeros((16, HEAD_DIM), f32)
    for m in range(HEADS):
        gg_ref[m : m + 1] = gains[:, HEAD_DIM * m : HEAD_DIM * (m + 1)]
    grad_middle = up_ref[...].astype(f32) + norm_back(grad_two * gain_ref[...], normed, inv)
    gm_ref[...] = grad_middle
    grad_attn = grad_middle.astype(bf16)
    ga_ref[...] = grad_attn
    gh_ref[...] = dg(grad_attn, w_ref[...], NT).astype(bf16)


def middle_back(pieces, middle, upstream, gain, w_all):
    return pl.pallas_call(
        middle_back_kernel,
        grid=(1,),
        in_specs=[
            whole((HALF, BLOCK, WIDTH)),
            whole((BLOCK, WIDTH)),
            whole((BLOCK, WIDTH)),
            whole((1, WIDTH)),
            w_cols(WIDTH, 1),
        ],
        out_specs=[whole((BLOCK, WIDTH))] * 3 + [whole((16, HEAD_DIM))],
        out_shape=[
            jax.ShapeDtypeStruct((BLOCK, WIDTH), f32),
            jax.ShapeDtypeStruct((BLOCK, WIDTH), bf16),
            jax.ShapeDtypeStruct((BLOCK, WIDTH), bf16),
            jax.ShapeDtypeStruct((16, HEAD_DIM), f32),
        ],
        cost_estimate=cost(5),
        compiler_params=params(48),
        name="middle_back",
    )(pieces, middle, upstream, gain, w_all)


def place_kernel(
    at_ref, up_ref, down_ref, sdown_ref, place_ref, geo_ref, geh_ref, gsh_ref, gate_ref
):
    lane = lax.broadcasted_iota(jnp.int32, (BLOCK, META), 1)
    row = lax.broadcasted_iota(jnp.int32, (BLOCK, META), 0)
    before = (row > lane).astype(bf16)
    slot = (lane % 64).astype(f32)
    first_id = (at_ref[0] * LOCAL_E).astype(f32)
    row_id = first_id + (row >= 64).astype(f32)

    for chip in range(HALF):
        meta = up_ref[chip, 0, :, WIDTH:].astype(f32)
        named = lane < TOPK
        zero = jnp.zeros((BLOCK, META), f32)
        hit0 = jnp.where(named & (meta == first_id), 1.0, zero)
        hit1 = jnp.where(named & (meta == first_id + 1.0), 1.0, zero)
        mask = jnp.where(
            lane < 64,
            jnp.sum(hit0, axis=1, keepdims=True),
            jnp.sum(hit1, axis=1, keepdims=True),
        )
        rank = dg(before, mask.astype(bf16), NN)
        place = jnp.where((mask > 0.5) & (rank == slot), 1.0, zero).astype(bf16)
        place_ref[chip, 0] = place
        rows = dg(place, up_ref[chip, 0], TN)
        slot_meta = rows[:, WIDTH:]
        gates = pltpu.roll(slot_meta, META - TOPK, 1) + pltpu.roll(
            slot_meta, META - 2 * TOPK, 1
        )
        gate = jnp.sum(
            jnp.where(named & (slot_meta == row_id), gates, zero), axis=1, keepdims=True
        )
        geo = (gate * rows[:, :WIDTH]).astype(bf16)
        wide_gate = jnp.broadcast_to(gate, (BLOCK, META))
        at = chip * CAP
        for e in range(LOCAL_E):
            geo_ref[e, 0, at : at + CAP] = geo[64 * e : 64 * e + CAP]
            gate_ref[e, 0, at : at + CAP] = wide_gate[64 * e : 64 * e + CAP]
        gsh_ref[chip, 0] = dg(up_ref[chip, 0, :, :WIDTH], sdown_ref[...], NT)
    for e in range(LOCAL_E):
        geh_ref[e, 0] = dg(geo_ref[e, 0], down_ref[e], NT)


def by_core(cols):
    return pl.BlockSpec(
        (HALF, 1, BLOCK, cols),
        lambda s, at: (0, jnp.where(s == 0, 1 - at[0] % 2, at[0] % 2), 0, 0),
    )


def by_step(cols):
    return pl.BlockSpec((LOCAL_E, 1, ROWS, cols), lambda s, at: (0, s, 0, 0))


def place_rows(exp_at, up_all, expert_down, shared_two):
    return pl.pallas_call(
        place_kernel,
        grid_spec=pltpu.PrefetchScalarGridSpec(
            num_scalar_prefetch=1,
            grid=(2,),
            in_specs=[
                by_core(WIDTH + META),
                whole((LOCAL_E, FF_E, WIDTH)),
                whole((2 * SHARED, WIDTH)),
            ],
            out_specs=[by_core(META), by_step(WIDTH), by_step(FF_E), by_core(META), by_step(META)],
        ),
        out_shape=[
            jax.ShapeDtypeStruct((HALF, 2, BLOCK, META), bf16),
            jax.ShapeDtypeStruct((LOCAL_E, 2, ROWS, WIDTH), bf16),
            jax.ShapeDtypeStruct((LOCAL_E, 2, ROWS, FF_E), f32),
            jax.ShapeDtypeStruct((HALF, 2, BLOCK, META), f32),
            jax.ShapeDtypeStruct((LOCAL_E, 2, ROWS, META), f32),
        ],
        cost_estimate=cost(14),
        compiler_params=params(56),
        name="place_rows",
    )(exp_at, up_all, expert_down, shared_two)


def expert_kernel(
    at_ref,
    hid_ref,
    place_ref,
    geh_ref,
    gsh_ref,
    wg_ref,
    wu_ref,
    ws_ref,
    part_ref,
    x_ref,
    act_ref,
    dgu_ref,
    sact_ref,
    sgrad_ref,
):
    for chip in range(HALF):
        rows = dg(place_ref[chip, 0], hid_ref[chip, 0], TN).astype(bf16)
        at = chip * CAP
        for e in range(LOCAL_E):
            x_ref[e, 0, at : at + CAP] = rows[64 * e : 64 * e + CAP]
    pairs = []
    for e in range(LOCAL_E):
        pre_gate = dg(x_ref[e, 0], wg_ref[e], NN)
        pre_up = dg(x_ref[e, 0], wu_ref[e], NN)
        sig = sigmoid(pre_gate)
        act = pre_gate * sig
        act_ref[e, 0] = (act * pre_up).astype(bf16)
        geh = geh_ref[e, 0]
        d_gate = (geh * pre_up * (sig * (1.0 + pre_gate * (1.0 - sig)))).astype(bf16)
        d_up = (geh * act).astype(bf16)
        dgu_ref[e, 0, :, :FF_E] = d_gate
        dgu_ref[e, 0, :, FF_E:] = d_up
        pairs.append((dg(d_gate, wg_ref[e], NT) + dg(d_up, wu_ref[e], NT)).astype(bf16))
    lane = lax.broadcasted_iota(jnp.int32, (BLOCK, 2 * SHARED), 1) < SHARED
    gap = jnp.zeros((64 - CAP, WIDTH), bf16)
    for chip in range(HALF):
        pre = dg(hid_ref[chip, 0], ws_ref[...], NN)
        turned = pltpu.roll(pre, SHARED, 1)
        gate, up = jnp.where(lane, pre, turned), jnp.where(lane, turned, pre)
        sig = sigmoid(gate)
        act = gate * sig
        sact_ref[chip, 0] = jnp.where(lane, act * up, 0.0).astype(bf16)
        slope = sig * (1.0 + gate * (1.0 - sig))
        sgrad = (gsh_ref[chip, 0] * jnp.where(lane, up * slope, act)).astype(bf16)
        sgrad_ref[chip, 0] = sgrad
        at = chip * CAP
        stacked = jnp.concatenate([pairs[0][at : at + CAP], gap, pairs[1][at : at + CAP], gap], 0)
        part_ref[0, chip] = (
            dg(place_ref[chip, 0], stacked, NN) + dg(sgrad, ws_ref[...], NT)
        ).astype(bf16)


def expert_back(exp_at, hidden, place, geh, gsh, wg, wu, ws):
    return pl.pallas_call(
        expert_kernel,
        grid_spec=pltpu.PrefetchScalarGridSpec(
            num_scalar_prefetch=1,
            grid=(2,),
            in_specs=[
                by_core(WIDTH),
                by_core(META),
                by_step(FF_E),
                by_core(META),
                whole((LOCAL_E, WIDTH, FF_E)),
                whole((LOCAL_E, WIDTH, FF_E)),
                whole((WIDTH, 2 * SHARED)),
            ],
            out_specs=[
                pl.BlockSpec((1, HALF, BLOCK, WIDTH), lambda s, at: (s, 0, 0, 0)),
                by_step(WIDTH),
                by_step(FF_E),
                by_step(2 * FF_E),
                by_core(META),
                by_core(META),
            ],
        ),
        out_shape=[
            jax.ShapeDtypeStruct((2, HALF, BLOCK, WIDTH), bf16),
            jax.ShapeDtypeStruct((LOCAL_E, 2, ROWS, WIDTH), bf16),
            jax.ShapeDtypeStruct((LOCAL_E, 2, ROWS, FF_E), bf16),
            jax.ShapeDtypeStruct((LOCAL_E, 2, ROWS, 2 * FF_E), bf16),
            jax.ShapeDtypeStruct((HALF, 2, BLOCK, META), bf16),
            jax.ShapeDtypeStruct((HALF, 2, BLOCK, META), bf16),
        ],
        cost_estimate=cost(28),
        compiler_params=params(60),
        name="expert_back",
    )(exp_at, hidden, place, geh, gsh, wg, wu, ws)


def output_kernel(at_ref, act_ref, gate_ref, place_ref, sact_ref, wd_ref, sd_ref, part_ref):
    outs = []
    for e in range(LOCAL_E):
        out = dg(act_ref[e, 0], wd_ref[e], NN).astype(bf16).astype(f32)
        outs.append((out * gate_ref[e, 0, :, :1]).astype(bf16))
    gap = jnp.zeros((64 - CAP, WIDTH), bf16)
    for chip in range(HALF):
        at = chip * CAP
        stacked = jnp.concatenate([outs[0][at : at + CAP], gap, outs[1][at : at + CAP], gap], 0)
        part_ref[0, chip] = (
            dg(place_ref[chip, 0], stacked, NN) + dg(sact_ref[chip, 0], sd_ref[...], NN)
        ).astype(bf16)


def expert_output(exp_at, act, gate, place, sact, wd, sd):
    return pl.pallas_call(
        output_kernel,
        grid_spec=pltpu.PrefetchScalarGridSpec(
            num_scalar_prefetch=1,
            grid=(2,),
            in_specs=[
                by_step(FF_E),
                by_step(META),
                by_core(META),
                by_core(META),
                whole((LOCAL_E, FF_E, WIDTH)),
                whole((2 * SHARED, WIDTH)),
            ],
            out_specs=pl.BlockSpec((1, HALF, BLOCK, WIDTH), lambda s, at: (s, 0, 0, 0)),
        ),
        out_shape=jax.ShapeDtypeStruct((2, HALF, BLOCK, WIDTH), bf16),
        cost_estimate=cost(10),
        compiler_params=params(48),
        name="expert_output",
    )(exp_at, act, gate, place, sact, wd, sd)


def columns_kernel(got_ref, hidden_ref, att_ref, sent_ref, kv_ref, down_ref):
    total = got_ref[0, :SEQ].astype(f32)
    for src in range(1, N_CTX):
        total = total + got_ref[src, :SEQ].astype(f32)
    grad_kv = total.astype(bf16)
    kv_ref[...] = grad_kv.reshape(N_CTX, BLOCK, HEAD_DIM)

    def rows_of(at, order):
        return jnp.concatenate([got_ref[src, at : at + BLOCK] for src in order], axis=0)

    in_order = list(range(N_CTX))
    y_order = [(i % 2) * 4 + i // 2 for i in range(N_CTX)]
    lane = lax.broadcasted_iota(jnp.int32, (SEQ, HEAD_DIM), 1)
    zero = jnp.zeros((SEQ, HEAD_DIM), bf16)
    mixed_q = jnp.where(lane < 64, rows_of(AT_MIXED, in_order), zero)
    mixed_o = jnp.where(lane < 64, zero, rows_of(AT_MIXED, y_order))
    left = jnp.concatenate([rows_of(AT_QUERY, in_order).T, mixed_q.T, grad_kv.T], axis=0)
    right = jnp.concatenate([mixed_o.T, rows_of(AT_OUT, y_order).T], axis=0)
    by_hidden = dg(left, hidden_ref[...].reshape(SEQ, WIDTH), NN)
    by_att = dg(right, att_ref[...].reshape(SEQ, WIDTH), NN)
    tiles = [
        by_hidden[:BLOCK],
        by_hidden[BLOCK : 2 * BLOCK] + by_att[:BLOCK],
        by_att[BLOCK:],
        by_hidden[2 * BLOCK :],
    ]
    for t, tile in enumerate(tiles):
        sent_ref[:, :96, HEAD_DIM * t : HEAD_DIM * (t + 1)] = (
            tile.T.astype(bf16).reshape(N_EXP, 96, HEAD_DIM)
        )

    def summed(start, stop):
        out = got_ref[0, start:stop].astype(f32)
        for src in range(1, N_CTX):
            out = out + got_ref[src, start:stop].astype(f32)
        return out

    down_ref[...] = summed(AT_DOWN, AT_GAIN).astype(bf16)
    shared = summed(AT_SHARED, AT_DOWN)
    gains = summed(AT_GAIN, SENT_ROWS)
    row = lax.broadcasted_iota(jnp.int32, (16, HEAD_DIM), 0)
    one_lane = lax.broadcasted_iota(jnp.int32, (1, HEAD_DIM), 1)
    for i in range(N_EXP):
        m, offset = (96 * i) // HEAD_DIM, (96 * i) % HEAD_DIM
        gain = gains[m : m + 1]
        if offset:
            shift = HEAD_DIM - offset
            gain = jnp.where(
                one_lane < shift,
                pltpu.roll(gain, shift, 1),
                pltpu.roll(gains[m + 1 : m + 2], shift, 1),
            )
        rows = jnp.where(row == 12, jnp.broadcast_to(gain, (16, HEAD_DIM)), shared[16 * i : 16 * i + 16])
        sent_ref[i, 96:, :HEAD_DIM] = rows.astype(bf16)
        sent_ref[i, 96:, HEAD_DIM:] = jnp.zeros((16, 512 - HEAD_DIM), bf16)


def column_grads(got, hidden_seq, att_seq):
    return pl.pallas_call(
        columns_kernel,
        out_shape=[
            jax.ShapeDtypeStruct((N_EXP, 112, 512), bf16),
            jax.ShapeDtypeStruct((N_CTX, BLOCK, HEAD_DIM), bf16),
            jax.ShapeDtypeStruct((96, HEAD_DIM), bf16),
        ],
        cost_estimate=cost(8),
        compiler_params=params(56),
        name="column_grads",
    )(got, hidden_seq, att_seq)


OWNED_ROWS = 4 * 96 + 16 * N_EXP + 96


def owned_kernel(got_ref, down_ref, owned_ref, gain_ref):
    total = got_ref[0, :96].astype(f32)
    gains = got_ref[0, 96:, :HEAD_DIM].astype(f32)
    for src in range(1, N_EXP):
        total = total + got_ref[src, :96].astype(f32)
        gains = gains + got_ref[src, 96:, :HEAD_DIM].astype(f32)
    gain_ref[...] = gains
    for t in range(4):
        owned_ref[96 * t : 96 * t + 96] = total[:, HEAD_DIM * t : HEAD_DIM * (t + 1)].astype(bf16)
    for src in range(N_EXP):
        at = 384 + 16 * src
        owned_ref[at : at + 16] = got_ref[src, 96:, :HEAD_DIM]
    owned_ref[384 + 16 * N_EXP :] = down_ref[...]


def owned_sums(got, down):
    return pl.pallas_call(
        owned_kernel,
        out_shape=[
            jax.ShapeDtypeStruct((OWNED_ROWS, HEAD_DIM), bf16),
            jax.ShapeDtypeStruct((16, HEAD_DIM), f32),
        ],
        cost_estimate=cost(3),
        compiler_params=params(32),
        name="owned_sums",
    )(got, down)


def finish_kernel(
    got_ref,
    gain_in_ref,
    wq_ref,
    wk_ref,
    wv_ref,
    gain_ref,
    q_ref,
    k_ref,
    v_ref,
    out_ref,
    sg_ref,
    su_ref,
    sd_ref,
):
    lane = lax.broadcasted_iota(jnp.int32, (96, HEAD_DIM), 1)

    def tile(c, t):
        return got_ref[c, 96 * t : 96 * t + 96].astype(f32)

    for c in range(N_CTX):
        at = HEAD_DIM * c
        q_ref[:, at : at + HEAD_DIM] = tile(c, 0)
        out_ref[:, at : at + HEAD_DIM] = tile(c, 2)
    for m in range(N_CTX // 2):
        at = HEAD_DIM * m
        low, high = halves(tile(2 * m, 1), tile(2 * m + 1, 1), lane)
        q_ref[:, 1024 + at : 1024 + at + HEAD_DIM] = low
        out_ref[:, 1024 + at : 1024 + at + HEAD_DIM] = high
        low, high = halves(tile(2 * m, 3), tile(2 * m + 1, 3), lane)
        k_ref[:, at : at + HEAD_DIM] = low
        v_ref[:, at : at + HEAD_DIM] = high
    gain = (
        jnp.sum(q_ref[...] * wq_ref[...].astype(f32), axis=1, keepdims=True)
        + jnp.sum(k_ref[...] * wk_ref[...].astype(f32), axis=1, keepdims=True)
        + jnp.sum(v_ref[...] * wv_ref[...].astype(f32), axis=1, keepdims=True)
    ) / gain_in_ref[...]
    gain_ref[...] = jnp.broadcast_to(gain, (96, HEAD_DIM))
    row = lax.broadcasted_iota(jnp.int32, (96, HEAD_DIM), 0)
    picks = jnp.where((lane % 16 < 12) & (row == 12 * (lane // 16) + lane % 16), 1.0, 0.0)
    picks = picks.astype(bf16)

    def shared_tile(j):
        at = 384 + 16 * j
        rows = jnp.concatenate([got_ref[c, at : at + 16] for c in range(N_CTX)], axis=0)
        return dg(picks, rows, NN)

    for m in range(N_EXP // 2):
        at = HEAD_DIM * m
        low, high = halves(shared_tile(2 * m), shared_tile(2 * m + 1), lane)
        sg_ref[:, at : at + HEAD_DIM] = low
        su_ref[:, at : at + HEAD_DIM] = high
    for c in range(N_CTX):
        rows = got_ref[c, 384 + 16 * N_EXP :].astype(f32)
        for m in range(HEADS):
            sd_ref[8 * c : 8 * c + 8, HEAD_DIM * m : HEAD_DIM * (m + 1)] = rows[8 * m : 8 * m + 8]


def finish(got, gain_column, query_weight, key_weight, value_weight):
    shapes = [(96, 128), (96, 1536), (96, 512), (96, 512), (96, 1536), (96, 1024), (96, 1024)]
    return pl.pallas_call(
        finish_kernel,
        out_shape=[jax.ShapeDtypeStruct(s, f32) for s in shapes + [(SHARED, WIDTH)]],
        cost_estimate=cost(4),
        compiler_params=params(32),
        name="finish",
    )(got, gain_column, query_weight, key_weight, value_weight)


def input_kernel(dq_ref, got_ref, wq_ref, wkv_ref, x_ref, gain_ref, gm_ref, out_ref):
    lane = lax.broadcasted_iota(jnp.int32, (BLOCK, HEAD_DIM), 1)
    lows, highs = [], []
    for m in range(KV_HEADS):
        low, high = halves(got_ref[2 * m].astype(f32), got_ref[2 * m + 1].astype(f32), lane)
        lows.append(low.astype(bf16))
        highs.append(high.astype(bf16))
    grad_kv = jnp.concatenate(lows + highs, axis=1)
    grad_one = dg(dq_ref[...], wq_ref[...], NT) + dg(grad_kv, wkv_ref[...], NT)
    inputs = x_ref[...].astype(f32)
    inv = lax.rsqrt(jnp.mean(inputs * inputs, axis=-1, keepdims=True) + epsilon)
    out_ref[...] = (gm_ref[...] + norm_back(grad_one * gain_ref[...], inputs * inv, inv)).astype(bf16)


def input_back(grad_query, grad_kv, w_all, tokens, gain, grad_middle):
    return pl.pallas_call(
        input_kernel,
        grid=(1,),
        in_specs=[
            whole((BLOCK, WIDTH)),
            whole((N_CTX, BLOCK, HEAD_DIM)),
            w_cols(WIDTH, 0),
            w_cols(2 * KV_WIDTH, 3),
            whole((BLOCK, WIDTH)),
            whole((1, WIDTH)),
            whole((BLOCK, WIDTH)),
        ],
        out_specs=whole((BLOCK, WIDTH)),
        out_shape=jax.ShapeDtypeStruct((BLOCK, WIDTH), bf16),
        cost_estimate=cost(7),
        compiler_params=params(48),
        name="input_back",
    )(grad_query, grad_kv, w_all, w_all, tokens, gain, grad_middle)


def norm_rows_kernel(x_ref, gain_ref, out_ref):
    inputs = x_ref[0].astype(f32)
    inv = lax.rsqrt(jnp.mean(inputs * inputs, axis=-1, keepdims=True) + epsilon)
    out_ref[0] = (inputs * inv * gain_ref[...]).astype(bf16)


def norm_rows(rows, gain):
    count = rows.shape[0]
    spec = pl.BlockSpec((1, BLOCK, WIDTH), lambda i: (i, 0, 0))
    turned = pl.BlockSpec((1, BLOCK, WIDTH), lambda i: ((i % 2) * 4 + i // 2, 0, 0))
    return pl.pallas_call(
        norm_rows_kernel,
        grid=(count,),
        in_specs=[spec, whole((1, WIDTH))],
        out_specs=spec if count == 1 else turned,
        out_shape=jax.ShapeDtypeStruct(rows.shape, bf16),
        cost_estimate=cost(2),
        compiler_params=params(32),
        name="norm_rows",
    )(rows, gain)


def project_kernel(own_ref, seq_ref, w_ref, q_ref, kv_ref):
    step = pl.program_id(0)

    @pl.when(step < 3)
    def _():
        q_ref[...] = dg(own_ref[0], w_ref[...], NN).astype(bf16)

    @pl.when(step >= 3)
    def _():
        rows = seq_ref[...].reshape(N_CTX * BLOCK, WIDTH)
        kv_ref[...] = dg(rows, w_ref[...], NN).astype(bf16).reshape(N_CTX, BLOCK, KV_WIDTH)


def project(own, seq, w_all):
    return pl.pallas_call(
        project_kernel,
        grid=(5,),
        in_specs=[
            whole((1, BLOCK, WIDTH)),
            whole((N_CTX, BLOCK, WIDTH)),
            pl.BlockSpec((WIDTH, KV_WIDTH), lambda i: (0, jnp.where(i < 3, i, i + 3))),
        ],
        out_specs=[
            pl.BlockSpec((BLOCK, KV_WIDTH), lambda i: (0, jnp.minimum(i, 2))),
            pl.BlockSpec((N_CTX, BLOCK, KV_WIDTH), lambda i: (0, 0, jnp.maximum(i - 3, 0))),
        ],
        out_shape=[
            jax.ShapeDtypeStruct((BLOCK, WIDTH), bf16),
            jax.ShapeDtypeStruct((N_CTX, BLOCK, 2 * KV_WIDTH), bf16),
        ],
        cost_estimate=cost(8),
        compiler_params=params(48),
        name="project",
    )(own, seq, w_all)


PIECE = 2 * WIDTH + WIDTH * BLOCK // HEAD_DIM


def of_step(values, step):
    out = jnp.int32(values[0])
    for i, value in enumerate(values[1:], 1):
        out = jnp.where(step == i, value, out)
    return out


def expert_weights_kernel(halved, at_ref, x_ref, geo_ref, act_ref, dgate_ref, dup_ref, *outs):
    step = pl.program_id(0)
    rhs = jnp.concatenate([dgate_ref[0], dup_ref[0]], axis=1)
    both = dg(x_ref[0], rhs, TN).astype(bf16)
    down = dg(act_ref[0], geo_ref[0], TN).astype(bf16)
    for i in range(4):

        @pl.when(step == i)
        def _():
            start = (i % 2) * PIECE if halved else 0
            out = outs[i // 2 if halved else i].at[pl.ds(start, PIECE)]
            out[:WIDTH] = both[:, :HEAD_DIM]
            out[WIDTH : 2 * WIDTH] = both[:, HEAD_DIM:]
            for m in range(WIDTH // HEAD_DIM):
                at = 2 * WIDTH + m * BLOCK
                out[at : at + BLOCK] = down[:, m * HEAD_DIM : (m + 1) * HEAD_DIM]


def expert_weights(ctx_at, steps, halved, arrived, grad_eo, act, grad_gu):
    rows = 2 * ROWS

    def expert(s, at):
        return (at[0] >> 2) ^ of_step([side for _, side in steps], s)

    def lanes(shift):
        return pl.BlockSpec(
            (1, rows, HEAD_DIM),
            lambda s, at: (
                expert(s, at),
                0,
                shift + ((at[0] & 3) ^ of_step([r for r, _ in steps], s)),
            ),
        )

    rows_of = pl.BlockSpec((1, rows, WIDTH), lambda s, at: (expert(s, at), 0, 0))
    count, length = (2, 2 * PIECE) if halved else (4, PIECE)
    return pl.pallas_call(
        lambda *refs: expert_weights_kernel(halved, *refs),
        grid_spec=pltpu.PrefetchScalarGridSpec(
            num_scalar_prefetch=1,
            grid=(4,),
            in_specs=[rows_of, rows_of, lanes(0), lanes(0), lanes(4)],
            out_specs=[whole((length, HEAD_DIM))] * count,
        ),
        out_shape=[jax.ShapeDtypeStruct((length, HEAD_DIM), bf16)] * count,
        cost_estimate=cost(9),
        compiler_params=params(56),
        name="expert_weights",
    )(ctx_at, arrived, grad_eo, act, grad_gu, grad_gu)


def unpack_kernel(count, at_ref, *refs):
    pieces, (gate_ref, up_ref, down_ref) = refs[:count], refs[-3:]
    step = pl.program_id(0)
    for i in range(count):

        @pl.when(step == i)
        def _():
            piece = pieces[i]
            gate_ref[0] = piece[:WIDTH].astype(f32)
            up_ref[0] = piece[WIDTH : 2 * WIDTH].astype(f32)
            for m in range(WIDTH // HEAD_DIM):
                at = 2 * WIDTH + m * BLOCK
                down_ref[0, :, m * HEAD_DIM : (m + 1) * HEAD_DIM] = piece[at : at + BLOCK].astype(
                    f32
                )


def unpack_experts(ctx_at, steps, pieces, filled=()):
    count = len(steps)

    def expert(s, at):
        return (at[0] >> 2) ^ of_step([side for _, side in steps], s)

    def units(s, at):
        return (at[0] & 3) ^ of_step([r for r, _ in steps], s)

    cols = pl.BlockSpec((1, WIDTH, HEAD_DIM), lambda s, at: (expert(s, at), 0, units(s, at)))
    rows = pl.BlockSpec((1, BLOCK, WIDTH), lambda s, at: (expert(s, at), units(s, at), 0))
    anywhere = pl.BlockSpec(memory_space=pl.ANY)
    return pl.pallas_call(
        lambda *refs: unpack_kernel(count, *refs),
        grid_spec=pltpu.PrefetchScalarGridSpec(
            num_scalar_prefetch=1,
            grid=(count,),
            in_specs=[whole((PIECE, HEAD_DIM))] * count + [anywhere] * len(filled),
            out_specs=[cols, cols, rows],
        ),
        out_shape=[
            jax.ShapeDtypeStruct((LOCAL_E, WIDTH, FF_E), f32),
            jax.ShapeDtypeStruct((LOCAL_E, WIDTH, FF_E), f32),
            jax.ShapeDtypeStruct((LOCAL_E, FF_E, WIDTH), f32),
        ],
        input_output_aliases={1 + count + i: i for i in range(len(filled))},
        cost_estimate=cost(2 * count),
        compiler_params=params(48),
        name="unpack_experts",
    )(ctx_at, *pieces, *filled)


def relay_kernel(
    p0, p1, p3, p6, relay_a, relay_b, got_10, got_31, add_a, add_b, part_0, part_1
):
    add_a[...] = (p6[...].astype(f32) + relay_a[...].astype(f32)).astype(bf16)
    add_b[...] = (p3[...].astype(f32) + relay_b[...].astype(f32)).astype(bf16)
    part_0[...] = p0[...].astype(f32) + got_10[...].astype(f32)
    part_1[...] = p1[...].astype(f32) + got_31[...].astype(f32)


def side_kernel(part_0, part_1, got_11, got_30, own, side):
    own[...] = part_0[...] + got_30[...].astype(f32)
    side[...] = (part_1[...] + got_11[...].astype(f32)).astype(bf16)


def piece_sums(kernel, kinds, *pieces):
    specs, arrays = [], []
    for piece in pieces:
        array, second = piece if isinstance(piece, tuple) else (piece, 0)
        specs.append(pl.BlockSpec((PIECE // 4, HEAD_DIM), lambda i, at=4 * second: (i + at, 0)))
        arrays.append(array)
    return pl.pallas_call(
        kernel,
        grid=(4,),
        in_specs=specs,
        out_specs=[pl.BlockSpec((PIECE // 4, HEAD_DIM), lambda i: (i, 0))] * len(kinds),
        out_shape=[jax.ShapeDtypeStruct((PIECE, HEAD_DIM), kind) for kind in kinds],
        cost_estimate=cost(4),
        compiler_params=params(32),
        name="piece_sums",
    )(*arrays)


same_core = [[2 * i + c for i in range(8)] for c in range(2)]
core_swap = [(i, i ^ 1) for i in range(N_EXP)]
y_groups = [[0, 1, 2, 3], [4, 5, 6, 7]]
z_swap = [(i, i ^ 4) for i in range(N_CTX)]


def swap_all(rows, axis, groups=None):
    return lax.all_to_all(
        rows, axis, split_axis=0, concat_axis=0, tiled=True, axis_index_groups=groups
    )


def after(value, *others):
    return lax.optimization_barrier((value,) + others)[0]


def add_low(a, b):
    return (a.astype(f32) + b.astype(f32)).astype(bf16)


def on_device(
    tokens,
    routes,
    route_gates,
    norm_attn,
    norm_ffn,
    query_weight,
    key_weight,
    value_weight,
    out_weight,
    shared_gate,
    shared_up,
    shared_down,
    expert_gate,
    expert_up,
    expert_down,
    cotangent,
):
    exp_at = lax.axis_index("exp").astype(jnp.int32)
    ctx_at = lax.axis_index("ctx").astype(jnp.int32)
    exp_s, ctx_s = exp_at.reshape(1), ctx_at.reshape(1)

    z_at = ctx_at // 4

    w_cat = jnp.concatenate([query_weight, out_weight, key_weight, value_weight], axis=1)
    w_all = lax.all_gather(w_cat, "exp", axis=0, tiled=True)
    gates_high = route_gates[0].astype(bf16)
    gates_low = (route_gates[0] - gates_high.astype(f32)).astype(bf16)
    pad = jnp.zeros((BLOCK, META - 3 * TOPK), bf16)
    up_meta = jnp.concatenate(
        [cotangent[0], routes[0].astype(bf16), gates_high, gates_low, pad], axis=1
    )
    up_all = lax.all_gather(after(up_meta, w_cat), "exp", axis=0, tiled=True)
    gains = after(jnp.concatenate([norm_attn, norm_ffn]), w_cat)
    gains = swap_all(jnp.broadcast_to(gains, (N_EXP, gains.shape[0])), "exp")
    gain_attn = gains[:, :96].reshape(1, WIDTH).astype(f32)
    gain_ffn = gains[:, 96:].reshape(1, WIDTH).astype(f32)

    def of_sequence(rows):
        other = lax.ppermute(rows, "ctx", z_swap)
        pair = jnp.where(
            z_at == 0,
            jnp.concatenate([rows, other], axis=0),
            jnp.concatenate([other, rows], axis=0),
        )
        got = swap_all(jnp.broadcast_to(pair, (4, 2, BLOCK, WIDTH)), "ctx", y_groups)
        return got.reshape(N_CTX, BLOCK, WIDTH)

    tokens_seq = of_sequence(after(tokens, w_cat))
    shared_cols = jnp.concatenate(
        [shared_gate.reshape(96, N_EXP, SHARED), shared_up.reshape(96, N_EXP, SHARED)], axis=2
    ).transpose(1, 0, 2)
    w_shared = swap_all(shared_cols, "exp").reshape(WIDTH, 2 * SHARED)
    shared_two = jnp.concatenate([shared_down, shared_down], axis=0)

    hidden_one = norm_rows(tokens, gain_attn)
    hidden_seq = norm_rows(tokens_seq, gain_attn)
    hidden_seq = after(hidden_seq, w_shared)
    queries, kv_all = project(hidden_one, hidden_seq, w_all)
    attended, att_f, logs = attend(ctx_s, queries, kv_all)
    middle, hidden_two = middle_norm(attended, w_all, tokens[0], gain_ffn)

    hidden_all = lax.all_gather(hidden_two, "exp", axis=0, tiled=True)
    hidden_all = hidden_all.reshape(HALF, 2, BLOCK, WIDTH)
    att_seq = of_sequence(attended[None])
    place, grad_eo, grad_eh, grad_sh, slot_gate = place_rows(
        exp_s,
        after(up_all, hidden_two).reshape(HALF, 2, BLOCK, WIDTH + META),
        expert_down,
        shared_two,
    )
    part, arrived, act, grad_gu, shared_act, shared_grad = expert_back(
        exp_s, after(hidden_all, att_seq), place, grad_eh, grad_sh, expert_gate, expert_up, w_shared
    )
    summed = add_low(part[1], lax.ppermute(part[0], "exp", core_swap))
    grad_two = swap_all(summed, "exp", same_core)

    rows_e = 2 * ROWS
    operands = (
        after(arrived, summed).reshape(LOCAL_E, rows_e, WIDTH),
        grad_eo.reshape(LOCAL_E, rows_e, WIDTH),
        act.reshape(LOCAL_E, rows_e, FF_E),
        grad_gu.reshape(LOCAL_E, rows_e, 2 * FF_E),
    )
    for_1, for_3 = expert_weights(ctx_s, ((2, 0), (1, 0), (2, 1), (3, 1)), True, *operands)
    operands = (after(operands[0], for_1),) + operands[1:]
    p0, p6, p1, p3 = expert_weights(ctx_s, ((0, 0), (3, 0), (0, 1), (1, 1)), False, *operands)

    def to(rows, k):
        return lax.ppermute(rows, "ctx", [(i, i ^ k) for i in range(N_CTX)])

    from_1, from_3 = to(for_1, 1), to(for_3, 3)
    shared_grad_late = after(shared_grad, p0).reshape(N_EXP * BLOCK, META)
    grad_scols = dg(hidden_all.reshape(N_EXP * BLOCK, WIDTH), shared_grad_late, TN).astype(bf16)
    act_late = after(shared_act, p0).reshape(N_EXP * BLOCK, META)
    grad_sdown = dg(act_late, up_all, TN)[:SHARED, :WIDTH].astype(bf16)

    extra = jnp.concatenate(
        [
            jnp.pad(
                grad_scols.reshape(N_EXP, N_CTX, 12, META).transpose(1, 0, 2, 3),
                ((0, 0), (0, 0), (0, 4), (0, 0)),
            ).reshape(N_CTX, 16 * N_EXP, META),
            grad_sdown.reshape(N_CTX, 8, HEADS, 128).transpose(0, 2, 1, 3).reshape(N_CTX, 96, 128),
        ],
        axis=1,
    )
    grad_two = after(grad_two, p0, extra)
    grad_middle, grad_attn, grad_heads, gain_rows = middle_back(
        grad_two, middle, cotangent[0], gain_ffn, w_all
    )
    grad_query, sent = attend_back(
        ctx_s, queries, grad_heads, att_f, logs, kv_all, grad_attn, extra, gain_rows
    )
    from_1, from_3 = after((from_1, from_3), sent)
    add_a, add_b, part_0, part_1 = piece_sums(
        relay_kernel,
        (bf16, bf16, f32, f32),
        p0,
        p1,
        p3,
        p6,
        (from_1, 0),
        (from_3, 0),
        (from_1, 1),
        (from_3, 1),
    )
    got_11, got_30 = to(add_b, 1), to(add_a, 3)
    got = swap_all(after(sent, add_a), "ctx")

    columns, grad_kv, grad_down = column_grads(got, hidden_seq, att_seq)
    grad_kv = swap_all(grad_kv, "ctx")
    got_11, got_30, columns = after((got_11, got_30, columns), grad_kv)
    own_part, side = piece_sums(side_kernel, (f32, bf16), part_0, part_1, got_11, got_30)
    across = to(side, 4)
    owned = swap_all(columns, "exp")
    out_part = expert_output(
        exp_s, after(act, columns), slot_gate, place, shared_act, expert_down, shared_two
    )
    out_sum = add_low(out_part[1], lax.ppermute(out_part[0], "exp", core_swap))
    owned, gain_sum = owned_sums(owned, grad_down)
    own = (own_part + after(across, owned).astype(f32)).astype(bf16)
    at_1, at_3, at_z = to(own, 1), to(own, 3), to(own, 4)
    owned = swap_all(jnp.broadcast_to(owned, (N_CTX, OWNED_ROWS, HEAD_DIM)), "ctx")
    experts = unpack_experts(
        ctx_s, ((0, 0), (1, 0), (3, 0), (0, 1)), (own, at_1, at_3, at_z)
    )
    gain_attn_sum, *dense = finish(
        after(owned, experts[0]),
        norm_attn.astype(f32).reshape(96, 1),
        query_weight,
        key_weight,
        value_weight,
    )

    at_z1, at_z3 = to(at_z, 1), to(at_z, 3)
    at_2, at_z2 = to(at_3, 1), to(at_z1, 3)
    out_pieces = swap_all(after(out_sum, owned, experts[0]), "exp", same_core)
    mixed = (middle + jnp.sum(out_pieces.astype(f32), axis=0)).astype(bf16)[None]
    experts = unpack_experts(ctx_s, ((1, 1), (3, 1)), (at_z1, at_z3), experts)
    input_grad = input_back(
        after(grad_query, experts[0]),
        grad_kv,
        w_all,
        tokens[0],
        gain_attn,
        grad_middle,
    )
    at_2 = after(at_2, mixed, input_grad, *dense)
    experts = unpack_experts(ctx_s, ((2, 0), (2, 1)), (at_2, at_z2), experts)
    return (
        mixed,
        input_grad[None],
        gain_attn_sum[:, 0],
        gain_sum[12, :96],
        *dense,
        *experts,
    )


def solution(mesh):
    token_spec = P("exp", "ctx", None)
    rows = P("exp", None)
    expert = P("exp", None, None)
    placed = (token_spec,) * 3 + (P("exp"),) * 2 + (rows,) * 7 + (expert,) * 3 + (token_spec,)
    return jax.shard_map(
        on_device,
        mesh=mesh,
        in_specs=placed,
        out_specs=(token_spec,) * 2 + (P("exp"),) * 2 + (rows,) * 7 + (expert,) * 3,
        check_vma=False,
    )
```

```python
import jax
import jax.numpy as jnp
from jax import lax
from jax.sharding import PartitionSpec as P
from jax.experimental import pallas as pl
from jax.experimental.pallas import tpu as pltpu

HEADS = 12
KV_HEADS = 4
HEAD_DIM = 128
TOPK = 6
GROUP = 3
BLOCK = 128
WIDTH = 1536
KV_WIDTH = KV_HEADS * HEAD_DIM
CAP = 48
N_EXP = 16
N_CTX = 8
LOCAL_E = 2
FF_E = 512
SHARED = 64
META = 128
HALF = 8
ROWS = HALF * CAP

epsilon = 1e-05
masked_score = -1e30
f32 = jnp.float32
bf16 = jnp.bfloat16
log2_e = 1.4426950408889634
score_scale = HEAD_DIM ** (-0.5) * log2_e

NN = (((1,), (0,)), ((), ()))
NT = (((1,), (1,)), ((), ()))
TN = (((0,), (0,)), ((), ()))


def dg(a, b, dims):
    return lax.dot_general(a, b, dims, preferred_element_type=f32)


def params(mib):
    return pltpu.CompilerParams(vmem_limit_bytes=mib * 1024 * 1024)


def cost(us):
    return pl.CostEstimate(flops=0, bytes_accessed=int(us * 3690000), transcendentals=0)


def whole(shape):
    return pl.BlockSpec(shape, lambda *_: (0,) * len(shape), pipeline_mode=pl.Buffered(1))


def sigmoid(v):
    return 1.0 / (1.0 + jnp.exp(-v))


def allowed_scores(ctx_at):
    rows = lax.broadcasted_iota(jnp.int32, (GROUP * BLOCK, N_CTX * BLOCK), 0) % BLOCK
    cols = lax.broadcasted_iota(jnp.int32, (GROUP * BLOCK, N_CTX * BLOCK), 1)
    return rows + ctx_at * BLOCK >= cols


def stack_heads(block):
    return jnp.concatenate([block[:, j * HEAD_DIM : (j + 1) * HEAD_DIM] for j in range(GROUP)], axis=0)


def unstack_heads(rows):
    return jnp.concatenate([rows[j * BLOCK : (j + 1) * BLOCK] for j in range(GROUP)], axis=1)


def attend_kernel(ctx_ref, q_ref, k_ref, v_ref, att_ref, attf_ref, log_ref):
    q = stack_heads(q_ref[...])
    keys = k_ref[...].reshape(N_CTX * BLOCK, HEAD_DIM)
    values = v_ref[...].reshape(N_CTX * BLOCK, HEAD_DIM)
    scores = jnp.where(allowed_scores(ctx_ref[0]), dg(q, keys, NT) * score_scale, masked_score)
    top = jnp.max(scores, axis=-1, keepdims=True)
    weights = jnp.exp2(scores - top)
    total = jnp.sum(weights, axis=-1, keepdims=True)
    out = dg(weights.astype(bf16), values, NN) * (1.0 / total)
    out = unstack_heads(out)
    attf_ref[...] = out
    att_ref[...] = out.astype(bf16)
    log_ref[...] = jnp.broadcast_to(top + jnp.log2(total), (GROUP * BLOCK, HEAD_DIM))


def kv_specs():
    return [
        pl.BlockSpec((N_CTX, BLOCK, HEAD_DIM), lambda g: (0, 0, g)),
        pl.BlockSpec((N_CTX, BLOCK, HEAD_DIM), lambda g: (0, 0, KV_HEADS + g)),
    ]


def head_spec():
    return pl.BlockSpec((BLOCK, GROUP * HEAD_DIM), lambda g: (0, g))


def attend(ctx_at, qkv, kv_all):
    return pl.pallas_call(
        attend_kernel,
        grid=(KV_HEADS,),
        in_specs=[pl.BlockSpec(memory_space=pltpu.SMEM), head_spec()] + kv_specs(),
        out_specs=[
            head_spec(),
            head_spec(),
            pl.BlockSpec((GROUP * BLOCK, HEAD_DIM), lambda g: (g, 0)),
        ],
        out_shape=[
            jax.ShapeDtypeStruct((BLOCK, WIDTH), bf16),
            jax.ShapeDtypeStruct((BLOCK, WIDTH), f32),
            jax.ShapeDtypeStruct((HEADS * BLOCK, HEAD_DIM), f32),
        ],
        cost_estimate=cost(6),
        compiler_params=params(48),
        name="attend",
    )(ctx_at, qkv, kv_all, kv_all)


SEQ = N_CTX * BLOCK
AT_QUERY, AT_MIXED, AT_OUT = SEQ, SEQ + BLOCK, SEQ + 2 * BLOCK
AT_SHARED = SEQ + 3 * BLOCK
AT_DOWN = AT_SHARED + 16 * N_EXP
AT_GAIN = AT_DOWN + 96
SENT_ROWS = AT_GAIN + 16


def halves(a, b, lane):
    low = jnp.where(lane < 64, a, pltpu.roll(b, 64, 1))
    high = jnp.where(lane < 64, pltpu.roll(a, 64, 1), b)
    return low, high


def attend_back_kernel(
    ctx_ref,
    q_ref,
    ga_ref,
    attf_ref,
    log_ref,
    k_ref,
    v_ref,
    all_ga_ref,
    extra_ref,
    gain_ref,
    dq_ref,
    sent_ref,
    kept_ref,
):
    group = pl.program_id(0)
    q = stack_heads(q_ref[...])
    grad = stack_heads(ga_ref[...])
    delta = jnp.sum(grad.astype(f32) * stack_heads(attf_ref[...]), axis=-1, keepdims=True)
    keys = k_ref[...].reshape(SEQ, HEAD_DIM)
    values = v_ref[...].reshape(SEQ, HEAD_DIM)
    scores = jnp.where(allowed_scores(ctx_ref[0]), dg(q, keys, NT) * score_scale, masked_score)
    weights = jnp.exp2(scores - log_ref[:, :1])
    grad_weights = dg(grad, values, NT)
    grad_raw = (weights * (grad_weights - delta)).astype(bf16)
    scale = HEAD_DIM ** (-0.5)
    dq = unstack_heads(dg(grad_raw, keys, NN) * scale)
    dq_ref[...] = dq.astype(bf16)
    kept_ref[group] = dq
    grad_k = dg(grad_raw, q, TN) * scale
    grad_v = dg(weights.astype(bf16), grad, TN)
    low, high = halves(grad_k, grad_v, lax.broadcasted_iota(jnp.int32, (SEQ, HEAD_DIM), 1))
    sent_ref[2 * group, :SEQ] = low.astype(bf16)
    sent_ref[2 * group + 1, :SEQ] = high.astype(bf16)

    @pl.when(group == KV_HEADS - 1)
    def _():
        lane = lax.broadcasted_iota(jnp.int32, (BLOCK, HEAD_DIM), 1)

        def dq_tile(m):
            return kept_ref[m // GROUP, :, HEAD_DIM * (m % GROUP) : HEAD_DIM * (m % GROUP + 1)]

        def ga_tile(m):
            return all_ga_ref[:, HEAD_DIM * m : HEAD_DIM * (m + 1)].astype(f32)

        for m in range(KV_HEADS):
            low, high = halves(dq_tile(N_CTX + m), ga_tile(N_CTX + m), lane)
            sent_ref[2 * m, AT_MIXED:AT_OUT] = low.astype(bf16)
            sent_ref[2 * m + 1, AT_MIXED:AT_OUT] = high.astype(bf16)
        gains = gain_ref[...].astype(bf16)
        for c in range(N_CTX):
            sent_ref[c, AT_QUERY:AT_MIXED] = dq_tile(c).astype(bf16)
            sent_ref[c, AT_OUT:AT_SHARED] = ga_tile(c).astype(bf16)
            sent_ref[c, AT_SHARED:AT_GAIN] = extra_ref[c]
            sent_ref[c, AT_GAIN:] = gains


def attend_back(ctx_at, qkv, grad_att, att_f, logs, kv_all, grad_attn, extra, gain_rows):
    return pl.pallas_call(
        attend_back_kernel,
        grid=(KV_HEADS,),
        in_specs=[
            pl.BlockSpec(memory_space=pltpu.SMEM),
            head_spec(),
            head_spec(),
            head_spec(),
            pl.BlockSpec((GROUP * BLOCK, HEAD_DIM), lambda g: (g, 0)),
        ]
        + kv_specs()
        + [
            whole((BLOCK, WIDTH)),
            whole((N_CTX, AT_GAIN - AT_SHARED, HEAD_DIM)),
            whole((16, HEAD_DIM)),
        ],
        out_specs=[head_spec(), whole((N_CTX, SENT_ROWS, HEAD_DIM))],
        out_shape=[
            jax.ShapeDtypeStruct((BLOCK, WIDTH), bf16),
            jax.ShapeDtypeStruct((N_CTX, SENT_ROWS, HEAD_DIM), bf16),
        ],
        scratch_shapes=[pltpu.VMEM((KV_HEADS, BLOCK, GROUP * HEAD_DIM), f32)],
        cost_estimate=cost(2),
        compiler_params=params(48),
        name="attend_back",
    )(ctx_at, qkv, grad_att, att_f, logs, kv_all, kv_all, grad_attn, extra, gain_rows)


def middle_kernel(att_ref, w_ref, x_ref, gain_ref, middle_ref, hidden_ref):
    middle = x_ref[...].astype(f32) + dg(att_ref[...], w_ref[...], NN)
    inv = lax.rsqrt(jnp.mean(middle * middle, axis=-1, keepdims=True) + epsilon)
    middle_ref[...] = middle
    hidden_ref[...] = (middle * inv * gain_ref[...]).astype(bf16)


def w_cols(width, at):
    return pl.BlockSpec((WIDTH, width), lambda *_: (0, at), pipeline_mode=pl.Buffered(1))


def middle_norm(attended, w_all, tokens, gain):
    return pl.pallas_call(
        middle_kernel,
        grid=(1,),
        in_specs=[
            whole((BLOCK, WIDTH)),
            w_cols(WIDTH, 1),
            whole((BLOCK, WIDTH)),
            whole((1, WIDTH)),
        ],
        out_specs=[whole((BLOCK, WIDTH)), whole((BLOCK, WIDTH))],
        out_shape=[
            jax.ShapeDtypeStruct((BLOCK, WIDTH), f32),
            jax.ShapeDtypeStruct((BLOCK, WIDTH), bf16),
        ],
        cost_estimate=cost(2),
        compiler_params=params(32),
        name="middle_norm",
    )(attended, w_all, tokens, gain)


def norm_back(grad_normed, normed, inv_root):
    return inv_root * (
        grad_normed - normed * jnp.mean(grad_normed * normed, axis=-1, keepdims=True)
    )


def middle_back_kernel(
    pieces_ref, middle_ref, up_ref, gain_ref, w_ref, gm_ref, ga_ref, gh_ref, gg_ref
):
    grad_two = pieces_ref[0].astype(f32)
    for i in range(1, HALF):
        grad_two = grad_two + pieces_ref[i].astype(f32)
    middle = middle_ref[...]
    inv = lax.rsqrt(jnp.mean(middle * middle, axis=-1, keepdims=True) + epsilon)
    normed = middle * inv
    gains = jnp.sum(grad_two * normed, axis=0, keepdims=True)
    gg_ref[...] = jnp.zeros((16, HEAD_DIM), f32)
    for m in range(HEADS):
        gg_ref[m : m + 1] = gains[:, HEAD_DIM * m : HEAD_DIM * (m + 1)]
    grad_middle = up_ref[...].astype(f32) + norm_back(grad_two * gain_ref[...], normed, inv)
    gm_ref[...] = grad_middle
    grad_attn = grad_middle.astype(bf16)
    ga_ref[...] = grad_attn
    gh_ref[...] = dg(grad_attn, w_ref[...], NT).astype(bf16)


def middle_back(pieces, middle, upstream, gain, w_all):
    return pl.pallas_call(
        middle_back_kernel,
        grid=(1,),
        in_specs=[
            whole((HALF, BLOCK, WIDTH)),
            whole((BLOCK, WIDTH)),
            whole((BLOCK, WIDTH)),
            whole((1, WIDTH)),
            w_cols(WIDTH, 1),
        ],
        out_specs=[whole((BLOCK, WIDTH))] * 3 + [whole((16, HEAD_DIM))],
        out_shape=[
            jax.ShapeDtypeStruct((BLOCK, WIDTH), f32),
            jax.ShapeDtypeStruct((BLOCK, WIDTH), bf16),
            jax.ShapeDtypeStruct((BLOCK, WIDTH), bf16),
            jax.ShapeDtypeStruct((16, HEAD_DIM), f32),
        ],
        cost_estimate=cost(1),
        compiler_params=params(48),
        name="middle_back",
    )(pieces, middle, upstream, gain, w_all)


def place_kernel(
    at_ref, up_ref, down_ref, sdown_ref, place_ref, geo_ref, geh_ref, gsh_ref, gate_ref
):
    lane = lax.broadcasted_iota(jnp.int32, (BLOCK, META), 1)
    row = lax.broadcasted_iota(jnp.int32, (BLOCK, META), 0)
    before = (row > lane).astype(bf16)
    slot = (lane % 64).astype(f32)
    first_id = (at_ref[0] * LOCAL_E).astype(f32)
    row_id = first_id + (row >= 64).astype(f32)

    for chip in range(HALF):
        meta = up_ref[chip, 0, :, WIDTH:].astype(f32)
        named = lane < TOPK
        zero = jnp.zeros((BLOCK, META), f32)
        hit0 = jnp.where(named & (meta == first_id), 1.0, zero)
        hit1 = jnp.where(named & (meta == first_id + 1.0), 1.0, zero)
        mask = jnp.where(
            lane < 64,
            jnp.sum(hit0, axis=1, keepdims=True),
            jnp.sum(hit1, axis=1, keepdims=True),
        )
        rank = dg(before, mask.astype(bf16), NN)
        place = jnp.where((mask > 0.5) & (rank == slot), 1.0, zero).astype(bf16)
        place_ref[chip, 0] = place
        rows = dg(place, up_ref[chip, 0], TN)
        slot_meta = rows[:, WIDTH:]
        gates = pltpu.roll(slot_meta, META - TOPK, 1) + pltpu.roll(
            slot_meta, META - 2 * TOPK, 1
        )
        gate = jnp.sum(
            jnp.where(named & (slot_meta == row_id), gates, zero), axis=1, keepdims=True
        )
        geo = (gate * rows[:, :WIDTH]).astype(bf16)
        wide_gate = jnp.broadcast_to(gate, (BLOCK, META))
        at = chip * CAP
        for e in range(LOCAL_E):
            geo_ref[e, 0, at : at + CAP] = geo[64 * e : 64 * e + CAP]
            gate_ref[e, 0, at : at + CAP] = wide_gate[64 * e : 64 * e + CAP]
        gsh_ref[chip, 0] = dg(up_ref[chip, 0, :, :WIDTH], sdown_ref[...], NT)
    for e in range(LOCAL_E):
        geh_ref[e, 0] = dg(geo_ref[e, 0], down_ref[e], NT)


def by_core(cols):
    return pl.BlockSpec(
        (HALF, 1, BLOCK, cols),
        lambda s, at: (0, jnp.where(s == 0, 1 - at[0] % 2, at[0] % 2), 0, 0),
    )


def by_step(cols):
    return pl.BlockSpec((LOCAL_E, 1, ROWS, cols), lambda s, at: (0, s, 0, 0))


def place_rows(exp_at, up_all, expert_down, shared_two):
    return pl.pallas_call(
        place_kernel,
        grid_spec=pltpu.PrefetchScalarGridSpec(
            num_scalar_prefetch=1,
            grid=(2,),
            in_specs=[
                by_core(WIDTH + META),
                whole((LOCAL_E, FF_E, WIDTH)),
                whole((2 * SHARED, WIDTH)),
            ],
            out_specs=[by_core(META), by_step(WIDTH), by_step(FF_E), by_core(META), by_step(META)],
        ),
        out_shape=[
            jax.ShapeDtypeStruct((HALF, 2, BLOCK, META), bf16),
            jax.ShapeDtypeStruct((LOCAL_E, 2, ROWS, WIDTH), bf16),
            jax.ShapeDtypeStruct((LOCAL_E, 2, ROWS, FF_E), f32),
            jax.ShapeDtypeStruct((HALF, 2, BLOCK, META), f32),
            jax.ShapeDtypeStruct((LOCAL_E, 2, ROWS, META), f32),
        ],
        cost_estimate=cost(14),
        compiler_params=params(56),
        name="place_rows",
    )(exp_at, up_all, expert_down, shared_two)


def store_part(chip, rows, others, own_ref):
    step, each = pl.program_id(0), HALF // len(others)

    @pl.when(step == 0)
    def _():
        others[chip // each][chip % each] = rows

    @pl.when(step == 1)
    def _():
        own_ref[chip] = rows


def expert_kernel(
    at_ref,
    hid_ref,
    place_ref,
    geh_ref,
    gsh_ref,
    wg_ref,
    wu_ref,
    ws_ref,
    other_ref,
    own_ref,
    x_ref,
    act_ref,
    dgu_ref,
    sact_ref,
    sgrad_ref,
):
    for chip in range(HALF):
        rows = dg(place_ref[chip, 0], hid_ref[chip, 0], TN).astype(bf16)
        at = chip * CAP
        for e in range(LOCAL_E):
            x_ref[e, 0, at : at + CAP] = rows[64 * e : 64 * e + CAP]
    pairs = []
    for e in range(LOCAL_E):
        pre_gate = dg(x_ref[e, 0], wg_ref[e], NN)
        pre_up = dg(x_ref[e, 0], wu_ref[e], NN)
        sig = sigmoid(pre_gate)
        act = pre_gate * sig
        act_ref[e, 0] = (act * pre_up).astype(bf16)
        geh = geh_ref[e, 0]
        d_gate = (geh * pre_up * (sig * (1.0 + pre_gate * (1.0 - sig)))).astype(bf16)
        d_up = (geh * act).astype(bf16)
        dgu_ref[e, 0, :, :FF_E] = d_gate
        dgu_ref[e, 0, :, FF_E:] = d_up
        pairs.append((dg(d_gate, wg_ref[e], NT) + dg(d_up, wu_ref[e], NT)).astype(bf16))
    lane = lax.broadcasted_iota(jnp.int32, (BLOCK, 2 * SHARED), 1) < SHARED
    gap = jnp.zeros((64 - CAP, WIDTH), bf16)
    for chip in range(HALF):
        pre = dg(hid_ref[chip, 0], ws_ref[...], NN)
        turned = pltpu.roll(pre, SHARED, 1)
        gate, up = jnp.where(lane, pre, turned), jnp.where(lane, turned, pre)
        sig = sigmoid(gate)
        act = gate * sig
        sact_ref[chip, 0] = jnp.where(lane, act * up, 0.0).astype(bf16)
        slope = sig * (1.0 + gate * (1.0 - sig))
        sgrad = (gsh_ref[chip, 0] * jnp.where(lane, up * slope, act)).astype(bf16)
        sgrad_ref[chip, 0] = sgrad
        at = chip * CAP
        stacked = jnp.concatenate([pairs[0][at : at + CAP], gap, pairs[1][at : at + CAP], gap], 0)
        rows = (dg(place_ref[chip, 0], stacked, NN) + dg(sgrad, ws_ref[...], NT)).astype(bf16)
        store_part(chip, rows, (other_ref,), own_ref)


def expert_back(exp_at, hidden, place, geh, gsh, wg, wu, ws):
    return pl.pallas_call(
        expert_kernel,
        grid_spec=pltpu.PrefetchScalarGridSpec(
            num_scalar_prefetch=1,
            grid=(2,),
            in_specs=[
                by_core(WIDTH),
                by_core(META),
                by_step(FF_E),
                by_core(META),
                whole((LOCAL_E, WIDTH, FF_E)),
                whole((LOCAL_E, WIDTH, FF_E)),
                whole((WIDTH, 2 * SHARED)),
            ],
            out_specs=[
                whole((HALF, BLOCK, WIDTH)),
                whole((HALF, BLOCK, WIDTH)),
                by_step(WIDTH),
                by_step(FF_E),
                by_step(2 * FF_E),
                by_core(META),
                by_core(META),
            ],
        ),
        out_shape=[
            jax.ShapeDtypeStruct((HALF, BLOCK, WIDTH), bf16),
            jax.ShapeDtypeStruct((HALF, BLOCK, WIDTH), bf16),
            jax.ShapeDtypeStruct((LOCAL_E, 2, ROWS, WIDTH), bf16),
            jax.ShapeDtypeStruct((LOCAL_E, 2, ROWS, FF_E), bf16),
            jax.ShapeDtypeStruct((LOCAL_E, 2, ROWS, 2 * FF_E), bf16),
            jax.ShapeDtypeStruct((HALF, 2, BLOCK, META), bf16),
            jax.ShapeDtypeStruct((HALF, 2, BLOCK, META), bf16),
        ],
        cost_estimate=cost(28),
        compiler_params=params(60),
        name="expert_back",
    )(exp_at, hidden, place, geh, gsh, wg, wu, ws)


def output_kernel(at_ref, act_ref, gate_ref, place_ref, sact_ref, wd_ref, sd_ref, own_ref, *others):
    outs = []
    for e in range(LOCAL_E):
        out = dg(act_ref[e, 0], wd_ref[e], NN).astype(bf16).astype(f32)
        outs.append((out * gate_ref[e, 0, :, :1]).astype(bf16))
    gap = jnp.zeros((64 - CAP, WIDTH), bf16)
    for chip in range(HALF):
        at = chip * CAP
        stacked = jnp.concatenate([outs[0][at : at + CAP], gap, outs[1][at : at + CAP], gap], 0)
        rows = dg(place_ref[chip, 0], stacked, NN) + dg(sact_ref[chip, 0], sd_ref[...], NN)
        store_part(chip, rows.astype(bf16), others, own_ref)


def expert_output(exp_at, act, gate, place, sact, wd, sd):
    return pl.pallas_call(
        output_kernel,
        grid_spec=pltpu.PrefetchScalarGridSpec(
            num_scalar_prefetch=1,
            grid=(2,),
            in_specs=[
                by_step(FF_E),
                by_step(META),
                by_core(META),
                by_core(META),
                whole((LOCAL_E, FF_E, WIDTH)),
                whole((2 * SHARED, WIDTH)),
            ],
            out_specs=[whole((HALF, BLOCK, WIDTH))] * 2,
        ),
        out_shape=[jax.ShapeDtypeStruct((HALF, BLOCK, WIDTH), bf16)] * 2,
        cost_estimate=cost(2),
        compiler_params=params(48),
        name="expert_output",
    )(exp_at, act, gate, place, sact, wd, sd)


def columns_kernel(got_ref, hidden_ref, att_ref, sent_ref, kv_ref, down_ref):
    total = got_ref[0, :SEQ].astype(f32)
    for src in range(1, N_CTX):
        total = total + got_ref[src, :SEQ].astype(f32)
    grad_kv = total.astype(bf16)
    kv_ref[...] = grad_kv.reshape(N_CTX, BLOCK, HEAD_DIM)

    def rows_of(at, order):
        return jnp.concatenate([got_ref[src, at : at + BLOCK] for src in order], axis=0)

    in_order = list(range(N_CTX))
    y_order = [(i % 2) * 4 + i // 2 for i in range(N_CTX)]
    lane = lax.broadcasted_iota(jnp.int32, (SEQ, HEAD_DIM), 1)
    zero = jnp.zeros((SEQ, HEAD_DIM), bf16)
    mixed_q = jnp.where(lane < 64, rows_of(AT_MIXED, in_order), zero)
    mixed_o = jnp.where(lane < 64, zero, rows_of(AT_MIXED, y_order))
    left = jnp.concatenate([rows_of(AT_QUERY, in_order).T, mixed_q.T, grad_kv.T], axis=0)
    right = jnp.concatenate([mixed_o.T, rows_of(AT_OUT, y_order).T], axis=0)
    by_hidden = dg(left, hidden_ref[...].reshape(SEQ, WIDTH), NN)
    by_att = dg(right, att_ref[...].reshape(SEQ, WIDTH), NN)
    tiles = [
        by_hidden[:BLOCK],
        by_hidden[BLOCK : 2 * BLOCK] + by_att[:BLOCK],
        by_att[BLOCK:],
        by_hidden[2 * BLOCK :],
    ]
    for t, tile in enumerate(tiles):
        sent_ref[:, :96, HEAD_DIM * t : HEAD_DIM * (t + 1)] = (
            tile.T.astype(bf16).reshape(N_EXP, 96, HEAD_DIM)
        )

    def summed(start, stop):
        out = got_ref[0, start:stop].astype(f32)
        for src in range(1, N_CTX):
            out = out + got_ref[src, start:stop].astype(f32)
        return out

    down_ref[...] = summed(AT_DOWN, AT_GAIN).astype(bf16)
    shared = summed(AT_SHARED, AT_DOWN)
    gains = summed(AT_GAIN, SENT_ROWS)
    row = lax.broadcasted_iota(jnp.int32, (16, HEAD_DIM), 0)
    one_lane = lax.broadcasted_iota(jnp.int32, (1, HEAD_DIM), 1)
    for i in range(N_EXP):
        m, offset = (96 * i) // HEAD_DIM, (96 * i) % HEAD_DIM
        gain = gains[m : m + 1]
        if offset:
            shift = HEAD_DIM - offset
            gain = jnp.where(
                one_lane < shift,
                pltpu.roll(gain, shift, 1),
                pltpu.roll(gains[m + 1 : m + 2], shift, 1),
            )
        rows = jnp.where(row == 12, jnp.broadcast_to(gain, (16, HEAD_DIM)), shared[16 * i : 16 * i + 16])
        sent_ref[i, 96:, :HEAD_DIM] = rows.astype(bf16)
        sent_ref[i, 96:, HEAD_DIM:] = jnp.zeros((16, 512 - HEAD_DIM), bf16)


def column_grads(got, hidden_seq, att_seq):
    return pl.pallas_call(
        columns_kernel,
        out_shape=[
            jax.ShapeDtypeStruct((N_EXP, 112, 512), bf16),
            jax.ShapeDtypeStruct((N_CTX, BLOCK, HEAD_DIM), bf16),
            jax.ShapeDtypeStruct((96, HEAD_DIM), bf16),
        ],
        cost_estimate=cost(8),
        compiler_params=params(56),
        name="column_grads",
    )(got, hidden_seq, att_seq)


OWNED_ROWS = 4 * 96 + 16 * N_EXP + 96


def owned_kernel(got_ref, down_ref, owned_ref, gain_ref):
    total = got_ref[0, :96].astype(f32)
    gains = got_ref[0, 96:, :HEAD_DIM].astype(f32)
    for src in range(1, N_EXP):
        total = total + got_ref[src, :96].astype(f32)
        gains = gains + got_ref[src, 96:, :HEAD_DIM].astype(f32)
    gain_ref[...] = gains
    for t in range(4):
        owned_ref[96 * t : 96 * t + 96] = total[:, HEAD_DIM * t : HEAD_DIM * (t + 1)].astype(bf16)
    for src in range(N_EXP):
        at = 384 + 16 * src
        owned_ref[at : at + 16] = got_ref[src, 96:, :HEAD_DIM]
    owned_ref[384 + 16 * N_EXP :] = down_ref[...]


def owned_sums(got, down):
    return pl.pallas_call(
        owned_kernel,
        out_shape=[
            jax.ShapeDtypeStruct((OWNED_ROWS, HEAD_DIM), bf16),
            jax.ShapeDtypeStruct((16, HEAD_DIM), f32),
        ],
        cost_estimate=cost(3),
        compiler_params=params(32),
        name="owned_sums",
    )(got, down)


def finish_kernel(
    got_ref,
    gain_in_ref,
    wq_ref,
    wk_ref,
    wv_ref,
    gain_ref,
    q_ref,
    k_ref,
    v_ref,
    out_ref,
    sg_ref,
    su_ref,
    sd_ref,
):
    lane = lax.broadcasted_iota(jnp.int32, (96, HEAD_DIM), 1)

    def tile(c, t):
        return got_ref[c, 96 * t : 96 * t + 96].astype(f32)

    for c in range(N_CTX):
        at = HEAD_DIM * c
        q_ref[:, at : at + HEAD_DIM] = tile(c, 0)
        out_ref[:, at : at + HEAD_DIM] = tile(c, 2)
    for m in range(N_CTX // 2):
        at = HEAD_DIM * m
        low, high = halves(tile(2 * m, 1), tile(2 * m + 1, 1), lane)
        q_ref[:, 1024 + at : 1024 + at + HEAD_DIM] = low
        out_ref[:, 1024 + at : 1024 + at + HEAD_DIM] = high
        low, high = halves(tile(2 * m, 3), tile(2 * m + 1, 3), lane)
        k_ref[:, at : at + HEAD_DIM] = low
        v_ref[:, at : at + HEAD_DIM] = high
    gain = (
        jnp.sum(q_ref[...] * wq_ref[...].astype(f32), axis=1, keepdims=True)
        + jnp.sum(k_ref[...] * wk_ref[...].astype(f32), axis=1, keepdims=True)
        + jnp.sum(v_ref[...] * wv_ref[...].astype(f32), axis=1, keepdims=True)
    ) / gain_in_ref[...]
    gain_ref[...] = jnp.broadcast_to(gain, (96, HEAD_DIM))
    row = lax.broadcasted_iota(jnp.int32, (96, HEAD_DIM), 0)
    picks = jnp.where((lane % 16 < 12) & (row == 12 * (lane // 16) + lane % 16), 1.0, 0.0)
    picks = picks.astype(bf16)

    def shared_tile(j):
        at = 384 + 16 * j
        rows = jnp.concatenate([got_ref[c, at : at + 16] for c in range(N_CTX)], axis=0)
        return dg(picks, rows, NN)

    for m in range(N_EXP // 2):
        at = HEAD_DIM * m
        low, high = halves(shared_tile(2 * m), shared_tile(2 * m + 1), lane)
        sg_ref[:, at : at + HEAD_DIM] = low
        su_ref[:, at : at + HEAD_DIM] = high
    for c in range(N_CTX):
        rows = got_ref[c, 384 + 16 * N_EXP :].astype(f32)
        for m in range(HEADS):
            sd_ref[8 * c : 8 * c + 8, HEAD_DIM * m : HEAD_DIM * (m + 1)] = rows[8 * m : 8 * m + 8]


def finish(got, gain_column, query_weight, key_weight, value_weight):
    shapes = [(96, 128), (96, 1536), (96, 512), (96, 512), (96, 1536), (96, 1024), (96, 1024)]
    return pl.pallas_call(
        finish_kernel,
        out_shape=[jax.ShapeDtypeStruct(s, f32) for s in shapes + [(SHARED, WIDTH)]],
        cost_estimate=cost(4),
        compiler_params=params(32),
        name="finish",
    )(got, gain_column, query_weight, key_weight, value_weight)


def input_kernel(dq_ref, got_ref, wq_ref, wkv_ref, x_ref, gain_ref, gm_ref, out_ref):
    lane = lax.broadcasted_iota(jnp.int32, (BLOCK, HEAD_DIM), 1)
    lows, highs = [], []
    for m in range(KV_HEADS):
        low, high = halves(got_ref[2 * m].astype(f32), got_ref[2 * m + 1].astype(f32), lane)
        lows.append(low.astype(bf16))
        highs.append(high.astype(bf16))
    grad_kv = jnp.concatenate(lows + highs, axis=1)
    grad_one = dg(dq_ref[...], wq_ref[...], NT) + dg(grad_kv, wkv_ref[...], NT)
    inputs = x_ref[...].astype(f32)
    inv = lax.rsqrt(jnp.mean(inputs * inputs, axis=-1, keepdims=True) + epsilon)
    out_ref[...] = (gm_ref[...] + norm_back(grad_one * gain_ref[...], inputs * inv, inv)).astype(bf16)


def input_back(grad_query, grad_kv, w_all, tokens, gain, grad_middle):
    return pl.pallas_call(
        input_kernel,
        grid=(1,),
        in_specs=[
            whole((BLOCK, WIDTH)),
            whole((N_CTX, BLOCK, HEAD_DIM)),
            w_cols(WIDTH, 0),
            w_cols(2 * KV_WIDTH, 3),
            whole((BLOCK, WIDTH)),
            whole((1, WIDTH)),
            whole((BLOCK, WIDTH)),
        ],
        out_specs=whole((BLOCK, WIDTH)),
        out_shape=jax.ShapeDtypeStruct((BLOCK, WIDTH), bf16),
        cost_estimate=cost(7),
        compiler_params=params(48),
        name="input_back",
    )(grad_query, grad_kv, w_all, w_all, tokens, gain, grad_middle)


def norm_rows_kernel(x_ref, gain_ref, out_ref):
    inputs = x_ref[0].astype(f32)
    inv = lax.rsqrt(jnp.mean(inputs * inputs, axis=-1, keepdims=True) + epsilon)
    out_ref[0] = (inputs * inv * gain_ref[...]).astype(bf16)


def norm_rows(rows, gain):
    count = rows.shape[0]
    spec = pl.BlockSpec((1, BLOCK, WIDTH), lambda i: (i, 0, 0))
    turned = pl.BlockSpec((1, BLOCK, WIDTH), lambda i: ((i % 2) * 4 + i // 2, 0, 0))
    return pl.pallas_call(
        norm_rows_kernel,
        grid=(count,),
        in_specs=[spec, whole((1, WIDTH))],
        out_specs=spec if count == 1 else turned,
        out_shape=jax.ShapeDtypeStruct(rows.shape, bf16),
        cost_estimate=cost(2),
        compiler_params=params(32),
        name="norm_rows",
    )(rows, gain)


def project_kernel(own_ref, seq_ref, w_ref, q_ref, kv_ref):
    step = pl.program_id(0)

    @pl.when(step < 3)
    def _():
        q_ref[...] = dg(own_ref[0], w_ref[...], NN).astype(bf16)

    @pl.when(step >= 3)
    def _():
        rows = seq_ref[...].reshape(N_CTX * BLOCK, WIDTH)
        kv_ref[...] = dg(rows, w_ref[...], NN).astype(bf16).reshape(N_CTX, BLOCK, KV_WIDTH)


def project(own, seq, w_all):
    return pl.pallas_call(
        project_kernel,
        grid=(5,),
        in_specs=[
            whole((1, BLOCK, WIDTH)),
            whole((N_CTX, BLOCK, WIDTH)),
            pl.BlockSpec((WIDTH, KV_WIDTH), lambda i: (0, jnp.where(i < 3, i, i + 3))),
        ],
        out_specs=[
            pl.BlockSpec((BLOCK, KV_WIDTH), lambda i: (0, jnp.minimum(i, 2))),
            pl.BlockSpec((N_CTX, BLOCK, KV_WIDTH), lambda i: (0, 0, jnp.maximum(i - 3, 0))),
        ],
        out_shape=[
            jax.ShapeDtypeStruct((BLOCK, WIDTH), bf16),
            jax.ShapeDtypeStruct((N_CTX, BLOCK, 2 * KV_WIDTH), bf16),
        ],
        cost_estimate=cost(8),
        compiler_params=params(48),
        name="project",
    )(own, seq, w_all)


PIECE = 2 * WIDTH + WIDTH * BLOCK // HEAD_DIM


def spread_kernel(at_ref, own_ref, got_ref, *outs):
    total = (own_ref[0].astype(f32) + got_ref[0].astype(f32)).astype(bf16)
    for k in range(HALF):

        @pl.when(pl.program_id(0) == k)
        def _():
            outs[k][...] = total


def spread_sums(exp_at, own, got):
    spec = pl.BlockSpec((1, BLOCK, WIDTH), lambda k, at: ((at[0] >> 1) ^ k, 0, 0))
    return pl.pallas_call(
        spread_kernel,
        grid_spec=pltpu.PrefetchScalarGridSpec(
            num_scalar_prefetch=1,
            grid=(HALF,),
            in_specs=[spec, spec],
            out_specs=[whole((BLOCK, WIDTH))] * HALF,
        ),
        out_shape=[jax.ShapeDtypeStruct((BLOCK, WIDTH), bf16)] * HALF,
        cost_estimate=cost(4),
        compiler_params=params(32),
        name="spread_sums",
    )(exp_at, own, got)


def of_step(values, step):
    out = jnp.int32(values[0])
    for i, value in enumerate(values[1:], 1):
        out = jnp.where(step == i, value, out)
    return out


def expert_weights_kernel(halved, at_ref, x_ref, geo_ref, act_ref, dgate_ref, dup_ref, *outs):
    step = pl.program_id(0)
    rhs = jnp.concatenate([dgate_ref[0], dup_ref[0]], axis=1)
    both = dg(x_ref[0], rhs, TN).astype(bf16)
    down = dg(act_ref[0], geo_ref[0], TN).astype(bf16)
    for i in range(4):

        @pl.when(step == i)
        def _():
            start = (i % 2) * PIECE if halved else 0
            out = outs[i // 2 if halved else i].at[pl.ds(start, PIECE)]
            out[:WIDTH] = both[:, :HEAD_DIM]
            out[WIDTH : 2 * WIDTH] = both[:, HEAD_DIM:]
            for m in range(WIDTH // HEAD_DIM):
                at = 2 * WIDTH + m * BLOCK
                out[at : at + BLOCK] = down[:, m * HEAD_DIM : (m + 1) * HEAD_DIM]


def expert_weights(ctx_at, steps, halved, arrived, grad_eo, act, grad_gu):
    rows = 2 * ROWS

    def expert(s, at):
        return (at[0] >> 2) ^ of_step([side for _, side in steps], s)

    def lanes(shift):
        return pl.BlockSpec(
            (1, rows, HEAD_DIM),
            lambda s, at: (
                expert(s, at),
                0,
                shift + ((at[0] & 3) ^ of_step([r for r, _ in steps], s)),
            ),
        )

    rows_of = pl.BlockSpec((1, rows, WIDTH), lambda s, at: (expert(s, at), 0, 0))
    count, length = (2, 2 * PIECE) if halved else (4, PIECE)
    return pl.pallas_call(
        lambda *refs: expert_weights_kernel(halved, *refs),
        grid_spec=pltpu.PrefetchScalarGridSpec(
            num_scalar_prefetch=1,
            grid=(4,),
            in_specs=[rows_of, rows_of, lanes(0), lanes(0), lanes(4)],
            out_specs=[whole((length, HEAD_DIM))] * count,
        ),
        out_shape=[jax.ShapeDtypeStruct((length, HEAD_DIM), bf16)] * count,
        cost_estimate=cost(2),
        compiler_params=params(56),
        name="expert_weights",
    )(ctx_at, arrived, grad_eo, act, grad_gu, grad_gu)


def unpack_kernel(count, at_ref, *refs):
    pieces, (gate_ref, up_ref, down_ref) = refs[:count], refs[-3:]
    step = pl.program_id(0)
    for i in range(count):

        @pl.when(step == i)
        def _():
            piece = pieces[i]
            gate_ref[0] = piece[:WIDTH].astype(f32)
            up_ref[0] = piece[WIDTH : 2 * WIDTH].astype(f32)
            for m in range(WIDTH // HEAD_DIM):
                at = 2 * WIDTH + m * BLOCK
                down_ref[0, :, m * HEAD_DIM : (m + 1) * HEAD_DIM] = piece[at : at + BLOCK].astype(
                    f32
                )


def unpack_experts(ctx_at, steps, pieces, filled=()):
    count = len(steps)

    def expert(s, at):
        return (at[0] >> 2) ^ of_step([side for _, side in steps], s)

    def units(s, at):
        return (at[0] & 3) ^ of_step([r for r, _ in steps], s)

    cols = pl.BlockSpec((1, WIDTH, HEAD_DIM), lambda s, at: (expert(s, at), 0, units(s, at)))
    rows = pl.BlockSpec((1, BLOCK, WIDTH), lambda s, at: (expert(s, at), units(s, at), 0))
    anywhere = pl.BlockSpec(memory_space=pl.ANY)
    return pl.pallas_call(
        lambda *refs: unpack_kernel(count, *refs),
        grid_spec=pltpu.PrefetchScalarGridSpec(
            num_scalar_prefetch=1,
            grid=(count,),
            in_specs=[whole((PIECE, HEAD_DIM))] * count + [anywhere] * len(filled),
            out_specs=[cols, cols, rows],
        ),
        out_shape=[
            jax.ShapeDtypeStruct((LOCAL_E, WIDTH, FF_E), f32),
            jax.ShapeDtypeStruct((LOCAL_E, WIDTH, FF_E), f32),
            jax.ShapeDtypeStruct((LOCAL_E, FF_E, WIDTH), f32),
        ],
        input_output_aliases={1 + count + i: i for i in range(len(filled))},
        cost_estimate=cost(2 * count),
        compiler_params=params(48),
        name="unpack_experts",
    )(ctx_at, *pieces, *filled)


def relay_kernel(
    p0, p1, p3, p6, relay_a, relay_b, got_10, got_31, add_a, add_b, part_0, part_1
):
    add_a[...] = (p6[...].astype(f32) + relay_a[...].astype(f32)).astype(bf16)
    add_b[...] = (p3[...].astype(f32) + relay_b[...].astype(f32)).astype(bf16)
    part_0[...] = p0[...].astype(f32) + got_10[...].astype(f32)
    part_1[...] = p1[...].astype(f32) + got_31[...].astype(f32)


def side_kernel(part_0, part_1, got_11, got_30, own, side):
    own[...] = part_0[...] + got_30[...].astype(f32)
    side[...] = (part_1[...] + got_11[...].astype(f32)).astype(bf16)


def piece_sums(kernel, kinds, *pieces):
    specs, arrays = [], []
    for piece in pieces:
        array, second = piece if isinstance(piece, tuple) else (piece, 0)
        specs.append(pl.BlockSpec((PIECE // 4, HEAD_DIM), lambda i, at=4 * second: (i + at, 0)))
        arrays.append(array)
    return pl.pallas_call(
        kernel,
        grid=(4,),
        in_specs=specs,
        out_specs=[pl.BlockSpec((PIECE // 4, HEAD_DIM), lambda i: (i, 0))] * len(kinds),
        out_shape=[jax.ShapeDtypeStruct((PIECE, HEAD_DIM), kind) for kind in kinds],
        cost_estimate=cost(1),
        compiler_params=params(32),
        name="piece_sums",
    )(*arrays)


same_core = [[2 * i + c for i in range(8)] for c in range(2)]
core_swap = [(i, i ^ 1) for i in range(N_EXP)]
y_groups = [[0, 1, 2, 3], [4, 5, 6, 7]]
z_swap = [(i, i ^ 4) for i in range(N_CTX)]


def swap_all(rows, axis, groups=None):
    return lax.all_to_all(
        rows, axis, split_axis=0, concat_axis=0, tiled=True, axis_index_groups=groups
    )


def after(value, *others):
    return lax.optimization_barrier((value,) + others)[0]


def add_low(a, b):
    return (a.astype(f32) + b.astype(f32)).astype(bf16)


def on_device(
    tokens,
    routes,
    route_gates,
    norm_attn,
    norm_ffn,
    query_weight,
    key_weight,
    value_weight,
    out_weight,
    shared_gate,
    shared_up,
    shared_down,
    expert_gate,
    expert_up,
    expert_down,
    cotangent,
):
    exp_at = lax.axis_index("exp").astype(jnp.int32)
    ctx_at = lax.axis_index("ctx").astype(jnp.int32)
    exp_s, ctx_s = exp_at.reshape(1), ctx_at.reshape(1)

    z_at = ctx_at // 4

    w_cat = jnp.concatenate([query_weight, out_weight, key_weight, value_weight], axis=1)
    w_all = lax.all_gather(w_cat, "exp", axis=0, tiled=True)
    gates_high = route_gates[0].astype(bf16)
    gates_low = (route_gates[0] - gates_high.astype(f32)).astype(bf16)
    pad = jnp.zeros((BLOCK, META - 3 * TOPK), bf16)
    up_meta = jnp.concatenate(
        [cotangent[0], routes[0].astype(bf16), gates_high, gates_low, pad], axis=1
    )
    up_all = lax.all_gather(after(up_meta, w_cat), "exp", axis=0, tiled=True)
    gains = after(jnp.concatenate([norm_attn, norm_ffn]), w_cat)
    gains = swap_all(jnp.broadcast_to(gains, (N_EXP, gains.shape[0])), "exp")
    gain_attn = gains[:, :96].reshape(1, WIDTH).astype(f32)
    gain_ffn = gains[:, 96:].reshape(1, WIDTH).astype(f32)

    def of_sequence(rows):
        other = lax.ppermute(rows, "ctx", z_swap)
        pair = jnp.where(
            z_at == 0,
            jnp.concatenate([rows, other], axis=0),
            jnp.concatenate([other, rows], axis=0),
        )
        got = swap_all(jnp.broadcast_to(pair, (4, 2, BLOCK, WIDTH)), "ctx", y_groups)
        return got.reshape(N_CTX, BLOCK, WIDTH)

    tokens_seq = of_sequence(after(tokens, w_cat))
    shared_cols = jnp.concatenate(
        [shared_gate.reshape(96, N_EXP, SHARED), shared_up.reshape(96, N_EXP, SHARED)], axis=2
    ).transpose(1, 0, 2)
    w_shared = swap_all(shared_cols, "exp").reshape(WIDTH, 2 * SHARED)
    shared_two = jnp.concatenate([shared_down, shared_down], axis=0)

    hidden_one = norm_rows(tokens, gain_attn)
    hidden_seq = norm_rows(tokens_seq, gain_attn)
    hidden_seq = after(hidden_seq, w_shared)
    queries, kv_all = project(hidden_one, hidden_seq, w_all)
    attended, att_f, logs = attend(ctx_s, queries, kv_all)
    middle, hidden_two = middle_norm(attended, w_all, tokens[0], gain_ffn)

    hidden_all = lax.all_gather(hidden_two, "exp", axis=0, tiled=True)
    hidden_all = hidden_all.reshape(HALF, 2, BLOCK, WIDTH)
    att_seq = of_sequence(attended[None])
    place, grad_eo, grad_eh, grad_sh, slot_gate = place_rows(
        exp_s,
        after(up_all, hidden_two).reshape(HALF, 2, BLOCK, WIDTH + META),
        expert_down,
        shared_two,
    )
    other, part, arrived, act, grad_gu, shared_act, shared_grad = expert_back(
        exp_s, after(hidden_all, att_seq), place, grad_eh, grad_sh, expert_gate, expert_up, w_shared
    )
    summed = add_low(part, lax.ppermute(other, "exp", core_swap))
    grad_two = swap_all(summed, "exp", same_core)

    rows_e = 2 * ROWS
    operands = (
        after(arrived, summed).reshape(LOCAL_E, rows_e, WIDTH),
        grad_eo.reshape(LOCAL_E, rows_e, WIDTH),
        act.reshape(LOCAL_E, rows_e, FF_E),
        grad_gu.reshape(LOCAL_E, rows_e, 2 * FF_E),
    )
    for_1, for_3 = expert_weights(ctx_s, ((2, 0), (1, 0), (2, 1), (3, 1)), True, *operands)
    operands = (after(operands[0], for_1),) + operands[1:]
    p0, p6, p1, p3 = expert_weights(ctx_s, ((0, 0), (3, 0), (0, 1), (1, 1)), False, *operands)

    def to(rows, k):
        return lax.ppermute(rows, "ctx", [(i, i ^ k) for i in range(N_CTX)])

    from_1, from_3 = to(for_1, 1), to(for_3, 3)
    shared_grad_late = after(shared_grad, p0).reshape(N_EXP * BLOCK, META)
    grad_scols = dg(hidden_all.reshape(N_EXP * BLOCK, WIDTH), shared_grad_late, TN).astype(bf16)
    act_late = after(shared_act, p0).reshape(N_EXP * BLOCK, META)
    grad_sdown = dg(act_late, up_all, TN)[:SHARED, :WIDTH].astype(bf16)
    extra = jnp.concatenate(
        [
            jnp.pad(
                grad_scols.reshape(N_EXP, N_CTX, 12, META).transpose(1, 0, 2, 3),
                ((0, 0), (0, 0), (0, 4), (0, 0)),
            ).reshape(N_CTX, 16 * N_EXP, META),
            grad_sdown.reshape(N_CTX, 8, HEADS, 128).transpose(0, 2, 1, 3).reshape(N_CTX, 96, 128),
        ],
        axis=1,
    )

    grad_two = after(grad_two, p0, extra)
    grad_middle, grad_attn, grad_heads, gain_rows = middle_back(
        grad_two, middle, cotangent[0], gain_ffn, w_all
    )
    grad_query, sent = attend_back(
        ctx_s, queries, grad_heads, att_f, logs, kv_all, grad_attn, extra, gain_rows
    )
    from_1, from_3 = after((from_1, from_3), sent)
    add_a, add_b, part_0, part_1 = piece_sums(
        relay_kernel,
        (bf16, bf16, f32, f32),
        p0,
        p1,
        p3,
        p6,
        (from_1, 0),
        (from_3, 0),
        (from_1, 1),
        (from_3, 1),
    )
    own_part, side = piece_sums(
        side_kernel, (f32, bf16), part_0, part_1, to(add_b, 1), to(add_a, 3)
    )
    across = to(side, 4)

    got = swap_all(after(sent, side), "ctx")
    out_part, out_other = expert_output(
        exp_s, after(act, side), slot_gate, place, shared_act, expert_down, shared_two
    )
    out_sums = spread_sums(exp_s, out_part, lax.ppermute(out_other, "exp", core_swap))
    own = (own_part + after(across, out_part).astype(f32)).astype(bf16)
    at_1, at_3, at_z = to(own, 1), to(own, 3), to(own, 4)
    columns, grad_kv, grad_down = column_grads(got, after(hidden_seq, own, out_sums[0]), att_seq)
    columns, at_1, at_3 = lax.optimization_barrier((columns, at_1, at_3))
    owned = swap_all(columns, "exp")
    owned, gain_sum = owned_sums(owned, grad_down)
    owned, at_z1, at_z3 = lax.optimization_barrier((owned, to(at_z, 1), to(at_z, 3)))
    at_2, at_z2 = to(at_3, 1), to(at_z1, 3)
    out_rows = middle + out_sums[0].astype(f32)
    for k in range(1, HALF):
        moved = lax.ppermute(
            after(out_sums[k], owned), "exp", [(i, i ^ (2 * k)) for i in range(N_EXP)]
        )
        out_rows = out_rows + moved.astype(f32)
    mixed = out_rows.astype(bf16)[None]
    experts = unpack_experts(
        ctx_s, ((0, 0), (1, 0), (3, 0), (0, 1)), (after(own, owned), at_1, at_3, at_z)
    )
    owned = swap_all(jnp.broadcast_to(owned, (N_CTX, OWNED_ROWS, HEAD_DIM)), "ctx")
    grad_kv = swap_all(after(grad_kv, owned), "ctx")
    experts = unpack_experts(
        ctx_s, ((2, 0), (1, 1), (3, 1), (2, 1)), (at_2, at_z1, at_z3, at_z2), experts
    )
    gain_attn_sum, *dense = finish(
        after(owned, experts[0]),
        norm_attn.astype(f32).reshape(96, 1),
        query_weight,
        key_weight,
        value_weight,
    )
    input_grad = input_back(
        after(grad_query, dense[0]), grad_kv, w_all, tokens[0], gain_attn, grad_middle
    )
    return (
        mixed,
        input_grad[None],
        gain_attn_sum[:, 0],
        gain_sum[12, :96],
        *dense,
        *experts,
    )


def solution(mesh):
    token_spec = P("exp", "ctx", None)
    rows = P("exp", None)
    expert = P("exp", None, None)
    placed = (token_spec,) * 3 + (P("exp"),) * 2 + (rows,) * 7 + (expert,) * 3 + (token_spec,)
    return jax.shard_map(
        on_device,
        mesh=mesh,
        in_specs=placed,
        out_specs=(token_spec,) * 2 + (P("exp"),) * 2 + (rows,) * 7 + (expert,) * 3,
        check_vma=False,
    )
```

```python
import jax
import jax.numpy as jnp
from jax import lax
from jax.sharding import PartitionSpec as P
from jax.experimental import pallas as pl
from jax.experimental.pallas import tpu as pltpu

HEADS = 12
KV_HEADS = 4
HEAD_DIM = 128
TOPK = 6
GROUP = 3
BLOCK = 128
WIDTH = 1536
KV_WIDTH = KV_HEADS * HEAD_DIM
CAP = 48
N_EXP = 16
N_CTX = 8
LOCAL_E = 2
FF_E = 512
SHARED = 64
META = 128
HALF = 8
ROWS = HALF * CAP

epsilon = 1e-05
masked_score = -1e30
f32 = jnp.float32
bf16 = jnp.bfloat16
log2_e = 1.4426950408889634
score_scale = HEAD_DIM ** (-0.5) * log2_e

NN = (((1,), (0,)), ((), ()))
NT = (((1,), (1,)), ((), ()))
TN = (((0,), (0,)), ((), ()))


def dg(a, b, dims):
    return lax.dot_general(a, b, dims, preferred_element_type=f32)


def params(mib):
    return pltpu.CompilerParams(vmem_limit_bytes=mib * 1024 * 1024)


def cost(us):
    return pl.CostEstimate(flops=0, bytes_accessed=int(us * 3690000), transcendentals=0)


def whole(shape):
    return pl.BlockSpec(shape, lambda *_: (0,) * len(shape), pipeline_mode=pl.Buffered(1))


def sigmoid(v):
    return 1.0 / (1.0 + jnp.exp(-v))


def allowed_scores(ctx_at):
    rows = lax.broadcasted_iota(jnp.int32, (GROUP * BLOCK, N_CTX * BLOCK), 0) % BLOCK
    cols = lax.broadcasted_iota(jnp.int32, (GROUP * BLOCK, N_CTX * BLOCK), 1)
    return rows + ctx_at * BLOCK >= cols


def stack_heads(block):
    return jnp.concatenate([block[:, j * HEAD_DIM : (j + 1) * HEAD_DIM] for j in range(GROUP)], axis=0)


def unstack_heads(rows):
    return jnp.concatenate([rows[j * BLOCK : (j + 1) * BLOCK] for j in range(GROUP)], axis=1)


def attend_kernel(ctx_ref, q_ref, k_ref, v_ref, att_ref, attf_ref, log_ref):
    q = stack_heads(q_ref[...])
    keys = k_ref[...].reshape(N_CTX * BLOCK, HEAD_DIM)
    values = v_ref[...].reshape(N_CTX * BLOCK, HEAD_DIM)
    scores = jnp.where(allowed_scores(ctx_ref[0]), dg(q, keys, NT) * score_scale, masked_score)
    top = jnp.max(scores, axis=-1, keepdims=True)
    weights = jnp.exp2(scores - top)
    total = jnp.sum(weights, axis=-1, keepdims=True)
    out = dg(weights.astype(bf16), values, NN) * (1.0 / total)
    out = unstack_heads(out)
    attf_ref[...] = out
    att_ref[...] = out.astype(bf16)
    log_ref[...] = jnp.broadcast_to(top + jnp.log2(total), (GROUP * BLOCK, HEAD_DIM))


def kv_specs():
    return [
        pl.BlockSpec((N_CTX, BLOCK, HEAD_DIM), lambda g: (0, 0, g)),
        pl.BlockSpec((N_CTX, BLOCK, HEAD_DIM), lambda g: (0, 0, KV_HEADS + g)),
    ]


def head_spec():
    return pl.BlockSpec((BLOCK, GROUP * HEAD_DIM), lambda g: (0, g))


def attend(ctx_at, qkv, kv_all):
    return pl.pallas_call(
        attend_kernel,
        grid=(KV_HEADS,),
        in_specs=[pl.BlockSpec(memory_space=pltpu.SMEM), head_spec()] + kv_specs(),
        out_specs=[
            head_spec(),
            head_spec(),
            pl.BlockSpec((GROUP * BLOCK, HEAD_DIM), lambda g: (g, 0)),
        ],
        out_shape=[
            jax.ShapeDtypeStruct((BLOCK, WIDTH), bf16),
            jax.ShapeDtypeStruct((BLOCK, WIDTH), f32),
            jax.ShapeDtypeStruct((HEADS * BLOCK, HEAD_DIM), f32),
        ],
        cost_estimate=cost(6),
        compiler_params=params(48),
        name="attend",
    )(ctx_at, qkv, kv_all, kv_all)


SEQ = N_CTX * BLOCK
AT_QUERY, AT_MIXED, AT_OUT = SEQ, SEQ + BLOCK, SEQ + 2 * BLOCK
AT_SHARED = SEQ + 3 * BLOCK
AT_DOWN = AT_SHARED + 16 * N_EXP
AT_GAIN = AT_DOWN + 96
SENT_ROWS = AT_GAIN + 16


def halves(a, b, lane):
    low = jnp.where(lane < 64, a, pltpu.roll(b, 64, 1))
    high = jnp.where(lane < 64, pltpu.roll(a, 64, 1), b)
    return low, high


def attend_back_kernel(
    ctx_ref,
    q_ref,
    ga_ref,
    attf_ref,
    log_ref,
    k_ref,
    v_ref,
    all_ga_ref,
    extra_ref,
    gain_ref,
    dq_ref,
    near_ref,
    far_ref,
    kept_ref,
):
    group = pl.program_id(0)
    z_at = ctx_ref[0] // 4

    def send(dest, z, start, stop, rows):
        @pl.when(z_at == z)
        def _():
            near_ref[dest, start:stop] = rows

        @pl.when(z_at != z)
        def _():
            far_ref[dest, start:stop] = rows

    q = stack_heads(q_ref[...])
    grad = stack_heads(ga_ref[...])
    delta = jnp.sum(grad.astype(f32) * stack_heads(attf_ref[...]), axis=-1, keepdims=True)
    keys = k_ref[...].reshape(SEQ, HEAD_DIM)
    values = v_ref[...].reshape(SEQ, HEAD_DIM)
    scores = jnp.where(allowed_scores(ctx_ref[0]), dg(q, keys, NT) * score_scale, masked_score)
    weights = jnp.exp2(scores - log_ref[:, :1])
    grad_weights = dg(grad, values, NT)
    grad_raw = (weights * (grad_weights - delta)).astype(bf16)
    scale = HEAD_DIM ** (-0.5)
    dq = unstack_heads(dg(grad_raw, keys, NN) * scale)
    dq_ref[...] = dq.astype(bf16)
    kept_ref[group] = dq
    grad_k = dg(grad_raw, q, TN) * scale
    grad_v = dg(weights.astype(bf16), grad, TN)
    low, high = halves(grad_k, grad_v, lax.broadcasted_iota(jnp.int32, (SEQ, HEAD_DIM), 1))
    low, high = low.astype(bf16), high.astype(bf16)
    send(2 * (group % 2), group // 2, 0, SEQ, low)
    send(2 * (group % 2) + 1, group // 2, 0, SEQ, high)

    @pl.when(group == KV_HEADS - 1)
    def _():
        lane = lax.broadcasted_iota(jnp.int32, (BLOCK, HEAD_DIM), 1)

        def dq_tile(m):
            return kept_ref[m // GROUP, :, HEAD_DIM * (m % GROUP) : HEAD_DIM * (m % GROUP + 1)]

        def ga_tile(m):
            return all_ga_ref[:, HEAD_DIM * m : HEAD_DIM * (m + 1)].astype(f32)

        mixed = []
        for m in range(KV_HEADS):
            mixed += halves(dq_tile(N_CTX + m), ga_tile(N_CTX + m), lane)
        gains = gain_ref[...].astype(bf16)
        for c in range(N_CTX):
            tiles = [dq_tile(c).astype(bf16), mixed[c].astype(bf16), ga_tile(c).astype(bf16)]
            rows = jnp.concatenate(tiles + [extra_ref[c], gains], axis=0)
            send(c % 4, c // 4, AT_QUERY, SENT_ROWS, rows)


def attend_back(ctx_at, qkv, grad_att, att_f, logs, kv_all, grad_attn, extra, gain_rows):
    return pl.pallas_call(
        attend_back_kernel,
        grid=(KV_HEADS,),
        in_specs=[
            pl.BlockSpec(memory_space=pltpu.SMEM),
            head_spec(),
            head_spec(),
            head_spec(),
            pl.BlockSpec((GROUP * BLOCK, HEAD_DIM), lambda g: (g, 0)),
        ]
        + kv_specs()
        + [
            whole((BLOCK, WIDTH)),
            whole((N_CTX, AT_GAIN - AT_SHARED, HEAD_DIM)),
            whole((16, HEAD_DIM)),
        ],
        out_specs=[head_spec()] + [whole((4, SENT_ROWS, HEAD_DIM))] * 2,
        out_shape=[
            jax.ShapeDtypeStruct((BLOCK, WIDTH), bf16),
            jax.ShapeDtypeStruct((4, SENT_ROWS, HEAD_DIM), bf16),
            jax.ShapeDtypeStruct((4, SENT_ROWS, HEAD_DIM), bf16),
        ],
        scratch_shapes=[pltpu.VMEM((KV_HEADS, BLOCK, GROUP * HEAD_DIM), f32)],
        cost_estimate=cost(2),
        compiler_params=params(48),
        name="attend_back",
    )(ctx_at, qkv, grad_att, att_f, logs, kv_all, kv_all, grad_attn, extra, gain_rows)


def middle_kernel(att_ref, w_ref, x_ref, gain_ref, middle_ref, hidden_ref):
    middle = x_ref[...].astype(f32) + dg(att_ref[...], w_ref[...], NN)
    inv = lax.rsqrt(jnp.mean(middle * middle, axis=-1, keepdims=True) + epsilon)
    middle_ref[...] = middle
    hidden_ref[...] = (middle * inv * gain_ref[...]).astype(bf16)


def w_cols(width, at):
    return pl.BlockSpec((WIDTH, width), lambda *_: (0, at), pipeline_mode=pl.Buffered(1))


def middle_norm(attended, w_all, tokens, gain):
    return pl.pallas_call(
        middle_kernel,
        grid=(1,),
        in_specs=[
            whole((BLOCK, WIDTH)),
            w_cols(WIDTH, 1),
            whole((BLOCK, WIDTH)),
            whole((1, WIDTH)),
        ],
        out_specs=[whole((BLOCK, WIDTH)), whole((BLOCK, WIDTH))],
        out_shape=[
            jax.ShapeDtypeStruct((BLOCK, WIDTH), f32),
            jax.ShapeDtypeStruct((BLOCK, WIDTH), bf16),
        ],
        cost_estimate=cost(2),
        compiler_params=params(32),
        name="middle_norm",
    )(attended, w_all, tokens, gain)


def norm_back(grad_normed, normed, inv_root):
    return inv_root * (
        grad_normed - normed * jnp.mean(grad_normed * normed, axis=-1, keepdims=True)
    )


def middle_back_kernel(
    pieces_ref, middle_ref, up_ref, gain_ref, w_ref, gm_ref, ga_ref, gh_ref, gg_ref
):
    grad_two = pieces_ref[0].astype(f32)
    for i in range(1, HALF):
        grad_two = grad_two + pieces_ref[i].astype(f32)
    middle = middle_ref[...]
    inv = lax.rsqrt(jnp.mean(middle * middle, axis=-1, keepdims=True) + epsilon)
    normed = middle * inv
    gains = jnp.sum(grad_two * normed, axis=0, keepdims=True)
    gg_ref[...] = jnp.zeros((16, HEAD_DIM), f32)
    for m in range(HEADS):
        gg_ref[m : m + 1] = gains[:, HEAD_DIM * m : HEAD_DIM * (m + 1)]
    grad_middle = up_ref[...].astype(f32) + norm_back(grad_two * gain_ref[...], normed, inv)
    gm_ref[...] = grad_middle
    grad_attn = grad_middle.astype(bf16)
    ga_ref[...] = grad_attn
    gh_ref[...] = dg(grad_attn, w_ref[...], NT).astype(bf16)


def middle_back(pieces, middle, upstream, gain, w_all):
    return pl.pallas_call(
        middle_back_kernel,
        grid=(1,),
        in_specs=[
            whole((HALF, BLOCK, WIDTH)),
            whole((BLOCK, WIDTH)),
            whole((BLOCK, WIDTH)),
            whole((1, WIDTH)),
            w_cols(WIDTH, 1),
        ],
        out_specs=[whole((BLOCK, WIDTH))] * 3 + [whole((16, HEAD_DIM))],
        out_shape=[
            jax.ShapeDtypeStruct((BLOCK, WIDTH), f32),
            jax.ShapeDtypeStruct((BLOCK, WIDTH), bf16),
            jax.ShapeDtypeStruct((BLOCK, WIDTH), bf16),
            jax.ShapeDtypeStruct((16, HEAD_DIM), f32),
        ],
        cost_estimate=cost(1),
        compiler_params=params(48),
        name="middle_back",
    )(pieces, middle, upstream, gain, w_all)


def place_kernel(
    at_ref, up_ref, down_ref, sdown_ref, place_ref, geo_ref, geh_ref, gsh_ref, gate_ref
):
    lane = lax.broadcasted_iota(jnp.int32, (BLOCK, META), 1)
    row = lax.broadcasted_iota(jnp.int32, (BLOCK, META), 0)
    before = (row > lane).astype(bf16)
    slot = (lane % 64).astype(f32)
    first_id = (at_ref[0] * LOCAL_E).astype(f32)
    row_id = first_id + (row >= 64).astype(f32)

    for chip in range(HALF):
        meta = up_ref[chip, 0, :, WIDTH:].astype(f32)
        named = lane < TOPK
        zero = jnp.zeros((BLOCK, META), f32)
        hit0 = jnp.where(named & (meta == first_id), 1.0, zero)
        hit1 = jnp.where(named & (meta == first_id + 1.0), 1.0, zero)
        mask = jnp.where(
            lane < 64,
            jnp.sum(hit0, axis=1, keepdims=True),
            jnp.sum(hit1, axis=1, keepdims=True),
        )
        rank = dg(before, mask.astype(bf16), NN)
        place = jnp.where((mask > 0.5) & (rank == slot), 1.0, zero).astype(bf16)
        place_ref[chip, 0] = place
        rows = dg(place, up_ref[chip, 0], TN)
        slot_meta = rows[:, WIDTH:]
        gates = pltpu.roll(slot_meta, META - TOPK, 1) + pltpu.roll(
            slot_meta, META - 2 * TOPK, 1
        )
        gate = jnp.sum(
            jnp.where(named & (slot_meta == row_id), gates, zero), axis=1, keepdims=True
        )
        geo = (gate * rows[:, :WIDTH]).astype(bf16)
        wide_gate = jnp.broadcast_to(gate, (BLOCK, META))
        at = chip * CAP
        for e in range(LOCAL_E):
            geo_ref[e, 0, at : at + CAP] = geo[64 * e : 64 * e + CAP]
            gate_ref[e, 0, at : at + CAP] = wide_gate[64 * e : 64 * e + CAP]
        gsh_ref[chip, 0] = dg(up_ref[chip, 0, :, :WIDTH], sdown_ref[...], NT)
    for e in range(LOCAL_E):
        geh_ref[e, 0] = dg(geo_ref[e, 0], down_ref[e], NT)


def by_core(cols):
    return pl.BlockSpec(
        (HALF, 1, BLOCK, cols),
        lambda s, at: (0, jnp.where(s == 0, 1 - at[0] % 2, at[0] % 2), 0, 0),
    )


def by_step(cols):
    return pl.BlockSpec((LOCAL_E, 1, ROWS, cols), lambda s, at: (0, s, 0, 0))


def place_rows(exp_at, up_all, expert_down, shared_two):
    return pl.pallas_call(
        place_kernel,
        grid_spec=pltpu.PrefetchScalarGridSpec(
            num_scalar_prefetch=1,
            grid=(2,),
            in_specs=[
                by_core(WIDTH + META),
                whole((LOCAL_E, FF_E, WIDTH)),
                whole((2 * SHARED, WIDTH)),
            ],
            out_specs=[by_core(META), by_step(WIDTH), by_step(FF_E), by_core(META), by_step(META)],
        ),
        out_shape=[
            jax.ShapeDtypeStruct((HALF, 2, BLOCK, META), bf16),
            jax.ShapeDtypeStruct((LOCAL_E, 2, ROWS, WIDTH), bf16),
            jax.ShapeDtypeStruct((LOCAL_E, 2, ROWS, FF_E), f32),
            jax.ShapeDtypeStruct((HALF, 2, BLOCK, META), f32),
            jax.ShapeDtypeStruct((LOCAL_E, 2, ROWS, META), f32),
        ],
        cost_estimate=cost(14),
        compiler_params=params(56),
        name="place_rows",
    )(exp_at, up_all, expert_down, shared_two)


def expert_kernel(
    at_ref,
    hid_ref,
    place_ref,
    geh_ref,
    gsh_ref,
    wg_ref,
    wu_ref,
    ws_ref,
    part_ref,
    x_ref,
    act_ref,
    dgu_ref,
    sact_ref,
    sgrad_ref,
):
    for chip in range(HALF):
        rows = dg(place_ref[chip, 0], hid_ref[chip, 0], TN).astype(bf16)
        at = chip * CAP
        for e in range(LOCAL_E):
            x_ref[e, 0, at : at + CAP] = rows[64 * e : 64 * e + CAP]
    pairs = []
    for e in range(LOCAL_E):
        pre_gate = dg(x_ref[e, 0], wg_ref[e], NN)
        pre_up = dg(x_ref[e, 0], wu_ref[e], NN)
        sig = sigmoid(pre_gate)
        act = pre_gate * sig
        act_ref[e, 0] = (act * pre_up).astype(bf16)
        geh = geh_ref[e, 0]
        d_gate = (geh * pre_up * (sig * (1.0 + pre_gate * (1.0 - sig)))).astype(bf16)
        d_up = (geh * act).astype(bf16)
        dgu_ref[e, 0, :, :FF_E] = d_gate
        dgu_ref[e, 0, :, FF_E:] = d_up
        pairs.append((dg(d_gate, wg_ref[e], NT) + dg(d_up, wu_ref[e], NT)).astype(bf16))
    lane = lax.broadcasted_iota(jnp.int32, (BLOCK, 2 * SHARED), 1) < SHARED
    gap = jnp.zeros((64 - CAP, WIDTH), bf16)
    for chip in range(HALF):
        pre = dg(hid_ref[chip, 0], ws_ref[...], NN)
        turned = pltpu.roll(pre, SHARED, 1)
        gate, up = jnp.where(lane, pre, turned), jnp.where(lane, turned, pre)
        sig = sigmoid(gate)
        act = gate * sig
        sact_ref[chip, 0] = jnp.where(lane, act * up, 0.0).astype(bf16)
        slope = sig * (1.0 + gate * (1.0 - sig))
        sgrad = (gsh_ref[chip, 0] * jnp.where(lane, up * slope, act)).astype(bf16)
        sgrad_ref[chip, 0] = sgrad
        at = chip * CAP
        stacked = jnp.concatenate([pairs[0][at : at + CAP], gap, pairs[1][at : at + CAP], gap], 0)
        part_ref[0, chip] = (
            dg(place_ref[chip, 0], stacked, NN) + dg(sgrad, ws_ref[...], NT)
        ).astype(bf16)


def expert_back(exp_at, hidden, place, geh, gsh, wg, wu, ws):
    return pl.pallas_call(
        expert_kernel,
        grid_spec=pltpu.PrefetchScalarGridSpec(
            num_scalar_prefetch=1,
            grid=(2,),
            in_specs=[
                by_core(WIDTH),
                by_core(META),
                by_step(FF_E),
                by_core(META),
                whole((LOCAL_E, WIDTH, FF_E)),
                whole((LOCAL_E, WIDTH, FF_E)),
                whole((WIDTH, 2 * SHARED)),
            ],
            out_specs=[
                pl.BlockSpec((1, HALF, BLOCK, WIDTH), lambda s, at: (s, 0, 0, 0)),
                by_step(WIDTH),
                by_step(FF_E),
                by_step(2 * FF_E),
                by_core(META),
                by_core(META),
            ],
        ),
        out_shape=[
            jax.ShapeDtypeStruct((2, HALF, BLOCK, WIDTH), bf16),
            jax.ShapeDtypeStruct((LOCAL_E, 2, ROWS, WIDTH), bf16),
            jax.ShapeDtypeStruct((LOCAL_E, 2, ROWS, FF_E), bf16),
            jax.ShapeDtypeStruct((LOCAL_E, 2, ROWS, 2 * FF_E), bf16),
            jax.ShapeDtypeStruct((HALF, 2, BLOCK, META), bf16),
            jax.ShapeDtypeStruct((HALF, 2, BLOCK, META), bf16),
        ],
        cost_estimate=cost(28),
        compiler_params=params(60),
        name="expert_back",
    )(exp_at, hidden, place, geh, gsh, wg, wu, ws)


def output_kernel(at_ref, act_ref, gate_ref, place_ref, sact_ref, wd_ref, sd_ref, part_ref):
    outs = []
    for e in range(LOCAL_E):
        out = dg(act_ref[e, 0], wd_ref[e], NN).astype(bf16).astype(f32)
        outs.append((out * gate_ref[e, 0, :, :1]).astype(bf16))
    gap = jnp.zeros((64 - CAP, WIDTH), bf16)
    for chip in range(HALF):
        at = chip * CAP
        stacked = jnp.concatenate([outs[0][at : at + CAP], gap, outs[1][at : at + CAP], gap], 0)
        part_ref[0, chip] = (
            dg(place_ref[chip, 0], stacked, NN) + dg(sact_ref[chip, 0], sd_ref[...], NN)
        ).astype(bf16)


def expert_output(exp_at, act, gate, place, sact, wd, sd):
    return pl.pallas_call(
        output_kernel,
        grid_spec=pltpu.PrefetchScalarGridSpec(
            num_scalar_prefetch=1,
            grid=(2,),
            in_specs=[
                by_step(FF_E),
                by_step(META),
                by_core(META),
                by_core(META),
                whole((LOCAL_E, FF_E, WIDTH)),
                whole((2 * SHARED, WIDTH)),
            ],
            out_specs=pl.BlockSpec((1, HALF, BLOCK, WIDTH), lambda s, at: (s, 0, 0, 0)),
        ),
        out_shape=jax.ShapeDtypeStruct((2, HALF, BLOCK, WIDTH), bf16),
        cost_estimate=cost(2),
        compiler_params=params(48),
        name="expert_output",
    )(exp_at, act, gate, place, sact, wd, sd)


SHARE = 3 * BLOCK
TO_SHARED = SEQ + 2 * SHARE
TO_DOWN = TO_SHARED + 16 * N_EXP
TO_GAIN = TO_DOWN + 96
MERGED_ROWS = TO_GAIN + 16


def merge_kernel(ctx_ref, near_ref, got_ref, out_ref):
    z_at = ctx_ref[0] // 4
    near, got = near_ref[0], got_ref[0]

    def add(a, b):
        return (a.astype(f32) + b.astype(f32)).astype(bf16)

    out_ref[0, :SEQ] = add(near[:SEQ], got[:SEQ])
    out_ref[0, TO_SHARED:] = add(near[AT_SHARED:], got[AT_SHARED:])
    mine, theirs = near[AT_QUERY:AT_SHARED], got[AT_QUERY:AT_SHARED]
    out_ref[0, SEQ : SEQ + SHARE] = jnp.where(z_at == 0, mine, theirs)
    out_ref[0, SEQ + SHARE : TO_SHARED] = jnp.where(z_at == 0, theirs, mine)


def merge_shares(ctx_at, near, got):
    spec = pl.BlockSpec((1, SENT_ROWS, HEAD_DIM), lambda i: (i, 0, 0))
    return pl.pallas_call(
        merge_kernel,
        grid=(4,),
        in_specs=[pl.BlockSpec(memory_space=pltpu.SMEM), spec, spec],
        out_specs=pl.BlockSpec((1, MERGED_ROWS, HEAD_DIM), lambda i: (i, 0, 0)),
        out_shape=jax.ShapeDtypeStruct((4, MERGED_ROWS, HEAD_DIM), bf16),
        cost_estimate=cost(3),
        compiler_params=params(32),
        name="merge_shares",
    )(ctx_at, near, got)


def columns_kernel(got_ref, hidden_ref, att_ref, sent_ref, kv_ref, down_ref):
    def summed(start, stop):
        out = got_ref[0, start:stop].astype(f32)
        for src in range(1, 4):
            out = out + got_ref[src, start:stop].astype(f32)
        return out

    grad_kv = summed(0, SEQ).astype(bf16)
    kv_ref[...] = grad_kv.reshape(N_CTX, BLOCK, HEAD_DIM)

    def rows_of(tile, order):
        at = SEQ + BLOCK * tile
        return jnp.concatenate(
            [got_ref[y, at + SHARE * z : at + SHARE * z + BLOCK] for z, y in order], axis=0
        )

    in_order = [(i // 4, i % 4) for i in range(N_CTX)]
    y_order = [(i % 2, i // 2) for i in range(N_CTX)]
    lane = lax.broadcasted_iota(jnp.int32, (SEQ, HEAD_DIM), 1)
    zero = jnp.zeros((SEQ, HEAD_DIM), bf16)
    mixed_q = jnp.where(lane < 64, rows_of(1, in_order), zero)
    mixed_o = jnp.where(lane < 64, zero, rows_of(1, y_order))
    left = jnp.concatenate([rows_of(0, in_order).T, mixed_q.T, grad_kv.T], axis=0)
    right = jnp.concatenate([mixed_o.T, rows_of(2, y_order).T], axis=0)
    by_hidden = dg(left, hidden_ref[...].reshape(SEQ, WIDTH), NN)
    by_att = dg(right, att_ref[...].reshape(SEQ, WIDTH), NN)
    tiles = [
        by_hidden[:BLOCK],
        by_hidden[BLOCK : 2 * BLOCK] + by_att[:BLOCK],
        by_att[BLOCK:],
        by_hidden[2 * BLOCK :],
    ]
    for t, tile in enumerate(tiles):
        sent_ref[:, :96, HEAD_DIM * t : HEAD_DIM * (t + 1)] = (
            tile.T.astype(bf16).reshape(N_EXP, 96, HEAD_DIM)
        )

    down_ref[...] = summed(TO_DOWN, TO_GAIN).astype(bf16)
    shared = summed(TO_SHARED, TO_DOWN)
    gains = summed(TO_GAIN, MERGED_ROWS)
    row = lax.broadcasted_iota(jnp.int32, (16, HEAD_DIM), 0)
    one_lane = lax.broadcasted_iota(jnp.int32, (1, HEAD_DIM), 1)
    for i in range(N_EXP):
        m, offset = (96 * i) // HEAD_DIM, (96 * i) % HEAD_DIM
        gain = gains[m : m + 1]
        if offset:
            shift = HEAD_DIM - offset
            gain = jnp.where(
                one_lane < shift,
                pltpu.roll(gain, shift, 1),
                pltpu.roll(gains[m + 1 : m + 2], shift, 1),
            )
        rows = jnp.where(row == 12, jnp.broadcast_to(gain, (16, HEAD_DIM)), shared[16 * i : 16 * i + 16])
        sent_ref[i, 96:, :HEAD_DIM] = rows.astype(bf16)
        sent_ref[i, 96:, HEAD_DIM:] = jnp.zeros((16, 512 - HEAD_DIM), bf16)


def column_grads(got, hidden_seq, att_seq):
    return pl.pallas_call(
        columns_kernel,
        out_shape=[
            jax.ShapeDtypeStruct((N_EXP, 112, 512), bf16),
            jax.ShapeDtypeStruct((N_CTX, BLOCK, HEAD_DIM), bf16),
            jax.ShapeDtypeStruct((96, HEAD_DIM), bf16),
        ],
        cost_estimate=cost(8),
        compiler_params=params(56),
        name="column_grads",
    )(got, hidden_seq, att_seq)


OWNED_ROWS = 4 * 96 + 16 * N_EXP + 96


def owned_kernel(got_ref, down_ref, owned_ref, gain_ref):
    total = got_ref[0, :96].astype(f32)
    gains = got_ref[0, 96:, :HEAD_DIM].astype(f32)
    for src in range(1, N_EXP):
        total = total + got_ref[src, :96].astype(f32)
        gains = gains + got_ref[src, 96:, :HEAD_DIM].astype(f32)
    gain_ref[...] = gains
    for t in range(4):
        owned_ref[96 * t : 96 * t + 96] = total[:, HEAD_DIM * t : HEAD_DIM * (t + 1)].astype(bf16)
    for src in range(N_EXP):
        at = 384 + 16 * src
        owned_ref[at : at + 16] = got_ref[src, 96:, :HEAD_DIM]
    owned_ref[384 + 16 * N_EXP :] = down_ref[...]


def owned_sums(got, down):
    return pl.pallas_call(
        owned_kernel,
        out_shape=[
            jax.ShapeDtypeStruct((OWNED_ROWS, HEAD_DIM), bf16),
            jax.ShapeDtypeStruct((16, HEAD_DIM), f32),
        ],
        cost_estimate=cost(3),
        compiler_params=params(32),
        name="owned_sums",
    )(got, down)


def finish_kernel(
    got_ref,
    gain_in_ref,
    wq_ref,
    wk_ref,
    wv_ref,
    gain_ref,
    q_ref,
    k_ref,
    v_ref,
    out_ref,
    sg_ref,
    su_ref,
    sd_ref,
):
    lane = lax.broadcasted_iota(jnp.int32, (96, HEAD_DIM), 1)

    def tile(c, t):
        return got_ref[c, 96 * t : 96 * t + 96].astype(f32)

    for c in range(N_CTX):
        at = HEAD_DIM * c
        q_ref[:, at : at + HEAD_DIM] = tile(c, 0)
        out_ref[:, at : at + HEAD_DIM] = tile(c, 2)
    for m in range(N_CTX // 2):
        at = HEAD_DIM * m
        low, high = halves(tile(2 * m, 1), tile(2 * m + 1, 1), lane)
        q_ref[:, 1024 + at : 1024 + at + HEAD_DIM] = low
        out_ref[:, 1024 + at : 1024 + at + HEAD_DIM] = high
        low, high = halves(tile(2 * m, 3), tile(2 * m + 1, 3), lane)
        k_ref[:, at : at + HEAD_DIM] = low
        v_ref[:, at : at + HEAD_DIM] = high
    gain = (
        jnp.sum(q_ref[...] * wq_ref[...].astype(f32), axis=1, keepdims=True)
        + jnp.sum(k_ref[...] * wk_ref[...].astype(f32), axis=1, keepdims=True)
        + jnp.sum(v_ref[...] * wv_ref[...].astype(f32), axis=1, keepdims=True)
    ) / gain_in_ref[...]
    gain_ref[...] = jnp.broadcast_to(gain, (96, HEAD_DIM))
    row = lax.broadcasted_iota(jnp.int32, (96, HEAD_DIM), 0)
    picks = jnp.where((lane % 16 < 12) & (row == 12 * (lane // 16) + lane % 16), 1.0, 0.0)
    picks = picks.astype(bf16)

    def shared_tile(j):
        at = 384 + 16 * j
        rows = jnp.concatenate([got_ref[c, at : at + 16] for c in range(N_CTX)], axis=0)
        return dg(picks, rows, NN)

    for m in range(N_EXP // 2):
        at = HEAD_DIM * m
        low, high = halves(shared_tile(2 * m), shared_tile(2 * m + 1), lane)
        sg_ref[:, at : at + HEAD_DIM] = low
        su_ref[:, at : at + HEAD_DIM] = high
    for c in range(N_CTX):
        rows = got_ref[c, 384 + 16 * N_EXP :].astype(f32)
        for m in range(HEADS):
            sd_ref[8 * c : 8 * c + 8, HEAD_DIM * m : HEAD_DIM * (m + 1)] = rows[8 * m : 8 * m + 8]


def finish(got, gain_column, query_weight, key_weight, value_weight):
    shapes = [(96, 128), (96, 1536), (96, 512), (96, 512), (96, 1536), (96, 1024), (96, 1024)]
    return pl.pallas_call(
        finish_kernel,
        out_shape=[jax.ShapeDtypeStruct(s, f32) for s in shapes + [(SHARED, WIDTH)]],
        cost_estimate=cost(4),
        compiler_params=params(32),
        name="finish",
    )(got, gain_column, query_weight, key_weight, value_weight)


def input_kernel(dq_ref, got_ref, wq_ref, wkv_ref, x_ref, gain_ref, gm_ref, out_ref):
    lane = lax.broadcasted_iota(jnp.int32, (BLOCK, HEAD_DIM), 1)
    lows, highs = [], []
    for m in range(KV_HEADS):
        low, high = halves(got_ref[2 * m].astype(f32), got_ref[2 * m + 1].astype(f32), lane)
        lows.append(low.astype(bf16))
        highs.append(high.astype(bf16))
    grad_kv = jnp.concatenate(lows + highs, axis=1)
    grad_one = dg(dq_ref[...], wq_ref[...], NT) + dg(grad_kv, wkv_ref[...], NT)
    inputs = x_ref[...].astype(f32)
    inv = lax.rsqrt(jnp.mean(inputs * inputs, axis=-1, keepdims=True) + epsilon)
    out_ref[...] = (gm_ref[...] + norm_back(grad_one * gain_ref[...], inputs * inv, inv)).astype(bf16)


def input_back(grad_query, grad_kv, w_all, tokens, gain, grad_middle):
    return pl.pallas_call(
        input_kernel,
        grid=(1,),
        in_specs=[
            whole((BLOCK, WIDTH)),
            whole((N_CTX, BLOCK, HEAD_DIM)),
            w_cols(WIDTH, 0),
            w_cols(2 * KV_WIDTH, 3),
            whole((BLOCK, WIDTH)),
            whole((1, WIDTH)),
            whole((BLOCK, WIDTH)),
        ],
        out_specs=whole((BLOCK, WIDTH)),
        out_shape=jax.ShapeDtypeStruct((BLOCK, WIDTH), bf16),
        cost_estimate=cost(7),
        compiler_params=params(48),
        name="input_back",
    )(grad_query, grad_kv, w_all, w_all, tokens, gain, grad_middle)


def norm_rows_kernel(x_ref, gain_ref, out_ref):
    inputs = x_ref[0].astype(f32)
    inv = lax.rsqrt(jnp.mean(inputs * inputs, axis=-1, keepdims=True) + epsilon)
    out_ref[0] = (inputs * inv * gain_ref[...]).astype(bf16)


def norm_rows(rows, gain):
    count = rows.shape[0]
    spec = pl.BlockSpec((1, BLOCK, WIDTH), lambda i: (i, 0, 0))
    turned = pl.BlockSpec((1, BLOCK, WIDTH), lambda i: ((i % 2) * 4 + i // 2, 0, 0))
    return pl.pallas_call(
        norm_rows_kernel,
        grid=(count,),
        in_specs=[spec, whole((1, WIDTH))],
        out_specs=spec if count == 1 else turned,
        out_shape=jax.ShapeDtypeStruct(rows.shape, bf16),
        cost_estimate=cost(2),
        compiler_params=params(32),
        name="norm_rows",
    )(rows, gain)


def project_kernel(own_ref, seq_ref, w_ref, q_ref, kv_ref):
    step = pl.program_id(0)

    @pl.when(step < 3)
    def _():
        q_ref[...] = dg(own_ref[0], w_ref[...], NN).astype(bf16)

    @pl.when(step >= 3)
    def _():
        rows = seq_ref[...].reshape(N_CTX * BLOCK, WIDTH)
        kv_ref[...] = dg(rows, w_ref[...], NN).astype(bf16).reshape(N_CTX, BLOCK, KV_WIDTH)


def project(own, seq, w_all):
    return pl.pallas_call(
        project_kernel,
        grid=(5,),
        in_specs=[
            whole((1, BLOCK, WIDTH)),
            whole((N_CTX, BLOCK, WIDTH)),
            pl.BlockSpec((WIDTH, KV_WIDTH), lambda i: (0, jnp.where(i < 3, i, i + 3))),
        ],
        out_specs=[
            pl.BlockSpec((BLOCK, KV_WIDTH), lambda i: (0, jnp.minimum(i, 2))),
            pl.BlockSpec((N_CTX, BLOCK, KV_WIDTH), lambda i: (0, 0, jnp.maximum(i - 3, 0))),
        ],
        out_shape=[
            jax.ShapeDtypeStruct((BLOCK, WIDTH), bf16),
            jax.ShapeDtypeStruct((N_CTX, BLOCK, 2 * KV_WIDTH), bf16),
        ],
        cost_estimate=cost(8),
        compiler_params=params(48),
        name="project",
    )(own, seq, w_all)


PIECE = 2 * WIDTH + WIDTH * BLOCK // HEAD_DIM


def spread_kernel(at_ref, own_ref, got_ref, *outs):
    total = (own_ref[0, 0].astype(f32) + got_ref[0].astype(f32)).astype(bf16)
    for k in range(HALF):

        @pl.when(pl.program_id(0) == k)
        def _():
            outs[k // 2][k % 2] = total


def spread_sums(exp_at, parts, got):
    return pl.pallas_call(
        spread_kernel,
        grid_spec=pltpu.PrefetchScalarGridSpec(
            num_scalar_prefetch=1,
            grid=(HALF,),
            in_specs=[
                pl.BlockSpec((1, 1, BLOCK, WIDTH), lambda k, at: (1, (at[0] >> 1) ^ k, 0, 0)),
                pl.BlockSpec((1, BLOCK, WIDTH), lambda k, at: ((at[0] >> 1) ^ k, 0, 0)),
            ],
            out_specs=[whole((2, BLOCK, WIDTH))] * 4,
        ),
        out_shape=[jax.ShapeDtypeStruct((2, BLOCK, WIDTH), bf16)] * 4,
        cost_estimate=cost(4),
        compiler_params=params(32),
        name="spread_sums",
    )(exp_at, parts, got)


def of_step(values, step):
    out = jnp.int32(values[0])
    for i, value in enumerate(values[1:], 1):
        out = jnp.where(step == i, value, out)
    return out


def expert_weights_kernel(halved, at_ref, x_ref, geo_ref, act_ref, dgate_ref, dup_ref, *outs):
    step = pl.program_id(0)
    rhs = jnp.concatenate([dgate_ref[0], dup_ref[0]], axis=1)
    both = dg(x_ref[0], rhs, TN).astype(bf16)
    down = dg(act_ref[0], geo_ref[0], TN).astype(bf16)
    for i in range(4):

        @pl.when(step == i)
        def _():
            start = (i % 2) * PIECE if halved else 0
            out = outs[i // 2 if halved else i].at[pl.ds(start, PIECE)]
            out[:WIDTH] = both[:, :HEAD_DIM]
            out[WIDTH : 2 * WIDTH] = both[:, HEAD_DIM:]
            for m in range(WIDTH // HEAD_DIM):
                at = 2 * WIDTH + m * BLOCK
                out[at : at + BLOCK] = down[:, m * HEAD_DIM : (m + 1) * HEAD_DIM]


def expert_weights(ctx_at, steps, halved, arrived, grad_eo, act, grad_gu):
    rows = 2 * ROWS

    def expert(s, at):
        return (at[0] >> 2) ^ of_step([side for _, side in steps], s)

    def lanes(shift):
        return pl.BlockSpec(
            (1, rows, HEAD_DIM),
            lambda s, at: (
                expert(s, at),
                0,
                shift + ((at[0] & 3) ^ of_step([r for r, _ in steps], s)),
            ),
        )

    rows_of = pl.BlockSpec((1, rows, WIDTH), lambda s, at: (expert(s, at), 0, 0))
    count, length = (2, 2 * PIECE) if halved else (4, PIECE)
    return pl.pallas_call(
        lambda *refs: expert_weights_kernel(halved, *refs),
        grid_spec=pltpu.PrefetchScalarGridSpec(
            num_scalar_prefetch=1,
            grid=(4,),
            in_specs=[rows_of, rows_of, lanes(0), lanes(0), lanes(4)],
            out_specs=[whole((length, HEAD_DIM))] * count,
        ),
        out_shape=[jax.ShapeDtypeStruct((length, HEAD_DIM), bf16)] * count,
        cost_estimate=cost(2),
        compiler_params=params(56),
        name="expert_weights",
    )(ctx_at, arrived, grad_eo, act, grad_gu, grad_gu)


def unpack_kernel(count, at_ref, *refs):
    pieces, (gate_ref, up_ref, down_ref) = refs[:count], refs[-3:]
    step = pl.program_id(0)
    for i in range(count):

        @pl.when(step == i)
        def _():
            piece = pieces[i]
            gate_ref[0] = piece[:WIDTH].astype(f32)
            up_ref[0] = piece[WIDTH : 2 * WIDTH].astype(f32)
            for m in range(WIDTH // HEAD_DIM):
                at = 2 * WIDTH + m * BLOCK
                down_ref[0, :, m * HEAD_DIM : (m + 1) * HEAD_DIM] = piece[at : at + BLOCK].astype(
                    f32
                )


def unpack_experts(ctx_at, steps, pieces, filled=()):
    count = len(steps)

    def expert(s, at):
        return (at[0] >> 2) ^ of_step([side for _, side in steps], s)

    def units(s, at):
        return (at[0] & 3) ^ of_step([r for r, _ in steps], s)

    cols = pl.BlockSpec((1, WIDTH, HEAD_DIM), lambda s, at: (expert(s, at), 0, units(s, at)))
    rows = pl.BlockSpec((1, BLOCK, WIDTH), lambda s, at: (expert(s, at), units(s, at), 0))
    anywhere = pl.BlockSpec(memory_space=pl.ANY)
    return pl.pallas_call(
        lambda *refs: unpack_kernel(count, *refs),
        grid_spec=pltpu.PrefetchScalarGridSpec(
            num_scalar_prefetch=1,
            grid=(count,),
            in_specs=[whole((PIECE, HEAD_DIM))] * count + [anywhere] * len(filled),
            out_specs=[cols, cols, rows],
        ),
        out_shape=[
            jax.ShapeDtypeStruct((LOCAL_E, WIDTH, FF_E), f32),
            jax.ShapeDtypeStruct((LOCAL_E, WIDTH, FF_E), f32),
            jax.ShapeDtypeStruct((LOCAL_E, FF_E, WIDTH), f32),
        ],
        input_output_aliases={1 + count + i: i for i in range(len(filled))},
        cost_estimate=cost(2 * count),
        compiler_params=params(48),
        name="unpack_experts",
    )(ctx_at, *pieces, *filled)


def relay_kernel(
    p0, p1, p3, p6, relay_a, relay_b, got_10, got_31, add_a, add_b, part_0, part_1
):
    add_a[...] = (p6[...].astype(f32) + relay_a[...].astype(f32)).astype(bf16)
    add_b[...] = (p3[...].astype(f32) + relay_b[...].astype(f32)).astype(bf16)
    part_0[...] = p0[...].astype(f32) + got_10[...].astype(f32)
    part_1[...] = p1[...].astype(f32) + got_31[...].astype(f32)


def side_kernel(part_0, part_1, got_11, got_30, own, side):
    own[...] = part_0[...] + got_30[...].astype(f32)
    side[...] = (part_1[...] + got_11[...].astype(f32)).astype(bf16)


def piece_sums(kernel, kinds, *pieces):
    specs, arrays = [], []
    for piece in pieces:
        array, second = piece if isinstance(piece, tuple) else (piece, 0)
        specs.append(pl.BlockSpec((PIECE // 4, HEAD_DIM), lambda i, at=4 * second: (i + at, 0)))
        arrays.append(array)
    return pl.pallas_call(
        kernel,
        grid=(4,),
        in_specs=specs,
        out_specs=[pl.BlockSpec((PIECE // 4, HEAD_DIM), lambda i: (i, 0))] * len(kinds),
        out_shape=[jax.ShapeDtypeStruct((PIECE, HEAD_DIM), kind) for kind in kinds],
        cost_estimate=cost(1),
        compiler_params=params(32),
        name="piece_sums",
    )(*arrays)


same_core = [[2 * i + c for i in range(8)] for c in range(2)]
core_swap = [(i, i ^ 1) for i in range(N_EXP)]
y_groups = [[0, 1, 2, 3], [4, 5, 6, 7]]
z_swap = [(i, i ^ 4) for i in range(N_CTX)]


def swap_all(rows, axis, groups=None):
    return lax.all_to_all(
        rows, axis, split_axis=0, concat_axis=0, tiled=True, axis_index_groups=groups
    )


def after(value, *others):
    return lax.optimization_barrier((value,) + others)[0]


def add_low(a, b):
    return (a.astype(f32) + b.astype(f32)).astype(bf16)


def on_device(
    tokens,
    routes,
    route_gates,
    norm_attn,
    norm_ffn,
    query_weight,
    key_weight,
    value_weight,
    out_weight,
    shared_gate,
    shared_up,
    shared_down,
    expert_gate,
    expert_up,
    expert_down,
    cotangent,
):
    exp_at = lax.axis_index("exp").astype(jnp.int32)
    ctx_at = lax.axis_index("ctx").astype(jnp.int32)
    exp_s, ctx_s = exp_at.reshape(1), ctx_at.reshape(1)

    z_at = ctx_at // 4

    w_cat = jnp.concatenate([query_weight, out_weight, key_weight, value_weight], axis=1)
    w_all = lax.all_gather(w_cat, "exp", axis=0, tiled=True)
    gates_high = route_gates[0].astype(bf16)
    gates_low = (route_gates[0] - gates_high.astype(f32)).astype(bf16)
    pad = jnp.zeros((BLOCK, META - 3 * TOPK), bf16)
    up_meta = jnp.concatenate(
        [cotangent[0], routes[0].astype(bf16), gates_high, gates_low, pad], axis=1
    )
    up_all = lax.all_gather(after(up_meta, w_cat), "exp", axis=0, tiled=True)
    gains = after(jnp.concatenate([norm_attn, norm_ffn]), w_cat)
    gains = swap_all(jnp.broadcast_to(gains, (N_EXP, gains.shape[0])), "exp")
    gain_attn = gains[:, :96].reshape(1, WIDTH).astype(f32)
    gain_ffn = gains[:, 96:].reshape(1, WIDTH).astype(f32)

    def of_sequence(rows):
        other = lax.ppermute(rows, "ctx", z_swap)
        pair = jnp.where(
            z_at == 0,
            jnp.concatenate([rows, other], axis=0),
            jnp.concatenate([other, rows], axis=0),
        )
        got = swap_all(jnp.broadcast_to(pair, (4, 2, BLOCK, WIDTH)), "ctx", y_groups)
        return got.reshape(N_CTX, BLOCK, WIDTH)

    tokens_seq = of_sequence(after(tokens, w_cat))
    shared_cols = jnp.concatenate(
        [shared_gate.reshape(96, N_EXP, SHARED), shared_up.reshape(96, N_EXP, SHARED)], axis=2
    ).transpose(1, 0, 2)
    w_shared = swap_all(shared_cols, "exp").reshape(WIDTH, 2 * SHARED)
    shared_two = jnp.concatenate([shared_down, shared_down], axis=0)

    hidden_one = norm_rows(tokens, gain_attn)
    hidden_seq = norm_rows(tokens_seq, gain_attn)
    hidden_seq = after(hidden_seq, w_shared)
    queries, kv_all = project(hidden_one, hidden_seq, w_all)
    attended, att_f, logs = attend(ctx_s, queries, kv_all)
    middle, hidden_two = middle_norm(attended, w_all, tokens[0], gain_ffn)

    hidden_all = lax.all_gather(hidden_two, "exp", axis=0, tiled=True)
    hidden_all = hidden_all.reshape(HALF, 2, BLOCK, WIDTH)
    att_seq = of_sequence(attended[None])
    place, grad_eo, grad_eh, grad_sh, slot_gate = place_rows(
        exp_s,
        after(up_all, hidden_two).reshape(HALF, 2, BLOCK, WIDTH + META),
        expert_down,
        shared_two,
    )
    part, arrived, act, grad_gu, shared_act, shared_grad = expert_back(
        exp_s, after(hidden_all, att_seq), place, grad_eh, grad_sh, expert_gate, expert_up, w_shared
    )
    summed = add_low(part[1], lax.ppermute(part[0], "exp", core_swap))
    grad_two = swap_all(summed, "exp", same_core)

    rows_e = 2 * ROWS
    operands = (
        after(arrived, summed).reshape(LOCAL_E, rows_e, WIDTH),
        grad_eo.reshape(LOCAL_E, rows_e, WIDTH),
        act.reshape(LOCAL_E, rows_e, FF_E),
        grad_gu.reshape(LOCAL_E, rows_e, 2 * FF_E),
    )
    for_1, for_3 = expert_weights(ctx_s, ((2, 0), (1, 0), (2, 1), (3, 1)), True, *operands)
    operands = (after(operands[0], for_1),) + operands[1:]
    p0, p6, p1, p3 = expert_weights(ctx_s, ((0, 0), (3, 0), (0, 1), (1, 1)), False, *operands)

    def to(rows, k):
        return lax.ppermute(rows, "ctx", [(i, i ^ k) for i in range(N_CTX)])

    from_1, from_3 = to(for_1, 1), to(for_3, 3)
    shared_grad_late = after(shared_grad, p0).reshape(N_EXP * BLOCK, META)
    grad_scols = dg(hidden_all.reshape(N_EXP * BLOCK, WIDTH), shared_grad_late, TN).astype(bf16)
    act_late = after(shared_act, p0).reshape(N_EXP * BLOCK, META)
    grad_sdown = dg(act_late, up_all, TN)[:SHARED, :WIDTH].astype(bf16)
    extra = jnp.concatenate(
        [
            jnp.pad(
                grad_scols.reshape(N_EXP, N_CTX, 12, META).transpose(1, 0, 2, 3),
                ((0, 0), (0, 0), (0, 4), (0, 0)),
            ).reshape(N_CTX, 16 * N_EXP, META),
            grad_sdown.reshape(N_CTX, 8, HEADS, 128).transpose(0, 2, 1, 3).reshape(N_CTX, 96, 128),
        ],
        axis=1,
    )

    out_part = expert_output(
        exp_s, after(act, p0), slot_gate, place, shared_act, expert_down, shared_two
    )
    grad_two = after(grad_two, extra, out_part)
    grad_middle, grad_attn, grad_heads, gain_rows = middle_back(
        grad_two, middle, cotangent[0], gain_ffn, w_all
    )
    grad_query, near, far = attend_back(
        ctx_s, queries, grad_heads, att_f, logs, kv_all, grad_attn, extra, gain_rows
    )
    far = lax.ppermute(far, "ctx", z_swap)
    from_1, from_3 = after((from_1, from_3), near)
    add_a, add_b, part_0, part_1 = piece_sums(
        relay_kernel,
        (bf16, bf16, f32, f32),
        p0,
        p1,
        p3,
        p6,
        (from_1, 0),
        (from_3, 0),
        (from_1, 1),
        (from_3, 1),
    )
    got_11, got_30 = to(add_b, 1), to(add_a, 3)

    out_sums = spread_sums(
        exp_s, out_part, lax.ppermute(after(out_part[0], near), "exp", core_swap)
    )
    got_11, got_30 = after((got_11, got_30), out_sums[0])
    own_part, side = piece_sums(side_kernel, (f32, bf16), part_0, part_1, got_11, got_30)
    out_rows = out_sums[0].astype(f32)
    for k in range(1, 4):
        moved = lax.ppermute(out_sums[k], "exp", [(i, i ^ (4 * k)) for i in range(N_EXP)])
        out_rows = out_rows + moved.astype(f32)
    out_across = lax.ppermute(
        out_rows[1].astype(bf16), "exp", [(i, i ^ 2) for i in range(N_EXP)]
    )
    across = to(side, 4)

    shares = merge_shares(ctx_s, near, after(far, side))
    got = swap_all(shares, "ctx", y_groups)
    own = (own_part + after(across, shares).astype(f32)).astype(bf16)
    at_1, at_3, at_z = to(own, 1), to(own, 3), to(own, 4)
    columns, grad_kv, grad_down = column_grads(got, after(hidden_seq, own, out_rows), att_seq)
    columns, at_1, at_3 = lax.optimization_barrier((columns, at_1, at_3))
    owned = swap_all(columns, "exp")
    owned, gain_sum = owned_sums(owned, grad_down)
    owned, at_z1, at_z3 = lax.optimization_barrier((owned, to(at_z, 1), to(at_z, 3)))
    at_2, at_z2 = to(at_3, 1), to(at_z1, 3)
    mixed = (middle + out_rows[0] + out_across.astype(f32)).astype(bf16)[None]
    experts = unpack_experts(
        ctx_s, ((0, 0), (1, 0), (3, 0), (0, 1)), (after(own, owned), at_1, at_3, at_z)
    )
    owned = swap_all(jnp.broadcast_to(owned, (N_CTX, OWNED_ROWS, HEAD_DIM)), "ctx")
    grad_kv = swap_all(after(grad_kv, owned, mixed), "ctx")
    experts = unpack_experts(
        ctx_s, ((2, 0), (1, 1), (3, 1), (2, 1)), (at_2, at_z1, at_z3, at_z2), experts
    )
    gain_attn_sum, *dense = finish(
        after(owned, experts[0]),
        norm_attn.astype(f32).reshape(96, 1),
        query_weight,
        key_weight,
        value_weight,
    )
    input_grad = input_back(
        after(grad_query, dense[0]), grad_kv, w_all, tokens[0], gain_attn, grad_middle
    )
    return (
        mixed,
        input_grad[None],
        gain_attn_sum[:, 0],
        gain_sum[12, :96],
        *dense,
        *experts,
    )


def solution(mesh):
    token_spec = P("exp", "ctx", None)
    rows = P("exp", None)
    expert = P("exp", None, None)
    placed = (token_spec,) * 3 + (P("exp"),) * 2 + (rows,) * 7 + (expert,) * 3 + (token_spec,)
    return jax.shard_map(
        on_device,
        mesh=mesh,
        in_specs=placed,
        out_specs=(token_spec,) * 2 + (P("exp"),) * 2 + (rows,) * 7 + (expert,) * 3,
        check_vma=False,
    )
```

```python
import jax
import jax.numpy as jnp
from jax import lax
from jax.sharding import PartitionSpec as P
from jax.experimental import pallas as pl
from jax.experimental.pallas import tpu as pltpu

HEADS = 12
KV_HEADS = 4
HEAD_DIM = 128
TOPK = 6
GROUP = 3
BLOCK = 128
WIDTH = 1536
KV_WIDTH = KV_HEADS * HEAD_DIM
CAP = 48
N_EXP = 16
N_CTX = 8
LOCAL_E = 2
FF_E = 512
SHARED = 64
META = 128
HALF = 8
ROWS = HALF * CAP

epsilon = 1e-05
masked_score = -1e30
f32 = jnp.float32
bf16 = jnp.bfloat16
log2_e = 1.4426950408889634
score_scale = HEAD_DIM ** (-0.5) * log2_e

NN = (((1,), (0,)), ((), ()))
NT = (((1,), (1,)), ((), ()))
TN = (((0,), (0,)), ((), ()))


def dg(a, b, dims):
    return lax.dot_general(a, b, dims, preferred_element_type=f32)


def params(mib):
    return pltpu.CompilerParams(vmem_limit_bytes=mib * 1024 * 1024)


def cost(us):
    return pl.CostEstimate(flops=0, bytes_accessed=int(us * 3690000), transcendentals=0)


def whole(shape):
    return pl.BlockSpec(shape, lambda *_: (0,) * len(shape), pipeline_mode=pl.Buffered(1))


def sigmoid(v):
    return 1.0 / (1.0 + jnp.exp(-v))


def allowed_scores(ctx_at):
    rows = lax.broadcasted_iota(jnp.int32, (GROUP * BLOCK, N_CTX * BLOCK), 0) % BLOCK
    cols = lax.broadcasted_iota(jnp.int32, (GROUP * BLOCK, N_CTX * BLOCK), 1)
    return rows + ctx_at * BLOCK >= cols


def stack_heads(block):
    return jnp.concatenate([block[:, j * HEAD_DIM : (j + 1) * HEAD_DIM] for j in range(GROUP)], axis=0)


def unstack_heads(rows):
    return jnp.concatenate([rows[j * BLOCK : (j + 1) * BLOCK] for j in range(GROUP)], axis=1)


def attend_kernel(ctx_ref, q_ref, k_ref, v_ref, att_ref, attf_ref, log_ref):
    q = stack_heads(q_ref[...])
    keys = k_ref[...].reshape(N_CTX * BLOCK, HEAD_DIM)
    values = v_ref[...].reshape(N_CTX * BLOCK, HEAD_DIM)
    scores = jnp.where(allowed_scores(ctx_ref[0]), dg(q, keys, NT) * score_scale, masked_score)
    top = jnp.max(scores, axis=-1, keepdims=True)
    weights = jnp.exp2(scores - top)
    total = jnp.sum(weights, axis=-1, keepdims=True)
    out = dg(weights.astype(bf16), values, NN) * (1.0 / total)
    out = unstack_heads(out)
    attf_ref[...] = out
    att_ref[...] = out.astype(bf16)
    log_ref[...] = jnp.broadcast_to(top + jnp.log2(total), (GROUP * BLOCK, HEAD_DIM))


def kv_specs():
    return [
        pl.BlockSpec((N_CTX, BLOCK, HEAD_DIM), lambda g: (0, 0, g)),
        pl.BlockSpec((N_CTX, BLOCK, HEAD_DIM), lambda g: (0, 0, KV_HEADS + g)),
    ]


def head_spec():
    return pl.BlockSpec((BLOCK, GROUP * HEAD_DIM), lambda g: (0, g))


def attend(ctx_at, qkv, kv_all):
    return pl.pallas_call(
        attend_kernel,
        grid=(KV_HEADS,),
        in_specs=[pl.BlockSpec(memory_space=pltpu.SMEM), head_spec()] + kv_specs(),
        out_specs=[
            head_spec(),
            head_spec(),
            pl.BlockSpec((GROUP * BLOCK, HEAD_DIM), lambda g: (g, 0)),
        ],
        out_shape=[
            jax.ShapeDtypeStruct((BLOCK, WIDTH), bf16),
            jax.ShapeDtypeStruct((BLOCK, WIDTH), f32),
            jax.ShapeDtypeStruct((HEADS * BLOCK, HEAD_DIM), f32),
        ],
        cost_estimate=cost(6),
        compiler_params=params(48),
        name="attend",
    )(ctx_at, qkv, kv_all, kv_all)


SEQ = N_CTX * BLOCK
AT_QUERY, AT_MIXED, AT_OUT = SEQ, SEQ + BLOCK, SEQ + 2 * BLOCK
AT_SHARED = SEQ + 3 * BLOCK
AT_DOWN = AT_SHARED + 16 * N_EXP
AT_GAIN = AT_DOWN + 96
SENT_ROWS = AT_GAIN + 16


def halves(a, b, lane):
    low = jnp.where(lane < 64, a, pltpu.roll(b, 64, 1))
    high = jnp.where(lane < 64, pltpu.roll(a, 64, 1), b)
    return low, high


def attend_back_kernel(
    ctx_ref,
    q_ref,
    ga_ref,
    attf_ref,
    log_ref,
    k_ref,
    v_ref,
    all_ga_ref,
    extra_ref,
    gain_ref,
    dq_ref,
    near_ref,
    far_ref,
    kept_ref,
):
    group = pl.program_id(0)
    z_at = ctx_ref[0] // 4

    def send(dest, z, start, stop, rows):
        @pl.when(z_at == z)
        def _():
            near_ref[dest, start:stop] = rows

        @pl.when(z_at != z)
        def _():
            far_ref[dest, start:stop] = rows

    q = stack_heads(q_ref[...])
    grad = stack_heads(ga_ref[...])
    delta = jnp.sum(grad.astype(f32) * stack_heads(attf_ref[...]), axis=-1, keepdims=True)
    keys = k_ref[...].reshape(SEQ, HEAD_DIM)
    values = v_ref[...].reshape(SEQ, HEAD_DIM)
    scores = jnp.where(allowed_scores(ctx_ref[0]), dg(q, keys, NT) * score_scale, masked_score)
    weights = jnp.exp2(scores - log_ref[:, :1])
    grad_weights = dg(grad, values, NT)
    grad_raw = (weights * (grad_weights - delta)).astype(bf16)
    scale = HEAD_DIM ** (-0.5)
    dq = unstack_heads(dg(grad_raw, keys, NN) * scale)
    dq_ref[...] = dq.astype(bf16)
    kept_ref[group] = dq
    grad_k = dg(grad_raw, q, TN) * scale
    grad_v = dg(weights.astype(bf16), grad, TN)
    low, high = halves(grad_k, grad_v, lax.broadcasted_iota(jnp.int32, (SEQ, HEAD_DIM), 1))
    low, high = low.astype(bf16), high.astype(bf16)
    send(2 * (group % 2), group // 2, 0, SEQ, low)
    send(2 * (group % 2) + 1, group // 2, 0, SEQ, high)

    @pl.when(group == KV_HEADS - 1)
    def _():
        lane = lax.broadcasted_iota(jnp.int32, (BLOCK, HEAD_DIM), 1)

        def dq_tile(m):
            return kept_ref[m // GROUP, :, HEAD_DIM * (m % GROUP) : HEAD_DIM * (m % GROUP + 1)]

        def ga_tile(m):
            return all_ga_ref[:, HEAD_DIM * m : HEAD_DIM * (m + 1)].astype(f32)

        mixed = []
        for m in range(KV_HEADS):
            mixed += halves(dq_tile(N_CTX + m), ga_tile(N_CTX + m), lane)
        gains = gain_ref[...].astype(bf16)
        for c in range(N_CTX):
            tiles = [dq_tile(c).astype(bf16), mixed[c].astype(bf16), ga_tile(c).astype(bf16)]
            rows = jnp.concatenate(tiles + [extra_ref[c], gains], axis=0)
            send(c % 4, c // 4, AT_QUERY, SENT_ROWS, rows)


def attend_back(ctx_at, qkv, grad_att, att_f, logs, kv_all, grad_attn, extra, gain_rows):
    return pl.pallas_call(
        attend_back_kernel,
        grid=(KV_HEADS,),
        in_specs=[
            pl.BlockSpec(memory_space=pltpu.SMEM),
            head_spec(),
            head_spec(),
            head_spec(),
            pl.BlockSpec((GROUP * BLOCK, HEAD_DIM), lambda g: (g, 0)),
        ]
        + kv_specs()
        + [
            whole((BLOCK, WIDTH)),
            whole((N_CTX, AT_GAIN - AT_SHARED, HEAD_DIM)),
            whole((16, HEAD_DIM)),
        ],
        out_specs=[head_spec()] + [whole((4, SENT_ROWS, HEAD_DIM))] * 2,
        out_shape=[
            jax.ShapeDtypeStruct((BLOCK, WIDTH), bf16),
            jax.ShapeDtypeStruct((4, SENT_ROWS, HEAD_DIM), bf16),
            jax.ShapeDtypeStruct((4, SENT_ROWS, HEAD_DIM), bf16),
        ],
        scratch_shapes=[pltpu.VMEM((KV_HEADS, BLOCK, GROUP * HEAD_DIM), f32)],
        cost_estimate=cost(2),
        compiler_params=params(48),
        name="attend_back",
    )(ctx_at, qkv, grad_att, att_f, logs, kv_all, kv_all, grad_attn, extra, gain_rows)


def middle_kernel(att_ref, w_ref, x_ref, gain_ref, middle_ref, hidden_ref):
    middle = x_ref[...].astype(f32) + dg(att_ref[...], w_ref[...], NN)
    inv = lax.rsqrt(jnp.mean(middle * middle, axis=-1, keepdims=True) + epsilon)
    middle_ref[...] = middle
    hidden_ref[...] = (middle * inv * gain_ref[...]).astype(bf16)


def w_cols(width, at):
    return pl.BlockSpec((WIDTH, width), lambda *_: (0, at), pipeline_mode=pl.Buffered(1))


def middle_norm(attended, w_all, tokens, gain):
    return pl.pallas_call(
        middle_kernel,
        grid=(1,),
        in_specs=[
            whole((BLOCK, WIDTH)),
            w_cols(WIDTH, 1),
            whole((BLOCK, WIDTH)),
            whole((1, WIDTH)),
        ],
        out_specs=[whole((BLOCK, WIDTH)), whole((BLOCK, WIDTH))],
        out_shape=[
            jax.ShapeDtypeStruct((BLOCK, WIDTH), f32),
            jax.ShapeDtypeStruct((BLOCK, WIDTH), bf16),
        ],
        cost_estimate=cost(2),
        compiler_params=params(32),
        name="middle_norm",
    )(attended, w_all, tokens, gain)


def norm_back(grad_normed, normed, inv_root):
    return inv_root * (
        grad_normed - normed * jnp.mean(grad_normed * normed, axis=-1, keepdims=True)
    )


def middle_back_kernel(
    pieces_ref, middle_ref, up_ref, gain_ref, w_ref, gm_ref, ga_ref, gh_ref, gg_ref
):
    grad_two = pieces_ref[0].astype(f32)
    for i in range(1, HALF):
        grad_two = grad_two + pieces_ref[i].astype(f32)
    middle = middle_ref[...]
    inv = lax.rsqrt(jnp.mean(middle * middle, axis=-1, keepdims=True) + epsilon)
    normed = middle * inv
    gains = jnp.sum(grad_two * normed, axis=0, keepdims=True)
    gg_ref[...] = jnp.zeros((16, HEAD_DIM), f32)
    for m in range(HEADS):
        gg_ref[m : m + 1] = gains[:, HEAD_DIM * m : HEAD_DIM * (m + 1)]
    grad_middle = up_ref[...].astype(f32) + norm_back(grad_two * gain_ref[...], normed, inv)
    gm_ref[...] = grad_middle
    grad_attn = grad_middle.astype(bf16)
    ga_ref[...] = grad_attn
    gh_ref[...] = dg(grad_attn, w_ref[...], NT).astype(bf16)


def middle_back(pieces, middle, upstream, gain, w_all):
    return pl.pallas_call(
        middle_back_kernel,
        grid=(1,),
        in_specs=[
            whole((HALF, BLOCK, WIDTH)),
            whole((BLOCK, WIDTH)),
            whole((BLOCK, WIDTH)),
            whole((1, WIDTH)),
            w_cols(WIDTH, 1),
        ],
        out_specs=[whole((BLOCK, WIDTH))] * 3 + [whole((16, HEAD_DIM))],
        out_shape=[
            jax.ShapeDtypeStruct((BLOCK, WIDTH), f32),
            jax.ShapeDtypeStruct((BLOCK, WIDTH), bf16),
            jax.ShapeDtypeStruct((BLOCK, WIDTH), bf16),
            jax.ShapeDtypeStruct((16, HEAD_DIM), f32),
        ],
        cost_estimate=cost(1),
        compiler_params=params(48),
        name="middle_back",
    )(pieces, middle, upstream, gain, w_all)


def place_kernel(
    at_ref, up_ref, down_ref, sdown_ref, place_ref, geo_ref, geh_ref, gsh_ref, gate_ref
):
    lane = lax.broadcasted_iota(jnp.int32, (BLOCK, META), 1)
    row = lax.broadcasted_iota(jnp.int32, (BLOCK, META), 0)
    before = (row > lane).astype(bf16)
    slot = (lane % 64).astype(f32)
    first_id = (at_ref[0] * LOCAL_E).astype(f32)
    row_id = first_id + (row >= 64).astype(f32)

    for chip in range(HALF):
        meta = up_ref[chip, 0, :, WIDTH:].astype(f32)
        named = lane < TOPK
        zero = jnp.zeros((BLOCK, META), f32)
        hit0 = jnp.where(named & (meta == first_id), 1.0, zero)
        hit1 = jnp.where(named & (meta == first_id + 1.0), 1.0, zero)
        mask = jnp.where(
            lane < 64,
            jnp.sum(hit0, axis=1, keepdims=True),
            jnp.sum(hit1, axis=1, keepdims=True),
        )
        rank = dg(before, mask.astype(bf16), NN)
        place = jnp.where((mask > 0.5) & (rank == slot), 1.0, zero).astype(bf16)
        place_ref[chip, 0] = place
        rows = dg(place, up_ref[chip, 0], TN)
        slot_meta = rows[:, WIDTH:]
        gates = pltpu.roll(slot_meta, META - TOPK, 1) + pltpu.roll(
            slot_meta, META - 2 * TOPK, 1
        )
        gate = jnp.sum(
            jnp.where(named & (slot_meta == row_id), gates, zero), axis=1, keepdims=True
        )
        geo = (gate * rows[:, :WIDTH]).astype(bf16)
        wide_gate = jnp.broadcast_to(gate, (BLOCK, META))
        at = chip * CAP
        for e in range(LOCAL_E):
            geo_ref[e, 0, at : at + CAP] = geo[64 * e : 64 * e + CAP]
            gate_ref[e, 0, at : at + CAP] = wide_gate[64 * e : 64 * e + CAP]
        gsh_ref[chip, 0] = dg(up_ref[chip, 0, :, :WIDTH], sdown_ref[...], NT)
    for e in range(LOCAL_E):
        geh_ref[e, 0] = dg(geo_ref[e, 0], down_ref[e], NT)


def by_core(cols):
    return pl.BlockSpec(
        (HALF, 1, BLOCK, cols),
        lambda s, at: (0, jnp.where(s == 0, 1 - at[0] % 2, at[0] % 2), 0, 0),
    )


def by_step(cols):
    return pl.BlockSpec((LOCAL_E, 1, ROWS, cols), lambda s, at: (0, s, 0, 0))


def place_rows(exp_at, up_all, expert_down, shared_two):
    return pl.pallas_call(
        place_kernel,
        grid_spec=pltpu.PrefetchScalarGridSpec(
            num_scalar_prefetch=1,
            grid=(2,),
            in_specs=[
                by_core(WIDTH + META),
                whole((LOCAL_E, FF_E, WIDTH)),
                whole((2 * SHARED, WIDTH)),
            ],
            out_specs=[by_core(META), by_step(WIDTH), by_step(FF_E), by_core(META), by_step(META)],
        ),
        out_shape=[
            jax.ShapeDtypeStruct((HALF, 2, BLOCK, META), bf16),
            jax.ShapeDtypeStruct((LOCAL_E, 2, ROWS, WIDTH), bf16),
            jax.ShapeDtypeStruct((LOCAL_E, 2, ROWS, FF_E), f32),
            jax.ShapeDtypeStruct((HALF, 2, BLOCK, META), f32),
            jax.ShapeDtypeStruct((LOCAL_E, 2, ROWS, META), f32),
        ],
        cost_estimate=cost(14),
        compiler_params=params(56),
        name="place_rows",
    )(exp_at, up_all, expert_down, shared_two)


def expert_kernel(
    at_ref,
    hid_ref,
    place_ref,
    geh_ref,
    gsh_ref,
    wg_ref,
    wu_ref,
    ws_ref,
    part_ref,
    x_ref,
    act_ref,
    dgu_ref,
    sact_ref,
    sgrad_ref,
):
    for chip in range(HALF):
        rows = dg(place_ref[chip, 0], hid_ref[chip, 0], TN).astype(bf16)
        at = chip * CAP
        for e in range(LOCAL_E):
            x_ref[e, 0, at : at + CAP] = rows[64 * e : 64 * e + CAP]
    pairs = []
    for e in range(LOCAL_E):
        pre_gate = dg(x_ref[e, 0], wg_ref[e], NN)
        pre_up = dg(x_ref[e, 0], wu_ref[e], NN)
        sig = sigmoid(pre_gate)
        act = pre_gate * sig
        act_ref[e, 0] = (act * pre_up).astype(bf16)
        geh = geh_ref[e, 0]
        d_gate = (geh * pre_up * (sig * (1.0 + pre_gate * (1.0 - sig)))).astype(bf16)
        d_up = (geh * act).astype(bf16)
        dgu_ref[e, 0, :, :FF_E] = d_gate
        dgu_ref[e, 0, :, FF_E:] = d_up
        pairs.append((dg(d_gate, wg_ref[e], NT) + dg(d_up, wu_ref[e], NT)).astype(bf16))
    lane = lax.broadcasted_iota(jnp.int32, (BLOCK, 2 * SHARED), 1) < SHARED
    gap = jnp.zeros((64 - CAP, WIDTH), bf16)
    for chip in range(HALF):
        pre = dg(hid_ref[chip, 0], ws_ref[...], NN)
        turned = pltpu.roll(pre, SHARED, 1)
        gate, up = jnp.where(lane, pre, turned), jnp.where(lane, turned, pre)
        sig = sigmoid(gate)
        act = gate * sig
        sact_ref[chip, 0] = jnp.where(lane, act * up, 0.0).astype(bf16)
        slope = sig * (1.0 + gate * (1.0 - sig))
        sgrad = (gsh_ref[chip, 0] * jnp.where(lane, up * slope, act)).astype(bf16)
        sgrad_ref[chip, 0] = sgrad
        at = chip * CAP
        stacked = jnp.concatenate([pairs[0][at : at + CAP], gap, pairs[1][at : at + CAP], gap], 0)
        part_ref[0, chip] = (
            dg(place_ref[chip, 0], stacked, NN) + dg(sgrad, ws_ref[...], NT)
        ).astype(bf16)


def expert_back(exp_at, hidden, place, geh, gsh, wg, wu, ws):
    return pl.pallas_call(
        expert_kernel,
        grid_spec=pltpu.PrefetchScalarGridSpec(
            num_scalar_prefetch=1,
            grid=(2,),
            in_specs=[
                by_core(WIDTH),
                by_core(META),
                by_step(FF_E),
                by_core(META),
                whole((LOCAL_E, WIDTH, FF_E)),
                whole((LOCAL_E, WIDTH, FF_E)),
                whole((WIDTH, 2 * SHARED)),
            ],
            out_specs=[
                pl.BlockSpec((1, HALF, BLOCK, WIDTH), lambda s, at: (s, 0, 0, 0)),
                by_step(WIDTH),
                by_step(FF_E),
                by_step(2 * FF_E),
                by_core(META),
                by_core(META),
            ],
        ),
        out_shape=[
            jax.ShapeDtypeStruct((2, HALF, BLOCK, WIDTH), bf16),
            jax.ShapeDtypeStruct((LOCAL_E, 2, ROWS, WIDTH), bf16),
            jax.ShapeDtypeStruct((LOCAL_E, 2, ROWS, FF_E), bf16),
            jax.ShapeDtypeStruct((LOCAL_E, 2, ROWS, 2 * FF_E), bf16),
            jax.ShapeDtypeStruct((HALF, 2, BLOCK, META), bf16),
            jax.ShapeDtypeStruct((HALF, 2, BLOCK, META), bf16),
        ],
        cost_estimate=cost(28),
        compiler_params=params(60),
        name="expert_back",
    )(exp_at, hidden, place, geh, gsh, wg, wu, ws)


def output_kernel(at_ref, act_ref, gate_ref, place_ref, sact_ref, wd_ref, sd_ref, part_ref):
    outs = []
    for e in range(LOCAL_E):
        out = dg(act_ref[e, 0], wd_ref[e], NN).astype(bf16).astype(f32)
        outs.append((out * gate_ref[e, 0, :, :1]).astype(bf16))
    gap = jnp.zeros((64 - CAP, WIDTH), bf16)
    for chip in range(HALF):
        at = chip * CAP
        stacked = jnp.concatenate([outs[0][at : at + CAP], gap, outs[1][at : at + CAP], gap], 0)
        part_ref[0, chip] = (
            dg(place_ref[chip, 0], stacked, NN) + dg(sact_ref[chip, 0], sd_ref[...], NN)
        ).astype(bf16)


def expert_output(exp_at, act, gate, place, sact, wd, sd):
    return pl.pallas_call(
        output_kernel,
        grid_spec=pltpu.PrefetchScalarGridSpec(
            num_scalar_prefetch=1,
            grid=(2,),
            in_specs=[
                by_step(FF_E),
                by_step(META),
                by_core(META),
                by_core(META),
                whole((LOCAL_E, FF_E, WIDTH)),
                whole((2 * SHARED, WIDTH)),
            ],
            out_specs=pl.BlockSpec((1, HALF, BLOCK, WIDTH), lambda s, at: (s, 0, 0, 0)),
        ),
        out_shape=jax.ShapeDtypeStruct((2, HALF, BLOCK, WIDTH), bf16),
        cost_estimate=cost(2),
        compiler_params=params(48),
        name="expert_output",
    )(exp_at, act, gate, place, sact, wd, sd)


SHARE = 3 * BLOCK
TO_SHARED = SEQ + 2 * SHARE
TO_DOWN = TO_SHARED + 16 * N_EXP
TO_GAIN = TO_DOWN + 96
MERGED_ROWS = TO_GAIN + 16


def merge_kernel(ctx_ref, near_ref, got_ref, out_ref):
    z_at = ctx_ref[0] // 4
    near, got = near_ref[0], got_ref[0]

    def add(a, b):
        return (a.astype(f32) + b.astype(f32)).astype(bf16)

    out_ref[0, :SEQ] = add(near[:SEQ], got[:SEQ])
    out_ref[0, TO_SHARED:] = add(near[AT_SHARED:], got[AT_SHARED:])
    mine, theirs = near[AT_QUERY:AT_SHARED], got[AT_QUERY:AT_SHARED]
    out_ref[0, SEQ : SEQ + SHARE] = jnp.where(z_at == 0, mine, theirs)
    out_ref[0, SEQ + SHARE : TO_SHARED] = jnp.where(z_at == 0, theirs, mine)


def merge_shares(ctx_at, near, got):
    spec = pl.BlockSpec((1, SENT_ROWS, HEAD_DIM), lambda i: (i, 0, 0))
    return pl.pallas_call(
        merge_kernel,
        grid=(4,),
        in_specs=[pl.BlockSpec(memory_space=pltpu.SMEM), spec, spec],
        out_specs=pl.BlockSpec((1, MERGED_ROWS, HEAD_DIM), lambda i: (i, 0, 0)),
        out_shape=jax.ShapeDtypeStruct((4, MERGED_ROWS, HEAD_DIM), bf16),
        cost_estimate=cost(3),
        compiler_params=params(32),
        name="merge_shares",
    )(ctx_at, near, got)


def columns_kernel(got_ref, hidden_ref, att_ref, sent_ref, kv_ref, down_ref):
    def summed(start, stop):
        out = got_ref[0, start:stop].astype(f32)
        for src in range(1, 4):
            out = out + got_ref[src, start:stop].astype(f32)
        return out

    grad_kv = summed(0, SEQ).astype(bf16)
    kv_ref[...] = grad_kv.reshape(N_CTX, BLOCK, HEAD_DIM)

    def rows_of(tile, order):
        at = SEQ + BLOCK * tile
        return jnp.concatenate(
            [got_ref[y, at + SHARE * z : at + SHARE * z + BLOCK] for z, y in order], axis=0
        )

    in_order = [(i // 4, i % 4) for i in range(N_CTX)]
    y_order = [(i % 2, i // 2) for i in range(N_CTX)]
    lane = lax.broadcasted_iota(jnp.int32, (SEQ, HEAD_DIM), 1)
    zero = jnp.zeros((SEQ, HEAD_DIM), bf16)
    mixed_q = jnp.where(lane < 64, rows_of(1, in_order), zero)
    mixed_o = jnp.where(lane < 64, zero, rows_of(1, y_order))
    left = jnp.concatenate([rows_of(0, in_order).T, mixed_q.T, grad_kv.T], axis=0)
    right = jnp.concatenate([mixed_o.T, rows_of(2, y_order).T], axis=0)
    by_hidden = dg(left, hidden_ref[...].reshape(SEQ, WIDTH), NN)
    by_att = dg(right, att_ref[...].reshape(SEQ, WIDTH), NN)
    tiles = [
        by_hidden[:BLOCK],
        by_hidden[BLOCK : 2 * BLOCK] + by_att[:BLOCK],
        by_att[BLOCK:],
        by_hidden[2 * BLOCK :],
    ]
    for t, tile in enumerate(tiles):
        sent_ref[:, :96, HEAD_DIM * t : HEAD_DIM * (t + 1)] = (
            tile.T.astype(bf16).reshape(N_EXP, 96, HEAD_DIM)
        )

    down_ref[...] = summed(TO_DOWN, TO_GAIN).astype(bf16)
    shared = summed(TO_SHARED, TO_DOWN)
    gains = summed(TO_GAIN, MERGED_ROWS)
    row = lax.broadcasted_iota(jnp.int32, (16, HEAD_DIM), 0)
    one_lane = lax.broadcasted_iota(jnp.int32, (1, HEAD_DIM), 1)
    for i in range(N_EXP):
        m, offset = (96 * i) // HEAD_DIM, (96 * i) % HEAD_DIM
        gain = gains[m : m + 1]
        if offset:
            shift = HEAD_DIM - offset
            gain = jnp.where(
                one_lane < shift,
                pltpu.roll(gain, shift, 1),
                pltpu.roll(gains[m + 1 : m + 2], shift, 1),
            )
        rows = jnp.where(row == 12, jnp.broadcast_to(gain, (16, HEAD_DIM)), shared[16 * i : 16 * i + 16])
        sent_ref[i, 96:, :HEAD_DIM] = rows.astype(bf16)
        sent_ref[i, 96:, HEAD_DIM:] = jnp.zeros((16, 512 - HEAD_DIM), bf16)


def column_grads(got, hidden_seq, att_seq):
    return pl.pallas_call(
        columns_kernel,
        out_shape=[
            jax.ShapeDtypeStruct((N_EXP, 112, 512), bf16),
            jax.ShapeDtypeStruct((N_CTX, BLOCK, HEAD_DIM), bf16),
            jax.ShapeDtypeStruct((96, HEAD_DIM), bf16),
        ],
        cost_estimate=cost(8),
        compiler_params=params(56),
        name="column_grads",
    )(got, hidden_seq, att_seq)


OWNED_ROWS = 4 * 96 + 16 * N_EXP + 96


def owned_kernel(got_ref, down_ref, owned_ref, gain_ref):
    total = got_ref[0, :96].astype(f32)
    gains = got_ref[0, 96:, :HEAD_DIM].astype(f32)
    for src in range(1, N_EXP):
        total = total + got_ref[src, :96].astype(f32)
        gains = gains + got_ref[src, 96:, :HEAD_DIM].astype(f32)
    gain_ref[...] = gains
    for t in range(4):
        owned_ref[96 * t : 96 * t + 96] = total[:, HEAD_DIM * t : HEAD_DIM * (t + 1)].astype(bf16)
    for src in range(N_EXP):
        at = 384 + 16 * src
        owned_ref[at : at + 16] = got_ref[src, 96:, :HEAD_DIM]
    owned_ref[384 + 16 * N_EXP :] = down_ref[...]


def owned_sums(got, down):
    return pl.pallas_call(
        owned_kernel,
        out_shape=[
            jax.ShapeDtypeStruct((OWNED_ROWS, HEAD_DIM), bf16),
            jax.ShapeDtypeStruct((16, HEAD_DIM), f32),
        ],
        cost_estimate=cost(3),
        compiler_params=params(32),
        name="owned_sums",
    )(got, down)


def finish_kernel(
    got_ref,
    gain_in_ref,
    wq_ref,
    wk_ref,
    wv_ref,
    gain_ref,
    q_ref,
    k_ref,
    v_ref,
    out_ref,
    sg_ref,
    su_ref,
    sd_ref,
):
    lane = lax.broadcasted_iota(jnp.int32, (96, HEAD_DIM), 1)

    def tile(c, t):
        return got_ref[c, 96 * t : 96 * t + 96].astype(f32)

    for c in range(N_CTX):
        at = HEAD_DIM * c
        q_ref[:, at : at + HEAD_DIM] = tile(c, 0)
        out_ref[:, at : at + HEAD_DIM] = tile(c, 2)
    for m in range(N_CTX // 2):
        at = HEAD_DIM * m
        low, high = halves(tile(2 * m, 1), tile(2 * m + 1, 1), lane)
        q_ref[:, 1024 + at : 1024 + at + HEAD_DIM] = low
        out_ref[:, 1024 + at : 1024 + at + HEAD_DIM] = high
        low, high = halves(tile(2 * m, 3), tile(2 * m + 1, 3), lane)
        k_ref[:, at : at + HEAD_DIM] = low
        v_ref[:, at : at + HEAD_DIM] = high
    gain = (
        jnp.sum(q_ref[...] * wq_ref[...].astype(f32), axis=1, keepdims=True)
        + jnp.sum(k_ref[...] * wk_ref[...].astype(f32), axis=1, keepdims=True)
        + jnp.sum(v_ref[...] * wv_ref[...].astype(f32), axis=1, keepdims=True)
    ) / gain_in_ref[...]
    gain_ref[...] = jnp.broadcast_to(gain, (96, HEAD_DIM))
    row = lax.broadcasted_iota(jnp.int32, (96, HEAD_DIM), 0)
    picks = jnp.where((lane % 16 < 12) & (row == 12 * (lane // 16) + lane % 16), 1.0, 0.0)
    picks = picks.astype(bf16)

    def shared_tile(j):
        at = 384 + 16 * j
        rows = jnp.concatenate([got_ref[c, at : at + 16] for c in range(N_CTX)], axis=0)
        return dg(picks, rows, NN)

    for m in range(N_EXP // 2):
        at = HEAD_DIM * m
        low, high = halves(shared_tile(2 * m), shared_tile(2 * m + 1), lane)
        sg_ref[:, at : at + HEAD_DIM] = low
        su_ref[:, at : at + HEAD_DIM] = high
    for c in range(N_CTX):
        rows = got_ref[c, 384 + 16 * N_EXP :].astype(f32)
        for m in range(HEADS):
            sd_ref[8 * c : 8 * c + 8, HEAD_DIM * m : HEAD_DIM * (m + 1)] = rows[8 * m : 8 * m + 8]


def finish(got, gain_column, query_weight, key_weight, value_weight):
    shapes = [(96, 128), (96, 1536), (96, 512), (96, 512), (96, 1536), (96, 1024), (96, 1024)]
    return pl.pallas_call(
        finish_kernel,
        out_shape=[jax.ShapeDtypeStruct(s, f32) for s in shapes + [(SHARED, WIDTH)]],
        cost_estimate=cost(4),
        compiler_params=params(32),
        name="finish",
    )(got, gain_column, query_weight, key_weight, value_weight)


def input_kernel(dq_ref, got_ref, wq_ref, wkv_ref, x_ref, gain_ref, gm_ref, out_ref):
    lane = lax.broadcasted_iota(jnp.int32, (BLOCK, HEAD_DIM), 1)
    lows, highs = [], []
    for m in range(KV_HEADS):
        low, high = halves(got_ref[2 * m].astype(f32), got_ref[2 * m + 1].astype(f32), lane)
        lows.append(low.astype(bf16))
        highs.append(high.astype(bf16))
    grad_kv = jnp.concatenate(lows + highs, axis=1)
    grad_one = dg(dq_ref[...], wq_ref[...], NT) + dg(grad_kv, wkv_ref[...], NT)
    inputs = x_ref[...].astype(f32)
    inv = lax.rsqrt(jnp.mean(inputs * inputs, axis=-1, keepdims=True) + epsilon)
    out_ref[...] = (gm_ref[...] + norm_back(grad_one * gain_ref[...], inputs * inv, inv)).astype(bf16)


def input_back(grad_query, grad_kv, w_all, tokens, gain, grad_middle):
    return pl.pallas_call(
        input_kernel,
        grid=(1,),
        in_specs=[
            whole((BLOCK, WIDTH)),
            whole((N_CTX, BLOCK, HEAD_DIM)),
            w_cols(WIDTH, 0),
            w_cols(2 * KV_WIDTH, 3),
            whole((BLOCK, WIDTH)),
            whole((1, WIDTH)),
            whole((BLOCK, WIDTH)),
        ],
        out_specs=whole((BLOCK, WIDTH)),
        out_shape=jax.ShapeDtypeStruct((BLOCK, WIDTH), bf16),
        cost_estimate=cost(7),
        compiler_params=params(48),
        name="input_back",
    )(grad_query, grad_kv, w_all, w_all, tokens, gain, grad_middle)


def norm_rows_kernel(x_ref, gain_ref, out_ref):
    inputs = x_ref[0].astype(f32)
    inv = lax.rsqrt(jnp.mean(inputs * inputs, axis=-1, keepdims=True) + epsilon)
    out_ref[0] = (inputs * inv * gain_ref[...]).astype(bf16)


def norm_rows(rows, gain):
    count = rows.shape[0]
    spec = pl.BlockSpec((1, BLOCK, WIDTH), lambda i: (i, 0, 0))
    turned = pl.BlockSpec((1, BLOCK, WIDTH), lambda i: ((i % 2) * 4 + i // 2, 0, 0))
    return pl.pallas_call(
        norm_rows_kernel,
        grid=(count,),
        in_specs=[spec, whole((1, WIDTH))],
        out_specs=spec if count == 1 else turned,
        out_shape=jax.ShapeDtypeStruct(rows.shape, bf16),
        cost_estimate=cost(2),
        compiler_params=params(32),
        name="norm_rows",
    )(rows, gain)


def project_kernel(own_ref, seq_ref, w_ref, q_ref, kv_ref):
    step = pl.program_id(0)

    @pl.when(step < 3)
    def _():
        q_ref[...] = dg(own_ref[0], w_ref[...], NN).astype(bf16)

    @pl.when(step >= 3)
    def _():
        rows = seq_ref[...].reshape(N_CTX * BLOCK, WIDTH)
        kv_ref[...] = dg(rows, w_ref[...], NN).astype(bf16).reshape(N_CTX, BLOCK, KV_WIDTH)


def project(own, seq, w_all):
    return pl.pallas_call(
        project_kernel,
        grid=(5,),
        in_specs=[
            whole((1, BLOCK, WIDTH)),
            whole((N_CTX, BLOCK, WIDTH)),
            pl.BlockSpec((WIDTH, KV_WIDTH), lambda i: (0, jnp.where(i < 3, i, i + 3))),
        ],
        out_specs=[
            pl.BlockSpec((BLOCK, KV_WIDTH), lambda i: (0, jnp.minimum(i, 2))),
            pl.BlockSpec((N_CTX, BLOCK, KV_WIDTH), lambda i: (0, 0, jnp.maximum(i - 3, 0))),
        ],
        out_shape=[
            jax.ShapeDtypeStruct((BLOCK, WIDTH), bf16),
            jax.ShapeDtypeStruct((N_CTX, BLOCK, 2 * KV_WIDTH), bf16),
        ],
        cost_estimate=cost(8),
        compiler_params=params(48),
        name="project",
    )(own, seq, w_all)


PIECE = 2 * WIDTH + WIDTH * BLOCK // HEAD_DIM


def spread_kernel(at_ref, own_ref, low_ref, high_ref, *outs):
    chip = (at_ref[0] >> 1) ^ pl.program_id(0)
    got = jnp.where(chip < 4, low_ref[0], high_ref[0])
    total = (own_ref[0, 0].astype(f32) + got.astype(f32)).astype(bf16)
    for k in range(HALF):

        @pl.when(pl.program_id(0) == k)
        def _():
            outs[k // 2][k % 2] = total


def spread_sums(exp_at, parts, low, high):
    half = pl.BlockSpec((1, BLOCK, WIDTH), lambda k, at: (((at[0] >> 1) ^ k) & 3, 0, 0))
    return pl.pallas_call(
        spread_kernel,
        grid_spec=pltpu.PrefetchScalarGridSpec(
            num_scalar_prefetch=1,
            grid=(HALF,),
            in_specs=[
                pl.BlockSpec((1, 1, BLOCK, WIDTH), lambda k, at: (1, (at[0] >> 1) ^ k, 0, 0)),
                half,
                half,
            ],
            out_specs=[whole((2, BLOCK, WIDTH))] * 4,
        ),
        out_shape=[jax.ShapeDtypeStruct((2, BLOCK, WIDTH), bf16)] * 4,
        cost_estimate=cost(4),
        compiler_params=params(32),
        name="spread_sums",
    )(exp_at, parts, low, high)


def of_step(values, step):
    out = jnp.int32(values[0])
    for i, value in enumerate(values[1:], 1):
        out = jnp.where(step == i, value, out)
    return out


def expert_weights_kernel(halved, at_ref, x_ref, geo_ref, act_ref, dgate_ref, dup_ref, *outs):
    step = pl.program_id(0)
    rhs = jnp.concatenate([dgate_ref[0], dup_ref[0]], axis=1)
    both = dg(x_ref[0], rhs, TN).astype(bf16)
    down = dg(act_ref[0], geo_ref[0], TN).astype(bf16)
    for i in range(4):

        @pl.when(step == i)
        def _():
            start = (i % 2) * PIECE if halved else 0
            out = outs[i // 2 if halved else i].at[pl.ds(start, PIECE)]
            out[:WIDTH] = both[:, :HEAD_DIM]
            out[WIDTH : 2 * WIDTH] = both[:, HEAD_DIM:]
            for m in range(WIDTH // HEAD_DIM):
                at = 2 * WIDTH + m * BLOCK
                out[at : at + BLOCK] = down[:, m * HEAD_DIM : (m + 1) * HEAD_DIM]


def expert_weights(ctx_at, steps, halved, arrived, grad_eo, act, grad_gu):
    rows = 2 * ROWS

    def expert(s, at):
        return (at[0] >> 2) ^ of_step([side for _, side in steps], s)

    def lanes(shift):
        return pl.BlockSpec(
            (1, rows, HEAD_DIM),
            lambda s, at: (
                expert(s, at),
                0,
                shift + ((at[0] & 3) ^ of_step([r for r, _ in steps], s)),
            ),
        )

    rows_of = pl.BlockSpec((1, rows, WIDTH), lambda s, at: (expert(s, at), 0, 0))
    count, length = (2, 2 * PIECE) if halved else (4, PIECE)
    return pl.pallas_call(
        lambda *refs: expert_weights_kernel(halved, *refs),
        grid_spec=pltpu.PrefetchScalarGridSpec(
            num_scalar_prefetch=1,
            grid=(4,),
            in_specs=[rows_of, rows_of, lanes(0), lanes(0), lanes(4)],
            out_specs=[whole((length, HEAD_DIM))] * count,
        ),
        out_shape=[jax.ShapeDtypeStruct((length, HEAD_DIM), bf16)] * count,
        cost_estimate=cost(2),
        compiler_params=params(56),
        name="expert_weights",
    )(ctx_at, arrived, grad_eo, act, grad_gu, grad_gu)


def unpack_kernel(count, at_ref, *refs):
    pieces, (gate_ref, up_ref, down_ref) = refs[:count], refs[-3:]
    step = pl.program_id(0)
    for i in range(count):

        @pl.when(step == i)
        def _():
            piece = pieces[i]
            gate_ref[0] = piece[:WIDTH].astype(f32)
            up_ref[0] = piece[WIDTH : 2 * WIDTH].astype(f32)
            for m in range(WIDTH // HEAD_DIM):
                at = 2 * WIDTH + m * BLOCK
                down_ref[0, :, m * HEAD_DIM : (m + 1) * HEAD_DIM] = piece[at : at + BLOCK].astype(
                    f32
                )


def unpack_experts(ctx_at, steps, pieces, filled=()):
    count = len(steps)

    def expert(s, at):
        return (at[0] >> 2) ^ of_step([side for _, side in steps], s)

    def units(s, at):
        return (at[0] & 3) ^ of_step([r for r, _ in steps], s)

    cols = pl.BlockSpec((1, WIDTH, HEAD_DIM), lambda s, at: (expert(s, at), 0, units(s, at)))
    rows = pl.BlockSpec((1, BLOCK, WIDTH), lambda s, at: (expert(s, at), units(s, at), 0))
    anywhere = pl.BlockSpec(memory_space=pl.ANY)
    return pl.pallas_call(
        lambda *refs: unpack_kernel(count, *refs),
        grid_spec=pltpu.PrefetchScalarGridSpec(
            num_scalar_prefetch=1,
            grid=(count,),
            in_specs=[whole((PIECE, HEAD_DIM))] * count + [anywhere] * len(filled),
            out_specs=[cols, cols, rows],
        ),
        out_shape=[
            jax.ShapeDtypeStruct((LOCAL_E, WIDTH, FF_E), f32),
            jax.ShapeDtypeStruct((LOCAL_E, WIDTH, FF_E), f32),
            jax.ShapeDtypeStruct((LOCAL_E, FF_E, WIDTH), f32),
        ],
        input_output_aliases={1 + count + i: i for i in range(len(filled))},
        cost_estimate=cost(2 * count),
        compiler_params=params(48),
        name="unpack_experts",
    )(ctx_at, *pieces, *filled)


def relay_kernel(
    p0, p1, p3, p6, relay_a, relay_b, got_10, got_31, add_a, add_b, part_0, part_1
):
    add_a[...] = (p6[...].astype(f32) + relay_a[...].astype(f32)).astype(bf16)
    add_b[...] = (p3[...].astype(f32) + relay_b[...].astype(f32)).astype(bf16)
    part_0[...] = p0[...].astype(f32) + got_10[...].astype(f32)
    part_1[...] = p1[...].astype(f32) + got_31[...].astype(f32)


def side_kernel(part_0, part_1, got_11, got_30, own, side):
    own[...] = part_0[...] + got_30[...].astype(f32)
    side[...] = (part_1[...] + got_11[...].astype(f32)).astype(bf16)


def piece_sums(kernel, kinds, *pieces):
    specs, arrays = [], []
    for piece in pieces:
        array, second = piece if isinstance(piece, tuple) else (piece, 0)
        specs.append(pl.BlockSpec((PIECE // 4, HEAD_DIM), lambda i, at=4 * second: (i + at, 0)))
        arrays.append(array)
    return pl.pallas_call(
        kernel,
        grid=(4,),
        in_specs=specs,
        out_specs=[pl.BlockSpec((PIECE // 4, HEAD_DIM), lambda i: (i, 0))] * len(kinds),
        out_shape=[jax.ShapeDtypeStruct((PIECE, HEAD_DIM), kind) for kind in kinds],
        cost_estimate=cost(1),
        compiler_params=params(32),
        name="piece_sums",
    )(*arrays)


same_core = [[2 * i + c for i in range(8)] for c in range(2)]
core_swap = [(i, i ^ 1) for i in range(N_EXP)]
y_groups = [[0, 1, 2, 3], [4, 5, 6, 7]]
z_swap = [(i, i ^ 4) for i in range(N_CTX)]


def swap_all(rows, axis, groups=None):
    return lax.all_to_all(
        rows, axis, split_axis=0, concat_axis=0, tiled=True, axis_index_groups=groups
    )


def after(value, *others):
    return lax.optimization_barrier((value,) + others)[0]


def add_low(a, b):
    return (a.astype(f32) + b.astype(f32)).astype(bf16)


def on_device(
    tokens,
    routes,
    route_gates,
    norm_attn,
    norm_ffn,
    query_weight,
    key_weight,
    value_weight,
    out_weight,
    shared_gate,
    shared_up,
    shared_down,
    expert_gate,
    expert_up,
    expert_down,
    cotangent,
):
    exp_at = lax.axis_index("exp").astype(jnp.int32)
    ctx_at = lax.axis_index("ctx").astype(jnp.int32)
    exp_s, ctx_s = exp_at.reshape(1), ctx_at.reshape(1)

    z_at = ctx_at // 4

    w_cat = jnp.concatenate([query_weight, out_weight, key_weight, value_weight], axis=1)
    w_all = lax.all_gather(w_cat, "exp", axis=0, tiled=True)
    gates_high = route_gates[0].astype(bf16)
    gates_low = (route_gates[0] - gates_high.astype(f32)).astype(bf16)
    pad = jnp.zeros((BLOCK, META - 3 * TOPK), bf16)
    up_meta = jnp.concatenate(
        [cotangent[0], routes[0].astype(bf16), gates_high, gates_low, pad], axis=1
    )
    up_all = lax.all_gather(after(up_meta, w_cat), "exp", axis=0, tiled=True)
    gains = after(jnp.concatenate([norm_attn, norm_ffn]), w_cat)
    gains = swap_all(jnp.broadcast_to(gains, (N_EXP, gains.shape[0])), "exp")
    gain_attn = gains[:, :96].reshape(1, WIDTH).astype(f32)
    gain_ffn = gains[:, 96:].reshape(1, WIDTH).astype(f32)

    def of_sequence(rows):
        other = lax.ppermute(rows, "ctx", z_swap)
        pair = jnp.where(
            z_at == 0,
            jnp.concatenate([rows, other], axis=0),
            jnp.concatenate([other, rows], axis=0),
        )
        got = swap_all(jnp.broadcast_to(pair, (4, 2, BLOCK, WIDTH)), "ctx", y_groups)
        return got.reshape(N_CTX, BLOCK, WIDTH)

    tokens_seq = of_sequence(after(tokens, w_cat))
    shared_cols = jnp.concatenate(
        [shared_gate.reshape(96, N_EXP, SHARED), shared_up.reshape(96, N_EXP, SHARED)], axis=2
    ).transpose(1, 0, 2)
    w_shared = swap_all(shared_cols, "exp").reshape(WIDTH, 2 * SHARED)
    shared_two = jnp.concatenate([shared_down, shared_down], axis=0)

    hidden_one = norm_rows(tokens, gain_attn)
    hidden_seq = norm_rows(tokens_seq, gain_attn)
    hidden_seq = after(hidden_seq, w_shared)
    queries, kv_all = project(hidden_one, hidden_seq, w_all)
    attended, att_f, logs = attend(ctx_s, queries, kv_all)
    middle, hidden_two = middle_norm(attended, w_all, tokens[0], gain_ffn)

    hidden_all = lax.all_gather(hidden_two, "exp", axis=0, tiled=True)
    hidden_all = hidden_all.reshape(HALF, 2, BLOCK, WIDTH)
    att_seq = of_sequence(attended[None])
    place, grad_eo, grad_eh, grad_sh, slot_gate = place_rows(
        exp_s,
        after(up_all, hidden_two).reshape(HALF, 2, BLOCK, WIDTH + META),
        expert_down,
        shared_two,
    )
    part, arrived, act, grad_gu, shared_act, shared_grad = expert_back(
        exp_s, after(hidden_all, att_seq), place, grad_eh, grad_sh, expert_gate, expert_up, w_shared
    )
    summed = add_low(part[1], lax.ppermute(part[0], "exp", core_swap))
    grad_two = swap_all(summed, "exp", same_core)

    rows_e = 2 * ROWS
    operands = (
        after(arrived, summed).reshape(LOCAL_E, rows_e, WIDTH),
        grad_eo.reshape(LOCAL_E, rows_e, WIDTH),
        act.reshape(LOCAL_E, rows_e, FF_E),
        grad_gu.reshape(LOCAL_E, rows_e, 2 * FF_E),
    )
    for_1, for_3 = expert_weights(ctx_s, ((2, 0), (1, 0), (2, 1), (3, 1)), True, *operands)
    operands = (after(operands[0], for_1),) + operands[1:]
    p0, p6, p1, p3 = expert_weights(ctx_s, ((0, 0), (3, 0), (0, 1), (1, 1)), False, *operands)

    def to(rows, k):
        return lax.ppermute(rows, "ctx", [(i, i ^ k) for i in range(N_CTX)])

    from_1, from_3 = to(for_1, 1), to(for_3, 3)
    shared_grad_late = after(shared_grad, p0).reshape(N_EXP * BLOCK, META)
    grad_scols = dg(hidden_all.reshape(N_EXP * BLOCK, WIDTH), shared_grad_late, TN).astype(bf16)
    act_late = after(shared_act, p0).reshape(N_EXP * BLOCK, META)
    grad_sdown = dg(act_late, up_all, TN)[:SHARED, :WIDTH].astype(bf16)
    extra = jnp.concatenate(
        [
            jnp.pad(
                grad_scols.reshape(N_EXP, N_CTX, 12, META).transpose(1, 0, 2, 3),
                ((0, 0), (0, 0), (0, 4), (0, 0)),
            ).reshape(N_CTX, 16 * N_EXP, META),
            grad_sdown.reshape(N_CTX, 8, HEADS, 128).transpose(0, 2, 1, 3).reshape(N_CTX, 96, 128),
        ],
        axis=1,
    )

    grad_two = after(grad_two, p0, extra)
    grad_middle, grad_attn, grad_heads, gain_rows = middle_back(
        grad_two, middle, cotangent[0], gain_ffn, w_all
    )
    grad_query, near, far = attend_back(
        ctx_s, queries, grad_heads, att_f, logs, kv_all, grad_attn, extra, gain_rows
    )
    far = lax.ppermute(far, "ctx", z_swap)
    from_1, from_3 = after((from_1, from_3), near)
    add_a, add_b, part_0, part_1 = piece_sums(
        relay_kernel,
        (bf16, bf16, f32, f32),
        p0,
        p1,
        p3,
        p6,
        (from_1, 0),
        (from_3, 0),
        (from_1, 1),
        (from_3, 1),
    )
    got_11, got_30 = to(add_b, 1), to(add_a, 3)

    got_11, got_30 = after((got_11, got_30), far)
    own_part, side = piece_sums(side_kernel, (f32, bf16), part_0, part_1, got_11, got_30)
    across = to(side, 4)

    shares = merge_shares(ctx_s, near, after(far, side))
    got = swap_all(shares, "ctx", y_groups)
    own = (own_part + after(across, shares).astype(f32)).astype(bf16)
    at_1, at_3, at_z = to(own, 1), to(own, 3), to(own, 4)

    out_part = expert_output(
        exp_s, after(act, side), slot_gate, place, shared_act, expert_down, shared_two
    )
    out_sums = spread_sums(
        exp_s,
        out_part,
        lax.ppermute(out_part[0, :4], "exp", core_swap),
        lax.ppermute(out_part[0, 4:], "exp", core_swap),
    )
    columns, grad_kv, grad_down = column_grads(got, after(hidden_seq, own), att_seq)
    grad_kv = swap_all(grad_kv, "ctx")
    columns = after(columns, grad_kv, at_1, at_3, out_sums[0])
    owned = swap_all(columns, "exp")
    out_rows = out_sums[0].astype(f32)
    for k in range(1, 4):
        moved = lax.ppermute(out_sums[k], "exp", [(i, i ^ (4 * k)) for i in range(N_EXP)])
        out_rows = out_rows + moved.astype(f32)
    out_across = lax.ppermute(
        out_rows[1].astype(bf16), "exp", [(i, i ^ 2) for i in range(N_EXP)]
    )
    input_grad = input_back(grad_query, grad_kv, w_all, tokens[0], gain_attn, grad_middle)
    owned, gain_sum = owned_sums(owned, grad_down)
    owned, at_z1, at_z3 = lax.optimization_barrier(
        (after(owned, out_rows, input_grad), to(at_z, 1), to(at_z, 3))
    )
    at_2, at_z2 = to(at_3, 1), to(at_z1, 3)
    mixed = (middle + out_rows[0] + out_across.astype(f32)).astype(bf16)[None]
    experts = unpack_experts(
        ctx_s, ((0, 0), (1, 0), (3, 0), (0, 1)), (after(own, owned), at_1, at_3, at_z)
    )
    owned = swap_all(jnp.broadcast_to(owned, (N_CTX, OWNED_ROWS, HEAD_DIM)), "ctx")
    experts = unpack_experts(
        ctx_s, ((2, 0), (1, 1), (3, 1), (2, 1)), (at_2, at_z1, at_z3, at_z2), experts
    )
    gain_attn_sum, *dense = finish(
        after(owned, experts[0], mixed),
        norm_attn.astype(f32).reshape(96, 1),
        query_weight,
        key_weight,
        value_weight,
    )
    return (
        mixed,
        input_grad[None],
        gain_attn_sum[:, 0],
        gain_sum[12, :96],
        *dense,
        *experts,
    )


def solution(mesh):
    token_spec = P("exp", "ctx", None)
    rows = P("exp", None)
    expert = P("exp", None, None)
    placed = (token_spec,) * 3 + (P("exp"),) * 2 + (rows,) * 7 + (expert,) * 3 + (token_spec,)
    return jax.shard_map(
        on_device,
        mesh=mesh,
        in_specs=placed,
        out_specs=(token_spec,) * 2 + (P("exp"),) * 2 + (rows,) * 7 + (expert,) * 3,
        check_vma=False,
    )
```

```python
import jax
import jax.numpy as jnp
from jax import lax
from jax.sharding import PartitionSpec as P
from jax.experimental import pallas as pl
from jax.experimental.pallas import tpu as pltpu

HEADS = 12
KV_HEADS = 4
HEAD_DIM = 128
TOPK = 6
GROUP = 3
BLOCK = 128
WIDTH = 1536
KV_WIDTH = KV_HEADS * HEAD_DIM
CAP = 48
N_EXP = 16
N_CTX = 8
LOCAL_E = 2
FF_E = 512
SHARED = 64
META = 128
HALF = 8
ROWS = HALF * CAP

epsilon = 1e-05
masked_score = -1e30
f32 = jnp.float32
bf16 = jnp.bfloat16
log2_e = 1.4426950408889634
score_scale = HEAD_DIM ** (-0.5) * log2_e

NN = (((1,), (0,)), ((), ()))
NT = (((1,), (1,)), ((), ()))
TN = (((0,), (0,)), ((), ()))


def dg(a, b, dims):
    return lax.dot_general(a, b, dims, preferred_element_type=f32)


def params(mib):
    return pltpu.CompilerParams(vmem_limit_bytes=mib * 1024 * 1024)


def cost(us):
    return pl.CostEstimate(flops=0, bytes_accessed=int(us * 3690000), transcendentals=0)


def whole(shape):
    return pl.BlockSpec(shape, lambda *_: (0,) * len(shape), pipeline_mode=pl.Buffered(1))


def sigmoid(v):
    return 1.0 / (1.0 + jnp.exp(-v))


def allowed_scores(ctx_at):
    rows = lax.broadcasted_iota(jnp.int32, (GROUP * BLOCK, N_CTX * BLOCK), 0) % BLOCK
    cols = lax.broadcasted_iota(jnp.int32, (GROUP * BLOCK, N_CTX * BLOCK), 1)
    return rows + ctx_at * BLOCK >= cols


def stack_heads(block):
    return jnp.concatenate([block[:, j * HEAD_DIM : (j + 1) * HEAD_DIM] for j in range(GROUP)], axis=0)


def unstack_heads(rows):
    return jnp.concatenate([rows[j * BLOCK : (j + 1) * BLOCK] for j in range(GROUP)], axis=1)


def attend_kernel(ctx_ref, q_ref, k_ref, v_ref, att_ref, attf_ref, log_ref):
    q = stack_heads(q_ref[...])
    keys = k_ref[...].reshape(N_CTX * BLOCK, HEAD_DIM)
    values = v_ref[...].reshape(N_CTX * BLOCK, HEAD_DIM)
    scores = jnp.where(allowed_scores(ctx_ref[0]), dg(q, keys, NT) * score_scale, masked_score)
    top = jnp.max(scores, axis=-1, keepdims=True)
    weights = jnp.exp2(scores - top)
    total = jnp.sum(weights, axis=-1, keepdims=True)
    out = dg(weights.astype(bf16), values, NN) * (1.0 / total)
    out = unstack_heads(out)
    attf_ref[...] = out
    att_ref[...] = out.astype(bf16)
    log_ref[...] = jnp.broadcast_to(top + jnp.log2(total), (GROUP * BLOCK, HEAD_DIM))


def kv_specs():
    return [
        pl.BlockSpec((N_CTX, BLOCK, HEAD_DIM), lambda g: (0, 0, g)),
        pl.BlockSpec((N_CTX, BLOCK, HEAD_DIM), lambda g: (0, 0, KV_HEADS + g)),
    ]


def head_spec():
    return pl.BlockSpec((BLOCK, GROUP * HEAD_DIM), lambda g: (0, g))


def attend(ctx_at, qkv, kv_all):
    return pl.pallas_call(
        attend_kernel,
        grid=(KV_HEADS,),
        in_specs=[pl.BlockSpec(memory_space=pltpu.SMEM), head_spec()] + kv_specs(),
        out_specs=[
            head_spec(),
            head_spec(),
            pl.BlockSpec((GROUP * BLOCK, HEAD_DIM), lambda g: (g, 0)),
        ],
        out_shape=[
            jax.ShapeDtypeStruct((BLOCK, WIDTH), bf16),
            jax.ShapeDtypeStruct((BLOCK, WIDTH), f32),
            jax.ShapeDtypeStruct((HEADS * BLOCK, HEAD_DIM), f32),
        ],
        cost_estimate=cost(6),
        compiler_params=params(48),
        name="attend",
    )(ctx_at, qkv, kv_all, kv_all)


SEQ = N_CTX * BLOCK
AT_QUERY, AT_MIXED, AT_OUT = SEQ, SEQ + BLOCK, SEQ + 2 * BLOCK
AT_SHARED = SEQ + 3 * BLOCK
AT_DOWN = AT_SHARED + 16 * N_EXP
AT_GAIN = AT_DOWN + 96
SENT_ROWS = AT_GAIN + 16


def halves(a, b, lane):
    low = jnp.where(lane < 64, a, pltpu.roll(b, 64, 1))
    high = jnp.where(lane < 64, pltpu.roll(a, 64, 1), b)
    return low, high


def attend_back_kernel(
    ctx_ref,
    q_ref,
    ga_ref,
    attf_ref,
    log_ref,
    k_ref,
    v_ref,
    all_ga_ref,
    extra_ref,
    gain_ref,
    dq_ref,
    near_ref,
    far_ref,
    kept_ref,
):
    group = pl.program_id(0)
    z_at = ctx_ref[0] // 4

    def send(dest, z, start, stop, rows):
        @pl.when(z_at == z)
        def _():
            near_ref[dest, start:stop] = rows

        @pl.when(z_at != z)
        def _():
            far_ref[dest, start:stop] = rows

    q = stack_heads(q_ref[...])
    grad = stack_heads(ga_ref[...])
    delta = jnp.sum(grad.astype(f32) * stack_heads(attf_ref[...]), axis=-1, keepdims=True)
    keys = k_ref[...].reshape(SEQ, HEAD_DIM)
    values = v_ref[...].reshape(SEQ, HEAD_DIM)
    scores = jnp.where(allowed_scores(ctx_ref[0]), dg(q, keys, NT) * score_scale, masked_score)
    weights = jnp.exp2(scores - log_ref[:, :1])
    grad_weights = dg(grad, values, NT)
    grad_raw = (weights * (grad_weights - delta)).astype(bf16)
    scale = HEAD_DIM ** (-0.5)
    dq = unstack_heads(dg(grad_raw, keys, NN) * scale)
    dq_ref[...] = dq.astype(bf16)
    kept_ref[group] = dq
    grad_k = dg(grad_raw, q, TN) * scale
    grad_v = dg(weights.astype(bf16), grad, TN)
    low, high = halves(grad_k, grad_v, lax.broadcasted_iota(jnp.int32, (SEQ, HEAD_DIM), 1))
    low, high = low.astype(bf16), high.astype(bf16)
    send(2 * (group % 2), group // 2, 0, SEQ, low)
    send(2 * (group % 2) + 1, group // 2, 0, SEQ, high)

    @pl.when(group == KV_HEADS - 1)
    def _():
        lane = lax.broadcasted_iota(jnp.int32, (BLOCK, HEAD_DIM), 1)

        def dq_tile(m):
            return kept_ref[m // GROUP, :, HEAD_DIM * (m % GROUP) : HEAD_DIM * (m % GROUP + 1)]

        def ga_tile(m):
            return all_ga_ref[:, HEAD_DIM * m : HEAD_DIM * (m + 1)].astype(f32)

        mixed = []
        for m in range(KV_HEADS):
            mixed += halves(dq_tile(N_CTX + m), ga_tile(N_CTX + m), lane)
        gains = gain_ref[...].astype(bf16)
        for c in range(N_CTX):
            tiles = [dq_tile(c).astype(bf16), mixed[c].astype(bf16), ga_tile(c).astype(bf16)]
            rows = jnp.concatenate(tiles + [extra_ref[c], gains], axis=0)
            send(c % 4, c // 4, AT_QUERY, SENT_ROWS, rows)


def attend_back(ctx_at, qkv, grad_att, att_f, logs, kv_all, grad_attn, extra, gain_rows):
    return pl.pallas_call(
        attend_back_kernel,
        grid=(KV_HEADS,),
        in_specs=[
            pl.BlockSpec(memory_space=pltpu.SMEM),
            head_spec(),
            head_spec(),
            head_spec(),
            pl.BlockSpec((GROUP * BLOCK, HEAD_DIM), lambda g: (g, 0)),
        ]
        + kv_specs()
        + [
            whole((BLOCK, WIDTH)),
            whole((N_CTX, AT_GAIN - AT_SHARED, HEAD_DIM)),
            whole((16, HEAD_DIM)),
        ],
        out_specs=[head_spec()] + [whole((4, SENT_ROWS, HEAD_DIM))] * 2,
        out_shape=[
            jax.ShapeDtypeStruct((BLOCK, WIDTH), bf16),
            jax.ShapeDtypeStruct((4, SENT_ROWS, HEAD_DIM), bf16),
            jax.ShapeDtypeStruct((4, SENT_ROWS, HEAD_DIM), bf16),
        ],
        scratch_shapes=[pltpu.VMEM((KV_HEADS, BLOCK, GROUP * HEAD_DIM), f32)],
        cost_estimate=cost(2),
        compiler_params=params(48),
        name="attend_back",
    )(ctx_at, qkv, grad_att, att_f, logs, kv_all, kv_all, grad_attn, extra, gain_rows)


def middle_kernel(att_ref, w_ref, x_ref, gain_ref, middle_ref, hidden_ref):
    middle = x_ref[...].astype(f32) + dg(att_ref[...], w_ref[...], NN)
    inv = lax.rsqrt(jnp.mean(middle * middle, axis=-1, keepdims=True) + epsilon)
    middle_ref[...] = middle
    hidden_ref[...] = (middle * inv * gain_ref[...]).astype(bf16)


def w_cols(width, at):
    return pl.BlockSpec((WIDTH, width), lambda *_: (0, at), pipeline_mode=pl.Buffered(1))


def middle_norm(attended, w_all, tokens, gain):
    return pl.pallas_call(
        middle_kernel,
        grid=(1,),
        in_specs=[
            whole((BLOCK, WIDTH)),
            w_cols(WIDTH, 1),
            whole((BLOCK, WIDTH)),
            whole((1, WIDTH)),
        ],
        out_specs=[whole((BLOCK, WIDTH)), whole((BLOCK, WIDTH))],
        out_shape=[
            jax.ShapeDtypeStruct((BLOCK, WIDTH), f32),
            jax.ShapeDtypeStruct((BLOCK, WIDTH), bf16),
        ],
        cost_estimate=cost(2),
        compiler_params=params(32),
        name="middle_norm",
    )(attended, w_all, tokens, gain)


def norm_back(grad_normed, normed, inv_root):
    return inv_root * (
        grad_normed - normed * jnp.mean(grad_normed * normed, axis=-1, keepdims=True)
    )


def middle_back_kernel(
    pieces_ref, middle_ref, up_ref, gain_ref, w_ref, gm_ref, ga_ref, gh_ref, gg_ref
):
    grad_two = pieces_ref[0].astype(f32)
    for i in range(1, HALF):
        grad_two = grad_two + pieces_ref[i].astype(f32)
    middle = middle_ref[...]
    inv = lax.rsqrt(jnp.mean(middle * middle, axis=-1, keepdims=True) + epsilon)
    normed = middle * inv
    gains = jnp.sum(grad_two * normed, axis=0, keepdims=True)
    gg_ref[...] = jnp.zeros((16, HEAD_DIM), f32)
    for m in range(HEADS):
        gg_ref[m : m + 1] = gains[:, HEAD_DIM * m : HEAD_DIM * (m + 1)]
    grad_middle = up_ref[...].astype(f32) + norm_back(grad_two * gain_ref[...], normed, inv)
    gm_ref[...] = grad_middle
    grad_attn = grad_middle.astype(bf16)
    ga_ref[...] = grad_attn
    gh_ref[...] = dg(grad_attn, w_ref[...], NT).astype(bf16)


def middle_back(pieces, middle, upstream, gain, w_all):
    return pl.pallas_call(
        middle_back_kernel,
        grid=(1,),
        in_specs=[
            whole((HALF, BLOCK, WIDTH)),
            whole((BLOCK, WIDTH)),
            whole((BLOCK, WIDTH)),
            whole((1, WIDTH)),
            w_cols(WIDTH, 1),
        ],
        out_specs=[whole((BLOCK, WIDTH))] * 3 + [whole((16, HEAD_DIM))],
        out_shape=[
            jax.ShapeDtypeStruct((BLOCK, WIDTH), f32),
            jax.ShapeDtypeStruct((BLOCK, WIDTH), bf16),
            jax.ShapeDtypeStruct((BLOCK, WIDTH), bf16),
            jax.ShapeDtypeStruct((16, HEAD_DIM), f32),
        ],
        cost_estimate=cost(1),
        compiler_params=params(48),
        name="middle_back",
    )(pieces, middle, upstream, gain, w_all)


def place_kernel(
    at_ref, up_ref, down_ref, sdown_ref, place_ref, geo_ref, geh_ref, gsh_ref, gate_ref
):
    lane = lax.broadcasted_iota(jnp.int32, (BLOCK, META), 1)
    row = lax.broadcasted_iota(jnp.int32, (BLOCK, META), 0)
    before = (row > lane).astype(bf16)
    slot = (lane % 64).astype(f32)
    first_id = (at_ref[0] * LOCAL_E).astype(f32)
    row_id = first_id + (row >= 64).astype(f32)

    for chip in range(HALF):
        meta = up_ref[chip, 0, :, WIDTH:].astype(f32)
        named = lane < TOPK
        zero = jnp.zeros((BLOCK, META), f32)
        hit0 = jnp.where(named & (meta == first_id), 1.0, zero)
        hit1 = jnp.where(named & (meta == first_id + 1.0), 1.0, zero)
        mask = jnp.where(
            lane < 64,
            jnp.sum(hit0, axis=1, keepdims=True),
            jnp.sum(hit1, axis=1, keepdims=True),
        )
        rank = dg(before, mask.astype(bf16), NN)
        place = jnp.where((mask > 0.5) & (rank == slot), 1.0, zero).astype(bf16)
        place_ref[chip, 0] = place
        rows = dg(place, up_ref[chip, 0], TN)
        slot_meta = rows[:, WIDTH:]
        gates = pltpu.roll(slot_meta, META - TOPK, 1) + pltpu.roll(
            slot_meta, META - 2 * TOPK, 1
        )
        gate = jnp.sum(
            jnp.where(named & (slot_meta == row_id), gates, zero), axis=1, keepdims=True
        )
        geo = (gate * rows[:, :WIDTH]).astype(bf16)
        wide_gate = jnp.broadcast_to(gate, (BLOCK, META))
        at = chip * CAP
        for e in range(LOCAL_E):
            geo_ref[e, 0, at : at + CAP] = geo[64 * e : 64 * e + CAP]
            gate_ref[e, 0, at : at + CAP] = wide_gate[64 * e : 64 * e + CAP]
        gsh_ref[chip, 0] = dg(up_ref[chip, 0, :, :WIDTH], sdown_ref[...], NT)
    for e in range(LOCAL_E):
        geh_ref[e, 0] = dg(geo_ref[e, 0], down_ref[e], NT)


def by_core(cols):
    return pl.BlockSpec(
        (HALF, 1, BLOCK, cols),
        lambda s, at: (0, jnp.where(s == 0, 1 - at[0] % 2, at[0] % 2), 0, 0),
    )


def by_step(cols):
    return pl.BlockSpec((LOCAL_E, 1, ROWS, cols), lambda s, at: (0, s, 0, 0))


def place_rows(exp_at, up_all, expert_down, shared_two):
    return pl.pallas_call(
        place_kernel,
        grid_spec=pltpu.PrefetchScalarGridSpec(
            num_scalar_prefetch=1,
            grid=(2,),
            in_specs=[
                by_core(WIDTH + META),
                whole((LOCAL_E, FF_E, WIDTH)),
                whole((2 * SHARED, WIDTH)),
            ],
            out_specs=[by_core(META), by_step(WIDTH), by_step(FF_E), by_core(META), by_step(META)],
        ),
        out_shape=[
            jax.ShapeDtypeStruct((HALF, 2, BLOCK, META), bf16),
            jax.ShapeDtypeStruct((LOCAL_E, 2, ROWS, WIDTH), bf16),
            jax.ShapeDtypeStruct((LOCAL_E, 2, ROWS, FF_E), f32),
            jax.ShapeDtypeStruct((HALF, 2, BLOCK, META), f32),
            jax.ShapeDtypeStruct((LOCAL_E, 2, ROWS, META), f32),
        ],
        cost_estimate=cost(14),
        compiler_params=params(56),
        name="place_rows",
    )(exp_at, up_all, expert_down, shared_two)


def expert_kernel(
    at_ref,
    hid_ref,
    place_ref,
    geh_ref,
    gsh_ref,
    wg_ref,
    wu_ref,
    ws_ref,
    part_ref,
    x_ref,
    act_ref,
    dgu_ref,
    sact_ref,
    sgrad_ref,
):
    for chip in range(HALF):
        rows = dg(place_ref[chip, 0], hid_ref[chip, 0], TN).astype(bf16)
        at = chip * CAP
        for e in range(LOCAL_E):
            x_ref[e, 0, at : at + CAP] = rows[64 * e : 64 * e + CAP]
    pairs = []
    for e in range(LOCAL_E):
        pre_gate = dg(x_ref[e, 0], wg_ref[e], NN)
        pre_up = dg(x_ref[e, 0], wu_ref[e], NN)
        sig = sigmoid(pre_gate)
        act = pre_gate * sig
        act_ref[e, 0] = (act * pre_up).astype(bf16)
        geh = geh_ref[e, 0]
        d_gate = (geh * pre_up * (sig * (1.0 + pre_gate * (1.0 - sig)))).astype(bf16)
        d_up = (geh * act).astype(bf16)
        dgu_ref[e, 0, :, :FF_E] = d_gate
        dgu_ref[e, 0, :, FF_E:] = d_up
        pairs.append((dg(d_gate, wg_ref[e], NT) + dg(d_up, wu_ref[e], NT)).astype(bf16))
    lane = lax.broadcasted_iota(jnp.int32, (BLOCK, 2 * SHARED), 1) < SHARED
    gap = jnp.zeros((64 - CAP, WIDTH), bf16)
    for chip in range(HALF):
        pre = dg(hid_ref[chip, 0], ws_ref[...], NN)
        turned = pltpu.roll(pre, SHARED, 1)
        gate, up = jnp.where(lane, pre, turned), jnp.where(lane, turned, pre)
        sig = sigmoid(gate)
        act = gate * sig
        sact_ref[chip, 0] = jnp.where(lane, act * up, 0.0).astype(bf16)
        slope = sig * (1.0 + gate * (1.0 - sig))
        sgrad = (gsh_ref[chip, 0] * jnp.where(lane, up * slope, act)).astype(bf16)
        sgrad_ref[chip, 0] = sgrad
        at = chip * CAP
        stacked = jnp.concatenate([pairs[0][at : at + CAP], gap, pairs[1][at : at + CAP], gap], 0)
        part_ref[0, chip] = (
            dg(place_ref[chip, 0], stacked, NN) + dg(sgrad, ws_ref[...], NT)
        ).astype(bf16)


def expert_back(exp_at, hidden, place, geh, gsh, wg, wu, ws):
    return pl.pallas_call(
        expert_kernel,
        grid_spec=pltpu.PrefetchScalarGridSpec(
            num_scalar_prefetch=1,
            grid=(2,),
            in_specs=[
                by_core(WIDTH),
                by_core(META),
                by_step(FF_E),
                by_core(META),
                whole((LOCAL_E, WIDTH, FF_E)),
                whole((LOCAL_E, WIDTH, FF_E)),
                whole((WIDTH, 2 * SHARED)),
            ],
            out_specs=[
                pl.BlockSpec((1, HALF, BLOCK, WIDTH), lambda s, at: (s, 0, 0, 0)),
                by_step(WIDTH),
                by_step(FF_E),
                by_step(2 * FF_E),
                by_core(META),
                by_core(META),
            ],
        ),
        out_shape=[
            jax.ShapeDtypeStruct((2, HALF, BLOCK, WIDTH), bf16),
            jax.ShapeDtypeStruct((LOCAL_E, 2, ROWS, WIDTH), bf16),
            jax.ShapeDtypeStruct((LOCAL_E, 2, ROWS, FF_E), bf16),
            jax.ShapeDtypeStruct((LOCAL_E, 2, ROWS, 2 * FF_E), bf16),
            jax.ShapeDtypeStruct((HALF, 2, BLOCK, META), bf16),
            jax.ShapeDtypeStruct((HALF, 2, BLOCK, META), bf16),
        ],
        cost_estimate=cost(28),
        compiler_params=params(60),
        name="expert_back",
    )(exp_at, hidden, place, geh, gsh, wg, wu, ws)


def output_kernel(at_ref, act_ref, gate_ref, place_ref, sact_ref, wd_ref, sd_ref, part_ref):
    outs = []
    for e in range(LOCAL_E):
        out = dg(act_ref[e, 0], wd_ref[e], NN).astype(bf16).astype(f32)
        outs.append((out * gate_ref[e, 0, :, :1]).astype(bf16))
    gap = jnp.zeros((64 - CAP, WIDTH), bf16)
    for chip in range(HALF):
        at = chip * CAP
        stacked = jnp.concatenate([outs[0][at : at + CAP], gap, outs[1][at : at + CAP], gap], 0)
        part_ref[0, chip] = (
            dg(place_ref[chip, 0], stacked, NN) + dg(sact_ref[chip, 0], sd_ref[...], NN)
        ).astype(bf16)


def expert_output(exp_at, act, gate, place, sact, wd, sd):
    return pl.pallas_call(
        output_kernel,
        grid_spec=pltpu.PrefetchScalarGridSpec(
            num_scalar_prefetch=1,
            grid=(2,),
            in_specs=[
                by_step(FF_E),
                by_step(META),
                by_core(META),
                by_core(META),
                whole((LOCAL_E, FF_E, WIDTH)),
                whole((2 * SHARED, WIDTH)),
            ],
            out_specs=pl.BlockSpec((1, HALF, BLOCK, WIDTH), lambda s, at: (s, 0, 0, 0)),
        ),
        out_shape=jax.ShapeDtypeStruct((2, HALF, BLOCK, WIDTH), bf16),
        cost_estimate=cost(2),
        compiler_params=params(48),
        name="expert_output",
    )(exp_at, act, gate, place, sact, wd, sd)


SHARE = 3 * BLOCK
TO_SHARED = SEQ + 2 * SHARE
TO_DOWN = TO_SHARED + 16 * N_EXP
TO_GAIN = TO_DOWN + 96
MERGED_ROWS = TO_GAIN + 16


def merge_kernel(ctx_ref, near_ref, got_ref, out_ref):
    z_at = ctx_ref[0] // 4
    near, got = near_ref[0], got_ref[0]

    def add(a, b):
        return (a.astype(f32) + b.astype(f32)).astype(bf16)

    out_ref[0, :SEQ] = add(near[:SEQ], got[:SEQ])
    out_ref[0, TO_SHARED:] = add(near[AT_SHARED:], got[AT_SHARED:])
    mine, theirs = near[AT_QUERY:AT_SHARED], got[AT_QUERY:AT_SHARED]
    out_ref[0, SEQ : SEQ + SHARE] = jnp.where(z_at == 0, mine, theirs)
    out_ref[0, SEQ + SHARE : TO_SHARED] = jnp.where(z_at == 0, theirs, mine)


def merge_shares(ctx_at, near, got):
    spec = pl.BlockSpec((1, SENT_ROWS, HEAD_DIM), lambda i: (i, 0, 0))
    return pl.pallas_call(
        merge_kernel,
        grid=(4,),
        in_specs=[pl.BlockSpec(memory_space=pltpu.SMEM), spec, spec],
        out_specs=pl.BlockSpec((1, MERGED_ROWS, HEAD_DIM), lambda i: (i, 0, 0)),
        out_shape=jax.ShapeDtypeStruct((4, MERGED_ROWS, HEAD_DIM), bf16),
        cost_estimate=cost(3),
        compiler_params=params(32),
        name="merge_shares",
    )(ctx_at, near, got)


def columns_kernel(got_ref, hidden_ref, att_ref, sent_ref, kv_ref, down_ref):
    def summed(start, stop):
        out = got_ref[0, start:stop].astype(f32)
        for src in range(1, 4):
            out = out + got_ref[src, start:stop].astype(f32)
        return out

    grad_kv = summed(0, SEQ).astype(bf16)
    kv_ref[...] = grad_kv.reshape(N_CTX, BLOCK, HEAD_DIM)

    def rows_of(tile, order):
        at = SEQ + BLOCK * tile
        return jnp.concatenate(
            [got_ref[y, at + SHARE * z : at + SHARE * z + BLOCK] for z, y in order], axis=0
        )

    in_order = [(i // 4, i % 4) for i in range(N_CTX)]
    y_order = [(i % 2, i // 2) for i in range(N_CTX)]
    lane = lax.broadcasted_iota(jnp.int32, (SEQ, HEAD_DIM), 1)
    zero = jnp.zeros((SEQ, HEAD_DIM), bf16)
    mixed_q = jnp.where(lane < 64, rows_of(1, in_order), zero)
    mixed_o = jnp.where(lane < 64, zero, rows_of(1, y_order))
    left = jnp.concatenate([rows_of(0, in_order).T, mixed_q.T, grad_kv.T], axis=0)
    right = jnp.concatenate([mixed_o.T, rows_of(2, y_order).T], axis=0)
    by_hidden = dg(left, hidden_ref[...].reshape(SEQ, WIDTH), NN)
    by_att = dg(right, att_ref[...].reshape(SEQ, WIDTH), NN)
    tiles = [
        by_hidden[:BLOCK],
        by_hidden[BLOCK : 2 * BLOCK] + by_att[:BLOCK],
        by_att[BLOCK:],
        by_hidden[2 * BLOCK :],
    ]
    for t, tile in enumerate(tiles):
        sent_ref[:, :96, HEAD_DIM * t : HEAD_DIM * (t + 1)] = (
            tile.T.astype(bf16).reshape(N_EXP, 96, HEAD_DIM)
        )

    down_ref[...] = summed(TO_DOWN, TO_GAIN).astype(bf16)
    shared = summed(TO_SHARED, TO_DOWN)
    gains = summed(TO_GAIN, MERGED_ROWS)
    row = lax.broadcasted_iota(jnp.int32, (16, HEAD_DIM), 0)
    one_lane = lax.broadcasted_iota(jnp.int32, (1, HEAD_DIM), 1)
    for i in range(N_EXP):
        m, offset = (96 * i) // HEAD_DIM, (96 * i) % HEAD_DIM
        gain = gains[m : m + 1]
        if offset:
            shift = HEAD_DIM - offset
            gain = jnp.where(
                one_lane < shift,
                pltpu.roll(gain, shift, 1),
                pltpu.roll(gains[m + 1 : m + 2], shift, 1),
            )
        rows = jnp.where(row == 12, jnp.broadcast_to(gain, (16, HEAD_DIM)), shared[16 * i : 16 * i + 16])
        sent_ref[i, 96:, :HEAD_DIM] = rows.astype(bf16)
        sent_ref[i, 96:, HEAD_DIM:] = jnp.zeros((16, 512 - HEAD_DIM), bf16)


def column_grads(got, hidden_seq, att_seq):
    return pl.pallas_call(
        columns_kernel,
        out_shape=[
            jax.ShapeDtypeStruct((N_EXP, 112, 512), bf16),
            jax.ShapeDtypeStruct((N_CTX, BLOCK, HEAD_DIM), bf16),
            jax.ShapeDtypeStruct((96, HEAD_DIM), bf16),
        ],
        cost_estimate=cost(8),
        compiler_params=params(56),
        name="column_grads",
    )(got, hidden_seq, att_seq)


OWNED_ROWS = 4 * 96 + 16 * N_EXP + 96


def owned_kernel(got_ref, down_ref, owned_ref, gain_ref):
    total = got_ref[0, :96].astype(f32)
    gains = got_ref[0, 96:, :HEAD_DIM].astype(f32)
    for src in range(1, N_EXP):
        total = total + got_ref[src, :96].astype(f32)
        gains = gains + got_ref[src, 96:, :HEAD_DIM].astype(f32)
    gain_ref[...] = gains
    for t in range(4):
        owned_ref[96 * t : 96 * t + 96] = total[:, HEAD_DIM * t : HEAD_DIM * (t + 1)].astype(bf16)
    for src in range(N_EXP):
        at = 384 + 16 * src
        owned_ref[at : at + 16] = got_ref[src, 96:, :HEAD_DIM]
    owned_ref[384 + 16 * N_EXP :] = down_ref[...]


def owned_sums(got, down):
    return pl.pallas_call(
        owned_kernel,
        out_shape=[
            jax.ShapeDtypeStruct((OWNED_ROWS, HEAD_DIM), bf16),
            jax.ShapeDtypeStruct((16, HEAD_DIM), f32),
        ],
        cost_estimate=cost(3),
        compiler_params=params(32),
        name="owned_sums",
    )(got, down)


def finish_kernel(
    got_ref,
    gain_in_ref,
    wq_ref,
    wk_ref,
    wv_ref,
    gain_ref,
    q_ref,
    k_ref,
    v_ref,
    out_ref,
    sg_ref,
    su_ref,
    sd_ref,
):
    lane = lax.broadcasted_iota(jnp.int32, (96, HEAD_DIM), 1)

    def tile(c, t):
        return got_ref[c, 96 * t : 96 * t + 96].astype(f32)

    for c in range(N_CTX):
        at = HEAD_DIM * c
        q_ref[:, at : at + HEAD_DIM] = tile(c, 0)
        out_ref[:, at : at + HEAD_DIM] = tile(c, 2)
    for m in range(N_CTX // 2):
        at = HEAD_DIM * m
        low, high = halves(tile(2 * m, 1), tile(2 * m + 1, 1), lane)
        q_ref[:, 1024 + at : 1024 + at + HEAD_DIM] = low
        out_ref[:, 1024 + at : 1024 + at + HEAD_DIM] = high
        low, high = halves(tile(2 * m, 3), tile(2 * m + 1, 3), lane)
        k_ref[:, at : at + HEAD_DIM] = low
        v_ref[:, at : at + HEAD_DIM] = high
    gain = (
        jnp.sum(q_ref[...] * wq_ref[...].astype(f32), axis=1, keepdims=True)
        + jnp.sum(k_ref[...] * wk_ref[...].astype(f32), axis=1, keepdims=True)
        + jnp.sum(v_ref[...] * wv_ref[...].astype(f32), axis=1, keepdims=True)
    ) / gain_in_ref[...]
    gain_ref[...] = jnp.broadcast_to(gain, (96, HEAD_DIM))
    row = lax.broadcasted_iota(jnp.int32, (96, HEAD_DIM), 0)
    picks = jnp.where((lane % 16 < 12) & (row == 12 * (lane // 16) + lane % 16), 1.0, 0.0)
    picks = picks.astype(bf16)

    def shared_tile(j):
        at = 384 + 16 * j
        rows = jnp.concatenate([got_ref[c, at : at + 16] for c in range(N_CTX)], axis=0)
        return dg(picks, rows, NN)

    for m in range(N_EXP // 2):
        at = HEAD_DIM * m
        low, high = halves(shared_tile(2 * m), shared_tile(2 * m + 1), lane)
        sg_ref[:, at : at + HEAD_DIM] = low
        su_ref[:, at : at + HEAD_DIM] = high
    for c in range(N_CTX):
        rows = got_ref[c, 384 + 16 * N_EXP :].astype(f32)
        for m in range(HEADS):
            sd_ref[8 * c : 8 * c + 8, HEAD_DIM * m : HEAD_DIM * (m + 1)] = rows[8 * m : 8 * m + 8]


def finish(got, gain_column, query_weight, key_weight, value_weight):
    shapes = [(96, 128), (96, 1536), (96, 512), (96, 512), (96, 1536), (96, 1024), (96, 1024)]
    return pl.pallas_call(
        finish_kernel,
        out_shape=[jax.ShapeDtypeStruct(s, f32) for s in shapes + [(SHARED, WIDTH)]],
        cost_estimate=cost(4),
        compiler_params=params(32),
        name="finish",
    )(got, gain_column, query_weight, key_weight, value_weight)


def input_kernel(dq_ref, got_ref, wq_ref, wkv_ref, x_ref, gain_ref, gm_ref, out_ref):
    lane = lax.broadcasted_iota(jnp.int32, (BLOCK, HEAD_DIM), 1)
    lows, highs = [], []
    for m in range(KV_HEADS):
        low, high = halves(got_ref[2 * m].astype(f32), got_ref[2 * m + 1].astype(f32), lane)
        lows.append(low.astype(bf16))
        highs.append(high.astype(bf16))
    grad_kv = jnp.concatenate(lows + highs, axis=1)
    grad_one = dg(dq_ref[...], wq_ref[...], NT) + dg(grad_kv, wkv_ref[...], NT)
    inputs = x_ref[...].astype(f32)
    inv = lax.rsqrt(jnp.mean(inputs * inputs, axis=-1, keepdims=True) + epsilon)
    out_ref[...] = (gm_ref[...] + norm_back(grad_one * gain_ref[...], inputs * inv, inv)).astype(bf16)


def input_back(grad_query, grad_kv, w_all, tokens, gain, grad_middle):
    return pl.pallas_call(
        input_kernel,
        grid=(1,),
        in_specs=[
            whole((BLOCK, WIDTH)),
            whole((N_CTX, BLOCK, HEAD_DIM)),
            w_cols(WIDTH, 0),
            w_cols(2 * KV_WIDTH, 3),
            whole((BLOCK, WIDTH)),
            whole((1, WIDTH)),
            whole((BLOCK, WIDTH)),
        ],
        out_specs=whole((BLOCK, WIDTH)),
        out_shape=jax.ShapeDtypeStruct((BLOCK, WIDTH), bf16),
        cost_estimate=cost(7),
        compiler_params=params(48),
        name="input_back",
    )(grad_query, grad_kv, w_all, w_all, tokens, gain, grad_middle)


def norm_rows_kernel(x_ref, gain_ref, out_ref):
    inputs = x_ref[0].astype(f32)
    inv = lax.rsqrt(jnp.mean(inputs * inputs, axis=-1, keepdims=True) + epsilon)
    out_ref[0] = (inputs * inv * gain_ref[...]).astype(bf16)


def norm_rows(rows, gain):
    count = rows.shape[0]
    spec = pl.BlockSpec((1, BLOCK, WIDTH), lambda i: (i, 0, 0))
    turned = pl.BlockSpec((1, BLOCK, WIDTH), lambda i: ((i % 2) * 4 + i // 2, 0, 0))
    return pl.pallas_call(
        norm_rows_kernel,
        grid=(count,),
        in_specs=[spec, whole((1, WIDTH))],
        out_specs=spec if count == 1 else turned,
        out_shape=jax.ShapeDtypeStruct(rows.shape, bf16),
        cost_estimate=cost(2),
        compiler_params=params(32),
        name="norm_rows",
    )(rows, gain)


def project_kernel(own_ref, seq_ref, w_ref, q_ref, kv_ref):
    step = pl.program_id(0)

    @pl.when(step < 3)
    def _():
        q_ref[...] = dg(own_ref[0], w_ref[...], NN).astype(bf16)

    @pl.when(step >= 3)
    def _():
        rows = seq_ref[...].reshape(N_CTX * BLOCK, WIDTH)
        kv_ref[...] = dg(rows, w_ref[...], NN).astype(bf16).reshape(N_CTX, BLOCK, KV_WIDTH)


def project(own, seq, w_all):
    return pl.pallas_call(
        project_kernel,
        grid=(5,),
        in_specs=[
            whole((1, BLOCK, WIDTH)),
            whole((N_CTX, BLOCK, WIDTH)),
            pl.BlockSpec((WIDTH, KV_WIDTH), lambda i: (0, jnp.where(i < 3, i, i + 3))),
        ],
        out_specs=[
            pl.BlockSpec((BLOCK, KV_WIDTH), lambda i: (0, jnp.minimum(i, 2))),
            pl.BlockSpec((N_CTX, BLOCK, KV_WIDTH), lambda i: (0, 0, jnp.maximum(i - 3, 0))),
        ],
        out_shape=[
            jax.ShapeDtypeStruct((BLOCK, WIDTH), bf16),
            jax.ShapeDtypeStruct((N_CTX, BLOCK, 2 * KV_WIDTH), bf16),
        ],
        cost_estimate=cost(8),
        compiler_params=params(48),
        name="project",
    )(own, seq, w_all)


PIECE = 2 * WIDTH + WIDTH * BLOCK // HEAD_DIM


def spread_kernel(at_ref, own_ref, low_ref, high_ref, *outs):
    chip = (at_ref[0] >> 1) ^ pl.program_id(0)
    got = jnp.where(chip < 4, low_ref[0], high_ref[0])
    total = (own_ref[0, 0].astype(f32) + got.astype(f32)).astype(bf16)
    for k in range(HALF):

        @pl.when(pl.program_id(0) == k)
        def _():
            outs[k // 2][k % 2] = total


def spread_sums(exp_at, parts, low, high):
    half = pl.BlockSpec((1, BLOCK, WIDTH), lambda k, at: (((at[0] >> 1) ^ k) & 3, 0, 0))
    return pl.pallas_call(
        spread_kernel,
        grid_spec=pltpu.PrefetchScalarGridSpec(
            num_scalar_prefetch=1,
            grid=(HALF,),
            in_specs=[
                pl.BlockSpec((1, 1, BLOCK, WIDTH), lambda k, at: (1, (at[0] >> 1) ^ k, 0, 0)),
                half,
                half,
            ],
            out_specs=[whole((2, BLOCK, WIDTH))] * 4,
        ),
        out_shape=[jax.ShapeDtypeStruct((2, BLOCK, WIDTH), bf16)] * 4,
        cost_estimate=cost(4),
        compiler_params=params(32),
        name="spread_sums",
    )(exp_at, parts, low, high)


def of_step(values, step):
    out = jnp.int32(values[0])
    for i, value in enumerate(values[1:], 1):
        out = jnp.where(step == i, value, out)
    return out


def expert_weights_kernel(halved, at_ref, x_ref, geo_ref, act_ref, dgate_ref, dup_ref, *outs):
    step = pl.program_id(0)
    rhs = jnp.concatenate([dgate_ref[0], dup_ref[0]], axis=1)
    both = dg(x_ref[0], rhs, TN).astype(bf16)
    down = dg(act_ref[0], geo_ref[0], TN).astype(bf16)
    for i in range(4):

        @pl.when(step == i)
        def _():
            start = (i % 2) * PIECE if halved else 0
            out = outs[i // 2 if halved else i].at[pl.ds(start, PIECE)]
            out[:WIDTH] = both[:, :HEAD_DIM]
            out[WIDTH : 2 * WIDTH] = both[:, HEAD_DIM:]
            for m in range(WIDTH // HEAD_DIM):
                at = 2 * WIDTH + m * BLOCK
                out[at : at + BLOCK] = down[:, m * HEAD_DIM : (m + 1) * HEAD_DIM]


def expert_weights(ctx_at, steps, halved, arrived, grad_eo, act, grad_gu):
    rows = 2 * ROWS

    def expert(s, at):
        return (at[0] >> 2) ^ of_step([side for _, side in steps], s)

    def lanes(shift):
        return pl.BlockSpec(
            (1, rows, HEAD_DIM),
            lambda s, at: (
                expert(s, at),
                0,
                shift + ((at[0] & 3) ^ of_step([r for r, _ in steps], s)),
            ),
        )

    rows_of = pl.BlockSpec((1, rows, WIDTH), lambda s, at: (expert(s, at), 0, 0))
    count, length = (2, 2 * PIECE) if halved else (4, PIECE)
    return pl.pallas_call(
        lambda *refs: expert_weights_kernel(halved, *refs),
        grid_spec=pltpu.PrefetchScalarGridSpec(
            num_scalar_prefetch=1,
            grid=(4,),
            in_specs=[rows_of, rows_of, lanes(0), lanes(0), lanes(4)],
            out_specs=[whole((length, HEAD_DIM))] * count,
        ),
        out_shape=[jax.ShapeDtypeStruct((length, HEAD_DIM), bf16)] * count,
        cost_estimate=cost(2),
        compiler_params=params(56),
        name="expert_weights",
    )(ctx_at, arrived, grad_eo, act, grad_gu, grad_gu)


def unpack_kernel(count, at_ref, *refs):
    pieces, (gate_ref, up_ref, down_ref) = refs[:count], refs[-3:]
    step = pl.program_id(0)
    for i in range(count):

        @pl.when(step == i)
        def _():
            piece = pieces[i]
            gate_ref[0] = piece[:WIDTH].astype(f32)
            up_ref[0] = piece[WIDTH : 2 * WIDTH].astype(f32)
            for m in range(WIDTH // HEAD_DIM):
                at = 2 * WIDTH + m * BLOCK
                down_ref[0, :, m * HEAD_DIM : (m + 1) * HEAD_DIM] = piece[at : at + BLOCK].astype(
                    f32
                )


def unpack_experts(ctx_at, steps, pieces, filled=()):
    count = len(steps)

    def expert(s, at):
        return (at[0] >> 2) ^ of_step([side for _, side in steps], s)

    def units(s, at):
        return (at[0] & 3) ^ of_step([r for r, _ in steps], s)

    cols = pl.BlockSpec((1, WIDTH, HEAD_DIM), lambda s, at: (expert(s, at), 0, units(s, at)))
    rows = pl.BlockSpec((1, BLOCK, WIDTH), lambda s, at: (expert(s, at), units(s, at), 0))
    anywhere = pl.BlockSpec(memory_space=pl.ANY)
    return pl.pallas_call(
        lambda *refs: unpack_kernel(count, *refs),
        grid_spec=pltpu.PrefetchScalarGridSpec(
            num_scalar_prefetch=1,
            grid=(count,),
            in_specs=[whole((PIECE, HEAD_DIM))] * count + [anywhere] * len(filled),
            out_specs=[cols, cols, rows],
        ),
        out_shape=[
            jax.ShapeDtypeStruct((LOCAL_E, WIDTH, FF_E), f32),
            jax.ShapeDtypeStruct((LOCAL_E, WIDTH, FF_E), f32),
            jax.ShapeDtypeStruct((LOCAL_E, FF_E, WIDTH), f32),
        ],
        input_output_aliases={1 + count + i: i for i in range(len(filled))},
        cost_estimate=cost(2 * count),
        compiler_params=params(48),
        name="unpack_experts",
    )(ctx_at, *pieces, *filled)


def relay_kernel(
    p0, p1, p3, p6, relay_a, relay_b, got_10, got_31, add_a, add_b, part_0, part_1
):
    add_a[...] = (p6[...].astype(f32) + relay_a[...].astype(f32)).astype(bf16)
    add_b[...] = (p3[...].astype(f32) + relay_b[...].astype(f32)).astype(bf16)
    part_0[...] = p0[...].astype(f32) + got_10[...].astype(f32)
    part_1[...] = p1[...].astype(f32) + got_31[...].astype(f32)


def side_kernel(part_0, part_1, got_11, got_30, own, side):
    own[...] = part_0[...] + got_30[...].astype(f32)
    side[...] = (part_1[...] + got_11[...].astype(f32)).astype(bf16)


def piece_sums(kernel, kinds, *pieces):
    specs, arrays = [], []
    for piece in pieces:
        array, second = piece if isinstance(piece, tuple) else (piece, 0)
        specs.append(pl.BlockSpec((PIECE // 4, HEAD_DIM), lambda i, at=4 * second: (i + at, 0)))
        arrays.append(array)
    return pl.pallas_call(
        kernel,
        grid=(4,),
        in_specs=specs,
        out_specs=[pl.BlockSpec((PIECE // 4, HEAD_DIM), lambda i: (i, 0))] * len(kinds),
        out_shape=[jax.ShapeDtypeStruct((PIECE, HEAD_DIM), kind) for kind in kinds],
        cost_estimate=cost(1),
        compiler_params=params(32),
        name="piece_sums",
    )(*arrays)


same_core = [[2 * i + c for i in range(8)] for c in range(2)]
core_swap = [(i, i ^ 1) for i in range(N_EXP)]
y_groups = [[0, 1, 2, 3], [4, 5, 6, 7]]
z_swap = [(i, i ^ 4) for i in range(N_CTX)]


def swap_all(rows, axis, groups=None):
    return lax.all_to_all(
        rows, axis, split_axis=0, concat_axis=0, tiled=True, axis_index_groups=groups
    )


def after(value, *others):
    return lax.optimization_barrier((value,) + others)[0]


def add_low(a, b):
    return (a.astype(f32) + b.astype(f32)).astype(bf16)


def on_device(
    tokens,
    routes,
    route_gates,
    norm_attn,
    norm_ffn,
    query_weight,
    key_weight,
    value_weight,
    out_weight,
    shared_gate,
    shared_up,
    shared_down,
    expert_gate,
    expert_up,
    expert_down,
    cotangent,
):
    exp_at = lax.axis_index("exp").astype(jnp.int32)
    ctx_at = lax.axis_index("ctx").astype(jnp.int32)
    exp_s, ctx_s = exp_at.reshape(1), ctx_at.reshape(1)

    z_at = ctx_at // 4

    w_cat = jnp.concatenate([query_weight, out_weight, key_weight, value_weight], axis=1)
    w_all = lax.all_gather(w_cat, "exp", axis=0, tiled=True)
    gates_high = route_gates[0].astype(bf16)
    gates_low = (route_gates[0] - gates_high.astype(f32)).astype(bf16)
    pad = jnp.zeros((BLOCK, META - 3 * TOPK), bf16)
    up_meta = jnp.concatenate(
        [cotangent[0], routes[0].astype(bf16), gates_high, gates_low, pad], axis=1
    )
    up_all = lax.all_gather(after(up_meta, w_cat), "exp", axis=0, tiled=True)
    gains = after(jnp.concatenate([norm_attn, norm_ffn]), w_cat)
    gains = swap_all(jnp.broadcast_to(gains, (N_EXP, gains.shape[0])), "exp")
    gain_attn = gains[:, :96].reshape(1, WIDTH).astype(f32)
    gain_ffn = gains[:, 96:].reshape(1, WIDTH).astype(f32)

    def of_sequence(rows):
        other = lax.ppermute(rows, "ctx", z_swap)
        pair = jnp.where(
            z_at == 0,
            jnp.concatenate([rows, other], axis=0),
            jnp.concatenate([other, rows], axis=0),
        )
        got = swap_all(jnp.broadcast_to(pair, (4, 2, BLOCK, WIDTH)), "ctx", y_groups)
        return got.reshape(N_CTX, BLOCK, WIDTH)

    tokens_seq = of_sequence(after(tokens, w_cat))
    shared_cols = jnp.concatenate(
        [shared_gate.reshape(96, N_EXP, SHARED), shared_up.reshape(96, N_EXP, SHARED)], axis=2
    ).transpose(1, 0, 2)
    w_shared = swap_all(shared_cols, "exp").reshape(WIDTH, 2 * SHARED)
    shared_two = jnp.concatenate([shared_down, shared_down], axis=0)

    hidden_one = norm_rows(tokens, gain_attn)
    hidden_seq = norm_rows(tokens_seq, gain_attn)
    hidden_seq = after(hidden_seq, w_shared)
    queries, kv_all = project(hidden_one, hidden_seq, w_all)
    attended, att_f, logs = attend(ctx_s, queries, kv_all)
    middle, hidden_two = middle_norm(attended, w_all, tokens[0], gain_ffn)

    hidden_all = lax.all_gather(hidden_two, "exp", axis=0, tiled=True)
    hidden_all = hidden_all.reshape(HALF, 2, BLOCK, WIDTH)
    att_seq = of_sequence(attended[None])
    place, grad_eo, grad_eh, grad_sh, slot_gate = place_rows(
        exp_s,
        after(up_all, hidden_two).reshape(HALF, 2, BLOCK, WIDTH + META),
        expert_down,
        shared_two,
    )
    part, arrived, act, grad_gu, shared_act, shared_grad = expert_back(
        exp_s, after(hidden_all, att_seq), place, grad_eh, grad_sh, expert_gate, expert_up, w_shared
    )
    summed = add_low(part[1], lax.ppermute(part[0], "exp", core_swap))
    grad_two = swap_all(summed, "exp", same_core)

    rows_e = 2 * ROWS
    operands = (
        after(arrived, summed).reshape(LOCAL_E, rows_e, WIDTH),
        grad_eo.reshape(LOCAL_E, rows_e, WIDTH),
        act.reshape(LOCAL_E, rows_e, FF_E),
        grad_gu.reshape(LOCAL_E, rows_e, 2 * FF_E),
    )
    for_1, for_3 = expert_weights(ctx_s, ((2, 0), (1, 0), (2, 1), (3, 1)), True, *operands)
    operands = (after(operands[0], for_1),) + operands[1:]
    p0, p6, p1, p3 = expert_weights(ctx_s, ((0, 0), (3, 0), (0, 1), (1, 1)), False, *operands)

    def to(rows, k):
        return lax.ppermute(rows, "ctx", [(i, i ^ k) for i in range(N_CTX)])

    from_1, from_3 = to(for_1, 1), to(for_3, 3)
    shared_grad_late = after(shared_grad, p0).reshape(N_EXP * BLOCK, META)
    grad_scols = dg(hidden_all.reshape(N_EXP * BLOCK, WIDTH), shared_grad_late, TN).astype(bf16)
    act_late = after(shared_act, p0).reshape(N_EXP * BLOCK, META)
    grad_sdown = dg(act_late, up_all, TN)[:SHARED, :WIDTH].astype(bf16)
    extra = jnp.concatenate(
        [
            jnp.pad(
                grad_scols.reshape(N_EXP, N_CTX, 12, META).transpose(1, 0, 2, 3),
                ((0, 0), (0, 0), (0, 4), (0, 0)),
            ).reshape(N_CTX, 16 * N_EXP, META),
            grad_sdown.reshape(N_CTX, 8, HEADS, 128).transpose(0, 2, 1, 3).reshape(N_CTX, 96, 128),
        ],
        axis=1,
    )

    out_part = expert_output(
        exp_s, after(act, p0), slot_gate, place, shared_act, expert_down, shared_two
    )
    grad_two = after(grad_two, extra, out_part)
    grad_middle, grad_attn, grad_heads, gain_rows = middle_back(
        grad_two, middle, cotangent[0], gain_ffn, w_all
    )
    grad_query, near, far = attend_back(
        ctx_s, queries, grad_heads, att_f, logs, kv_all, grad_attn, extra, gain_rows
    )
    far = lax.ppermute(far, "ctx", z_swap)
    from_1, from_3 = after((from_1, from_3), near)
    add_a, add_b, part_0, part_1 = piece_sums(
        relay_kernel,
        (bf16, bf16, f32, f32),
        p0,
        p1,
        p3,
        p6,
        (from_1, 0),
        (from_3, 0),
        (from_1, 1),
        (from_3, 1),
    )
    got_11, got_30 = to(add_b, 1), to(add_a, 3)

    def from_x(rows, k):
        moved = lax.ppermute(rows, "exp", [(i, i ^ (4 * k)) for i in range(N_EXP)])
        return moved.astype(f32)

    out_sums = spread_sums(
        exp_s,
        out_part,
        lax.ppermute(out_part[0, :4], "exp", core_swap),
        lax.ppermute(out_part[0, 4:], "exp", core_swap),
    )
    out_rows = out_sums[0].astype(f32) + from_x(out_sums[1], 1) + from_x(out_sums[3], 3)
    got_11, got_30 = after((got_11, got_30), far, out_rows)
    own_part, side = piece_sums(side_kernel, (f32, bf16), part_0, part_1, got_11, got_30)
    across = to(side, 4)
    out_rows = out_rows + from_x(after(out_sums[2], side), 2)
    out_across = lax.ppermute(
        out_rows[1].astype(bf16), "exp", [(i, i ^ 2) for i in range(N_EXP)]
    )

    shares = merge_shares(ctx_s, near, after(far, side))
    got = swap_all(shares, "ctx", y_groups)
    own = (own_part + after(across, shares).astype(f32)).astype(bf16)
    at_1, at_3, at_z = to(own, 1), to(own, 3), to(own, 4)

    columns, grad_kv, grad_down = column_grads(got, after(hidden_seq, own, out_rows), att_seq)
    grad_kv = swap_all(grad_kv, "ctx")
    columns = after(columns, grad_kv, at_1, at_3, out_across)
    owned = swap_all(columns, "exp")
    input_grad = input_back(grad_query, grad_kv, w_all, tokens[0], gain_attn, grad_middle)
    owned, gain_sum = owned_sums(owned, grad_down)
    owned, at_z1, at_z3 = lax.optimization_barrier(
        (after(owned, input_grad), to(at_z, 1), to(at_z, 3))
    )
    at_2, at_z2 = to(at_3, 1), to(at_z1, 3)
    mixed = (middle + out_rows[0] + out_across.astype(f32)).astype(bf16)[None]
    experts = unpack_experts(
        ctx_s, ((0, 0), (1, 0), (3, 0), (0, 1)), (after(own, owned), at_1, at_3, at_z)
    )
    owned = swap_all(jnp.broadcast_to(owned, (N_CTX, OWNED_ROWS, HEAD_DIM)), "ctx")
    experts = unpack_experts(
        ctx_s, ((2, 0), (1, 1), (3, 1), (2, 1)), (at_2, at_z1, at_z3, at_z2), experts
    )
    gain_attn_sum, *dense = finish(
        after(owned, experts[0], mixed),
        norm_attn.astype(f32).reshape(96, 1),
        query_weight,
        key_weight,
        value_weight,
    )
    return (
        mixed,
        input_grad[None],
        gain_attn_sum[:, 0],
        gain_sum[12, :96],
        *dense,
        *experts,
    )


def solution(mesh):
    token_spec = P("exp", "ctx", None)
    rows = P("exp", None)
    expert = P("exp", None, None)
    placed = (token_spec,) * 3 + (P("exp"),) * 2 + (rows,) * 7 + (expert,) * 3 + (token_spec,)
    return jax.shard_map(
        on_device,
        mesh=mesh,
        in_specs=placed,
        out_specs=(token_spec,) * 2 + (P("exp"),) * 2 + (rows,) * 7 + (expert,) * 3,
        check_vma=False,
    )
```

```python
import jax
import jax.numpy as jnp
from jax import lax
from jax.sharding import PartitionSpec as P
from jax.experimental import pallas as pl
from jax.experimental.pallas import tpu as pltpu

HEADS = 12
KV_HEADS = 4
HEAD_DIM = 128
TOPK = 6
GROUP = 3
BLOCK = 128
WIDTH = 1536
KV_WIDTH = KV_HEADS * HEAD_DIM
CAP = 48
N_EXP = 16
N_CTX = 8
LOCAL_E = 2
FF_E = 512
SHARED = 64
META = 128
HALF = 8
ROWS = HALF * CAP

epsilon = 1e-05
masked_score = -1e30
f32 = jnp.float32
bf16 = jnp.bfloat16
log2_e = 1.4426950408889634
score_scale = HEAD_DIM ** (-0.5) * log2_e

NN = (((1,), (0,)), ((), ()))
NT = (((1,), (1,)), ((), ()))
TN = (((0,), (0,)), ((), ()))


def dg(a, b, dims):
    return lax.dot_general(a, b, dims, preferred_element_type=f32)


def params(mib):
    return pltpu.CompilerParams(vmem_limit_bytes=mib * 1024 * 1024)


def cost(us):
    return pl.CostEstimate(flops=0, bytes_accessed=int(us * 3690000), transcendentals=0)


def whole(shape):
    return pl.BlockSpec(shape, lambda *_: (0,) * len(shape), pipeline_mode=pl.Buffered(1))


def sigmoid(v):
    return 1.0 / (1.0 + jnp.exp(-v))


def allowed_scores(ctx_at):
    rows = lax.broadcasted_iota(jnp.int32, (GROUP * BLOCK, N_CTX * BLOCK), 0) % BLOCK
    cols = lax.broadcasted_iota(jnp.int32, (GROUP * BLOCK, N_CTX * BLOCK), 1)
    return rows + ctx_at * BLOCK >= cols


def stack_heads(block):
    return jnp.concatenate([block[:, j * HEAD_DIM : (j + 1) * HEAD_DIM] for j in range(GROUP)], axis=0)


def unstack_heads(rows):
    return jnp.concatenate([rows[j * BLOCK : (j + 1) * BLOCK] for j in range(GROUP)], axis=1)


def attend_kernel(ctx_ref, q_ref, k_ref, v_ref, att_ref, attf_ref, log_ref):
    q = stack_heads(q_ref[...])
    keys = k_ref[...].reshape(N_CTX * BLOCK, HEAD_DIM)
    values = v_ref[...].reshape(N_CTX * BLOCK, HEAD_DIM)
    scores = jnp.where(allowed_scores(ctx_ref[0]), dg(q, keys, NT) * score_scale, masked_score)
    top = jnp.max(scores, axis=-1, keepdims=True)
    weights = jnp.exp2(scores - top)
    total = jnp.sum(weights, axis=-1, keepdims=True)
    out = dg(weights.astype(bf16), values, NN) * (1.0 / total)
    out = unstack_heads(out)
    attf_ref[...] = out
    att_ref[...] = out.astype(bf16)
    log_ref[...] = jnp.broadcast_to(top + jnp.log2(total), (GROUP * BLOCK, HEAD_DIM))


def kv_specs():
    return [
        pl.BlockSpec((N_CTX, BLOCK, HEAD_DIM), lambda g: (0, 0, g)),
        pl.BlockSpec((N_CTX, BLOCK, HEAD_DIM), lambda g: (0, 0, KV_HEADS + g)),
    ]


def head_spec():
    return pl.BlockSpec((BLOCK, GROUP * HEAD_DIM), lambda g: (0, g))


def attend(ctx_at, qkv, kv_all):
    return pl.pallas_call(
        attend_kernel,
        grid=(KV_HEADS,),
        in_specs=[pl.BlockSpec(memory_space=pltpu.SMEM), head_spec()] + kv_specs(),
        out_specs=[
            head_spec(),
            head_spec(),
            pl.BlockSpec((GROUP * BLOCK, HEAD_DIM), lambda g: (g, 0)),
        ],
        out_shape=[
            jax.ShapeDtypeStruct((BLOCK, WIDTH), bf16),
            jax.ShapeDtypeStruct((BLOCK, WIDTH), f32),
            jax.ShapeDtypeStruct((HEADS * BLOCK, HEAD_DIM), f32),
        ],
        cost_estimate=cost(6),
        compiler_params=params(48),
        name="attend",
    )(ctx_at, qkv, kv_all, kv_all)


SEQ = N_CTX * BLOCK
AT_QUERY, AT_MIXED, AT_OUT = SEQ, SEQ + BLOCK, SEQ + 2 * BLOCK
AT_SHARED = SEQ + 3 * BLOCK
AT_DOWN = AT_SHARED + 16 * N_EXP
AT_GAIN = AT_DOWN + 96
SENT_ROWS = AT_GAIN + 16


def halves(a, b, lane):
    low = jnp.where(lane < 64, a, pltpu.roll(b, 64, 1))
    high = jnp.where(lane < 64, pltpu.roll(a, 64, 1), b)
    return low, high


def attend_back_kernel(
    ctx_ref,
    q_ref,
    ga_ref,
    attf_ref,
    log_ref,
    k_ref,
    v_ref,
    all_ga_ref,
    extra_ref,
    gain_ref,
    dq_ref,
    near_ref,
    far_ref,
    kept_ref,
):
    group = pl.program_id(0)
    z_at = ctx_ref[0] // 4

    def send(dest, z, start, stop, rows):
        @pl.when(z_at == z)
        def _():
            near_ref[dest, start:stop] = rows

        @pl.when(z_at != z)
        def _():
            far_ref[dest, start:stop] = rows

    q = stack_heads(q_ref[...])
    grad = stack_heads(ga_ref[...])
    delta = jnp.sum(grad.astype(f32) * stack_heads(attf_ref[...]), axis=-1, keepdims=True)
    keys = k_ref[...].reshape(SEQ, HEAD_DIM)
    values = v_ref[...].reshape(SEQ, HEAD_DIM)
    scores = jnp.where(allowed_scores(ctx_ref[0]), dg(q, keys, NT) * score_scale, masked_score)
    weights = jnp.exp2(scores - log_ref[:, :1])
    grad_weights = dg(grad, values, NT)
    grad_raw = (weights * (grad_weights - delta)).astype(bf16)
    scale = HEAD_DIM ** (-0.5)
    dq = unstack_heads(dg(grad_raw, keys, NN) * scale)
    dq_ref[...] = dq.astype(bf16)
    kept_ref[group] = dq
    grad_k = dg(grad_raw, q, TN) * scale
    grad_v = dg(weights.astype(bf16), grad, TN)
    low, high = halves(grad_k, grad_v, lax.broadcasted_iota(jnp.int32, (SEQ, HEAD_DIM), 1))
    low, high = low.astype(bf16), high.astype(bf16)
    send(2 * (group % 2), group // 2, 0, SEQ, low)
    send(2 * (group % 2) + 1, group // 2, 0, SEQ, high)

    @pl.when(group == KV_HEADS - 1)
    def _():
        lane = lax.broadcasted_iota(jnp.int32, (BLOCK, HEAD_DIM), 1)

        def dq_tile(m):
            return kept_ref[m // GROUP, :, HEAD_DIM * (m % GROUP) : HEAD_DIM * (m % GROUP + 1)]

        def ga_tile(m):
            return all_ga_ref[:, HEAD_DIM * m : HEAD_DIM * (m + 1)].astype(f32)

        mixed = []
        for m in range(KV_HEADS):
            mixed += halves(dq_tile(N_CTX + m), ga_tile(N_CTX + m), lane)
        gains = gain_ref[...].astype(bf16)
        for c in range(N_CTX):
            tiles = [dq_tile(c).astype(bf16), mixed[c].astype(bf16), ga_tile(c).astype(bf16)]
            rows = jnp.concatenate(tiles + [extra_ref[c], gains], axis=0)
            send(c % 4, c // 4, AT_QUERY, SENT_ROWS, rows)


def attend_back(ctx_at, qkv, grad_att, att_f, logs, kv_all, grad_attn, extra, gain_rows):
    return pl.pallas_call(
        attend_back_kernel,
        grid=(KV_HEADS,),
        in_specs=[
            pl.BlockSpec(memory_space=pltpu.SMEM),
            head_spec(),
            head_spec(),
            head_spec(),
            pl.BlockSpec((GROUP * BLOCK, HEAD_DIM), lambda g: (g, 0)),
        ]
        + kv_specs()
        + [
            whole((BLOCK, WIDTH)),
            whole((N_CTX, AT_GAIN - AT_SHARED, HEAD_DIM)),
            whole((16, HEAD_DIM)),
        ],
        out_specs=[head_spec()] + [whole((4, SENT_ROWS, HEAD_DIM))] * 2,
        out_shape=[
            jax.ShapeDtypeStruct((BLOCK, WIDTH), bf16),
            jax.ShapeDtypeStruct((4, SENT_ROWS, HEAD_DIM), bf16),
            jax.ShapeDtypeStruct((4, SENT_ROWS, HEAD_DIM), bf16),
        ],
        scratch_shapes=[pltpu.VMEM((KV_HEADS, BLOCK, GROUP * HEAD_DIM), f32)],
        cost_estimate=cost(2),
        compiler_params=params(48),
        name="attend_back",
    )(ctx_at, qkv, grad_att, att_f, logs, kv_all, kv_all, grad_attn, extra, gain_rows)


def middle_kernel(att_ref, w_ref, x_ref, gain_ref, middle_ref, hidden_ref):
    middle = x_ref[...].astype(f32) + dg(att_ref[...], w_ref[...], NN)
    inv = lax.rsqrt(jnp.mean(middle * middle, axis=-1, keepdims=True) + epsilon)
    middle_ref[...] = middle
    hidden_ref[...] = (middle * inv * gain_ref[...]).astype(bf16)


def w_cols(width, at):
    return pl.BlockSpec((WIDTH, width), lambda *_: (0, at), pipeline_mode=pl.Buffered(1))


def middle_norm(attended, w_all, tokens, gain):
    return pl.pallas_call(
        middle_kernel,
        grid=(1,),
        in_specs=[
            whole((BLOCK, WIDTH)),
            w_cols(WIDTH, 1),
            whole((BLOCK, WIDTH)),
            whole((1, WIDTH)),
        ],
        out_specs=[whole((BLOCK, WIDTH)), whole((BLOCK, WIDTH))],
        out_shape=[
            jax.ShapeDtypeStruct((BLOCK, WIDTH), f32),
            jax.ShapeDtypeStruct((BLOCK, WIDTH), bf16),
        ],
        cost_estimate=cost(2),
        compiler_params=params(32),
        name="middle_norm",
    )(attended, w_all, tokens, gain)


def norm_back(grad_normed, normed, inv_root):
    return inv_root * (
        grad_normed - normed * jnp.mean(grad_normed * normed, axis=-1, keepdims=True)
    )


def middle_back_kernel(
    pieces_ref, middle_ref, up_ref, gain_ref, w_ref, gm_ref, ga_ref, gh_ref, gg_ref
):
    grad_two = pieces_ref[0].astype(f32)
    for i in range(1, HALF):
        grad_two = grad_two + pieces_ref[i].astype(f32)
    middle = middle_ref[...]
    inv = lax.rsqrt(jnp.mean(middle * middle, axis=-1, keepdims=True) + epsilon)
    normed = middle * inv
    gains = jnp.sum(grad_two * normed, axis=0, keepdims=True)
    gg_ref[...] = jnp.zeros((16, HEAD_DIM), f32)
    for m in range(HEADS):
        gg_ref[m : m + 1] = gains[:, HEAD_DIM * m : HEAD_DIM * (m + 1)]
    grad_middle = up_ref[...].astype(f32) + norm_back(grad_two * gain_ref[...], normed, inv)
    gm_ref[...] = grad_middle
    grad_attn = grad_middle.astype(bf16)
    ga_ref[...] = grad_attn
    gh_ref[...] = dg(grad_attn, w_ref[...], NT).astype(bf16)


def middle_back(pieces, middle, upstream, gain, w_all):
    return pl.pallas_call(
        middle_back_kernel,
        grid=(1,),
        in_specs=[
            whole((HALF, BLOCK, WIDTH)),
            whole((BLOCK, WIDTH)),
            whole((BLOCK, WIDTH)),
            whole((1, WIDTH)),
            w_cols(WIDTH, 1),
        ],
        out_specs=[whole((BLOCK, WIDTH))] * 3 + [whole((16, HEAD_DIM))],
        out_shape=[
            jax.ShapeDtypeStruct((BLOCK, WIDTH), f32),
            jax.ShapeDtypeStruct((BLOCK, WIDTH), bf16),
            jax.ShapeDtypeStruct((BLOCK, WIDTH), bf16),
            jax.ShapeDtypeStruct((16, HEAD_DIM), f32),
        ],
        cost_estimate=cost(1),
        compiler_params=params(48),
        name="middle_back",
    )(pieces, middle, upstream, gain, w_all)


def place_kernel(
    at_ref, up_ref, down_ref, sdown_ref, place_ref, geo_ref, geh_ref, gsh_ref, gate_ref
):
    lane = lax.broadcasted_iota(jnp.int32, (BLOCK, META), 1)
    row = lax.broadcasted_iota(jnp.int32, (BLOCK, META), 0)
    before = (row > lane).astype(bf16)
    slot = (lane % 64).astype(f32)
    first_id = (at_ref[0] * LOCAL_E).astype(f32)
    row_id = first_id + (row >= 64).astype(f32)

    for chip in range(HALF):
        meta = up_ref[chip, 0, :, WIDTH:].astype(f32)
        named = lane < TOPK
        zero = jnp.zeros((BLOCK, META), f32)
        hit0 = jnp.where(named & (meta == first_id), 1.0, zero)
        hit1 = jnp.where(named & (meta == first_id + 1.0), 1.0, zero)
        mask = jnp.where(
            lane < 64,
            jnp.sum(hit0, axis=1, keepdims=True),
            jnp.sum(hit1, axis=1, keepdims=True),
        )
        rank = dg(before, mask.astype(bf16), NN)
        place = jnp.where((mask > 0.5) & (rank == slot), 1.0, zero).astype(bf16)
        place_ref[chip, 0] = place
        rows = dg(place, up_ref[chip, 0], TN)
        slot_meta = rows[:, WIDTH:]
        gates = pltpu.roll(slot_meta, META - TOPK, 1) + pltpu.roll(
            slot_meta, META - 2 * TOPK, 1
        )
        gate = jnp.sum(
            jnp.where(named & (slot_meta == row_id), gates, zero), axis=1, keepdims=True
        )
        geo = (gate * rows[:, :WIDTH]).astype(bf16)
        wide_gate = jnp.broadcast_to(gate, (BLOCK, META))
        at = chip * CAP
        for e in range(LOCAL_E):
            geo_ref[e, 0, at : at + CAP] = geo[64 * e : 64 * e + CAP]
            gate_ref[e, 0, at : at + CAP] = wide_gate[64 * e : 64 * e + CAP]
        gsh_ref[chip, 0] = dg(up_ref[chip, 0, :, :WIDTH], sdown_ref[...], NT)
    for e in range(LOCAL_E):
        geh_ref[e, 0] = dg(geo_ref[e, 0], down_ref[e], NT)


def by_core(cols):
    return pl.BlockSpec(
        (HALF, 1, BLOCK, cols),
        lambda s, at: (0, jnp.where(s == 0, 1 - at[0] % 2, at[0] % 2), 0, 0),
    )


def by_step(cols):
    return pl.BlockSpec((LOCAL_E, 1, ROWS, cols), lambda s, at: (0, s, 0, 0))


def place_rows(exp_at, up_all, expert_down, shared_two):
    return pl.pallas_call(
        place_kernel,
        grid_spec=pltpu.PrefetchScalarGridSpec(
            num_scalar_prefetch=1,
            grid=(2,),
            in_specs=[
                by_core(WIDTH + META),
                whole((LOCAL_E, FF_E, WIDTH)),
                whole((2 * SHARED, WIDTH)),
            ],
            out_specs=[by_core(META), by_step(WIDTH), by_step(FF_E), by_core(META), by_step(META)],
        ),
        out_shape=[
            jax.ShapeDtypeStruct((HALF, 2, BLOCK, META), bf16),
            jax.ShapeDtypeStruct((LOCAL_E, 2, ROWS, WIDTH), bf16),
            jax.ShapeDtypeStruct((LOCAL_E, 2, ROWS, FF_E), f32),
            jax.ShapeDtypeStruct((HALF, 2, BLOCK, META), f32),
            jax.ShapeDtypeStruct((LOCAL_E, 2, ROWS, META), f32),
        ],
        cost_estimate=cost(14),
        compiler_params=params(56),
        name="place_rows",
    )(exp_at, up_all, expert_down, shared_two)


def expert_kernel(
    at_ref,
    hid_ref,
    place_ref,
    geh_ref,
    gsh_ref,
    wg_ref,
    wu_ref,
    ws_ref,
    part_ref,
    x_ref,
    act_ref,
    dgu_ref,
    sact_ref,
    sgrad_ref,
):
    for chip in range(HALF):
        rows = dg(place_ref[chip, 0], hid_ref[chip, 0], TN).astype(bf16)
        at = chip * CAP
        for e in range(LOCAL_E):
            x_ref[e, 0, at : at + CAP] = rows[64 * e : 64 * e + CAP]
    pairs = []
    for e in range(LOCAL_E):
        pre_gate = dg(x_ref[e, 0], wg_ref[e], NN)
        pre_up = dg(x_ref[e, 0], wu_ref[e], NN)
        sig = sigmoid(pre_gate)
        act = pre_gate * sig
        act_ref[e, 0] = (act * pre_up).astype(bf16)
        geh = geh_ref[e, 0]
        d_gate = (geh * pre_up * (sig * (1.0 + pre_gate * (1.0 - sig)))).astype(bf16)
        d_up = (geh * act).astype(bf16)
        dgu_ref[e, 0, :, :FF_E] = d_gate
        dgu_ref[e, 0, :, FF_E:] = d_up
        pairs.append((dg(d_gate, wg_ref[e], NT) + dg(d_up, wu_ref[e], NT)).astype(bf16))
    lane = lax.broadcasted_iota(jnp.int32, (BLOCK, 2 * SHARED), 1) < SHARED
    gap = jnp.zeros((64 - CAP, WIDTH), bf16)
    for chip in range(HALF):
        pre = dg(hid_ref[chip, 0], ws_ref[...], NN)
        turned = pltpu.roll(pre, SHARED, 1)
        gate, up = jnp.where(lane, pre, turned), jnp.where(lane, turned, pre)
        sig = sigmoid(gate)
        act = gate * sig
        sact_ref[chip, 0] = jnp.where(lane, act * up, 0.0).astype(bf16)
        slope = sig * (1.0 + gate * (1.0 - sig))
        sgrad = (gsh_ref[chip, 0] * jnp.where(lane, up * slope, act)).astype(bf16)
        sgrad_ref[chip, 0] = sgrad
        at = chip * CAP
        stacked = jnp.concatenate([pairs[0][at : at + CAP], gap, pairs[1][at : at + CAP], gap], 0)
        part_ref[0, chip] = (
            dg(place_ref[chip, 0], stacked, NN) + dg(sgrad, ws_ref[...], NT)
        ).astype(bf16)


def expert_back(exp_at, hidden, place, geh, gsh, wg, wu, ws):
    return pl.pallas_call(
        expert_kernel,
        grid_spec=pltpu.PrefetchScalarGridSpec(
            num_scalar_prefetch=1,
            grid=(2,),
            in_specs=[
                by_core(WIDTH),
                by_core(META),
                by_step(FF_E),
                by_core(META),
                whole((LOCAL_E, WIDTH, FF_E)),
                whole((LOCAL_E, WIDTH, FF_E)),
                whole((WIDTH, 2 * SHARED)),
            ],
            out_specs=[
                pl.BlockSpec((1, HALF, BLOCK, WIDTH), lambda s, at: (s, 0, 0, 0)),
                by_step(WIDTH),
                by_step(FF_E),
                by_step(2 * FF_E),
                by_core(META),
                by_core(META),
            ],
        ),
        out_shape=[
            jax.ShapeDtypeStruct((2, HALF, BLOCK, WIDTH), bf16),
            jax.ShapeDtypeStruct((LOCAL_E, 2, ROWS, WIDTH), bf16),
            jax.ShapeDtypeStruct((LOCAL_E, 2, ROWS, FF_E), bf16),
            jax.ShapeDtypeStruct((LOCAL_E, 2, ROWS, 2 * FF_E), bf16),
            jax.ShapeDtypeStruct((HALF, 2, BLOCK, META), bf16),
            jax.ShapeDtypeStruct((HALF, 2, BLOCK, META), bf16),
        ],
        cost_estimate=cost(28),
        compiler_params=params(60),
        name="expert_back",
    )(exp_at, hidden, place, geh, gsh, wg, wu, ws)


def output_kernel(at_ref, act_ref, gate_ref, place_ref, sact_ref, wd_ref, sd_ref, part_ref):
    outs = []
    for e in range(LOCAL_E):
        out = dg(act_ref[e, 0], wd_ref[e], NN).astype(bf16).astype(f32)
        outs.append((out * gate_ref[e, 0, :, :1]).astype(bf16))
    gap = jnp.zeros((64 - CAP, WIDTH), bf16)
    for chip in range(HALF):
        at = chip * CAP
        stacked = jnp.concatenate([outs[0][at : at + CAP], gap, outs[1][at : at + CAP], gap], 0)
        part_ref[0, chip] = (
            dg(place_ref[chip, 0], stacked, NN) + dg(sact_ref[chip, 0], sd_ref[...], NN)
        ).astype(bf16)


def expert_output(exp_at, act, gate, place, sact, wd, sd):
    return pl.pallas_call(
        output_kernel,
        grid_spec=pltpu.PrefetchScalarGridSpec(
            num_scalar_prefetch=1,
            grid=(2,),
            in_specs=[
                by_step(FF_E),
                by_step(META),
                by_core(META),
                by_core(META),
                whole((LOCAL_E, FF_E, WIDTH)),
                whole((2 * SHARED, WIDTH)),
            ],
            out_specs=pl.BlockSpec((1, HALF, BLOCK, WIDTH), lambda s, at: (s, 0, 0, 0)),
        ),
        out_shape=jax.ShapeDtypeStruct((2, HALF, BLOCK, WIDTH), bf16),
        cost_estimate=cost(2),
        compiler_params=params(48),
        name="expert_output",
    )(exp_at, act, gate, place, sact, wd, sd)


SHARE = 3 * BLOCK
TO_SHARED = SEQ + 2 * SHARE
TO_DOWN = TO_SHARED + 16 * N_EXP
TO_GAIN = TO_DOWN + 96
MERGED_ROWS = TO_GAIN + 16


def merge_kernel(ctx_ref, near_ref, got_ref, out_ref):
    z_at = ctx_ref[0] // 4
    near, got = near_ref[0], got_ref[0]

    def add(a, b):
        return (a.astype(f32) + b.astype(f32)).astype(bf16)

    out_ref[0, :SEQ] = add(near[:SEQ], got[:SEQ])
    out_ref[0, TO_SHARED:] = add(near[AT_SHARED:], got[AT_SHARED:])
    mine, theirs = near[AT_QUERY:AT_SHARED], got[AT_QUERY:AT_SHARED]
    out_ref[0, SEQ : SEQ + SHARE] = jnp.where(z_at == 0, mine, theirs)
    out_ref[0, SEQ + SHARE : TO_SHARED] = jnp.where(z_at == 0, theirs, mine)


def merge_shares(ctx_at, near, got):
    spec = pl.BlockSpec((1, SENT_ROWS, HEAD_DIM), lambda i: (i, 0, 0))
    return pl.pallas_call(
        merge_kernel,
        grid=(4,),
        in_specs=[pl.BlockSpec(memory_space=pltpu.SMEM), spec, spec],
        out_specs=pl.BlockSpec((1, MERGED_ROWS, HEAD_DIM), lambda i: (i, 0, 0)),
        out_shape=jax.ShapeDtypeStruct((4, MERGED_ROWS, HEAD_DIM), bf16),
        cost_estimate=cost(3),
        compiler_params=params(32),
        name="merge_shares",
    )(ctx_at, near, got)


def columns_kernel(got_ref, hidden_ref, att_ref, sent_ref, kv_ref, down_ref):
    def summed(start, stop):
        out = got_ref[0, start:stop].astype(f32)
        for src in range(1, 4):
            out = out + got_ref[src, start:stop].astype(f32)
        return out

    grad_kv = summed(0, SEQ).astype(bf16)
    kv_ref[...] = grad_kv.reshape(N_CTX, BLOCK, HEAD_DIM)

    def rows_of(tile, order):
        at = SEQ + BLOCK * tile
        return jnp.concatenate(
            [got_ref[y, at + SHARE * z : at + SHARE * z + BLOCK] for z, y in order], axis=0
        )

    in_order = [(i // 4, i % 4) for i in range(N_CTX)]
    y_order = [(i % 2, i // 2) for i in range(N_CTX)]
    lane = lax.broadcasted_iota(jnp.int32, (SEQ, HEAD_DIM), 1)
    zero = jnp.zeros((SEQ, HEAD_DIM), bf16)
    mixed_q = jnp.where(lane < 64, rows_of(1, in_order), zero)
    mixed_o = jnp.where(lane < 64, zero, rows_of(1, y_order))
    left = jnp.concatenate([rows_of(0, in_order).T, mixed_q.T, grad_kv.T], axis=0)
    right = jnp.concatenate([mixed_o.T, rows_of(2, y_order).T], axis=0)
    by_hidden = dg(left, hidden_ref[...].reshape(SEQ, WIDTH), NN)
    by_att = dg(right, att_ref[...].reshape(SEQ, WIDTH), NN)
    tiles = [
        by_hidden[:BLOCK],
        by_hidden[BLOCK : 2 * BLOCK] + by_att[:BLOCK],
        by_att[BLOCK:],
        by_hidden[2 * BLOCK :],
    ]
    for t, tile in enumerate(tiles):
        sent_ref[:, :96, HEAD_DIM * t : HEAD_DIM * (t + 1)] = (
            tile.T.astype(bf16).reshape(N_EXP, 96, HEAD_DIM)
        )

    down_ref[...] = summed(TO_DOWN, TO_GAIN).astype(bf16)
    shared = summed(TO_SHARED, TO_DOWN)
    gains = summed(TO_GAIN, MERGED_ROWS)
    row = lax.broadcasted_iota(jnp.int32, (16, HEAD_DIM), 0)
    one_lane = lax.broadcasted_iota(jnp.int32, (1, HEAD_DIM), 1)
    for i in range(N_EXP):
        m, offset = (96 * i) // HEAD_DIM, (96 * i) % HEAD_DIM
        gain = gains[m : m + 1]
        if offset:
            shift = HEAD_DIM - offset
            gain = jnp.where(
                one_lane < shift,
                pltpu.roll(gain, shift, 1),
                pltpu.roll(gains[m + 1 : m + 2], shift, 1),
            )
        rows = jnp.where(row == 12, jnp.broadcast_to(gain, (16, HEAD_DIM)), shared[16 * i : 16 * i + 16])
        sent_ref[i, 96:, :HEAD_DIM] = rows.astype(bf16)
        sent_ref[i, 96:, HEAD_DIM:] = jnp.zeros((16, 512 - HEAD_DIM), bf16)


def column_grads(got, hidden_seq, att_seq):
    return pl.pallas_call(
        columns_kernel,
        out_shape=[
            jax.ShapeDtypeStruct((N_EXP, 112, 512), bf16),
            jax.ShapeDtypeStruct((N_CTX, BLOCK, HEAD_DIM), bf16),
            jax.ShapeDtypeStruct((96, HEAD_DIM), bf16),
        ],
        cost_estimate=cost(8),
        compiler_params=params(56),
        name="column_grads",
    )(got, hidden_seq, att_seq)


OWNED_ROWS = 4 * 96 + 16 * N_EXP + 96


def owned_kernel(got_ref, down_ref, owned_ref, gain_ref):
    total = got_ref[0, :96].astype(f32)
    gains = got_ref[0, 96:, :HEAD_DIM].astype(f32)
    for src in range(1, N_EXP):
        total = total + got_ref[src, :96].astype(f32)
        gains = gains + got_ref[src, 96:, :HEAD_DIM].astype(f32)
    gain_ref[...] = gains
    for t in range(4):
        owned_ref[96 * t : 96 * t + 96] = total[:, HEAD_DIM * t : HEAD_DIM * (t + 1)].astype(bf16)
    for src in range(N_EXP):
        at = 384 + 16 * src
        owned_ref[at : at + 16] = got_ref[src, 96:, :HEAD_DIM]
    owned_ref[384 + 16 * N_EXP :] = down_ref[...]


def owned_sums(got, down):
    return pl.pallas_call(
        owned_kernel,
        out_shape=[
            jax.ShapeDtypeStruct((OWNED_ROWS, HEAD_DIM), bf16),
            jax.ShapeDtypeStruct((16, HEAD_DIM), f32),
        ],
        cost_estimate=cost(3),
        compiler_params=params(32),
        name="owned_sums",
    )(got, down)


def finish_kernel(
    got_ref,
    gain_in_ref,
    wq_ref,
    wk_ref,
    wv_ref,
    gain_ref,
    q_ref,
    k_ref,
    v_ref,
    out_ref,
    sg_ref,
    su_ref,
    sd_ref,
):
    lane = lax.broadcasted_iota(jnp.int32, (96, HEAD_DIM), 1)

    def tile(c, t):
        return got_ref[c, 96 * t : 96 * t + 96].astype(f32)

    for c in range(N_CTX):
        at = HEAD_DIM * c
        q_ref[:, at : at + HEAD_DIM] = tile(c, 0)
        out_ref[:, at : at + HEAD_DIM] = tile(c, 2)
    for m in range(N_CTX // 2):
        at = HEAD_DIM * m
        low, high = halves(tile(2 * m, 1), tile(2 * m + 1, 1), lane)
        q_ref[:, 1024 + at : 1024 + at + HEAD_DIM] = low
        out_ref[:, 1024 + at : 1024 + at + HEAD_DIM] = high
        low, high = halves(tile(2 * m, 3), tile(2 * m + 1, 3), lane)
        k_ref[:, at : at + HEAD_DIM] = low
        v_ref[:, at : at + HEAD_DIM] = high
    gain = (
        jnp.sum(q_ref[...] * wq_ref[...].astype(f32), axis=1, keepdims=True)
        + jnp.sum(k_ref[...] * wk_ref[...].astype(f32), axis=1, keepdims=True)
        + jnp.sum(v_ref[...] * wv_ref[...].astype(f32), axis=1, keepdims=True)
    ) / gain_in_ref[...]
    gain_ref[...] = jnp.broadcast_to(gain, (96, HEAD_DIM))
    row = lax.broadcasted_iota(jnp.int32, (96, HEAD_DIM), 0)
    picks = jnp.where((lane % 16 < 12) & (row == 12 * (lane // 16) + lane % 16), 1.0, 0.0)
    picks = picks.astype(bf16)

    def shared_tile(j):
        at = 384 + 16 * j
        rows = jnp.concatenate([got_ref[c, at : at + 16] for c in range(N_CTX)], axis=0)
        return dg(picks, rows, NN)

    for m in range(N_EXP // 2):
        at = HEAD_DIM * m
        low, high = halves(shared_tile(2 * m), shared_tile(2 * m + 1), lane)
        sg_ref[:, at : at + HEAD_DIM] = low
        su_ref[:, at : at + HEAD_DIM] = high
    for c in range(N_CTX):
        rows = got_ref[c, 384 + 16 * N_EXP :].astype(f32)
        for m in range(HEADS):
            sd_ref[8 * c : 8 * c + 8, HEAD_DIM * m : HEAD_DIM * (m + 1)] = rows[8 * m : 8 * m + 8]


def finish(got, gain_column, query_weight, key_weight, value_weight):
    shapes = [(96, 128), (96, 1536), (96, 512), (96, 512), (96, 1536), (96, 1024), (96, 1024)]
    return pl.pallas_call(
        finish_kernel,
        out_shape=[jax.ShapeDtypeStruct(s, f32) for s in shapes + [(SHARED, WIDTH)]],
        cost_estimate=cost(4),
        compiler_params=params(32),
        name="finish",
    )(got, gain_column, query_weight, key_weight, value_weight)


def input_kernel(dq_ref, got_ref, wq_ref, wkv_ref, x_ref, gain_ref, gm_ref, out_ref):
    lane = lax.broadcasted_iota(jnp.int32, (BLOCK, HEAD_DIM), 1)
    lows, highs = [], []
    for m in range(KV_HEADS):
        low, high = halves(got_ref[2 * m].astype(f32), got_ref[2 * m + 1].astype(f32), lane)
        lows.append(low.astype(bf16))
        highs.append(high.astype(bf16))
    grad_kv = jnp.concatenate(lows + highs, axis=1)
    grad_one = dg(dq_ref[...], wq_ref[...], NT) + dg(grad_kv, wkv_ref[...], NT)
    inputs = x_ref[...].astype(f32)
    inv = lax.rsqrt(jnp.mean(inputs * inputs, axis=-1, keepdims=True) + epsilon)
    out_ref[...] = (gm_ref[...] + norm_back(grad_one * gain_ref[...], inputs * inv, inv)).astype(bf16)


def input_back(grad_query, grad_kv, w_all, tokens, gain, grad_middle):
    return pl.pallas_call(
        input_kernel,
        grid=(1,),
        in_specs=[
            whole((BLOCK, WIDTH)),
            whole((N_CTX, BLOCK, HEAD_DIM)),
            w_cols(WIDTH, 0),
            w_cols(2 * KV_WIDTH, 3),
            whole((BLOCK, WIDTH)),
            whole((1, WIDTH)),
            whole((BLOCK, WIDTH)),
        ],
        out_specs=whole((BLOCK, WIDTH)),
        out_shape=jax.ShapeDtypeStruct((BLOCK, WIDTH), bf16),
        cost_estimate=cost(7),
        compiler_params=params(48),
        name="input_back",
    )(grad_query, grad_kv, w_all, w_all, tokens, gain, grad_middle)


def norm_rows_kernel(x_ref, gain_ref, out_ref):
    inputs = x_ref[0].astype(f32)
    inv = lax.rsqrt(jnp.mean(inputs * inputs, axis=-1, keepdims=True) + epsilon)
    out_ref[0] = (inputs * inv * gain_ref[...]).astype(bf16)


def norm_rows(rows, gain):
    count = rows.shape[0]
    spec = pl.BlockSpec((1, BLOCK, WIDTH), lambda i: (i, 0, 0))
    turned = pl.BlockSpec((1, BLOCK, WIDTH), lambda i: ((i % 2) * 4 + i // 2, 0, 0))
    return pl.pallas_call(
        norm_rows_kernel,
        grid=(count,),
        in_specs=[spec, whole((1, WIDTH))],
        out_specs=spec if count == 1 else turned,
        out_shape=jax.ShapeDtypeStruct(rows.shape, bf16),
        cost_estimate=cost(2),
        compiler_params=params(32),
        name="norm_rows",
    )(rows, gain)


def project_kernel(own_ref, seq_ref, w_ref, q_ref, kv_ref):
    step = pl.program_id(0)

    @pl.when(step < 3)
    def _():
        q_ref[...] = dg(own_ref[0], w_ref[...], NN).astype(bf16)

    @pl.when(step >= 3)
    def _():
        rows = seq_ref[...].reshape(N_CTX * BLOCK, WIDTH)
        kv_ref[...] = dg(rows, w_ref[...], NN).astype(bf16).reshape(N_CTX, BLOCK, KV_WIDTH)


def project(own, seq, w_all):
    return pl.pallas_call(
        project_kernel,
        grid=(5,),
        in_specs=[
            whole((1, BLOCK, WIDTH)),
            whole((N_CTX, BLOCK, WIDTH)),
            pl.BlockSpec((WIDTH, KV_WIDTH), lambda i: (0, jnp.where(i < 3, i, i + 3))),
        ],
        out_specs=[
            pl.BlockSpec((BLOCK, KV_WIDTH), lambda i: (0, jnp.minimum(i, 2))),
            pl.BlockSpec((N_CTX, BLOCK, KV_WIDTH), lambda i: (0, 0, jnp.maximum(i - 3, 0))),
        ],
        out_shape=[
            jax.ShapeDtypeStruct((BLOCK, WIDTH), bf16),
            jax.ShapeDtypeStruct((N_CTX, BLOCK, 2 * KV_WIDTH), bf16),
        ],
        cost_estimate=cost(8),
        compiler_params=params(48),
        name="project",
    )(own, seq, w_all)


PIECE = 2 * WIDTH + WIDTH * BLOCK // HEAD_DIM


def spread_kernel(at_ref, own_ref, low_ref, high_ref, *outs):
    chip = (at_ref[0] >> 1) ^ pl.program_id(0)
    got = jnp.where(chip < 4, low_ref[0], high_ref[0])
    total = (own_ref[0, 0].astype(f32) + got.astype(f32)).astype(bf16)
    for k in range(HALF):

        @pl.when(pl.program_id(0) == k)
        def _():
            outs[k // 2][k % 2] = total


def spread_sums(exp_at, parts, low, high):
    half = pl.BlockSpec((1, BLOCK, WIDTH), lambda k, at: (((at[0] >> 1) ^ k) & 3, 0, 0))
    return pl.pallas_call(
        spread_kernel,
        grid_spec=pltpu.PrefetchScalarGridSpec(
            num_scalar_prefetch=1,
            grid=(HALF,),
            in_specs=[
                pl.BlockSpec((1, 1, BLOCK, WIDTH), lambda k, at: (1, (at[0] >> 1) ^ k, 0, 0)),
                half,
                half,
            ],
            out_specs=[whole((2, BLOCK, WIDTH))] * 4,
        ),
        out_shape=[jax.ShapeDtypeStruct((2, BLOCK, WIDTH), bf16)] * 4,
        cost_estimate=cost(4),
        compiler_params=params(32),
        name="spread_sums",
    )(exp_at, parts, low, high)


def of_step(values, step):
    out = jnp.int32(values[0])
    for i, value in enumerate(values[1:], 1):
        out = jnp.where(step == i, value, out)
    return out


def expert_weights_kernel(halved, at_ref, x_ref, geo_ref, act_ref, dgate_ref, dup_ref, *outs):
    step = pl.program_id(0)
    rhs = jnp.concatenate([dgate_ref[0], dup_ref[0]], axis=1)
    both = dg(x_ref[0], rhs, TN).astype(bf16)
    down = dg(act_ref[0], geo_ref[0], TN).astype(bf16)
    for i in range(4):

        @pl.when(step == i)
        def _():
            start = (i % 2) * PIECE if halved else 0
            out = outs[i // 2 if halved else i].at[pl.ds(start, PIECE)]
            out[:WIDTH] = both[:, :HEAD_DIM]
            out[WIDTH : 2 * WIDTH] = both[:, HEAD_DIM:]
            for m in range(WIDTH // HEAD_DIM):
                at = 2 * WIDTH + m * BLOCK
                out[at : at + BLOCK] = down[:, m * HEAD_DIM : (m + 1) * HEAD_DIM]


def expert_weights(ctx_at, steps, halved, arrived, grad_eo, act, grad_gu):
    rows = 2 * ROWS

    def expert(s, at):
        return (at[0] >> 2) ^ of_step([side for _, side in steps], s)

    def lanes(shift):
        return pl.BlockSpec(
            (1, rows, HEAD_DIM),
            lambda s, at: (
                expert(s, at),
                0,
                shift + ((at[0] & 3) ^ of_step([r for r, _ in steps], s)),
            ),
        )

    rows_of = pl.BlockSpec((1, rows, WIDTH), lambda s, at: (expert(s, at), 0, 0))
    count, length = (2, 2 * PIECE) if halved else (4, PIECE)
    return pl.pallas_call(
        lambda *refs: expert_weights_kernel(halved, *refs),
        grid_spec=pltpu.PrefetchScalarGridSpec(
            num_scalar_prefetch=1,
            grid=(4,),
            in_specs=[rows_of, rows_of, lanes(0), lanes(0), lanes(4)],
            out_specs=[whole((length, HEAD_DIM))] * count,
        ),
        out_shape=[jax.ShapeDtypeStruct((length, HEAD_DIM), bf16)] * count,
        cost_estimate=cost(2),
        compiler_params=params(56),
        name="expert_weights",
    )(ctx_at, arrived, grad_eo, act, grad_gu, grad_gu)


def unpack_kernel(count, at_ref, *refs):
    pieces, (gate_ref, up_ref, down_ref) = refs[:count], refs[-3:]
    step = pl.program_id(0)
    for i in range(count):

        @pl.when(step == i)
        def _():
            piece = pieces[i]
            gate_ref[0] = piece[:WIDTH].astype(f32)
            up_ref[0] = piece[WIDTH : 2 * WIDTH].astype(f32)
            for m in range(WIDTH // HEAD_DIM):
                at = 2 * WIDTH + m * BLOCK
                down_ref[0, :, m * HEAD_DIM : (m + 1) * HEAD_DIM] = piece[at : at + BLOCK].astype(
                    f32
                )


def unpack_experts(ctx_at, steps, pieces, filled=()):
    count = len(steps)

    def expert(s, at):
        return (at[0] >> 2) ^ of_step([side for _, side in steps], s)

    def units(s, at):
        return (at[0] & 3) ^ of_step([r for r, _ in steps], s)

    cols = pl.BlockSpec((1, WIDTH, HEAD_DIM), lambda s, at: (expert(s, at), 0, units(s, at)))
    rows = pl.BlockSpec((1, BLOCK, WIDTH), lambda s, at: (expert(s, at), units(s, at), 0))
    anywhere = pl.BlockSpec(memory_space=pl.ANY)
    return pl.pallas_call(
        lambda *refs: unpack_kernel(count, *refs),
        grid_spec=pltpu.PrefetchScalarGridSpec(
            num_scalar_prefetch=1,
            grid=(count,),
            in_specs=[whole((PIECE, HEAD_DIM))] * count + [anywhere] * len(filled),
            out_specs=[cols, cols, rows],
        ),
        out_shape=[
            jax.ShapeDtypeStruct((LOCAL_E, WIDTH, FF_E), f32),
            jax.ShapeDtypeStruct((LOCAL_E, WIDTH, FF_E), f32),
            jax.ShapeDtypeStruct((LOCAL_E, FF_E, WIDTH), f32),
        ],
        input_output_aliases={1 + count + i: i for i in range(len(filled))},
        cost_estimate=cost(2 * count),
        compiler_params=params(48),
        name="unpack_experts",
    )(ctx_at, *pieces, *filled)


def relay_kernel(
    p0, p1, p3, p6, relay_a, relay_b, got_10, got_31, add_a, add_b, part_0, part_1
):
    add_a[...] = (p6[...].astype(f32) + relay_a[...].astype(f32)).astype(bf16)
    add_b[...] = (p3[...].astype(f32) + relay_b[...].astype(f32)).astype(bf16)
    part_0[...] = p0[...].astype(f32) + got_10[...].astype(f32)
    part_1[...] = p1[...].astype(f32) + got_31[...].astype(f32)


def side_kernel(part_0, part_1, got_11, got_30, own, side):
    own[...] = part_0[...] + got_30[...].astype(f32)
    side[...] = (part_1[...] + got_11[...].astype(f32)).astype(bf16)


def piece_sums(kernel, kinds, *pieces):
    specs, arrays = [], []
    for piece in pieces:
        array, second = piece if isinstance(piece, tuple) else (piece, 0)
        specs.append(pl.BlockSpec((PIECE // 4, HEAD_DIM), lambda i, at=4 * second: (i + at, 0)))
        arrays.append(array)
    return pl.pallas_call(
        kernel,
        grid=(4,),
        in_specs=specs,
        out_specs=[pl.BlockSpec((PIECE // 4, HEAD_DIM), lambda i: (i, 0))] * len(kinds),
        out_shape=[jax.ShapeDtypeStruct((PIECE, HEAD_DIM), kind) for kind in kinds],
        cost_estimate=cost(1),
        compiler_params=params(32),
        name="piece_sums",
    )(*arrays)


same_core = [[2 * i + c for i in range(8)] for c in range(2)]
core_swap = [(i, i ^ 1) for i in range(N_EXP)]
y_groups = [[0, 1, 2, 3], [4, 5, 6, 7]]
z_swap = [(i, i ^ 4) for i in range(N_CTX)]


def swap_all(rows, axis, groups=None):
    return lax.all_to_all(
        rows, axis, split_axis=0, concat_axis=0, tiled=True, axis_index_groups=groups
    )


def after(value, *others):
    return lax.optimization_barrier((value,) + others)[0]


def add_low(a, b):
    return (a.astype(f32) + b.astype(f32)).astype(bf16)


def on_device(
    tokens,
    routes,
    route_gates,
    norm_attn,
    norm_ffn,
    query_weight,
    key_weight,
    value_weight,
    out_weight,
    shared_gate,
    shared_up,
    shared_down,
    expert_gate,
    expert_up,
    expert_down,
    cotangent,
):
    exp_at = lax.axis_index("exp").astype(jnp.int32)
    ctx_at = lax.axis_index("ctx").astype(jnp.int32)
    exp_s, ctx_s = exp_at.reshape(1), ctx_at.reshape(1)

    z_at = ctx_at // 4

    w_cat = jnp.concatenate([query_weight, out_weight, key_weight, value_weight], axis=1)
    w_all = lax.all_gather(w_cat, "exp", axis=0, tiled=True)
    gates_high = route_gates[0].astype(bf16)
    gates_low = (route_gates[0] - gates_high.astype(f32)).astype(bf16)
    pad = jnp.zeros((BLOCK, META - 3 * TOPK), bf16)
    up_meta = jnp.concatenate(
        [cotangent[0], routes[0].astype(bf16), gates_high, gates_low, pad], axis=1
    )
    up_all = lax.all_gather(after(up_meta, w_cat), "exp", axis=0, tiled=True)
    gains = after(jnp.concatenate([norm_attn, norm_ffn]), w_cat)
    gains = swap_all(jnp.broadcast_to(gains, (N_EXP, gains.shape[0])), "exp")
    gain_attn = gains[:, :96].reshape(1, WIDTH).astype(f32)
    gain_ffn = gains[:, 96:].reshape(1, WIDTH).astype(f32)

    def of_sequence(rows):
        other = lax.ppermute(rows, "ctx", z_swap)
        pair = jnp.where(
            z_at == 0,
            jnp.concatenate([rows, other], axis=0),
            jnp.concatenate([other, rows], axis=0),
        )
        got = swap_all(jnp.broadcast_to(pair, (4, 2, BLOCK, WIDTH)), "ctx", y_groups)
        return got.reshape(N_CTX, BLOCK, WIDTH)

    tokens_seq = of_sequence(after(tokens, w_cat))
    shared_cols = jnp.concatenate(
        [shared_gate.reshape(96, N_EXP, SHARED), shared_up.reshape(96, N_EXP, SHARED)], axis=2
    ).transpose(1, 0, 2)
    w_shared = swap_all(shared_cols, "exp").reshape(WIDTH, 2 * SHARED)
    shared_two = jnp.concatenate([shared_down, shared_down], axis=0)

    hidden_one = norm_rows(tokens, gain_attn)
    hidden_seq = norm_rows(tokens_seq, gain_attn)
    hidden_seq = after(hidden_seq, w_shared)
    queries, kv_all = project(hidden_one, hidden_seq, w_all)
    attended, att_f, logs = attend(ctx_s, queries, kv_all)
    middle, hidden_two = middle_norm(attended, w_all, tokens[0], gain_ffn)

    hidden_all = lax.all_gather(hidden_two, "exp", axis=0, tiled=True)
    hidden_all = hidden_all.reshape(HALF, 2, BLOCK, WIDTH)
    att_seq = of_sequence(attended[None])
    place, grad_eo, grad_eh, grad_sh, slot_gate = place_rows(
        exp_s,
        after(up_all, hidden_two).reshape(HALF, 2, BLOCK, WIDTH + META),
        expert_down,
        shared_two,
    )
    part, arrived, act, grad_gu, shared_act, shared_grad = expert_back(
        exp_s, after(hidden_all, att_seq), place, grad_eh, grad_sh, expert_gate, expert_up, w_shared
    )
    summed = add_low(part[1], lax.ppermute(part[0], "exp", core_swap))
    grad_two = swap_all(summed, "exp", same_core)

    rows_e = 2 * ROWS
    operands = (
        after(arrived, summed).reshape(LOCAL_E, rows_e, WIDTH),
        grad_eo.reshape(LOCAL_E, rows_e, WIDTH),
        act.reshape(LOCAL_E, rows_e, FF_E),
        grad_gu.reshape(LOCAL_E, rows_e, 2 * FF_E),
    )
    for_1, for_3 = expert_weights(ctx_s, ((2, 0), (1, 0), (2, 1), (3, 1)), True, *operands)
    operands = (after(operands[0], for_1),) + operands[1:]
    p0, p6, p1, p3 = expert_weights(ctx_s, ((0, 0), (3, 0), (0, 1), (1, 1)), False, *operands)

    def to(rows, k):
        return lax.ppermute(rows, "ctx", [(i, i ^ k) for i in range(N_CTX)])

    from_1, from_3 = to(for_1, 1), to(for_3, 3)
    shared_grad_late = after(shared_grad, p0).reshape(N_EXP * BLOCK, META)
    grad_scols = dg(hidden_all.reshape(N_EXP * BLOCK, WIDTH), shared_grad_late, TN).astype(bf16)
    act_late = after(shared_act, p0).reshape(N_EXP * BLOCK, META)
    grad_sdown = dg(act_late, up_all, TN)[:SHARED, :WIDTH].astype(bf16)
    extra = jnp.concatenate(
        [
            jnp.pad(
                grad_scols.reshape(N_EXP, N_CTX, 12, META).transpose(1, 0, 2, 3),
                ((0, 0), (0, 0), (0, 4), (0, 0)),
            ).reshape(N_CTX, 16 * N_EXP, META),
            grad_sdown.reshape(N_CTX, 8, HEADS, 128).transpose(0, 2, 1, 3).reshape(N_CTX, 96, 128),
        ],
        axis=1,
    )

    out_part = expert_output(
        exp_s, after(act, p0), slot_gate, place, shared_act, expert_down, shared_two
    )
    grad_two = after(grad_two, extra, out_part)
    grad_middle, grad_attn, grad_heads, gain_rows = middle_back(
        grad_two, middle, cotangent[0], gain_ffn, w_all
    )
    grad_query, near, far = attend_back(
        ctx_s, queries, grad_heads, att_f, logs, kv_all, grad_attn, extra, gain_rows
    )
    far = lax.ppermute(far, "ctx", z_swap)
    from_1, from_3 = after((from_1, from_3), near)
    add_a, add_b, part_0, part_1 = piece_sums(
        relay_kernel,
        (bf16, bf16, f32, f32),
        p0,
        p1,
        p3,
        p6,
        (from_1, 0),
        (from_3, 0),
        (from_1, 1),
        (from_3, 1),
    )
    got_11, got_30 = to(add_b, 1), to(add_a, 3)

    def from_x(rows, k):
        return lax.ppermute(rows, "exp", [(i, i ^ (4 * k)) for i in range(N_EXP)])

    out_sums = spread_sums(
        exp_s,
        after(out_part, add_a),
        lax.ppermute(out_part[0, :4], "exp", core_swap),
        lax.ppermute(out_part[0, 4:], "exp", core_swap),
    )
    out_near = (
        out_sums[0].astype(f32)
        + from_x(out_sums[1], 1).astype(f32)
        + from_x(out_sums[3], 3).astype(f32)
    )
    got_11, got_30 = after((got_11, got_30), far)
    own_part, side = piece_sums(side_kernel, (f32, bf16), part_0, part_1, got_11, got_30)
    across = to(side, 4)
    out_2 = from_x(after(out_sums[2], side), 2)

    shares = merge_shares(ctx_s, near, after(far, side, out_near))
    got = swap_all(shares, "ctx", y_groups)
    own = (own_part + after(across, shares).astype(f32)).astype(bf16)
    at_1, at_3, at_z = to(own, 1), to(own, 3), to(own, 4)

    columns, grad_kv, grad_down = column_grads(got, after(hidden_seq, own, out_2), att_seq)
    out_rows = after(out_near, columns) + out_2.astype(f32)
    out_across = lax.ppermute(
        out_rows[1].astype(bf16), "exp", [(i, i ^ 2) for i in range(N_EXP)]
    )
    grad_kv = swap_all(grad_kv, "ctx")
    columns = after(columns, grad_kv, at_1, at_3)
    owned = swap_all(columns, "exp")
    input_grad = input_back(grad_query, grad_kv, w_all, tokens[0], gain_attn, grad_middle)
    owned, gain_sum = owned_sums(owned, grad_down)
    owned, at_z1, at_z3 = lax.optimization_barrier(
        (after(owned, input_grad, out_across), to(at_z, 1), to(at_z, 3))
    )
    at_2, at_z2 = to(at_3, 1), to(at_z1, 3)
    mixed = (middle + out_rows[0] + out_across.astype(f32)).astype(bf16)[None]
    experts = unpack_experts(
        ctx_s, ((0, 0), (1, 0), (3, 0), (0, 1)), (after(own, owned), at_1, at_3, at_z)
    )
    owned = swap_all(jnp.broadcast_to(owned, (N_CTX, OWNED_ROWS, HEAD_DIM)), "ctx")
    experts = unpack_experts(
        ctx_s, ((2, 0), (1, 1), (3, 1), (2, 1)), (at_2, at_z1, at_z3, at_z2), experts
    )
    gain_attn_sum, *dense = finish(
        after(owned, experts[0], mixed),
        norm_attn.astype(f32).reshape(96, 1),
        query_weight,
        key_weight,
        value_weight,
    )
    return (
        mixed,
        input_grad[None],
        gain_attn_sum[:, 0],
        gain_sum[12, :96],
        *dense,
        *experts,
    )


def solution(mesh):
    token_spec = P("exp", "ctx", None)
    rows = P("exp", None)
    expert = P("exp", None, None)
    placed = (token_spec,) * 3 + (P("exp"),) * 2 + (rows,) * 7 + (expert,) * 3 + (token_spec,)
    return jax.shard_map(
        on_device,
        mesh=mesh,
        in_specs=placed,
        out_specs=(token_spec,) * 2 + (P("exp"),) * 2 + (rows,) * 7 + (expert,) * 3,
        check_vma=False,
    )
```

```python
import jax
import jax.numpy as jnp
from jax import lax
from jax.sharding import PartitionSpec as P
from jax.experimental import pallas as pl
from jax.experimental.pallas import tpu as pltpu

HEADS = 12
KV_HEADS = 4
HEAD_DIM = 128
TOPK = 6
GROUP = 3
BLOCK = 128
WIDTH = 1536
KV_WIDTH = KV_HEADS * HEAD_DIM
CAP = 48
N_EXP = 16
N_CTX = 8
LOCAL_E = 2
FF_E = 512
SHARED = 64
META = 128
HALF = 8
ROWS = HALF * CAP

epsilon = 1e-05
masked_score = -1e30
f32 = jnp.float32
bf16 = jnp.bfloat16
log2_e = 1.4426950408889634
score_scale = HEAD_DIM ** (-0.5) * log2_e

NN = (((1,), (0,)), ((), ()))
NT = (((1,), (1,)), ((), ()))
TN = (((0,), (0,)), ((), ()))


def dg(a, b, dims):
    return lax.dot_general(a, b, dims, preferred_element_type=f32)


def params(mib):
    return pltpu.CompilerParams(vmem_limit_bytes=mib * 1024 * 1024)


def cost(us):
    return pl.CostEstimate(flops=0, bytes_accessed=int(us * 3690000), transcendentals=0)


def whole(shape):
    return pl.BlockSpec(shape, lambda *_: (0,) * len(shape), pipeline_mode=pl.Buffered(1))


def sigmoid(v):
    return 1.0 / (1.0 + jnp.exp(-v))


def allowed_scores(ctx_at):
    rows = lax.broadcasted_iota(jnp.int32, (GROUP * BLOCK, N_CTX * BLOCK), 0) % BLOCK
    cols = lax.broadcasted_iota(jnp.int32, (GROUP * BLOCK, N_CTX * BLOCK), 1)
    return rows + ctx_at * BLOCK >= cols


def stack_heads(block):
    return jnp.concatenate([block[:, j * HEAD_DIM : (j + 1) * HEAD_DIM] for j in range(GROUP)], axis=0)


def unstack_heads(rows):
    return jnp.concatenate([rows[j * BLOCK : (j + 1) * BLOCK] for j in range(GROUP)], axis=1)


def attend_kernel(ctx_ref, q_ref, k_ref, v_ref, att_ref, attf_ref, log_ref):
    q = stack_heads(q_ref[...])
    keys = k_ref[...].reshape(N_CTX * BLOCK, HEAD_DIM)
    values = v_ref[...].reshape(N_CTX * BLOCK, HEAD_DIM)
    scores = jnp.where(allowed_scores(ctx_ref[0]), dg(q, keys, NT) * score_scale, masked_score)
    top = jnp.max(scores, axis=-1, keepdims=True)
    weights = jnp.exp2(scores - top)
    total = jnp.sum(weights, axis=-1, keepdims=True)
    out = dg(weights.astype(bf16), values, NN) * (1.0 / total)
    out = unstack_heads(out)
    attf_ref[...] = out
    att_ref[...] = out.astype(bf16)
    log_ref[...] = jnp.broadcast_to(top + jnp.log2(total), (GROUP * BLOCK, HEAD_DIM))


def kv_specs():
    return [
        pl.BlockSpec((N_CTX, BLOCK, HEAD_DIM), lambda g: (0, 0, g)),
        pl.BlockSpec((N_CTX, BLOCK, HEAD_DIM), lambda g: (0, 0, KV_HEADS + g)),
    ]


def head_spec():
    return pl.BlockSpec((BLOCK, GROUP * HEAD_DIM), lambda g: (0, g))


def attend(ctx_at, qkv, kv_all):
    return pl.pallas_call(
        attend_kernel,
        grid=(KV_HEADS,),
        in_specs=[pl.BlockSpec(memory_space=pltpu.SMEM), head_spec()] + kv_specs(),
        out_specs=[
            head_spec(),
            head_spec(),
            pl.BlockSpec((GROUP * BLOCK, HEAD_DIM), lambda g: (g, 0)),
        ],
        out_shape=[
            jax.ShapeDtypeStruct((BLOCK, WIDTH), bf16),
            jax.ShapeDtypeStruct((BLOCK, WIDTH), f32),
            jax.ShapeDtypeStruct((HEADS * BLOCK, HEAD_DIM), f32),
        ],
        cost_estimate=cost(6),
        compiler_params=params(48),
        name="attend",
    )(ctx_at, qkv, kv_all, kv_all)


SEQ = N_CTX * BLOCK
AT_QUERY, AT_MIXED, AT_OUT = SEQ, SEQ + BLOCK, SEQ + 2 * BLOCK
AT_SHARED = SEQ + 3 * BLOCK
AT_DOWN = AT_SHARED + 16 * N_EXP
AT_GAIN = AT_DOWN + 96
SENT_ROWS = AT_GAIN + 16


def halves(a, b, lane):
    low = jnp.where(lane < 64, a, pltpu.roll(b, 64, 1))
    high = jnp.where(lane < 64, pltpu.roll(a, 64, 1), b)
    return low, high


def attend_back_kernel(
    ctx_ref,
    q_ref,
    ga_ref,
    attf_ref,
    log_ref,
    k_ref,
    v_ref,
    all_ga_ref,
    extra_ref,
    gain_ref,
    dq_ref,
    near_ref,
    far_ref,
    kept_ref,
):
    group = pl.program_id(0)
    z_at = ctx_ref[0] // 4

    def send(dest, z, start, stop, rows):
        @pl.when(z_at == z)
        def _():
            near_ref[dest, start:stop] = rows

        @pl.when(z_at != z)
        def _():
            far_ref[dest, start:stop] = rows

    q = stack_heads(q_ref[...])
    grad = stack_heads(ga_ref[...])
    delta = jnp.sum(grad.astype(f32) * stack_heads(attf_ref[...]), axis=-1, keepdims=True)
    keys = k_ref[...].reshape(SEQ, HEAD_DIM)
    values = v_ref[...].reshape(SEQ, HEAD_DIM)
    scores = jnp.where(allowed_scores(ctx_ref[0]), dg(q, keys, NT) * score_scale, masked_score)
    weights = jnp.exp2(scores - log_ref[:, :1])
    grad_weights = dg(grad, values, NT)
    grad_raw = (weights * (grad_weights - delta)).astype(bf16)
    scale = HEAD_DIM ** (-0.5)
    dq = unstack_heads(dg(grad_raw, keys, NN) * scale)
    dq_ref[...] = dq.astype(bf16)
    kept_ref[group] = dq
    grad_k = dg(grad_raw, q, TN) * scale
    grad_v = dg(weights.astype(bf16), grad, TN)
    low, high = halves(grad_k, grad_v, lax.broadcasted_iota(jnp.int32, (SEQ, HEAD_DIM), 1))
    low, high = low.astype(bf16), high.astype(bf16)
    send(2 * (group % 2), group // 2, 0, SEQ, low)
    send(2 * (group % 2) + 1, group // 2, 0, SEQ, high)

    @pl.when(group == KV_HEADS - 1)
    def _():
        lane = lax.broadcasted_iota(jnp.int32, (BLOCK, HEAD_DIM), 1)

        def dq_tile(m):
            return kept_ref[m // GROUP, :, HEAD_DIM * (m % GROUP) : HEAD_DIM * (m % GROUP + 1)]

        def ga_tile(m):
            return all_ga_ref[:, HEAD_DIM * m : HEAD_DIM * (m + 1)].astype(f32)

        mixed = []
        for m in range(KV_HEADS):
            mixed += halves(dq_tile(N_CTX + m), ga_tile(N_CTX + m), lane)
        gains = gain_ref[...].astype(bf16)
        for c in range(N_CTX):
            tiles = [dq_tile(c).astype(bf16), mixed[c].astype(bf16), ga_tile(c).astype(bf16)]
            rows = jnp.concatenate(tiles + [extra_ref[c], gains], axis=0)
            send(c % 4, c // 4, AT_QUERY, SENT_ROWS, rows)


def attend_back(ctx_at, qkv, grad_att, att_f, logs, kv_all, grad_attn, extra, gain_rows):
    return pl.pallas_call(
        attend_back_kernel,
        grid=(KV_HEADS,),
        in_specs=[
            pl.BlockSpec(memory_space=pltpu.SMEM),
            head_spec(),
            head_spec(),
            head_spec(),
            pl.BlockSpec((GROUP * BLOCK, HEAD_DIM), lambda g: (g, 0)),
        ]
        + kv_specs()
        + [
            whole((BLOCK, WIDTH)),
            whole((N_CTX, AT_GAIN - AT_SHARED, HEAD_DIM)),
            whole((16, HEAD_DIM)),
        ],
        out_specs=[head_spec()] + [whole((4, SENT_ROWS, HEAD_DIM))] * 2,
        out_shape=[
            jax.ShapeDtypeStruct((BLOCK, WIDTH), bf16),
            jax.ShapeDtypeStruct((4, SENT_ROWS, HEAD_DIM), bf16),
            jax.ShapeDtypeStruct((4, SENT_ROWS, HEAD_DIM), bf16),
        ],
        scratch_shapes=[pltpu.VMEM((KV_HEADS, BLOCK, GROUP * HEAD_DIM), f32)],
        cost_estimate=cost(2),
        compiler_params=params(48),
        name="attend_back",
    )(ctx_at, qkv, grad_att, att_f, logs, kv_all, kv_all, grad_attn, extra, gain_rows)


def middle_kernel(att_ref, w_ref, x_ref, gain_ref, middle_ref, hidden_ref):
    middle = x_ref[...].astype(f32) + dg(att_ref[...], w_ref[...], NN)
    inv = lax.rsqrt(jnp.mean(middle * middle, axis=-1, keepdims=True) + epsilon)
    middle_ref[...] = middle
    hidden_ref[...] = (middle * inv * gain_ref[...]).astype(bf16)


def w_cols(width, at):
    return pl.BlockSpec((WIDTH, width), lambda *_: (0, at), pipeline_mode=pl.Buffered(1))


def middle_norm(attended, w_all, tokens, gain):
    return pl.pallas_call(
        middle_kernel,
        grid=(1,),
        in_specs=[
            whole((BLOCK, WIDTH)),
            w_cols(WIDTH, 1),
            whole((BLOCK, WIDTH)),
            whole((1, WIDTH)),
        ],
        out_specs=[whole((BLOCK, WIDTH)), whole((BLOCK, WIDTH))],
        out_shape=[
            jax.ShapeDtypeStruct((BLOCK, WIDTH), f32),
            jax.ShapeDtypeStruct((BLOCK, WIDTH), bf16),
        ],
        cost_estimate=cost(2),
        compiler_params=params(32),
        name="middle_norm",
    )(attended, w_all, tokens, gain)


def norm_back(grad_normed, normed, inv_root):
    return inv_root * (
        grad_normed - normed * jnp.mean(grad_normed * normed, axis=-1, keepdims=True)
    )


def middle_back_kernel(
    pieces_ref, middle_ref, up_ref, gain_ref, w_ref, gm_ref, ga_ref, gh_ref, gg_ref
):
    grad_two = pieces_ref[0].astype(f32)
    for i in range(1, HALF):
        grad_two = grad_two + pieces_ref[i].astype(f32)
    middle = middle_ref[...]
    inv = lax.rsqrt(jnp.mean(middle * middle, axis=-1, keepdims=True) + epsilon)
    normed = middle * inv
    gains = jnp.sum(grad_two * normed, axis=0, keepdims=True)
    gg_ref[...] = jnp.zeros((16, HEAD_DIM), f32)
    for m in range(HEADS):
        gg_ref[m : m + 1] = gains[:, HEAD_DIM * m : HEAD_DIM * (m + 1)]
    grad_middle = up_ref[...].astype(f32) + norm_back(grad_two * gain_ref[...], normed, inv)
    gm_ref[...] = grad_middle
    grad_attn = grad_middle.astype(bf16)
    ga_ref[...] = grad_attn
    gh_ref[...] = dg(grad_attn, w_ref[...], NT).astype(bf16)


def middle_back(pieces, middle, upstream, gain, w_all):
    return pl.pallas_call(
        middle_back_kernel,
        grid=(1,),
        in_specs=[
            whole((HALF, BLOCK, WIDTH)),
            whole((BLOCK, WIDTH)),
            whole((BLOCK, WIDTH)),
            whole((1, WIDTH)),
            w_cols(WIDTH, 1),
        ],
        out_specs=[whole((BLOCK, WIDTH))] * 3 + [whole((16, HEAD_DIM))],
        out_shape=[
            jax.ShapeDtypeStruct((BLOCK, WIDTH), f32),
            jax.ShapeDtypeStruct((BLOCK, WIDTH), bf16),
            jax.ShapeDtypeStruct((BLOCK, WIDTH), bf16),
            jax.ShapeDtypeStruct((16, HEAD_DIM), f32),
        ],
        cost_estimate=cost(1),
        compiler_params=params(48),
        name="middle_back",
    )(pieces, middle, upstream, gain, w_all)


def place_kernel(
    at_ref, up_ref, down_ref, sdown_ref, place_ref, geo_ref, geh_ref, gsh_ref, gate_ref
):
    lane = lax.broadcasted_iota(jnp.int32, (BLOCK, META), 1)
    row = lax.broadcasted_iota(jnp.int32, (BLOCK, META), 0)
    before = (row > lane).astype(bf16)
    slot = (lane % 64).astype(f32)
    first_id = (at_ref[0] * LOCAL_E).astype(f32)
    row_id = first_id + (row >= 64).astype(f32)

    for chip in range(HALF):
        meta = up_ref[chip, 0, :, WIDTH:].astype(f32)
        named = lane < TOPK
        zero = jnp.zeros((BLOCK, META), f32)
        hit0 = jnp.where(named & (meta == first_id), 1.0, zero)
        hit1 = jnp.where(named & (meta == first_id + 1.0), 1.0, zero)
        mask = jnp.where(
            lane < 64,
            jnp.sum(hit0, axis=1, keepdims=True),
            jnp.sum(hit1, axis=1, keepdims=True),
        )
        rank = dg(before, mask.astype(bf16), NN)
        place = jnp.where((mask > 0.5) & (rank == slot), 1.0, zero).astype(bf16)
        place_ref[chip, 0] = place
        rows = dg(place, up_ref[chip, 0], TN)
        slot_meta = rows[:, WIDTH:]
        gates = pltpu.roll(slot_meta, META - TOPK, 1) + pltpu.roll(
            slot_meta, META - 2 * TOPK, 1
        )
        gate = jnp.sum(
            jnp.where(named & (slot_meta == row_id), gates, zero), axis=1, keepdims=True
        )
        geo = (gate * rows[:, :WIDTH]).astype(bf16)
        wide_gate = jnp.broadcast_to(gate, (BLOCK, META))
        at = chip * CAP
        for e in range(LOCAL_E):
            geo_ref[e, 0, at : at + CAP] = geo[64 * e : 64 * e + CAP]
            gate_ref[e, 0, at : at + CAP] = wide_gate[64 * e : 64 * e + CAP]
        gsh_ref[chip, 0] = dg(up_ref[chip, 0, :, :WIDTH], sdown_ref[...], NT)
    for e in range(LOCAL_E):
        geh_ref[e, 0] = dg(geo_ref[e, 0], down_ref[e], NT)


def by_core(cols):
    return pl.BlockSpec(
        (HALF, 1, BLOCK, cols),
        lambda s, at: (0, jnp.where(s == 0, 1 - at[0] % 2, at[0] % 2), 0, 0),
    )


def by_step(cols):
    return pl.BlockSpec((LOCAL_E, 1, ROWS, cols), lambda s, at: (0, s, 0, 0))


def place_rows(exp_at, up_all, expert_down, shared_two):
    return pl.pallas_call(
        place_kernel,
        grid_spec=pltpu.PrefetchScalarGridSpec(
            num_scalar_prefetch=1,
            grid=(2,),
            in_specs=[
                by_core(WIDTH + META),
                whole((LOCAL_E, FF_E, WIDTH)),
                whole((2 * SHARED, WIDTH)),
            ],
            out_specs=[by_core(META), by_step(WIDTH), by_step(FF_E), by_core(META), by_step(META)],
        ),
        out_shape=[
            jax.ShapeDtypeStruct((HALF, 2, BLOCK, META), bf16),
            jax.ShapeDtypeStruct((LOCAL_E, 2, ROWS, WIDTH), bf16),
            jax.ShapeDtypeStruct((LOCAL_E, 2, ROWS, FF_E), f32),
            jax.ShapeDtypeStruct((HALF, 2, BLOCK, META), f32),
            jax.ShapeDtypeStruct((LOCAL_E, 2, ROWS, META), f32),
        ],
        cost_estimate=cost(14),
        compiler_params=params(56),
        name="place_rows",
    )(exp_at, up_all, expert_down, shared_two)


def expert_kernel(
    at_ref,
    hid_ref,
    place_ref,
    geh_ref,
    gsh_ref,
    wg_ref,
    wu_ref,
    ws_ref,
    part_ref,
    x_ref,
    act_ref,
    dgu_ref,
    sact_ref,
    sgrad_ref,
):
    for chip in range(HALF):
        rows = dg(place_ref[chip, 0], hid_ref[chip, 0], TN).astype(bf16)
        at = chip * CAP
        for e in range(LOCAL_E):
            x_ref[e, 0, at : at + CAP] = rows[64 * e : 64 * e + CAP]
    pairs = []
    for e in range(LOCAL_E):
        pre_gate = dg(x_ref[e, 0], wg_ref[e], NN)
        pre_up = dg(x_ref[e, 0], wu_ref[e], NN)
        sig = sigmoid(pre_gate)
        act = pre_gate * sig
        act_ref[e, 0] = (act * pre_up).astype(bf16)
        geh = geh_ref[e, 0]
        d_gate = (geh * pre_up * (sig * (1.0 + pre_gate * (1.0 - sig)))).astype(bf16)
        d_up = (geh * act).astype(bf16)
        dgu_ref[e, 0, :, :FF_E] = d_gate
        dgu_ref[e, 0, :, FF_E:] = d_up
        pairs.append((dg(d_gate, wg_ref[e], NT) + dg(d_up, wu_ref[e], NT)).astype(bf16))
    lane = lax.broadcasted_iota(jnp.int32, (BLOCK, 2 * SHARED), 1) < SHARED
    gap = jnp.zeros((64 - CAP, WIDTH), bf16)
    for chip in range(HALF):
        pre = dg(hid_ref[chip, 0], ws_ref[...], NN)
        turned = pltpu.roll(pre, SHARED, 1)
        gate, up = jnp.where(lane, pre, turned), jnp.where(lane, turned, pre)
        sig = sigmoid(gate)
        act = gate * sig
        sact_ref[chip, 0] = jnp.where(lane, act * up, 0.0).astype(bf16)
        slope = sig * (1.0 + gate * (1.0 - sig))
        sgrad = (gsh_ref[chip, 0] * jnp.where(lane, up * slope, act)).astype(bf16)
        sgrad_ref[chip, 0] = sgrad
        at = chip * CAP
        stacked = jnp.concatenate([pairs[0][at : at + CAP], gap, pairs[1][at : at + CAP], gap], 0)
        part_ref[0, chip] = (
            dg(place_ref[chip, 0], stacked, NN) + dg(sgrad, ws_ref[...], NT)
        ).astype(bf16)


def expert_back(exp_at, hidden, place, geh, gsh, wg, wu, ws):
    return pl.pallas_call(
        expert_kernel,
        grid_spec=pltpu.PrefetchScalarGridSpec(
            num_scalar_prefetch=1,
            grid=(2,),
            in_specs=[
                by_core(WIDTH),
                by_core(META),
                by_step(FF_E),
                by_core(META),
                whole((LOCAL_E, WIDTH, FF_E)),
                whole((LOCAL_E, WIDTH, FF_E)),
                whole((WIDTH, 2 * SHARED)),
            ],
            out_specs=[
                pl.BlockSpec((1, HALF, BLOCK, WIDTH), lambda s, at: (s, 0, 0, 0)),
                by_step(WIDTH),
                by_step(FF_E),
                by_step(2 * FF_E),
                by_core(META),
                by_core(META),
            ],
        ),
        out_shape=[
            jax.ShapeDtypeStruct((2, HALF, BLOCK, WIDTH), bf16),
            jax.ShapeDtypeStruct((LOCAL_E, 2, ROWS, WIDTH), bf16),
            jax.ShapeDtypeStruct((LOCAL_E, 2, ROWS, FF_E), bf16),
            jax.ShapeDtypeStruct((LOCAL_E, 2, ROWS, 2 * FF_E), bf16),
            jax.ShapeDtypeStruct((HALF, 2, BLOCK, META), bf16),
            jax.ShapeDtypeStruct((HALF, 2, BLOCK, META), bf16),
        ],
        cost_estimate=cost(28),
        compiler_params=params(60),
        name="expert_back",
    )(exp_at, hidden, place, geh, gsh, wg, wu, ws)


def output_kernel(at_ref, act_ref, gate_ref, place_ref, sact_ref, wd_ref, sd_ref, part_ref):
    outs = []
    for e in range(LOCAL_E):
        out = dg(act_ref[e, 0], wd_ref[e], NN).astype(bf16).astype(f32)
        outs.append((out * gate_ref[e, 0, :, :1]).astype(bf16))
    gap = jnp.zeros((64 - CAP, WIDTH), bf16)
    for chip in range(HALF):
        at = chip * CAP
        stacked = jnp.concatenate([outs[0][at : at + CAP], gap, outs[1][at : at + CAP], gap], 0)
        part_ref[0, chip] = (
            dg(place_ref[chip, 0], stacked, NN) + dg(sact_ref[chip, 0], sd_ref[...], NN)
        ).astype(bf16)


def expert_output(exp_at, act, gate, place, sact, wd, sd):
    return pl.pallas_call(
        output_kernel,
        grid_spec=pltpu.PrefetchScalarGridSpec(
            num_scalar_prefetch=1,
            grid=(2,),
            in_specs=[
                by_step(FF_E),
                by_step(META),
                by_core(META),
                by_core(META),
                whole((LOCAL_E, FF_E, WIDTH)),
                whole((2 * SHARED, WIDTH)),
            ],
            out_specs=pl.BlockSpec((1, HALF, BLOCK, WIDTH), lambda s, at: (s, 0, 0, 0)),
        ),
        out_shape=jax.ShapeDtypeStruct((2, HALF, BLOCK, WIDTH), bf16),
        cost_estimate=cost(2),
        compiler_params=params(48),
        name="expert_output",
    )(exp_at, act, gate, place, sact, wd, sd)


SHARE = 3 * BLOCK
TO_SHARED = SEQ + 2 * SHARE
TO_DOWN = TO_SHARED + 16 * N_EXP
TO_GAIN = TO_DOWN + 96
MERGED_ROWS = TO_GAIN + 16


def merge_kernel(ctx_ref, near_ref, got_ref, out_ref):
    z_at = ctx_ref[0] // 4
    near, got = near_ref[0], got_ref[0]

    def add(a, b):
        return (a.astype(f32) + b.astype(f32)).astype(bf16)

    out_ref[0, :SEQ] = add(near[:SEQ], got[:SEQ])
    out_ref[0, TO_SHARED:] = add(near[AT_SHARED:], got[AT_SHARED:])
    mine, theirs = near[AT_QUERY:AT_SHARED], got[AT_QUERY:AT_SHARED]
    out_ref[0, SEQ : SEQ + SHARE] = jnp.where(z_at == 0, mine, theirs)
    out_ref[0, SEQ + SHARE : TO_SHARED] = jnp.where(z_at == 0, theirs, mine)


def merge_shares(ctx_at, near, got):
    spec = pl.BlockSpec((1, SENT_ROWS, HEAD_DIM), lambda i: (i, 0, 0))
    return pl.pallas_call(
        merge_kernel,
        grid=(4,),
        in_specs=[pl.BlockSpec(memory_space=pltpu.SMEM), spec, spec],
        out_specs=pl.BlockSpec((1, MERGED_ROWS, HEAD_DIM), lambda i: (i, 0, 0)),
        out_shape=jax.ShapeDtypeStruct((4, MERGED_ROWS, HEAD_DIM), bf16),
        cost_estimate=cost(3),
        compiler_params=params(32),
        name="merge_shares",
    )(ctx_at, near, got)


def columns_kernel(got_ref, hidden_ref, att_ref, sent_ref, kv_ref, down_ref):
    def summed(start, stop):
        out = got_ref[0, start:stop].astype(f32)
        for src in range(1, 4):
            out = out + got_ref[src, start:stop].astype(f32)
        return out

    grad_kv = summed(0, SEQ).astype(bf16)
    kv_ref[...] = grad_kv.reshape(N_CTX, BLOCK, HEAD_DIM)

    def rows_of(tile, order):
        at = SEQ + BLOCK * tile
        return jnp.concatenate(
            [got_ref[y, at + SHARE * z : at + SHARE * z + BLOCK] for z, y in order], axis=0
        )

    in_order = [(i // 4, i % 4) for i in range(N_CTX)]
    y_order = [(i % 2, i // 2) for i in range(N_CTX)]
    lane = lax.broadcasted_iota(jnp.int32, (SEQ, HEAD_DIM), 1)
    zero = jnp.zeros((SEQ, HEAD_DIM), bf16)
    mixed_q = jnp.where(lane < 64, rows_of(1, in_order), zero)
    mixed_o = jnp.where(lane < 64, zero, rows_of(1, y_order))
    left = jnp.concatenate([rows_of(0, in_order).T, mixed_q.T, grad_kv.T], axis=0)
    right = jnp.concatenate([mixed_o.T, rows_of(2, y_order).T], axis=0)
    by_hidden = dg(left, hidden_ref[...].reshape(SEQ, WIDTH), NN)
    by_att = dg(right, att_ref[...].reshape(SEQ, WIDTH), NN)
    tiles = [
        by_hidden[:BLOCK],
        by_hidden[BLOCK : 2 * BLOCK] + by_att[:BLOCK],
        by_att[BLOCK:],
        by_hidden[2 * BLOCK :],
    ]
    for t, tile in enumerate(tiles):
        sent_ref[:, :96, HEAD_DIM * t : HEAD_DIM * (t + 1)] = (
            tile.T.astype(bf16).reshape(N_EXP, 96, HEAD_DIM)
        )

    down_ref[...] = summed(TO_DOWN, TO_GAIN).astype(bf16)
    shared = summed(TO_SHARED, TO_DOWN)
    gains = summed(TO_GAIN, MERGED_ROWS)
    row = lax.broadcasted_iota(jnp.int32, (16, HEAD_DIM), 0)
    one_lane = lax.broadcasted_iota(jnp.int32, (1, HEAD_DIM), 1)
    for i in range(N_EXP):
        m, offset = (96 * i) // HEAD_DIM, (96 * i) % HEAD_DIM
        gain = gains[m : m + 1]
        if offset:
            shift = HEAD_DIM - offset
            gain = jnp.where(
                one_lane < shift,
                pltpu.roll(gain, shift, 1),
                pltpu.roll(gains[m + 1 : m + 2], shift, 1),
            )
        rows = jnp.where(row == 12, jnp.broadcast_to(gain, (16, HEAD_DIM)), shared[16 * i : 16 * i + 16])
        sent_ref[i, 96:, :HEAD_DIM] = rows.astype(bf16)
        sent_ref[i, 96:, HEAD_DIM:] = jnp.zeros((16, 512 - HEAD_DIM), bf16)


def column_grads(got, hidden_seq, att_seq):
    return pl.pallas_call(
        columns_kernel,
        out_shape=[
            jax.ShapeDtypeStruct((N_EXP, 112, 512), bf16),
            jax.ShapeDtypeStruct((N_CTX, BLOCK, HEAD_DIM), bf16),
            jax.ShapeDtypeStruct((96, HEAD_DIM), bf16),
        ],
        cost_estimate=cost(8),
        compiler_params=params(56),
        name="column_grads",
    )(got, hidden_seq, att_seq)


OWNED_ROWS = 4 * 96 + 16 * N_EXP + 96


def owned_kernel(got_ref, down_ref, owned_ref, gain_ref):
    total = got_ref[0, :96].astype(f32)
    gains = got_ref[0, 96:, :HEAD_DIM].astype(f32)
    for src in range(1, N_EXP):
        total = total + got_ref[src, :96].astype(f32)
        gains = gains + got_ref[src, 96:, :HEAD_DIM].astype(f32)
    gain_ref[...] = gains
    for t in range(4):
        owned_ref[96 * t : 96 * t + 96] = total[:, HEAD_DIM * t : HEAD_DIM * (t + 1)].astype(bf16)
    for src in range(N_EXP):
        at = 384 + 16 * src
        owned_ref[at : at + 16] = got_ref[src, 96:, :HEAD_DIM]
    owned_ref[384 + 16 * N_EXP :] = down_ref[...]


def owned_sums(got, down):
    return pl.pallas_call(
        owned_kernel,
        out_shape=[
            jax.ShapeDtypeStruct((OWNED_ROWS, HEAD_DIM), bf16),
            jax.ShapeDtypeStruct((16, HEAD_DIM), f32),
        ],
        cost_estimate=cost(3),
        compiler_params=params(32),
        name="owned_sums",
    )(got, down)


def finish_kernel(
    got_ref,
    gain_in_ref,
    wq_ref,
    wk_ref,
    wv_ref,
    gain_ref,
    q_ref,
    k_ref,
    v_ref,
    out_ref,
    sg_ref,
    su_ref,
    sd_ref,
):
    lane = lax.broadcasted_iota(jnp.int32, (96, HEAD_DIM), 1)

    def tile(c, t):
        at = BLOCK + 96 * t
        return got_ref[c, at : at + 96].astype(f32)

    for c in range(N_CTX):
        at = HEAD_DIM * c
        q_ref[:, at : at + HEAD_DIM] = tile(c, 0)
        out_ref[:, at : at + HEAD_DIM] = tile(c, 2)
    for m in range(N_CTX // 2):
        at = HEAD_DIM * m
        low, high = halves(tile(2 * m, 1), tile(2 * m + 1, 1), lane)
        q_ref[:, 1024 + at : 1024 + at + HEAD_DIM] = low
        out_ref[:, 1024 + at : 1024 + at + HEAD_DIM] = high
        low, high = halves(tile(2 * m, 3), tile(2 * m + 1, 3), lane)
        k_ref[:, at : at + HEAD_DIM] = low
        v_ref[:, at : at + HEAD_DIM] = high
    gain = (
        jnp.sum(q_ref[...] * wq_ref[...].astype(f32), axis=1, keepdims=True)
        + jnp.sum(k_ref[...] * wk_ref[...].astype(f32), axis=1, keepdims=True)
        + jnp.sum(v_ref[...] * wv_ref[...].astype(f32), axis=1, keepdims=True)
    ) / gain_in_ref[...]
    gain_ref[...] = jnp.broadcast_to(gain, (96, HEAD_DIM))
    row = lax.broadcasted_iota(jnp.int32, (96, HEAD_DIM), 0)
    picks = jnp.where((lane % 16 < 12) & (row == 12 * (lane // 16) + lane % 16), 1.0, 0.0)
    picks = picks.astype(bf16)

    def shared_tile(j):
        at = BLOCK + 384 + 16 * j
        rows = jnp.concatenate([got_ref[c, at : at + 16] for c in range(N_CTX)], axis=0)
        return dg(picks, rows, NN)

    for m in range(N_EXP // 2):
        at = HEAD_DIM * m
        low, high = halves(shared_tile(2 * m), shared_tile(2 * m + 1), lane)
        sg_ref[:, at : at + HEAD_DIM] = low
        su_ref[:, at : at + HEAD_DIM] = high
    for c in range(N_CTX):
        rows = got_ref[c, BLOCK + 384 + 16 * N_EXP :].astype(f32)
        for m in range(HEADS):
            sd_ref[8 * c : 8 * c + 8, HEAD_DIM * m : HEAD_DIM * (m + 1)] = rows[8 * m : 8 * m + 8]


def finish(got, gain_column, query_weight, key_weight, value_weight):
    shapes = [(96, 128), (96, 1536), (96, 512), (96, 512), (96, 1536), (96, 1024), (96, 1024)]
    return pl.pallas_call(
        finish_kernel,
        out_shape=[jax.ShapeDtypeStruct(s, f32) for s in shapes + [(SHARED, WIDTH)]],
        cost_estimate=cost(4),
        compiler_params=params(32),
        name="finish",
    )(got, gain_column, query_weight, key_weight, value_weight)


def input_kernel(dq_ref, got_ref, wq_ref, wkv_ref, x_ref, gain_ref, gm_ref, out_ref):
    lane = lax.broadcasted_iota(jnp.int32, (BLOCK, HEAD_DIM), 1)
    lows, highs = [], []
    for m in range(KV_HEADS):
        low, high = halves(got_ref[2 * m].astype(f32), got_ref[2 * m + 1].astype(f32), lane)
        lows.append(low.astype(bf16))
        highs.append(high.astype(bf16))
    grad_kv = jnp.concatenate(lows + highs, axis=1)
    grad_one = dg(dq_ref[...], wq_ref[...], NT) + dg(grad_kv, wkv_ref[...], NT)
    inputs = x_ref[...].astype(f32)
    inv = lax.rsqrt(jnp.mean(inputs * inputs, axis=-1, keepdims=True) + epsilon)
    out_ref[...] = (gm_ref[...] + norm_back(grad_one * gain_ref[...], inputs * inv, inv)).astype(bf16)


def input_back(grad_query, grad_kv, w_all, tokens, gain, grad_middle):
    return pl.pallas_call(
        input_kernel,
        grid=(1,),
        in_specs=[
            whole((BLOCK, WIDTH)),
            whole((N_CTX, BLOCK, HEAD_DIM)),
            w_cols(WIDTH, 0),
            w_cols(2 * KV_WIDTH, 3),
            whole((BLOCK, WIDTH)),
            whole((1, WIDTH)),
            whole((BLOCK, WIDTH)),
        ],
        out_specs=whole((BLOCK, WIDTH)),
        out_shape=jax.ShapeDtypeStruct((BLOCK, WIDTH), bf16),
        cost_estimate=cost(7),
        compiler_params=params(48),
        name="input_back",
    )(grad_query, grad_kv, w_all, w_all, tokens, gain, grad_middle)


def norm_rows_kernel(x_ref, gain_ref, out_ref):
    inputs = x_ref[0].astype(f32)
    inv = lax.rsqrt(jnp.mean(inputs * inputs, axis=-1, keepdims=True) + epsilon)
    out_ref[0] = (inputs * inv * gain_ref[...]).astype(bf16)


def norm_rows(rows, gain):
    count = rows.shape[0]
    spec = pl.BlockSpec((1, BLOCK, WIDTH), lambda i: (i, 0, 0))
    turned = pl.BlockSpec((1, BLOCK, WIDTH), lambda i: ((i % 2) * 4 + i // 2, 0, 0))
    return pl.pallas_call(
        norm_rows_kernel,
        grid=(count,),
        in_specs=[spec, whole((1, WIDTH))],
        out_specs=spec if count == 1 else turned,
        out_shape=jax.ShapeDtypeStruct(rows.shape, bf16),
        cost_estimate=cost(2),
        compiler_params=params(32),
        name="norm_rows",
    )(rows, gain)


def project_kernel(own_ref, seq_ref, w_ref, q_ref, kv_ref):
    step = pl.program_id(0)

    @pl.when(step < 3)
    def _():
        q_ref[...] = dg(own_ref[0], w_ref[...], NN).astype(bf16)

    @pl.when(step >= 3)
    def _():
        rows = seq_ref[...].reshape(N_CTX * BLOCK, WIDTH)
        kv_ref[...] = dg(rows, w_ref[...], NN).astype(bf16).reshape(N_CTX, BLOCK, KV_WIDTH)


def project(own, seq, w_all):
    return pl.pallas_call(
        project_kernel,
        grid=(5,),
        in_specs=[
            whole((1, BLOCK, WIDTH)),
            whole((N_CTX, BLOCK, WIDTH)),
            pl.BlockSpec((WIDTH, KV_WIDTH), lambda i: (0, jnp.where(i < 3, i, i + 3))),
        ],
        out_specs=[
            pl.BlockSpec((BLOCK, KV_WIDTH), lambda i: (0, jnp.minimum(i, 2))),
            pl.BlockSpec((N_CTX, BLOCK, KV_WIDTH), lambda i: (0, 0, jnp.maximum(i - 3, 0))),
        ],
        out_shape=[
            jax.ShapeDtypeStruct((BLOCK, WIDTH), bf16),
            jax.ShapeDtypeStruct((N_CTX, BLOCK, 2 * KV_WIDTH), bf16),
        ],
        cost_estimate=cost(8),
        compiler_params=params(48),
        name="project",
    )(own, seq, w_all)


PIECE = 2 * WIDTH + WIDTH * BLOCK // HEAD_DIM


def spread_kernel(at_ref, own_ref, low_ref, high_ref, *outs):
    chip = (at_ref[0] >> 1) ^ pl.program_id(0)
    got = jnp.where(chip < 4, low_ref[0], high_ref[0])
    total = (own_ref[0, 0].astype(f32) + got.astype(f32)).astype(bf16)
    for k in range(HALF):

        @pl.when(pl.program_id(0) == k)
        def _():
            outs[k // 2][k % 2] = total


def spread_sums(exp_at, parts, low, high):
    half = pl.BlockSpec((1, BLOCK, WIDTH), lambda k, at: (((at[0] >> 1) ^ k) & 3, 0, 0))
    return pl.pallas_call(
        spread_kernel,
        grid_spec=pltpu.PrefetchScalarGridSpec(
            num_scalar_prefetch=1,
            grid=(HALF,),
            in_specs=[
                pl.BlockSpec((1, 1, BLOCK, WIDTH), lambda k, at: (1, (at[0] >> 1) ^ k, 0, 0)),
                half,
                half,
            ],
            out_specs=[whole((2, BLOCK, WIDTH))] * 4,
        ),
        out_shape=[jax.ShapeDtypeStruct((2, BLOCK, WIDTH), bf16)] * 4,
        cost_estimate=cost(4),
        compiler_params=params(32),
        name="spread_sums",
    )(exp_at, parts, low, high)


def of_step(values, step):
    out = jnp.int32(values[0])
    for i, value in enumerate(values[1:], 1):
        out = jnp.where(step == i, value, out)
    return out


def expert_weights_kernel(halved, at_ref, x_ref, geo_ref, act_ref, dgate_ref, dup_ref, *outs):
    step = pl.program_id(0)
    rhs = jnp.concatenate([dgate_ref[0], dup_ref[0]], axis=1)
    both = dg(x_ref[0], rhs, TN).astype(bf16)
    down = dg(act_ref[0], geo_ref[0], TN).astype(bf16)
    for i in range(4):

        @pl.when(step == i)
        def _():
            start = (i % 2) * PIECE if halved else 0
            out = outs[i // 2 if halved else i].at[pl.ds(start, PIECE)]
            out[:WIDTH] = both[:, :HEAD_DIM]
            out[WIDTH : 2 * WIDTH] = both[:, HEAD_DIM:]
            for m in range(WIDTH // HEAD_DIM):
                at = 2 * WIDTH + m * BLOCK
                out[at : at + BLOCK] = down[:, m * HEAD_DIM : (m + 1) * HEAD_DIM]


def expert_weights(ctx_at, steps, halved, arrived, grad_eo, act, grad_gu):
    rows = 2 * ROWS

    def expert(s, at):
        return (at[0] >> 2) ^ of_step([side for _, side in steps], s)

    def lanes(shift):
        return pl.BlockSpec(
            (1, rows, HEAD_DIM),
            lambda s, at: (
                expert(s, at),
                0,
                shift + ((at[0] & 3) ^ of_step([r for r, _ in steps], s)),
            ),
        )

    rows_of = pl.BlockSpec((1, rows, WIDTH), lambda s, at: (expert(s, at), 0, 0))
    count, length = (2, 2 * PIECE) if halved else (4, PIECE)
    return pl.pallas_call(
        lambda *refs: expert_weights_kernel(halved, *refs),
        grid_spec=pltpu.PrefetchScalarGridSpec(
            num_scalar_prefetch=1,
            grid=(4,),
            in_specs=[rows_of, rows_of, lanes(0), lanes(0), lanes(4)],
            out_specs=[whole((length, HEAD_DIM))] * count,
        ),
        out_shape=[jax.ShapeDtypeStruct((length, HEAD_DIM), bf16)] * count,
        cost_estimate=cost(2),
        compiler_params=params(56),
        name="expert_weights",
    )(ctx_at, arrived, grad_eo, act, grad_gu, grad_gu)


def unpack_kernel(count, at_ref, *refs):
    pieces, (gate_ref, up_ref, down_ref) = refs[:count], refs[-3:]
    step = pl.program_id(0)
    for i in range(count):

        @pl.when(step == i)
        def _():
            piece = pieces[i]
            gate_ref[0] = piece[:WIDTH].astype(f32)
            up_ref[0] = piece[WIDTH : 2 * WIDTH].astype(f32)
            for m in range(WIDTH // HEAD_DIM):
                at = 2 * WIDTH + m * BLOCK
                down_ref[0, :, m * HEAD_DIM : (m + 1) * HEAD_DIM] = piece[at : at + BLOCK].astype(
                    f32
                )


def unpack_experts(ctx_at, steps, pieces, filled=()):
    count = len(steps)

    def expert(s, at):
        return (at[0] >> 2) ^ of_step([side for _, side in steps], s)

    def units(s, at):
        return (at[0] & 3) ^ of_step([r for r, _ in steps], s)

    cols = pl.BlockSpec((1, WIDTH, HEAD_DIM), lambda s, at: (expert(s, at), 0, units(s, at)))
    rows = pl.BlockSpec((1, BLOCK, WIDTH), lambda s, at: (expert(s, at), units(s, at), 0))
    anywhere = pl.BlockSpec(memory_space=pl.ANY)
    return pl.pallas_call(
        lambda *refs: unpack_kernel(count, *refs),
        grid_spec=pltpu.PrefetchScalarGridSpec(
            num_scalar_prefetch=1,
            grid=(count,),
            in_specs=[whole((PIECE, HEAD_DIM))] * count + [anywhere] * len(filled),
            out_specs=[cols, cols, rows],
        ),
        out_shape=[
            jax.ShapeDtypeStruct((LOCAL_E, WIDTH, FF_E), f32),
            jax.ShapeDtypeStruct((LOCAL_E, WIDTH, FF_E), f32),
            jax.ShapeDtypeStruct((LOCAL_E, FF_E, WIDTH), f32),
        ],
        input_output_aliases={1 + count + i: i for i in range(len(filled))},
        cost_estimate=cost(2 * count),
        compiler_params=params(48),
        name="unpack_experts",
    )(ctx_at, *pieces, *filled)


def relay_kernel(
    p0, p1, p3, p6, relay_a, relay_b, got_10, got_31, add_a, add_b, part_0, part_1
):
    add_a[...] = (p6[...].astype(f32) + relay_a[...].astype(f32)).astype(bf16)
    add_b[...] = (p3[...].astype(f32) + relay_b[...].astype(f32)).astype(bf16)
    part_0[...] = p0[...].astype(f32) + got_10[...].astype(f32)
    part_1[...] = p1[...].astype(f32) + got_31[...].astype(f32)


def side_kernel(part_0, part_1, got_11, got_30, own, side):
    own[...] = part_0[...] + got_30[...].astype(f32)
    side[...] = (part_1[...] + got_11[...].astype(f32)).astype(bf16)


def piece_sums(kernel, kinds, *pieces):
    specs, arrays = [], []
    for piece in pieces:
        array, second = piece if isinstance(piece, tuple) else (piece, 0)
        specs.append(pl.BlockSpec((PIECE // 4, HEAD_DIM), lambda i, at=4 * second: (i + at, 0)))
        arrays.append(array)
    return pl.pallas_call(
        kernel,
        grid=(4,),
        in_specs=specs,
        out_specs=[pl.BlockSpec((PIECE // 4, HEAD_DIM), lambda i: (i, 0))] * len(kinds),
        out_shape=[jax.ShapeDtypeStruct((PIECE, HEAD_DIM), kind) for kind in kinds],
        cost_estimate=cost(1),
        compiler_params=params(32),
        name="piece_sums",
    )(*arrays)


same_core = [[2 * i + c for i in range(8)] for c in range(2)]
core_swap = [(i, i ^ 1) for i in range(N_EXP)]
y_groups = [[0, 1, 2, 3], [4, 5, 6, 7]]
z_swap = [(i, i ^ 4) for i in range(N_CTX)]


def swap_all(rows, axis, groups=None):
    return lax.all_to_all(
        rows, axis, split_axis=0, concat_axis=0, tiled=True, axis_index_groups=groups
    )


def after(value, *others):
    return lax.optimization_barrier((value,) + others)[0]


def add_low(a, b):
    return (a.astype(f32) + b.astype(f32)).astype(bf16)


def on_device(
    tokens,
    routes,
    route_gates,
    norm_attn,
    norm_ffn,
    query_weight,
    key_weight,
    value_weight,
    out_weight,
    shared_gate,
    shared_up,
    shared_down,
    expert_gate,
    expert_up,
    expert_down,
    cotangent,
):
    exp_at = lax.axis_index("exp").astype(jnp.int32)
    ctx_at = lax.axis_index("ctx").astype(jnp.int32)
    exp_s, ctx_s = exp_at.reshape(1), ctx_at.reshape(1)

    z_at = ctx_at // 4

    w_cat = jnp.concatenate([query_weight, out_weight, key_weight, value_weight], axis=1)
    w_all = lax.all_gather(w_cat, "exp", axis=0, tiled=True)
    gates_high = route_gates[0].astype(bf16)
    gates_low = (route_gates[0] - gates_high.astype(f32)).astype(bf16)
    pad = jnp.zeros((BLOCK, META - 3 * TOPK), bf16)
    up_meta = jnp.concatenate(
        [cotangent[0], routes[0].astype(bf16), gates_high, gates_low, pad], axis=1
    )
    up_all = lax.all_gather(after(up_meta, w_cat), "exp", axis=0, tiled=True)
    gains = after(jnp.concatenate([norm_attn, norm_ffn]), w_cat)
    gains = swap_all(jnp.broadcast_to(gains, (N_EXP, gains.shape[0])), "exp")
    gain_attn = gains[:, :96].reshape(1, WIDTH).astype(f32)
    gain_ffn = gains[:, 96:].reshape(1, WIDTH).astype(f32)

    def of_sequence(rows):
        other = lax.ppermute(rows, "ctx", z_swap)
        pair = jnp.where(
            z_at == 0,
            jnp.concatenate([rows, other], axis=0),
            jnp.concatenate([other, rows], axis=0),
        )
        got = swap_all(jnp.broadcast_to(pair, (4, 2, BLOCK, WIDTH)), "ctx", y_groups)
        return got.reshape(N_CTX, BLOCK, WIDTH)

    tokens_seq = of_sequence(after(tokens, w_cat))
    shared_cols = jnp.concatenate(
        [shared_gate.reshape(96, N_EXP, SHARED), shared_up.reshape(96, N_EXP, SHARED)], axis=2
    ).transpose(1, 0, 2)
    w_shared = swap_all(shared_cols, "exp").reshape(WIDTH, 2 * SHARED)
    shared_two = jnp.concatenate([shared_down, shared_down], axis=0)

    hidden_one = norm_rows(tokens, gain_attn)
    hidden_seq = norm_rows(tokens_seq, gain_attn)
    hidden_seq = after(hidden_seq, w_shared)
    queries, kv_all = project(hidden_one, hidden_seq, w_all)
    attended, att_f, logs = attend(ctx_s, queries, kv_all)
    middle, hidden_two = middle_norm(attended, w_all, tokens[0], gain_ffn)

    hidden_all = lax.all_gather(hidden_two, "exp", axis=0, tiled=True)
    hidden_all = hidden_all.reshape(HALF, 2, BLOCK, WIDTH)
    att_seq = of_sequence(attended[None])
    place, grad_eo, grad_eh, grad_sh, slot_gate = place_rows(
        exp_s,
        after(up_all, hidden_two).reshape(HALF, 2, BLOCK, WIDTH + META),
        expert_down,
        shared_two,
    )
    part, arrived, act, grad_gu, shared_act, shared_grad = expert_back(
        exp_s, after(hidden_all, att_seq), place, grad_eh, grad_sh, expert_gate, expert_up, w_shared
    )
    summed = add_low(part[1], lax.ppermute(part[0], "exp", core_swap))
    grad_two = swap_all(summed, "exp", same_core)

    rows_e = 2 * ROWS
    operands = (
        after(arrived, summed).reshape(LOCAL_E, rows_e, WIDTH),
        grad_eo.reshape(LOCAL_E, rows_e, WIDTH),
        act.reshape(LOCAL_E, rows_e, FF_E),
        grad_gu.reshape(LOCAL_E, rows_e, 2 * FF_E),
    )
    for_1, for_3 = expert_weights(ctx_s, ((2, 0), (1, 0), (2, 1), (3, 1)), True, *operands)
    operands = (after(operands[0], for_1),) + operands[1:]
    p0, p6, p1, p3 = expert_weights(ctx_s, ((0, 0), (3, 0), (0, 1), (1, 1)), False, *operands)

    def to(rows, k):
        return lax.ppermute(rows, "ctx", [(i, i ^ k) for i in range(N_CTX)])

    from_1, from_3 = to(for_1, 1), to(for_3, 3)
    shared_grad_late = after(shared_grad, p0).reshape(N_EXP * BLOCK, META)
    grad_scols = dg(hidden_all.reshape(N_EXP * BLOCK, WIDTH), shared_grad_late, TN).astype(bf16)
    act_late = after(shared_act, p0).reshape(N_EXP * BLOCK, META)
    grad_sdown = dg(act_late, up_all, TN)[:SHARED, :WIDTH].astype(bf16)
    extra = jnp.concatenate(
        [
            jnp.pad(
                grad_scols.reshape(N_EXP, N_CTX, 12, META).transpose(1, 0, 2, 3),
                ((0, 0), (0, 0), (0, 4), (0, 0)),
            ).reshape(N_CTX, 16 * N_EXP, META),
            grad_sdown.reshape(N_CTX, 8, HEADS, 128).transpose(0, 2, 1, 3).reshape(N_CTX, 96, 128),
        ],
        axis=1,
    )

    out_part = expert_output(
        exp_s, after(act, p0), slot_gate, place, shared_act, expert_down, shared_two
    )
    grad_two = after(grad_two, extra, out_part)
    grad_middle, grad_attn, grad_heads, gain_rows = middle_back(
        grad_two, middle, cotangent[0], gain_ffn, w_all
    )
    grad_query, near, far = attend_back(
        ctx_s, queries, grad_heads, att_f, logs, kv_all, grad_attn, extra, gain_rows
    )
    far = lax.ppermute(far, "ctx", z_swap)
    from_1, from_3 = after((from_1, from_3), near)
    add_a, add_b, part_0, part_1 = piece_sums(
        relay_kernel,
        (bf16, bf16, f32, f32),
        p0,
        p1,
        p3,
        p6,
        (from_1, 0),
        (from_3, 0),
        (from_1, 1),
        (from_3, 1),
    )
    got_11, got_30 = to(add_b, 1), to(add_a, 3)

    def from_x(rows, k):
        return lax.ppermute(rows, "exp", [(i, i ^ (4 * k)) for i in range(N_EXP)])

    out_sums = spread_sums(
        exp_s,
        after(out_part, add_a),
        lax.ppermute(out_part[0, :4], "exp", core_swap),
        lax.ppermute(out_part[0, 4:], "exp", core_swap),
    )
    out_near = (
        out_sums[0].astype(f32)
        + from_x(out_sums[1], 1).astype(f32)
        + from_x(out_sums[3], 3).astype(f32)
    )
    got_11, got_30 = after((got_11, got_30), far)
    own_part, side = piece_sums(side_kernel, (f32, bf16), part_0, part_1, got_11, got_30)
    across = to(side, 4)
    out_2 = from_x(after(out_sums[2], side), 2)

    shares = merge_shares(ctx_s, near, after(far, side, out_near))
    got = swap_all(shares, "ctx", y_groups)
    own = (own_part + after(across, shares).astype(f32)).astype(bf16)
    at_1, at_3, at_z = to(own, 1), to(own, 3), to(own, 4)

    columns, grad_kv, grad_down = column_grads(got, after(hidden_seq, own), att_seq)
    out_rows = after(out_near, columns) + out_2.astype(f32)
    out_across = lax.ppermute(
        out_rows[1].astype(bf16), "exp", [(i, i ^ 2) for i in range(N_EXP)]
    )
    columns = after(columns, at_1, at_3, out_2)
    owned = swap_all(columns, "exp")
    owned, gain_sum = owned_sums(owned, grad_down)
    owned, at_z1, at_z3 = lax.optimization_barrier(
        (after(owned, out_across), to(at_z, 1), to(at_z, 3))
    )
    at_2, at_z2 = to(at_3, 1), to(at_z1, 3)
    mixed = (middle + out_rows[0] + out_across.astype(f32)).astype(bf16)[None]
    experts = unpack_experts(
        ctx_s, ((0, 0), (1, 0), (3, 0), (2, 0)), (after(own, owned), at_1, at_3, at_2)
    )
    owned = jnp.broadcast_to(owned, (N_CTX, OWNED_ROWS, HEAD_DIM))
    owned = swap_all(jnp.concatenate([grad_kv, owned], axis=1), "ctx")
    experts = unpack_experts(
        ctx_s, ((0, 1), (1, 1), (3, 1), (2, 1)), (at_z, at_z1, at_z3, at_z2), experts
    )
    input_grad = input_back(grad_query, owned, w_all, tokens[0], gain_attn, grad_middle)
    gain_attn_sum, *dense = finish(
        after(owned, experts[0], mixed),
        norm_attn.astype(f32).reshape(96, 1),
        query_weight,
        key_weight,
        value_weight,
    )
    return (
        mixed,
        input_grad[None],
        gain_attn_sum[:, 0],
        gain_sum[12, :96],
        *dense,
        *experts,
    )


def solution(mesh):
    token_spec = P("exp", "ctx", None)
    rows = P("exp", None)
    expert = P("exp", None, None)
    placed = (token_spec,) * 3 + (P("exp"),) * 2 + (rows,) * 7 + (expert,) * 3 + (token_spec,)
    return jax.shard_map(
        on_device,
        mesh=mesh,
        in_specs=placed,
        out_specs=(token_spec,) * 2 + (P("exp"),) * 2 + (rows,) * 7 + (expert,) * 3,
        check_vma=False,
    )
```

```python
import jax
import jax.numpy as jnp
from jax import lax
from jax.sharding import PartitionSpec as P
from jax.experimental import pallas as pl
from jax.experimental.pallas import tpu as pltpu

HEADS = 12
KV_HEADS = 4
HEAD_DIM = 128
TOPK = 6
GROUP = 3
BLOCK = 128
WIDTH = 1536
KV_WIDTH = KV_HEADS * HEAD_DIM
CAP = 48
N_EXP = 16
N_CTX = 8
LOCAL_E = 2
FF_E = 512
SHARED = 64
META = 128
HALF = 8
ROWS = HALF * CAP

epsilon = 1e-05
masked_score = -1e30
f32 = jnp.float32
bf16 = jnp.bfloat16
log2_e = 1.4426950408889634
score_scale = HEAD_DIM ** (-0.5) * log2_e

NN = (((1,), (0,)), ((), ()))
NT = (((1,), (1,)), ((), ()))
TN = (((0,), (0,)), ((), ()))


def dg(a, b, dims):
    return lax.dot_general(a, b, dims, preferred_element_type=f32)


def params(mib):
    return pltpu.CompilerParams(vmem_limit_bytes=mib * 1024 * 1024)


def cost(us):
    return pl.CostEstimate(flops=0, bytes_accessed=int(us * 3690000), transcendentals=0)


def whole(shape):
    return pl.BlockSpec(shape, lambda *_: (0,) * len(shape), pipeline_mode=pl.Buffered(1))


def sigmoid(v):
    return 1.0 / (1.0 + jnp.exp(-v))


def allowed_scores(ctx_at):
    rows = lax.broadcasted_iota(jnp.int32, (GROUP * BLOCK, N_CTX * BLOCK), 0) % BLOCK
    cols = lax.broadcasted_iota(jnp.int32, (GROUP * BLOCK, N_CTX * BLOCK), 1)
    return rows + ctx_at * BLOCK >= cols


def stack_heads(block):
    return jnp.concatenate([block[:, j * HEAD_DIM : (j + 1) * HEAD_DIM] for j in range(GROUP)], axis=0)


def unstack_heads(rows):
    return jnp.concatenate([rows[j * BLOCK : (j + 1) * BLOCK] for j in range(GROUP)], axis=1)


def attend_kernel(ctx_ref, q_ref, k_ref, v_ref, att_ref, attf_ref, log_ref):
    q = stack_heads(q_ref[...])
    keys = k_ref[...].reshape(N_CTX * BLOCK, HEAD_DIM)
    values = v_ref[...].reshape(N_CTX * BLOCK, HEAD_DIM)
    scores = jnp.where(allowed_scores(ctx_ref[0]), dg(q, keys, NT) * score_scale, masked_score)
    top = jnp.max(scores, axis=-1, keepdims=True)
    weights = jnp.exp2(scores - top)
    total = jnp.sum(weights, axis=-1, keepdims=True)
    out = dg(weights.astype(bf16), values, NN) * (1.0 / total)
    out = unstack_heads(out)
    attf_ref[...] = out
    att_ref[...] = out.astype(bf16)
    log_ref[...] = jnp.broadcast_to(top + jnp.log2(total), (GROUP * BLOCK, HEAD_DIM))


def kv_specs():
    return [
        pl.BlockSpec((N_CTX, BLOCK, HEAD_DIM), lambda g: (0, 0, g)),
        pl.BlockSpec((N_CTX, BLOCK, HEAD_DIM), lambda g: (0, 0, KV_HEADS + g)),
    ]


def head_spec():
    return pl.BlockSpec((BLOCK, GROUP * HEAD_DIM), lambda g: (0, g))


def attend(ctx_at, qkv, kv_all):
    return pl.pallas_call(
        attend_kernel,
        grid=(KV_HEADS,),
        in_specs=[pl.BlockSpec(memory_space=pltpu.SMEM), head_spec()] + kv_specs(),
        out_specs=[
            head_spec(),
            head_spec(),
            pl.BlockSpec((GROUP * BLOCK, HEAD_DIM), lambda g: (g, 0)),
        ],
        out_shape=[
            jax.ShapeDtypeStruct((BLOCK, WIDTH), bf16),
            jax.ShapeDtypeStruct((BLOCK, WIDTH), f32),
            jax.ShapeDtypeStruct((HEADS * BLOCK, HEAD_DIM), f32),
        ],
        cost_estimate=cost(6),
        compiler_params=params(48),
        name="attend",
    )(ctx_at, qkv, kv_all, kv_all)


SEQ = N_CTX * BLOCK
AT_QUERY, AT_MIXED, AT_OUT = SEQ, SEQ + BLOCK, SEQ + 2 * BLOCK
AT_SHARED = SEQ + 3 * BLOCK
AT_DOWN = AT_SHARED + 16 * N_EXP
AT_GAIN = AT_DOWN + 96
SENT_ROWS = AT_GAIN + 16


def halves(a, b, lane):
    low = jnp.where(lane < 64, a, pltpu.roll(b, 64, 1))
    high = jnp.where(lane < 64, pltpu.roll(a, 64, 1), b)
    return low, high


def attend_back_kernel(
    ctx_ref,
    q_ref,
    ga_ref,
    attf_ref,
    log_ref,
    k_ref,
    v_ref,
    all_ga_ref,
    extra_ref,
    gain_ref,
    dq_ref,
    near_ref,
    far_ref,
    kept_ref,
):
    group = pl.program_id(0)
    z_at = ctx_ref[0] // 4

    def send(dest, z, start, stop, rows):
        @pl.when(z_at == z)
        def _():
            near_ref[dest, start:stop] = rows

        @pl.when(z_at != z)
        def _():
            far_ref[dest, start:stop] = rows

    q = stack_heads(q_ref[...])
    grad = stack_heads(ga_ref[...])
    delta = jnp.sum(grad.astype(f32) * stack_heads(attf_ref[...]), axis=-1, keepdims=True)
    keys = k_ref[...].reshape(SEQ, HEAD_DIM)
    values = v_ref[...].reshape(SEQ, HEAD_DIM)
    scores = jnp.where(allowed_scores(ctx_ref[0]), dg(q, keys, NT) * score_scale, masked_score)
    weights = jnp.exp2(scores - log_ref[:, :1])
    grad_weights = dg(grad, values, NT)
    grad_raw = (weights * (grad_weights - delta)).astype(bf16)
    scale = HEAD_DIM ** (-0.5)
    dq = unstack_heads(dg(grad_raw, keys, NN) * scale)
    dq_ref[...] = dq.astype(bf16)
    kept_ref[group] = dq
    grad_k = dg(grad_raw, q, TN) * scale
    grad_v = dg(weights.astype(bf16), grad, TN)
    low, high = halves(grad_k, grad_v, lax.broadcasted_iota(jnp.int32, (SEQ, HEAD_DIM), 1))
    low, high = low.astype(bf16), high.astype(bf16)
    send(2 * (group % 2), group // 2, 0, SEQ, low)
    send(2 * (group % 2) + 1, group // 2, 0, SEQ, high)

    @pl.when(group == KV_HEADS - 1)
    def _():
        lane = lax.broadcasted_iota(jnp.int32, (BLOCK, HEAD_DIM), 1)

        def dq_tile(m):
            return kept_ref[m // GROUP, :, HEAD_DIM * (m % GROUP) : HEAD_DIM * (m % GROUP + 1)]

        def ga_tile(m):
            return all_ga_ref[:, HEAD_DIM * m : HEAD_DIM * (m + 1)].astype(f32)

        mixed = []
        for m in range(KV_HEADS):
            mixed += halves(dq_tile(N_CTX + m), ga_tile(N_CTX + m), lane)
        gains = gain_ref[...].astype(bf16)
        for c in range(N_CTX):
            tiles = [dq_tile(c).astype(bf16), mixed[c].astype(bf16), ga_tile(c).astype(bf16)]
            rows = jnp.concatenate(tiles + [extra_ref[c], gains], axis=0)
            send(c % 4, c // 4, AT_QUERY, SENT_ROWS, rows)


def attend_back(ctx_at, qkv, grad_att, att_f, logs, kv_all, grad_attn, extra, gain_rows):
    return pl.pallas_call(
        attend_back_kernel,
        grid=(KV_HEADS,),
        in_specs=[
            pl.BlockSpec(memory_space=pltpu.SMEM),
            head_spec(),
            head_spec(),
            head_spec(),
            pl.BlockSpec((GROUP * BLOCK, HEAD_DIM), lambda g: (g, 0)),
        ]
        + kv_specs()
        + [
            whole((BLOCK, WIDTH)),
            whole((N_CTX, AT_GAIN - AT_SHARED, HEAD_DIM)),
            whole((16, HEAD_DIM)),
        ],
        out_specs=[head_spec()] + [whole((4, SENT_ROWS, HEAD_DIM))] * 2,
        out_shape=[
            jax.ShapeDtypeStruct((BLOCK, WIDTH), bf16),
            jax.ShapeDtypeStruct((4, SENT_ROWS, HEAD_DIM), bf16),
            jax.ShapeDtypeStruct((4, SENT_ROWS, HEAD_DIM), bf16),
        ],
        scratch_shapes=[pltpu.VMEM((KV_HEADS, BLOCK, GROUP * HEAD_DIM), f32)],
        cost_estimate=cost(2),
        compiler_params=params(60),
        name="attend_back",
    )(ctx_at, qkv, grad_att, att_f, logs, kv_all, kv_all, grad_attn, extra, gain_rows)


def middle_kernel(att_ref, w_ref, x_ref, gain_ref, middle_ref, hidden_ref):
    middle = x_ref[...].astype(f32) + dg(att_ref[...], w_ref[...], NN)
    inv = lax.rsqrt(jnp.mean(middle * middle, axis=-1, keepdims=True) + epsilon)
    middle_ref[...] = middle
    hidden_ref[...] = (middle * inv * gain_ref[...]).astype(bf16)


def w_cols(width, at):
    return pl.BlockSpec((WIDTH, width), lambda *_: (0, at), pipeline_mode=pl.Buffered(1))


def middle_norm(attended, w_all, tokens, gain):
    return pl.pallas_call(
        middle_kernel,
        grid=(1,),
        in_specs=[
            whole((BLOCK, WIDTH)),
            w_cols(WIDTH, 1),
            whole((BLOCK, WIDTH)),
            whole((1, WIDTH)),
        ],
        out_specs=[whole((BLOCK, WIDTH)), whole((BLOCK, WIDTH))],
        out_shape=[
            jax.ShapeDtypeStruct((BLOCK, WIDTH), f32),
            jax.ShapeDtypeStruct((BLOCK, WIDTH), bf16),
        ],
        cost_estimate=cost(2),
        compiler_params=params(60),
        name="middle_norm",
    )(attended, w_all, tokens, gain)


def norm_back(grad_normed, normed, inv_root):
    return inv_root * (
        grad_normed - normed * jnp.mean(grad_normed * normed, axis=-1, keepdims=True)
    )


def middle_back_kernel(
    pieces_ref, middle_ref, up_ref, gain_ref, w_ref, gm_ref, ga_ref, gh_ref, gg_ref
):
    grad_two = pieces_ref[0].astype(f32)
    for i in range(1, HALF):
        grad_two = grad_two + pieces_ref[i].astype(f32)
    middle = middle_ref[...]
    inv = lax.rsqrt(jnp.mean(middle * middle, axis=-1, keepdims=True) + epsilon)
    normed = middle * inv
    gains = jnp.sum(grad_two * normed, axis=0, keepdims=True)
    gg_ref[...] = jnp.zeros((16, HEAD_DIM), f32)
    for m in range(HEADS):
        gg_ref[m : m + 1] = gains[:, HEAD_DIM * m : HEAD_DIM * (m + 1)]
    grad_middle = up_ref[...].astype(f32) + norm_back(grad_two * gain_ref[...], normed, inv)
    gm_ref[...] = grad_middle
    grad_attn = grad_middle.astype(bf16)
    ga_ref[...] = grad_attn
    gh_ref[...] = dg(grad_attn, w_ref[...], NT).astype(bf16)


def middle_back(pieces, middle, upstream, gain, w_all):
    return pl.pallas_call(
        middle_back_kernel,
        grid=(1,),
        in_specs=[
            whole((HALF, BLOCK, WIDTH)),
            whole((BLOCK, WIDTH)),
            whole((BLOCK, WIDTH)),
            whole((1, WIDTH)),
            w_cols(WIDTH, 1),
        ],
        out_specs=[whole((BLOCK, WIDTH))] * 3 + [whole((16, HEAD_DIM))],
        out_shape=[
            jax.ShapeDtypeStruct((BLOCK, WIDTH), f32),
            jax.ShapeDtypeStruct((BLOCK, WIDTH), bf16),
            jax.ShapeDtypeStruct((BLOCK, WIDTH), bf16),
            jax.ShapeDtypeStruct((16, HEAD_DIM), f32),
        ],
        cost_estimate=cost(1),
        compiler_params=params(48),
        name="middle_back",
    )(pieces, middle, upstream, gain, w_all)


def place_kernel(
    at_ref, up_ref, down_ref, sdown_ref, place_ref, geo_ref, geh_ref, gsh_ref, gate_ref
):
    lane = lax.broadcasted_iota(jnp.int32, (BLOCK, META), 1)
    row = lax.broadcasted_iota(jnp.int32, (BLOCK, META), 0)
    before = (row > lane).astype(bf16)
    slot = (lane % 64).astype(f32)
    first_id = (at_ref[0] * LOCAL_E).astype(f32)
    row_id = first_id + (row >= 64).astype(f32)

    for chip in range(HALF):
        meta = up_ref[chip, 0, :, WIDTH:].astype(f32)
        named = lane < TOPK
        zero = jnp.zeros((BLOCK, META), f32)
        hit0 = jnp.where(named & (meta == first_id), 1.0, zero)
        hit1 = jnp.where(named & (meta == first_id + 1.0), 1.0, zero)
        mask = jnp.where(
            lane < 64,
            jnp.sum(hit0, axis=1, keepdims=True),
            jnp.sum(hit1, axis=1, keepdims=True),
        )
        rank = dg(before, mask.astype(bf16), NN)
        place = jnp.where((mask > 0.5) & (rank == slot), 1.0, zero).astype(bf16)
        place_ref[chip, 0] = place
        rows = dg(place, up_ref[chip, 0], TN)
        slot_meta = rows[:, WIDTH:]
        gates = pltpu.roll(slot_meta, META - TOPK, 1) + pltpu.roll(
            slot_meta, META - 2 * TOPK, 1
        )
        gate = jnp.sum(
            jnp.where(named & (slot_meta == row_id), gates, zero), axis=1, keepdims=True
        )
        geo = (gate * rows[:, :WIDTH]).astype(bf16)
        wide_gate = jnp.broadcast_to(gate, (BLOCK, META))
        at = chip * CAP
        for e in range(LOCAL_E):
            geo_ref[e, 0, at : at + CAP] = geo[64 * e : 64 * e + CAP]
            gate_ref[e, 0, at : at + CAP] = wide_gate[64 * e : 64 * e + CAP]
        gsh_ref[chip, 0] = dg(up_ref[chip, 0, :, :WIDTH], sdown_ref[...], NT)
    for e in range(LOCAL_E):
        geh_ref[e, 0] = dg(geo_ref[e, 0], down_ref[e], NT)


def by_core(cols):
    return pl.BlockSpec(
        (HALF, 1, BLOCK, cols),
        lambda s, at: (0, jnp.where(s == 0, 1 - at[0] % 2, at[0] % 2), 0, 0),
    )


def by_step(cols):
    return pl.BlockSpec((LOCAL_E, 1, ROWS, cols), lambda s, at: (0, s, 0, 0))


def place_rows(exp_at, up_all, expert_down, shared_two):
    return pl.pallas_call(
        place_kernel,
        grid_spec=pltpu.PrefetchScalarGridSpec(
            num_scalar_prefetch=1,
            grid=(2,),
            in_specs=[
                by_core(WIDTH + META),
                whole((LOCAL_E, FF_E, WIDTH)),
                whole((2 * SHARED, WIDTH)),
            ],
            out_specs=[by_core(META), by_step(WIDTH), by_step(FF_E), by_core(META), by_step(META)],
        ),
        out_shape=[
            jax.ShapeDtypeStruct((HALF, 2, BLOCK, META), bf16),
            jax.ShapeDtypeStruct((LOCAL_E, 2, ROWS, WIDTH), bf16),
            jax.ShapeDtypeStruct((LOCAL_E, 2, ROWS, FF_E), f32),
            jax.ShapeDtypeStruct((HALF, 2, BLOCK, META), f32),
            jax.ShapeDtypeStruct((LOCAL_E, 2, ROWS, META), f32),
        ],
        cost_estimate=cost(14),
        compiler_params=params(56),
        name="place_rows",
    )(exp_at, up_all, expert_down, shared_two)


def expert_kernel(
    at_ref,
    hid_ref,
    place_ref,
    geh_ref,
    gsh_ref,
    wg_ref,
    wu_ref,
    ws_ref,
    part_ref,
    x_ref,
    act_ref,
    dgu_ref,
    sact_ref,
    sgrad_ref,
):
    for chip in range(HALF):
        rows = dg(place_ref[chip, 0], hid_ref[chip, 0], TN).astype(bf16)
        at = chip * CAP
        for e in range(LOCAL_E):
            x_ref[e, 0, at : at + CAP] = rows[64 * e : 64 * e + CAP]
    pairs = []
    for e in range(LOCAL_E):
        pre_gate = dg(x_ref[e, 0], wg_ref[e], NN)
        pre_up = dg(x_ref[e, 0], wu_ref[e], NN)
        sig = sigmoid(pre_gate)
        act = pre_gate * sig
        act_ref[e, 0] = (act * pre_up).astype(bf16)
        geh = geh_ref[e, 0]
        d_gate = (geh * pre_up * (sig * (1.0 + pre_gate * (1.0 - sig)))).astype(bf16)
        d_up = (geh * act).astype(bf16)
        dgu_ref[e, 0, :, :FF_E] = d_gate
        dgu_ref[e, 0, :, FF_E:] = d_up
        pairs.append((dg(d_gate, wg_ref[e], NT) + dg(d_up, wu_ref[e], NT)).astype(bf16))
    lane = lax.broadcasted_iota(jnp.int32, (BLOCK, 2 * SHARED), 1) < SHARED
    gap = jnp.zeros((64 - CAP, WIDTH), bf16)
    for chip in range(HALF):
        pre = dg(hid_ref[chip, 0], ws_ref[...], NN)
        turned = pltpu.roll(pre, SHARED, 1)
        gate, up = jnp.where(lane, pre, turned), jnp.where(lane, turned, pre)
        sig = sigmoid(gate)
        act = gate * sig
        sact_ref[chip, 0] = jnp.where(lane, act * up, 0.0).astype(bf16)
        slope = sig * (1.0 + gate * (1.0 - sig))
        sgrad = (gsh_ref[chip, 0] * jnp.where(lane, up * slope, act)).astype(bf16)
        sgrad_ref[chip, 0] = sgrad
        at = chip * CAP
        stacked = jnp.concatenate([pairs[0][at : at + CAP], gap, pairs[1][at : at + CAP], gap], 0)
        part_ref[0, chip] = (
            dg(place_ref[chip, 0], stacked, NN) + dg(sgrad, ws_ref[...], NT)
        ).astype(bf16)


def expert_back(exp_at, hidden, place, geh, gsh, wg, wu, ws):
    return pl.pallas_call(
        expert_kernel,
        grid_spec=pltpu.PrefetchScalarGridSpec(
            num_scalar_prefetch=1,
            grid=(2,),
            in_specs=[
                by_core(WIDTH),
                by_core(META),
                by_step(FF_E),
                by_core(META),
                whole((LOCAL_E, WIDTH, FF_E)),
                whole((LOCAL_E, WIDTH, FF_E)),
                whole((WIDTH, 2 * SHARED)),
            ],
            out_specs=[
                pl.BlockSpec((1, HALF, BLOCK, WIDTH), lambda s, at: (s, 0, 0, 0)),
                by_step(WIDTH),
                by_step(FF_E),
                by_step(2 * FF_E),
                by_core(META),
                by_core(META),
            ],
        ),
        out_shape=[
            jax.ShapeDtypeStruct((2, HALF, BLOCK, WIDTH), bf16),
            jax.ShapeDtypeStruct((LOCAL_E, 2, ROWS, WIDTH), bf16),
            jax.ShapeDtypeStruct((LOCAL_E, 2, ROWS, FF_E), bf16),
            jax.ShapeDtypeStruct((LOCAL_E, 2, ROWS, 2 * FF_E), bf16),
            jax.ShapeDtypeStruct((HALF, 2, BLOCK, META), bf16),
            jax.ShapeDtypeStruct((HALF, 2, BLOCK, META), bf16),
        ],
        cost_estimate=cost(28),
        compiler_params=params(60),
        name="expert_back",
    )(exp_at, hidden, place, geh, gsh, wg, wu, ws)


def output_kernel(at_ref, act_ref, gate_ref, place_ref, sact_ref, wd_ref, sd_ref, part_ref):
    outs = []
    for e in range(LOCAL_E):
        out = dg(act_ref[e, 0], wd_ref[e], NN).astype(bf16).astype(f32)
        outs.append((out * gate_ref[e, 0, :, :1]).astype(bf16))
    gap = jnp.zeros((64 - CAP, WIDTH), bf16)
    for chip in range(HALF):
        at = chip * CAP
        stacked = jnp.concatenate([outs[0][at : at + CAP], gap, outs[1][at : at + CAP], gap], 0)
        part_ref[0, chip] = (
            dg(place_ref[chip, 0], stacked, NN) + dg(sact_ref[chip, 0], sd_ref[...], NN)
        ).astype(bf16)


def expert_output(exp_at, act, gate, place, sact, wd, sd):
    return pl.pallas_call(
        output_kernel,
        grid_spec=pltpu.PrefetchScalarGridSpec(
            num_scalar_prefetch=1,
            grid=(2,),
            in_specs=[
                by_step(FF_E),
                by_step(META),
                by_core(META),
                by_core(META),
                whole((LOCAL_E, FF_E, WIDTH)),
                whole((2 * SHARED, WIDTH)),
            ],
            out_specs=pl.BlockSpec((1, HALF, BLOCK, WIDTH), lambda s, at: (s, 0, 0, 0)),
        ),
        out_shape=jax.ShapeDtypeStruct((2, HALF, BLOCK, WIDTH), bf16),
        cost_estimate=cost(2),
        compiler_params=params(48),
        name="expert_output",
    )(exp_at, act, gate, place, sact, wd, sd)


SHARE = 3 * BLOCK
TO_SHARED = SEQ + 2 * SHARE
TO_DOWN = TO_SHARED + 16 * N_EXP
TO_GAIN = TO_DOWN + 96
MERGED_ROWS = TO_GAIN + 16


def merge_kernel(ctx_ref, near_ref, got_ref, out_ref):
    z_at = ctx_ref[0] // 4
    near, got = near_ref[0], got_ref[0]

    def add(a, b):
        return (a.astype(f32) + b.astype(f32)).astype(bf16)

    out_ref[0, :SEQ] = add(near[:SEQ], got[:SEQ])
    out_ref[0, TO_SHARED:] = add(near[AT_SHARED:], got[AT_SHARED:])
    mine, theirs = near[AT_QUERY:AT_SHARED], got[AT_QUERY:AT_SHARED]
    out_ref[0, SEQ : SEQ + SHARE] = jnp.where(z_at == 0, mine, theirs)
    out_ref[0, SEQ + SHARE : TO_SHARED] = jnp.where(z_at == 0, theirs, mine)


def merge_shares(ctx_at, near, got):
    spec = pl.BlockSpec((1, SENT_ROWS, HEAD_DIM), lambda i: (i, 0, 0))
    return pl.pallas_call(
        merge_kernel,
        grid=(4,),
        in_specs=[pl.BlockSpec(memory_space=pltpu.SMEM), spec, spec],
        out_specs=pl.BlockSpec((1, MERGED_ROWS, HEAD_DIM), lambda i: (i, 0, 0)),
        out_shape=jax.ShapeDtypeStruct((4, MERGED_ROWS, HEAD_DIM), bf16),
        cost_estimate=cost(3),
        compiler_params=params(32),
        name="merge_shares",
    )(ctx_at, near, got)


def columns_kernel(got_ref, hidden_ref, att_ref, sent_ref, kv_ref, down_ref):
    def summed(start, stop):
        out = got_ref[0, start:stop].astype(f32)
        for src in range(1, 4):
            out = out + got_ref[src, start:stop].astype(f32)
        return out

    grad_kv = summed(0, SEQ).astype(bf16)
    kv_ref[...] = grad_kv.reshape(N_CTX, BLOCK, HEAD_DIM)

    def rows_of(tile, order):
        at = SEQ + BLOCK * tile
        return jnp.concatenate(
            [got_ref[y, at + SHARE * z : at + SHARE * z + BLOCK] for z, y in order], axis=0
        )

    in_order = [(i // 4, i % 4) for i in range(N_CTX)]
    y_order = [(i % 2, i // 2) for i in range(N_CTX)]
    lane = lax.broadcasted_iota(jnp.int32, (SEQ, HEAD_DIM), 1)
    zero = jnp.zeros((SEQ, HEAD_DIM), bf16)
    mixed_q = jnp.where(lane < 64, rows_of(1, in_order), zero)
    mixed_o = jnp.where(lane < 64, zero, rows_of(1, y_order))
    left = jnp.concatenate([rows_of(0, in_order).T, mixed_q.T, grad_kv.T], axis=0)
    right = jnp.concatenate([mixed_o.T, rows_of(2, y_order).T], axis=0)
    by_hidden = dg(left, hidden_ref[...].reshape(SEQ, WIDTH), NN)
    by_att = dg(right, att_ref[...].reshape(SEQ, WIDTH), NN)
    tiles = [
        by_hidden[:BLOCK],
        by_hidden[BLOCK : 2 * BLOCK] + by_att[:BLOCK],
        by_att[BLOCK:],
        by_hidden[2 * BLOCK :],
    ]
    for t, tile in enumerate(tiles):
        sent_ref[:, :96, HEAD_DIM * t : HEAD_DIM * (t + 1)] = (
            tile.T.astype(bf16).reshape(N_EXP, 96, HEAD_DIM)
        )

    down_ref[...] = summed(TO_DOWN, TO_GAIN).astype(bf16)
    shared = summed(TO_SHARED, TO_DOWN)
    gains = summed(TO_GAIN, MERGED_ROWS)
    row = lax.broadcasted_iota(jnp.int32, (16, HEAD_DIM), 0)
    one_lane = lax.broadcasted_iota(jnp.int32, (1, HEAD_DIM), 1)
    for i in range(N_EXP):
        m, offset = (96 * i) // HEAD_DIM, (96 * i) % HEAD_DIM
        gain = gains[m : m + 1]
        if offset:
            shift = HEAD_DIM - offset
            gain = jnp.where(
                one_lane < shift,
                pltpu.roll(gain, shift, 1),
                pltpu.roll(gains[m + 1 : m + 2], shift, 1),
            )
        rows = jnp.where(row == 12, jnp.broadcast_to(gain, (16, HEAD_DIM)), shared[16 * i : 16 * i + 16])
        sent_ref[i, 96:, :HEAD_DIM] = rows.astype(bf16)
        sent_ref[i, 96:, HEAD_DIM:] = jnp.zeros((16, 512 - HEAD_DIM), bf16)


def column_grads(got, hidden_seq, att_seq):
    return pl.pallas_call(
        columns_kernel,
        out_shape=[
            jax.ShapeDtypeStruct((N_EXP, 112, 512), bf16),
            jax.ShapeDtypeStruct((N_CTX, BLOCK, HEAD_DIM), bf16),
            jax.ShapeDtypeStruct((96, HEAD_DIM), bf16),
        ],
        cost_estimate=cost(8),
        compiler_params=params(56),
        name="column_grads",
    )(got, hidden_seq, att_seq)


OWNED_ROWS = 4 * 96 + 16 * N_EXP + 96


def owned_kernel(got_ref, down_ref, owned_ref, gain_ref):
    total = got_ref[0, :96].astype(f32)
    gains = got_ref[0, 96:, :HEAD_DIM].astype(f32)
    for src in range(1, N_EXP):
        total = total + got_ref[src, :96].astype(f32)
        gains = gains + got_ref[src, 96:, :HEAD_DIM].astype(f32)
    gain_ref[...] = gains
    for t in range(4):
        owned_ref[96 * t : 96 * t + 96] = total[:, HEAD_DIM * t : HEAD_DIM * (t + 1)].astype(bf16)
    for src in range(N_EXP):
        at = 384 + 16 * src
        owned_ref[at : at + 16] = got_ref[src, 96:, :HEAD_DIM]
    owned_ref[384 + 16 * N_EXP :] = down_ref[...]


def owned_sums(got, down):
    return pl.pallas_call(
        owned_kernel,
        out_shape=[
            jax.ShapeDtypeStruct((OWNED_ROWS, HEAD_DIM), bf16),
            jax.ShapeDtypeStruct((16, HEAD_DIM), f32),
        ],
        cost_estimate=cost(3),
        compiler_params=params(32),
        name="owned_sums",
    )(got, down)


def finish_kernel(
    got_ref,
    gain_in_ref,
    wq_ref,
    wk_ref,
    wv_ref,
    gain_ref,
    q_ref,
    k_ref,
    v_ref,
    out_ref,
    sg_ref,
    su_ref,
    sd_ref,
):
    lane = lax.broadcasted_iota(jnp.int32, (96, HEAD_DIM), 1)

    def tile(c, t):
        at = BLOCK + 96 * t
        return got_ref[c, at : at + 96].astype(f32)

    for c in range(N_CTX):
        at = HEAD_DIM * c
        q_ref[:, at : at + HEAD_DIM] = tile(c, 0)
        out_ref[:, at : at + HEAD_DIM] = tile(c, 2)
    for m in range(N_CTX // 2):
        at = HEAD_DIM * m
        low, high = halves(tile(2 * m, 1), tile(2 * m + 1, 1), lane)
        q_ref[:, 1024 + at : 1024 + at + HEAD_DIM] = low
        out_ref[:, 1024 + at : 1024 + at + HEAD_DIM] = high
        low, high = halves(tile(2 * m, 3), tile(2 * m + 1, 3), lane)
        k_ref[:, at : at + HEAD_DIM] = low
        v_ref[:, at : at + HEAD_DIM] = high
    gain = (
        jnp.sum(q_ref[...] * wq_ref[...].astype(f32), axis=1, keepdims=True)
        + jnp.sum(k_ref[...] * wk_ref[...].astype(f32), axis=1, keepdims=True)
        + jnp.sum(v_ref[...] * wv_ref[...].astype(f32), axis=1, keepdims=True)
    ) / gain_in_ref[...]
    gain_ref[...] = jnp.broadcast_to(gain, (96, HEAD_DIM))
    row = lax.broadcasted_iota(jnp.int32, (96, HEAD_DIM), 0)
    picks = jnp.where((lane % 16 < 12) & (row == 12 * (lane // 16) + lane % 16), 1.0, 0.0)
    picks = picks.astype(bf16)

    def shared_tile(j):
        at = BLOCK + 384 + 16 * j
        rows = jnp.concatenate([got_ref[c, at : at + 16] for c in range(N_CTX)], axis=0)
        return dg(picks, rows, NN)

    for m in range(N_EXP // 2):
        at = HEAD_DIM * m
        low, high = halves(shared_tile(2 * m), shared_tile(2 * m + 1), lane)
        sg_ref[:, at : at + HEAD_DIM] = low
        su_ref[:, at : at + HEAD_DIM] = high
    for c in range(N_CTX):
        rows = got_ref[c, BLOCK + 384 + 16 * N_EXP :].astype(f32)
        for m in range(HEADS):
            sd_ref[8 * c : 8 * c + 8, HEAD_DIM * m : HEAD_DIM * (m + 1)] = rows[8 * m : 8 * m + 8]


def finish(got, gain_column, query_weight, key_weight, value_weight):
    shapes = [(96, 128), (96, 1536), (96, 512), (96, 512), (96, 1536), (96, 1024), (96, 1024)]
    return pl.pallas_call(
        finish_kernel,
        out_shape=[jax.ShapeDtypeStruct(s, f32) for s in shapes + [(SHARED, WIDTH)]],
        cost_estimate=cost(4),
        compiler_params=params(32),
        name="finish",
    )(got, gain_column, query_weight, key_weight, value_weight)


def input_kernel(dq_ref, got_ref, wq_ref, wkv_ref, x_ref, gain_ref, gm_ref, out_ref):
    lane = lax.broadcasted_iota(jnp.int32, (BLOCK, HEAD_DIM), 1)
    lows, highs = [], []
    for m in range(KV_HEADS):
        low, high = halves(got_ref[2 * m].astype(f32), got_ref[2 * m + 1].astype(f32), lane)
        lows.append(low.astype(bf16))
        highs.append(high.astype(bf16))
    grad_kv = jnp.concatenate(lows + highs, axis=1)
    grad_one = dg(dq_ref[...], wq_ref[...], NT) + dg(grad_kv, wkv_ref[...], NT)
    inputs = x_ref[...].astype(f32)
    inv = lax.rsqrt(jnp.mean(inputs * inputs, axis=-1, keepdims=True) + epsilon)
    out_ref[...] = (gm_ref[...] + norm_back(grad_one * gain_ref[...], inputs * inv, inv)).astype(bf16)


def input_back(grad_query, grad_kv, w_all, tokens, gain, grad_middle):
    return pl.pallas_call(
        input_kernel,
        grid=(1,),
        in_specs=[
            whole((BLOCK, WIDTH)),
            whole((N_CTX, BLOCK, HEAD_DIM)),
            w_cols(WIDTH, 0),
            w_cols(2 * KV_WIDTH, 3),
            whole((BLOCK, WIDTH)),
            whole((1, WIDTH)),
            whole((BLOCK, WIDTH)),
        ],
        out_specs=whole((BLOCK, WIDTH)),
        out_shape=jax.ShapeDtypeStruct((BLOCK, WIDTH), bf16),
        cost_estimate=cost(7),
        compiler_params=params(48),
        name="input_back",
    )(grad_query, grad_kv, w_all, w_all, tokens, gain, grad_middle)


def norm_rows_kernel(x_ref, gain_ref, out_ref):
    inputs = x_ref[0].astype(f32)
    inv = lax.rsqrt(jnp.mean(inputs * inputs, axis=-1, keepdims=True) + epsilon)
    out_ref[0] = (inputs * inv * gain_ref[...]).astype(bf16)


def norm_rows(rows, gain):
    count = rows.shape[0]
    spec = pl.BlockSpec((1, BLOCK, WIDTH), lambda i: (i, 0, 0))
    turned = pl.BlockSpec((1, BLOCK, WIDTH), lambda i: ((i % 2) * 4 + i // 2, 0, 0))
    return pl.pallas_call(
        norm_rows_kernel,
        grid=(count,),
        in_specs=[spec, whole((1, WIDTH))],
        out_specs=spec if count == 1 else turned,
        out_shape=jax.ShapeDtypeStruct(rows.shape, bf16),
        cost_estimate=cost(2),
        compiler_params=params(32),
        name="norm_rows",
    )(rows, gain)


def project_kernel(own_ref, seq_ref, w_ref, q_ref, kv_ref):
    step = pl.program_id(0)

    @pl.when(step < 3)
    def _():
        q_ref[...] = dg(own_ref[0], w_ref[...], NN).astype(bf16)

    @pl.when(step >= 3)
    def _():
        rows = seq_ref[...].reshape(N_CTX * BLOCK, WIDTH)
        kv_ref[...] = dg(rows, w_ref[...], NN).astype(bf16).reshape(N_CTX, BLOCK, KV_WIDTH)


def project(own, seq, w_all):
    return pl.pallas_call(
        project_kernel,
        grid=(5,),
        in_specs=[
            whole((1, BLOCK, WIDTH)),
            whole((N_CTX, BLOCK, WIDTH)),
            pl.BlockSpec((WIDTH, KV_WIDTH), lambda i: (0, jnp.where(i < 3, i, i + 3))),
        ],
        out_specs=[
            pl.BlockSpec((BLOCK, KV_WIDTH), lambda i: (0, jnp.minimum(i, 2))),
            pl.BlockSpec((N_CTX, BLOCK, KV_WIDTH), lambda i: (0, 0, jnp.maximum(i - 3, 0))),
        ],
        out_shape=[
            jax.ShapeDtypeStruct((BLOCK, WIDTH), bf16),
            jax.ShapeDtypeStruct((N_CTX, BLOCK, 2 * KV_WIDTH), bf16),
        ],
        cost_estimate=cost(8),
        compiler_params=params(48),
        name="project",
    )(own, seq, w_all)


PIECE = 2 * WIDTH + WIDTH * BLOCK // HEAD_DIM


def spread_kernel(at_ref, own_ref, low_ref, high_ref, *outs):
    chip = (at_ref[0] >> 1) ^ pl.program_id(0)
    got = jnp.where(chip < 4, low_ref[0], high_ref[0])
    total = (own_ref[0, 0].astype(f32) + got.astype(f32)).astype(bf16)
    for k in range(HALF):

        @pl.when(pl.program_id(0) == k)
        def _():
            outs[k // 2][k % 2] = total


def spread_sums(exp_at, parts, low, high):
    half = pl.BlockSpec((1, BLOCK, WIDTH), lambda k, at: (((at[0] >> 1) ^ k) & 3, 0, 0))
    return pl.pallas_call(
        spread_kernel,
        grid_spec=pltpu.PrefetchScalarGridSpec(
            num_scalar_prefetch=1,
            grid=(HALF,),
            in_specs=[
                pl.BlockSpec((1, 1, BLOCK, WIDTH), lambda k, at: (1, (at[0] >> 1) ^ k, 0, 0)),
                half,
                half,
            ],
            out_specs=[whole((2, BLOCK, WIDTH))] * 4,
        ),
        out_shape=[jax.ShapeDtypeStruct((2, BLOCK, WIDTH), bf16)] * 4,
        cost_estimate=cost(4),
        compiler_params=params(32),
        name="spread_sums",
    )(exp_at, parts, low, high)


def of_step(values, step):
    out = jnp.int32(values[0])
    for i, value in enumerate(values[1:], 1):
        out = jnp.where(step == i, value, out)
    return out


def expert_weights_kernel(halved, at_ref, x_ref, geo_ref, act_ref, dgate_ref, dup_ref, *outs):
    step = pl.program_id(0)
    rhs = jnp.concatenate([dgate_ref[0], dup_ref[0]], axis=1)
    both = dg(x_ref[0], rhs, TN).astype(bf16)
    down = dg(act_ref[0], geo_ref[0], TN).astype(bf16)
    for i in range(4):

        @pl.when(step == i)
        def _():
            start = (i % 2) * PIECE if halved else 0
            out = outs[i // 2 if halved else i].at[pl.ds(start, PIECE)]
            out[:WIDTH] = both[:, :HEAD_DIM]
            out[WIDTH : 2 * WIDTH] = both[:, HEAD_DIM:]
            for m in range(WIDTH // HEAD_DIM):
                at = 2 * WIDTH + m * BLOCK
                out[at : at + BLOCK] = down[:, m * HEAD_DIM : (m + 1) * HEAD_DIM]


def expert_weights(ctx_at, steps, halved, arrived, grad_eo, act, grad_gu):
    rows = 2 * ROWS

    def expert(s, at):
        return (at[0] >> 2) ^ of_step([side for _, side in steps], s)

    def lanes(shift):
        return pl.BlockSpec(
            (1, rows, HEAD_DIM),
            lambda s, at: (
                expert(s, at),
                0,
                shift + ((at[0] & 3) ^ of_step([r for r, _ in steps], s)),
            ),
        )

    rows_of = pl.BlockSpec((1, rows, WIDTH), lambda s, at: (expert(s, at), 0, 0))
    count, length = (2, 2 * PIECE) if halved else (4, PIECE)
    return pl.pallas_call(
        lambda *refs: expert_weights_kernel(halved, *refs),
        grid_spec=pltpu.PrefetchScalarGridSpec(
            num_scalar_prefetch=1,
            grid=(4,),
            in_specs=[rows_of, rows_of, lanes(0), lanes(0), lanes(4)],
            out_specs=[whole((length, HEAD_DIM))] * count,
        ),
        out_shape=[jax.ShapeDtypeStruct((length, HEAD_DIM), bf16)] * count,
        cost_estimate=cost(2),
        compiler_params=params(56),
        name="expert_weights",
    )(ctx_at, arrived, grad_eo, act, grad_gu, grad_gu)


def unpack_kernel(count, at_ref, *refs):
    pieces, (gate_ref, up_ref, down_ref) = refs[:count], refs[-3:]
    step = pl.program_id(0)
    for i in range(count):

        @pl.when(step == i)
        def _():
            piece = pieces[i]
            gate_ref[0] = piece[:WIDTH].astype(f32)
            up_ref[0] = piece[WIDTH : 2 * WIDTH].astype(f32)
            for m in range(WIDTH // HEAD_DIM):
                at = 2 * WIDTH + m * BLOCK
                down_ref[0, :, m * HEAD_DIM : (m + 1) * HEAD_DIM] = piece[at : at + BLOCK].astype(
                    f32
                )


def unpack_experts(ctx_at, steps, pieces, filled=()):
    count = len(steps)

    def expert(s, at):
        return (at[0] >> 2) ^ of_step([side for _, side in steps], s)

    def units(s, at):
        return (at[0] & 3) ^ of_step([r for r, _ in steps], s)

    cols = pl.BlockSpec((1, WIDTH, HEAD_DIM), lambda s, at: (expert(s, at), 0, units(s, at)))
    rows = pl.BlockSpec((1, BLOCK, WIDTH), lambda s, at: (expert(s, at), units(s, at), 0))
    anywhere = pl.BlockSpec(memory_space=pl.ANY)
    return pl.pallas_call(
        lambda *refs: unpack_kernel(count, *refs),
        grid_spec=pltpu.PrefetchScalarGridSpec(
            num_scalar_prefetch=1,
            grid=(count,),
            in_specs=[whole((PIECE, HEAD_DIM))] * count + [anywhere] * len(filled),
            out_specs=[cols, cols, rows],
        ),
        out_shape=[
            jax.ShapeDtypeStruct((LOCAL_E, WIDTH, FF_E), f32),
            jax.ShapeDtypeStruct((LOCAL_E, WIDTH, FF_E), f32),
            jax.ShapeDtypeStruct((LOCAL_E, FF_E, WIDTH), f32),
        ],
        input_output_aliases={1 + count + i: i for i in range(len(filled))},
        cost_estimate=cost(2 * count),
        compiler_params=params(48),
        name="unpack_experts",
    )(ctx_at, *pieces, *filled)


def relay_kernel(
    p0, p1, p3, p6, relay_a, relay_b, got_10, got_31, add_a, add_b, part_0, part_1
):
    add_a[...] = (p6[...].astype(f32) + relay_a[...].astype(f32)).astype(bf16)
    add_b[...] = (p3[...].astype(f32) + relay_b[...].astype(f32)).astype(bf16)
    part_0[...] = p0[...].astype(f32) + got_10[...].astype(f32)
    part_1[...] = p1[...].astype(f32) + got_31[...].astype(f32)


def side_kernel(part_0, part_1, got_11, got_30, own, side):
    own[...] = part_0[...] + got_30[...].astype(f32)
    side[...] = (part_1[...] + got_11[...].astype(f32)).astype(bf16)


def piece_sums(kernel, kinds, *pieces):
    specs, arrays = [], []
    for piece in pieces:
        array, second = piece if isinstance(piece, tuple) else (piece, 0)
        specs.append(pl.BlockSpec((PIECE // 4, HEAD_DIM), lambda i, at=4 * second: (i + at, 0)))
        arrays.append(array)
    return pl.pallas_call(
        kernel,
        grid=(4,),
        in_specs=specs,
        out_specs=[pl.BlockSpec((PIECE // 4, HEAD_DIM), lambda i: (i, 0))] * len(kinds),
        out_shape=[jax.ShapeDtypeStruct((PIECE, HEAD_DIM), kind) for kind in kinds],
        cost_estimate=cost(1),
        compiler_params=params(32),
        name="piece_sums",
    )(*arrays)


same_core = [[2 * i + c for i in range(8)] for c in range(2)]
core_swap = [(i, i ^ 1) for i in range(N_EXP)]
y_groups = [[0, 1, 2, 3], [4, 5, 6, 7]]
z_swap = [(i, i ^ 4) for i in range(N_CTX)]


def swap_all(rows, axis, groups=None):
    return lax.all_to_all(
        rows, axis, split_axis=0, concat_axis=0, tiled=True, axis_index_groups=groups
    )


def after(value, *others):
    return lax.optimization_barrier((value,) + others)[0]


def add_low(a, b):
    return (a.astype(f32) + b.astype(f32)).astype(bf16)


def on_device(
    tokens,
    routes,
    route_gates,
    norm_attn,
    norm_ffn,
    query_weight,
    key_weight,
    value_weight,
    out_weight,
    shared_gate,
    shared_up,
    shared_down,
    expert_gate,
    expert_up,
    expert_down,
    cotangent,
):
    exp_at = lax.axis_index("exp").astype(jnp.int32)
    ctx_at = lax.axis_index("ctx").astype(jnp.int32)
    exp_s, ctx_s = exp_at.reshape(1), ctx_at.reshape(1)

    z_at = ctx_at // 4

    w_cat = jnp.concatenate([query_weight, out_weight, key_weight, value_weight], axis=1)
    w_all = lax.all_gather(w_cat, "exp", axis=0, tiled=True)
    gates_high = route_gates[0].astype(bf16)
    gates_low = (route_gates[0] - gates_high.astype(f32)).astype(bf16)
    pad = jnp.zeros((BLOCK, META - 3 * TOPK), bf16)
    up_meta = jnp.concatenate(
        [cotangent[0], routes[0].astype(bf16), gates_high, gates_low, pad], axis=1
    )
    up_all = lax.all_gather(after(up_meta, w_cat), "exp", axis=0, tiled=True)
    gains = after(jnp.concatenate([norm_attn, norm_ffn]), w_cat)
    gains = swap_all(jnp.broadcast_to(gains, (N_EXP, gains.shape[0])), "exp")
    gain_attn = gains[:, :96].reshape(1, WIDTH).astype(f32)
    gain_ffn = gains[:, 96:].reshape(1, WIDTH).astype(f32)

    def of_sequence(rows):
        other = lax.ppermute(rows, "ctx", z_swap)
        pair = jnp.where(
            z_at == 0,
            jnp.concatenate([rows, other], axis=0),
            jnp.concatenate([other, rows], axis=0),
        )
        got = swap_all(jnp.broadcast_to(pair, (4, 2, BLOCK, WIDTH)), "ctx", y_groups)
        return got.reshape(N_CTX, BLOCK, WIDTH)

    tokens_seq = of_sequence(after(tokens, w_cat))
    shared_cols = jnp.concatenate(
        [shared_gate.reshape(96, N_EXP, SHARED), shared_up.reshape(96, N_EXP, SHARED)], axis=2
    ).transpose(1, 0, 2)
    w_shared = swap_all(shared_cols, "exp").reshape(WIDTH, 2 * SHARED)
    shared_two = jnp.concatenate([shared_down, shared_down], axis=0)

    hidden_one = norm_rows(tokens, gain_attn)
    hidden_seq = norm_rows(tokens_seq, gain_attn)
    hidden_seq = after(hidden_seq, w_shared)
    queries, kv_all = project(hidden_one, hidden_seq, w_all)
    attended, att_f, logs = attend(ctx_s, queries, kv_all)
    middle, hidden_two = middle_norm(attended, w_all, tokens[0], gain_ffn)

    hidden_all = lax.all_gather(hidden_two, "exp", axis=0, tiled=True)
    hidden_all = hidden_all.reshape(HALF, 2, BLOCK, WIDTH)
    att_seq = of_sequence(attended[None])
    place, grad_eo, grad_eh, grad_sh, slot_gate = place_rows(
        exp_s,
        after(up_all, hidden_two).reshape(HALF, 2, BLOCK, WIDTH + META),
        expert_down,
        shared_two,
    )
    part, arrived, act, grad_gu, shared_act, shared_grad = expert_back(
        exp_s, after(hidden_all, att_seq), place, grad_eh, grad_sh, expert_gate, expert_up, w_shared
    )
    summed = add_low(part[1], lax.ppermute(part[0], "exp", core_swap))
    grad_two = swap_all(summed, "exp", same_core)

    rows_e = 2 * ROWS
    operands = (
        after(arrived, summed).reshape(LOCAL_E, rows_e, WIDTH),
        grad_eo.reshape(LOCAL_E, rows_e, WIDTH),
        act.reshape(LOCAL_E, rows_e, FF_E),
        grad_gu.reshape(LOCAL_E, rows_e, 2 * FF_E),
    )
    for_1, for_3 = expert_weights(ctx_s, ((2, 0), (1, 0), (2, 1), (3, 1)), True, *operands)
    operands = (after(operands[0], for_1),) + operands[1:]
    p0, p6, p1, p3 = expert_weights(ctx_s, ((0, 0), (3, 0), (0, 1), (1, 1)), False, *operands)

    def to(rows, k):
        return lax.ppermute(rows, "ctx", [(i, i ^ k) for i in range(N_CTX)])

    from_1, from_3 = to(for_1, 1), to(for_3, 3)
    shared_grad_late = after(shared_grad, p0).reshape(N_EXP * BLOCK, META)
    grad_scols = dg(hidden_all.reshape(N_EXP * BLOCK, WIDTH), shared_grad_late, TN).astype(bf16)
    act_late = after(shared_act, p0).reshape(N_EXP * BLOCK, META)
    grad_sdown = dg(act_late, up_all, TN)[:SHARED, :WIDTH].astype(bf16)
    extra = jnp.concatenate(
        [
            jnp.pad(
                grad_scols.reshape(N_EXP, N_CTX, 12, META).transpose(1, 0, 2, 3),
                ((0, 0), (0, 0), (0, 4), (0, 0)),
            ).reshape(N_CTX, 16 * N_EXP, META),
            grad_sdown.reshape(N_CTX, 8, HEADS, 128).transpose(0, 2, 1, 3).reshape(N_CTX, 96, 128),
        ],
        axis=1,
    )

    out_part = expert_output(
        exp_s, after(act, p0), slot_gate, place, shared_act, expert_down, shared_two
    )
    grad_two = after(grad_two, extra, out_part)
    grad_middle, grad_attn, grad_heads, gain_rows = middle_back(
        grad_two, middle, cotangent[0], gain_ffn, w_all
    )
    grad_query, near, far = attend_back(
        ctx_s, queries, grad_heads, att_f, logs, kv_all, grad_attn, extra, gain_rows
    )
    far = lax.ppermute(far, "ctx", z_swap)
    from_1, from_3 = after((from_1, from_3), near)
    add_a, add_b, part_0, part_1 = piece_sums(
        relay_kernel,
        (bf16, bf16, f32, f32),
        p0,
        p1,
        p3,
        p6,
        (from_1, 0),
        (from_3, 0),
        (from_1, 1),
        (from_3, 1),
    )
    got_11, got_30 = to(add_b, 1), to(add_a, 3)

    def from_x(rows, k):
        return lax.ppermute(rows, "exp", [(i, i ^ (4 * k)) for i in range(N_EXP)])

    out_sums = spread_sums(
        exp_s,
        after(out_part, add_a),
        lax.ppermute(out_part[0, :4], "exp", core_swap),
        lax.ppermute(out_part[0, 4:], "exp", core_swap),
    )
    out_near = (
        out_sums[0].astype(f32)
        + from_x(out_sums[1], 1).astype(f32)
        + from_x(out_sums[3], 3).astype(f32)
    )
    got_11, got_30 = after((got_11, got_30), far)
    own_part, side = piece_sums(side_kernel, (f32, bf16), part_0, part_1, got_11, got_30)
    across = to(side, 4)
    out_2 = from_x(after(out_sums[2], side), 2)

    shares = merge_shares(ctx_s, near, after(far, side, out_near))
    got = swap_all(shares, "ctx", y_groups)
    own = (own_part + after(across, shares).astype(f32)).astype(bf16)
    at_1, at_3, at_z = to(own, 1), to(own, 3), to(own, 4)

    columns, grad_kv, grad_down = column_grads(got, after(hidden_seq, own), att_seq)
    out_rows = after(out_near, columns) + out_2.astype(f32)
    out_across = lax.ppermute(
        out_rows[1].astype(bf16), "exp", [(i, i ^ 2) for i in range(N_EXP)]
    )
    columns = after(columns, at_1, at_3, out_2)
    owned = swap_all(columns, "exp")
    owned, gain_sum = owned_sums(owned, grad_down)
    owned, at_z1, at_z3 = lax.optimization_barrier(
        (after(owned, out_across), to(at_z, 1), to(at_z, 3))
    )
    at_2, at_z2 = to(at_3, 1), to(at_z1, 3)
    mixed = (middle + out_rows[0] + out_across.astype(f32)).astype(bf16)[None]
    experts = unpack_experts(
        ctx_s, ((0, 0), (1, 0), (3, 0), (0, 1)), (after(own, owned), at_1, at_3, at_z)
    )
    owned = jnp.broadcast_to(owned, (N_CTX, OWNED_ROWS, HEAD_DIM))
    owned = swap_all(jnp.concatenate([grad_kv, owned], axis=1), "ctx")
    gain_attn_sum, *dense = finish(
        after(owned, experts[0], mixed),
        norm_attn.astype(f32).reshape(96, 1),
        query_weight,
        key_weight,
        value_weight,
    )
    input_grad = input_back(grad_query, owned, w_all, tokens[0], gain_attn, grad_middle)
    at_2 = after(at_2, input_grad, *dense)
    experts = unpack_experts(
        ctx_s, ((2, 0), (1, 1), (3, 1), (2, 1)), (at_2, at_z1, at_z3, at_z2), experts
    )
    return (
        mixed,
        input_grad[None],
        gain_attn_sum[:, 0],
        gain_sum[12, :96],
        *dense,
        *experts,
    )


def solution(mesh):
    token_spec = P("exp", "ctx", None)
    rows = P("exp", None)
    expert = P("exp", None, None)
    placed = (token_spec,) * 3 + (P("exp"),) * 2 + (rows,) * 7 + (expert,) * 3 + (token_spec,)
    return jax.shard_map(
        on_device,
        mesh=mesh,
        in_specs=placed,
        out_specs=(token_spec,) * 2 + (P("exp"),) * 2 + (rows,) * 7 + (expert,) * 3,
        check_vma=False,
    )
```

```python
import jax
import jax.numpy as jnp
from jax import lax
from jax.sharding import PartitionSpec as P
from jax.experimental import pallas as pl
from jax.experimental.pallas import tpu as pltpu

HEADS = 12
KV_HEADS = 4
HEAD_DIM = 128
TOPK = 6
GROUP = 3
BLOCK = 128
WIDTH = 1536
KV_WIDTH = KV_HEADS * HEAD_DIM
CAP = 48
N_EXP = 16
N_CTX = 8
LOCAL_E = 2
FF_E = 512
SHARED = 64
META = 128
HALF = 8
ROWS = HALF * CAP

epsilon = 1e-05
masked_score = -1e30
f32 = jnp.float32
bf16 = jnp.bfloat16
log2_e = 1.4426950408889634
score_scale = HEAD_DIM ** (-0.5) * log2_e

NN = (((1,), (0,)), ((), ()))
NT = (((1,), (1,)), ((), ()))
TN = (((0,), (0,)), ((), ()))


def dg(a, b, dims):
    return lax.dot_general(a, b, dims, preferred_element_type=f32)


def params(mib):
    return pltpu.CompilerParams(vmem_limit_bytes=mib * 1024 * 1024)


def cost(us):
    return pl.CostEstimate(flops=0, bytes_accessed=int(us * 3690000), transcendentals=0)


def whole(shape):
    return pl.BlockSpec(shape, lambda *_: (0,) * len(shape), pipeline_mode=pl.Buffered(1))


def sigmoid(v):
    return 1.0 / (1.0 + jnp.exp(-v))


def allowed_scores(ctx_at):
    rows = lax.broadcasted_iota(jnp.int32, (GROUP * BLOCK, N_CTX * BLOCK), 0) % BLOCK
    cols = lax.broadcasted_iota(jnp.int32, (GROUP * BLOCK, N_CTX * BLOCK), 1)
    return rows + ctx_at * BLOCK >= cols


def stack_heads(block):
    return jnp.concatenate([block[:, j * HEAD_DIM : (j + 1) * HEAD_DIM] for j in range(GROUP)], axis=0)


def unstack_heads(rows):
    return jnp.concatenate([rows[j * BLOCK : (j + 1) * BLOCK] for j in range(GROUP)], axis=1)


def attend_kernel(ctx_ref, q_ref, k_ref, v_ref, att_ref, attf_ref, log_ref):
    q = stack_heads(q_ref[...])
    keys = k_ref[...].reshape(N_CTX * BLOCK, HEAD_DIM)
    values = v_ref[...].reshape(N_CTX * BLOCK, HEAD_DIM)
    scores = jnp.where(allowed_scores(ctx_ref[0]), dg(q, keys, NT) * score_scale, masked_score)
    top = jnp.max(scores, axis=-1, keepdims=True)
    weights = jnp.exp2(scores - top)
    total = jnp.sum(weights, axis=-1, keepdims=True)
    out = dg(weights.astype(bf16), values, NN) * (1.0 / total)
    out = unstack_heads(out)
    attf_ref[...] = out
    att_ref[...] = out.astype(bf16)
    log_ref[...] = jnp.broadcast_to(top + jnp.log2(total), (GROUP * BLOCK, HEAD_DIM))


def kv_specs():
    return [
        pl.BlockSpec((N_CTX, BLOCK, HEAD_DIM), lambda g: (0, 0, g)),
        pl.BlockSpec((N_CTX, BLOCK, HEAD_DIM), lambda g: (0, 0, KV_HEADS + g)),
    ]


def head_spec():
    return pl.BlockSpec((BLOCK, GROUP * HEAD_DIM), lambda g: (0, g))


def attend(ctx_at, qkv, kv_all):
    return pl.pallas_call(
        attend_kernel,
        grid=(KV_HEADS,),
        in_specs=[pl.BlockSpec(memory_space=pltpu.SMEM), head_spec()] + kv_specs(),
        out_specs=[
            head_spec(),
            head_spec(),
            pl.BlockSpec((GROUP * BLOCK, HEAD_DIM), lambda g: (g, 0)),
        ],
        out_shape=[
            jax.ShapeDtypeStruct((BLOCK, WIDTH), bf16),
            jax.ShapeDtypeStruct((BLOCK, WIDTH), f32),
            jax.ShapeDtypeStruct((HEADS * BLOCK, HEAD_DIM), f32),
        ],
        cost_estimate=cost(6),
        compiler_params=params(48),
        name="attend",
    )(ctx_at, qkv, kv_all, kv_all)


SEQ = N_CTX * BLOCK
AT_QUERY, AT_MIXED, AT_OUT = SEQ, SEQ + BLOCK, SEQ + 2 * BLOCK
AT_SHARED = SEQ + 3 * BLOCK
AT_DOWN = AT_SHARED + 16 * N_EXP
AT_GAIN = AT_DOWN + 96
SENT_ROWS = AT_GAIN + 16


def halves(a, b, lane):
    low = jnp.where(lane < 64, a, pltpu.roll(b, 64, 1))
    high = jnp.where(lane < 64, pltpu.roll(a, 64, 1), b)
    return low, high


def attend_back_kernel(
    ctx_ref,
    q_ref,
    ga_ref,
    attf_ref,
    log_ref,
    k_ref,
    v_ref,
    all_ga_ref,
    extra_ref,
    gain_ref,
    dq_ref,
    near_ref,
    far_ref,
    kept_ref,
):
    group = pl.program_id(0)
    z_at = ctx_ref[0] // 4

    def send(dest, z, start, stop, rows):
        @pl.when(z_at == z)
        def _():
            near_ref[dest, start:stop] = rows

        @pl.when(z_at != z)
        def _():
            far_ref[dest, start:stop] = rows

    q = stack_heads(q_ref[...])
    grad = stack_heads(ga_ref[...])
    delta = jnp.sum(grad.astype(f32) * stack_heads(attf_ref[...]), axis=-1, keepdims=True)
    keys = k_ref[...].reshape(SEQ, HEAD_DIM)
    values = v_ref[...].reshape(SEQ, HEAD_DIM)
    scores = jnp.where(allowed_scores(ctx_ref[0]), dg(q, keys, NT) * score_scale, masked_score)
    weights = jnp.exp2(scores - log_ref[:, :1])
    grad_weights = dg(grad, values, NT)
    grad_raw = (weights * (grad_weights - delta)).astype(bf16)
    scale = HEAD_DIM ** (-0.5)
    dq = unstack_heads(dg(grad_raw, keys, NN) * scale)
    dq_ref[...] = dq.astype(bf16)
    kept_ref[group] = dq
    grad_k = dg(grad_raw, q, TN) * scale
    grad_v = dg(weights.astype(bf16), grad, TN)
    low, high = halves(grad_k, grad_v, lax.broadcasted_iota(jnp.int32, (SEQ, HEAD_DIM), 1))
    low, high = low.astype(bf16), high.astype(bf16)
    send(2 * (group % 2), group // 2, 0, SEQ, low)
    send(2 * (group % 2) + 1, group // 2, 0, SEQ, high)

    @pl.when(group == KV_HEADS - 1)
    def _():
        lane = lax.broadcasted_iota(jnp.int32, (BLOCK, HEAD_DIM), 1)

        def dq_tile(m):
            return kept_ref[m // GROUP, :, HEAD_DIM * (m % GROUP) : HEAD_DIM * (m % GROUP + 1)]

        def ga_tile(m):
            return all_ga_ref[:, HEAD_DIM * m : HEAD_DIM * (m + 1)].astype(f32)

        mixed = []
        for m in range(KV_HEADS):
            mixed += halves(dq_tile(N_CTX + m), ga_tile(N_CTX + m), lane)
        gains = gain_ref[...].astype(bf16)
        for c in range(N_CTX):
            tiles = [dq_tile(c).astype(bf16), mixed[c].astype(bf16), ga_tile(c).astype(bf16)]
            rows = jnp.concatenate(tiles + [extra_ref[c], gains], axis=0)
            send(c % 4, c // 4, AT_QUERY, SENT_ROWS, rows)


def attend_back(ctx_at, qkv, grad_att, att_f, logs, kv_all, grad_attn, extra, gain_rows):
    return pl.pallas_call(
        attend_back_kernel,
        grid=(KV_HEADS,),
        in_specs=[
            pl.BlockSpec(memory_space=pltpu.SMEM),
            head_spec(),
            head_spec(),
            head_spec(),
            pl.BlockSpec((GROUP * BLOCK, HEAD_DIM), lambda g: (g, 0)),
        ]
        + kv_specs()
        + [
            whole((BLOCK, WIDTH)),
            whole((N_CTX, AT_GAIN - AT_SHARED, HEAD_DIM)),
            whole((16, HEAD_DIM)),
        ],
        out_specs=[head_spec()] + [whole((4, SENT_ROWS, HEAD_DIM))] * 2,
        out_shape=[
            jax.ShapeDtypeStruct((BLOCK, WIDTH), bf16),
            jax.ShapeDtypeStruct((4, SENT_ROWS, HEAD_DIM), bf16),
            jax.ShapeDtypeStruct((4, SENT_ROWS, HEAD_DIM), bf16),
        ],
        scratch_shapes=[pltpu.VMEM((KV_HEADS, BLOCK, GROUP * HEAD_DIM), f32)],
        cost_estimate=cost(2),
        compiler_params=params(60),
        name="attend_back",
    )(ctx_at, qkv, grad_att, att_f, logs, kv_all, kv_all, grad_attn, extra, gain_rows)


def middle_kernel(att_ref, w_ref, x_ref, gain_ref, middle_ref, hidden_ref):
    middle = x_ref[...].astype(f32) + dg(att_ref[...], w_ref[...], NN)
    inv = lax.rsqrt(jnp.mean(middle * middle, axis=-1, keepdims=True) + epsilon)
    middle_ref[...] = middle
    hidden_ref[...] = (middle * inv * gain_ref[...]).astype(bf16)


def w_cols(width, at):
    return pl.BlockSpec((WIDTH, width), lambda *_: (0, at), pipeline_mode=pl.Buffered(1))


def middle_norm(attended, w_all, tokens, gain):
    return pl.pallas_call(
        middle_kernel,
        grid=(1,),
        in_specs=[
            whole((BLOCK, WIDTH)),
            w_cols(WIDTH, 1),
            whole((BLOCK, WIDTH)),
            whole((1, WIDTH)),
        ],
        out_specs=[whole((BLOCK, WIDTH)), whole((BLOCK, WIDTH))],
        out_shape=[
            jax.ShapeDtypeStruct((BLOCK, WIDTH), f32),
            jax.ShapeDtypeStruct((BLOCK, WIDTH), bf16),
        ],
        cost_estimate=cost(2),
        compiler_params=params(60),
        name="middle_norm",
    )(attended, w_all, tokens, gain)


def norm_back(grad_normed, normed, inv_root):
    return inv_root * (
        grad_normed - normed * jnp.mean(grad_normed * normed, axis=-1, keepdims=True)
    )


def middle_back_kernel(
    pieces_ref, middle_ref, up_ref, gain_ref, w_ref, gm_ref, ga_ref, gh_ref, gg_ref
):
    grad_two = pieces_ref[0].astype(f32)
    for i in range(1, HALF):
        grad_two = grad_two + pieces_ref[i].astype(f32)
    middle = middle_ref[...]
    inv = lax.rsqrt(jnp.mean(middle * middle, axis=-1, keepdims=True) + epsilon)
    normed = middle * inv
    gains = jnp.sum(grad_two * normed, axis=0, keepdims=True)
    gg_ref[...] = jnp.zeros((16, HEAD_DIM), f32)
    for m in range(HEADS):
        gg_ref[m : m + 1] = gains[:, HEAD_DIM * m : HEAD_DIM * (m + 1)]
    grad_middle = up_ref[...].astype(f32) + norm_back(grad_two * gain_ref[...], normed, inv)
    gm_ref[...] = grad_middle
    grad_attn = grad_middle.astype(bf16)
    ga_ref[...] = grad_attn
    gh_ref[...] = dg(grad_attn, w_ref[...], NT).astype(bf16)


def middle_back(pieces, middle, upstream, gain, w_all):
    return pl.pallas_call(
        middle_back_kernel,
        grid=(1,),
        in_specs=[
            whole((HALF, BLOCK, WIDTH)),
            whole((BLOCK, WIDTH)),
            whole((BLOCK, WIDTH)),
            whole((1, WIDTH)),
            w_cols(WIDTH, 1),
        ],
        out_specs=[whole((BLOCK, WIDTH))] * 3 + [whole((16, HEAD_DIM))],
        out_shape=[
            jax.ShapeDtypeStruct((BLOCK, WIDTH), f32),
            jax.ShapeDtypeStruct((BLOCK, WIDTH), bf16),
            jax.ShapeDtypeStruct((BLOCK, WIDTH), bf16),
            jax.ShapeDtypeStruct((16, HEAD_DIM), f32),
        ],
        cost_estimate=cost(1),
        compiler_params=params(48),
        name="middle_back",
    )(pieces, middle, upstream, gain, w_all)


def place_kernel(
    at_ref, up_ref, down_ref, sdown_ref, place_ref, geo_ref, geh_ref, gsh_ref, gate_ref
):
    lane = lax.broadcasted_iota(jnp.int32, (BLOCK, META), 1)
    row = lax.broadcasted_iota(jnp.int32, (BLOCK, META), 0)
    before = (row > lane).astype(bf16)
    slot = (lane % 64).astype(f32)
    first_id = (at_ref[0] * LOCAL_E).astype(f32)
    row_id = first_id + (row >= 64).astype(f32)

    for chip in range(HALF):
        meta = up_ref[chip, 0, :, WIDTH:].astype(f32)
        named = lane < TOPK
        zero = jnp.zeros((BLOCK, META), f32)
        hit0 = jnp.where(named & (meta == first_id), 1.0, zero)
        hit1 = jnp.where(named & (meta == first_id + 1.0), 1.0, zero)
        mask = jnp.where(
            lane < 64,
            jnp.sum(hit0, axis=1, keepdims=True),
            jnp.sum(hit1, axis=1, keepdims=True),
        )
        rank = dg(before, mask.astype(bf16), NN)
        place = jnp.where((mask > 0.5) & (rank == slot), 1.0, zero).astype(bf16)
        place_ref[chip, 0] = place
        rows = dg(place, up_ref[chip, 0], TN)
        slot_meta = rows[:, WIDTH:]
        gates = pltpu.roll(slot_meta, META - TOPK, 1) + pltpu.roll(
            slot_meta, META - 2 * TOPK, 1
        )
        gate = jnp.sum(
            jnp.where(named & (slot_meta == row_id), gates, zero), axis=1, keepdims=True
        )
        geo = (gate * rows[:, :WIDTH]).astype(bf16)
        wide_gate = jnp.broadcast_to(gate, (BLOCK, META))
        at = chip * CAP
        for e in range(LOCAL_E):
            geo_ref[e, 0, at : at + CAP] = geo[64 * e : 64 * e + CAP]
            gate_ref[e, 0, at : at + CAP] = wide_gate[64 * e : 64 * e + CAP]
        gsh_ref[chip, 0] = dg(up_ref[chip, 0, :, :WIDTH], sdown_ref[...], NT)
    for e in range(LOCAL_E):
        geh_ref[e, 0] = dg(geo_ref[e, 0], down_ref[e], NT)


def by_core(cols):
    return pl.BlockSpec(
        (HALF, 1, BLOCK, cols),
        lambda s, at: (0, jnp.where(s == 0, 1 - at[0] % 2, at[0] % 2), 0, 0),
    )


def by_step(cols):
    return pl.BlockSpec((LOCAL_E, 1, ROWS, cols), lambda s, at: (0, s, 0, 0))


def place_rows(exp_at, up_all, expert_down, shared_two):
    return pl.pallas_call(
        place_kernel,
        grid_spec=pltpu.PrefetchScalarGridSpec(
            num_scalar_prefetch=1,
            grid=(2,),
            in_specs=[
                by_core(WIDTH + META),
                whole((LOCAL_E, FF_E, WIDTH)),
                whole((2 * SHARED, WIDTH)),
            ],
            out_specs=[by_core(META), by_step(WIDTH), by_step(FF_E), by_core(META), by_step(META)],
        ),
        out_shape=[
            jax.ShapeDtypeStruct((HALF, 2, BLOCK, META), bf16),
            jax.ShapeDtypeStruct((LOCAL_E, 2, ROWS, WIDTH), bf16),
            jax.ShapeDtypeStruct((LOCAL_E, 2, ROWS, FF_E), f32),
            jax.ShapeDtypeStruct((HALF, 2, BLOCK, META), f32),
            jax.ShapeDtypeStruct((LOCAL_E, 2, ROWS, META), f32),
        ],
        cost_estimate=cost(14),
        compiler_params=params(56),
        name="place_rows",
    )(exp_at, up_all, expert_down, shared_two)


def expert_kernel(
    at_ref,
    hid_ref,
    place_ref,
    geh_ref,
    gsh_ref,
    wg_ref,
    wu_ref,
    ws_ref,
    part_ref,
    x_ref,
    act_ref,
    dgu_ref,
    sact_ref,
    sgrad_ref,
):
    for chip in range(HALF):
        rows = dg(place_ref[chip, 0], hid_ref[chip, 0], TN).astype(bf16)
        at = chip * CAP
        for e in range(LOCAL_E):
            x_ref[e, 0, at : at + CAP] = rows[64 * e : 64 * e + CAP]
    pairs = []
    for e in range(LOCAL_E):
        pre_gate = dg(x_ref[e, 0], wg_ref[e], NN)
        pre_up = dg(x_ref[e, 0], wu_ref[e], NN)
        sig = sigmoid(pre_gate)
        act = pre_gate * sig
        act_ref[e, 0] = (act * pre_up).astype(bf16)
        geh = geh_ref[e, 0]
        d_gate = (geh * pre_up * (sig * (1.0 + pre_gate * (1.0 - sig)))).astype(bf16)
        d_up = (geh * act).astype(bf16)
        dgu_ref[e, 0, :, :FF_E] = d_gate
        dgu_ref[e, 0, :, FF_E:] = d_up
        pairs.append((dg(d_gate, wg_ref[e], NT) + dg(d_up, wu_ref[e], NT)).astype(bf16))
    lane = lax.broadcasted_iota(jnp.int32, (BLOCK, 2 * SHARED), 1) < SHARED
    gap = jnp.zeros((64 - CAP, WIDTH), bf16)
    for chip in range(HALF):
        pre = dg(hid_ref[chip, 0], ws_ref[...], NN)
        turned = pltpu.roll(pre, SHARED, 1)
        gate, up = jnp.where(lane, pre, turned), jnp.where(lane, turned, pre)
        sig = sigmoid(gate)
        act = gate * sig
        sact_ref[chip, 0] = jnp.where(lane, act * up, 0.0).astype(bf16)
        slope = sig * (1.0 + gate * (1.0 - sig))
        sgrad = (gsh_ref[chip, 0] * jnp.where(lane, up * slope, act)).astype(bf16)
        sgrad_ref[chip, 0] = sgrad
        at = chip * CAP
        stacked = jnp.concatenate([pairs[0][at : at + CAP], gap, pairs[1][at : at + CAP], gap], 0)
        part_ref[0, chip] = (
            dg(place_ref[chip, 0], stacked, NN) + dg(sgrad, ws_ref[...], NT)
        ).astype(bf16)


def expert_back(exp_at, hidden, place, geh, gsh, wg, wu, ws):
    return pl.pallas_call(
        expert_kernel,
        grid_spec=pltpu.PrefetchScalarGridSpec(
            num_scalar_prefetch=1,
            grid=(2,),
            in_specs=[
                by_core(WIDTH),
                by_core(META),
                by_step(FF_E),
                by_core(META),
                whole((LOCAL_E, WIDTH, FF_E)),
                whole((LOCAL_E, WIDTH, FF_E)),
                whole((WIDTH, 2 * SHARED)),
            ],
            out_specs=[
                pl.BlockSpec((1, HALF, BLOCK, WIDTH), lambda s, at: (s, 0, 0, 0)),
                by_step(WIDTH),
                by_step(FF_E),
                by_step(2 * FF_E),
                by_core(META),
                by_core(META),
            ],
        ),
        out_shape=[
            jax.ShapeDtypeStruct((2, HALF, BLOCK, WIDTH), bf16),
            jax.ShapeDtypeStruct((LOCAL_E, 2, ROWS, WIDTH), bf16),
            jax.ShapeDtypeStruct((LOCAL_E, 2, ROWS, FF_E), bf16),
            jax.ShapeDtypeStruct((LOCAL_E, 2, ROWS, 2 * FF_E), bf16),
            jax.ShapeDtypeStruct((HALF, 2, BLOCK, META), bf16),
            jax.ShapeDtypeStruct((HALF, 2, BLOCK, META), bf16),
        ],
        cost_estimate=cost(28),
        compiler_params=params(60),
        name="expert_back",
    )(exp_at, hidden, place, geh, gsh, wg, wu, ws)


def output_kernel(at_ref, act_ref, gate_ref, place_ref, sact_ref, wd_ref, sd_ref, part_ref):
    outs = []
    for e in range(LOCAL_E):
        out = dg(act_ref[e, 0], wd_ref[e], NN).astype(bf16).astype(f32)
        outs.append((out * gate_ref[e, 0, :, :1]).astype(bf16))
    gap = jnp.zeros((64 - CAP, WIDTH), bf16)
    for chip in range(HALF):
        at = chip * CAP
        stacked = jnp.concatenate([outs[0][at : at + CAP], gap, outs[1][at : at + CAP], gap], 0)
        part_ref[0, chip] = (
            dg(place_ref[chip, 0], stacked, NN) + dg(sact_ref[chip, 0], sd_ref[...], NN)
        ).astype(bf16)


def expert_output(exp_at, act, gate, place, sact, wd, sd):
    return pl.pallas_call(
        output_kernel,
        grid_spec=pltpu.PrefetchScalarGridSpec(
            num_scalar_prefetch=1,
            grid=(2,),
            in_specs=[
                by_step(FF_E),
                by_step(META),
                by_core(META),
                by_core(META),
                whole((LOCAL_E, FF_E, WIDTH)),
                whole((2 * SHARED, WIDTH)),
            ],
            out_specs=pl.BlockSpec((1, HALF, BLOCK, WIDTH), lambda s, at: (s, 0, 0, 0)),
        ),
        out_shape=jax.ShapeDtypeStruct((2, HALF, BLOCK, WIDTH), bf16),
        cost_estimate=cost(2),
        compiler_params=params(48),
        name="expert_output",
    )(exp_at, act, gate, place, sact, wd, sd)


SHARE = 3 * BLOCK
TO_SHARED = SEQ + 2 * SHARE
TO_DOWN = TO_SHARED + 16 * N_EXP
TO_GAIN = TO_DOWN + 96
MERGED_ROWS = TO_GAIN + 16


def merge_kernel(ctx_ref, near_ref, got_ref, out_ref):
    z_at = ctx_ref[0] // 4
    near, got = near_ref[0], got_ref[0]

    def add(a, b):
        return (a.astype(f32) + b.astype(f32)).astype(bf16)

    out_ref[0, :SEQ] = add(near[:SEQ], got[:SEQ])
    out_ref[0, TO_SHARED:] = add(near[AT_SHARED:], got[AT_SHARED:])
    mine, theirs = near[AT_QUERY:AT_SHARED], got[AT_QUERY:AT_SHARED]
    out_ref[0, SEQ : SEQ + SHARE] = jnp.where(z_at == 0, mine, theirs)
    out_ref[0, SEQ + SHARE : TO_SHARED] = jnp.where(z_at == 0, theirs, mine)


def merge_shares(ctx_at, near, got):
    spec = pl.BlockSpec((1, SENT_ROWS, HEAD_DIM), lambda i: (i, 0, 0))
    return pl.pallas_call(
        merge_kernel,
        grid=(4,),
        in_specs=[pl.BlockSpec(memory_space=pltpu.SMEM), spec, spec],
        out_specs=pl.BlockSpec((1, MERGED_ROWS, HEAD_DIM), lambda i: (i, 0, 0)),
        out_shape=jax.ShapeDtypeStruct((4, MERGED_ROWS, HEAD_DIM), bf16),
        cost_estimate=cost(3),
        compiler_params=params(32),
        name="merge_shares",
    )(ctx_at, near, got)


def columns_kernel(got_ref, hidden_ref, att_ref, sent_ref, kv_ref, down_ref):
    def summed(start, stop):
        out = got_ref[0, start:stop].astype(f32)
        for src in range(1, 4):
            out = out + got_ref[src, start:stop].astype(f32)
        return out

    grad_kv = summed(0, SEQ).astype(bf16)
    kv_ref[...] = grad_kv.reshape(N_CTX, BLOCK, HEAD_DIM)

    def rows_of(tile, order):
        at = SEQ + BLOCK * tile
        return jnp.concatenate(
            [got_ref[y, at + SHARE * z : at + SHARE * z + BLOCK] for z, y in order], axis=0
        )

    in_order = [(i // 4, i % 4) for i in range(N_CTX)]
    y_order = [(i % 2, i // 2) for i in range(N_CTX)]
    lane = lax.broadcasted_iota(jnp.int32, (SEQ, HEAD_DIM), 1)
    zero = jnp.zeros((SEQ, HEAD_DIM), bf16)
    mixed_q = jnp.where(lane < 64, rows_of(1, in_order), zero)
    mixed_o = jnp.where(lane < 64, zero, rows_of(1, y_order))
    left = jnp.concatenate([rows_of(0, in_order).T, mixed_q.T, grad_kv.T], axis=0)
    right = jnp.concatenate([mixed_o.T, rows_of(2, y_order).T], axis=0)
    by_hidden = dg(left, hidden_ref[...].reshape(SEQ, WIDTH), NN)
    by_att = dg(right, att_ref[...].reshape(SEQ, WIDTH), NN)
    tiles = [
        by_hidden[:BLOCK],
        by_hidden[BLOCK : 2 * BLOCK] + by_att[:BLOCK],
        by_att[BLOCK:],
        by_hidden[2 * BLOCK :],
    ]
    for t, tile in enumerate(tiles):
        sent_ref[:, :96, HEAD_DIM * t : HEAD_DIM * (t + 1)] = (
            tile.T.astype(bf16).reshape(N_EXP, 96, HEAD_DIM)
        )

    down_ref[...] = summed(TO_DOWN, TO_GAIN).astype(bf16)
    shared = summed(TO_SHARED, TO_DOWN)
    gains = summed(TO_GAIN, MERGED_ROWS)
    row = lax.broadcasted_iota(jnp.int32, (16, HEAD_DIM), 0)
    one_lane = lax.broadcasted_iota(jnp.int32, (1, HEAD_DIM), 1)
    for i in range(N_EXP):
        m, offset = (96 * i) // HEAD_DIM, (96 * i) % HEAD_DIM
        gain = gains[m : m + 1]
        if offset:
            shift = HEAD_DIM - offset
            gain = jnp.where(
                one_lane < shift,
                pltpu.roll(gain, shift, 1),
                pltpu.roll(gains[m + 1 : m + 2], shift, 1),
            )
        rows = jnp.where(row == 12, jnp.broadcast_to(gain, (16, HEAD_DIM)), shared[16 * i : 16 * i + 16])
        sent_ref[i, 96:, :HEAD_DIM] = rows.astype(bf16)
        sent_ref[i, 96:, HEAD_DIM:] = jnp.zeros((16, 512 - HEAD_DIM), bf16)


def column_grads(got, hidden_seq, att_seq):
    return pl.pallas_call(
        columns_kernel,
        out_shape=[
            jax.ShapeDtypeStruct((N_EXP, 112, 512), bf16),
            jax.ShapeDtypeStruct((N_CTX, BLOCK, HEAD_DIM), bf16),
            jax.ShapeDtypeStruct((96, HEAD_DIM), bf16),
        ],
        cost_estimate=cost(8),
        compiler_params=params(56),
        name="column_grads",
    )(got, hidden_seq, att_seq)


OWNED_ROWS = 4 * 96 + 16 * N_EXP + 96


def owned_kernel(got_ref, down_ref, owned_ref, gain_ref):
    total = got_ref[0, :96].astype(f32)
    gains = got_ref[0, 96:, :HEAD_DIM].astype(f32)
    for src in range(1, N_EXP):
        total = total + got_ref[src, :96].astype(f32)
        gains = gains + got_ref[src, 96:, :HEAD_DIM].astype(f32)
    gain_ref[...] = gains
    for t in range(4):
        owned_ref[96 * t : 96 * t + 96] = total[:, HEAD_DIM * t : HEAD_DIM * (t + 1)].astype(bf16)
    for src in range(N_EXP):
        at = 384 + 16 * src
        owned_ref[at : at + 16] = got_ref[src, 96:, :HEAD_DIM]
    owned_ref[384 + 16 * N_EXP :] = down_ref[...]


def owned_sums(got, down):
    return pl.pallas_call(
        owned_kernel,
        out_shape=[
            jax.ShapeDtypeStruct((OWNED_ROWS, HEAD_DIM), bf16),
            jax.ShapeDtypeStruct((16, HEAD_DIM), f32),
        ],
        cost_estimate=cost(3),
        compiler_params=params(32),
        name="owned_sums",
    )(got, down)


def finish_kernel(
    got_ref,
    gain_in_ref,
    wq_ref,
    wk_ref,
    wv_ref,
    gain_ref,
    q_ref,
    k_ref,
    v_ref,
    out_ref,
    sg_ref,
    su_ref,
    sd_ref,
):
    lane = lax.broadcasted_iota(jnp.int32, (96, HEAD_DIM), 1)

    def tile(c, t):
        at = BLOCK + 96 * t
        return got_ref[c, at : at + 96].astype(f32)

    for c in range(N_CTX):
        at = HEAD_DIM * c
        q_ref[:, at : at + HEAD_DIM] = tile(c, 0)
        out_ref[:, at : at + HEAD_DIM] = tile(c, 2)
    for m in range(N_CTX // 2):
        at = HEAD_DIM * m
        low, high = halves(tile(2 * m, 1), tile(2 * m + 1, 1), lane)
        q_ref[:, 1024 + at : 1024 + at + HEAD_DIM] = low
        out_ref[:, 1024 + at : 1024 + at + HEAD_DIM] = high
        low, high = halves(tile(2 * m, 3), tile(2 * m + 1, 3), lane)
        k_ref[:, at : at + HEAD_DIM] = low
        v_ref[:, at : at + HEAD_DIM] = high
    gain = (
        jnp.sum(q_ref[...] * wq_ref[...].astype(f32), axis=1, keepdims=True)
        + jnp.sum(k_ref[...] * wk_ref[...].astype(f32), axis=1, keepdims=True)
        + jnp.sum(v_ref[...] * wv_ref[...].astype(f32), axis=1, keepdims=True)
    ) / gain_in_ref[...]
    gain_ref[...] = jnp.broadcast_to(gain, (96, HEAD_DIM))
    row = lax.broadcasted_iota(jnp.int32, (96, HEAD_DIM), 0)
    picks = jnp.where((lane % 16 < 12) & (row == 12 * (lane // 16) + lane % 16), 1.0, 0.0)
    picks = picks.astype(bf16)

    def shared_tile(j):
        at = BLOCK + 384 + 16 * j
        rows = jnp.concatenate([got_ref[c, at : at + 16] for c in range(N_CTX)], axis=0)
        return dg(picks, rows, NN)

    for m in range(N_EXP // 2):
        at = HEAD_DIM * m
        low, high = halves(shared_tile(2 * m), shared_tile(2 * m + 1), lane)
        sg_ref[:, at : at + HEAD_DIM] = low
        su_ref[:, at : at + HEAD_DIM] = high
    for c in range(N_CTX):
        rows = got_ref[c, BLOCK + 384 + 16 * N_EXP :].astype(f32)
        for m in range(HEADS):
            sd_ref[8 * c : 8 * c + 8, HEAD_DIM * m : HEAD_DIM * (m + 1)] = rows[8 * m : 8 * m + 8]


def finish(got, gain_column, query_weight, key_weight, value_weight):
    shapes = [(96, 128), (96, 1536), (96, 512), (96, 512), (96, 1536), (96, 1024), (96, 1024)]
    return pl.pallas_call(
        finish_kernel,
        out_shape=[jax.ShapeDtypeStruct(s, f32) for s in shapes + [(SHARED, WIDTH)]],
        cost_estimate=cost(4),
        compiler_params=params(32),
        name="finish",
    )(got, gain_column, query_weight, key_weight, value_weight)


def input_kernel(dq_ref, got_ref, wq_ref, wkv_ref, x_ref, gain_ref, gm_ref, out_ref):
    lane = lax.broadcasted_iota(jnp.int32, (BLOCK, HEAD_DIM), 1)
    lows, highs = [], []
    for m in range(KV_HEADS):
        low, high = halves(got_ref[2 * m].astype(f32), got_ref[2 * m + 1].astype(f32), lane)
        lows.append(low.astype(bf16))
        highs.append(high.astype(bf16))
    grad_kv = jnp.concatenate(lows + highs, axis=1)
    grad_one = dg(dq_ref[...], wq_ref[...], NT) + dg(grad_kv, wkv_ref[...], NT)
    inputs = x_ref[...].astype(f32)
    inv = lax.rsqrt(jnp.mean(inputs * inputs, axis=-1, keepdims=True) + epsilon)
    out_ref[...] = (gm_ref[...] + norm_back(grad_one * gain_ref[...], inputs * inv, inv)).astype(bf16)


def input_back(grad_query, grad_kv, w_all, tokens, gain, grad_middle):
    return pl.pallas_call(
        input_kernel,
        grid=(1,),
        in_specs=[
            whole((BLOCK, WIDTH)),
            whole((N_CTX, BLOCK, HEAD_DIM)),
            w_cols(WIDTH, 0),
            w_cols(2 * KV_WIDTH, 3),
            whole((BLOCK, WIDTH)),
            whole((1, WIDTH)),
            whole((BLOCK, WIDTH)),
        ],
        out_specs=whole((BLOCK, WIDTH)),
        out_shape=jax.ShapeDtypeStruct((BLOCK, WIDTH), bf16),
        cost_estimate=cost(7),
        compiler_params=params(48),
        name="input_back",
    )(grad_query, grad_kv, w_all, w_all, tokens, gain, grad_middle)


def norm_rows_kernel(x_ref, gain_ref, out_ref):
    inputs = x_ref[0].astype(f32)
    inv = lax.rsqrt(jnp.mean(inputs * inputs, axis=-1, keepdims=True) + epsilon)
    out_ref[0] = (inputs * inv * gain_ref[...]).astype(bf16)


def norm_rows(rows, gain):
    count = rows.shape[0]
    spec = pl.BlockSpec((1, BLOCK, WIDTH), lambda i: (i, 0, 0))
    turned = pl.BlockSpec((1, BLOCK, WIDTH), lambda i: ((i % 2) * 4 + i // 2, 0, 0))
    return pl.pallas_call(
        norm_rows_kernel,
        grid=(count,),
        in_specs=[spec, whole((1, WIDTH))],
        out_specs=spec if count == 1 else turned,
        out_shape=jax.ShapeDtypeStruct(rows.shape, bf16),
        cost_estimate=cost(2),
        compiler_params=params(32),
        name="norm_rows",
    )(rows, gain)


def project_kernel(own_ref, seq_ref, w_ref, q_ref, kv_ref):
    step = pl.program_id(0)

    @pl.when(step < 3)
    def _():
        q_ref[...] = dg(own_ref[0], w_ref[...], NN).astype(bf16)

    @pl.when(step >= 3)
    def _():
        rows = seq_ref[...].reshape(N_CTX * BLOCK, WIDTH)
        kv_ref[...] = dg(rows, w_ref[...], NN).astype(bf16).reshape(N_CTX, BLOCK, KV_WIDTH)


def project(own, seq, w_all):
    return pl.pallas_call(
        project_kernel,
        grid=(5,),
        in_specs=[
            whole((1, BLOCK, WIDTH)),
            whole((N_CTX, BLOCK, WIDTH)),
            pl.BlockSpec((WIDTH, KV_WIDTH), lambda i: (0, jnp.where(i < 3, i, i + 3))),
        ],
        out_specs=[
            pl.BlockSpec((BLOCK, KV_WIDTH), lambda i: (0, jnp.minimum(i, 2))),
            pl.BlockSpec((N_CTX, BLOCK, KV_WIDTH), lambda i: (0, 0, jnp.maximum(i - 3, 0))),
        ],
        out_shape=[
            jax.ShapeDtypeStruct((BLOCK, WIDTH), bf16),
            jax.ShapeDtypeStruct((N_CTX, BLOCK, 2 * KV_WIDTH), bf16),
        ],
        cost_estimate=cost(8),
        compiler_params=params(48),
        name="project",
    )(own, seq, w_all)


PIECE = 2 * WIDTH + WIDTH * BLOCK // HEAD_DIM


def spread_kernel(at_ref, own_ref, low_ref, high_ref, *outs):
    chip = (at_ref[0] >> 1) ^ pl.program_id(0)
    got = jnp.where(chip < 4, low_ref[0], high_ref[0])
    total = (own_ref[0, 0].astype(f32) + got.astype(f32)).astype(bf16)
    for k in range(HALF):

        @pl.when(pl.program_id(0) == k)
        def _():
            outs[k // 2][k % 2] = total


def spread_sums(exp_at, parts, low, high):
    half = pl.BlockSpec((1, BLOCK, WIDTH), lambda k, at: (((at[0] >> 1) ^ k) & 3, 0, 0))
    return pl.pallas_call(
        spread_kernel,
        grid_spec=pltpu.PrefetchScalarGridSpec(
            num_scalar_prefetch=1,
            grid=(HALF,),
            in_specs=[
                pl.BlockSpec((1, 1, BLOCK, WIDTH), lambda k, at: (1, (at[0] >> 1) ^ k, 0, 0)),
                half,
                half,
            ],
            out_specs=[whole((2, BLOCK, WIDTH))] * 4,
        ),
        out_shape=[jax.ShapeDtypeStruct((2, BLOCK, WIDTH), bf16)] * 4,
        cost_estimate=cost(4),
        compiler_params=params(32),
        name="spread_sums",
    )(exp_at, parts, low, high)


def of_step(values, step):
    out = jnp.int32(values[0])
    for i, value in enumerate(values[1:], 1):
        out = jnp.where(step == i, value, out)
    return out


def expert_weights_kernel(halved, at_ref, x_ref, geo_ref, act_ref, dgate_ref, dup_ref, *outs):
    step = pl.program_id(0)
    rhs = jnp.concatenate([dgate_ref[0], dup_ref[0]], axis=1)
    both = dg(x_ref[0], rhs, TN).astype(bf16)
    down = dg(act_ref[0], geo_ref[0], TN).astype(bf16)
    for i in range(4):

        @pl.when(step == i)
        def _():
            start = (i % 2) * PIECE if halved else 0
            out = outs[i // 2 if halved else i].at[pl.ds(start, PIECE)]
            out[:WIDTH] = both[:, :HEAD_DIM]
            out[WIDTH : 2 * WIDTH] = both[:, HEAD_DIM:]
            for m in range(WIDTH // HEAD_DIM):
                at = 2 * WIDTH + m * BLOCK
                out[at : at + BLOCK] = down[:, m * HEAD_DIM : (m + 1) * HEAD_DIM]


def expert_weights(ctx_at, steps, halved, arrived, grad_eo, act, grad_gu):
    rows = 2 * ROWS

    def expert(s, at):
        return (at[0] >> 2) ^ of_step([side for _, side in steps], s)

    def lanes(shift):
        return pl.BlockSpec(
            (1, rows, HEAD_DIM),
            lambda s, at: (
                expert(s, at),
                0,
                shift + ((at[0] & 3) ^ of_step([r for r, _ in steps], s)),
            ),
        )

    rows_of = pl.BlockSpec((1, rows, WIDTH), lambda s, at: (expert(s, at), 0, 0))
    count, length = (2, 2 * PIECE) if halved else (4, PIECE)
    return pl.pallas_call(
        lambda *refs: expert_weights_kernel(halved, *refs),
        grid_spec=pltpu.PrefetchScalarGridSpec(
            num_scalar_prefetch=1,
            grid=(4,),
            in_specs=[rows_of, rows_of, lanes(0), lanes(0), lanes(4)],
            out_specs=[whole((length, HEAD_DIM))] * count,
        ),
        out_shape=[jax.ShapeDtypeStruct((length, HEAD_DIM), bf16)] * count,
        cost_estimate=cost(2),
        compiler_params=params(56),
        name="expert_weights",
    )(ctx_at, arrived, grad_eo, act, grad_gu, grad_gu)


def unpack_kernel(count, at_ref, *refs):
    pieces, (gate_ref, up_ref, down_ref) = refs[:count], refs[-3:]
    step = pl.program_id(0)
    for i in range(count):

        @pl.when(step == i)
        def _():
            piece = pieces[i]
            gate_ref[0] = piece[:WIDTH].astype(f32)
            up_ref[0] = piece[WIDTH : 2 * WIDTH].astype(f32)
            for m in range(WIDTH // HEAD_DIM):
                at = 2 * WIDTH + m * BLOCK
                down_ref[0, :, m * HEAD_DIM : (m + 1) * HEAD_DIM] = piece[at : at + BLOCK].astype(
                    f32
                )


def unpack_experts(ctx_at, steps, pieces, filled=()):
    count = len(steps)

    def expert(s, at):
        return (at[0] >> 2) ^ of_step([side for _, side in steps], s)

    def units(s, at):
        return (at[0] & 3) ^ of_step([r for r, _ in steps], s)

    cols = pl.BlockSpec((1, WIDTH, HEAD_DIM), lambda s, at: (expert(s, at), 0, units(s, at)))
    rows = pl.BlockSpec((1, BLOCK, WIDTH), lambda s, at: (expert(s, at), units(s, at), 0))
    anywhere = pl.BlockSpec(memory_space=pl.ANY)
    return pl.pallas_call(
        lambda *refs: unpack_kernel(count, *refs),
        grid_spec=pltpu.PrefetchScalarGridSpec(
            num_scalar_prefetch=1,
            grid=(count,),
            in_specs=[whole((PIECE, HEAD_DIM))] * count + [anywhere] * len(filled),
            out_specs=[cols, cols, rows],
        ),
        out_shape=[
            jax.ShapeDtypeStruct((LOCAL_E, WIDTH, FF_E), f32),
            jax.ShapeDtypeStruct((LOCAL_E, WIDTH, FF_E), f32),
            jax.ShapeDtypeStruct((LOCAL_E, FF_E, WIDTH), f32),
        ],
        input_output_aliases={1 + count + i: i for i in range(len(filled))},
        cost_estimate=cost(2 * count),
        compiler_params=params(48),
        name="unpack_experts",
    )(ctx_at, *pieces, *filled)


def relay_kernel(
    p0, p1, p3, p6, relay_a, relay_b, got_10, got_31, add_a, add_b, part_0, part_1
):
    add_a[...] = (p6[...].astype(f32) + relay_a[...].astype(f32)).astype(bf16)
    add_b[...] = (p3[...].astype(f32) + relay_b[...].astype(f32)).astype(bf16)
    part_0[...] = p0[...].astype(f32) + got_10[...].astype(f32)
    part_1[...] = p1[...].astype(f32) + got_31[...].astype(f32)


def side_kernel(part_0, part_1, got_11, got_30, own, side):
    own[...] = part_0[...] + got_30[...].astype(f32)
    side[...] = (part_1[...] + got_11[...].astype(f32)).astype(bf16)


def piece_sums(kernel, kinds, *pieces):
    specs, arrays = [], []
    for piece in pieces:
        array, second = piece if isinstance(piece, tuple) else (piece, 0)
        specs.append(pl.BlockSpec((PIECE // 4, HEAD_DIM), lambda i, at=4 * second: (i + at, 0)))
        arrays.append(array)
    return pl.pallas_call(
        kernel,
        grid=(4,),
        in_specs=specs,
        out_specs=[pl.BlockSpec((PIECE // 4, HEAD_DIM), lambda i: (i, 0))] * len(kinds),
        out_shape=[jax.ShapeDtypeStruct((PIECE, HEAD_DIM), kind) for kind in kinds],
        cost_estimate=cost(1),
        compiler_params=params(32),
        name="piece_sums",
    )(*arrays)


same_core = [[2 * i + c for i in range(8)] for c in range(2)]
core_swap = [(i, i ^ 1) for i in range(N_EXP)]
y_groups = [[0, 1, 2, 3], [4, 5, 6, 7]]
z_swap = [(i, i ^ 4) for i in range(N_CTX)]


def swap_all(rows, axis, groups=None):
    return lax.all_to_all(
        rows, axis, split_axis=0, concat_axis=0, tiled=True, axis_index_groups=groups
    )


def after(value, *others):
    return lax.optimization_barrier((value,) + others)[0]


def add_low(a, b):
    return (a.astype(f32) + b.astype(f32)).astype(bf16)


def on_device(
    tokens,
    routes,
    route_gates,
    norm_attn,
    norm_ffn,
    query_weight,
    key_weight,
    value_weight,
    out_weight,
    shared_gate,
    shared_up,
    shared_down,
    expert_gate,
    expert_up,
    expert_down,
    cotangent,
):
    exp_at = lax.axis_index("exp").astype(jnp.int32)
    ctx_at = lax.axis_index("ctx").astype(jnp.int32)
    exp_s, ctx_s = exp_at.reshape(1), ctx_at.reshape(1)

    z_at = ctx_at // 4

    w_cat = jnp.concatenate([query_weight, out_weight, key_weight, value_weight], axis=1)
    w_all = lax.all_gather(w_cat, "exp", axis=0, tiled=True)
    gates_high = route_gates[0].astype(bf16)
    gates_low = (route_gates[0] - gates_high.astype(f32)).astype(bf16)
    pad = jnp.zeros((BLOCK, META - 3 * TOPK), bf16)
    up_meta = jnp.concatenate(
        [cotangent[0], routes[0].astype(bf16), gates_high, gates_low, pad], axis=1
    )
    up_all = lax.all_gather(after(up_meta, w_cat), "exp", axis=0, tiled=True)
    gains = after(jnp.concatenate([norm_attn, norm_ffn]), w_cat)
    gains = swap_all(jnp.broadcast_to(gains, (N_EXP, gains.shape[0])), "exp")
    gain_attn = gains[:, :96].reshape(1, WIDTH).astype(f32)
    gain_ffn = gains[:, 96:].reshape(1, WIDTH).astype(f32)

    def of_sequence(rows):
        other = lax.ppermute(rows, "ctx", z_swap)
        pair = jnp.where(
            z_at == 0,
            jnp.concatenate([rows, other], axis=0),
            jnp.concatenate([other, rows], axis=0),
        )
        got = swap_all(jnp.broadcast_to(pair, (4, 2, BLOCK, WIDTH)), "ctx", y_groups)
        return got.reshape(N_CTX, BLOCK, WIDTH)

    tokens_seq = of_sequence(after(tokens, w_cat))
    shared_cols = jnp.concatenate(
        [shared_gate.reshape(96, N_EXP, SHARED), shared_up.reshape(96, N_EXP, SHARED)], axis=2
    ).transpose(1, 0, 2)
    w_shared = swap_all(shared_cols, "exp").reshape(WIDTH, 2 * SHARED)
    shared_two = jnp.concatenate([shared_down, shared_down], axis=0)

    hidden_one = norm_rows(tokens, gain_attn)
    hidden_seq = norm_rows(tokens_seq, gain_attn)
    hidden_seq = after(hidden_seq, w_shared)
    queries, kv_all = project(hidden_one, hidden_seq, w_all)
    attended, att_f, logs = attend(ctx_s, queries, kv_all)
    middle, hidden_two = middle_norm(attended, w_all, tokens[0], gain_ffn)

    hidden_all = lax.all_gather(hidden_two, "exp", axis=0, tiled=True)
    hidden_all = hidden_all.reshape(HALF, 2, BLOCK, WIDTH)
    att_seq = of_sequence(attended[None])
    place, grad_eo, grad_eh, grad_sh, slot_gate = place_rows(
        exp_s,
        after(up_all, hidden_two).reshape(HALF, 2, BLOCK, WIDTH + META),
        expert_down,
        shared_two,
    )
    part, arrived, act, grad_gu, shared_act, shared_grad = expert_back(
        exp_s, after(hidden_all, att_seq), place, grad_eh, grad_sh, expert_gate, expert_up, w_shared
    )
    summed = add_low(part[1], lax.ppermute(part[0], "exp", core_swap))
    grad_two = swap_all(summed, "exp", same_core)

    rows_e = 2 * ROWS
    operands = (
        after(arrived, summed).reshape(LOCAL_E, rows_e, WIDTH),
        grad_eo.reshape(LOCAL_E, rows_e, WIDTH),
        act.reshape(LOCAL_E, rows_e, FF_E),
        grad_gu.reshape(LOCAL_E, rows_e, 2 * FF_E),
    )
    for_1, for_3 = expert_weights(ctx_s, ((2, 0), (1, 0), (2, 1), (3, 1)), True, *operands)
    operands = (after(operands[0], for_1),) + operands[1:]
    p0, p6, p1, p3 = expert_weights(ctx_s, ((0, 0), (3, 0), (0, 1), (1, 1)), False, *operands)

    def to(rows, k):
        return lax.ppermute(rows, "ctx", [(i, i ^ k) for i in range(N_CTX)])

    from_1, from_3 = to(for_1, 1), to(for_3, 3)
    shared_grad_late = after(shared_grad, p0).reshape(N_EXP * BLOCK, META)
    grad_scols = dg(hidden_all.reshape(N_EXP * BLOCK, WIDTH), shared_grad_late, TN).astype(bf16)
    act_late = after(shared_act, p0).reshape(N_EXP * BLOCK, META)
    grad_sdown = dg(act_late, up_all, TN)[:SHARED, :WIDTH].astype(bf16)
    extra = jnp.concatenate(
        [
            jnp.pad(
                grad_scols.reshape(N_EXP, N_CTX, 12, META).transpose(1, 0, 2, 3),
                ((0, 0), (0, 0), (0, 4), (0, 0)),
            ).reshape(N_CTX, 16 * N_EXP, META),
            grad_sdown.reshape(N_CTX, 8, HEADS, 128).transpose(0, 2, 1, 3).reshape(N_CTX, 96, 128),
        ],
        axis=1,
    )

    out_part = expert_output(
        exp_s, after(act, p0), slot_gate, place, shared_act, expert_down, shared_two
    )
    grad_two = after(grad_two, extra, out_part)
    grad_middle, grad_attn, grad_heads, gain_rows = middle_back(
        grad_two, middle, cotangent[0], gain_ffn, w_all
    )
    grad_query, near, far = attend_back(
        ctx_s, queries, grad_heads, att_f, logs, kv_all, grad_attn, extra, gain_rows
    )
    far = lax.ppermute(far, "ctx", z_swap)
    from_1, from_3 = after((from_1, from_3), near)
    add_a, add_b, part_0, part_1 = piece_sums(
        relay_kernel,
        (bf16, bf16, f32, f32),
        p0,
        p1,
        p3,
        p6,
        (from_1, 0),
        (from_3, 0),
        (from_1, 1),
        (from_3, 1),
    )
    got_11, got_30 = to(add_b, 1), to(add_a, 3)

    def from_x(rows, k):
        return lax.ppermute(rows, "exp", [(i, i ^ (4 * k)) for i in range(N_EXP)])

    out_sums = spread_sums(
        exp_s,
        after(out_part, add_a),
        lax.ppermute(out_part[0, :4], "exp", core_swap),
        lax.ppermute(out_part[0, 4:], "exp", core_swap),
    )
    out_near = (
        out_sums[0].astype(f32)
        + from_x(out_sums[1], 1).astype(f32)
        + from_x(out_sums[3], 3).astype(f32)
    )
    got_11, got_30 = after((got_11, got_30), far)
    own_part, side = piece_sums(side_kernel, (f32, bf16), part_0, part_1, got_11, got_30)
    across = to(side, 4)
    out_2 = from_x(after(out_sums[2], side), 2)

    shares = merge_shares(ctx_s, near, after(far, side, out_near))
    got = swap_all(shares, "ctx", y_groups)
    own = (own_part + after(across, shares).astype(f32)).astype(bf16)
    at_1, at_3, at_z = to(own, 1), to(own, 3), to(own, 4)

    columns, grad_kv, grad_down = column_grads(got, after(hidden_seq, own), att_seq)
    out_rows = after(out_near, columns) + out_2.astype(f32)
    out_across = lax.ppermute(
        out_rows[1].astype(bf16), "exp", [(i, i ^ 2) for i in range(N_EXP)]
    )
    owned = swap_all(columns, "exp")
    owned, gain_sum = owned_sums(owned, grad_down)
    at_z, at_1, at_3 = lax.optimization_barrier((after(at_z, out_2), at_1, at_3))
    owned, at_z1, at_z3 = lax.optimization_barrier((owned, to(at_z, 1), to(at_z, 3)))
    at_2, at_z2 = to(at_3, 1), to(at_z1, 3)
    mixed = (middle + out_rows[0] + out_across.astype(f32)).astype(bf16)[None]
    experts = unpack_experts(
        ctx_s, ((0, 0), (1, 0), (3, 0), (0, 1)), (after(own, owned), at_1, at_3, at_z)
    )
    owned = jnp.broadcast_to(owned, (N_CTX, OWNED_ROWS, HEAD_DIM))
    owned = swap_all(jnp.concatenate([grad_kv, owned], axis=1), "ctx")
    gain_attn_sum, *dense = finish(
        after(owned, experts[0], mixed),
        norm_attn.astype(f32).reshape(96, 1),
        query_weight,
        key_weight,
        value_weight,
    )
    input_grad = input_back(grad_query, owned, w_all, tokens[0], gain_attn, grad_middle)
    at_2 = after(at_2, input_grad, *dense)
    experts = unpack_experts(
        ctx_s, ((2, 0), (1, 1), (3, 1), (2, 1)), (at_2, at_z1, at_z3, at_z2), experts
    )
    return (
        mixed,
        input_grad[None],
        gain_attn_sum[:, 0],
        gain_sum[12, :96],
        *dense,
        *experts,
    )


def solution(mesh):
    token_spec = P("exp", "ctx", None)
    rows = P("exp", None)
    expert = P("exp", None, None)
    placed = (token_spec,) * 3 + (P("exp"),) * 2 + (rows,) * 7 + (expert,) * 3 + (token_spec,)
    return jax.shard_map(
        on_device,
        mesh=mesh,
        in_specs=placed,
        out_specs=(token_spec,) * 2 + (P("exp"),) * 2 + (rows,) * 7 + (expert,) * 3,
        check_vma=False,
    )
```

```python
import jax
import jax.numpy as jnp
from jax import lax
from jax.sharding import PartitionSpec as P
from jax.experimental import pallas as pl
from jax.experimental.pallas import tpu as pltpu

HEADS = 12
KV_HEADS = 4
HEAD_DIM = 128
TOPK = 6
GROUP = 3
BLOCK = 128
WIDTH = 1536
KV_WIDTH = KV_HEADS * HEAD_DIM
CAP = 48
N_EXP = 16
N_CTX = 8
LOCAL_E = 2
FF_E = 512
SHARED = 64
META = 128
HALF = 8
ROWS = HALF * CAP

epsilon = 1e-05
masked_score = -1e30
f32 = jnp.float32
bf16 = jnp.bfloat16
log2_e = 1.4426950408889634
score_scale = HEAD_DIM ** (-0.5) * log2_e

NN = (((1,), (0,)), ((), ()))
NT = (((1,), (1,)), ((), ()))
TN = (((0,), (0,)), ((), ()))


def dg(a, b, dims):
    return lax.dot_general(a, b, dims, preferred_element_type=f32)


def params(mib):
    return pltpu.CompilerParams(vmem_limit_bytes=mib * 1024 * 1024)


def cost(us):
    return pl.CostEstimate(flops=0, bytes_accessed=int(us * 3690000), transcendentals=0)


def whole(shape):
    return pl.BlockSpec(shape, lambda *_: (0,) * len(shape), pipeline_mode=pl.Buffered(1))


def sigmoid(v):
    return 1.0 / (1.0 + jnp.exp(-v))


def allowed_scores(ctx_at):
    rows = lax.broadcasted_iota(jnp.int32, (GROUP * BLOCK, N_CTX * BLOCK), 0) % BLOCK
    cols = lax.broadcasted_iota(jnp.int32, (GROUP * BLOCK, N_CTX * BLOCK), 1)
    return rows + ctx_at * BLOCK >= cols


def stack_heads(block):
    return jnp.concatenate([block[:, j * HEAD_DIM : (j + 1) * HEAD_DIM] for j in range(GROUP)], axis=0)


def unstack_heads(rows):
    return jnp.concatenate([rows[j * BLOCK : (j + 1) * BLOCK] for j in range(GROUP)], axis=1)


def attend_kernel(ctx_ref, q_ref, k_ref, v_ref, att_ref, attf_ref, log_ref):
    q = stack_heads(q_ref[...])
    keys = k_ref[...].reshape(N_CTX * BLOCK, HEAD_DIM)
    values = v_ref[...].reshape(N_CTX * BLOCK, HEAD_DIM)
    scores = jnp.where(allowed_scores(ctx_ref[0]), dg(q, keys, NT) * score_scale, masked_score)
    top = jnp.max(scores, axis=-1, keepdims=True)
    weights = jnp.exp2(scores - top)
    total = jnp.sum(weights, axis=-1, keepdims=True)
    out = dg(weights.astype(bf16), values, NN) * (1.0 / total)
    out = unstack_heads(out)
    attf_ref[...] = out
    att_ref[...] = out.astype(bf16)
    log_ref[...] = jnp.broadcast_to(top + jnp.log2(total), (GROUP * BLOCK, HEAD_DIM))


def kv_specs():
    return [
        pl.BlockSpec((N_CTX, BLOCK, HEAD_DIM), lambda g: (0, 0, g)),
        pl.BlockSpec((N_CTX, BLOCK, HEAD_DIM), lambda g: (0, 0, KV_HEADS + g)),
    ]


def head_spec():
    return pl.BlockSpec((BLOCK, GROUP * HEAD_DIM), lambda g: (0, g))


def attend(ctx_at, qkv, kv_all):
    return pl.pallas_call(
        attend_kernel,
        grid=(KV_HEADS,),
        in_specs=[pl.BlockSpec(memory_space=pltpu.SMEM), head_spec()] + kv_specs(),
        out_specs=[
            head_spec(),
            head_spec(),
            pl.BlockSpec((GROUP * BLOCK, HEAD_DIM), lambda g: (g, 0)),
        ],
        out_shape=[
            jax.ShapeDtypeStruct((BLOCK, WIDTH), bf16),
            jax.ShapeDtypeStruct((BLOCK, WIDTH), f32),
            jax.ShapeDtypeStruct((HEADS * BLOCK, HEAD_DIM), f32),
        ],
        cost_estimate=cost(6),
        compiler_params=params(48),
        name="attend",
    )(ctx_at, qkv, kv_all, kv_all)


SEQ = N_CTX * BLOCK
AT_QUERY, AT_MIXED, AT_OUT = SEQ, SEQ + BLOCK, SEQ + 2 * BLOCK
AT_SHARED = SEQ + 3 * BLOCK
AT_DOWN = AT_SHARED + 16 * N_EXP
AT_GAIN = AT_DOWN + 96
SENT_ROWS = AT_GAIN + 16


def halves(a, b, lane):
    low = jnp.where(lane < 64, a, pltpu.roll(b, 64, 1))
    high = jnp.where(lane < 64, pltpu.roll(a, 64, 1), b)
    return low, high


def attend_back_kernel(
    ctx_ref,
    q_ref,
    ga_ref,
    attf_ref,
    log_ref,
    k_ref,
    v_ref,
    all_ga_ref,
    extra_ref,
    gain_ref,
    dq_ref,
    near_ref,
    far_ref,
    kept_ref,
):
    group = pl.program_id(0)
    z_at = ctx_ref[0] // 4

    def send(dest, z, start, stop, rows):
        @pl.when(z_at == z)
        def _():
            near_ref[dest, start:stop] = rows

        @pl.when(z_at != z)
        def _():
            far_ref[dest, start:stop] = rows

    q = stack_heads(q_ref[...])
    grad = stack_heads(ga_ref[...])
    delta = jnp.sum(grad.astype(f32) * stack_heads(attf_ref[...]), axis=-1, keepdims=True)
    keys = k_ref[...].reshape(SEQ, HEAD_DIM)
    values = v_ref[...].reshape(SEQ, HEAD_DIM)
    scores = jnp.where(allowed_scores(ctx_ref[0]), dg(q, keys, NT) * score_scale, masked_score)
    weights = jnp.exp2(scores - log_ref[:, :1])
    grad_weights = dg(grad, values, NT)
    grad_raw = (weights * (grad_weights - delta)).astype(bf16)
    scale = HEAD_DIM ** (-0.5)
    dq = unstack_heads(dg(grad_raw, keys, NN) * scale)
    dq_ref[...] = dq.astype(bf16)
    kept_ref[group] = dq
    grad_k = dg(grad_raw, q, TN) * scale
    grad_v = dg(weights.astype(bf16), grad, TN)
    low, high = halves(grad_k, grad_v, lax.broadcasted_iota(jnp.int32, (SEQ, HEAD_DIM), 1))
    low, high = low.astype(bf16), high.astype(bf16)
    send(2 * (group % 2), group // 2, 0, SEQ, low)
    send(2 * (group % 2) + 1, group // 2, 0, SEQ, high)

    @pl.when(group == KV_HEADS - 1)
    def _():
        lane = lax.broadcasted_iota(jnp.int32, (BLOCK, HEAD_DIM), 1)

        def dq_tile(m):
            return kept_ref[m // GROUP, :, HEAD_DIM * (m % GROUP) : HEAD_DIM * (m % GROUP + 1)]

        def ga_tile(m):
            return all_ga_ref[:, HEAD_DIM * m : HEAD_DIM * (m + 1)].astype(f32)

        mixed = []
        for m in range(KV_HEADS):
            mixed += halves(dq_tile(N_CTX + m), ga_tile(N_CTX + m), lane)
        gains = gain_ref[...].astype(bf16)
        for c in range(N_CTX):
            tiles = [dq_tile(c).astype(bf16), mixed[c].astype(bf16), ga_tile(c).astype(bf16)]
            rows = jnp.concatenate(tiles + [extra_ref[c], gains], axis=0)
            send(c % 4, c // 4, AT_QUERY, SENT_ROWS, rows)


def attend_back(ctx_at, qkv, grad_att, att_f, logs, kv_all, grad_attn, extra, gain_rows):
    return pl.pallas_call(
        attend_back_kernel,
        grid=(KV_HEADS,),
        in_specs=[
            pl.BlockSpec(memory_space=pltpu.SMEM),
            head_spec(),
            head_spec(),
            head_spec(),
            pl.BlockSpec((GROUP * BLOCK, HEAD_DIM), lambda g: (g, 0)),
        ]
        + kv_specs()
        + [
            whole((BLOCK, WIDTH)),
            whole((N_CTX, AT_GAIN - AT_SHARED, HEAD_DIM)),
            whole((16, HEAD_DIM)),
        ],
        out_specs=[head_spec()] + [whole((4, SENT_ROWS, HEAD_DIM))] * 2,
        out_shape=[
            jax.ShapeDtypeStruct((BLOCK, WIDTH), bf16),
            jax.ShapeDtypeStruct((4, SENT_ROWS, HEAD_DIM), bf16),
            jax.ShapeDtypeStruct((4, SENT_ROWS, HEAD_DIM), bf16),
        ],
        scratch_shapes=[pltpu.VMEM((KV_HEADS, BLOCK, GROUP * HEAD_DIM), f32)],
        cost_estimate=cost(2),
        compiler_params=params(60),
        name="attend_back",
    )(ctx_at, qkv, grad_att, att_f, logs, kv_all, kv_all, grad_attn, extra, gain_rows)


def middle_kernel(att_ref, w_ref, x_ref, gain_ref, middle_ref, hidden_ref):
    middle = x_ref[...].astype(f32) + dg(att_ref[...], w_ref[...], NN)
    inv = lax.rsqrt(jnp.mean(middle * middle, axis=-1, keepdims=True) + epsilon)
    middle_ref[...] = middle
    hidden_ref[...] = (middle * inv * gain_ref[...]).astype(bf16)


def w_cols(width, at):
    return pl.BlockSpec((WIDTH, width), lambda *_: (0, at), pipeline_mode=pl.Buffered(1))


def middle_norm(attended, w_all, tokens, gain):
    return pl.pallas_call(
        middle_kernel,
        grid=(1,),
        in_specs=[
            whole((BLOCK, WIDTH)),
            w_cols(WIDTH, 1),
            whole((BLOCK, WIDTH)),
            whole((1, WIDTH)),
        ],
        out_specs=[whole((BLOCK, WIDTH)), whole((BLOCK, WIDTH))],
        out_shape=[
            jax.ShapeDtypeStruct((BLOCK, WIDTH), f32),
            jax.ShapeDtypeStruct((BLOCK, WIDTH), bf16),
        ],
        cost_estimate=cost(2),
        compiler_params=params(60),
        name="middle_norm",
    )(attended, w_all, tokens, gain)


def norm_back(grad_normed, normed, inv_root):
    return inv_root * (
        grad_normed - normed * jnp.mean(grad_normed * normed, axis=-1, keepdims=True)
    )


def middle_back_kernel(
    pieces_ref, middle_ref, up_ref, gain_ref, w_ref, gm_ref, ga_ref, gh_ref, gg_ref
):
    grad_two = pieces_ref[0].astype(f32)
    for i in range(1, HALF):
        grad_two = grad_two + pieces_ref[i].astype(f32)
    middle = middle_ref[...]
    inv = lax.rsqrt(jnp.mean(middle * middle, axis=-1, keepdims=True) + epsilon)
    normed = middle * inv
    gains = jnp.sum(grad_two * normed, axis=0, keepdims=True)
    gg_ref[...] = jnp.zeros((16, HEAD_DIM), f32)
    for m in range(HEADS):
        gg_ref[m : m + 1] = gains[:, HEAD_DIM * m : HEAD_DIM * (m + 1)]
    grad_middle = up_ref[...].astype(f32) + norm_back(grad_two * gain_ref[...], normed, inv)
    gm_ref[...] = grad_middle
    grad_attn = grad_middle.astype(bf16)
    ga_ref[...] = grad_attn
    gh_ref[...] = dg(grad_attn, w_ref[...], NT).astype(bf16)


def middle_back(pieces, middle, upstream, gain, w_all):
    return pl.pallas_call(
        middle_back_kernel,
        grid=(1,),
        in_specs=[
            whole((HALF, BLOCK, WIDTH)),
            whole((BLOCK, WIDTH)),
            whole((BLOCK, WIDTH)),
            whole((1, WIDTH)),
            w_cols(WIDTH, 1),
        ],
        out_specs=[whole((BLOCK, WIDTH))] * 3 + [whole((16, HEAD_DIM))],
        out_shape=[
            jax.ShapeDtypeStruct((BLOCK, WIDTH), f32),
            jax.ShapeDtypeStruct((BLOCK, WIDTH), bf16),
            jax.ShapeDtypeStruct((BLOCK, WIDTH), bf16),
            jax.ShapeDtypeStruct((16, HEAD_DIM), f32),
        ],
        cost_estimate=cost(1),
        compiler_params=params(48),
        name="middle_back",
    )(pieces, middle, upstream, gain, w_all)


def place_kernel(
    at_ref, up_ref, down_ref, sdown_ref, place_ref, geo_ref, geh_ref, gsh_ref, gate_ref
):
    lane = lax.broadcasted_iota(jnp.int32, (BLOCK, META), 1)
    row = lax.broadcasted_iota(jnp.int32, (BLOCK, META), 0)
    before = (row > lane).astype(bf16)
    slot = (lane % 64).astype(f32)
    first_id = (at_ref[0] * LOCAL_E).astype(f32)
    row_id = first_id + (row >= 64).astype(f32)

    for chip in range(HALF):
        meta = up_ref[chip, 0, :, WIDTH:].astype(f32)
        named = lane < TOPK
        zero = jnp.zeros((BLOCK, META), f32)
        hit0 = jnp.where(named & (meta == first_id), 1.0, zero)
        hit1 = jnp.where(named & (meta == first_id + 1.0), 1.0, zero)
        mask = jnp.where(
            lane < 64,
            jnp.sum(hit0, axis=1, keepdims=True),
            jnp.sum(hit1, axis=1, keepdims=True),
        )
        rank = dg(before, mask.astype(bf16), NN)
        place = jnp.where((mask > 0.5) & (rank == slot), 1.0, zero).astype(bf16)
        place_ref[chip, 0] = place
        rows = dg(place, up_ref[chip, 0], TN)
        slot_meta = rows[:, WIDTH:]
        gates = pltpu.roll(slot_meta, META - TOPK, 1) + pltpu.roll(
            slot_meta, META - 2 * TOPK, 1
        )
        gate = jnp.sum(
            jnp.where(named & (slot_meta == row_id), gates, zero), axis=1, keepdims=True
        )
        geo = (gate * rows[:, :WIDTH]).astype(bf16)
        wide_gate = jnp.broadcast_to(gate, (BLOCK, META))
        at = chip * CAP
        for e in range(LOCAL_E):
            geo_ref[e, 0, at : at + CAP] = geo[64 * e : 64 * e + CAP]
            gate_ref[e, 0, at : at + CAP] = wide_gate[64 * e : 64 * e + CAP]
        gsh_ref[chip, 0] = dg(up_ref[chip, 0, :, :WIDTH], sdown_ref[...], NT)
    for e in range(LOCAL_E):
        geh_ref[e, 0] = dg(geo_ref[e, 0], down_ref[e], NT)


def by_core(cols):
    return pl.BlockSpec(
        (HALF, 1, BLOCK, cols),
        lambda s, at: (0, jnp.where(s == 0, 1 - at[0] % 2, at[0] % 2), 0, 0),
    )


def by_step(cols):
    return pl.BlockSpec((LOCAL_E, 1, ROWS, cols), lambda s, at: (0, s, 0, 0))


def place_rows(exp_at, up_all, expert_down, shared_two):
    return pl.pallas_call(
        place_kernel,
        grid_spec=pltpu.PrefetchScalarGridSpec(
            num_scalar_prefetch=1,
            grid=(2,),
            in_specs=[
                by_core(WIDTH + META),
                whole((LOCAL_E, FF_E, WIDTH)),
                whole((2 * SHARED, WIDTH)),
            ],
            out_specs=[by_core(META), by_step(WIDTH), by_step(FF_E), by_core(META), by_step(META)],
        ),
        out_shape=[
            jax.ShapeDtypeStruct((HALF, 2, BLOCK, META), bf16),
            jax.ShapeDtypeStruct((LOCAL_E, 2, ROWS, WIDTH), bf16),
            jax.ShapeDtypeStruct((LOCAL_E, 2, ROWS, FF_E), f32),
            jax.ShapeDtypeStruct((HALF, 2, BLOCK, META), f32),
            jax.ShapeDtypeStruct((LOCAL_E, 2, ROWS, META), f32),
        ],
        cost_estimate=cost(14),
        compiler_params=params(56),
        name="place_rows",
    )(exp_at, up_all, expert_down, shared_two)


def expert_kernel(
    at_ref,
    hid_ref,
    place_ref,
    geh_ref,
    gsh_ref,
    wg_ref,
    wu_ref,
    ws_ref,
    part_ref,
    x_ref,
    act_ref,
    dgu_ref,
    sact_ref,
    sgrad_ref,
):
    for chip in range(HALF):
        rows = dg(place_ref[chip, 0], hid_ref[chip, 0], TN).astype(bf16)
        at = chip * CAP
        for e in range(LOCAL_E):
            x_ref[e, 0, at : at + CAP] = rows[64 * e : 64 * e + CAP]
    pairs = []
    for e in range(LOCAL_E):
        pre_gate = dg(x_ref[e, 0], wg_ref[e], NN)
        pre_up = dg(x_ref[e, 0], wu_ref[e], NN)
        sig = sigmoid(pre_gate)
        act = pre_gate * sig
        act_ref[e, 0] = (act * pre_up).astype(bf16)
        geh = geh_ref[e, 0]
        d_gate = (geh * pre_up * (sig * (1.0 + pre_gate * (1.0 - sig)))).astype(bf16)
        d_up = (geh * act).astype(bf16)
        dgu_ref[e, 0, :, :FF_E] = d_gate
        dgu_ref[e, 0, :, FF_E:] = d_up
        pairs.append((dg(d_gate, wg_ref[e], NT) + dg(d_up, wu_ref[e], NT)).astype(bf16))
    lane = lax.broadcasted_iota(jnp.int32, (BLOCK, 2 * SHARED), 1) < SHARED
    gap = jnp.zeros((64 - CAP, WIDTH), bf16)
    for chip in range(HALF):
        pre = dg(hid_ref[chip, 0], ws_ref[...], NN)
        turned = pltpu.roll(pre, SHARED, 1)
        gate, up = jnp.where(lane, pre, turned), jnp.where(lane, turned, pre)
        sig = sigmoid(gate)
        act = gate * sig
        sact_ref[chip, 0] = jnp.where(lane, act * up, 0.0).astype(bf16)
        slope = sig * (1.0 + gate * (1.0 - sig))
        sgrad = (gsh_ref[chip, 0] * jnp.where(lane, up * slope, act)).astype(bf16)
        sgrad_ref[chip, 0] = sgrad
        at = chip * CAP
        stacked = jnp.concatenate([pairs[0][at : at + CAP], gap, pairs[1][at : at + CAP], gap], 0)
        part_ref[0, chip] = (
            dg(place_ref[chip, 0], stacked, NN) + dg(sgrad, ws_ref[...], NT)
        ).astype(bf16)


def expert_back(exp_at, hidden, place, geh, gsh, wg, wu, ws):
    return pl.pallas_call(
        expert_kernel,
        grid_spec=pltpu.PrefetchScalarGridSpec(
            num_scalar_prefetch=1,
            grid=(2,),
            in_specs=[
                by_core(WIDTH),
                by_core(META),
                by_step(FF_E),
                by_core(META),
                whole((LOCAL_E, WIDTH, FF_E)),
                whole((LOCAL_E, WIDTH, FF_E)),
                whole((WIDTH, 2 * SHARED)),
            ],
            out_specs=[
                pl.BlockSpec((1, HALF, BLOCK, WIDTH), lambda s, at: (s, 0, 0, 0)),
                by_step(WIDTH),
                by_step(FF_E),
                by_step(2 * FF_E),
                by_core(META),
                by_core(META),
            ],
        ),
        out_shape=[
            jax.ShapeDtypeStruct((2, HALF, BLOCK, WIDTH), bf16),
            jax.ShapeDtypeStruct((LOCAL_E, 2, ROWS, WIDTH), bf16),
            jax.ShapeDtypeStruct((LOCAL_E, 2, ROWS, FF_E), bf16),
            jax.ShapeDtypeStruct((LOCAL_E, 2, ROWS, 2 * FF_E), bf16),
            jax.ShapeDtypeStruct((HALF, 2, BLOCK, META), bf16),
            jax.ShapeDtypeStruct((HALF, 2, BLOCK, META), bf16),
        ],
        cost_estimate=cost(28),
        compiler_params=params(60),
        name="expert_back",
    )(exp_at, hidden, place, geh, gsh, wg, wu, ws)


def output_kernel(at_ref, act_ref, gate_ref, place_ref, sact_ref, wd_ref, sd_ref, part_ref):
    outs = []
    for e in range(LOCAL_E):
        out = dg(act_ref[e, 0], wd_ref[e], NN).astype(bf16).astype(f32)
        outs.append((out * gate_ref[e, 0, :, :1]).astype(bf16))
    gap = jnp.zeros((64 - CAP, WIDTH), bf16)
    for chip in range(HALF):
        at = chip * CAP
        stacked = jnp.concatenate([outs[0][at : at + CAP], gap, outs[1][at : at + CAP], gap], 0)
        part_ref[0, chip] = (
            dg(place_ref[chip, 0], stacked, NN) + dg(sact_ref[chip, 0], sd_ref[...], NN)
        ).astype(bf16)


def expert_output(exp_at, act, gate, place, sact, wd, sd):
    return pl.pallas_call(
        output_kernel,
        grid_spec=pltpu.PrefetchScalarGridSpec(
            num_scalar_prefetch=1,
            grid=(2,),
            in_specs=[
                by_step(FF_E),
                by_step(META),
                by_core(META),
                by_core(META),
                whole((LOCAL_E, FF_E, WIDTH)),
                whole((2 * SHARED, WIDTH)),
            ],
            out_specs=pl.BlockSpec((1, HALF, BLOCK, WIDTH), lambda s, at: (s, 0, 0, 0)),
        ),
        out_shape=jax.ShapeDtypeStruct((2, HALF, BLOCK, WIDTH), bf16),
        cost_estimate=cost(2),
        compiler_params=params(48),
        name="expert_output",
    )(exp_at, act, gate, place, sact, wd, sd)


SHARE = 3 * BLOCK
TO_SHARED = SEQ + 2 * SHARE
TO_DOWN = TO_SHARED + 16 * N_EXP
TO_GAIN = TO_DOWN + 96
MERGED_ROWS = TO_GAIN + 16


def merge_kernel(ctx_ref, near_ref, got_ref, out_ref):
    z_at = ctx_ref[0] // 4
    near, got = near_ref[0], got_ref[0]

    def add(a, b):
        return (a.astype(f32) + b.astype(f32)).astype(bf16)

    out_ref[0, :SEQ] = add(near[:SEQ], got[:SEQ])
    out_ref[0, TO_SHARED:] = add(near[AT_SHARED:], got[AT_SHARED:])
    mine, theirs = near[AT_QUERY:AT_SHARED], got[AT_QUERY:AT_SHARED]
    out_ref[0, SEQ : SEQ + SHARE] = jnp.where(z_at == 0, mine, theirs)
    out_ref[0, SEQ + SHARE : TO_SHARED] = jnp.where(z_at == 0, theirs, mine)


def merge_shares(ctx_at, near, got):
    spec = pl.BlockSpec((1, SENT_ROWS, HEAD_DIM), lambda i: (i, 0, 0))
    return pl.pallas_call(
        merge_kernel,
        grid=(4,),
        in_specs=[pl.BlockSpec(memory_space=pltpu.SMEM), spec, spec],
        out_specs=pl.BlockSpec((1, MERGED_ROWS, HEAD_DIM), lambda i: (i, 0, 0)),
        out_shape=jax.ShapeDtypeStruct((4, MERGED_ROWS, HEAD_DIM), bf16),
        cost_estimate=cost(3),
        compiler_params=params(32),
        name="merge_shares",
    )(ctx_at, near, got)


def columns_kernel(got_ref, hidden_ref, att_ref, sent_ref, kv_ref, down_ref):
    def summed(start, stop):
        out = got_ref[0, start:stop].astype(f32)
        for src in range(1, 4):
            out = out + got_ref[src, start:stop].astype(f32)
        return out

    grad_kv = summed(0, SEQ).astype(bf16)
    kv_ref[...] = grad_kv.reshape(N_CTX, BLOCK, HEAD_DIM)

    def rows_of(tile, order):
        at = SEQ + BLOCK * tile
        return jnp.concatenate(
            [got_ref[y, at + SHARE * z : at + SHARE * z + BLOCK] for z, y in order], axis=0
        )

    in_order = [(i // 4, i % 4) for i in range(N_CTX)]
    y_order = [(i % 2, i // 2) for i in range(N_CTX)]
    lane = lax.broadcasted_iota(jnp.int32, (SEQ, HEAD_DIM), 1)
    zero = jnp.zeros((SEQ, HEAD_DIM), bf16)
    mixed_q = jnp.where(lane < 64, rows_of(1, in_order), zero)
    mixed_o = jnp.where(lane < 64, zero, rows_of(1, y_order))
    left = jnp.concatenate([rows_of(0, in_order).T, mixed_q.T, grad_kv.T], axis=0)
    right = jnp.concatenate([mixed_o.T, rows_of(2, y_order).T], axis=0)
    by_hidden = dg(left, hidden_ref[...].reshape(SEQ, WIDTH), NN)
    by_att = dg(right, att_ref[...].reshape(SEQ, WIDTH), NN)
    tiles = [
        by_hidden[:BLOCK],
        by_hidden[BLOCK : 2 * BLOCK] + by_att[:BLOCK],
        by_att[BLOCK:],
        by_hidden[2 * BLOCK :],
    ]
    for t, tile in enumerate(tiles):
        sent_ref[:, :96, HEAD_DIM * t : HEAD_DIM * (t + 1)] = (
            tile.T.astype(bf16).reshape(N_EXP, 96, HEAD_DIM)
        )

    down_ref[...] = summed(TO_DOWN, TO_GAIN).astype(bf16)
    shared = summed(TO_SHARED, TO_DOWN)
    gains = summed(TO_GAIN, MERGED_ROWS)
    row = lax.broadcasted_iota(jnp.int32, (16, HEAD_DIM), 0)
    one_lane = lax.broadcasted_iota(jnp.int32, (1, HEAD_DIM), 1)
    for i in range(N_EXP):
        m, offset = (96 * i) // HEAD_DIM, (96 * i) % HEAD_DIM
        gain = gains[m : m + 1]
        if offset:
            shift = HEAD_DIM - offset
            gain = jnp.where(
                one_lane < shift,
                pltpu.roll(gain, shift, 1),
                pltpu.roll(gains[m + 1 : m + 2], shift, 1),
            )
        rows = jnp.where(row == 12, jnp.broadcast_to(gain, (16, HEAD_DIM)), shared[16 * i : 16 * i + 16])
        sent_ref[i, 96:, :HEAD_DIM] = rows.astype(bf16)
        sent_ref[i, 96:, HEAD_DIM:] = jnp.zeros((16, 512 - HEAD_DIM), bf16)


def column_grads(got, hidden_seq, att_seq):
    return pl.pallas_call(
        columns_kernel,
        out_shape=[
            jax.ShapeDtypeStruct((N_EXP, 112, 512), bf16),
            jax.ShapeDtypeStruct((N_CTX, BLOCK, HEAD_DIM), bf16),
            jax.ShapeDtypeStruct((96, HEAD_DIM), bf16),
        ],
        cost_estimate=cost(8),
        compiler_params=params(56),
        name="column_grads",
    )(got, hidden_seq, att_seq)


OWNED_ROWS = 4 * 96 + 16 * N_EXP + 96


def owned_kernel(got_ref, down_ref, owned_ref, gain_ref):
    total = got_ref[0, :96].astype(f32)
    gains = got_ref[0, 96:, :HEAD_DIM].astype(f32)
    for src in range(1, N_EXP):
        total = total + got_ref[src, :96].astype(f32)
        gains = gains + got_ref[src, 96:, :HEAD_DIM].astype(f32)
    gain_ref[...] = gains
    for t in range(4):
        owned_ref[96 * t : 96 * t + 96] = total[:, HEAD_DIM * t : HEAD_DIM * (t + 1)].astype(bf16)
    for src in range(N_EXP):
        at = 384 + 16 * src
        owned_ref[at : at + 16] = got_ref[src, 96:, :HEAD_DIM]
    owned_ref[384 + 16 * N_EXP :] = down_ref[...]


def owned_sums(got, down):
    return pl.pallas_call(
        owned_kernel,
        out_shape=[
            jax.ShapeDtypeStruct((OWNED_ROWS, HEAD_DIM), bf16),
            jax.ShapeDtypeStruct((16, HEAD_DIM), f32),
        ],
        cost_estimate=cost(3),
        compiler_params=params(32),
        name="owned_sums",
    )(got, down)


def finish_kernel(
    got_ref,
    gain_in_ref,
    wq_ref,
    wk_ref,
    wv_ref,
    gain_ref,
    q_ref,
    k_ref,
    v_ref,
    out_ref,
    sg_ref,
    su_ref,
    sd_ref,
):
    lane = lax.broadcasted_iota(jnp.int32, (96, HEAD_DIM), 1)

    def tile(c, t):
        at = BLOCK + 96 * t
        return got_ref[c, at : at + 96].astype(f32)

    for c in range(N_CTX):
        at = HEAD_DIM * c
        q_ref[:, at : at + HEAD_DIM] = tile(c, 0)
        out_ref[:, at : at + HEAD_DIM] = tile(c, 2)
    for m in range(N_CTX // 2):
        at = HEAD_DIM * m
        low, high = halves(tile(2 * m, 1), tile(2 * m + 1, 1), lane)
        q_ref[:, 1024 + at : 1024 + at + HEAD_DIM] = low
        out_ref[:, 1024 + at : 1024 + at + HEAD_DIM] = high
        low, high = halves(tile(2 * m, 3), tile(2 * m + 1, 3), lane)
        k_ref[:, at : at + HEAD_DIM] = low
        v_ref[:, at : at + HEAD_DIM] = high
    gain = (
        jnp.sum(q_ref[...] * wq_ref[...].astype(f32), axis=1, keepdims=True)
        + jnp.sum(k_ref[...] * wk_ref[...].astype(f32), axis=1, keepdims=True)
        + jnp.sum(v_ref[...] * wv_ref[...].astype(f32), axis=1, keepdims=True)
    ) / gain_in_ref[...]
    gain_ref[...] = jnp.broadcast_to(gain, (96, HEAD_DIM))
    row = lax.broadcasted_iota(jnp.int32, (96, HEAD_DIM), 0)
    picks = jnp.where((lane % 16 < 12) & (row == 12 * (lane // 16) + lane % 16), 1.0, 0.0)
    picks = picks.astype(bf16)

    def shared_tile(j):
        at = BLOCK + 384 + 16 * j
        rows = jnp.concatenate([got_ref[c, at : at + 16] for c in range(N_CTX)], axis=0)
        return dg(picks, rows, NN)

    for m in range(N_EXP // 2):
        at = HEAD_DIM * m
        low, high = halves(shared_tile(2 * m), shared_tile(2 * m + 1), lane)
        sg_ref[:, at : at + HEAD_DIM] = low
        su_ref[:, at : at + HEAD_DIM] = high
    for c in range(N_CTX):
        rows = got_ref[c, BLOCK + 384 + 16 * N_EXP :].astype(f32)
        for m in range(HEADS):
            sd_ref[8 * c : 8 * c + 8, HEAD_DIM * m : HEAD_DIM * (m + 1)] = rows[8 * m : 8 * m + 8]


def finish(got, gain_column, query_weight, key_weight, value_weight):
    shapes = [(96, 128), (96, 1536), (96, 512), (96, 512), (96, 1536), (96, 1024), (96, 1024)]
    return pl.pallas_call(
        finish_kernel,
        out_shape=[jax.ShapeDtypeStruct(s, f32) for s in shapes + [(SHARED, WIDTH)]],
        cost_estimate=cost(4),
        compiler_params=params(32),
        name="finish",
    )(got, gain_column, query_weight, key_weight, value_weight)


def input_kernel(part_ref, got_ref, wkv_ref, x_ref, gain_ref, gm_ref, out_ref):
    lane = lax.broadcasted_iota(jnp.int32, (BLOCK, HEAD_DIM), 1)
    lows, highs = [], []
    for m in range(KV_HEADS):
        low, high = halves(got_ref[2 * m].astype(f32), got_ref[2 * m + 1].astype(f32), lane)
        lows.append(low.astype(bf16))
        highs.append(high.astype(bf16))
    grad_kv = jnp.concatenate(lows + highs, axis=1)
    grad_one = part_ref[...] + dg(grad_kv, wkv_ref[...], NT)
    inputs = x_ref[...].astype(f32)
    inv = lax.rsqrt(jnp.mean(inputs * inputs, axis=-1, keepdims=True) + epsilon)
    out_ref[...] = (gm_ref[...] + norm_back(grad_one * gain_ref[...], inputs * inv, inv)).astype(bf16)


def query_kernel(dq_ref, wq_ref, out_ref):
    out_ref[...] = dg(dq_ref[...], wq_ref[...], NT)


def query_back(grad_query, w_all):
    return pl.pallas_call(
        query_kernel,
        grid=(1,),
        in_specs=[whole((BLOCK, WIDTH)), w_cols(WIDTH, 0)],
        out_specs=whole((BLOCK, WIDTH)),
        out_shape=jax.ShapeDtypeStruct((BLOCK, WIDTH), f32),
        cost_estimate=cost(4),
        compiler_params=params(32),
        name="query_back",
    )(grad_query, w_all)


def input_back(query_part, grad_kv, w_all, tokens, gain, grad_middle):
    return pl.pallas_call(
        input_kernel,
        grid=(1,),
        in_specs=[
            whole((BLOCK, WIDTH)),
            whole((N_CTX, BLOCK, HEAD_DIM)),
            w_cols(2 * KV_WIDTH, 3),
            whole((BLOCK, WIDTH)),
            whole((1, WIDTH)),
            whole((BLOCK, WIDTH)),
        ],
        out_specs=whole((BLOCK, WIDTH)),
        out_shape=jax.ShapeDtypeStruct((BLOCK, WIDTH), bf16),
        cost_estimate=cost(4),
        compiler_params=params(32),
        name="input_back",
    )(query_part, grad_kv, w_all, tokens, gain, grad_middle)


def norm_rows_kernel(x_ref, gain_ref, out_ref):
    inputs = x_ref[0].astype(f32)
    inv = lax.rsqrt(jnp.mean(inputs * inputs, axis=-1, keepdims=True) + epsilon)
    out_ref[0] = (inputs * inv * gain_ref[...]).astype(bf16)


def norm_rows(rows, gain):
    count = rows.shape[0]
    spec = pl.BlockSpec((1, BLOCK, WIDTH), lambda i: (i, 0, 0))
    turned = pl.BlockSpec((1, BLOCK, WIDTH), lambda i: ((i % 2) * 4 + i // 2, 0, 0))
    return pl.pallas_call(
        norm_rows_kernel,
        grid=(count,),
        in_specs=[spec, whole((1, WIDTH))],
        out_specs=spec if count == 1 else turned,
        out_shape=jax.ShapeDtypeStruct(rows.shape, bf16),
        cost_estimate=cost(2),
        compiler_params=params(32),
        name="norm_rows",
    )(rows, gain)


def project_kernel(own_ref, seq_ref, w_ref, q_ref, kv_ref):
    step = pl.program_id(0)

    @pl.when(step < 3)
    def _():
        q_ref[...] = dg(own_ref[0], w_ref[...], NN).astype(bf16)

    @pl.when(step >= 3)
    def _():
        rows = seq_ref[...].reshape(N_CTX * BLOCK, WIDTH)
        kv_ref[...] = dg(rows, w_ref[...], NN).astype(bf16).reshape(N_CTX, BLOCK, KV_WIDTH)


def project(own, seq, w_all):
    return pl.pallas_call(
        project_kernel,
        grid=(5,),
        in_specs=[
            whole((1, BLOCK, WIDTH)),
            whole((N_CTX, BLOCK, WIDTH)),
            pl.BlockSpec((WIDTH, KV_WIDTH), lambda i: (0, jnp.where(i < 3, i, i + 3))),
        ],
        out_specs=[
            pl.BlockSpec((BLOCK, KV_WIDTH), lambda i: (0, jnp.minimum(i, 2))),
            pl.BlockSpec((N_CTX, BLOCK, KV_WIDTH), lambda i: (0, 0, jnp.maximum(i - 3, 0))),
        ],
        out_shape=[
            jax.ShapeDtypeStruct((BLOCK, WIDTH), bf16),
            jax.ShapeDtypeStruct((N_CTX, BLOCK, 2 * KV_WIDTH), bf16),
        ],
        cost_estimate=cost(8),
        compiler_params=params(48),
        name="project",
    )(own, seq, w_all)


PIECE = 2 * WIDTH + WIDTH * BLOCK // HEAD_DIM


def spread_kernel(at_ref, own_ref, low_ref, high_ref, *outs):
    chip = (at_ref[0] >> 1) ^ pl.program_id(0)
    got = jnp.where(chip < 4, low_ref[0], high_ref[0])
    total = (own_ref[0, 0].astype(f32) + got.astype(f32)).astype(bf16)
    for k in range(HALF):

        @pl.when(pl.program_id(0) == k)
        def _():
            outs[k // 2][k % 2] = total


def spread_sums(exp_at, parts, low, high):
    half = pl.BlockSpec((1, BLOCK, WIDTH), lambda k, at: (((at[0] >> 1) ^ k) & 3, 0, 0))
    return pl.pallas_call(
        spread_kernel,
        grid_spec=pltpu.PrefetchScalarGridSpec(
            num_scalar_prefetch=1,
            grid=(HALF,),
            in_specs=[
                pl.BlockSpec((1, 1, BLOCK, WIDTH), lambda k, at: (1, (at[0] >> 1) ^ k, 0, 0)),
                half,
                half,
            ],
            out_specs=[whole((2, BLOCK, WIDTH))] * 4,
        ),
        out_shape=[jax.ShapeDtypeStruct((2, BLOCK, WIDTH), bf16)] * 4,
        cost_estimate=cost(4),
        compiler_params=params(32),
        name="spread_sums",
    )(exp_at, parts, low, high)


def of_step(values, step):
    out = jnp.int32(values[0])
    for i, value in enumerate(values[1:], 1):
        out = jnp.where(step == i, value, out)
    return out


def expert_weights_kernel(halved, at_ref, x_ref, geo_ref, act_ref, dgate_ref, dup_ref, *outs):
    step = pl.program_id(0)
    rhs = jnp.concatenate([dgate_ref[0], dup_ref[0]], axis=1)
    both = dg(x_ref[0], rhs, TN).astype(bf16)
    down = dg(act_ref[0], geo_ref[0], TN).astype(bf16)
    for i in range(4):

        @pl.when(step == i)
        def _():
            start = (i % 2) * PIECE if halved else 0
            out = outs[i // 2 if halved else i].at[pl.ds(start, PIECE)]
            out[:WIDTH] = both[:, :HEAD_DIM]
            out[WIDTH : 2 * WIDTH] = both[:, HEAD_DIM:]
            for m in range(WIDTH // HEAD_DIM):
                at = 2 * WIDTH + m * BLOCK
                out[at : at + BLOCK] = down[:, m * HEAD_DIM : (m + 1) * HEAD_DIM]


def expert_weights(ctx_at, steps, halved, arrived, grad_eo, act, grad_gu):
    rows = 2 * ROWS

    def expert(s, at):
        return (at[0] >> 2) ^ of_step([side for _, side in steps], s)

    def lanes(shift):
        return pl.BlockSpec(
            (1, rows, HEAD_DIM),
            lambda s, at: (
                expert(s, at),
                0,
                shift + ((at[0] & 3) ^ of_step([r for r, _ in steps], s)),
            ),
        )

    rows_of = pl.BlockSpec((1, rows, WIDTH), lambda s, at: (expert(s, at), 0, 0))
    count, length = (2, 2 * PIECE) if halved else (4, PIECE)
    return pl.pallas_call(
        lambda *refs: expert_weights_kernel(halved, *refs),
        grid_spec=pltpu.PrefetchScalarGridSpec(
            num_scalar_prefetch=1,
            grid=(4,),
            in_specs=[rows_of, rows_of, lanes(0), lanes(0), lanes(4)],
            out_specs=[whole((length, HEAD_DIM))] * count,
        ),
        out_shape=[jax.ShapeDtypeStruct((length, HEAD_DIM), bf16)] * count,
        cost_estimate=cost(2),
        compiler_params=params(56),
        name="expert_weights",
    )(ctx_at, arrived, grad_eo, act, grad_gu, grad_gu)


def unpack_kernel(count, at_ref, *refs):
    pieces, (gate_ref, up_ref, down_ref) = refs[:count], refs[-3:]
    step = pl.program_id(0)
    for i in range(count):

        @pl.when(step == i)
        def _():
            piece = pieces[i]
            gate_ref[0] = piece[:WIDTH].astype(f32)
            up_ref[0] = piece[WIDTH : 2 * WIDTH].astype(f32)
            for m in range(WIDTH // HEAD_DIM):
                at = 2 * WIDTH + m * BLOCK
                down_ref[0, :, m * HEAD_DIM : (m + 1) * HEAD_DIM] = piece[at : at + BLOCK].astype(
                    f32
                )


def unpack_experts(ctx_at, steps, pieces, filled=()):
    count = len(steps)

    def expert(s, at):
        return (at[0] >> 2) ^ of_step([side for _, side in steps], s)

    def units(s, at):
        return (at[0] & 3) ^ of_step([r for r, _ in steps], s)

    cols = pl.BlockSpec((1, WIDTH, HEAD_DIM), lambda s, at: (expert(s, at), 0, units(s, at)))
    rows = pl.BlockSpec((1, BLOCK, WIDTH), lambda s, at: (expert(s, at), units(s, at), 0))
    anywhere = pl.BlockSpec(memory_space=pl.ANY)
    return pl.pallas_call(
        lambda *refs: unpack_kernel(count, *refs),
        grid_spec=pltpu.PrefetchScalarGridSpec(
            num_scalar_prefetch=1,
            grid=(count,),
            in_specs=[whole((PIECE, HEAD_DIM))] * count + [anywhere] * len(filled),
            out_specs=[cols, cols, rows],
        ),
        out_shape=[
            jax.ShapeDtypeStruct((LOCAL_E, WIDTH, FF_E), f32),
            jax.ShapeDtypeStruct((LOCAL_E, WIDTH, FF_E), f32),
            jax.ShapeDtypeStruct((LOCAL_E, FF_E, WIDTH), f32),
        ],
        input_output_aliases={1 + count + i: i for i in range(len(filled))},
        cost_estimate=cost(2 * count),
        compiler_params=params(48),
        name="unpack_experts",
    )(ctx_at, *pieces, *filled)


def relay_kernel(
    p0, p1, p3, p6, relay_a, relay_b, got_10, got_31, add_a, add_b, part_0, part_1
):
    add_a[...] = (p6[...].astype(f32) + relay_a[...].astype(f32)).astype(bf16)
    add_b[...] = (p3[...].astype(f32) + relay_b[...].astype(f32)).astype(bf16)
    part_0[...] = p0[...].astype(f32) + got_10[...].astype(f32)
    part_1[...] = p1[...].astype(f32) + got_31[...].astype(f32)


def side_kernel(part_0, part_1, got_11, got_30, own, side):
    own[...] = part_0[...] + got_30[...].astype(f32)
    side[...] = (part_1[...] + got_11[...].astype(f32)).astype(bf16)


def piece_sums(kernel, kinds, *pieces):
    specs, arrays = [], []
    for piece in pieces:
        array, second = piece if isinstance(piece, tuple) else (piece, 0)
        specs.append(pl.BlockSpec((PIECE // 4, HEAD_DIM), lambda i, at=4 * second: (i + at, 0)))
        arrays.append(array)
    return pl.pallas_call(
        kernel,
        grid=(4,),
        in_specs=specs,
        out_specs=[pl.BlockSpec((PIECE // 4, HEAD_DIM), lambda i: (i, 0))] * len(kinds),
        out_shape=[jax.ShapeDtypeStruct((PIECE, HEAD_DIM), kind) for kind in kinds],
        cost_estimate=cost(1),
        compiler_params=params(32),
        name="piece_sums",
    )(*arrays)


same_core = [[2 * i + c for i in range(8)] for c in range(2)]
core_swap = [(i, i ^ 1) for i in range(N_EXP)]
y_groups = [[0, 1, 2, 3], [4, 5, 6, 7]]
z_swap = [(i, i ^ 4) for i in range(N_CTX)]


def swap_all(rows, axis, groups=None):
    return lax.all_to_all(
        rows, axis, split_axis=0, concat_axis=0, tiled=True, axis_index_groups=groups
    )


def after(value, *others):
    return lax.optimization_barrier((value,) + others)[0]


def add_low(a, b):
    return (a.astype(f32) + b.astype(f32)).astype(bf16)


def on_device(
    tokens,
    routes,
    route_gates,
    norm_attn,
    norm_ffn,
    query_weight,
    key_weight,
    value_weight,
    out_weight,
    shared_gate,
    shared_up,
    shared_down,
    expert_gate,
    expert_up,
    expert_down,
    cotangent,
):
    exp_at = lax.axis_index("exp").astype(jnp.int32)
    ctx_at = lax.axis_index("ctx").astype(jnp.int32)
    exp_s, ctx_s = exp_at.reshape(1), ctx_at.reshape(1)

    z_at = ctx_at // 4

    w_cat = jnp.concatenate([query_weight, out_weight, key_weight, value_weight], axis=1)
    w_all = lax.all_gather(w_cat, "exp", axis=0, tiled=True)
    gates_high = route_gates[0].astype(bf16)
    gates_low = (route_gates[0] - gates_high.astype(f32)).astype(bf16)
    pad = jnp.zeros((BLOCK, META - 3 * TOPK), bf16)
    up_meta = jnp.concatenate(
        [cotangent[0], routes[0].astype(bf16), gates_high, gates_low, pad], axis=1
    )
    up_all = lax.all_gather(after(up_meta, w_cat), "exp", axis=0, tiled=True)
    gains = after(jnp.concatenate([norm_attn, norm_ffn]), w_cat)
    gains = swap_all(jnp.broadcast_to(gains, (N_EXP, gains.shape[0])), "exp")
    gain_attn = gains[:, :96].reshape(1, WIDTH).astype(f32)
    gain_ffn = gains[:, 96:].reshape(1, WIDTH).astype(f32)

    def of_sequence(rows):
        other = lax.ppermute(rows, "ctx", z_swap)
        pair = jnp.where(
            z_at == 0,
            jnp.concatenate([rows, other], axis=0),
            jnp.concatenate([other, rows], axis=0),
        )
        got = swap_all(jnp.broadcast_to(pair, (4, 2, BLOCK, WIDTH)), "ctx", y_groups)
        return got.reshape(N_CTX, BLOCK, WIDTH)

    tokens_seq = of_sequence(after(tokens, w_cat))
    shared_cols = jnp.concatenate(
        [shared_gate.reshape(96, N_EXP, SHARED), shared_up.reshape(96, N_EXP, SHARED)], axis=2
    ).transpose(1, 0, 2)
    w_shared = swap_all(shared_cols, "exp").reshape(WIDTH, 2 * SHARED)
    shared_two = jnp.concatenate([shared_down, shared_down], axis=0)

    hidden_one = norm_rows(tokens, gain_attn)
    hidden_seq = norm_rows(tokens_seq, gain_attn)
    hidden_seq = after(hidden_seq, w_shared)
    queries, kv_all = project(hidden_one, hidden_seq, w_all)
    attended, att_f, logs = attend(ctx_s, queries, kv_all)
    middle, hidden_two = middle_norm(attended, w_all, tokens[0], gain_ffn)

    hidden_all = lax.all_gather(hidden_two, "exp", axis=0, tiled=True)
    hidden_all = hidden_all.reshape(HALF, 2, BLOCK, WIDTH)
    att_seq = of_sequence(attended[None])
    place, grad_eo, grad_eh, grad_sh, slot_gate = place_rows(
        exp_s,
        after(up_all, hidden_two).reshape(HALF, 2, BLOCK, WIDTH + META),
        expert_down,
        shared_two,
    )
    part, arrived, act, grad_gu, shared_act, shared_grad = expert_back(
        exp_s, after(hidden_all, att_seq), place, grad_eh, grad_sh, expert_gate, expert_up, w_shared
    )
    summed = add_low(part[1], lax.ppermute(part[0], "exp", core_swap))
    grad_two = swap_all(summed, "exp", same_core)

    rows_e = 2 * ROWS
    operands = (
        after(arrived, summed).reshape(LOCAL_E, rows_e, WIDTH),
        grad_eo.reshape(LOCAL_E, rows_e, WIDTH),
        act.reshape(LOCAL_E, rows_e, FF_E),
        grad_gu.reshape(LOCAL_E, rows_e, 2 * FF_E),
    )
    for_1, for_3 = expert_weights(ctx_s, ((2, 0), (1, 0), (2, 1), (3, 1)), True, *operands)
    operands = (after(operands[0], for_1),) + operands[1:]
    p0, p6, p1, p3 = expert_weights(ctx_s, ((0, 0), (3, 0), (0, 1), (1, 1)), False, *operands)

    def to(rows, k):
        return lax.ppermute(rows, "ctx", [(i, i ^ k) for i in range(N_CTX)])

    from_1, from_3 = to(for_1, 1), to(for_3, 3)
    shared_grad_late = after(shared_grad, p0).reshape(N_EXP * BLOCK, META)
    grad_scols = dg(hidden_all.reshape(N_EXP * BLOCK, WIDTH), shared_grad_late, TN).astype(bf16)
    act_late = after(shared_act, p0).reshape(N_EXP * BLOCK, META)
    grad_sdown = dg(act_late, up_all, TN)[:SHARED, :WIDTH].astype(bf16)
    extra = jnp.concatenate(
        [
            jnp.pad(
                grad_scols.reshape(N_EXP, N_CTX, 12, META).transpose(1, 0, 2, 3),
                ((0, 0), (0, 0), (0, 4), (0, 0)),
            ).reshape(N_CTX, 16 * N_EXP, META),
            grad_sdown.reshape(N_CTX, 8, HEADS, 128).transpose(0, 2, 1, 3).reshape(N_CTX, 96, 128),
        ],
        axis=1,
    )

    out_part = expert_output(
        exp_s, after(act, p0), slot_gate, place, shared_act, expert_down, shared_two
    )
    grad_two = after(grad_two, extra, out_part)
    grad_middle, grad_attn, grad_heads, gain_rows = middle_back(
        grad_two, middle, cotangent[0], gain_ffn, w_all
    )
    grad_query, near, far = attend_back(
        ctx_s, queries, grad_heads, att_f, logs, kv_all, grad_attn, extra, gain_rows
    )
    far = lax.ppermute(far, "ctx", z_swap)
    from_1, from_3 = after((from_1, from_3), near)
    add_a, add_b, part_0, part_1 = piece_sums(
        relay_kernel,
        (bf16, bf16, f32, f32),
        p0,
        p1,
        p3,
        p6,
        (from_1, 0),
        (from_3, 0),
        (from_1, 1),
        (from_3, 1),
    )
    got_11, got_30 = to(add_b, 1), to(add_a, 3)

    def from_x(rows, k):
        return lax.ppermute(rows, "exp", [(i, i ^ (4 * k)) for i in range(N_EXP)])

    out_sums = spread_sums(
        exp_s,
        after(out_part, add_a),
        lax.ppermute(out_part[0, :4], "exp", core_swap),
        lax.ppermute(out_part[0, 4:], "exp", core_swap),
    )
    out_near = (
        out_sums[0].astype(f32)
        + from_x(out_sums[1], 1).astype(f32)
        + from_x(out_sums[3], 3).astype(f32)
    )
    got_11, got_30 = after((got_11, got_30), far)
    own_part, side = piece_sums(side_kernel, (f32, bf16), part_0, part_1, got_11, got_30)
    across = to(side, 4)
    out_2 = from_x(after(out_sums[2], side), 2)

    shares = merge_shares(ctx_s, near, after(far, side, out_near))
    got = swap_all(shares, "ctx", y_groups)
    own = (own_part + after(across, shares).astype(f32)).astype(bf16)
    at_1, at_3, at_z = to(own, 1), to(own, 3), to(own, 4)

    columns, grad_kv, grad_down = column_grads(got, after(hidden_seq, own), att_seq)
    out_rows = after(out_near, columns) + out_2.astype(f32)
    out_across = lax.ppermute(
        out_rows[1].astype(bf16), "exp", [(i, i ^ 2) for i in range(N_EXP)]
    )
    owned = swap_all(columns, "exp")
    query_part = query_back(after(grad_query, columns), w_all)
    owned, gain_sum = owned_sums(owned, grad_down)
    at_z, at_1, at_3 = lax.optimization_barrier((after(at_z, out_2), at_1, at_3))
    owned, at_z1, at_z3 = lax.optimization_barrier((owned, to(at_z, 1), to(at_z, 3)))
    at_2, at_z2 = to(at_3, 1), to(at_z1, 3)
    mixed = (middle + out_rows[0] + out_across.astype(f32)).astype(bf16)[None]
    experts = unpack_experts(
        ctx_s,
        ((0, 0), (1, 0), (3, 0), (0, 1), (1, 1), (3, 1)),
        (after(own, owned), at_1, at_3, at_z, at_z1, at_z3),
    )
    owned = jnp.broadcast_to(owned, (N_CTX, OWNED_ROWS, HEAD_DIM))
    owned = swap_all(jnp.concatenate([grad_kv, owned], axis=1), "ctx")
    gain_attn_sum, *dense = finish(
        after(owned, experts[0], mixed, query_part),
        norm_attn.astype(f32).reshape(96, 1),
        query_weight,
        key_weight,
        value_weight,
    )
    input_grad = input_back(query_part, owned, w_all, tokens[0], gain_attn, grad_middle)
    at_2 = after(at_2, input_grad, *dense)
    experts = unpack_experts(
        ctx_s, ((2, 0), (2, 1)), (at_2, at_z2), experts
    )
    return (
        mixed,
        input_grad[None],
        gain_attn_sum[:, 0],
        gain_sum[12, :96],
        *dense,
        *experts,
    )


def solution(mesh):
    token_spec = P("exp", "ctx", None)
    rows = P("exp", None)
    expert = P("exp", None, None)
    placed = (token_spec,) * 3 + (P("exp"),) * 2 + (rows,) * 7 + (expert,) * 3 + (token_spec,)
    return jax.shard_map(
        on_device,
        mesh=mesh,
        in_specs=placed,
        out_specs=(token_spec,) * 2 + (P("exp"),) * 2 + (rows,) * 7 + (expert,) * 3,
        check_vma=False,
    )
```

```python
import jax
import jax.numpy as jnp
from jax import lax
from jax.sharding import PartitionSpec as P
from jax.experimental import pallas as pl
from jax.experimental.pallas import tpu as pltpu

HEADS = 12
KV_HEADS = 4
HEAD_DIM = 128
TOPK = 6
GROUP = 3
BLOCK = 128
WIDTH = 1536
KV_WIDTH = KV_HEADS * HEAD_DIM
CAP = 48
N_EXP = 16
N_CTX = 8
LOCAL_E = 2
FF_E = 512
SHARED = 64
META = 128
HALF = 8
ROWS = HALF * CAP

epsilon = 1e-05
masked_score = -1e30
f32 = jnp.float32
bf16 = jnp.bfloat16
log2_e = 1.4426950408889634
score_scale = HEAD_DIM ** (-0.5) * log2_e

NN = (((1,), (0,)), ((), ()))
NT = (((1,), (1,)), ((), ()))
TN = (((0,), (0,)), ((), ()))


def dg(a, b, dims):
    return lax.dot_general(a, b, dims, preferred_element_type=f32)


def params(mib):
    return pltpu.CompilerParams(vmem_limit_bytes=mib * 1024 * 1024)


def cost(us):
    return pl.CostEstimate(flops=0, bytes_accessed=int(us * 3690000), transcendentals=0)


def whole(shape):
    return pl.BlockSpec(shape, lambda *_: (0,) * len(shape), pipeline_mode=pl.Buffered(1))


def sigmoid(v):
    return 1.0 / (1.0 + jnp.exp(-v))


def allowed_scores(ctx_at):
    rows = lax.broadcasted_iota(jnp.int32, (GROUP * BLOCK, N_CTX * BLOCK), 0) % BLOCK
    cols = lax.broadcasted_iota(jnp.int32, (GROUP * BLOCK, N_CTX * BLOCK), 1)
    return rows + ctx_at * BLOCK >= cols


def stack_heads(block):
    return jnp.concatenate([block[:, j * HEAD_DIM : (j + 1) * HEAD_DIM] for j in range(GROUP)], axis=0)


def unstack_heads(rows):
    return jnp.concatenate([rows[j * BLOCK : (j + 1) * BLOCK] for j in range(GROUP)], axis=1)


def attend_kernel(ctx_ref, q_ref, k_ref, v_ref, att_ref, attf_ref, log_ref):
    q = stack_heads(q_ref[...])
    keys = k_ref[...].reshape(N_CTX * BLOCK, HEAD_DIM)
    values = v_ref[...].reshape(N_CTX * BLOCK, HEAD_DIM)
    scores = jnp.where(allowed_scores(ctx_ref[0]), dg(q, keys, NT) * score_scale, masked_score)
    top = jnp.max(scores, axis=-1, keepdims=True)
    weights = jnp.exp2(scores - top)
    total = jnp.sum(weights, axis=-1, keepdims=True)
    out = dg(weights.astype(bf16), values, NN) * (1.0 / total)
    out = unstack_heads(out)
    attf_ref[...] = out
    att_ref[...] = out.astype(bf16)
    log_ref[...] = jnp.broadcast_to(top + jnp.log2(total), (GROUP * BLOCK, HEAD_DIM))


def kv_specs():
    return [
        pl.BlockSpec((N_CTX, BLOCK, HEAD_DIM), lambda g: (0, 0, g)),
        pl.BlockSpec((N_CTX, BLOCK, HEAD_DIM), lambda g: (0, 0, KV_HEADS + g)),
    ]


def head_spec():
    return pl.BlockSpec((BLOCK, GROUP * HEAD_DIM), lambda g: (0, g))


def attend(ctx_at, qkv, kv_all):
    return pl.pallas_call(
        attend_kernel,
        grid=(KV_HEADS,),
        in_specs=[pl.BlockSpec(memory_space=pltpu.SMEM), head_spec()] + kv_specs(),
        out_specs=[
            head_spec(),
            head_spec(),
            pl.BlockSpec((GROUP * BLOCK, HEAD_DIM), lambda g: (g, 0)),
        ],
        out_shape=[
            jax.ShapeDtypeStruct((BLOCK, WIDTH), bf16),
            jax.ShapeDtypeStruct((BLOCK, WIDTH), f32),
            jax.ShapeDtypeStruct((HEADS * BLOCK, HEAD_DIM), f32),
        ],
        cost_estimate=cost(6),
        compiler_params=params(48),
        name="attend",
    )(ctx_at, qkv, kv_all, kv_all)


SEQ = N_CTX * BLOCK
AT_QUERY, AT_MIXED, AT_OUT = SEQ, SEQ + BLOCK, SEQ + 2 * BLOCK
AT_SHARED = SEQ + 3 * BLOCK
AT_DOWN = AT_SHARED + 16 * N_EXP
AT_GAIN = AT_DOWN + 96
SENT_ROWS = AT_GAIN + 16


def halves(a, b, lane):
    low = jnp.where(lane < 64, a, pltpu.roll(b, 64, 1))
    high = jnp.where(lane < 64, pltpu.roll(a, 64, 1), b)
    return low, high


def attend_back_kernel(
    ctx_ref,
    q_ref,
    ga_ref,
    attf_ref,
    log_ref,
    k_ref,
    v_ref,
    all_ga_ref,
    extra_ref,
    gain_ref,
    dq_ref,
    near_ref,
    far_ref,
    kept_ref,
):
    group = pl.program_id(0)
    z_at = ctx_ref[0] // 4

    def send(dest, z, start, stop, rows):
        @pl.when(z_at == z)
        def _():
            near_ref[dest, start:stop] = rows

        @pl.when(z_at != z)
        def _():
            far_ref[dest, start:stop] = rows

    q = stack_heads(q_ref[...])
    grad = stack_heads(ga_ref[...])
    delta = jnp.sum(grad.astype(f32) * stack_heads(attf_ref[...]), axis=-1, keepdims=True)
    keys = k_ref[...].reshape(SEQ, HEAD_DIM)
    values = v_ref[...].reshape(SEQ, HEAD_DIM)
    scores = jnp.where(allowed_scores(ctx_ref[0]), dg(q, keys, NT) * score_scale, masked_score)
    weights = jnp.exp2(scores - log_ref[:, :1])
    grad_weights = dg(grad, values, NT)
    grad_raw = (weights * (grad_weights - delta)).astype(bf16)
    scale = HEAD_DIM ** (-0.5)
    dq = unstack_heads(dg(grad_raw, keys, NN) * scale)
    dq_ref[...] = dq.astype(bf16)
    kept_ref[group] = dq
    grad_k = dg(grad_raw, q, TN) * scale
    grad_v = dg(weights.astype(bf16), grad, TN)
    low, high = halves(grad_k, grad_v, lax.broadcasted_iota(jnp.int32, (SEQ, HEAD_DIM), 1))
    low, high = low.astype(bf16), high.astype(bf16)
    send(2 * (group % 2), group // 2, 0, SEQ, low)
    send(2 * (group % 2) + 1, group // 2, 0, SEQ, high)

    @pl.when(group == KV_HEADS - 1)
    def _():
        lane = lax.broadcasted_iota(jnp.int32, (BLOCK, HEAD_DIM), 1)

        def dq_tile(m):
            return kept_ref[m // GROUP, :, HEAD_DIM * (m % GROUP) : HEAD_DIM * (m % GROUP + 1)]

        def ga_tile(m):
            return all_ga_ref[:, HEAD_DIM * m : HEAD_DIM * (m + 1)].astype(f32)

        mixed = []
        for m in range(KV_HEADS):
            mixed += halves(dq_tile(N_CTX + m), ga_tile(N_CTX + m), lane)
        gains = gain_ref[...].astype(bf16)
        for c in range(N_CTX):
            tiles = [dq_tile(c).astype(bf16), mixed[c].astype(bf16), ga_tile(c).astype(bf16)]
            rows = jnp.concatenate(tiles + [extra_ref[c], gains], axis=0)
            send(c % 4, c // 4, AT_QUERY, SENT_ROWS, rows)


def attend_back(ctx_at, qkv, grad_att, att_f, logs, kv_all, grad_attn, extra, gain_rows):
    return pl.pallas_call(
        attend_back_kernel,
        grid=(KV_HEADS,),
        in_specs=[
            pl.BlockSpec(memory_space=pltpu.SMEM),
            head_spec(),
            head_spec(),
            head_spec(),
            pl.BlockSpec((GROUP * BLOCK, HEAD_DIM), lambda g: (g, 0)),
        ]
        + kv_specs()
        + [
            whole((BLOCK, WIDTH)),
            whole((N_CTX, AT_GAIN - AT_SHARED, HEAD_DIM)),
            whole((16, HEAD_DIM)),
        ],
        out_specs=[head_spec()] + [whole((4, SENT_ROWS, HEAD_DIM))] * 2,
        out_shape=[
            jax.ShapeDtypeStruct((BLOCK, WIDTH), bf16),
            jax.ShapeDtypeStruct((4, SENT_ROWS, HEAD_DIM), bf16),
            jax.ShapeDtypeStruct((4, SENT_ROWS, HEAD_DIM), bf16),
        ],
        scratch_shapes=[pltpu.VMEM((KV_HEADS, BLOCK, GROUP * HEAD_DIM), f32)],
        cost_estimate=cost(2),
        compiler_params=params(60),
        name="attend_back",
    )(ctx_at, qkv, grad_att, att_f, logs, kv_all, kv_all, grad_attn, extra, gain_rows)


def middle_kernel(att_ref, w_ref, x_ref, gain_ref, middle_ref, hidden_ref):
    middle = x_ref[...].astype(f32) + dg(att_ref[...], w_ref[...], NN)
    inv = lax.rsqrt(jnp.mean(middle * middle, axis=-1, keepdims=True) + epsilon)
    middle_ref[...] = middle
    hidden_ref[...] = (middle * inv * gain_ref[...]).astype(bf16)


def w_cols(width, at):
    return pl.BlockSpec((WIDTH, width), lambda *_: (0, at), pipeline_mode=pl.Buffered(1))


def middle_norm(attended, w_all, tokens, gain):
    return pl.pallas_call(
        middle_kernel,
        grid=(1,),
        in_specs=[
            whole((BLOCK, WIDTH)),
            w_cols(WIDTH, 1),
            whole((BLOCK, WIDTH)),
            whole((1, WIDTH)),
        ],
        out_specs=[whole((BLOCK, WIDTH)), whole((BLOCK, WIDTH))],
        out_shape=[
            jax.ShapeDtypeStruct((BLOCK, WIDTH), f32),
            jax.ShapeDtypeStruct((BLOCK, WIDTH), bf16),
        ],
        cost_estimate=cost(2),
        compiler_params=params(60),
        name="middle_norm",
    )(attended, w_all, tokens, gain)


def norm_back(grad_normed, normed, inv_root):
    return inv_root * (
        grad_normed - normed * jnp.mean(grad_normed * normed, axis=-1, keepdims=True)
    )


def middle_back_kernel(
    pieces_ref, middle_ref, up_ref, gain_ref, w_ref, gm_ref, ga_ref, gh_ref, gg_ref
):
    grad_two = pieces_ref[0].astype(f32)
    for i in range(1, HALF):
        grad_two = grad_two + pieces_ref[i].astype(f32)
    middle = middle_ref[...]
    inv = lax.rsqrt(jnp.mean(middle * middle, axis=-1, keepdims=True) + epsilon)
    normed = middle * inv
    gains = jnp.sum(grad_two * normed, axis=0, keepdims=True)
    gg_ref[...] = jnp.zeros((16, HEAD_DIM), f32)
    for m in range(HEADS):
        gg_ref[m : m + 1] = gains[:, HEAD_DIM * m : HEAD_DIM * (m + 1)]
    grad_middle = up_ref[...].astype(f32) + norm_back(grad_two * gain_ref[...], normed, inv)
    gm_ref[...] = grad_middle
    grad_attn = grad_middle.astype(bf16)
    ga_ref[...] = grad_attn
    gh_ref[...] = dg(grad_attn, w_ref[...], NT).astype(bf16)


def middle_back(pieces, middle, upstream, gain, w_all):
    return pl.pallas_call(
        middle_back_kernel,
        grid=(1,),
        in_specs=[
            whole((HALF, BLOCK, WIDTH)),
            whole((BLOCK, WIDTH)),
            whole((BLOCK, WIDTH)),
            whole((1, WIDTH)),
            w_cols(WIDTH, 1),
        ],
        out_specs=[whole((BLOCK, WIDTH))] * 3 + [whole((16, HEAD_DIM))],
        out_shape=[
            jax.ShapeDtypeStruct((BLOCK, WIDTH), f32),
            jax.ShapeDtypeStruct((BLOCK, WIDTH), bf16),
            jax.ShapeDtypeStruct((BLOCK, WIDTH), bf16),
            jax.ShapeDtypeStruct((16, HEAD_DIM), f32),
        ],
        cost_estimate=cost(1),
        compiler_params=params(48),
        name="middle_back",
    )(pieces, middle, upstream, gain, w_all)


def place_kernel(
    at_ref, up_ref, down_ref, sdown_ref, place_ref, geo_ref, geh_ref, gsh_ref, gate_ref
):
    lane = lax.broadcasted_iota(jnp.int32, (BLOCK, META), 1)
    row = lax.broadcasted_iota(jnp.int32, (BLOCK, META), 0)
    before = (row > lane).astype(bf16)
    slot = (lane % 64).astype(f32)
    first_id = (at_ref[0] * LOCAL_E).astype(f32)
    row_id = first_id + (row >= 64).astype(f32)

    for chip in range(HALF):
        meta = up_ref[chip, 0, :, WIDTH:].astype(f32)
        named = lane < TOPK
        zero = jnp.zeros((BLOCK, META), f32)
        hit0 = jnp.where(named & (meta == first_id), 1.0, zero)
        hit1 = jnp.where(named & (meta == first_id + 1.0), 1.0, zero)
        mask = jnp.where(
            lane < 64,
            jnp.sum(hit0, axis=1, keepdims=True),
            jnp.sum(hit1, axis=1, keepdims=True),
        )
        rank = dg(before, mask.astype(bf16), NN)
        place = jnp.where((mask > 0.5) & (rank == slot), 1.0, zero).astype(bf16)
        place_ref[chip, 0] = place
        rows = dg(place, up_ref[chip, 0], TN)
        slot_meta = rows[:, WIDTH:]
        gates = pltpu.roll(slot_meta, META - TOPK, 1) + pltpu.roll(
            slot_meta, META - 2 * TOPK, 1
        )
        gate = jnp.sum(
            jnp.where(named & (slot_meta == row_id), gates, zero), axis=1, keepdims=True
        )
        geo = (gate * rows[:, :WIDTH]).astype(bf16)
        wide_gate = jnp.broadcast_to(gate, (BLOCK, META))
        at = chip * CAP
        for e in range(LOCAL_E):
            geo_ref[e, 0, at : at + CAP] = geo[64 * e : 64 * e + CAP]
            gate_ref[e, 0, at : at + CAP] = wide_gate[64 * e : 64 * e + CAP]
        gsh_ref[chip, 0] = dg(up_ref[chip, 0, :, :WIDTH], sdown_ref[...], NT)
    for e in range(LOCAL_E):
        geh_ref[e, 0] = dg(geo_ref[e, 0], down_ref[e], NT)


def by_core(cols):
    return pl.BlockSpec(
        (HALF, 1, BLOCK, cols),
        lambda s, at: (0, jnp.where(s == 0, 1 - at[0] % 2, at[0] % 2), 0, 0),
    )


def by_step(cols):
    return pl.BlockSpec((LOCAL_E, 1, ROWS, cols), lambda s, at: (0, s, 0, 0))


def place_rows(exp_at, up_all, expert_down, shared_two):
    return pl.pallas_call(
        place_kernel,
        grid_spec=pltpu.PrefetchScalarGridSpec(
            num_scalar_prefetch=1,
            grid=(2,),
            in_specs=[
                by_core(WIDTH + META),
                whole((LOCAL_E, FF_E, WIDTH)),
                whole((2 * SHARED, WIDTH)),
            ],
            out_specs=[by_core(META), by_step(WIDTH), by_step(FF_E), by_core(META), by_step(META)],
        ),
        out_shape=[
            jax.ShapeDtypeStruct((HALF, 2, BLOCK, META), bf16),
            jax.ShapeDtypeStruct((LOCAL_E, 2, ROWS, WIDTH), bf16),
            jax.ShapeDtypeStruct((LOCAL_E, 2, ROWS, FF_E), f32),
            jax.ShapeDtypeStruct((HALF, 2, BLOCK, META), f32),
            jax.ShapeDtypeStruct((LOCAL_E, 2, ROWS, META), f32),
        ],
        cost_estimate=cost(14),
        compiler_params=params(56),
        name="place_rows",
    )(exp_at, up_all, expert_down, shared_two)


def expert_kernel(
    at_ref,
    hid_ref,
    place_ref,
    geh_ref,
    gsh_ref,
    wg_ref,
    wu_ref,
    ws_ref,
    part_ref,
    x_ref,
    act_ref,
    dgu_ref,
    sact_ref,
    sgrad_ref,
):
    for chip in range(HALF):
        rows = dg(place_ref[chip, 0], hid_ref[chip, 0], TN).astype(bf16)
        at = chip * CAP
        for e in range(LOCAL_E):
            x_ref[e, 0, at : at + CAP] = rows[64 * e : 64 * e + CAP]
    pairs = []
    for e in range(LOCAL_E):
        pre_gate = dg(x_ref[e, 0], wg_ref[e], NN)
        pre_up = dg(x_ref[e, 0], wu_ref[e], NN)
        sig = sigmoid(pre_gate)
        act = pre_gate * sig
        act_ref[e, 0] = (act * pre_up).astype(bf16)
        geh = geh_ref[e, 0]
        d_gate = (geh * pre_up * (sig * (1.0 + pre_gate * (1.0 - sig)))).astype(bf16)
        d_up = (geh * act).astype(bf16)
        dgu_ref[e, 0, :, :FF_E] = d_gate
        dgu_ref[e, 0, :, FF_E:] = d_up
        pairs.append((dg(d_gate, wg_ref[e], NT) + dg(d_up, wu_ref[e], NT)).astype(bf16))
    lane = lax.broadcasted_iota(jnp.int32, (BLOCK, 2 * SHARED), 1) < SHARED
    gap = jnp.zeros((64 - CAP, WIDTH), bf16)
    for chip in range(HALF):
        pre = dg(hid_ref[chip, 0], ws_ref[...], NN)
        turned = pltpu.roll(pre, SHARED, 1)
        gate, up = jnp.where(lane, pre, turned), jnp.where(lane, turned, pre)
        sig = sigmoid(gate)
        act = gate * sig
        sact_ref[chip, 0] = jnp.where(lane, act * up, 0.0).astype(bf16)
        slope = sig * (1.0 + gate * (1.0 - sig))
        sgrad = (gsh_ref[chip, 0] * jnp.where(lane, up * slope, act)).astype(bf16)
        sgrad_ref[chip, 0] = sgrad
        at = chip * CAP
        stacked = jnp.concatenate([pairs[0][at : at + CAP], gap, pairs[1][at : at + CAP], gap], 0)
        part_ref[0, chip] = (
            dg(place_ref[chip, 0], stacked, NN) + dg(sgrad, ws_ref[...], NT)
        ).astype(bf16)


def expert_back(exp_at, hidden, place, geh, gsh, wg, wu, ws):
    return pl.pallas_call(
        expert_kernel,
        grid_spec=pltpu.PrefetchScalarGridSpec(
            num_scalar_prefetch=1,
            grid=(2,),
            in_specs=[
                by_core(WIDTH),
                by_core(META),
                by_step(FF_E),
                by_core(META),
                whole((LOCAL_E, WIDTH, FF_E)),
                whole((LOCAL_E, WIDTH, FF_E)),
                whole((WIDTH, 2 * SHARED)),
            ],
            out_specs=[
                pl.BlockSpec((1, HALF, BLOCK, WIDTH), lambda s, at: (s, 0, 0, 0)),
                by_step(WIDTH),
                by_step(FF_E),
                by_step(2 * FF_E),
                by_core(META),
                by_core(META),
            ],
        ),
        out_shape=[
            jax.ShapeDtypeStruct((2, HALF, BLOCK, WIDTH), bf16),
            jax.ShapeDtypeStruct((LOCAL_E, 2, ROWS, WIDTH), bf16),
            jax.ShapeDtypeStruct((LOCAL_E, 2, ROWS, FF_E), bf16),
            jax.ShapeDtypeStruct((LOCAL_E, 2, ROWS, 2 * FF_E), bf16),
            jax.ShapeDtypeStruct((HALF, 2, BLOCK, META), bf16),
            jax.ShapeDtypeStruct((HALF, 2, BLOCK, META), bf16),
        ],
        cost_estimate=cost(28),
        compiler_params=params(60),
        name="expert_back",
    )(exp_at, hidden, place, geh, gsh, wg, wu, ws)


def output_kernel(at_ref, act_ref, gate_ref, place_ref, sact_ref, wd_ref, sd_ref, part_ref):
    outs = []
    for e in range(LOCAL_E):
        out = dg(act_ref[e, 0], wd_ref[e], NN).astype(bf16).astype(f32)
        outs.append((out * gate_ref[e, 0, :, :1]).astype(bf16))
    gap = jnp.zeros((64 - CAP, WIDTH), bf16)
    for chip in range(HALF):
        at = chip * CAP
        stacked = jnp.concatenate([outs[0][at : at + CAP], gap, outs[1][at : at + CAP], gap], 0)
        part_ref[0, chip] = (
            dg(place_ref[chip, 0], stacked, NN) + dg(sact_ref[chip, 0], sd_ref[...], NN)
        ).astype(bf16)


def expert_output(exp_at, act, gate, place, sact, wd, sd):
    return pl.pallas_call(
        output_kernel,
        grid_spec=pltpu.PrefetchScalarGridSpec(
            num_scalar_prefetch=1,
            grid=(2,),
            in_specs=[
                by_step(FF_E),
                by_step(META),
                by_core(META),
                by_core(META),
                whole((LOCAL_E, FF_E, WIDTH)),
                whole((2 * SHARED, WIDTH)),
            ],
            out_specs=pl.BlockSpec((1, HALF, BLOCK, WIDTH), lambda s, at: (s, 0, 0, 0)),
        ),
        out_shape=jax.ShapeDtypeStruct((2, HALF, BLOCK, WIDTH), bf16),
        cost_estimate=cost(2),
        compiler_params=params(48),
        name="expert_output",
    )(exp_at, act, gate, place, sact, wd, sd)


SHARE = 3 * BLOCK
TO_SHARED = SEQ + 2 * SHARE
TO_DOWN = TO_SHARED + 16 * N_EXP
TO_GAIN = TO_DOWN + 96
MERGED_ROWS = TO_GAIN + 16


def merge_kernel(ctx_ref, near_ref, got_ref, out_ref):
    z_at = ctx_ref[0] // 4
    near, got = near_ref[0], got_ref[0]

    def add(a, b):
        return (a.astype(f32) + b.astype(f32)).astype(bf16)

    out_ref[0, :SEQ] = add(near[:SEQ], got[:SEQ])
    out_ref[0, TO_SHARED:] = add(near[AT_SHARED:], got[AT_SHARED:])
    mine, theirs = near[AT_QUERY:AT_SHARED], got[AT_QUERY:AT_SHARED]
    out_ref[0, SEQ : SEQ + SHARE] = jnp.where(z_at == 0, mine, theirs)
    out_ref[0, SEQ + SHARE : TO_SHARED] = jnp.where(z_at == 0, theirs, mine)


def merge_shares(ctx_at, near, got):
    spec = pl.BlockSpec((1, SENT_ROWS, HEAD_DIM), lambda i: (i, 0, 0))
    return pl.pallas_call(
        merge_kernel,
        grid=(4,),
        in_specs=[pl.BlockSpec(memory_space=pltpu.SMEM), spec, spec],
        out_specs=pl.BlockSpec((1, MERGED_ROWS, HEAD_DIM), lambda i: (i, 0, 0)),
        out_shape=jax.ShapeDtypeStruct((4, MERGED_ROWS, HEAD_DIM), bf16),
        cost_estimate=cost(3),
        compiler_params=params(32),
        name="merge_shares",
    )(ctx_at, near, got)


def columns_kernel(got_ref, hidden_ref, att_ref, sent_ref, kv_ref, down_ref):
    def summed(start, stop):
        out = got_ref[0, start:stop].astype(f32)
        for src in range(1, 4):
            out = out + got_ref[src, start:stop].astype(f32)
        return out

    grad_kv = summed(0, SEQ).astype(bf16)
    kv_ref[...] = grad_kv.reshape(N_CTX, BLOCK, HEAD_DIM)

    def rows_of(tile, order):
        at = SEQ + BLOCK * tile
        return jnp.concatenate(
            [got_ref[y, at + SHARE * z : at + SHARE * z + BLOCK] for z, y in order], axis=0
        )

    in_order = [(i // 4, i % 4) for i in range(N_CTX)]
    y_order = [(i % 2, i // 2) for i in range(N_CTX)]
    lane = lax.broadcasted_iota(jnp.int32, (SEQ, HEAD_DIM), 1)
    zero = jnp.zeros((SEQ, HEAD_DIM), bf16)
    mixed_q = jnp.where(lane < 64, rows_of(1, in_order), zero)
    mixed_o = jnp.where(lane < 64, zero, rows_of(1, y_order))
    left = jnp.concatenate([rows_of(0, in_order).T, mixed_q.T, grad_kv.T], axis=0)
    right = jnp.concatenate([mixed_o.T, rows_of(2, y_order).T], axis=0)
    by_hidden = dg(left, hidden_ref[...].reshape(SEQ, WIDTH), NN)
    by_att = dg(right, att_ref[...].reshape(SEQ, WIDTH), NN)
    tiles = [
        by_hidden[:BLOCK],
        by_hidden[BLOCK : 2 * BLOCK] + by_att[:BLOCK],
        by_att[BLOCK:],
        by_hidden[2 * BLOCK :],
    ]
    for t, tile in enumerate(tiles):
        sent_ref[:, :96, HEAD_DIM * t : HEAD_DIM * (t + 1)] = (
            tile.T.astype(bf16).reshape(N_EXP, 96, HEAD_DIM)
        )

    down_ref[...] = summed(TO_DOWN, TO_GAIN).astype(bf16)
    shared = summed(TO_SHARED, TO_DOWN)
    gains = summed(TO_GAIN, MERGED_ROWS)
    row = lax.broadcasted_iota(jnp.int32, (16, HEAD_DIM), 0)
    one_lane = lax.broadcasted_iota(jnp.int32, (1, HEAD_DIM), 1)
    for i in range(N_EXP):
        m, offset = (96 * i) // HEAD_DIM, (96 * i) % HEAD_DIM
        gain = gains[m : m + 1]
        if offset:
            shift = HEAD_DIM - offset
            gain = jnp.where(
                one_lane < shift,
                pltpu.roll(gain, shift, 1),
                pltpu.roll(gains[m + 1 : m + 2], shift, 1),
            )
        rows = jnp.where(row == 12, jnp.broadcast_to(gain, (16, HEAD_DIM)), shared[16 * i : 16 * i + 16])
        sent_ref[i, 96:, :HEAD_DIM] = rows.astype(bf16)
        sent_ref[i, 96:, HEAD_DIM:] = jnp.zeros((16, 512 - HEAD_DIM), bf16)


def column_grads(got, hidden_seq, att_seq):
    return pl.pallas_call(
        columns_kernel,
        out_shape=[
            jax.ShapeDtypeStruct((N_EXP, 112, 512), bf16),
            jax.ShapeDtypeStruct((N_CTX, BLOCK, HEAD_DIM), bf16),
            jax.ShapeDtypeStruct((96, HEAD_DIM), bf16),
        ],
        cost_estimate=cost(8),
        compiler_params=params(56),
        name="column_grads",
    )(got, hidden_seq, att_seq)


OWNED_ROWS = 4 * 96 + 16 * N_EXP + 96


def owned_kernel(got_ref, down_ref, owned_ref, gain_ref):
    total = got_ref[0, :96].astype(f32)
    gains = got_ref[0, 96:, :HEAD_DIM].astype(f32)
    for src in range(1, N_EXP):
        total = total + got_ref[src, :96].astype(f32)
        gains = gains + got_ref[src, 96:, :HEAD_DIM].astype(f32)
    gain_ref[...] = gains
    for t in range(4):
        owned_ref[96 * t : 96 * t + 96] = total[:, HEAD_DIM * t : HEAD_DIM * (t + 1)].astype(bf16)
    for src in range(N_EXP):
        at = 384 + 16 * src
        owned_ref[at : at + 16] = got_ref[src, 96:, :HEAD_DIM]
    owned_ref[384 + 16 * N_EXP :] = down_ref[...]


def owned_sums(got, down):
    return pl.pallas_call(
        owned_kernel,
        out_shape=[
            jax.ShapeDtypeStruct((OWNED_ROWS, HEAD_DIM), bf16),
            jax.ShapeDtypeStruct((16, HEAD_DIM), f32),
        ],
        cost_estimate=cost(3),
        compiler_params=params(32),
        name="owned_sums",
    )(got, down)


def finish_kernel(
    got_ref,
    gain_in_ref,
    wq_ref,
    wk_ref,
    wv_ref,
    gain_ref,
    q_ref,
    k_ref,
    v_ref,
    out_ref,
    sg_ref,
    su_ref,
    sd_ref,
):
    lane = lax.broadcasted_iota(jnp.int32, (96, HEAD_DIM), 1)

    def tile(c, t):
        at = BLOCK + 96 * t
        return got_ref[c, at : at + 96].astype(f32)

    for c in range(N_CTX):
        at = HEAD_DIM * c
        q_ref[:, at : at + HEAD_DIM] = tile(c, 0)
        out_ref[:, at : at + HEAD_DIM] = tile(c, 2)
    for m in range(N_CTX // 2):
        at = HEAD_DIM * m
        low, high = halves(tile(2 * m, 1), tile(2 * m + 1, 1), lane)
        q_ref[:, 1024 + at : 1024 + at + HEAD_DIM] = low
        out_ref[:, 1024 + at : 1024 + at + HEAD_DIM] = high
        low, high = halves(tile(2 * m, 3), tile(2 * m + 1, 3), lane)
        k_ref[:, at : at + HEAD_DIM] = low
        v_ref[:, at : at + HEAD_DIM] = high
    gain = (
        jnp.sum(q_ref[...] * wq_ref[...].astype(f32), axis=1, keepdims=True)
        + jnp.sum(k_ref[...] * wk_ref[...].astype(f32), axis=1, keepdims=True)
        + jnp.sum(v_ref[...] * wv_ref[...].astype(f32), axis=1, keepdims=True)
    ) / gain_in_ref[...]
    gain_ref[...] = jnp.broadcast_to(gain, (96, HEAD_DIM))
    row = lax.broadcasted_iota(jnp.int32, (96, HEAD_DIM), 0)
    picks = jnp.where((lane % 16 < 12) & (row == 12 * (lane // 16) + lane % 16), 1.0, 0.0)
    picks = picks.astype(bf16)

    def shared_tile(j):
        at = BLOCK + 384 + 16 * j
        rows = jnp.concatenate([got_ref[c, at : at + 16] for c in range(N_CTX)], axis=0)
        return dg(picks, rows, NN)

    for m in range(N_EXP // 2):
        at = HEAD_DIM * m
        low, high = halves(shared_tile(2 * m), shared_tile(2 * m + 1), lane)
        sg_ref[:, at : at + HEAD_DIM] = low
        su_ref[:, at : at + HEAD_DIM] = high
    for c in range(N_CTX):
        rows = got_ref[c, BLOCK + 384 + 16 * N_EXP :].astype(f32)
        for m in range(HEADS):
            sd_ref[8 * c : 8 * c + 8, HEAD_DIM * m : HEAD_DIM * (m + 1)] = rows[8 * m : 8 * m + 8]


def finish(got, gain_column, query_weight, key_weight, value_weight):
    shapes = [(96, 128), (96, 1536), (96, 512), (96, 512), (96, 1536), (96, 1024), (96, 1024)]
    return pl.pallas_call(
        finish_kernel,
        out_shape=[jax.ShapeDtypeStruct(s, f32) for s in shapes + [(SHARED, WIDTH)]],
        cost_estimate=cost(4),
        compiler_params=params(32),
        name="finish",
    )(got, gain_column, query_weight, key_weight, value_weight)


def input_kernel(part_ref, got_ref, wkv_ref, x_ref, gain_ref, gm_ref, out_ref):
    lane = lax.broadcasted_iota(jnp.int32, (BLOCK, HEAD_DIM), 1)
    lows, highs = [], []
    for m in range(KV_HEADS):
        low, high = halves(got_ref[2 * m].astype(f32), got_ref[2 * m + 1].astype(f32), lane)
        lows.append(low.astype(bf16))
        highs.append(high.astype(bf16))
    grad_kv = jnp.concatenate(lows + highs, axis=1)
    grad_one = part_ref[...] + dg(grad_kv, wkv_ref[...], NT)
    inputs = x_ref[...].astype(f32)
    inv = lax.rsqrt(jnp.mean(inputs * inputs, axis=-1, keepdims=True) + epsilon)
    out_ref[...] = (gm_ref[...] + norm_back(grad_one * gain_ref[...], inputs * inv, inv)).astype(bf16)


def query_kernel(dq_ref, wq_ref, out_ref):
    out_ref[...] = dg(dq_ref[...], wq_ref[...], NT)


def query_back(grad_query, w_all):
    return pl.pallas_call(
        query_kernel,
        grid=(1,),
        in_specs=[whole((BLOCK, WIDTH)), w_cols(WIDTH, 0)],
        out_specs=whole((BLOCK, WIDTH)),
        out_shape=jax.ShapeDtypeStruct((BLOCK, WIDTH), f32),
        cost_estimate=cost(4),
        compiler_params=params(60),
        name="query_back",
    )(grad_query, w_all)


def input_back(query_part, grad_kv, w_all, tokens, gain, grad_middle):
    return pl.pallas_call(
        input_kernel,
        grid=(1,),
        in_specs=[
            whole((BLOCK, WIDTH)),
            whole((N_CTX, BLOCK, HEAD_DIM)),
            w_cols(2 * KV_WIDTH, 3),
            whole((BLOCK, WIDTH)),
            whole((1, WIDTH)),
            whole((BLOCK, WIDTH)),
        ],
        out_specs=whole((BLOCK, WIDTH)),
        out_shape=jax.ShapeDtypeStruct((BLOCK, WIDTH), bf16),
        cost_estimate=cost(4),
        compiler_params=params(60),
        name="input_back",
    )(query_part, grad_kv, w_all, tokens, gain, grad_middle)


def norm_rows_kernel(x_ref, gain_ref, out_ref):
    inputs = x_ref[0].astype(f32)
    inv = lax.rsqrt(jnp.mean(inputs * inputs, axis=-1, keepdims=True) + epsilon)
    out_ref[0] = (inputs * inv * gain_ref[...]).astype(bf16)


def norm_rows(rows, gain):
    count = rows.shape[0]
    spec = pl.BlockSpec((1, BLOCK, WIDTH), lambda i: (i, 0, 0))
    turned = pl.BlockSpec((1, BLOCK, WIDTH), lambda i: ((i % 2) * 4 + i // 2, 0, 0))
    return pl.pallas_call(
        norm_rows_kernel,
        grid=(count,),
        in_specs=[spec, whole((1, WIDTH))],
        out_specs=spec if count == 1 else turned,
        out_shape=jax.ShapeDtypeStruct(rows.shape, bf16),
        cost_estimate=cost(2),
        compiler_params=params(32),
        name="norm_rows",
    )(rows, gain)


def project_kernel(own_ref, seq_ref, w_ref, q_ref, kv_ref):
    step = pl.program_id(0)

    @pl.when(step < 3)
    def _():
        q_ref[...] = dg(own_ref[0], w_ref[...], NN).astype(bf16)

    @pl.when(step >= 3)
    def _():
        rows = seq_ref[...].reshape(N_CTX * BLOCK, WIDTH)
        kv_ref[...] = dg(rows, w_ref[...], NN).astype(bf16).reshape(N_CTX, BLOCK, KV_WIDTH)


def project(own, seq, w_all):
    return pl.pallas_call(
        project_kernel,
        grid=(5,),
        in_specs=[
            whole((1, BLOCK, WIDTH)),
            whole((N_CTX, BLOCK, WIDTH)),
            pl.BlockSpec((WIDTH, KV_WIDTH), lambda i: (0, jnp.where(i < 3, i, i + 3))),
        ],
        out_specs=[
            pl.BlockSpec((BLOCK, KV_WIDTH), lambda i: (0, jnp.minimum(i, 2))),
            pl.BlockSpec((N_CTX, BLOCK, KV_WIDTH), lambda i: (0, 0, jnp.maximum(i - 3, 0))),
        ],
        out_shape=[
            jax.ShapeDtypeStruct((BLOCK, WIDTH), bf16),
            jax.ShapeDtypeStruct((N_CTX, BLOCK, 2 * KV_WIDTH), bf16),
        ],
        cost_estimate=cost(8),
        compiler_params=params(48),
        name="project",
    )(own, seq, w_all)


PIECE = 2 * WIDTH + WIDTH * BLOCK // HEAD_DIM


def spread_kernel(at_ref, own_ref, low_ref, high_ref, *outs):
    chip = (at_ref[0] >> 1) ^ pl.program_id(0)
    got = jnp.where(chip < 4, low_ref[0], high_ref[0])
    total = (own_ref[0, 0].astype(f32) + got.astype(f32)).astype(bf16)
    for k in range(HALF):

        @pl.when(pl.program_id(0) == k)
        def _():
            outs[k // 2][k % 2] = total


def spread_sums(exp_at, parts, low, high):
    half = pl.BlockSpec((1, BLOCK, WIDTH), lambda k, at: (((at[0] >> 1) ^ k) & 3, 0, 0))
    return pl.pallas_call(
        spread_kernel,
        grid_spec=pltpu.PrefetchScalarGridSpec(
            num_scalar_prefetch=1,
            grid=(HALF,),
            in_specs=[
                pl.BlockSpec((1, 1, BLOCK, WIDTH), lambda k, at: (1, (at[0] >> 1) ^ k, 0, 0)),
                half,
                half,
            ],
            out_specs=[whole((2, BLOCK, WIDTH))] * 4,
        ),
        out_shape=[jax.ShapeDtypeStruct((2, BLOCK, WIDTH), bf16)] * 4,
        cost_estimate=cost(4),
        compiler_params=params(32),
        name="spread_sums",
    )(exp_at, parts, low, high)


def of_step(values, step):
    out = jnp.int32(values[0])
    for i, value in enumerate(values[1:], 1):
        out = jnp.where(step == i, value, out)
    return out


def expert_weights_kernel(halved, at_ref, x_ref, geo_ref, act_ref, dgate_ref, dup_ref, *outs):
    step = pl.program_id(0)
    rhs = jnp.concatenate([dgate_ref[0], dup_ref[0]], axis=1)
    both = dg(x_ref[0], rhs, TN).astype(bf16)
    down = dg(act_ref[0], geo_ref[0], TN).astype(bf16)
    for i in range(4):

        @pl.when(step == i)
        def _():
            start = (i % 2) * PIECE if halved else 0
            out = outs[i // 2 if halved else i].at[pl.ds(start, PIECE)]
            out[:WIDTH] = both[:, :HEAD_DIM]
            out[WIDTH : 2 * WIDTH] = both[:, HEAD_DIM:]
            for m in range(WIDTH // HEAD_DIM):
                at = 2 * WIDTH + m * BLOCK
                out[at : at + BLOCK] = down[:, m * HEAD_DIM : (m + 1) * HEAD_DIM]


def expert_weights(ctx_at, steps, halved, arrived, grad_eo, act, grad_gu):
    rows = 2 * ROWS

    def expert(s, at):
        return (at[0] >> 2) ^ of_step([side for _, side in steps], s)

    def lanes(shift):
        return pl.BlockSpec(
            (1, rows, HEAD_DIM),
            lambda s, at: (
                expert(s, at),
                0,
                shift + ((at[0] & 3) ^ of_step([r for r, _ in steps], s)),
            ),
        )

    rows_of = pl.BlockSpec((1, rows, WIDTH), lambda s, at: (expert(s, at), 0, 0))
    count, length = (2, 2 * PIECE) if halved else (4, PIECE)
    return pl.pallas_call(
        lambda *refs: expert_weights_kernel(halved, *refs),
        grid_spec=pltpu.PrefetchScalarGridSpec(
            num_scalar_prefetch=1,
            grid=(4,),
            in_specs=[rows_of, rows_of, lanes(0), lanes(0), lanes(4)],
            out_specs=[whole((length, HEAD_DIM))] * count,
        ),
        out_shape=[jax.ShapeDtypeStruct((length, HEAD_DIM), bf16)] * count,
        cost_estimate=cost(2),
        compiler_params=params(56),
        name="expert_weights",
    )(ctx_at, arrived, grad_eo, act, grad_gu, grad_gu)


def unpack_kernel(count, at_ref, *refs):
    pieces, (gate_ref, up_ref, down_ref) = refs[:count], refs[-3:]
    step = pl.program_id(0)
    for i in range(count):

        @pl.when(step == i)
        def _():
            piece = pieces[i]
            gate_ref[0] = piece[:WIDTH].astype(f32)
            up_ref[0] = piece[WIDTH : 2 * WIDTH].astype(f32)
            for m in range(WIDTH // HEAD_DIM):
                at = 2 * WIDTH + m * BLOCK
                down_ref[0, :, m * HEAD_DIM : (m + 1) * HEAD_DIM] = piece[at : at + BLOCK].astype(
                    f32
                )


def unpack_experts(ctx_at, steps, pieces, filled=()):
    count = len(steps)

    def expert(s, at):
        return (at[0] >> 2) ^ of_step([side for _, side in steps], s)

    def units(s, at):
        return (at[0] & 3) ^ of_step([r for r, _ in steps], s)

    cols = pl.BlockSpec((1, WIDTH, HEAD_DIM), lambda s, at: (expert(s, at), 0, units(s, at)))
    rows = pl.BlockSpec((1, BLOCK, WIDTH), lambda s, at: (expert(s, at), units(s, at), 0))
    anywhere = pl.BlockSpec(memory_space=pl.ANY)
    return pl.pallas_call(
        lambda *refs: unpack_kernel(count, *refs),
        grid_spec=pltpu.PrefetchScalarGridSpec(
            num_scalar_prefetch=1,
            grid=(count,),
            in_specs=[whole((PIECE, HEAD_DIM))] * count + [anywhere] * len(filled),
            out_specs=[cols, cols, rows],
        ),
        out_shape=[
            jax.ShapeDtypeStruct((LOCAL_E, WIDTH, FF_E), f32),
            jax.ShapeDtypeStruct((LOCAL_E, WIDTH, FF_E), f32),
            jax.ShapeDtypeStruct((LOCAL_E, FF_E, WIDTH), f32),
        ],
        input_output_aliases={1 + count + i: i for i in range(len(filled))},
        cost_estimate=cost(2 * count),
        compiler_params=params(48),
        name="unpack_experts",
    )(ctx_at, *pieces, *filled)


def relay_kernel(
    p0, p1, p3, p6, relay_a, relay_b, got_10, got_31, add_a, add_b, part_0, part_1
):
    add_a[...] = (p6[...].astype(f32) + relay_a[...].astype(f32)).astype(bf16)
    add_b[...] = (p3[...].astype(f32) + relay_b[...].astype(f32)).astype(bf16)
    part_0[...] = p0[...].astype(f32) + got_10[...].astype(f32)
    part_1[...] = p1[...].astype(f32) + got_31[...].astype(f32)


def side_kernel(part_0, part_1, got_11, got_30, own, side):
    own[...] = part_0[...] + got_30[...].astype(f32)
    side[...] = (part_1[...] + got_11[...].astype(f32)).astype(bf16)


def piece_sums(kernel, kinds, *pieces):
    specs, arrays = [], []
    for piece in pieces:
        array, second = piece if isinstance(piece, tuple) else (piece, 0)
        specs.append(pl.BlockSpec((PIECE // 4, HEAD_DIM), lambda i, at=4 * second: (i + at, 0)))
        arrays.append(array)
    return pl.pallas_call(
        kernel,
        grid=(4,),
        in_specs=specs,
        out_specs=[pl.BlockSpec((PIECE // 4, HEAD_DIM), lambda i: (i, 0))] * len(kinds),
        out_shape=[jax.ShapeDtypeStruct((PIECE, HEAD_DIM), kind) for kind in kinds],
        cost_estimate=cost(1),
        compiler_params=params(32),
        name="piece_sums",
    )(*arrays)


same_core = [[2 * i + c for i in range(8)] for c in range(2)]
core_swap = [(i, i ^ 1) for i in range(N_EXP)]
y_groups = [[0, 1, 2, 3], [4, 5, 6, 7]]
z_swap = [(i, i ^ 4) for i in range(N_CTX)]


def swap_all(rows, axis, groups=None):
    return lax.all_to_all(
        rows, axis, split_axis=0, concat_axis=0, tiled=True, axis_index_groups=groups
    )


def after(value, *others):
    return lax.optimization_barrier((value,) + others)[0]


def add_low(a, b):
    return (a.astype(f32) + b.astype(f32)).astype(bf16)


def on_device(
    tokens,
    routes,
    route_gates,
    norm_attn,
    norm_ffn,
    query_weight,
    key_weight,
    value_weight,
    out_weight,
    shared_gate,
    shared_up,
    shared_down,
    expert_gate,
    expert_up,
    expert_down,
    cotangent,
):
    exp_at = lax.axis_index("exp").astype(jnp.int32)
    ctx_at = lax.axis_index("ctx").astype(jnp.int32)
    exp_s, ctx_s = exp_at.reshape(1), ctx_at.reshape(1)

    z_at = ctx_at // 4

    w_cat = jnp.concatenate([query_weight, out_weight, key_weight, value_weight], axis=1)
    w_all = lax.all_gather(w_cat, "exp", axis=0, tiled=True)
    gates_high = route_gates[0].astype(bf16)
    gates_low = (route_gates[0] - gates_high.astype(f32)).astype(bf16)
    pad = jnp.zeros((BLOCK, META - 3 * TOPK), bf16)
    up_meta = jnp.concatenate(
        [cotangent[0], routes[0].astype(bf16), gates_high, gates_low, pad], axis=1
    )
    up_all = lax.all_gather(after(up_meta, w_cat), "exp", axis=0, tiled=True)
    gains = after(jnp.concatenate([norm_attn, norm_ffn]), w_cat)
    gains = swap_all(jnp.broadcast_to(gains, (N_EXP, gains.shape[0])), "exp")
    gain_attn = gains[:, :96].reshape(1, WIDTH).astype(f32)
    gain_ffn = gains[:, 96:].reshape(1, WIDTH).astype(f32)

    def of_sequence(rows):
        other = lax.ppermute(rows, "ctx", z_swap)
        pair = jnp.where(
            z_at == 0,
            jnp.concatenate([rows, other], axis=0),
            jnp.concatenate([other, rows], axis=0),
        )
        got = swap_all(jnp.broadcast_to(pair, (4, 2, BLOCK, WIDTH)), "ctx", y_groups)
        return got.reshape(N_CTX, BLOCK, WIDTH)

    tokens_seq = of_sequence(after(tokens, w_cat))
    shared_cols = jnp.concatenate(
        [shared_gate.reshape(96, N_EXP, SHARED), shared_up.reshape(96, N_EXP, SHARED)], axis=2
    ).transpose(1, 0, 2)
    w_shared = swap_all(shared_cols, "exp").reshape(WIDTH, 2 * SHARED)
    shared_two = jnp.concatenate([shared_down, shared_down], axis=0)

    hidden_one = norm_rows(tokens, gain_attn)
    hidden_seq = norm_rows(tokens_seq, gain_attn)
    hidden_seq = after(hidden_seq, w_shared)
    queries, kv_all = project(hidden_one, hidden_seq, w_all)
    attended, att_f, logs = attend(ctx_s, queries, kv_all)
    middle, hidden_two = middle_norm(attended, w_all, tokens[0], gain_ffn)

    hidden_all = lax.all_gather(hidden_two, "exp", axis=0, tiled=True)
    hidden_all = hidden_all.reshape(HALF, 2, BLOCK, WIDTH)
    att_seq = of_sequence(attended[None])
    place, grad_eo, grad_eh, grad_sh, slot_gate = place_rows(
        exp_s,
        after(up_all, hidden_two).reshape(HALF, 2, BLOCK, WIDTH + META),
        expert_down,
        shared_two,
    )
    part, arrived, act, grad_gu, shared_act, shared_grad = expert_back(
        exp_s, after(hidden_all, att_seq), place, grad_eh, grad_sh, expert_gate, expert_up, w_shared
    )
    summed = add_low(part[1], lax.ppermute(part[0], "exp", core_swap))
    grad_two = swap_all(summed, "exp", same_core)

    rows_e = 2 * ROWS
    operands = (
        after(arrived, summed).reshape(LOCAL_E, rows_e, WIDTH),
        grad_eo.reshape(LOCAL_E, rows_e, WIDTH),
        act.reshape(LOCAL_E, rows_e, FF_E),
        grad_gu.reshape(LOCAL_E, rows_e, 2 * FF_E),
    )
    for_1, for_3 = expert_weights(ctx_s, ((2, 0), (1, 0), (2, 1), (3, 1)), True, *operands)
    operands = (after(operands[0], for_1),) + operands[1:]
    p0, p6, p1, p3 = expert_weights(ctx_s, ((0, 0), (3, 0), (0, 1), (1, 1)), False, *operands)

    def to(rows, k):
        return lax.ppermute(rows, "ctx", [(i, i ^ k) for i in range(N_CTX)])

    from_1, from_3 = to(for_1, 1), to(for_3, 3)
    shared_grad_late = after(shared_grad, p0).reshape(N_EXP * BLOCK, META)
    grad_scols = dg(hidden_all.reshape(N_EXP * BLOCK, WIDTH), shared_grad_late, TN).astype(bf16)
    act_late = after(shared_act, p0).reshape(N_EXP * BLOCK, META)
    grad_sdown = dg(act_late, up_all, TN)[:SHARED, :WIDTH].astype(bf16)
    extra = jnp.concatenate(
        [
            jnp.pad(
                grad_scols.reshape(N_EXP, N_CTX, 12, META).transpose(1, 0, 2, 3),
                ((0, 0), (0, 0), (0, 4), (0, 0)),
            ).reshape(N_CTX, 16 * N_EXP, META),
            grad_sdown.reshape(N_CTX, 8, HEADS, 128).transpose(0, 2, 1, 3).reshape(N_CTX, 96, 128),
        ],
        axis=1,
    )

    out_part = expert_output(
        exp_s, after(act, p0), slot_gate, place, shared_act, expert_down, shared_two
    )
    grad_two = after(grad_two, extra, out_part)
    grad_middle, grad_attn, grad_heads, gain_rows = middle_back(
        grad_two, middle, cotangent[0], gain_ffn, w_all
    )
    grad_query, near, far = attend_back(
        ctx_s, queries, grad_heads, att_f, logs, kv_all, grad_attn, extra, gain_rows
    )
    far = lax.ppermute(far, "ctx", z_swap)
    from_1, from_3 = after((from_1, from_3), near)
    add_a, add_b, part_0, part_1 = piece_sums(
        relay_kernel,
        (bf16, bf16, f32, f32),
        p0,
        p1,
        p3,
        p6,
        (from_1, 0),
        (from_3, 0),
        (from_1, 1),
        (from_3, 1),
    )
    got_11, got_30 = to(add_b, 1), to(add_a, 3)

    def from_x(rows, k):
        return lax.ppermute(rows, "exp", [(i, i ^ (4 * k)) for i in range(N_EXP)])

    out_sums = spread_sums(
        exp_s,
        after(out_part, add_a),
        lax.ppermute(out_part[0, :4], "exp", core_swap),
        lax.ppermute(out_part[0, 4:], "exp", core_swap),
    )
    out_near = (
        out_sums[0].astype(f32)
        + from_x(out_sums[1], 1).astype(f32)
        + from_x(out_sums[3], 3).astype(f32)
    )
    got_11, got_30 = after((got_11, got_30), far)
    own_part, side = piece_sums(side_kernel, (f32, bf16), part_0, part_1, got_11, got_30)
    across = to(side, 4)
    out_2 = from_x(after(out_sums[2], side), 2)

    shares = merge_shares(ctx_s, near, after(far, side, out_near))
    got = swap_all(shares, "ctx", y_groups)
    own = (own_part + after(across, shares).astype(f32)).astype(bf16)
    at_1, at_3, at_z = to(own, 1), to(own, 3), to(own, 4)

    columns, grad_kv, grad_down = column_grads(got, after(hidden_seq, own), att_seq)
    out_rows = after(out_near, columns) + out_2.astype(f32)
    out_across = lax.ppermute(
        out_rows[1].astype(bf16), "exp", [(i, i ^ 2) for i in range(N_EXP)]
    )
    owned = swap_all(columns, "exp")
    query_part = query_back(after(grad_query, columns), w_all)
    owned, gain_sum = owned_sums(owned, grad_down)
    at_z, at_1, at_3 = lax.optimization_barrier((after(at_z, out_2), at_1, at_3))
    owned, at_z1, at_z3 = lax.optimization_barrier((owned, to(at_z, 1), to(at_z, 3)))
    at_2, at_z2 = to(at_3, 1), to(at_z1, 3)
    mixed = (middle + out_rows[0] + out_across.astype(f32)).astype(bf16)[None]
    experts = unpack_experts(
        ctx_s,
        ((0, 0), (1, 0), (3, 0), (0, 1), (1, 1), (3, 1)),
        (after(own, owned), at_1, at_3, at_z, at_z1, at_z3),
    )
    owned = jnp.broadcast_to(owned, (N_CTX, OWNED_ROWS, HEAD_DIM))
    owned = swap_all(jnp.concatenate([grad_kv, owned], axis=1), "ctx")
    gain_attn_sum, *dense = finish(
        after(owned, experts[0], mixed, query_part),
        norm_attn.astype(f32).reshape(96, 1),
        query_weight,
        key_weight,
        value_weight,
    )
    input_grad = input_back(query_part, owned, w_all, tokens[0], gain_attn, grad_middle)
    at_2 = after(at_2, input_grad, *dense)
    experts = unpack_experts(
        ctx_s, ((2, 0), (2, 1)), (at_2, at_z2), experts
    )
    return (
        mixed,
        input_grad[None],
        gain_attn_sum[:, 0],
        gain_sum[12, :96],
        *dense,
        *experts,
    )


def solution(mesh):
    token_spec = P("exp", "ctx", None)
    rows = P("exp", None)
    expert = P("exp", None, None)
    placed = (token_spec,) * 3 + (P("exp"),) * 2 + (rows,) * 7 + (expert,) * 3 + (token_spec,)
    return jax.shard_map(
        on_device,
        mesh=mesh,
        in_specs=placed,
        out_specs=(token_spec,) * 2 + (P("exp"),) * 2 + (rows,) * 7 + (expert,) * 3,
        check_vma=False,
    )
```

```python
import jax
import jax.numpy as jnp
from jax import lax
from jax.sharding import PartitionSpec as P
from jax.experimental import pallas as pl
from jax.experimental.pallas import tpu as pltpu

HEADS = 12
KV_HEADS = 4
HEAD_DIM = 128
TOPK = 6
GROUP = 3
BLOCK = 128
WIDTH = 1536
KV_WIDTH = KV_HEADS * HEAD_DIM
CAP = 48
N_EXP = 16
N_CTX = 8
LOCAL_E = 2
FF_E = 512
SHARED = 64
META = 128
HALF = 8
ROWS = HALF * CAP

epsilon = 1e-05
masked_score = -1e30
f32 = jnp.float32
bf16 = jnp.bfloat16
log2_e = 1.4426950408889634
score_scale = HEAD_DIM ** (-0.5) * log2_e

NN = (((1,), (0,)), ((), ()))
NT = (((1,), (1,)), ((), ()))
TN = (((0,), (0,)), ((), ()))


def dg(a, b, dims):
    return lax.dot_general(a, b, dims, preferred_element_type=f32)


def params(mib):
    return pltpu.CompilerParams(vmem_limit_bytes=mib * 1024 * 1024)


def cost(us):
    return pl.CostEstimate(flops=0, bytes_accessed=int(us * 3690000), transcendentals=0)


def whole(shape):
    return pl.BlockSpec(shape, lambda *_: (0,) * len(shape), pipeline_mode=pl.Buffered(1))


def sigmoid(v):
    return 1.0 / (1.0 + jnp.exp(-v))


def allowed_scores(ctx_at):
    rows = lax.broadcasted_iota(jnp.int32, (GROUP * BLOCK, N_CTX * BLOCK), 0) % BLOCK
    cols = lax.broadcasted_iota(jnp.int32, (GROUP * BLOCK, N_CTX * BLOCK), 1)
    return rows + ctx_at * BLOCK >= cols


def stack_heads(block):
    return jnp.concatenate([block[:, j * HEAD_DIM : (j + 1) * HEAD_DIM] for j in range(GROUP)], axis=0)


def unstack_heads(rows):
    return jnp.concatenate([rows[j * BLOCK : (j + 1) * BLOCK] for j in range(GROUP)], axis=1)


def attend_kernel(ctx_ref, q_ref, k_ref, v_ref, att_ref, attf_ref, log_ref):
    q = stack_heads(q_ref[...])
    keys = k_ref[...].reshape(N_CTX * BLOCK, HEAD_DIM)
    values = v_ref[...].reshape(N_CTX * BLOCK, HEAD_DIM)
    scores = jnp.where(allowed_scores(ctx_ref[0]), dg(q, keys, NT) * score_scale, masked_score)
    top = jnp.max(scores, axis=-1, keepdims=True)
    weights = jnp.exp2(scores - top)
    total = jnp.sum(weights, axis=-1, keepdims=True)
    out = dg(weights.astype(bf16), values, NN) * (1.0 / total)
    out = unstack_heads(out)
    attf_ref[...] = out
    att_ref[...] = out.astype(bf16)
    log_ref[...] = jnp.broadcast_to(top + jnp.log2(total), (GROUP * BLOCK, HEAD_DIM))


def kv_specs():
    return [
        pl.BlockSpec((N_CTX, BLOCK, HEAD_DIM), lambda g: (0, 0, g)),
        pl.BlockSpec((N_CTX, BLOCK, HEAD_DIM), lambda g: (0, 0, KV_HEADS + g)),
    ]


def head_spec():
    return pl.BlockSpec((BLOCK, GROUP * HEAD_DIM), lambda g: (0, g))


def attend(ctx_at, qkv, kv_all):
    return pl.pallas_call(
        attend_kernel,
        grid=(KV_HEADS,),
        in_specs=[pl.BlockSpec(memory_space=pltpu.SMEM), head_spec()] + kv_specs(),
        out_specs=[
            head_spec(),
            head_spec(),
            pl.BlockSpec((GROUP * BLOCK, HEAD_DIM), lambda g: (g, 0)),
        ],
        out_shape=[
            jax.ShapeDtypeStruct((BLOCK, WIDTH), bf16),
            jax.ShapeDtypeStruct((BLOCK, WIDTH), f32),
            jax.ShapeDtypeStruct((HEADS * BLOCK, HEAD_DIM), f32),
        ],
        cost_estimate=cost(6),
        compiler_params=params(48),
        name="attend",
    )(ctx_at, qkv, kv_all, kv_all)


SEQ = N_CTX * BLOCK
AT_QUERY, AT_MIXED, AT_OUT = SEQ, SEQ + BLOCK, SEQ + 2 * BLOCK
AT_SHARED = SEQ + 3 * BLOCK
AT_DOWN = AT_SHARED + 16 * N_EXP
AT_GAIN = AT_DOWN + 96
SENT_ROWS = AT_GAIN + 16


def halves(a, b, lane):
    low = jnp.where(lane < 64, a, pltpu.roll(b, 64, 1))
    high = jnp.where(lane < 64, pltpu.roll(a, 64, 1), b)
    return low, high


def attend_back_kernel(
    ctx_ref,
    q_ref,
    ga_ref,
    attf_ref,
    log_ref,
    k_ref,
    v_ref,
    all_ga_ref,
    extra_ref,
    gain_ref,
    dq_ref,
    near_ref,
    far_ref,
    kept_ref,
):
    group = pl.program_id(0)
    z_at = ctx_ref[0] // 4

    def send(dest, z, start, stop, rows):
        @pl.when(z_at == z)
        def _():
            near_ref[dest, start:stop] = rows

        @pl.when(z_at != z)
        def _():
            far_ref[dest, start:stop] = rows

    q = stack_heads(q_ref[...])
    grad = stack_heads(ga_ref[...])
    delta = jnp.sum(grad.astype(f32) * stack_heads(attf_ref[...]), axis=-1, keepdims=True)
    keys = k_ref[...].reshape(SEQ, HEAD_DIM)
    values = v_ref[...].reshape(SEQ, HEAD_DIM)
    scores = jnp.where(allowed_scores(ctx_ref[0]), dg(q, keys, NT) * score_scale, masked_score)
    weights = jnp.exp2(scores - log_ref[:, :1])
    grad_weights = dg(grad, values, NT)
    grad_raw = (weights * (grad_weights - delta)).astype(bf16)
    scale = HEAD_DIM ** (-0.5)
    dq = unstack_heads(dg(grad_raw, keys, NN) * scale)
    dq_ref[...] = dq.astype(bf16)
    kept_ref[group] = dq
    grad_k = dg(grad_raw, q, TN) * scale
    grad_v = dg(weights.astype(bf16), grad, TN)
    low, high = halves(grad_k, grad_v, lax.broadcasted_iota(jnp.int32, (SEQ, HEAD_DIM), 1))
    low, high = low.astype(bf16), high.astype(bf16)
    send(2 * (group % 2), group // 2, 0, SEQ, low)
    send(2 * (group % 2) + 1, group // 2, 0, SEQ, high)

    @pl.when(group == KV_HEADS - 1)
    def _():
        lane = lax.broadcasted_iota(jnp.int32, (BLOCK, HEAD_DIM), 1)

        def dq_tile(m):
            return kept_ref[m // GROUP, :, HEAD_DIM * (m % GROUP) : HEAD_DIM * (m % GROUP + 1)]

        def ga_tile(m):
            return all_ga_ref[:, HEAD_DIM * m : HEAD_DIM * (m + 1)].astype(f32)

        mixed = []
        for m in range(KV_HEADS):
            mixed += halves(dq_tile(N_CTX + m), ga_tile(N_CTX + m), lane)
        gains = gain_ref[...].astype(bf16)
        for c in range(N_CTX):
            tiles = [dq_tile(c).astype(bf16), mixed[c].astype(bf16), ga_tile(c).astype(bf16)]
            rows = jnp.concatenate(tiles + [extra_ref[c], gains], axis=0)
            send(c % 4, c // 4, AT_QUERY, SENT_ROWS, rows)


def attend_back(ctx_at, qkv, grad_att, att_f, logs, kv_all, grad_attn, extra, gain_rows):
    return pl.pallas_call(
        attend_back_kernel,
        grid=(KV_HEADS,),
        in_specs=[
            pl.BlockSpec(memory_space=pltpu.SMEM),
            head_spec(),
            head_spec(),
            head_spec(),
            pl.BlockSpec((GROUP * BLOCK, HEAD_DIM), lambda g: (g, 0)),
        ]
        + kv_specs()
        + [
            whole((BLOCK, WIDTH)),
            whole((N_CTX, AT_GAIN - AT_SHARED, HEAD_DIM)),
            whole((16, HEAD_DIM)),
        ],
        out_specs=[head_spec()] + [whole((4, SENT_ROWS, HEAD_DIM))] * 2,
        out_shape=[
            jax.ShapeDtypeStruct((BLOCK, WIDTH), bf16),
            jax.ShapeDtypeStruct((4, SENT_ROWS, HEAD_DIM), bf16),
            jax.ShapeDtypeStruct((4, SENT_ROWS, HEAD_DIM), bf16),
        ],
        scratch_shapes=[pltpu.VMEM((KV_HEADS, BLOCK, GROUP * HEAD_DIM), f32)],
        cost_estimate=cost(2),
        compiler_params=params(60),
        name="attend_back",
    )(ctx_at, qkv, grad_att, att_f, logs, kv_all, kv_all, grad_attn, extra, gain_rows)


def middle_kernel(att_ref, w_ref, x_ref, gain_ref, middle_ref, hidden_ref):
    middle = x_ref[...].astype(f32) + dg(att_ref[...], w_ref[...], NN)
    inv = lax.rsqrt(jnp.mean(middle * middle, axis=-1, keepdims=True) + epsilon)
    middle_ref[...] = middle
    hidden_ref[...] = (middle * inv * gain_ref[...]).astype(bf16)


def w_cols(width, at):
    return pl.BlockSpec((WIDTH, width), lambda *_: (0, at), pipeline_mode=pl.Buffered(1))


def middle_norm(attended, w_all, tokens, gain):
    return pl.pallas_call(
        middle_kernel,
        grid=(1,),
        in_specs=[
            whole((BLOCK, WIDTH)),
            w_cols(WIDTH, 1),
            whole((BLOCK, WIDTH)),
            whole((1, WIDTH)),
        ],
        out_specs=[whole((BLOCK, WIDTH)), whole((BLOCK, WIDTH))],
        out_shape=[
            jax.ShapeDtypeStruct((BLOCK, WIDTH), f32),
            jax.ShapeDtypeStruct((BLOCK, WIDTH), bf16),
        ],
        cost_estimate=cost(2),
        compiler_params=params(60),
        name="middle_norm",
    )(attended, w_all, tokens, gain)


def norm_back(grad_normed, normed, inv_root):
    return inv_root * (
        grad_normed - normed * jnp.mean(grad_normed * normed, axis=-1, keepdims=True)
    )


def middle_back_kernel(
    pieces_ref, middle_ref, up_ref, gain_ref, w_ref, gm_ref, ga_ref, gh_ref, gg_ref
):
    grad_two = pieces_ref[0].astype(f32)
    for i in range(1, HALF):
        grad_two = grad_two + pieces_ref[i].astype(f32)
    middle = middle_ref[...]
    inv = lax.rsqrt(jnp.mean(middle * middle, axis=-1, keepdims=True) + epsilon)
    normed = middle * inv
    gains = jnp.sum(grad_two * normed, axis=0, keepdims=True)
    gg_ref[...] = jnp.zeros((16, HEAD_DIM), f32)
    for m in range(HEADS):
        gg_ref[m : m + 1] = gains[:, HEAD_DIM * m : HEAD_DIM * (m + 1)]
    grad_middle = up_ref[...].astype(f32) + norm_back(grad_two * gain_ref[...], normed, inv)
    gm_ref[...] = grad_middle
    grad_attn = grad_middle.astype(bf16)
    ga_ref[...] = grad_attn
    gh_ref[...] = dg(grad_attn, w_ref[...], NT).astype(bf16)


def middle_back(pieces, middle, upstream, gain, w_all):
    return pl.pallas_call(
        middle_back_kernel,
        grid=(1,),
        in_specs=[
            whole((HALF, BLOCK, WIDTH)),
            whole((BLOCK, WIDTH)),
            whole((BLOCK, WIDTH)),
            whole((1, WIDTH)),
            w_cols(WIDTH, 1),
        ],
        out_specs=[whole((BLOCK, WIDTH))] * 3 + [whole((16, HEAD_DIM))],
        out_shape=[
            jax.ShapeDtypeStruct((BLOCK, WIDTH), f32),
            jax.ShapeDtypeStruct((BLOCK, WIDTH), bf16),
            jax.ShapeDtypeStruct((BLOCK, WIDTH), bf16),
            jax.ShapeDtypeStruct((16, HEAD_DIM), f32),
        ],
        cost_estimate=cost(1),
        compiler_params=params(48),
        name="middle_back",
    )(pieces, middle, upstream, gain, w_all)


def place_kernel(
    at_ref, up_ref, down_ref, sdown_ref, place_ref, geo_ref, geh_ref, gsh_ref, gate_ref
):
    lane = lax.broadcasted_iota(jnp.int32, (BLOCK, META), 1)
    row = lax.broadcasted_iota(jnp.int32, (BLOCK, META), 0)
    before = (row > lane).astype(bf16)
    slot = (lane % 64).astype(f32)
    first_id = (at_ref[0] * LOCAL_E).astype(f32)
    row_id = first_id + (row >= 64).astype(f32)

    for chip in range(HALF):
        meta = up_ref[chip, 0, :, WIDTH:].astype(f32)
        named = lane < TOPK
        zero = jnp.zeros((BLOCK, META), f32)
        hit0 = jnp.where(named & (meta == first_id), 1.0, zero)
        hit1 = jnp.where(named & (meta == first_id + 1.0), 1.0, zero)
        mask = jnp.where(
            lane < 64,
            jnp.sum(hit0, axis=1, keepdims=True),
            jnp.sum(hit1, axis=1, keepdims=True),
        )
        rank = dg(before, mask.astype(bf16), NN)
        place = jnp.where((mask > 0.5) & (rank == slot), 1.0, zero).astype(bf16)
        place_ref[chip, 0] = place
        rows = dg(place, up_ref[chip, 0], TN)
        slot_meta = rows[:, WIDTH:]
        gates = pltpu.roll(slot_meta, META - TOPK, 1) + pltpu.roll(
            slot_meta, META - 2 * TOPK, 1
        )
        gate = jnp.sum(
            jnp.where(named & (slot_meta == row_id), gates, zero), axis=1, keepdims=True
        )
        geo = (gate * rows[:, :WIDTH]).astype(bf16)
        wide_gate = jnp.broadcast_to(gate, (BLOCK, META))
        at = chip * CAP
        for e in range(LOCAL_E):
            geo_ref[e, 0, at : at + CAP] = geo[64 * e : 64 * e + CAP]
            gate_ref[e, 0, at : at + CAP] = wide_gate[64 * e : 64 * e + CAP]
        gsh_ref[chip, 0] = dg(up_ref[chip, 0, :, :WIDTH], sdown_ref[...], NT)
    for e in range(LOCAL_E):
        geh_ref[e, 0] = dg(geo_ref[e, 0], down_ref[e], NT)


def by_core(cols):
    return pl.BlockSpec(
        (HALF, 1, BLOCK, cols),
        lambda s, at: (0, jnp.where(s == 0, 1 - at[0] % 2, at[0] % 2), 0, 0),
    )


def by_step(cols):
    return pl.BlockSpec((LOCAL_E, 1, ROWS, cols), lambda s, at: (0, s, 0, 0))


def place_rows(exp_at, up_all, expert_down, shared_two):
    return pl.pallas_call(
        place_kernel,
        grid_spec=pltpu.PrefetchScalarGridSpec(
            num_scalar_prefetch=1,
            grid=(2,),
            in_specs=[
                by_core(WIDTH + META),
                whole((LOCAL_E, FF_E, WIDTH)),
                whole((2 * SHARED, WIDTH)),
            ],
            out_specs=[by_core(META), by_step(WIDTH), by_step(FF_E), by_core(META), by_step(META)],
        ),
        out_shape=[
            jax.ShapeDtypeStruct((HALF, 2, BLOCK, META), bf16),
            jax.ShapeDtypeStruct((LOCAL_E, 2, ROWS, WIDTH), bf16),
            jax.ShapeDtypeStruct((LOCAL_E, 2, ROWS, FF_E), f32),
            jax.ShapeDtypeStruct((HALF, 2, BLOCK, META), f32),
            jax.ShapeDtypeStruct((LOCAL_E, 2, ROWS, META), f32),
        ],
        cost_estimate=cost(14),
        compiler_params=params(56),
        name="place_rows",
    )(exp_at, up_all, expert_down, shared_two)


def expert_kernel(
    at_ref,
    hid_ref,
    place_ref,
    geh_ref,
    gsh_ref,
    wg_ref,
    wu_ref,
    ws_ref,
    part_ref,
    x_ref,
    act_ref,
    dgu_ref,
    sact_ref,
    sgrad_ref,
):
    for chip in range(HALF):
        rows = dg(place_ref[chip, 0], hid_ref[chip, 0], TN).astype(bf16)
        at = chip * CAP
        for e in range(LOCAL_E):
            x_ref[e, 0, at : at + CAP] = rows[64 * e : 64 * e + CAP]
    pairs = []
    for e in range(LOCAL_E):
        pre_gate = dg(x_ref[e, 0], wg_ref[e], NN)
        pre_up = dg(x_ref[e, 0], wu_ref[e], NN)
        sig = sigmoid(pre_gate)
        act = pre_gate * sig
        act_ref[e, 0] = (act * pre_up).astype(bf16)
        geh = geh_ref[e, 0]
        d_gate = (geh * pre_up * (sig * (1.0 + pre_gate * (1.0 - sig)))).astype(bf16)
        d_up = (geh * act).astype(bf16)
        dgu_ref[e, 0, :, :FF_E] = d_gate
        dgu_ref[e, 0, :, FF_E:] = d_up
        pairs.append((dg(d_gate, wg_ref[e], NT) + dg(d_up, wu_ref[e], NT)).astype(bf16))
    lane = lax.broadcasted_iota(jnp.int32, (BLOCK, 2 * SHARED), 1) < SHARED
    gap = jnp.zeros((64 - CAP, WIDTH), bf16)
    for chip in range(HALF):
        pre = dg(hid_ref[chip, 0], ws_ref[...], NN)
        turned = pltpu.roll(pre, SHARED, 1)
        gate, up = jnp.where(lane, pre, turned), jnp.where(lane, turned, pre)
        sig = sigmoid(gate)
        act = gate * sig
        sact_ref[chip, 0] = jnp.where(lane, act * up, 0.0).astype(bf16)
        slope = sig * (1.0 + gate * (1.0 - sig))
        sgrad = (gsh_ref[chip, 0] * jnp.where(lane, up * slope, act)).astype(bf16)
        sgrad_ref[chip, 0] = sgrad
        at = chip * CAP
        stacked = jnp.concatenate([pairs[0][at : at + CAP], gap, pairs[1][at : at + CAP], gap], 0)
        part_ref[0, chip] = (
            dg(place_ref[chip, 0], stacked, NN) + dg(sgrad, ws_ref[...], NT)
        ).astype(bf16)


def expert_back(exp_at, hidden, place, geh, gsh, wg, wu, ws):
    return pl.pallas_call(
        expert_kernel,
        grid_spec=pltpu.PrefetchScalarGridSpec(
            num_scalar_prefetch=1,
            grid=(2,),
            in_specs=[
                by_core(WIDTH),
                by_core(META),
                by_step(FF_E),
                by_core(META),
                whole((LOCAL_E, WIDTH, FF_E)),
                whole((LOCAL_E, WIDTH, FF_E)),
                whole((WIDTH, 2 * SHARED)),
            ],
            out_specs=[
                pl.BlockSpec((1, HALF, BLOCK, WIDTH), lambda s, at: (s, 0, 0, 0)),
                by_step(WIDTH),
                by_step(FF_E),
                by_step(2 * FF_E),
                by_core(META),
                by_core(META),
            ],
        ),
        out_shape=[
            jax.ShapeDtypeStruct((2, HALF, BLOCK, WIDTH), bf16),
            jax.ShapeDtypeStruct((LOCAL_E, 2, ROWS, WIDTH), bf16),
            jax.ShapeDtypeStruct((LOCAL_E, 2, ROWS, FF_E), bf16),
            jax.ShapeDtypeStruct((LOCAL_E, 2, ROWS, 2 * FF_E), bf16),
            jax.ShapeDtypeStruct((HALF, 2, BLOCK, META), bf16),
            jax.ShapeDtypeStruct((HALF, 2, BLOCK, META), bf16),
        ],
        cost_estimate=cost(28),
        compiler_params=params(60),
        name="expert_back",
    )(exp_at, hidden, place, geh, gsh, wg, wu, ws)


def output_kernel(at_ref, act_ref, gate_ref, place_ref, sact_ref, wd_ref, sd_ref, part_ref):
    outs = []
    for e in range(LOCAL_E):
        out = dg(act_ref[e, 0], wd_ref[e], NN).astype(bf16).astype(f32)
        outs.append((out * gate_ref[e, 0, :, :1]).astype(bf16))
    gap = jnp.zeros((64 - CAP, WIDTH), bf16)
    for chip in range(HALF):
        at = chip * CAP
        stacked = jnp.concatenate([outs[0][at : at + CAP], gap, outs[1][at : at + CAP], gap], 0)
        part_ref[0, chip] = (
            dg(place_ref[chip, 0], stacked, NN) + dg(sact_ref[chip, 0], sd_ref[...], NN)
        ).astype(bf16)


def expert_output(exp_at, act, gate, place, sact, wd, sd):
    return pl.pallas_call(
        output_kernel,
        grid_spec=pltpu.PrefetchScalarGridSpec(
            num_scalar_prefetch=1,
            grid=(2,),
            in_specs=[
                by_step(FF_E),
                by_step(META),
                by_core(META),
                by_core(META),
                whole((LOCAL_E, FF_E, WIDTH)),
                whole((2 * SHARED, WIDTH)),
            ],
            out_specs=pl.BlockSpec((1, HALF, BLOCK, WIDTH), lambda s, at: (s, 0, 0, 0)),
        ),
        out_shape=jax.ShapeDtypeStruct((2, HALF, BLOCK, WIDTH), bf16),
        cost_estimate=cost(2),
        compiler_params=params(48),
        name="expert_output",
    )(exp_at, act, gate, place, sact, wd, sd)


SHARE = 3 * BLOCK
TO_SHARED = SEQ + 2 * SHARE
TO_DOWN = TO_SHARED + 16 * N_EXP
TO_GAIN = TO_DOWN + 96
MERGED_ROWS = TO_GAIN + 16


def merge_kernel(ctx_ref, near_ref, got_ref, out_ref):
    z_at = ctx_ref[0] // 4
    near, got = near_ref[0], got_ref[0]

    def add(a, b):
        return (a.astype(f32) + b.astype(f32)).astype(bf16)

    out_ref[0, :SEQ] = add(near[:SEQ], got[:SEQ])
    out_ref[0, TO_SHARED:] = add(near[AT_SHARED:], got[AT_SHARED:])
    mine, theirs = near[AT_QUERY:AT_SHARED], got[AT_QUERY:AT_SHARED]
    out_ref[0, SEQ : SEQ + SHARE] = jnp.where(z_at == 0, mine, theirs)
    out_ref[0, SEQ + SHARE : TO_SHARED] = jnp.where(z_at == 0, theirs, mine)


def merge_shares(ctx_at, near, got):
    spec = pl.BlockSpec((1, SENT_ROWS, HEAD_DIM), lambda i: (i, 0, 0))
    return pl.pallas_call(
        merge_kernel,
        grid=(4,),
        in_specs=[pl.BlockSpec(memory_space=pltpu.SMEM), spec, spec],
        out_specs=pl.BlockSpec((1, MERGED_ROWS, HEAD_DIM), lambda i: (i, 0, 0)),
        out_shape=jax.ShapeDtypeStruct((4, MERGED_ROWS, HEAD_DIM), bf16),
        cost_estimate=cost(3),
        compiler_params=params(32),
        name="merge_shares",
    )(ctx_at, near, got)


def columns_kernel(got_ref, hidden_ref, att_ref, sent_ref, kv_ref, down_ref):
    def summed(start, stop):
        out = got_ref[0, start:stop].astype(f32)
        for src in range(1, 4):
            out = out + got_ref[src, start:stop].astype(f32)
        return out

    grad_kv = summed(0, SEQ).astype(bf16)
    kv_ref[...] = grad_kv.reshape(N_CTX, BLOCK, HEAD_DIM)

    def rows_of(tile, order):
        at = SEQ + BLOCK * tile
        return jnp.concatenate(
            [got_ref[y, at + SHARE * z : at + SHARE * z + BLOCK] for z, y in order], axis=0
        )

    in_order = [(i // 4, i % 4) for i in range(N_CTX)]
    y_order = [(i % 2, i // 2) for i in range(N_CTX)]
    lane = lax.broadcasted_iota(jnp.int32, (SEQ, HEAD_DIM), 1)
    zero = jnp.zeros((SEQ, HEAD_DIM), bf16)
    mixed_q = jnp.where(lane < 64, rows_of(1, in_order), zero)
    mixed_o = jnp.where(lane < 64, zero, rows_of(1, y_order))
    left = jnp.concatenate([rows_of(0, in_order).T, mixed_q.T, grad_kv.T], axis=0)
    right = jnp.concatenate([mixed_o.T, rows_of(2, y_order).T], axis=0)
    by_hidden = dg(left, hidden_ref[...].reshape(SEQ, WIDTH), NN)
    by_att = dg(right, att_ref[...].reshape(SEQ, WIDTH), NN)
    tiles = [
        by_hidden[:BLOCK],
        by_hidden[BLOCK : 2 * BLOCK] + by_att[:BLOCK],
        by_att[BLOCK:],
        by_hidden[2 * BLOCK :],
    ]
    for t, tile in enumerate(tiles):
        sent_ref[:, :96, HEAD_DIM * t : HEAD_DIM * (t + 1)] = (
            tile.T.astype(bf16).reshape(N_EXP, 96, HEAD_DIM)
        )

    down_ref[...] = summed(TO_DOWN, TO_GAIN).astype(bf16)
    shared = summed(TO_SHARED, TO_DOWN)
    gains = summed(TO_GAIN, MERGED_ROWS)
    row = lax.broadcasted_iota(jnp.int32, (16, HEAD_DIM), 0)
    one_lane = lax.broadcasted_iota(jnp.int32, (1, HEAD_DIM), 1)
    for i in range(N_EXP):
        m, offset = (96 * i) // HEAD_DIM, (96 * i) % HEAD_DIM
        gain = gains[m : m + 1]
        if offset:
            shift = HEAD_DIM - offset
            gain = jnp.where(
                one_lane < shift,
                pltpu.roll(gain, shift, 1),
                pltpu.roll(gains[m + 1 : m + 2], shift, 1),
            )
        rows = jnp.where(row == 12, jnp.broadcast_to(gain, (16, HEAD_DIM)), shared[16 * i : 16 * i + 16])
        sent_ref[i, 96:, :HEAD_DIM] = rows.astype(bf16)
        sent_ref[i, 96:, HEAD_DIM:] = jnp.zeros((16, 512 - HEAD_DIM), bf16)


def column_grads(got, hidden_seq, att_seq):
    return pl.pallas_call(
        columns_kernel,
        out_shape=[
            jax.ShapeDtypeStruct((N_EXP, 112, 512), bf16),
            jax.ShapeDtypeStruct((N_CTX, BLOCK, HEAD_DIM), bf16),
            jax.ShapeDtypeStruct((96, HEAD_DIM), bf16),
        ],
        cost_estimate=cost(8),
        compiler_params=params(56),
        name="column_grads",
    )(got, hidden_seq, att_seq)


OWNED_ROWS = 4 * 96 + 16 * N_EXP + 96


def owned_kernel(got_ref, down_ref, owned_ref, gain_ref):
    total = got_ref[0, :96].astype(f32)
    gains = got_ref[0, 96:, :HEAD_DIM].astype(f32)
    for src in range(1, N_EXP):
        total = total + got_ref[src, :96].astype(f32)
        gains = gains + got_ref[src, 96:, :HEAD_DIM].astype(f32)
    gain_ref[...] = gains
    for t in range(4):
        owned_ref[96 * t : 96 * t + 96] = total[:, HEAD_DIM * t : HEAD_DIM * (t + 1)].astype(bf16)
    for src in range(N_EXP):
        at = 384 + 16 * src
        owned_ref[at : at + 16] = got_ref[src, 96:, :HEAD_DIM]
    owned_ref[384 + 16 * N_EXP :] = down_ref[...]


def owned_sums(got, down):
    return pl.pallas_call(
        owned_kernel,
        out_shape=[
            jax.ShapeDtypeStruct((OWNED_ROWS, HEAD_DIM), bf16),
            jax.ShapeDtypeStruct((16, HEAD_DIM), f32),
        ],
        cost_estimate=cost(3),
        compiler_params=params(32),
        name="owned_sums",
    )(got, down)


def finish_kernel(
    got_ref,
    gain_in_ref,
    wq_ref,
    wk_ref,
    wv_ref,
    gain_ref,
    q_ref,
    k_ref,
    v_ref,
    out_ref,
    sg_ref,
    su_ref,
    sd_ref,
):
    lane = lax.broadcasted_iota(jnp.int32, (96, HEAD_DIM), 1)

    def tile(c, t):
        at = BLOCK + 96 * t
        return got_ref[c, at : at + 96].astype(f32)

    for c in range(N_CTX):
        at = HEAD_DIM * c
        q_ref[:, at : at + HEAD_DIM] = tile(c, 0)
        out_ref[:, at : at + HEAD_DIM] = tile(c, 2)
    for m in range(N_CTX // 2):
        at = HEAD_DIM * m
        low, high = halves(tile(2 * m, 1), tile(2 * m + 1, 1), lane)
        q_ref[:, 1024 + at : 1024 + at + HEAD_DIM] = low
        out_ref[:, 1024 + at : 1024 + at + HEAD_DIM] = high
        low, high = halves(tile(2 * m, 3), tile(2 * m + 1, 3), lane)
        k_ref[:, at : at + HEAD_DIM] = low
        v_ref[:, at : at + HEAD_DIM] = high
    gain = (
        jnp.sum(q_ref[...] * wq_ref[...].astype(f32), axis=1, keepdims=True)
        + jnp.sum(k_ref[...] * wk_ref[...].astype(f32), axis=1, keepdims=True)
        + jnp.sum(v_ref[...] * wv_ref[...].astype(f32), axis=1, keepdims=True)
    ) / gain_in_ref[...]
    gain_ref[...] = jnp.broadcast_to(gain, (96, HEAD_DIM))
    row = lax.broadcasted_iota(jnp.int32, (96, HEAD_DIM), 0)
    picks = jnp.where((lane % 16 < 12) & (row == 12 * (lane // 16) + lane % 16), 1.0, 0.0)
    picks = picks.astype(bf16)

    def shared_tile(j):
        at = BLOCK + 384 + 16 * j
        rows = jnp.concatenate([got_ref[c, at : at + 16] for c in range(N_CTX)], axis=0)
        return dg(picks, rows, NN)

    for m in range(N_EXP // 2):
        at = HEAD_DIM * m
        low, high = halves(shared_tile(2 * m), shared_tile(2 * m + 1), lane)
        sg_ref[:, at : at + HEAD_DIM] = low
        su_ref[:, at : at + HEAD_DIM] = high
    for c in range(N_CTX):
        rows = got_ref[c, BLOCK + 384 + 16 * N_EXP :].astype(f32)
        for m in range(HEADS):
            sd_ref[8 * c : 8 * c + 8, HEAD_DIM * m : HEAD_DIM * (m + 1)] = rows[8 * m : 8 * m + 8]


def finish(got, gain_column, query_weight, key_weight, value_weight):
    shapes = [(96, 128), (96, 1536), (96, 512), (96, 512), (96, 1536), (96, 1024), (96, 1024)]
    return pl.pallas_call(
        finish_kernel,
        out_shape=[jax.ShapeDtypeStruct(s, f32) for s in shapes + [(SHARED, WIDTH)]],
        cost_estimate=cost(4),
        compiler_params=params(32),
        name="finish",
    )(got, gain_column, query_weight, key_weight, value_weight)


def input_kernel(part_ref, got_ref, wkv_ref, x_ref, gain_ref, gm_ref, out_ref):
    lane = lax.broadcasted_iota(jnp.int32, (BLOCK, HEAD_DIM), 1)
    lows, highs = [], []
    for m in range(KV_HEADS):
        low, high = halves(got_ref[2 * m].astype(f32), got_ref[2 * m + 1].astype(f32), lane)
        lows.append(low.astype(bf16))
        highs.append(high.astype(bf16))
    grad_kv = jnp.concatenate(lows + highs, axis=1)
    grad_one = part_ref[...] + dg(grad_kv, wkv_ref[...], NT)
    inputs = x_ref[...].astype(f32)
    inv = lax.rsqrt(jnp.mean(inputs * inputs, axis=-1, keepdims=True) + epsilon)
    out_ref[...] = (gm_ref[...] + norm_back(grad_one * gain_ref[...], inputs * inv, inv)).astype(bf16)


def query_kernel(dq_ref, wq_ref, out_ref):
    out_ref[...] = dg(dq_ref[...], wq_ref[...], NT)


def query_back(grad_query, w_all):
    return pl.pallas_call(
        query_kernel,
        grid=(1,),
        in_specs=[whole((BLOCK, WIDTH)), w_cols(WIDTH, 0)],
        out_specs=whole((BLOCK, WIDTH)),
        out_shape=jax.ShapeDtypeStruct((BLOCK, WIDTH), f32),
        cost_estimate=cost(4),
        compiler_params=params(32),
        name="query_back",
    )(grad_query, w_all)


def input_back(query_part, grad_kv, w_all, tokens, gain, grad_middle):
    return pl.pallas_call(
        input_kernel,
        grid=(1,),
        in_specs=[
            whole((BLOCK, WIDTH)),
            whole((N_CTX, BLOCK, HEAD_DIM)),
            w_cols(2 * KV_WIDTH, 3),
            whole((BLOCK, WIDTH)),
            whole((1, WIDTH)),
            whole((BLOCK, WIDTH)),
        ],
        out_specs=whole((BLOCK, WIDTH)),
        out_shape=jax.ShapeDtypeStruct((BLOCK, WIDTH), bf16),
        cost_estimate=cost(4),
        compiler_params=params(32),
        name="input_back",
    )(query_part, grad_kv, w_all, tokens, gain, grad_middle)


def norm_rows_kernel(x_ref, gain_ref, out_ref):
    inputs = x_ref[0].astype(f32)
    inv = lax.rsqrt(jnp.mean(inputs * inputs, axis=-1, keepdims=True) + epsilon)
    out_ref[0] = (inputs * inv * gain_ref[...]).astype(bf16)


def norm_rows(rows, gain):
    count = rows.shape[0]
    spec = pl.BlockSpec((1, BLOCK, WIDTH), lambda i: (i, 0, 0))
    turned = pl.BlockSpec((1, BLOCK, WIDTH), lambda i: ((i % 2) * 4 + i // 2, 0, 0))
    return pl.pallas_call(
        norm_rows_kernel,
        grid=(count,),
        in_specs=[spec, whole((1, WIDTH))],
        out_specs=spec if count == 1 else turned,
        out_shape=jax.ShapeDtypeStruct(rows.shape, bf16),
        cost_estimate=cost(2),
        compiler_params=params(32),
        name="norm_rows",
    )(rows, gain)


def project_kernel(own_ref, seq_ref, w_ref, q_ref, kv_ref):
    step = pl.program_id(0)

    @pl.when(step < 3)
    def _():
        q_ref[...] = dg(own_ref[0], w_ref[...], NN).astype(bf16)

    @pl.when(step >= 3)
    def _():
        rows = seq_ref[...].reshape(N_CTX * BLOCK, WIDTH)
        kv_ref[...] = dg(rows, w_ref[...], NN).astype(bf16).reshape(N_CTX, BLOCK, KV_WIDTH)


def project(own, seq, w_all):
    return pl.pallas_call(
        project_kernel,
        grid=(5,),
        in_specs=[
            whole((1, BLOCK, WIDTH)),
            whole((N_CTX, BLOCK, WIDTH)),
            pl.BlockSpec((WIDTH, KV_WIDTH), lambda i: (0, jnp.where(i < 3, i, i + 3))),
        ],
        out_specs=[
            pl.BlockSpec((BLOCK, KV_WIDTH), lambda i: (0, jnp.minimum(i, 2))),
            pl.BlockSpec((N_CTX, BLOCK, KV_WIDTH), lambda i: (0, 0, jnp.maximum(i - 3, 0))),
        ],
        out_shape=[
            jax.ShapeDtypeStruct((BLOCK, WIDTH), bf16),
            jax.ShapeDtypeStruct((N_CTX, BLOCK, 2 * KV_WIDTH), bf16),
        ],
        cost_estimate=cost(8),
        compiler_params=params(48),
        name="project",
    )(own, seq, w_all)


PIECE = 2 * WIDTH + WIDTH * BLOCK // HEAD_DIM


def spread_kernel(at_ref, own_ref, low_ref, high_ref, *outs):
    chip = (at_ref[0] >> 1) ^ pl.program_id(0)
    got = jnp.where(chip < 4, low_ref[0], high_ref[0])
    total = (own_ref[0, 0].astype(f32) + got.astype(f32)).astype(bf16)
    for k in range(HALF):

        @pl.when(pl.program_id(0) == k)
        def _():
            outs[k // 2][k % 2] = total


def spread_sums(exp_at, parts, low, high):
    half = pl.BlockSpec((1, BLOCK, WIDTH), lambda k, at: (((at[0] >> 1) ^ k) & 3, 0, 0))
    return pl.pallas_call(
        spread_kernel,
        grid_spec=pltpu.PrefetchScalarGridSpec(
            num_scalar_prefetch=1,
            grid=(HALF,),
            in_specs=[
                pl.BlockSpec((1, 1, BLOCK, WIDTH), lambda k, at: (1, (at[0] >> 1) ^ k, 0, 0)),
                half,
                half,
            ],
            out_specs=[whole((2, BLOCK, WIDTH))] * 4,
        ),
        out_shape=[jax.ShapeDtypeStruct((2, BLOCK, WIDTH), bf16)] * 4,
        cost_estimate=cost(4),
        compiler_params=params(32),
        name="spread_sums",
    )(exp_at, parts, low, high)


def of_step(values, step):
    out = jnp.int32(values[0])
    for i, value in enumerate(values[1:], 1):
        out = jnp.where(step == i, value, out)
    return out


def expert_weights_kernel(halved, at_ref, x_ref, geo_ref, act_ref, dgate_ref, dup_ref, *outs):
    step = pl.program_id(0)
    rhs = jnp.concatenate([dgate_ref[0], dup_ref[0]], axis=1)
    both = dg(x_ref[0], rhs, TN).astype(bf16)
    down = dg(act_ref[0], geo_ref[0], TN).astype(bf16)
    for i in range(4):

        @pl.when(step == i)
        def _():
            start = (i % 2) * PIECE if halved else 0
            out = outs[i // 2 if halved else i].at[pl.ds(start, PIECE)]
            out[:WIDTH] = both[:, :HEAD_DIM]
            out[WIDTH : 2 * WIDTH] = both[:, HEAD_DIM:]
            for m in range(WIDTH // HEAD_DIM):
                at = 2 * WIDTH + m * BLOCK
                out[at : at + BLOCK] = down[:, m * HEAD_DIM : (m + 1) * HEAD_DIM]


def expert_weights(ctx_at, steps, halved, arrived, grad_eo, act, grad_gu):
    rows = 2 * ROWS

    def expert(s, at):
        return (at[0] >> 2) ^ of_step([side for _, side in steps], s)

    def lanes(shift):
        return pl.BlockSpec(
            (1, rows, HEAD_DIM),
            lambda s, at: (
                expert(s, at),
                0,
                shift + ((at[0] & 3) ^ of_step([r for r, _ in steps], s)),
            ),
        )

    rows_of = pl.BlockSpec((1, rows, WIDTH), lambda s, at: (expert(s, at), 0, 0))
    count, length = (2, 2 * PIECE) if halved else (4, PIECE)
    return pl.pallas_call(
        lambda *refs: expert_weights_kernel(halved, *refs),
        grid_spec=pltpu.PrefetchScalarGridSpec(
            num_scalar_prefetch=1,
            grid=(4,),
            in_specs=[rows_of, rows_of, lanes(0), lanes(0), lanes(4)],
            out_specs=[whole((length, HEAD_DIM))] * count,
        ),
        out_shape=[jax.ShapeDtypeStruct((length, HEAD_DIM), bf16)] * count,
        cost_estimate=cost(2),
        compiler_params=params(56),
        name="expert_weights",
    )(ctx_at, arrived, grad_eo, act, grad_gu, grad_gu)


def unpack_kernel(count, at_ref, *refs):
    pieces, (gate_ref, up_ref, down_ref) = refs[:count], refs[-3:]
    step = pl.program_id(0)
    for i in range(count):

        @pl.when(step == i)
        def _():
            piece = pieces[i]
            gate_ref[0] = piece[:WIDTH].astype(f32)
            up_ref[0] = piece[WIDTH : 2 * WIDTH].astype(f32)
            for m in range(WIDTH // HEAD_DIM):
                at = 2 * WIDTH + m * BLOCK
                down_ref[0, :, m * HEAD_DIM : (m + 1) * HEAD_DIM] = piece[at : at + BLOCK].astype(
                    f32
                )


def unpack_experts(ctx_at, steps, pieces, filled=()):
    count = len(steps)

    def expert(s, at):
        return (at[0] >> 2) ^ of_step([side for _, side in steps], s)

    def units(s, at):
        return (at[0] & 3) ^ of_step([r for r, _ in steps], s)

    cols = pl.BlockSpec((1, WIDTH, HEAD_DIM), lambda s, at: (expert(s, at), 0, units(s, at)))
    rows = pl.BlockSpec((1, BLOCK, WIDTH), lambda s, at: (expert(s, at), units(s, at), 0))
    anywhere = pl.BlockSpec(memory_space=pl.ANY)
    return pl.pallas_call(
        lambda *refs: unpack_kernel(count, *refs),
        grid_spec=pltpu.PrefetchScalarGridSpec(
            num_scalar_prefetch=1,
            grid=(count,),
            in_specs=[whole((PIECE, HEAD_DIM))] * count + [anywhere] * len(filled),
            out_specs=[cols, cols, rows],
        ),
        out_shape=[
            jax.ShapeDtypeStruct((LOCAL_E, WIDTH, FF_E), f32),
            jax.ShapeDtypeStruct((LOCAL_E, WIDTH, FF_E), f32),
            jax.ShapeDtypeStruct((LOCAL_E, FF_E, WIDTH), f32),
        ],
        input_output_aliases={1 + count + i: i for i in range(len(filled))},
        cost_estimate=cost(2 * count),
        compiler_params=params(48),
        name="unpack_experts",
    )(ctx_at, *pieces, *filled)


def relay_kernel(
    p0, p1, p3, p6, relay_a, relay_b, got_10, got_31, add_a, add_b, part_0, part_1
):
    add_a[...] = (p6[...].astype(f32) + relay_a[...].astype(f32)).astype(bf16)
    add_b[...] = (p3[...].astype(f32) + relay_b[...].astype(f32)).astype(bf16)
    part_0[...] = p0[...].astype(f32) + got_10[...].astype(f32)
    part_1[...] = p1[...].astype(f32) + got_31[...].astype(f32)


def side_kernel(part_0, part_1, got_11, got_30, own, side):
    own[...] = part_0[...] + got_30[...].astype(f32)
    side[...] = (part_1[...] + got_11[...].astype(f32)).astype(bf16)


def piece_sums(kernel, kinds, *pieces):
    specs, arrays = [], []
    for piece in pieces:
        array, second = piece if isinstance(piece, tuple) else (piece, 0)
        specs.append(pl.BlockSpec((PIECE // 4, HEAD_DIM), lambda i, at=4 * second: (i + at, 0)))
        arrays.append(array)
    return pl.pallas_call(
        kernel,
        grid=(4,),
        in_specs=specs,
        out_specs=[pl.BlockSpec((PIECE // 4, HEAD_DIM), lambda i: (i, 0))] * len(kinds),
        out_shape=[jax.ShapeDtypeStruct((PIECE, HEAD_DIM), kind) for kind in kinds],
        cost_estimate=cost(1),
        compiler_params=params(32),
        name="piece_sums",
    )(*arrays)


same_core = [[2 * i + c for i in range(8)] for c in range(2)]
core_swap = [(i, i ^ 1) for i in range(N_EXP)]
y_groups = [[0, 1, 2, 3], [4, 5, 6, 7]]
z_swap = [(i, i ^ 4) for i in range(N_CTX)]


def swap_all(rows, axis, groups=None):
    return lax.all_to_all(
        rows, axis, split_axis=0, concat_axis=0, tiled=True, axis_index_groups=groups
    )


def after(value, *others):
    return lax.optimization_barrier((value,) + others)[0]


def add_low(a, b):
    return (a.astype(f32) + b.astype(f32)).astype(bf16)


def on_device(
    tokens,
    routes,
    route_gates,
    norm_attn,
    norm_ffn,
    query_weight,
    key_weight,
    value_weight,
    out_weight,
    shared_gate,
    shared_up,
    shared_down,
    expert_gate,
    expert_up,
    expert_down,
    cotangent,
):
    exp_at = lax.axis_index("exp").astype(jnp.int32)
    ctx_at = lax.axis_index("ctx").astype(jnp.int32)
    exp_s, ctx_s = exp_at.reshape(1), ctx_at.reshape(1)

    z_at = ctx_at // 4

    w_cat = jnp.concatenate([query_weight, out_weight, key_weight, value_weight], axis=1)
    w_all = lax.all_gather(w_cat, "exp", axis=0, tiled=True)
    gates_high = route_gates[0].astype(bf16)
    gates_low = (route_gates[0] - gates_high.astype(f32)).astype(bf16)
    pad = jnp.zeros((BLOCK, META - 3 * TOPK), bf16)
    up_meta = jnp.concatenate(
        [cotangent[0], routes[0].astype(bf16), gates_high, gates_low, pad], axis=1
    )
    up_all = lax.all_gather(after(up_meta, w_cat), "exp", axis=0, tiled=True)
    gains = after(jnp.concatenate([norm_attn, norm_ffn]), w_cat)
    gains = swap_all(jnp.broadcast_to(gains, (N_EXP, gains.shape[0])), "exp")
    gain_attn = gains[:, :96].reshape(1, WIDTH).astype(f32)
    gain_ffn = gains[:, 96:].reshape(1, WIDTH).astype(f32)

    def of_sequence(rows):
        other = lax.ppermute(rows, "ctx", z_swap)
        pair = jnp.where(
            z_at == 0,
            jnp.concatenate([rows, other], axis=0),
            jnp.concatenate([other, rows], axis=0),
        )
        got = swap_all(jnp.broadcast_to(pair, (4, 2, BLOCK, WIDTH)), "ctx", y_groups)
        return got.reshape(N_CTX, BLOCK, WIDTH)

    tokens_seq = of_sequence(after(tokens, w_cat))
    shared_cols = jnp.concatenate(
        [shared_gate.reshape(96, N_EXP, SHARED), shared_up.reshape(96, N_EXP, SHARED)], axis=2
    ).transpose(1, 0, 2)
    shared_two = jnp.concatenate([shared_down, shared_down], axis=0)

    hidden_one = norm_rows(tokens, gain_attn)
    hidden_seq = norm_rows(tokens_seq, gain_attn)
    queries, kv_all = project(hidden_one, hidden_seq, w_all)
    attended, att_f, logs = attend(ctx_s, queries, kv_all)
    middle, hidden_two = middle_norm(attended, w_all, tokens[0], gain_ffn)
    w_shared = swap_all(after(shared_cols, hidden_two), "exp").reshape(WIDTH, 2 * SHARED)

    hidden_all = lax.all_gather(hidden_two, "exp", axis=0, tiled=True)
    hidden_all = hidden_all.reshape(HALF, 2, BLOCK, WIDTH)
    att_seq = of_sequence(attended[None])
    place, grad_eo, grad_eh, grad_sh, slot_gate = place_rows(
        exp_s,
        after(up_all, hidden_two).reshape(HALF, 2, BLOCK, WIDTH + META),
        expert_down,
        shared_two,
    )
    part, arrived, act, grad_gu, shared_act, shared_grad = expert_back(
        exp_s, after(hidden_all, att_seq), place, grad_eh, grad_sh, expert_gate, expert_up, w_shared
    )
    summed = add_low(part[1], lax.ppermute(part[0], "exp", core_swap))
    grad_two = swap_all(summed, "exp", same_core)

    rows_e = 2 * ROWS
    operands = (
        after(arrived, summed).reshape(LOCAL_E, rows_e, WIDTH),
        grad_eo.reshape(LOCAL_E, rows_e, WIDTH),
        act.reshape(LOCAL_E, rows_e, FF_E),
        grad_gu.reshape(LOCAL_E, rows_e, 2 * FF_E),
    )
    for_1, for_3 = expert_weights(ctx_s, ((2, 0), (1, 0), (2, 1), (3, 1)), True, *operands)
    operands = (after(operands[0], for_1),) + operands[1:]
    p0, p6, p1, p3 = expert_weights(ctx_s, ((0, 0), (3, 0), (0, 1), (1, 1)), False, *operands)

    def to(rows, k):
        return lax.ppermute(rows, "ctx", [(i, i ^ k) for i in range(N_CTX)])

    from_1, from_3 = to(for_1, 1), to(for_3, 3)
    shared_grad_late = after(shared_grad, p0).reshape(N_EXP * BLOCK, META)
    grad_scols = dg(hidden_all.reshape(N_EXP * BLOCK, WIDTH), shared_grad_late, TN).astype(bf16)
    act_late = after(shared_act, p0).reshape(N_EXP * BLOCK, META)
    grad_sdown = dg(act_late, up_all, TN)[:SHARED, :WIDTH].astype(bf16)
    extra = jnp.concatenate(
        [
            jnp.pad(
                grad_scols.reshape(N_EXP, N_CTX, 12, META).transpose(1, 0, 2, 3),
                ((0, 0), (0, 0), (0, 4), (0, 0)),
            ).reshape(N_CTX, 16 * N_EXP, META),
            grad_sdown.reshape(N_CTX, 8, HEADS, 128).transpose(0, 2, 1, 3).reshape(N_CTX, 96, 128),
        ],
        axis=1,
    )

    out_part = expert_output(
        exp_s, after(act, p0), slot_gate, place, shared_act, expert_down, shared_two
    )
    grad_two = after(grad_two, extra, out_part)
    grad_middle, grad_attn, grad_heads, gain_rows = middle_back(
        grad_two, middle, cotangent[0], gain_ffn, w_all
    )
    grad_query, near, far = attend_back(
        ctx_s, queries, grad_heads, att_f, logs, kv_all, grad_attn, extra, gain_rows
    )
    far = lax.ppermute(far, "ctx", z_swap)
    from_1, from_3 = after((from_1, from_3), near)
    add_a, add_b, part_0, part_1 = piece_sums(
        relay_kernel,
        (bf16, bf16, f32, f32),
        p0,
        p1,
        p3,
        p6,
        (from_1, 0),
        (from_3, 0),
        (from_1, 1),
        (from_3, 1),
    )
    got_11, got_30 = to(add_b, 1), to(add_a, 3)

    def from_x(rows, k):
        return lax.ppermute(rows, "exp", [(i, i ^ (4 * k)) for i in range(N_EXP)])

    out_sums = spread_sums(
        exp_s,
        after(out_part, add_a),
        lax.ppermute(out_part[0, :4], "exp", core_swap),
        lax.ppermute(out_part[0, 4:], "exp", core_swap),
    )
    out_near = (
        out_sums[0].astype(f32)
        + from_x(out_sums[1], 1).astype(f32)
        + from_x(out_sums[3], 3).astype(f32)
    )
    got_11, got_30 = after((got_11, got_30), far)
    own_part, side = piece_sums(side_kernel, (f32, bf16), part_0, part_1, got_11, got_30)
    across = to(side, 4)
    out_2 = from_x(after(out_sums[2], side), 2)

    shares = merge_shares(ctx_s, near, after(far, side, out_near))
    got = swap_all(shares, "ctx", y_groups)
    own = (own_part + after(across, shares).astype(f32)).astype(bf16)
    at_1, at_3, at_z = to(own, 1), to(own, 3), to(own, 4)

    columns, grad_kv, grad_down = column_grads(got, after(hidden_seq, own), att_seq)
    out_rows = after(out_near, columns) + out_2.astype(f32)
    out_across = lax.ppermute(
        out_rows[1].astype(bf16), "exp", [(i, i ^ 2) for i in range(N_EXP)]
    )
    owned = swap_all(columns, "exp")
    query_part = query_back(after(grad_query, columns), w_all)
    owned, gain_sum = owned_sums(owned, grad_down)
    at_z, at_1, at_3 = lax.optimization_barrier((after(at_z, out_2), at_1, at_3))
    owned, at_z1, at_z3 = lax.optimization_barrier((owned, to(at_z, 1), to(at_z, 3)))
    at_2, at_z2 = to(at_3, 1), to(at_z1, 3)
    mixed = (middle + out_rows[0] + out_across.astype(f32)).astype(bf16)[None]
    experts = unpack_experts(
        ctx_s,
        ((0, 0), (1, 0), (3, 0), (0, 1), (1, 1), (3, 1)),
        (after(own, owned), at_1, at_3, at_z, at_z1, at_z3),
    )
    owned = jnp.broadcast_to(owned, (N_CTX, OWNED_ROWS, HEAD_DIM))
    owned = swap_all(jnp.concatenate([grad_kv, owned], axis=1), "ctx")
    gain_attn_sum, *dense = finish(
        after(owned, experts[0], mixed, query_part),
        norm_attn.astype(f32).reshape(96, 1),
        query_weight,
        key_weight,
        value_weight,
    )
    input_grad = input_back(query_part, owned, w_all, tokens[0], gain_attn, grad_middle)
    at_2 = after(at_2, input_grad, *dense)
    experts = unpack_experts(
        ctx_s, ((2, 0), (2, 1)), (at_2, at_z2), experts
    )
    return (
        mixed,
        input_grad[None],
        gain_attn_sum[:, 0],
        gain_sum[12, :96],
        *dense,
        *experts,
    )


def solution(mesh):
    token_spec = P("exp", "ctx", None)
    rows = P("exp", None)
    expert = P("exp", None, None)
    placed = (token_spec,) * 3 + (P("exp"),) * 2 + (rows,) * 7 + (expert,) * 3 + (token_spec,)
    return jax.shard_map(
        on_device,
        mesh=mesh,
        in_specs=placed,
        out_specs=(token_spec,) * 2 + (P("exp"),) * 2 + (rows,) * 7 + (expert,) * 3,
        check_vma=False,
    )
```
